32 devices in a mesh: pat: 4 (over x, core), seq: 8 (over z, y).
Axes of the slice: x: 2, y: 2, z: 4, core: 2. Of those that a mesh axis runs over, the one named last changes fastest.
Arguments:
- tokens: float32 [1536, 4, 768], P('seq', 'pat'), may hold values from -6 to 6
- w_qkv: bfloat16 [768, 2304], replicated, may hold values from -0.21875 to 0.21875
- w_out: bfloat16 [768, 768], replicated, may hold values from -0.21875 to 0.21875
- w_up: bfloat16 [768, 3072], replicated, may hold values from -0.21875 to 0.21875
- w_down: bfloat16 [3072, 768], replicated, may hold values from -0.109375 to 0.109375
- gain_attn: float32 [768], replicated, may hold values from 0.5 to 1.5
- gain_inner: float32 [768], replicated, may hold values from 0.5 to 1.5
- gain_ffn: float32 [768], replicated, may hold values from 0.5 to 1.5
- gain_hidden: float32 [3072], replicated, may hold values from 0.5 to 1.5
- offsets: int32 [5, 12], replicated, may hold values from 0 to 11, as said below
- grad_out: float32 [1536, 4, 768], P('seq', 'pat'), may hold values from -6 to 6
Outputs:
- mixed_out: float32 [1536, 4, 768], P('seq', 'pat')
- grad_tokens: float32 [1536, 4, 768], P('seq', 'pat')
- grad_w_qkv: float32 [768, 2304], P(('pat', 'seq'))
- grad_w_out: float32 [768, 768], P(('pat', 'seq'))
- grad_w_up: float32 [768, 3072], P(('pat', 'seq'))
- grad_w_down: float32 [3072, 768], P(('pat', 'seq'))
- grad_gain_attn: float32 [768], P(('pat', 'seq'))
- grad_gain_inner: float32 [768], P(('pat', 'seq'))
- grad_gain_ffn: float32 [768], P(('pat', 'seq'))
- grad_gain_hidden: float32 [3072], P(('pat', 'seq'))
- denominator_means: float32 [5], replicated
The draws below stay inside these ranges and needn't reach their ends.
Inputs may be any that keep to these rules, and one draw needn't show every extreme that they name: For pattern p, offsets[p-1, h] lies in 0 to r_p - 1.
All inputs are finite; a program needn't handle non-finite values.
Results may differ from the reference program's by a relative error of at most 0.0003.
Values sent between devices are 32-bit elements; how exact they have to be, the bound alone decides.
A program may use at most 320 MiB of HBM per device.

```python
import math
import jax
import jax.numpy as jnp
from jax import lax

D = 768
HEADS = 12
HD = 64
FF = 3072
PATTERNS = 5
SEG1 = 2048
SEG2 = 4096
SEG3 = 8192
SEG4 = 16384
SEG5 = 32768
DILATION_ONE = 1
DILATION_TWO = 2
DILATION_THREE = 4
DILATION_FOUR = 6
DILATION_FIVE = 12
LENGTH = 6144
N_PAT = 4


def draw_offsets(key, part):
    key = jax.random.fold_in(key, 7)
    offset_rows = []
    dilation_rates = (DILATION_ONE, DILATION_TWO, DILATION_THREE, DILATION_FOUR, DILATION_FIVE)
    for pattern_spec in range(PATTERNS):
        ordering = jax.random.permutation(jax.random.fold_in(key, pattern_spec), HEADS)
        rotation = jax.random.randint(jax.random.fold_in(key, 100 + pattern_spec), (), 0, dilation_rates[pattern_spec])
        offset_rows.append(((ordering + rotation) % dilation_rates[pattern_spec]).astype(jnp.int32))
    return jnp.stack(offset_rows)


def block_levels(key, shape, shards, low, top_value):
    level = 1.0
    for dim, blocks in shards:
        heights = jax.random.uniform(jax.random.fold_in(jax.random.fold_in(key, 6), dim), (blocks,), jnp.float32, low / len(shards), top_value / len(shards))
        level = level * jnp.repeat(jnp.exp(heights), shape[dim] // blocks).reshape((-1,) + (1,) * (len(shape) - 1 - dim))
    return level


def scatter_about(own_key, dims, spread, limit, pieces=(), kind=jnp.bfloat16):
    loudness = block_levels(own_key, dims, pieces, -0.22, 0.18) if pieces else 1.0
    array = jax.random.normal(own_key, dims, jnp.float32) * spread * loudness
    return jnp.minimum(jnp.maximum(array, -limit), limit).astype(kind)


def setup_inputs(seed: int = 0) -> dict:
    seeds = jax.random.split(jax.random.key(seed), 12)
    tokens = scatter_about(seeds[0], (LENGTH // N_PAT, N_PAT, D), 1.0, 6.0, ((0, 8), (1, 4)), jnp.float32)
    w_qkv = scatter_about(seeds[1], (D, 3 * D), D ** -0.5, 0.21875)
    w_out = scatter_about(seeds[2], (D, D), D ** -0.5, 0.21875)
    w_up = scatter_about(seeds[3], (D, FF), D ** -0.5, 0.21875)
    w_down = scatter_about(seeds[4], (FF, D), FF ** -0.5, 0.109375)
    gain_attn = jnp.clip(1.0 + 0.1 * jax.random.normal(seeds[5], (D,), jnp.float32), 0.5, 1.5)
    gain_inner = jnp.clip(1.0 + 0.1 * jax.random.normal(seeds[6], (D,), jnp.float32), 0.5, 1.5)
    gain_ffn = jnp.clip(1.0 + 0.1 * jax.random.normal(seeds[7], (D,), jnp.float32), 0.5, 1.5)
    gain_hidden = jnp.clip(1.0 + 0.1 * jax.random.normal(seeds[8], (FF,), jnp.float32), 0.5, 1.5)
    offsets = draw_offsets(jax.random.fold_in(seeds[11], 71), 0)
    grad_out = scatter_about(seeds[10], (LENGTH // N_PAT, N_PAT, D), 1.0, 6.0, ((0, 8), (1, 4)), jnp.float32)
    return {"tokens": tokens, "w_qkv": w_qkv, "w_out": w_out, "w_up": w_up, "w_down": w_down, "gain_attn": gain_attn, "gain_inner": gain_inner, "gain_ffn": gain_ffn, "gain_hidden": gain_hidden, "offsets": offsets, "grad_out": grad_out}


MATMUL_ACCURACY = lax.Precision.HIGHEST
LN_EPSILON = 1e-05
MASK_VALUE = -1e+30

@jax.custom_vjp
def low(v):
    return lax.optimization_barrier(v.astype(jnp.bfloat16)).astype(jnp.float32)

@jax.custom_vjp
def low_back(v):
    return v

def low_keep(v):
    return (low(v), None)

def low_pass(kept, grad):
    return (grad,)

def back_keep(v):
    return (v, None)

def back_low(kept, grad):
    return (low(grad),)
low.defvjp(low_keep, low_pass)
low_back.defvjp(back_keep, back_low)

def layer_norm(x, gain_vec):
    average = lax.optimization_barrier(jnp.mean(x, -1, keepdims=True))
    centred = x - average
    variance = lax.optimization_barrier(jnp.mean(centred * centred, -1, keepdims=True))
    return centred * lax.rsqrt(variance + LN_EPSILON) * gain_vec

def select_table(offsets_row, dilation_rate):
    return (jnp.arange(dilation_rate, dtype=jnp.int32)[:, None] == offsets_row[None, :]).astype(jnp.float32)

def spread_apart(x, select_option, dilation_rate):
    shaped = x.reshape(x.shape[0] // dilation_rate, dilation_rate, x.shape[1], x.shape[2])
    return jnp.einsum('trhd,rh->thd', shaped, select_option, precision=MATMUL_ACCURACY)

def spread_rows(x, select_option):
    return jnp.einsum('thd,rh->trhd', x, select_option, precision=MATMUL_ACCURACY).reshape(-1, x.shape[1], x.shape[2])

def spread_scalars(x, select_option):
    return jnp.einsum('th,rh->trh', x, select_option, precision=MATMUL_ACCURACY).reshape(-1, x.shape[1])

def pattern_attention(query_rows, key_row_set, value_row_set, offsets_row, dilation_rate, segment_length):
    select_option = select_table(offsets_row, dilation_rate)
    sparse_queries = spread_apart(query_rows, select_option, dilation_rate)
    sparse_keys = spread_apart(key_row_set, select_option, dilation_rate)
    sparse_values = spread_apart(value_row_set, select_option, dilation_rate)
    row_count = sparse_queries.shape[0]
    query_block = min(512, LENGTH // 12)
    returned_rows = (segment_length - 1) // dilation_rate
    places = (jnp.arange(row_count, dtype=jnp.int32)[:, None] * dilation_rate + offsets_row[None, :]).astype(jnp.int32)
    padded_keys = jnp.pad(sparse_keys, ((returned_rows, 0), (0, 0), (0, 0)))
    padded_values = jnp.pad(sparse_values, ((returned_rows, 0), (0, 0), (0, 0)))
    p_pad = jnp.pad(places, ((returned_rows, 0), (0, 0)), constant_values=-1)
    inverse_square_root = 1.0 / math.sqrt(HD)

    def one_block(block_id):
        leading_row = (block_id * query_block).astype(jnp.int32)
        query_tile = lax.dynamic_slice_in_dim(sparse_queries, leading_row, query_block, 0)
        query_position = lax.dynamic_slice_in_dim(places, leading_row, query_block, 0).T
        k_blk = lax.dynamic_slice_in_dim(padded_keys, leading_row, query_block + returned_rows, 0)
        v_blk = lax.dynamic_slice_in_dim(padded_values, leading_row, query_block + returned_rows, 0)
        key_position = lax.dynamic_slice_in_dim(p_pad, leading_row, query_block + returned_rows, 0).T
        score_matrix = jnp.einsum('ozt,bzt->zob', query_tile, k_blk, precision=MATMUL_ACCURACY) * inverse_square_root
        q_cols = query_position[:, :, None]
        k_cols = key_position[:, None, :]
        permitted_mask = (k_cols <= q_cols) & (k_cols >= 0) & (k_cols // segment_length == q_cols // segment_length)
        masked_logits = jnp.where(permitted_mask, score_matrix, MASK_VALUE)
        row_max = lax.optimization_barrier(jnp.max(masked_logits, -1))
        softmax_weights = jnp.where(permitted_mask, jnp.exp(masked_logits - row_max[..., None]), 0.0)
        row_sum = lax.optimization_barrier(jnp.sum(softmax_weights, -1))
        mixture = jnp.einsum('hqk,khd->qhd', softmax_weights, v_blk, precision=MATMUL_ACCURACY) / row_sum.T[..., None]
        return (mixture, (row_max + jnp.log(row_sum)).T)
    mixtures, log_sums = lax.map(jax.checkpoint(one_block), jnp.arange(row_count // query_block, dtype=jnp.int32))
    return (mixtures.reshape(row_count, query_rows.shape[1], query_rows.shape[2]), log_sums.reshape(row_count, query_rows.shape[1]), select_option)

def forward(flat_tokens, w_qkv, w_out, w_up, w_down, gain_attn, gain_inner, gain_ffn, gain_hidden, offsets):
    qkv = jnp.dot(layer_norm(flat_tokens, gain_attn), w_qkv, precision=MATMUL_ACCURACY).reshape(LENGTH, 3, HEADS, HD)
    dilation_rates = (DILATION_ONE, DILATION_TWO, DILATION_THREE, DILATION_FOUR, DILATION_FIVE)
    segment_lengths = (SEG1, SEG2, SEG3, SEG4, SEG5)
    full_lse = []
    full_mix = []
    log_means = []
    for pattern_spec in range(PATTERNS):
        mixture, log_sum, select_option = pattern_attention(qkv[:, 0], qkv[:, 1], qkv[:, 2], offsets[pattern_spec], dilation_rates[pattern_spec], segment_lengths[pattern_spec])
        covered = spread_scalars(jnp.ones_like(log_sum), select_option)
        full_lse.append(spread_scalars(log_sum, select_option) + (covered - 1.0) * 1e+30)
        full_mix.append(spread_rows(mixture, select_option))
        log_means.append(jnp.sum(log_sum) / float(LENGTH // dilation_rates[pattern_spec] * HEADS))
    stacked = jnp.stack(full_lse)
    row_max = lax.optimization_barrier(jnp.max(stacked, 0))
    softmax_weights = jnp.exp(stacked - row_max)
    row_sum = lax.optimization_barrier(jnp.sum(softmax_weights, 0))
    attended = full_mix[0] * softmax_weights[0][..., None]
    for pattern_spec in range(1, PATTERNS):
        attended = attended + full_mix[pattern_spec] * softmax_weights[pattern_spec][..., None]
    attended = attended / row_sum[..., None]
    residual = flat_tokens + jnp.dot(layer_norm(attended.reshape(LENGTH, D), gain_inner), w_out, precision=MATMUL_ACCURACY)
    hidden = jax.nn.gelu(jnp.dot(layer_norm(residual, gain_ffn), w_up, precision=MATMUL_ACCURACY), approximate=False)
    output = residual + jnp.dot(layer_norm(hidden, gain_hidden), w_down, precision=MATMUL_ACCURACY)
    return (output, jnp.stack(log_means))

def reference(tokens, w_qkv, w_out, w_up, w_down, gain_attn, gain_inner, gain_ffn, gain_hidden, offsets, grad_out):
    flat_tokens = tokens.reshape(LENGTH, D)
    w_qkv = w_qkv.astype(jnp.float32)
    w_out = w_out.astype(jnp.float32)
    w_up = w_up.astype(jnp.float32)
    w_down = w_down.astype(jnp.float32)

    def wrapped(flat_in, qkv_in, out_in, up_in, down_in, attn_in, inner_in, ffn_in, hidden_in):
        return forward(flat_in, qkv_in, out_in, up_in, down_in, attn_in, inner_in, ffn_in, hidden_in, offsets)
    output, pullback, log_means = jax.vjp(wrapped, flat_tokens, w_qkv, w_out, w_up, w_down, gain_attn, gain_inner, gain_ffn, gain_hidden, has_aux=True)
    gradients = pullback(grad_out.reshape(LENGTH, D))
    row_shape = (LENGTH // N_PAT, N_PAT, D)
    return (output.reshape(row_shape), gradients[0].reshape(row_shape), gradients[1], gradients[2], gradients[3], gradients[4], gradients[5], gradients[6], gradients[7], gradients[8], log_means)
```

```python
import functools
import math

import jax
import jax.numpy as jnp
from jax import lax
from jax.experimental import pallas as pl
from jax.experimental.pallas import tpu as pltpu
from jax.sharding import PartitionSpec as P

D = 768
HEADS = 12
HD = 64
FF = 3072
PATTERNS = 5
SEGMENTS = (2048, 4096, 8192, 16384, 32768)
DILATIONS = (1, 2, 4, 6, 12)
LN_EPSILON = 1e-05
NEG = -1e30
F32 = jnp.float32
BF16 = jnp.bfloat16
HIGHEST = lax.Precision.HIGHEST
VMEM_LIMIT = 58 * 1024 * 1024

ROWS = 192
HALF = ROWS // 2
RUNS = 8
TOTAL = ROWS * RUNS
PACK = ROWS + HALF
HOMES = 16
THIRD = TOTAL // 3
MESH = pl.DeviceIdType.MESH


def dot_nn(a, b):
    return lax.dot_general(a, b, (((1,), (0,)), ((), ())), preferred_element_type=F32)


def dot_nt(a, b):
    return lax.dot_general(a, b, (((1,), (1,)), ((), ())), preferred_element_type=F32)


def split(v):
    hi = v.astype(BF16)
    return hi, (v - hi.astype(F32)).astype(BF16)


def split32(v):
    hi = v.astype(BF16).astype(F32)
    return hi, v - hi


def lower_lanes(v):
    return lax.broadcasted_iota(jnp.int32, v.shape, v.ndim - 1) < HD


def swap(v):
    return pltpu.roll(v, HD, v.ndim - 1)


def pick(a, b):
    return jnp.where(lower_lanes(a), a, b)


def head_place(h):
    z = h // 3
    column = lax.rem(lax.rem(h, 3) + z + 1, 4)
    return column // 2, z * 2 + lax.rem(column, 2)


def head_here(p, s):
    z = s // 2
    column = (p // 2) * 2 + lax.rem(s, 2)
    k = lax.rem(column - z + 7, 4)
    return k < 3, z * 3 + jnp.minimum(k, 2)


def whole(*_):
    return pl.BlockSpec(memory_space=pltpu.VMEM)


VM = pl.BlockSpec(memory_space=pltpu.VMEM)
ANY = pl.BlockSpec(memory_space=pl.ANY)
SM = pl.BlockSpec(memory_space=pltpu.SMEM)


def params(**kw):
    return pltpu.CompilerParams(vmem_limit_bytes=VMEM_LIMIT, **kw)


def normed(v):
    centred = v - jnp.mean(v, -1, keepdims=True)
    rs = lax.rsqrt(jnp.mean(centred * centred, -1, keepdims=True) + LN_EPSILON)
    return centred * rs, rs


def put_split(ref, v):
    hi, lo = split(v)
    n = v.shape[0]
    ref[0:n, :] = hi
    ref[n : 2 * n, :] = lo


def front_kernel(x_ref, w_ref, gain_ref, pk_ref, lhs):
    n, _ = normed(x_ref[...])
    put_split(lhs, n * gain_ref[...])
    for jj in range(3):
        parts = []
        for kind in range(3):
            c0 = kind * D + 256 * jj
            r = dot_nn(lhs[...], w_ref[:, c0 : c0 + 256])
            parts.append(r[:ROWS] + r[ROWS:])
        for half in range(2):
            q, k, v = (a[:, 128 * half : 128 * half + 128] for a in parts)
            h = 4 * jj + 2 * half
            pk_ref[h, 0:ROWS, :] = pick(k, swap(v))
            pk_ref[h + 1, 0:ROWS, :] = pick(swap(k), v)
            top, bottom = q[:HALF], q[HALF:]
            pk_ref[h, ROWS:PACK, :] = pick(top, swap(bottom))
            pk_ref[h + 1, ROWS:PACK, :] = pick(swap(top), bottom)


def front(x, w, gain):
    return pl.pallas_call(
        front_kernel,
        out_shape=jax.ShapeDtypeStruct((HEADS, PACK, 128), F32),
        in_specs=[VM] * 3,
        out_specs=VM,
        scratch_shapes=[pltpu.VMEM((2 * ROWS, D), BF16)],
        compiler_params=params(),
    )(x, w, gain.reshape(1, D))


def place_facts():
    p, s = lax.axis_index("pat"), lax.axis_index("seq")
    x, core = p // 2, lax.rem(p, 2)
    active, head = head_here(p, s)
    return p, s, x, core, active, head


def home_device(core, m):
    return core * 2 + lax.rem(m, 2), m // 2


def head_device(h, b):
    hx, hs = head_place(h)
    return hx * 2 + b, hs


def same(p, s, q, t):
    return jnp.logical_and(p == q, s == t)


def to(p, s):
    return {"pat": p, "seq": s}


def scatter_kernel(forward, pk, own, *rest):
    if forward:
        sib, send, recv, fsend, frecv = rest
    else:
        send, recv = rest
    p, s, x, core, active, head = place_facts()
    slot = s * 2 + core
    barrier = pltpu.get_barrier_semaphore()

    @pl.when(active)
    def _():
        def greet(m, carry):
            q, t = home_device(core, m)

            @pl.when(jnp.logical_not(same(p, s, q, t)))
            def _():
                pl.semaphore_signal(barrier, inc=1, device_id=to(q, t), device_id_type=MESH)

            return carry

        lax.fori_loop(0, HOMES, greet, 0)
        if forward:
            pl.semaphore_signal(barrier, inc=1, device_id=to(x * 2 + 1 - core, s), device_id_type=MESH)

    mine = jnp.logical_and(active, core == x)
    waits = HEADS - mine.astype(jnp.int32)
    if forward:
        waits = waits + active.astype(jnp.int32)
    pl.semaphore_wait(barrier, waits)

    def copy(h):
        q, t = head_device(h, x)
        return q, t, pltpu.make_async_remote_copy(
            src_ref=pk.at[h],
            dst_ref=own.at[slot],
            send_sem=send.at[h],
            recv_sem=recv.at[slot],
            device_id=to(q, t),
            device_id_type=MESH,
        )

    def start(j, carry):
        h = lax.rem(j + 3 * (s // 2) + 2 * p, HEADS)
        q, t, remote = copy(h)

        @pl.when(same(p, s, q, t))
        def _():
            pltpu.make_async_copy(pk.at[h], own.at[slot], recv.at[slot]).start()

        @pl.when(jnp.logical_not(same(p, s, q, t)))
        def _():
            remote.start()

        return carry

    lax.fori_loop(0, HEADS, start, 0)

    def passed(m):
        return pltpu.make_async_remote_copy(
            src_ref=own.at[m, pl.ds(0, ROWS), :],
            dst_ref=sib.at[m],
            send_sem=fsend.at[m],
            recv_sem=frecv.at[m],
            device_id=to(x * 2 + 1 - core, s),
            device_id_type=MESH,
        )

    @pl.when(active)
    def _():
        def arrive(m, carry):
            pltpu.make_async_copy(own.at[m], own.at[m], recv.at[m]).wait()
            if forward:
                passed(m).start()
            return carry

        lax.fori_loop(0, HOMES, arrive, 0)
        if forward:

            def finish(m, carry):
                passed(m).wait()
                return carry

            lax.fori_loop(0, HOMES, finish, 0)

    def sent(h, carry):
        q, t, remote = copy(h)

        @pl.when(jnp.logical_not(same(p, s, q, t)))
        def _():
            remote.wait_send()

        return carry

    lax.fori_loop(0, HEADS, sent, 0)


def to_heads(packets, forward, cid):
    rows = packets.shape[1]
    shapes = [jax.ShapeDtypeStruct((HOMES, rows, 128), F32)]
    sems = [pltpu.SemaphoreType.DMA((HEADS,)), pltpu.SemaphoreType.DMA((HOMES,))]
    if forward:
        shapes.append(jax.ShapeDtypeStruct((HOMES, ROWS, 128), F32))
        sems += [pltpu.SemaphoreType.DMA((HOMES,)), pltpu.SemaphoreType.DMA((HOMES,))]
    return pl.pallas_call(
        functools.partial(scatter_kernel, forward),
        out_shape=shapes,
        in_specs=[ANY],
        out_specs=[ANY] * len(shapes),
        scratch_shapes=sems,
        compiler_params=params(collective_id=cid, has_side_effects=True),
    )(packets)


def home_barrier(p, s, x, core, active, barrier, also_sibling):
    def greet(h, carry):
        q, t = head_device(h, x)

        @pl.when(jnp.logical_not(same(p, s, q, t)))
        def _():
            pl.semaphore_signal(barrier, inc=1, device_id=to(q, t), device_id_type=MESH)

        return carry

    lax.fori_loop(0, HEADS, greet, 0)

    @pl.when(active)
    def _():
        if also_sibling:
            pl.semaphore_signal(barrier, inc=1, device_id=to(x * 2 + 1 - core, s), device_id_type=MESH)
        mine = (core == x).astype(jnp.int32)
        pl.semaphore_wait(barrier, HOMES - mine + (1 if also_sibling else 0))


def gather_kernel(pk, rec, send, recv):
    p, s, x, core, active, head = place_facts()
    barrier = pltpu.get_barrier_semaphore()
    home_barrier(p, s, x, core, active, barrier, False)

    def copy(m):
        q, t = home_device(core, m)
        return q, t, pltpu.make_async_remote_copy(
            src_ref=pk.at[m],
            dst_ref=rec.at[head],
            send_sem=send.at[m],
            recv_sem=recv.at[head],
            device_id=to(q, t),
            device_id_type=MESH,
        )

    @pl.when(active)
    def _():
        def start(j, carry):
            m = lax.rem(j + 2 * s + 1, HOMES)
            q, t, remote = copy(m)

            @pl.when(same(p, s, q, t))
            def _():
                pltpu.make_async_copy(pk.at[m], rec.at[head], recv.at[head]).start()

            @pl.when(jnp.logical_not(same(p, s, q, t)))
            def _():
                remote.start()

            return carry

        lax.fori_loop(0, HOMES, start, 0)

    def arrive(h, carry):
        pltpu.make_async_copy(rec.at[h], rec.at[h], recv.at[h]).wait()
        return carry

    lax.fori_loop(0, HEADS, arrive, 0)

    @pl.when(active)
    def _():
        def sent(m, carry):
            q, t, remote = copy(m)

            @pl.when(jnp.logical_not(same(p, s, q, t)))
            def _():
                remote.wait_send()

            return carry

        lax.fori_loop(0, HOMES, sent, 0)


def to_homes(packets, cid):
    rows = packets.shape[1]
    return pl.pallas_call(
        gather_kernel,
        out_shape=jax.ShapeDtypeStruct((HEADS, rows, 128), F32),
        in_specs=[ANY],
        out_specs=ANY,
        scratch_shapes=[pltpu.SemaphoreType.DMA((HOMES,)), pltpu.SemaphoreType.DMA((HEADS,))],
        compiler_params=params(collective_id=cid, has_side_effects=True),
    )(packets)


def grads_kernel(own, sib, rec, came, total, send, recv, qsend, qrecv, fsend, frecv):
    p, s, x, core, active, head = place_facts()
    barrier = pltpu.get_barrier_semaphore()
    home_barrier(p, s, x, core, active, barrier, True)
    here = slice(0, ROWS)

    def passed(m):
        return pltpu.make_async_remote_copy(
            src_ref=sib.at[m],
            dst_ref=came.at[m],
            send_sem=fsend.at[m],
            recv_sem=frecv.at[m],
            device_id=to(x * 2 + 1 - core, s),
            device_id_type=MESH,
        )

    def copies(m):
        q, t = home_device(core, m)
        kv = pltpu.make_async_remote_copy(
            src_ref=total.at[m],
            dst_ref=rec.at[head, pl.ds(0, ROWS), :],
            send_sem=send.at[m],
            recv_sem=recv.at[head],
            device_id=to(q, t),
            device_id_type=MESH,
        )
        dq = pltpu.make_async_remote_copy(
            src_ref=own.at[m, pl.ds(ROWS, HALF), :],
            dst_ref=rec.at[head, pl.ds(ROWS, HALF), :],
            send_sem=qsend.at[m],
            recv_sem=qrecv.at[head],
            device_id=to(q, t),
            device_id_type=MESH,
        )
        return q, t, kv, dq

    @pl.when(active)
    def _():
        def start(m, carry):
            passed(m).start()
            return carry

        lax.fori_loop(0, HOMES, start, 0)

        def add(m, carry):
            q, t, kv, dq = copies(m)
            passed(m).wait_recv()
            total[m] = own[m, here, :] + came[m]

            @pl.when(same(p, s, q, t))
            def _():
                pltpu.make_async_copy(
                    own.at[m, pl.ds(ROWS, HALF), :], rec.at[head, pl.ds(ROWS, HALF), :], qrecv.at[head]
                ).start()
                pltpu.make_async_copy(total.at[m], rec.at[head, pl.ds(0, ROWS), :], recv.at[head]).start()

            @pl.when(jnp.logical_not(same(p, s, q, t)))
            def _():
                dq.start()
                kv.start()

            return carry

        lax.fori_loop(0, HOMES, add, 0)

    def arrive(h, carry):
        a = rec.at[h, pl.ds(0, ROWS), :]
        b = rec.at[h, pl.ds(ROWS, HALF), :]
        pltpu.make_async_copy(a, a, recv.at[h]).wait()
        pltpu.make_async_copy(b, b, qrecv.at[h]).wait()
        return carry

    lax.fori_loop(0, HEADS, arrive, 0)

    @pl.when(active)
    def _():
        def sent(m, carry):
            q, t, kv, dq = copies(m)
            passed(m).wait_send()

            @pl.when(jnp.logical_not(same(p, s, q, t)))
            def _():
                dq.wait_send()
                kv.wait_send()

            return carry

        lax.fori_loop(0, HOMES, sent, 0)


def grads_to_homes(own, sib, cid):
    dma = pltpu.SemaphoreType.DMA
    return pl.pallas_call(
        grads_kernel,
        out_shape=jax.ShapeDtypeStruct((HEADS, PACK, 128), F32),
        in_specs=[VM, VM],
        out_specs=ANY,
        scratch_shapes=[
            pltpu.VMEM((HOMES, ROWS, 128), F32),
            pltpu.VMEM((HOMES, ROWS, 128), F32),
            dma((HOMES,)),
            dma((HEADS,)),
            dma((HOMES,)),
            dma((HEADS,)),
            dma((HOMES,)),
            dma((HOMES,)),
        ],
        compiler_params=params(collective_id=cid, has_side_effects=True),
    )(own, sib)


def tile_positions(rows, columns, row_classes, column_classes, t_step, class_step):
    r = lax.broadcasted_iota(jnp.int32, (rows, columns), 0)
    q = lax.broadcasted_iota(jnp.int32, (rows, columns), 1)
    rn, qn = rows // row_classes, columns // column_classes
    return (r % rn) * t_step + (r // rn) * class_step, (q % qn) * t_step + (q // qn) * class_step


def key_bias(q_shape, k_shape, t_step, class_step, shift, keys_first):
    nq, nk = q_shape[0] * q_shape[1], k_shape[0] * k_shape[1]
    if keys_first:
        kp, qp = tile_positions(nk, nq, k_shape[0], q_shape[0], t_step, class_step)
    else:
        qp, kp = tile_positions(nq, nk, q_shape[0], k_shape[0], t_step, class_step)
    return jnp.where(kp - qp <= shift, 0.0, NEG).astype(F32)


def unpack_keys(own, sib, b, kvf):
    def one(m, carry):
        c = 2 * b + lax.rem(m, 2)
        d = 2 * (1 - b) + lax.rem(m, 2)
        t = pl.multiple_of((m // 2) * ROWS, 64)
        kvf[c, pl.ds(t, ROWS), :] = own[m, 0:ROWS, :]
        kvf[d, pl.ds(t, ROWS), :] = sib[m]
        return carry

    lax.fori_loop(0, HOMES, one, 0)


def unpack_pairs(src, first, dst, scale):
    def one(m, carry):
        t = pl.multiple_of((m // 2) * ROWS, 32)
        v = src[m, first : first + HALF, :] * scale
        w = swap(v)
        dst[lax.rem(m, 2), pl.ds(t, HALF), :] = pick(v, w)
        dst[lax.rem(m, 2), pl.ds(t + HALF, HALF), :] = pick(w, v)
        return carry

    lax.fori_loop(0, HOMES, one, 0)


def keys_and_values(kv):
    hi, lo = split32(kv)
    k2 = pick(hi, swap(lo))
    v2 = pick(swap(hi), lo)
    return k2, v2


def doubled(v):
    return jnp.concatenate([v, v], 1)


def query_quads(qq):
    hi, lo = split32(qq)
    return jnp.concatenate([hi.astype(BF16), lo.astype(BF16)], 1), pick(hi, lo).astype(BF16)


def class_facts(o, b):
    o4, o5 = o[3], o[4]
    k4 = ((lax.rem(o4, 4), o4 // 4), (lax.rem(o4 + 6, 4), (o4 + 6) // 4))
    first = (k4[0][0] // 2) == b
    e4 = jnp.where(first, 0, 1)
    q4 = (jnp.where(first, k4[0][0], k4[1][0]), jnp.where(first, k4[0][1], k4[1][1]))
    k5 = (lax.rem(o5, 4), o5 // 4)
    return k4, e4, q4, k5


def forward_kernel(info, own, sib, ap, lse, sums, kvf, kc, vc, qf, qc, k4, v4, q4, k5, v5, q5, acc, mx, A, L, M, b1, b2, b3, b4):
    active = info[0] == 1
    b = info[1]
    offs = [info[2 + i] for i in range(PATTERNS)]
    sums[...] = jnp.zeros_like(sums)

    @pl.when(active)
    def _():
        ones = jnp.ones((128, 128), BF16)
        unpack_keys(own, sib, b, kvf)
        unpack_pairs(own, ROWS, qf, 1.0 / math.sqrt(HD))

        def prepare(i, carry):
            c, t = i // 12, pl.multiple_of(lax.rem(i, 12) * 128, 128)
            k2, v2 = keys_and_values(kvf[c, pl.ds(t, 128), :])
            kc[c, pl.ds(t, 128), :] = doubled(k2.astype(BF16))
            vc[c, pl.ds(t, 128), :] = jnp.concatenate([v2.astype(BF16), ones], 1)
            return carry

        lax.fori_loop(0, 48, prepare, 0)

        def prepare_q(i, carry):
            c, t = i // 12, pl.multiple_of(lax.rem(i, 12) * 128, 128)
            qc[c, pl.ds(t, 128), :] = query_quads(qf[c, pl.ds(t, 128), :])[0]
            return carry

        lax.fori_loop(0, 24, prepare_q, 0)

        keys4, e4, (qc4, qv4), (kc5, kv5) = class_facts(offs, b)
        for blk in range(4):
            r = slice(128 * blk, 128 * blk + 128)
            for e in range(2):
                c, v = keys4[e]
                k2, v2 = keys_and_values(kvf[c, pl.ds(v + 384 * blk, 128, stride=3), :])
                k4[e, r, :] = doubled(k2.astype(BF16))
                v4[e, r, :] = jnp.concatenate([v2.astype(BF16), ones], 1)
            q4[r, :] = query_quads(qf[qc4 - 2 * b, pl.ds(qv4 + 384 * blk, 128, stride=3), :])[0]
            k2, v2 = keys_and_values(kvf[kc5, pl.ds(kv5 + 384 * blk, 128, stride=3), :])
            k5[r, :] = doubled(k2.astype(BF16))
            v5[r, :] = jnp.concatenate([v2.astype(BF16), ones], 1)
            q5[r, :] = query_quads(qf[lax.rem(kc5, 2), pl.ds(kv5 + 384 * blk, 128, stride=3), :])[0]

        b1[...] = key_bias((2, 128), (4, 128), 4, 1, 2 * b, False)
        b2[...] = key_bias((1, 256), (2, 256), 4, 2, 2 * b, False)
        b3[...] = key_bias((1, 256), (1, 256), 1, 1, 0, False)
        b4[...] = key_bias((1, 256), (2, 256), 12, 6, 6 * e4, False)

        def tile(g, q, k, v, bias, first):
            s = dot_nt(q, k)
            if bias is not None:
                s = s + bias[...]
            top = jnp.max(s, -1, keepdims=True)
            n = k.shape[0] // 128
            if first:
                m = jnp.broadcast_to(top, (256, 128))
            else:
                old = mx[g]
                m = jnp.maximum(old, top)
            mx[g] = m
            p = jnp.exp(s - jnp.concatenate([m] * n, 1))
            hi, lo = split(p)
            new = dot_nn(hi, v) + dot_nn(lo, v)
            if first:
                acc[g] = new
            else:
                alpha = jnp.exp(old - m)
                acc[g] = acc[g] * doubled(alpha) + new

        def note(pattern, g):
            rows = mx[g] + jnp.log(acc[g][:, 128:])
            sums[pattern : pattern + 1, :] += jnp.sum(rows, 0, keepdims=True)

        def q1(qb, carry):
            def at(g, blk):
                return pl.ds(pl.multiple_of(512 * g + 128 * blk, 128), 128)

            def load_q(g):
                return qc[:, at(g, qb), :].reshape(256, 256)

            def step(kb, bias, first):
                for g in range(3):
                    k = kc[:, at(g, kb), :].reshape(512, 256)
                    v = vc[:, at(g, kb), :].reshape(512, 256)
                    tile(g, load_q(g), k, v, bias, first)

            step(qb, b1, True)

            def more(kb, inner):
                step(kb, None, False)
                return inner

            lax.fori_loop(0, qb, more, 0)
            for g in range(3):
                note(0, g)
                A[:, at(g, qb), :] = acc[g][:, :128].reshape(2, 128, 128)
                L[:, at(g, qb), :] = acc[g][:, 128:].reshape(2, 128, 128)
                M[:, at(g, qb), :] = mx[g].reshape(2, 128, 128)
            return carry

        lax.fori_loop(0, 4, q1, 0)

        def merge(g, ci, rows):
            m0, m1 = M[ci, rows, :], mx[g]
            m = jnp.maximum(m0, m1)
            w0, w1 = jnp.exp(m0 - m), jnp.exp(m1 - m)
            A[ci, rows, :] = A[ci, rows, :] * w0 + acc[g][:, :128] * w1
            L[ci, rows, :] = L[ci, rows, :] * w0 + acc[g][:, 128:] * w1
            M[ci, rows, :] = m

        def at256(blk):
            return pl.ds(pl.multiple_of(256 * blk, 128), 256)

        par = offs[1]

        def keys2(ref, blk):
            return jnp.concatenate([ref[par, at256(blk), :], ref[par + 2, at256(blk), :]], 0)

        def q2(qb, carry):
            q = qc[par, at256(qb), :]
            tile(0, q, keys2(kc, qb), keys2(vc, qb), b2, True)

            def more(kb, inner):
                tile(0, q, keys2(kc, kb), keys2(vc, kb), None, False)
                return inner

            lax.fori_loop(jnp.where(qb >= 4, 4, 0), qb, more, 0)
            note(1, 0)
            merge(0, par, at256(qb))
            return carry

        lax.fori_loop(0, TOTAL // 256, q2, 0)

        o3 = offs[2]

        @pl.when(o3 // 2 == b)
        def _():
            ci = lax.rem(o3, 2)

            def q3(qb, carry):
                q = qc[ci, at256(qb), :]
                tile(0, q, kc[o3, at256(qb), :], vc[o3, at256(qb), :], b3, True)

                def more(kb, inner):
                    tile(0, q, kc[o3, at256(kb), :], vc[o3, at256(kb), :], None, False)
                    return inner

                lax.fori_loop(0, qb, more, 0)
                note(2, 0)
                merge(0, ci, at256(qb))
                return carry

            lax.fori_loop(0, TOTAL // 256, q3, 0)

        for qb in range(2):
            q = q4[256 * qb : 256 * qb + 256, :]
            for kb in range(qb, -1, -1):
                ks = slice(256 * kb, 256 * kb + 256)
                k = k4[:, ks, :].reshape(512, 256)
                v = v4[:, ks, :].reshape(512, 256)
                tile(qb, q, k, v, b4 if kb == qb else None, kb == qb)
            note(3, qb)
            merge(qb, qc4 - 2 * b, pl.ds(qv4 + 768 * qb, 256, stride=3))

        @pl.when(kc5 // 2 == b)
        def _():
            for qb in range(2):
                q = q5[256 * qb : 256 * qb + 256, :]
                for kb in range(qb, -1, -1):
                    ks = slice(256 * kb, 256 * kb + 256)
                    tile(qb, q, k5[ks, :], v5[ks, :], b3 if kb == qb else None, kb == qb)
                note(4, qb)
                merge(qb, lax.rem(kc5, 2), pl.ds(kv5 + 768 * qb, 256, stride=3))

        def finish(m, carry):
            ci = lax.rem(m, 2)
            t = pl.multiple_of((m // 2) * ROWS, 64)
            rows = pl.ds(t, ROWS)
            a, l = A[ci, rows, :], L[ci, rows, :]
            out = (a + swap(a)) / l
            ap[m] = pick(out[:HALF], out[HALF:])
            lse[ci, rows, :] = M[ci, rows, :] + jnp.log(l)
            return carry

        lax.fori_loop(0, HOMES, finish, 0)


def attention_forward(info, own, sib):
    big = pltpu.VMEM((4, TOTAL, 256), BF16)
    state = pltpu.VMEM((2, TOTAL, 128), F32)
    return pl.pallas_call(
        forward_kernel,
        out_shape=[
            jax.ShapeDtypeStruct((HOMES, HALF, 128), F32),
            jax.ShapeDtypeStruct((2, TOTAL, 128), F32),
            jax.ShapeDtypeStruct((8, 128), F32),
        ],
        in_specs=[SM, VM, VM],
        out_specs=[VM, VM, VM],
        scratch_shapes=[
            pltpu.VMEM((4, TOTAL, 128), F32),
            big,
            big,
            state,
            pltpu.VMEM((2, TOTAL, 256), BF16),
            pltpu.VMEM((2, THIRD, 256), BF16),
            pltpu.VMEM((2, THIRD, 256), BF16),
            pltpu.VMEM((THIRD, 256), BF16),
            pltpu.VMEM((THIRD, 256), BF16),
            pltpu.VMEM((THIRD, 256), BF16),
            pltpu.VMEM((THIRD, 256), BF16),
            pltpu.VMEM((3, 256, 256), F32),
            pltpu.VMEM((3, 256, 128), F32),
            state,
            state,
            state,
            pltpu.VMEM((256, 512), F32),
            pltpu.VMEM((256, 512), F32),
            pltpu.VMEM((256, 256), F32),
            pltpu.VMEM((256, 512), F32),
        ],
        compiler_params=params(),
    )(info, own, sib)


def backward_kernel(info, own, sib, dap, ap, lse, down, dsib, kvf, kc, vc, kt, qf, qc, qn, dc, dn, X, lt, k4, v4, kt4, q4, qn4, d4, dn4, lt4, k5, v5, kt5, q5, qn5, d5, dn5, lt5, dqt, dk, dv, dq, dk4, dv4, b1, b2, b3, b4):
    active = info[0] == 1
    b = info[1]
    offs = [info[2 + i] for i in range(PATTERNS)]
    df = dq

    @pl.when(active)
    def _():
        unpack_keys(own, sib, b, kvf)
        unpack_pairs(own, ROWS, qf, 1.0 / math.sqrt(HD))
        unpack_pairs(dap, 0, df, 1.0)

        def facts(m, carry):
            ci = lax.rem(m, 2)
            t = pl.multiple_of((m // 2) * ROWS, 32)
            prod = dap[m] * ap[m]
            low = lower_lanes(prod)
            d0 = jnp.sum(jnp.where(low, prod, 0.0), -1, keepdims=True)
            d1 = jnp.sum(jnp.where(low, 0.0, prod), -1, keepdims=True)
            for part, d in ((0, d0), (1, d1)):
                rows = pl.ds(t + HALF * part, HALF)
                l = lse[ci, rows, :]
                X[ci, rows, :] = jnp.where(low, l, jnp.broadcast_to(d, l.shape))
            return carry

        lax.fori_loop(0, HOMES, facts, 0)

        def prepare(i, carry):
            c, t = i // 12, pl.multiple_of(lax.rem(i, 12) * 128, 128)
            k2, v2 = keys_and_values(kvf[c, pl.ds(t, 128), :])
            kc[c, pl.ds(t, 128), :] = doubled(k2.astype(BF16))
            vc[c, pl.ds(t, 128), :] = doubled(v2.astype(BF16))
            kt[c, :, pl.ds(t, 128)] = k2.T.astype(BF16)
            dk[c, pl.ds(t, 128), :] = jnp.zeros((128, 128), F32)
            dv[c, pl.ds(t, 128), :] = jnp.zeros((128, 128), F32)
            return carry

        lax.fori_loop(0, 48, prepare, 0)

        def prepare_q(i, carry):
            c, t = i // 12, pl.multiple_of(lax.rem(i, 12) * 128, 128)
            rows = pl.ds(t, 128)
            qc[c, rows, :], qn[c, rows, :] = query_quads(qf[c, rows, :])
            dc[c, rows, :], dn[c, rows, :] = query_quads(df[c, rows, :])
            lt[i] = X[c, rows, :].T
            return carry

        lax.fori_loop(0, 24, prepare_q, 0)

        keys4, e4, (qc4, qv4), (kc5, kv5) = class_facts(offs, b)
        qi4, qi5 = qc4 - 2 * b, lax.rem(kc5, 2)
        for blk in range(4):
            r = slice(128 * blk, 128 * blk + 128)
            for e in range(2):
                c, v = keys4[e]
                k2, v2 = keys_and_values(kvf[c, pl.ds(v + 384 * blk, 128, stride=3), :])
                k4[e, r, :] = doubled(k2.astype(BF16))
                v4[e, r, :] = doubled(v2.astype(BF16))
                kt4[e, :, r] = k2.T.astype(BF16)
            rows = pl.ds(qv4 + 384 * blk, 128, stride=3)
            q4[r, :], qn4[r, :] = query_quads(qf[qi4, rows, :])
            d4[r, :], dn4[r, :] = query_quads(df[qi4, rows, :])
            lt4[blk] = X[qi4, rows, :].T
            rows = pl.ds(kv5 + 384 * blk, 128, stride=3)
            k2, v2 = keys_and_values(kvf[kc5, rows, :])
            k5[r, :] = doubled(k2.astype(BF16))
            v5[r, :] = doubled(v2.astype(BF16))
            kt5[:, r] = k2.T.astype(BF16)
            q5[r, :], qn5[r, :] = query_quads(qf[qi5, rows, :])
            d5[r, :], dn5[r, :] = query_quads(df[qi5, rows, :])
            lt5[blk] = X[qi5, rows, :].T

        b1[...] = key_bias((2, 128), (4, 128), 4, 1, 2 * b, True)
        b2[...] = key_bias((1, 256), (2, 256), 4, 2, 2 * b, True)
        b3[...] = key_bias((1, 256), (1, 256), 1, 1, 0, True)
        b4[...] = key_bias((1, 256), (2, 256), 12, 6, 6 * e4, True)

        def tile(g, k, v, kT, q, q2, d, d2, facts_pair, bias, first):
            s = dot_nt(k, q)
            if bias is not None:
                s = s + bias[...]
            l0, l1 = facts_pair
            row = jnp.concatenate([l0[0:1, :], l1[0:1, :]], 1)
            delta = jnp.concatenate([l0[HD : HD + 1, :], l1[HD : HD + 1, :]], 1)
            p = jnp.exp(s - row)
            ds = p * (dot_nt(v, d) - delta)
            hi, lo = split(p)
            dv_new = dot_nn(hi, d2) + dot_nn(lo, d2)
            hi, lo = split(ds)
            dk_new = dot_nn(hi, q2) + dot_nn(lo, q2)
            dq_new = dot_nn(kT, hi) + dot_nn(kT, lo)
            dqt[g] = dq_new if first else dqt[g] + dq_new
            return dk_new, dv_new

        def q1(qb, carry):
            def at(g, blk):
                return pl.ds(pl.multiple_of(512 * g + 128 * blk, 128), 128)

            def step(kb, bias, first):
                for g in range(3):
                    ks, qs = at(g, kb), at(g, qb)
                    kT = jnp.concatenate([kt[c, :, ks] for c in range(4)], 1)
                    a, c = tile(
                        g,
                        kc[:, ks, :].reshape(512, 256),
                        vc[:, ks, :].reshape(512, 256),
                        kT,
                        qc[:, qs, :].reshape(256, 256),
                        qn[:, qs, :].reshape(256, 128),
                        dc[:, qs, :].reshape(256, 256),
                        dn[:, qs, :].reshape(256, 128),
                        (lt.at[4 * g + qb], lt.at[12 + 4 * g + qb]),
                        bias,
                        first,
                    )
                    dk[:, ks, :] += a.reshape(4, 128, 128)
                    dv[:, ks, :] += c.reshape(4, 128, 128)

            step(qb, b1, True)

            def more(kb, inner):
                step(kb, None, False)
                return inner

            lax.fori_loop(0, qb, more, 0)
            for g in range(3):
                dq[:, at(g, qb), :] = dqt[g].T.reshape(2, 128, 128)
            return carry

        lax.fori_loop(0, 4, q1, 0)

        def at256(blk):
            return pl.ds(pl.multiple_of(256 * blk, 128), 256)

        par = offs[1]

        def q2(qb, carry):
            def step(kb, bias, first):
                ks, qs = at256(kb), at256(qb)
                a, c = tile(
                    0,
                    jnp.concatenate([kc[par, ks, :], kc[par + 2, ks, :]], 0),
                    jnp.concatenate([vc[par, ks, :], vc[par + 2, ks, :]], 0),
                    jnp.concatenate([kt[par, :, ks], kt[par + 2, :, ks]], 1),
                    qc[par, qs, :],
                    qn[par, qs, :],
                    dc[par, qs, :],
                    dn[par, qs, :],
                    (lt.at[12 * par + 2 * qb], lt.at[12 * par + 2 * qb + 1]),
                    bias,
                    first,
                )
                dk[par, ks, :] += a[:256]
                dk[par + 2, ks, :] += a[256:]
                dv[par, ks, :] += c[:256]
                dv[par + 2, ks, :] += c[256:]

            step(qb, b2, True)

            def more(kb, inner):
                step(kb, None, False)
                return inner

            lax.fori_loop(jnp.where(qb >= 4, 4, 0), qb, more, 0)
            dq[par, at256(qb), :] += dqt[0].T
            return carry

        lax.fori_loop(0, TOTAL // 256, q2, 0)

        o3 = offs[2]

        @pl.when(o3 // 2 == b)
        def _():
            ci = lax.rem(o3, 2)

            def q3(qb, carry):
                def step(kb, bias, first):
                    ks, qs = at256(kb), at256(qb)
                    a, c = tile(
                        0,
                        kc[o3, ks, :],
                        vc[o3, ks, :],
                        kt[o3, :, ks],
                        qc[ci, qs, :],
                        qn[ci, qs, :],
                        dc[ci, qs, :],
                        dn[ci, qs, :],
                        (lt.at[12 * ci + 2 * qb], lt.at[12 * ci + 2 * qb + 1]),
                        bias,
                        first,
                    )
                    dk[o3, ks, :] += a
                    dv[o3, ks, :] += c

                step(qb, b3, True)

                def more(kb, inner):
                    step(kb, None, False)
                    return inner

                lax.fori_loop(0, qb, more, 0)
                dq[ci, at256(qb), :] += dqt[0].T
                return carry

            lax.fori_loop(0, TOTAL // 256, q3, 0)

        dk4[...] = jnp.zeros_like(dk4)
        dv4[...] = jnp.zeros_like(dv4)
        for qb in range(2):
            qs = slice(256 * qb, 256 * qb + 256)
            for kb in range(qb, -1, -1):
                ks = slice(256 * kb, 256 * kb + 256)
                a, c = tile(
                    qb,
                    k4[:, ks, :].reshape(512, 256),
                    v4[:, ks, :].reshape(512, 256),
                    jnp.concatenate([kt4[0, :, ks], kt4[1, :, ks]], 1),
                    q4[qs, :],
                    qn4[qs, :],
                    d4[qs, :],
                    dn4[qs, :],
                    (lt4.at[2 * qb], lt4.at[2 * qb + 1]),
                    b4 if kb == qb else None,
                    kb == qb,
                )
                dk4[:, ks, :] += a.reshape(2, 256, 128)
                dv4[:, ks, :] += c.reshape(2, 256, 128)
            dq[qi4, pl.ds(qv4 + 768 * qb, 256, stride=3), :] += dqt[qb].T
        for e in range(2):
            c, v = keys4[e]
            rows = pl.ds(v, THIRD, stride=3)
            dk[c, rows, :] += dk4[e]
            dv[c, rows, :] += dv4[e]

        @pl.when(kc5 // 2 == b)
        def _():
            dk4[0] = jnp.zeros((THIRD, 128), F32)
            dv4[0] = jnp.zeros((THIRD, 128), F32)
            for qb in range(2):
                qs = slice(256 * qb, 256 * qb + 256)
                for kb in range(qb, -1, -1):
                    ks = slice(256 * kb, 256 * kb + 256)
                    a, c = tile(
                        qb,
                        k5[ks, :],
                        v5[ks, :],
                        kt5[:, ks],
                        q5[qs, :],
                        qn5[qs, :],
                        d5[qs, :],
                        dn5[qs, :],
                        (lt5.at[2 * qb], lt5.at[2 * qb + 1]),
                        b3 if kb == qb else None,
                        kb == qb,
                    )
                    dk4[0, ks, :] += a
                    dv4[0, ks, :] += c
                dq[qi5, pl.ds(kv5 + 768 * qb, 256, stride=3), :] += dqt[qb].T
            rows = pl.ds(kv5, THIRD, stride=3)
            dk[kc5, rows, :] += dk4[0]
            dv[kc5, rows, :] += dv4[0]

        def finish(m, carry):
            ci = lax.rem(m, 2)
            rows = pl.ds(pl.multiple_of((m // 2) * ROWS, 64), ROWS)

            def kv(c):
                k, v = dk[c, rows, :], dv[c, rows, :]
                return pick(k + swap(k), v + swap(v))

            down[m, 0:ROWS, :] = kv(2 * b + ci)
            dsib[m] = kv(2 * (1 - b) + ci)
            q = dq[ci, rows, :]
            q = (q + swap(q)) * (1.0 / math.sqrt(HD))
            down[m, ROWS:PACK, :] = pick(q[:HALF], q[HALF:])
            return carry

        lax.fori_loop(0, HOMES, finish, 0)


def attention_backward(info, own, sib, dap, ap, lse):
    big = pltpu.VMEM((4, TOTAL, 256), BF16)
    state = pltpu.VMEM((2, TOTAL, 128), F32)
    quad = pltpu.VMEM((2, TOTAL, 256), BF16)
    pair = pltpu.VMEM((2, TOTAL, 128), BF16)
    quad3 = pltpu.VMEM((THIRD, 256), BF16)
    pair3 = pltpu.VMEM((THIRD, 128), BF16)
    turned = pltpu.VMEM((4, 128, 128), F32)
    full = pltpu.VMEM((4, TOTAL, 128), F32)
    return pl.pallas_call(
        backward_kernel,
        out_shape=[
            jax.ShapeDtypeStruct((HOMES, PACK, 128), F32),
            jax.ShapeDtypeStruct((HOMES, ROWS, 128), F32),
        ],
        in_specs=[SM, VM, VM, VM, VM, VM],
        out_specs=[VM, VM],
        scratch_shapes=[
            full,
            big,
            big,
            pltpu.VMEM((4, 128, TOTAL), BF16),
            state,
            quad,
            pair,
            quad,
            pair,
            state,
            pltpu.VMEM((24, 128, 128), F32),
            pltpu.VMEM((2, THIRD, 256), BF16),
            pltpu.VMEM((2, THIRD, 256), BF16),
            pltpu.VMEM((2, 128, THIRD), BF16),
            quad3,
            pair3,
            quad3,
            pair3,
            turned,
            quad3,
            quad3,
            pltpu.VMEM((128, THIRD), BF16),
            quad3,
            pair3,
            quad3,
            pair3,
            turned,
            pltpu.VMEM((3, 128, 256), F32),
            full,
            full,
            state,
            pltpu.VMEM((2, THIRD, 128), F32),
            pltpu.VMEM((2, THIRD, 128), F32),
            pltpu.VMEM((512, 256), F32),
            pltpu.VMEM((512, 256), F32),
            pltpu.VMEM((256, 256), F32),
            pltpu.VMEM((512, 256), F32),
        ],
        compiler_params=params(),
    )(info, own, sib, dap, ap, lse)


def rows_from_pairs(rec, dst):
    for j in range(HEADS // 2):
        u, v = rec[2 * j], rec[2 * j + 1]
        cols = slice(128 * j, 128 * j + 128)
        dst[0:HALF, cols] = pick(u, swap(v))
        dst[HALF:ROWS, cols] = pick(swap(u), v)


def pairs_from_rows(src, dst):
    for j in range(HEADS // 2):
        top = src[0:HALF, 128 * j : 128 * j + 128]
        bottom = src[HALF:ROWS, 128 * j : 128 * j + 128]
        dst[2 * j] = pick(top, swap(bottom))
        dst[2 * j + 1] = pick(swap(top), bottom)


def halves_sum(r):
    return r[:ROWS] + r[ROWS:]


def norm_back(f, n, rs):
    return (f - jnp.mean(f, -1, keepdims=True) - n * jnp.mean(f * n, -1, keepdims=True)) * rs


def put_turned(hi_ref, lo_ref, v):
    for j in range(D // 128):
        t = v[:, 128 * j : 128 * j + 128].T
        hi, lo = split(t)
        hi_ref[128 * j : 128 * j + 128, :] = hi
        lo_ref[128 * j : 128 * j + 128, :] = lo


FT = 512


class Spill:
    def __init__(self, tiles, sem):
        self.tiles, self.sem, self.count, self.open = tiles, sem, 0, [[], []]

    def emit(self, fill, copies):
        k = self.count % 2
        for c in self.open[k]:
            c.wait()
        fill(self.tiles.at[k])
        self.open[k] = copies(self.tiles.at[k], self.sem.at[k])
        for c in self.open[k]:
            c.start()
        self.count += 1

    def close(self):
        for k in range(2):
            for c in self.open[k]:
                c.wait()
            self.open[k] = []


def product(hi, lo, r_hi, r_lo, tile):
    def one(i, carry):
        rows = pl.ds(pl.multiple_of(i * 128, 128), 128)
        h, l = hi[rows, :], lo[rows, :]
        tile[rows, :] = dot_nn(h, r_hi[...]) + dot_nn(h, r_lo[...]) + dot_nn(l, r_hi[...])
        return carry

    lax.fori_loop(0, D // 128, one, 0)


def column_copies(G, chunk):
    def make(tile, sem):
        return [
            pltpu.make_async_copy(
                tile.at[pl.ds(24 * d, 24), :], G.at[d // 16, (d // 8) % 2, (d % 8) // 2, d % 2, chunk], sem.at[d]
            )
            for d in range(32)
        ]

    return make


def row_copies(G, part, chunk):
    def make(tile, sem):
        return [
            pltpu.make_async_copy(
                tile.at[pl.ds(24 * d, 24), :], G.at[part // 2, part % 2, d // 8, (d // 4) % 2, chunk + d % 4], sem.at[d]
            )
            for d in range(32)
        ]

    return make


def ff_kernel(rec, x_ref, g_ref, wo, wu, wd, gi, gf, gh, out_ref, dap, dy1_ref, gi_g, gf_g, gh_g, G, lhs, lhs2, V, N1, U, GP, E, ACC, th, tl, r_hi, r_lo, tiles, sem):
    spill = Spill(tiles, sem)
    rows_from_pairs(rec, V)
    na, rs_a = normed(V[...])
    V[...] = na
    put_split(lhs, na * gi[...])
    for j in range(3):
        cols = slice(256 * j, 256 * j + 256)
        N1[:, cols] = x_ref[:, cols] + halves_sum(dot_nn(lhs[...], wo[:, cols]))
    y1 = N1[...]
    out_ref[...] = y1
    ny, rs_y = normed(y1)
    N1[...] = ny
    put_split(lhs, ny * gf[...])

    def up(j, su):
        cols = pl.ds(pl.multiple_of(j * FT, FT), FT)
        z = halves_sum(dot_nn(lhs[...], wu[:, cols]))
        phi = 0.5 * (1.0 + lax.erf(z * math.sqrt(0.5)))
        u = z * phi
        U[:, cols] = u
        GP[:, cols] = phi + z * jnp.exp(-0.5 * z * z) * (1.0 / math.sqrt(2.0 * math.pi))
        return su + jnp.sum(u, -1, keepdims=True)

    zero = jnp.zeros((ROWS, 1), F32)
    mean = lax.fori_loop(0, FF // FT, up, zero) * (1.0 / FF)

    def spread(j, sv):
        cols = pl.ds(pl.multiple_of(j * FT, FT), FT)
        c = U[:, cols] - mean
        return sv + jnp.sum(c * c, -1, keepdims=True)

    rs_u = lax.rsqrt(lax.fori_loop(0, FF // FT, spread, zero) * (1.0 / FF) + LN_EPSILON)
    ACC[...] = jnp.zeros_like(ACC)

    def lower(j, carry):
        cols = pl.ds(pl.multiple_of(j * FT, FT), FT)
        n = (U[:, cols] - mean) * rs_u
        U[:, cols] = n
        put_split(lhs2, n * gh[:, cols])
        ACC[...] += halves_sum(dot_nn(lhs2[...], wd[cols, :]))
        return carry

    lax.fori_loop(0, FF // FT, lower, 0)
    out_ref[...] += ACC[...]

    put_split(lhs, g_ref[...])

    def back_down(j, sums):
        cols = pl.ds(pl.multiple_of(j * FT, FT), FT)
        e = halves_sum(dot_nt(lhs[...], wd[cols, :]))
        n = U[:, cols]
        gh_g[:, cols] = jnp.sum(e * n, 0, keepdims=True)
        f = e * gh[:, cols]
        E[:, cols] = f
        return sums[0] + jnp.sum(f, -1, keepdims=True), sums[1] + jnp.sum(f * n, -1, keepdims=True)

    sf, sfn = lax.fori_loop(0, FF // FT, back_down, (zero, zero))
    mf, mfn = sf * (1.0 / FF), sfn * (1.0 / FF)
    ACC[...] = jnp.zeros_like(ACC)

    def back_up(j, carry):
        cols = pl.ds(pl.multiple_of(j * FT, FT), FT)
        dz = (E[:, cols] - mf - U[:, cols] * mfn) * rs_u * GP[:, cols]
        E[:, cols] = dz
        put_split(lhs2, dz)
        ACC[...] += halves_sum(dot_nt(lhs2[...], wu[:, cols]))
        return carry

    lax.fori_loop(0, FF // FT, back_up, 0)
    e = ACC[...]
    ny = N1[...]
    gf_g[...] = jnp.sum(e * ny, 0, keepdims=True)
    dy1 = g_ref[...] + norm_back(e * gf[...], ny, rs_y)
    dy1_ref[...] = dy1
    put_split(lhs, dy1)
    for j in range(3):
        cols = slice(256 * j, 256 * j + 256)
        ACC[:, cols] = halves_sum(dot_nt(lhs[...], wo[cols, :]))
    e = ACC[...]
    na = V[...]
    gi_g[...] = jnp.sum(e * na, 0, keepdims=True)
    ACC[...] = norm_back(e * gi[...], na, rs_a)
    pairs_from_rows(ACC, dap)

    put_turned(th, tl, na * gi[...])
    r_hi[...], r_lo[...] = split(dy1)
    spill.emit(lambda t: product(th, tl, r_hi, r_lo, t), column_copies(G, 3))
    put_turned(th, tl, ny * gf[...])
    for j in range(4):
        r_hi[...], r_lo[...] = split(E[:, D * j : D * j + D])
        spill.emit(lambda t: product(th, tl, r_hi, r_lo, t), column_copies(G, 4 + j))
    r_hi[...], r_lo[...] = split(g_ref[...])
    for j in range(4):
        cols = slice(D * j, D * j + D)
        put_turned(th, tl, U[:, cols] * gh[:, cols])
        spill.emit(lambda t: product(th, tl, r_hi, r_lo, t), row_copies(G, j, 8))
    spill.close()


CHUNKS = 12
PIECE = 24


def grad_shape():
    return jax.ShapeDtypeStruct((2, 2, 4, 2, CHUNKS, PIECE, D), F32)


def tile_scratch():
    return [
        pltpu.VMEM((D, ROWS), BF16),
        pltpu.VMEM((D, ROWS), BF16),
        pltpu.VMEM((ROWS, D), BF16),
        pltpu.VMEM((ROWS, D), BF16),
        pltpu.VMEM((2, D, D), F32),
        pltpu.SemaphoreType.DMA((2, 32)),
    ]


def feed_forward(rec, x, g, wo, wu, wd, gi, gf, gh):
    act = jax.ShapeDtypeStruct((ROWS, D), F32)
    wide = pltpu.VMEM((ROWS, FF), F32)
    thin = pltpu.VMEM((ROWS, D), F32)
    return pl.pallas_call(
        ff_kernel,
        out_shape=[
            act,
            jax.ShapeDtypeStruct((HEADS, HALF, 128), F32),
            act,
            jax.ShapeDtypeStruct((1, D), F32),
            jax.ShapeDtypeStruct((1, D), F32),
            jax.ShapeDtypeStruct((1, FF), F32),
            grad_shape(),
        ],
        in_specs=[VM] * 9,
        out_specs=[VM] * 6 + [ANY],
        scratch_shapes=[
            pltpu.VMEM((2 * ROWS, D), BF16),
            pltpu.VMEM((2 * ROWS, FT), BF16),
            thin,
            thin,
            wide,
            wide,
            wide,
            thin,
        ]
        + tile_scratch(),
        compiler_params=params(),
    )(rec, x, g, wo, wu, wd, gi.reshape(1, D), gf.reshape(1, D), gh.reshape(1, FF))


def last_kernel(rec, x_ref, dy1_ref, w, ga, G_in, gx, ga_g, G, dqkv, lhs, th, tl, r_hi, r_lo, tiles, sem):
    spill = Spill(tiles, sem)
    for j in range(HEADS // 2):
        u, v = rec[2 * j, ROWS:PACK, :], rec[2 * j + 1, ROWS:PACK, :]
        cols = slice(128 * j, 128 * j + 128)
        dqkv[0:HALF, cols] = pick(u, swap(v))
        dqkv[HALF:ROWS, cols] = pick(swap(u), v)
        u, v = rec[2 * j, 0:ROWS, :], rec[2 * j + 1, 0:ROWS, :]
        dqkv[:, D + 128 * j : D + 128 * j + 128] = pick(u, swap(v))
        dqkv[:, 2 * D + 128 * j : 2 * D + 128 * j + 128] = pick(swap(u), v)
    n, rs = normed(x_ref[...])
    put_turned(th, tl, n * ga[...])
    e = None
    for j in range(3):
        cols = slice(D * j, D * j + D)
        part = dqkv[:, cols]
        hi, lo = split(part)
        r_hi[...], r_lo[...] = hi, lo
        lhs[0:ROWS, :], lhs[ROWS : 2 * ROWS, :] = hi, lo
        spill.emit(lambda t: product(th, tl, r_hi, r_lo, t), column_copies(G, j))
        more = halves_sum(dot_nt(lhs[...], w[:, cols]))
        e = more if e is None else e + more
    ga_g[...] = jnp.sum(e * n, 0, keepdims=True)
    gx[...] = dy1_ref[...] + norm_back(e * ga[...], n, rs)
    spill.close()


def last(rec, x, dy1, w, ga, G):
    return pl.pallas_call(
        last_kernel,
        out_shape=[
            jax.ShapeDtypeStruct((ROWS, D), F32),
            jax.ShapeDtypeStruct((1, D), F32),
            grad_shape(),
        ],
        in_specs=[VM] * 5 + [ANY],
        out_specs=[VM, VM, ANY],
        scratch_shapes=[pltpu.VMEM((ROWS, 3 * D), F32), pltpu.VMEM((2 * ROWS, D), BF16)] + tile_scratch(),
        input_output_aliases={5: 2},
        compiler_params=params(),
    )(rec, x, dy1, w, ga.reshape(1, D), G)


SMALL = 256


def reduce_kernel(G, S, out, s_out, own, c0, c1a, c1b, c2, zl, zr, sown, d0, d1, d2, dl, dr, osem, sc, rc, s1, r1, s2, r2, sl, rl, sr, rr):
    p, s = lax.axis_index("pat"), lax.axis_index("seq")
    x, core, z, y = p // 2, lax.rem(p, 2), s // 2, lax.rem(s, 2)
    peer = to(x * 2 + 1 - core, s)
    xn = to((1 - x) * 2 + core, s)
    yn = to(p, z * 2 + 1 - y)
    left, right = to(p, s - 2), to(p, s + 2)
    barrier = pltpu.get_barrier_semaphore()
    for d in (peer, xn, yn):
        pl.semaphore_signal(barrier, inc=1, device_id=d, device_id_type=MESH)

    @pl.when(z > 0)
    def _():
        pl.semaphore_signal(barrier, inc=1, device_id=left, device_id_type=MESH)

    @pl.when(z < 3)
    def _():
        pl.semaphore_signal(barrier, inc=1, device_id=right, device_id_type=MESH)

    pl.semaphore_wait(barrier, 3 + (z > 0).astype(jnp.int32) + (z < 3).astype(jnp.int32))

    def remote(src, dst, a, b, d):
        return pltpu.make_async_remote_copy(
            src_ref=src, dst_ref=dst, send_sem=a, recv_sem=b, device_id=d, device_id_type=MESH
        )

    class Chunk:
        def __init__(self, k, group, slot, o, b0, b1, b2, bl, br, put, x_first):
            self.k, self.group, self.slot, self.o = k, group, slot, o
            self.b0, self.b1, self.b2, self.bl, self.br = b0, b1, b2, bl, br
            self.put, self.x_first = put, x_first

        def core(self):
            k = self.k
            return [
                remote(self.group(i, 1 - core), self.b0.at[i], sc.at[k, i], rc.at[k, i], peer) for i in range(2)
            ]

        def load(self):
            return [
                pltpu.make_async_copy(self.group(i, core), self.o.at[i], osem.at[self.slot, i]) for i in range(2)
            ]

        def one(self):
            k = self.k
            if self.x_first:
                return remote(self.b0.at[1 - x], self.b1, s1.at[k], r1.at[k], xn)
            return remote(self.b0.at[:, :, 1 - y], self.b1, s1.at[k], r1.at[k], yn)

        def two(self):
            k = self.k
            if self.x_first:
                return remote(self.b1.at[:, 1 - y], self.b2, s2.at[k], r2.at[k], yn)
            return remote(self.b1.at[1 - x], self.b2, s2.at[k], r2.at[k], xn)

        def rightward(self, i):
            k, part = self.k, pl.ds(i + 1, 3 - i)
            src = self.b2 if i == 0 else self.bl
            return remote(src.at[part], self.bl.at[part], sr.at[k], rl.at[k], right)

        def leftward(self, i):
            k, part = self.k, pl.ds(0, i)
            src = self.b2 if i == 3 else self.br
            return remote(src.at[part], self.br.at[part], sl.at[k], rr.at[k], left)

        def stage1(self):
            for c in self.load() + self.core():
                if hasattr(c, "wait_recv") and c.is_remote:
                    c.wait_recv()
                else:
                    c.wait()
            self.b0[...] += self.o[...]
            self.one().start()

        def stage2(self):
            self.one().wait_recv()
            mine = self.b0[x] if self.x_first else self.b0[:, :, y]
            self.b1[...] += mine
            self.two().start()

        def stage3(self):
            self.two().wait_recv()
            mine = self.b1[:, y] if self.x_first else self.b1[x]
            self.b2[...] += mine

            @pl.when(z == 0)
            def _():
                self.rightward(0).start()

            @pl.when(z == 3)
            def _():
                self.leftward(3).start()

        def stage4(self):
            @pl.when(z == 1)
            def _():
                self.rightward(0).wait_recv()
                self.bl[2:4] += self.b2[2:4]
                self.rightward(1).start()

            @pl.when(z == 2)
            def _():
                self.leftward(3).wait_recv()
                self.br[0:2] += self.b2[0:2]
                self.leftward(2).start()

        def stage5(self):
            @pl.when(z == 2)
            def _():
                self.rightward(1).wait_recv()
                self.bl[3:4] += self.b2[3:4]
                self.rightward(2).start()

            @pl.when(z == 1)
            def _():
                self.leftward(2).wait_recv()
                self.br[0:1] += self.b2[0:1]
                self.leftward(1).start()

        def stage6(self):
            @pl.when(z == 3)
            def _():
                self.rightward(2).wait_recv()
                self.put(self.b2[3] + self.bl[3])

            @pl.when(z == 0)
            def _():
                self.leftward(1).wait_recv()
                self.put(self.b2[0] + self.br[0])

            @pl.when(z == 1)
            def _():
                self.put(self.b2[1] + self.bl[1] + self.br[1])

            @pl.when(z == 2)
            def _():
                self.put(self.b2[2] + self.bl[2] + self.br[2])

        def sent(self):
            for c in self.core() + [self.one(), self.two()]:
                c.wait_send()
            for i in range(4):

                @pl.when(z == i)
                def _(i=i):
                    if i < 3:
                        self.rightward(i).wait_send()
                    if i > 0:
                        self.leftward(i).wait_send()

    def chunk(k, x_first):
        def put(v):
            out[k] = v

        return Chunk(
            k,
            lambda i, c: G.at[i, c, :, :, k],
            lax.rem(k, 2),
            own.at[lax.rem(k, 2)],
            c0.at[k],
            (c1a if x_first else c1b).at[k // 2],
            c2.at[k],
            zl.at[k],
            zr.at[k],
            put,
            x_first,
        )

    def put_small(v):
        s_out[...] = v

    small = Chunk(CHUNKS, lambda i, c: S.at[i, c], 2, sown, d0, d1, d2, dl, dr, put_small, True)

    for c in small.core() + small.load():
        c.start()

    def begin(k, carry):
        for c in chunk(k, True).core():
            c.start()
        return carry

    lax.fori_loop(0, CHUNKS, begin, 0)
    for c in chunk(jnp.int32(0), True).load():
        c.start()

    def step(tau, carry):
        for stage in range(6, 0, -1):
            k = tau - stage

            @pl.when(tau == stage)
            def _(stage=stage):
                getattr(small, f"stage{stage}")()

            for parity in range(2):

                @pl.when(jnp.logical_and(jnp.logical_and(k >= 0, k < CHUNKS), lax.rem(k + 2, 2) == parity))
                def _(k=k, stage=stage, parity=parity):
                    here = chunk(k, parity == 0)
                    if stage == 1:

                        @pl.when(k + 1 < CHUNKS)
                        def _():
                            for c in chunk(k + 1, True).load():
                                c.start()

                    getattr(here, f"stage{stage}")()

        return carry

    lax.fori_loop(1, CHUNKS + 6, step, 0)

    def close(k, carry):
        for parity in range(2):

            @pl.when(lax.rem(k, 2) == parity)
            def _(parity=parity):
                chunk(k, parity == 0).sent()

        return carry

    lax.fori_loop(0, CHUNKS, close, 0)
    small.sent()


def reduce_scatter(G, S, cid):
    dma = pltpu.SemaphoreType.DMA
    n = CHUNKS

    def buf(*lead):
        return pltpu.VMEM(lead + (PIECE, D), F32)

    def tiny(*lead):
        return pltpu.VMEM(lead + (8, SMALL), F32)

    return pl.pallas_call(
        reduce_kernel,
        out_shape=[
            jax.ShapeDtypeStruct((n, PIECE, D), F32),
            jax.ShapeDtypeStruct((8, SMALL), F32),
        ],
        in_specs=[ANY, ANY],
        out_specs=[VM, VM],
        scratch_shapes=[
            buf(2, 2, 4, 2),
            buf(n, 2, 4, 2),
            buf(n // 2, 4, 2),
            buf(n // 2, 2, 4),
            buf(n, 4),
            buf(n, 4),
            buf(n, 4),
            tiny(2, 4, 2),
            tiny(2, 4, 2),
            tiny(4, 2),
            tiny(4),
            tiny(4),
            tiny(4),
            dma((3, 2)),
            dma((n + 1, 2)),
            dma((n + 1, 2)),
        ]
        + [dma((n + 1,)) for _ in range(8)],
        compiler_params=params(collective_id=cid, has_side_effects=True),
    )(G, S)


SEG1, SEG2, SEG3, SEG4, SEG5 = SEGMENTS
DILATION_ONE, DILATION_TWO, DILATION_THREE, DILATION_FOUR, DILATION_FIVE = DILATIONS
MASK_VALUE = -1e30
MATMUL_ACCURACY = lax.Precision.HIGHEST


def passed_along(value, axis, by):
    length = lax.axis_size(axis)
    pairs = [(i, i + by) for i in range(length) if 0 <= i + by < length]
    return lax.ppermute(value, axis, pairs)


def layer_norm(x, gain_vec):
    average = jnp.mean(x, -1, keepdims=True)
    centred = x - average
    variance = jnp.mean(centred * centred, -1, keepdims=True)
    return centred * lax.rsqrt(variance + LN_EPSILON) * gain_vec


def select_table(offsets_row, dilation_rate):
    return (jnp.arange(dilation_rate, dtype=jnp.int32)[:, None] == offsets_row[None, :]).astype(
        jnp.float32
    )


def spread_apart(x, select_option, dilation_rate):
    shaped = x.reshape(x.shape[0] // dilation_rate, dilation_rate, x.shape[1], x.shape[2])
    return jnp.einsum("trhd,rh->thd", shaped, select_option, precision=MATMUL_ACCURACY)


def spread_scalar_rows(x, select_option, dilation_rate):
    shaped = x.reshape(x.shape[0] // dilation_rate, dilation_rate, x.shape[1])
    return jnp.einsum("trh,rh->th", shaped, select_option, precision=MATMUL_ACCURACY)


def spread_rows(x, select_option):
    return jnp.einsum("thd,rh->trhd", x, select_option, precision=MATMUL_ACCURACY).reshape(
        -1, x.shape[1], x.shape[2]
    )


def spread_scalars(x, select_option):
    return jnp.einsum("th,rh->trh", x, select_option, precision=MATMUL_ACCURACY).reshape(
        -1, x.shape[1]
    )


def masked_score_matrix(sparse_queries, key_portion, query_position, key_position, segment_length):
    score_matrix = jnp.einsum(
        "ozt,bzt->zob", sparse_queries, key_portion, precision=MATMUL_ACCURACY
    ) * (1.0 / math.sqrt(key_portion.shape[-1]))
    q_cols = query_position.T[:, :, None]
    k_cols = key_position.T[:, None, :]
    permitted_mask = (k_cols <= q_cols) & (k_cols // segment_length == q_cols // segment_length)
    return (jnp.where(permitted_mask, score_matrix, MASK_VALUE), permitted_mask)


def prepare_pattern(
    query_sequence, key_sequence, value_sequence, offsets_row, dilation_rate, anchor_point
):
    select_option = select_table(offsets_row, dilation_rate)
    sparse_queries = spread_apart(query_sequence, select_option, dilation_rate)
    sparse_key_value = jnp.stack(
        (
            spread_apart(key_sequence, select_option, dilation_rate),
            spread_apart(value_sequence, select_option, dilation_rate),
        )
    )
    query_position = (
        anchor_point
        + jnp.arange(sparse_queries.shape[0], dtype=jnp.int32)[:, None] * dilation_rate
        + offsets_row[None, :]
    )
    return (select_option, sparse_queries, sparse_key_value, query_position)


def fetch_far(kv_list, reaches):
    remote_entry_lists = [[] for entry in kv_list]
    for pattern_spec in range(len(kv_list)):
        for distance in range(1, reaches[pattern_spec] + 1):
            remote_entry_lists[pattern_spec].append(
                passed_along(kv_list[pattern_spec], "seq", distance)
            )
    return remote_entry_lists


def return_grads(local_list, part_lists, reaches):
    totals = list(local_list)
    for pattern_spec in range(len(local_list)):
        for distance in range(1, reaches[pattern_spec] + 1):
            totals[pattern_spec] = totals[pattern_spec] + passed_along(
                part_lists[pattern_spec][distance - 1], "seq", -distance
            )
    return totals


def pattern_forward_pass(
    sparse_queries,
    sparse_key_value,
    query_position,
    remote_entries,
    segment_length,
    anchor_point,
    sequence_width,
):
    masked_logits, permitted_mask = masked_score_matrix(
        sparse_queries, sparse_key_value[0], query_position, query_position, segment_length
    )
    row_max = jnp.max(masked_logits, -1)
    softmax_weights = jnp.where(permitted_mask, jnp.exp(masked_logits - row_max[..., None]), 0.0)
    state = (
        row_max,
        jnp.sum(softmax_weights, -1),
        jnp.einsum("tlj,jtb->tlb", softmax_weights, sparse_key_value[1], precision=MATMUL_ACCURACY),
    )
    for distance in range(1, len(remote_entries) + 1):
        remote_key_value = remote_entries[distance - 1]
        key_position = query_position - distance * sequence_width
        is_live = (
            anchor_point - (distance - 1) * sequence_width - 1
        ) // segment_length == anchor_point // segment_length

        def update(state_in, remote_key_value=remote_key_value, key_position=key_position):
            old_max, old_sum, old_acc = state_in
            masked_remote, permitted_remote = masked_score_matrix(
                sparse_queries, remote_key_value[0], query_position, key_position, segment_length
            )
            new_max = jnp.maximum(old_max, jnp.max(masked_remote, -1))
            weights_far = jnp.where(
                permitted_remote, jnp.exp(masked_remote - new_max[..., None]), 0.0
            )
            factor = jnp.exp(old_max - new_max)
            added = jnp.einsum(
                "tlj,jtb->tlb", weights_far, remote_key_value[1], precision=MATMUL_ACCURACY
            )
            return (
                new_max,
                old_sum * factor + jnp.sum(weights_far, -1),
                old_acc * factor[..., None] + added,
            )

        def unchanged(state_in):
            return state_in

        state = lax.cond(is_live, update, unchanged, state)
    row_max, row_sum, accumulated = state
    mixture = jnp.transpose(accumulated / row_sum[..., None], (1, 0, 2))
    log_sum = (row_max + jnp.log(row_sum)).T
    return (mixture, log_sum)


def merge_patterns(forwards, prepared_inputs):
    full_lse = []
    full_mix = []
    for pattern_spec in range(len(forwards)):
        mixture, log_sum = forwards[pattern_spec]
        select_option = prepared_inputs[pattern_spec][0]
        covered = spread_scalars(jnp.ones_like(log_sum), select_option)
        full_lse.append(spread_scalars(log_sum, select_option) + (covered - 1.0) * 1e30)
        full_mix.append(spread_rows(mixture, select_option))
    stacked = jnp.stack(full_lse)
    row_max = jnp.max(stacked, 0)
    softmax_weights = jnp.exp(stacked - row_max)
    row_sum = jnp.sum(softmax_weights, 0)
    attended = full_mix[0] * softmax_weights[0][..., None]
    for pattern_spec in range(1, len(full_mix)):
        attended = attended + full_mix[pattern_spec] * softmax_weights[pattern_spec][..., None]
    return (attended / row_sum[..., None], row_max + jnp.log(row_sum))


def pattern_backward(
    select_option,
    dilation_rate,
    segment_length,
    anchor_point,
    sparse_queries,
    sparse_key_value,
    query_position,
    remote_entries,
    reach,
    sequence_gradient,
    row_difference,
    combined_logsumexp,
):
    sequence_width = sequence_gradient.shape[0]
    sparse_gradient = spread_apart(sequence_gradient, select_option, dilation_rate)
    sparse_output_grad = spread_scalar_rows(row_difference, select_option, dilation_rate).T
    sparse_logsumexp = spread_scalar_rows(combined_logsumexp, select_option, dilation_rate).T
    inverse_square_root = 1.0 / math.sqrt(sparse_queries.shape[-1])

    def portion_gradients(key_portion, value_portion, key_position):
        masked_logits, permitted_mask = masked_score_matrix(
            sparse_queries, key_portion, query_position, key_position, segment_length
        )
        softmax_weights = jnp.where(
            permitted_mask, jnp.exp(masked_logits - sparse_logsumexp[..., None]), 0.0
        )
        value_gradient = jnp.einsum(
            "tui,utx->itx", softmax_weights, sparse_gradient, precision=MATMUL_ACCURACY
        )
        pattern_gradient = jnp.einsum(
            "ozt,bzt->zob", sparse_gradient, value_portion, precision=MATMUL_ACCURACY
        )
        score_gradient = (
            softmax_weights
            * (pattern_gradient - sparse_output_grad[..., None])
            * inverse_square_root
        )
        query_gradient = jnp.einsum(
            "hqk,khd->qhd", score_gradient, key_portion, precision=MATMUL_ACCURACY
        )
        key_gradient = jnp.einsum(
            "tui,utx->itx", score_gradient, sparse_queries, precision=MATMUL_ACCURACY
        )
        return (query_gradient, jnp.stack((key_gradient, value_gradient)))

    query_gradient, key_value_gradient = portion_gradients(
        sparse_key_value[0], sparse_key_value[1], query_position
    )
    part_list = []
    for distance in range(1, reach + 1):
        remote_key_value = remote_entries[distance - 1]
        is_live = (
            anchor_point - (distance - 1) * sequence_width - 1
        ) // segment_length == anchor_point // segment_length
        key_position = query_position - distance * sequence_width

        def far_grads(remote_key_value=remote_key_value, key_position=key_position):
            return portion_gradients(remote_key_value[0], remote_key_value[1], key_position)

        def no_grads():
            return (jnp.zeros_like(query_gradient), jnp.zeros_like(key_value_gradient))

        part_q, part_kv = lax.cond(is_live, far_grads, no_grads)
        query_gradient = query_gradient + part_q
        part_list.append(part_kv)
    return (query_gradient, key_value_gradient, part_list)


def front_part(own_rows, w_qkv, gain_attn):
    return jnp.dot(layer_norm(own_rows, gain_attn), w_qkv, precision=MATMUL_ACCURACY)


def after_part(attn_rows, own_rows, w_out, w_up, w_down, gain_inner, gain_ffn, gain_hidden):
    residual = own_rows + jnp.dot(
        layer_norm(attn_rows, gain_inner), w_out, precision=MATMUL_ACCURACY
    )
    hidden = jax.nn.gelu(
        jnp.dot(layer_norm(residual, gain_ffn), w_up, precision=MATMUL_ACCURACY), approximate=False
    )
    return residual + jnp.dot(layer_norm(hidden, gain_hidden), w_down, precision=MATMUL_ACCURACY)


def shards(
    tokens,
    w_qkv,
    w_out,
    w_up,
    w_down,
    gain_attn,
    gain_inner,
    gain_ffn,
    gain_hidden,
    offsets,
    grad_out,
):
    w_qkv = w_qkv.astype(jnp.float32)
    w_out = w_out.astype(jnp.float32)
    w_up = w_up.astype(jnp.float32)
    w_down = w_down.astype(jnp.float32)
    groups = lax.axis_size("pat")
    local_rows = tokens.shape[0]
    sequence_width = local_rows * groups
    heads_here = HEADS // groups
    own_rows = tokens.reshape(local_rows, D)
    qkv_rows, front_back = jax.vjp(front_part, own_rows, w_qkv, gain_attn)
    gathered_qkv = lax.all_to_all(
        qkv_rows.reshape(local_rows, 1, 3, HEADS, HD),
        "pat",
        split_axis=3,
        concat_axis=1,
        tiled=True,
    )
    gathered_qkv = gathered_qkv.reshape(sequence_width, 3, heads_here, HD)
    head_offsets = lax.dynamic_slice_in_dim(
        offsets, lax.axis_index("pat") * heads_here, heads_here, 1
    )
    anchor_point = lax.axis_index("seq") * sequence_width
    dilation_rates = (DILATION_ONE, DILATION_TWO, DILATION_THREE, DILATION_FOUR, DILATION_FIVE)
    segment_lengths = (SEG1, SEG2, SEG3, SEG4, SEG5)
    reaches = [
        min((segment_lengths[pattern_spec] - 2) // sequence_width + 1, lax.axis_size("seq") - 1)
        for pattern_spec in range(PATTERNS)
    ]
    prepared_inputs = []
    for pattern_spec in range(PATTERNS):
        prepared_inputs.append(
            prepare_pattern(
                gathered_qkv[:, 0],
                gathered_qkv[:, 1],
                gathered_qkv[:, 2],
                head_offsets[pattern_spec],
                dilation_rates[pattern_spec],
                anchor_point,
            )
        )
    remote_entry_lists = fetch_far([entry[2] for entry in prepared_inputs], reaches)
    forwards = []
    for pattern_spec in range(PATTERNS):
        select_option, sparse_queries, sparse_key_value, query_position = prepared_inputs[
            pattern_spec
        ]
        forwards.append(
            pattern_forward_pass(
                sparse_queries,
                sparse_key_value,
                query_position,
                remote_entry_lists[pattern_spec],
                segment_lengths[pattern_spec],
                anchor_point,
                sequence_width,
            )
        )
    lse_sums = jnp.stack([jnp.sum(entry[1]) for entry in forwards])
    totals = lax.psum(lse_sums, ("pat", "seq"))
    full_length = sequence_width * lax.axis_size("seq")
    counts = jnp.array(
        [
            float(full_length // dilation_rates[pattern_spec] * HEADS)
            for pattern_spec in range(PATTERNS)
        ],
        jnp.float32,
    )
    log_means = totals / counts
    attended, combined_logsumexp = merge_patterns(forwards, prepared_inputs)
    returned_rows = lax.all_to_all(
        attended.reshape(local_rows, groups, heads_here, HD),
        "pat",
        split_axis=1,
        concat_axis=2,
        tiled=True,
    )
    attn_rows = returned_rows.reshape(local_rows, D)
    result, after_back = jax.vjp(
        after_part, attn_rows, own_rows, w_out, w_up, w_down, gain_inner, gain_ffn, gain_hidden
    )
    g_attn, g_resid, g_out, g_up, g_down, g_inner, g_ffn, g_hidden = after_back(
        grad_out.reshape(local_rows, D)
    )
    sequence_gradient = lax.all_to_all(
        g_attn.reshape(local_rows, 1, HEADS, HD), "pat", split_axis=2, concat_axis=1, tiled=True
    )
    sequence_gradient = sequence_gradient.reshape(sequence_width, heads_here, HD)
    row_difference = jnp.sum(sequence_gradient * attended, -1)
    q_grads = []
    kv_locals = []
    kv_parts = []
    for pattern_spec in range(PATTERNS):
        select_option, sparse_queries, sparse_key_value, query_position = prepared_inputs[
            pattern_spec
        ]
        part_q, local_kv, part_list = pattern_backward(
            select_option,
            dilation_rates[pattern_spec],
            segment_lengths[pattern_spec],
            anchor_point,
            sparse_queries,
            sparse_key_value,
            query_position,
            remote_entry_lists[pattern_spec],
            reaches[pattern_spec],
            sequence_gradient,
            row_difference,
            combined_logsumexp,
        )
        q_grads.append(part_q)
        kv_locals.append(local_kv)
        kv_parts.append(part_list)
    kv_grads = return_grads(kv_locals, kv_parts, reaches)
    grad_total = jnp.zeros((sequence_width, 3, heads_here, HD), jnp.float32)
    for pattern_spec in range(PATTERNS):
        select_option = prepared_inputs[pattern_spec][0]
        grad_total = grad_total + jnp.stack(
            (
                spread_rows(q_grads[pattern_spec], select_option),
                spread_rows(kv_grads[pattern_spec][0], select_option),
                spread_rows(kv_grads[pattern_spec][1], select_option),
            ),
            1,
        )
    grad_back = lax.all_to_all(
        grad_total.reshape(local_rows, groups, 3, heads_here, HD),
        "pat",
        split_axis=1,
        concat_axis=3,
        tiled=True,
    )
    g_tokens, g_qkv, g_attn_gain = front_back(grad_back.reshape(local_rows, 3 * D))
    grad_tokens = (g_resid + g_tokens).reshape(local_rows, 1, D)
    summed = (
        lax.psum_scatter(g_qkv, ("pat", "seq"), scatter_dimension=0, tiled=True),
        lax.psum_scatter(g_out, ("pat", "seq"), scatter_dimension=0, tiled=True),
        lax.psum_scatter(g_up, ("pat", "seq"), scatter_dimension=0, tiled=True),
        lax.psum_scatter(g_down, ("pat", "seq"), scatter_dimension=0, tiled=True),
        lax.psum_scatter(g_attn_gain, ("pat", "seq"), scatter_dimension=0, tiled=True),
        lax.psum_scatter(g_inner, ("pat", "seq"), scatter_dimension=0, tiled=True),
        lax.psum_scatter(g_ffn, ("pat", "seq"), scatter_dimension=0, tiled=True),
        lax.psum_scatter(g_hidden, ("pat", "seq"), scatter_dimension=0, tiled=True),
    )
    return (
        result.reshape(local_rows, 1, D),
        grad_tokens,
        summed[0],
        summed[1],
        summed[2],
        summed[3],
        summed[4],
        summed[5],
        summed[6],
        summed[7],
        log_means,
    )


def fast_shards(tokens, w_qkv, w_out, w_up, w_down, gain_attn, gain_inner, gain_ffn, gain_hidden, offsets, grad_out):
    x = tokens.reshape(ROWS, D)
    g = grad_out.reshape(ROWS, D)
    p, s = lax.axis_index("pat"), lax.axis_index("seq")
    active, head = head_here(p, s)
    mine = lax.dynamic_slice_in_dim(offsets, head, 1, 1)[:, 0]
    info = jnp.concatenate([jnp.stack([active.astype(jnp.int32), lax.rem(p, 2).astype(jnp.int32)]), mine])

    own, sib = to_heads(front(x, w_qkv, gain_attn), True, 0)
    ap, lse, sums = attention_forward(info, own, sib)
    rec = to_homes(ap, 1)
    mixed, dap, dy1, gi_g, gf_g, gh_g, G = feed_forward(
        rec, x, g, w_out, w_up, w_down, gain_inner, gain_ffn, gain_hidden
    )
    (drec,) = to_heads(dap, False, 2)
    down, dsib = attention_backward(info, own, sib, drec, ap, lse)
    grec = grads_to_homes(down, dsib, 3)
    gx, ga_g, G = last(grec, x, dy1, w_qkv, gain_attn, G)
    n = 4 * RUNS
    small = jnp.concatenate(
        [
            ga_g.reshape(n, -1),
            gi_g.reshape(n, -1),
            gf_g.reshape(n, -1),
            gh_g.reshape(n, -1),
            jnp.broadcast_to(sums[:PATTERNS, 0][None, :], (n, PATTERNS)),
        ],
        1,
    )
    small = jnp.pad(small, ((0, 0), (0, SMALL - small.shape[1])))
    S = jnp.broadcast_to(small[:, None, :], (n, 8, SMALL)).reshape(2, 2, 4, 2, 8, SMALL)
    out, s_out = reduce_scatter(G, S, 4)
    row = s_out[0]
    k = D // n
    counts = jnp.array([float(TOTAL * 4 // r * HEADS) for r in DILATIONS], F32)
    return (
        mixed.reshape(ROWS, 1, D),
        gx.reshape(ROWS, 1, D),
        jnp.concatenate([out[j] for j in range(3)], 1),
        out[3],
        jnp.concatenate([out[j] for j in range(4, 8)], 1),
        out[8:12].reshape(4 * PIECE, D),
        row[:k],
        row[k : 2 * k],
        row[2 * k : 3 * k],
        row[3 * k : 7 * k],
        row[7 * k : 7 * k + PATTERNS] / counts,
    )


def fits(mesh):
    return mesh.shape["pat"] == 4 and mesh.shape["seq"] == RUNS


def solution(mesh):
    rows = P("seq", "pat", None)
    split_rows = P(("pat", "seq"), None)
    split_one = P(("pat", "seq"))
    planned = jax.shard_map(
        fast_shards,
        mesh=mesh,
        in_specs=(rows,) + (P(),) * 9 + (rows,),
        out_specs=(rows, rows) + (split_rows,) * 4 + (split_one,) * 4 + (P(),),
        check_vma=False,
    )
    general = jax.shard_map(
        shards,
        mesh=mesh,
        in_specs=(rows,) + (P(),) * 9 + (rows,),
        out_specs=(rows, rows) + (split_rows,) * 4 + (split_one,) * 4 + (P(),),
        check_vma=False,
    )

    def layer(tokens, *rest):
        if fits(mesh) and tokens.shape[0] == TOTAL:
            return planned(tokens, *rest)
        return general(tokens, *rest)

    return layer
```

```python
import functools
import math

import jax
import jax.numpy as jnp
from jax import lax
from jax.experimental import pallas as pl
from jax.experimental.pallas import tpu as pltpu
from jax.sharding import PartitionSpec as P

D = 768
HEADS = 12
HD = 64
FF = 3072
PATTERNS = 5
SEGMENTS = (2048, 4096, 8192, 16384, 32768)
DILATIONS = (1, 2, 4, 6, 12)
LN_EPSILON = 1e-05
NEG = -1e30
F32 = jnp.float32
BF16 = jnp.bfloat16
HIGHEST = lax.Precision.HIGHEST
VMEM_LIMIT = 58 * 1024 * 1024

ROWS = 192
HALF = ROWS // 2
RUNS = 8
TOTAL = ROWS * RUNS
PACK = ROWS + HALF
HOMES = 16
THIRD = TOTAL // 3
MESH = pl.DeviceIdType.MESH


def dot_nn(a, b):
    return lax.dot_general(a, b, (((1,), (0,)), ((), ())), preferred_element_type=F32)


def dot_nt(a, b):
    return lax.dot_general(a, b, (((1,), (1,)), ((), ())), preferred_element_type=F32)


def split(v):
    hi = v.astype(BF16)
    return hi, (v - hi.astype(F32)).astype(BF16)


def split32(v):
    hi = v.astype(BF16).astype(F32)
    return hi, v - hi


def lower_lanes(v):
    return lax.broadcasted_iota(jnp.int32, v.shape, v.ndim - 1) < HD


def swap(v):
    return pltpu.roll(v, HD, v.ndim - 1)


def pick(a, b):
    return jnp.where(lower_lanes(a), a, b)


def head_place(h):
    z = h // 3
    column = lax.rem(lax.rem(h, 3) + z + 1, 4)
    return column // 2, z * 2 + lax.rem(column, 2)


def head_here(p, s):
    z = s // 2
    column = (p // 2) * 2 + lax.rem(s, 2)
    k = lax.rem(column - z + 7, 4)
    return k < 3, z * 3 + jnp.minimum(k, 2)


def whole(*_):
    return pl.BlockSpec(memory_space=pltpu.VMEM)


VM = pl.BlockSpec(memory_space=pltpu.VMEM)
ANY = pl.BlockSpec(memory_space=pl.ANY)
SM = pl.BlockSpec(memory_space=pltpu.SMEM)


def params(**kw):
    return pltpu.CompilerParams(vmem_limit_bytes=VMEM_LIMIT, **kw)


def normed(v):
    centred = v - jnp.mean(v, -1, keepdims=True)
    rs = lax.rsqrt(jnp.mean(centred * centred, -1, keepdims=True) + LN_EPSILON)
    return centred * rs, rs


def put_split(ref, v):
    hi, lo = split(v)
    n = v.shape[0]
    ref[0:n, :] = hi
    ref[n : 2 * n, :] = lo


def front_kernel(x_ref, w_ref, gain_ref, pk_ref, lhs):
    n, _ = normed(x_ref[...])
    put_split(lhs, n * gain_ref[...])
    for jj in range(3):
        parts = []
        for kind in range(3):
            c0 = kind * D + 256 * jj
            r = dot_nn(lhs[...], w_ref[:, c0 : c0 + 256])
            parts.append(r[:ROWS] + r[ROWS:])
        for half in range(2):
            q, k, v = (a[:, 128 * half : 128 * half + 128] for a in parts)
            h = 4 * jj + 2 * half
            pk_ref[h, 0:ROWS, :] = pick(k, swap(v))
            pk_ref[h + 1, 0:ROWS, :] = pick(swap(k), v)
            top, bottom = q[:HALF], q[HALF:]
            pk_ref[h, ROWS:PACK, :] = pick(top, swap(bottom))
            pk_ref[h + 1, ROWS:PACK, :] = pick(swap(top), bottom)


def front(x, w, gain):
    return pl.pallas_call(
        front_kernel,
        out_shape=jax.ShapeDtypeStruct((HEADS, PACK, 128), F32),
        in_specs=[VM] * 3,
        out_specs=VM,
        scratch_shapes=[pltpu.VMEM((2 * ROWS, D), BF16)],
        compiler_params=params(),
    )(x, w, gain.reshape(1, D))


def place_facts():
    p, s = lax.axis_index("pat"), lax.axis_index("seq")
    x, core = p // 2, lax.rem(p, 2)
    active, head = head_here(p, s)
    return p, s, x, core, active, head


def home_device(core, m):
    return core * 2 + lax.rem(m, 2), m // 2


def head_device(h, b):
    hx, hs = head_place(h)
    return hx * 2 + b, hs


def same(p, s, q, t):
    return jnp.logical_and(p == q, s == t)


def to(p, s):
    return {"pat": p, "seq": s}


def scatter_kernel(forward, pk, own, *rest):
    if forward:
        sib, send, recv, fsend, frecv = rest
    else:
        send, recv = rest
    p, s, x, core, active, head = place_facts()
    slot = s * 2 + core
    barrier = pltpu.get_barrier_semaphore()

    @pl.when(active)
    def _():
        def greet(m, carry):
            q, t = home_device(core, m)

            @pl.when(jnp.logical_not(same(p, s, q, t)))
            def _():
                pl.semaphore_signal(barrier, inc=1, device_id=to(q, t), device_id_type=MESH)

            return carry

        lax.fori_loop(0, HOMES, greet, 0)
        if forward:
            pl.semaphore_signal(barrier, inc=1, device_id=to(x * 2 + 1 - core, s), device_id_type=MESH)

    mine = jnp.logical_and(active, core == x)
    waits = HEADS - mine.astype(jnp.int32)
    if forward:
        waits = waits + active.astype(jnp.int32)
    pl.semaphore_wait(barrier, waits)

    def copy(h):
        q, t = head_device(h, x)
        return q, t, pltpu.make_async_remote_copy(
            src_ref=pk.at[h],
            dst_ref=own.at[slot],
            send_sem=send.at[h],
            recv_sem=recv.at[slot],
            device_id=to(q, t),
            device_id_type=MESH,
        )

    def start(j, carry):
        h = lax.rem(j + 3 * (s // 2) + 2 * p, HEADS)
        q, t, remote = copy(h)

        @pl.when(same(p, s, q, t))
        def _():
            pltpu.make_async_copy(pk.at[h], own.at[slot], recv.at[slot]).start()

        @pl.when(jnp.logical_not(same(p, s, q, t)))
        def _():
            remote.start()

        return carry

    lax.fori_loop(0, HEADS, start, 0)

    def passed(m):
        return pltpu.make_async_remote_copy(
            src_ref=own.at[m, pl.ds(0, ROWS), :],
            dst_ref=sib.at[m],
            send_sem=fsend.at[m],
            recv_sem=frecv.at[m],
            device_id=to(x * 2 + 1 - core, s),
            device_id_type=MESH,
        )

    @pl.when(active)
    def _():
        def arrive(m, carry):
            pltpu.make_async_copy(own.at[m], own.at[m], recv.at[m]).wait()
            if forward:
                passed(m).start()
            return carry

        lax.fori_loop(0, HOMES, arrive, 0)
        if forward:

            def finish(m, carry):
                passed(m).wait()
                return carry

            lax.fori_loop(0, HOMES, finish, 0)

    def sent(h, carry):
        q, t, remote = copy(h)

        @pl.when(jnp.logical_not(same(p, s, q, t)))
        def _():
            remote.wait_send()

        return carry

    lax.fori_loop(0, HEADS, sent, 0)


def to_heads(packets, forward, cid):
    rows = packets.shape[1]
    shapes = [jax.ShapeDtypeStruct((HOMES, rows, 128), F32)]
    sems = [pltpu.SemaphoreType.DMA((HEADS,)), pltpu.SemaphoreType.DMA((HOMES,))]
    if forward:
        shapes.append(jax.ShapeDtypeStruct((HOMES, ROWS, 128), F32))
        sems += [pltpu.SemaphoreType.DMA((HOMES,)), pltpu.SemaphoreType.DMA((HOMES,))]
    return pl.pallas_call(
        functools.partial(scatter_kernel, forward),
        out_shape=shapes,
        in_specs=[ANY],
        out_specs=[ANY] * len(shapes),
        scratch_shapes=sems,
        compiler_params=params(collective_id=cid, has_side_effects=True),
    )(packets)


def home_barrier(p, s, x, core, active, barrier, also_sibling):
    def greet(h, carry):
        q, t = head_device(h, x)

        @pl.when(jnp.logical_not(same(p, s, q, t)))
        def _():
            pl.semaphore_signal(barrier, inc=1, device_id=to(q, t), device_id_type=MESH)

        return carry

    lax.fori_loop(0, HEADS, greet, 0)

    @pl.when(active)
    def _():
        if also_sibling:
            pl.semaphore_signal(barrier, inc=1, device_id=to(x * 2 + 1 - core, s), device_id_type=MESH)
        mine = (core == x).astype(jnp.int32)
        pl.semaphore_wait(barrier, HOMES - mine + (1 if also_sibling else 0))


def gather_kernel(pk, rec, send, recv):
    p, s, x, core, active, head = place_facts()
    barrier = pltpu.get_barrier_semaphore()
    home_barrier(p, s, x, core, active, barrier, False)

    def copy(m):
        q, t = home_device(core, m)
        return q, t, pltpu.make_async_remote_copy(
            src_ref=pk.at[m],
            dst_ref=rec.at[head],
            send_sem=send.at[m],
            recv_sem=recv.at[head],
            device_id=to(q, t),
            device_id_type=MESH,
        )

    @pl.when(active)
    def _():
        def start(j, carry):
            m = lax.rem(j + 2 * s + 1, HOMES)
            q, t, remote = copy(m)

            @pl.when(same(p, s, q, t))
            def _():
                pltpu.make_async_copy(pk.at[m], rec.at[head], recv.at[head]).start()

            @pl.when(jnp.logical_not(same(p, s, q, t)))
            def _():
                remote.start()

            return carry

        lax.fori_loop(0, HOMES, start, 0)

    def arrive(h, carry):
        pltpu.make_async_copy(rec.at[h], rec.at[h], recv.at[h]).wait()
        return carry

    lax.fori_loop(0, HEADS, arrive, 0)

    @pl.when(active)
    def _():
        def sent(m, carry):
            q, t, remote = copy(m)

            @pl.when(jnp.logical_not(same(p, s, q, t)))
            def _():
                remote.wait_send()

            return carry

        lax.fori_loop(0, HOMES, sent, 0)


def to_homes(packets, cid):
    rows = packets.shape[1]
    return pl.pallas_call(
        gather_kernel,
        out_shape=jax.ShapeDtypeStruct((HEADS, rows, 128), F32),
        in_specs=[ANY],
        out_specs=ANY,
        scratch_shapes=[pltpu.SemaphoreType.DMA((HOMES,)), pltpu.SemaphoreType.DMA((HEADS,))],
        compiler_params=params(collective_id=cid, has_side_effects=True),
    )(packets)


def grads_kernel(own, sib, rec, came, total, send, recv, qsend, qrecv, fsend, frecv):
    p, s, x, core, active, head = place_facts()
    barrier = pltpu.get_barrier_semaphore()
    home_barrier(p, s, x, core, active, barrier, True)
    here = slice(0, ROWS)

    def passed(m):
        return pltpu.make_async_remote_copy(
            src_ref=sib.at[m],
            dst_ref=came.at[m],
            send_sem=fsend.at[m],
            recv_sem=frecv.at[m],
            device_id=to(x * 2 + 1 - core, s),
            device_id_type=MESH,
        )

    def copies(m):
        q, t = home_device(core, m)
        kv = pltpu.make_async_remote_copy(
            src_ref=total.at[m],
            dst_ref=rec.at[head, pl.ds(0, ROWS), :],
            send_sem=send.at[m],
            recv_sem=recv.at[head],
            device_id=to(q, t),
            device_id_type=MESH,
        )
        dq = pltpu.make_async_remote_copy(
            src_ref=own.at[m, pl.ds(ROWS, HALF), :],
            dst_ref=rec.at[head, pl.ds(ROWS, HALF), :],
            send_sem=qsend.at[m],
            recv_sem=qrecv.at[head],
            device_id=to(q, t),
            device_id_type=MESH,
        )
        return q, t, kv, dq

    @pl.when(active)
    def _():
        def start(m, carry):
            passed(m).start()
            return carry

        lax.fori_loop(0, HOMES, start, 0)

        def add(m, carry):
            q, t, kv, dq = copies(m)
            passed(m).wait_recv()
            total[m] = own[m, here, :] + came[m]

            @pl.when(same(p, s, q, t))
            def _():
                pltpu.make_async_copy(
                    own.at[m, pl.ds(ROWS, HALF), :], rec.at[head, pl.ds(ROWS, HALF), :], qrecv.at[head]
                ).start()
                pltpu.make_async_copy(total.at[m], rec.at[head, pl.ds(0, ROWS), :], recv.at[head]).start()

            @pl.when(jnp.logical_not(same(p, s, q, t)))
            def _():
                dq.start()
                kv.start()

            return carry

        lax.fori_loop(0, HOMES, add, 0)

    def arrive(h, carry):
        a = rec.at[h, pl.ds(0, ROWS), :]
        b = rec.at[h, pl.ds(ROWS, HALF), :]
        pltpu.make_async_copy(a, a, recv.at[h]).wait()
        pltpu.make_async_copy(b, b, qrecv.at[h]).wait()
        return carry

    lax.fori_loop(0, HEADS, arrive, 0)

    @pl.when(active)
    def _():
        def sent(m, carry):
            q, t, kv, dq = copies(m)
            passed(m).wait_send()

            @pl.when(jnp.logical_not(same(p, s, q, t)))
            def _():
                dq.wait_send()
                kv.wait_send()

            return carry

        lax.fori_loop(0, HOMES, sent, 0)


def grads_to_homes(own, sib, cid):
    dma = pltpu.SemaphoreType.DMA
    return pl.pallas_call(
        grads_kernel,
        out_shape=jax.ShapeDtypeStruct((HEADS, PACK, 128), F32),
        in_specs=[VM, VM],
        out_specs=ANY,
        scratch_shapes=[
            pltpu.VMEM((HOMES, ROWS, 128), F32),
            pltpu.VMEM((HOMES, ROWS, 128), F32),
            dma((HOMES,)),
            dma((HEADS,)),
            dma((HOMES,)),
            dma((HEADS,)),
            dma((HOMES,)),
            dma((HOMES,)),
        ],
        compiler_params=params(collective_id=cid, has_side_effects=True),
    )(own, sib)


def tile_positions(rows, columns, row_classes, column_classes, t_step, class_step):
    r = lax.broadcasted_iota(jnp.int32, (rows, columns), 0)
    q = lax.broadcasted_iota(jnp.int32, (rows, columns), 1)
    rn, qn = rows // row_classes, columns // column_classes
    return (r % rn) * t_step + (r // rn) * class_step, (q % qn) * t_step + (q // qn) * class_step


def key_bias(q_shape, k_shape, t_step, class_step, shift, keys_first):
    nq, nk = q_shape[0] * q_shape[1], k_shape[0] * k_shape[1]
    if keys_first:
        kp, qp = tile_positions(nk, nq, k_shape[0], q_shape[0], t_step, class_step)
    else:
        qp, kp = tile_positions(nq, nk, q_shape[0], k_shape[0], t_step, class_step)
    return jnp.where(kp - qp <= shift, 0.0, NEG).astype(F32)


def unpack_keys(own, sib, b, kvf):
    def one(m, carry):
        c = 2 * b + lax.rem(m, 2)
        d = 2 * (1 - b) + lax.rem(m, 2)
        t = pl.multiple_of((m // 2) * ROWS, 64)
        kvf[c, pl.ds(t, ROWS), :] = own[m, 0:ROWS, :]
        kvf[d, pl.ds(t, ROWS), :] = sib[m]
        return carry

    lax.fori_loop(0, HOMES, one, 0)


def unpack_pairs(src, first, dst, scale):
    def one(m, carry):
        t = pl.multiple_of((m // 2) * ROWS, 32)
        v = src[m, first : first + HALF, :] * scale
        w = swap(v)
        dst[lax.rem(m, 2), pl.ds(t, HALF), :] = pick(v, w)
        dst[lax.rem(m, 2), pl.ds(t + HALF, HALF), :] = pick(w, v)
        return carry

    lax.fori_loop(0, HOMES, one, 0)


def keys_and_values(kv):
    hi, lo = split32(kv)
    k2 = pick(hi, swap(lo))
    v2 = pick(swap(hi), lo)
    return k2, v2


def doubled(v):
    return jnp.concatenate([v, v], 1)


def query_quads(qq):
    hi, lo = split32(qq)
    return jnp.concatenate([hi.astype(BF16), lo.astype(BF16)], 1), pick(hi, lo).astype(BF16)


def class_facts(o, b):
    o4, o5 = o[3], o[4]
    k4 = ((lax.rem(o4, 4), o4 // 4), (lax.rem(o4 + 6, 4), (o4 + 6) // 4))
    first = (k4[0][0] // 2) == b
    e4 = jnp.where(first, 0, 1)
    q4 = (jnp.where(first, k4[0][0], k4[1][0]), jnp.where(first, k4[0][1], k4[1][1]))
    k5 = (lax.rem(o5, 4), o5 // 4)
    return k4, e4, q4, k5


def forward_kernel(info, own, sib, ap, lse, sums, kvf, kc, vc, qf, qc, k4, v4, q4, k5, v5, q5, acc, mx, A, L, M, b1, b2, b3, b4):
    active = info[0] == 1
    b = info[1]
    offs = [info[2 + i] for i in range(PATTERNS)]
    sums[...] = jnp.zeros_like(sums)

    @pl.when(active)
    def _():
        ones = jnp.ones((128, 128), BF16)
        unpack_keys(own, sib, b, kvf)
        unpack_pairs(own, ROWS, qf, 1.0 / math.sqrt(HD))

        def prepare(i, carry):
            c, t = i // 12, pl.multiple_of(lax.rem(i, 12) * 128, 128)
            k2, v2 = keys_and_values(kvf[c, pl.ds(t, 128), :])
            kc[c, pl.ds(t, 128), :] = doubled(k2.astype(BF16))
            vc[c, pl.ds(t, 128), :] = jnp.concatenate([v2.astype(BF16), ones], 1)
            return carry

        lax.fori_loop(0, 48, prepare, 0)

        def prepare_q(i, carry):
            c, t = i // 12, pl.multiple_of(lax.rem(i, 12) * 128, 128)
            qc[c, pl.ds(t, 128), :] = query_quads(qf[c, pl.ds(t, 128), :])[0]
            return carry

        lax.fori_loop(0, 24, prepare_q, 0)

        keys4, e4, (qc4, qv4), (kc5, kv5) = class_facts(offs, b)
        for blk in range(4):
            r = slice(128 * blk, 128 * blk + 128)
            for e in range(2):
                c, v = keys4[e]
                k2, v2 = keys_and_values(kvf[c, pl.ds(v + 384 * blk, 128, stride=3), :])
                k4[e, r, :] = doubled(k2.astype(BF16))
                v4[e, r, :] = jnp.concatenate([v2.astype(BF16), ones], 1)
            q4[r, :] = query_quads(qf[qc4 - 2 * b, pl.ds(qv4 + 384 * blk, 128, stride=3), :])[0]
            k2, v2 = keys_and_values(kvf[kc5, pl.ds(kv5 + 384 * blk, 128, stride=3), :])
            k5[r, :] = doubled(k2.astype(BF16))
            v5[r, :] = jnp.concatenate([v2.astype(BF16), ones], 1)
            q5[r, :] = query_quads(qf[lax.rem(kc5, 2), pl.ds(kv5 + 384 * blk, 128, stride=3), :])[0]

        b1[...] = key_bias((2, 128), (4, 128), 4, 1, 2 * b, False)
        b2[...] = key_bias((1, 256), (2, 256), 4, 2, 2 * b, False)
        b3[...] = key_bias((1, 256), (1, 256), 1, 1, 0, False)
        b4[...] = key_bias((1, 256), (2, 256), 12, 6, 6 * e4, False)

        def tile(g, q, k, v, bias, first):
            s = dot_nt(q, k)
            if bias is not None:
                s = s + bias[...]
            top = jnp.max(s, -1, keepdims=True)
            n = k.shape[0] // 128
            if first:
                m = jnp.broadcast_to(top, (256, 128))
            else:
                old = mx[g]
                m = jnp.maximum(old, top)
            mx[g] = m
            p = jnp.exp(s - jnp.concatenate([m] * n, 1))
            hi, lo = split(p)
            new = dot_nn(hi, v) + dot_nn(lo, v)
            if first:
                acc[g] = new
            else:
                alpha = jnp.exp(old - m)
                acc[g] = acc[g] * doubled(alpha) + new

        def note(pattern, g):
            rows = mx[g] + jnp.log(acc[g][:, 128:])
            sums[pattern : pattern + 1, :] += jnp.sum(rows, 0, keepdims=True)

        def q1(qb, carry):
            def at(g, blk):
                return pl.ds(pl.multiple_of(512 * g + 128 * blk, 128), 128)

            def load_q(g):
                return qc[:, at(g, qb), :].reshape(256, 256)

            def step(kb, bias, first):
                for g in range(3):
                    k = kc[:, at(g, kb), :].reshape(512, 256)
                    v = vc[:, at(g, kb), :].reshape(512, 256)
                    tile(g, load_q(g), k, v, bias, first)

            step(qb, b1, True)

            def more(kb, inner):
                step(kb, None, False)
                return inner

            lax.fori_loop(0, qb, more, 0)
            for g in range(3):
                note(0, g)
                A[:, at(g, qb), :] = acc[g][:, :128].reshape(2, 128, 128)
                L[:, at(g, qb), :] = acc[g][:, 128:].reshape(2, 128, 128)
                M[:, at(g, qb), :] = mx[g].reshape(2, 128, 128)
            return carry

        lax.fori_loop(0, 4, q1, 0)

        def merge(g, ci, rows):
            m0, m1 = M[ci, rows, :], mx[g]
            m = jnp.maximum(m0, m1)
            w0, w1 = jnp.exp(m0 - m), jnp.exp(m1 - m)
            A[ci, rows, :] = A[ci, rows, :] * w0 + acc[g][:, :128] * w1
            L[ci, rows, :] = L[ci, rows, :] * w0 + acc[g][:, 128:] * w1
            M[ci, rows, :] = m

        def at256(blk):
            return pl.ds(pl.multiple_of(256 * blk, 128), 256)

        par = offs[1]

        def keys2(ref, blk):
            return jnp.concatenate([ref[par, at256(blk), :], ref[par + 2, at256(blk), :]], 0)

        def q2(qb, carry):
            q = qc[par, at256(qb), :]
            tile(0, q, keys2(kc, qb), keys2(vc, qb), b2, True)

            def more(kb, inner):
                tile(0, q, keys2(kc, kb), keys2(vc, kb), None, False)
                return inner

            lax.fori_loop(jnp.where(qb >= 4, 4, 0), qb, more, 0)
            note(1, 0)
            merge(0, par, at256(qb))
            return carry

        lax.fori_loop(0, TOTAL // 256, q2, 0)

        o3 = offs[2]

        @pl.when(o3 // 2 == b)
        def _():
            ci = lax.rem(o3, 2)

            def q3(qb, carry):
                q = qc[ci, at256(qb), :]
                tile(0, q, kc[o3, at256(qb), :], vc[o3, at256(qb), :], b3, True)

                def more(kb, inner):
                    tile(0, q, kc[o3, at256(kb), :], vc[o3, at256(kb), :], None, False)
                    return inner

                lax.fori_loop(0, qb, more, 0)
                note(2, 0)
                merge(0, ci, at256(qb))
                return carry

            lax.fori_loop(0, TOTAL // 256, q3, 0)

        for qb in range(2):
            q = q4[256 * qb : 256 * qb + 256, :]
            for kb in range(qb, -1, -1):
                ks = slice(256 * kb, 256 * kb + 256)
                k = k4[:, ks, :].reshape(512, 256)
                v = v4[:, ks, :].reshape(512, 256)
                tile(qb, q, k, v, b4 if kb == qb else None, kb == qb)
            note(3, qb)
            merge(qb, qc4 - 2 * b, pl.ds(qv4 + 768 * qb, 256, stride=3))

        @pl.when(kc5 // 2 == b)
        def _():
            for qb in range(2):
                q = q5[256 * qb : 256 * qb + 256, :]
                for kb in range(qb, -1, -1):
                    ks = slice(256 * kb, 256 * kb + 256)
                    tile(qb, q, k5[ks, :], v5[ks, :], b3 if kb == qb else None, kb == qb)
                note(4, qb)
                merge(qb, lax.rem(kc5, 2), pl.ds(kv5 + 768 * qb, 256, stride=3))

        def finish(m, carry):
            ci = lax.rem(m, 2)
            t = pl.multiple_of((m // 2) * ROWS, 64)
            rows = pl.ds(t, ROWS)
            a, l = A[ci, rows, :], L[ci, rows, :]
            out = (a + swap(a)) / l
            ap[m] = pick(out[:HALF], out[HALF:])
            lse[ci, rows, :] = M[ci, rows, :] + jnp.log(l)
            return carry

        lax.fori_loop(0, HOMES, finish, 0)


def attention_forward(info, own, sib):
    big = pltpu.VMEM((4, TOTAL, 256), BF16)
    state = pltpu.VMEM((2, TOTAL, 128), F32)
    return pl.pallas_call(
        forward_kernel,
        out_shape=[
            jax.ShapeDtypeStruct((HOMES, HALF, 128), F32),
            jax.ShapeDtypeStruct((2, TOTAL, 128), F32),
            jax.ShapeDtypeStruct((8, 128), F32),
        ],
        in_specs=[SM, VM, VM],
        out_specs=[VM, VM, VM],
        scratch_shapes=[
            pltpu.VMEM((4, TOTAL, 128), F32),
            big,
            big,
            state,
            pltpu.VMEM((2, TOTAL, 256), BF16),
            pltpu.VMEM((2, THIRD, 256), BF16),
            pltpu.VMEM((2, THIRD, 256), BF16),
            pltpu.VMEM((THIRD, 256), BF16),
            pltpu.VMEM((THIRD, 256), BF16),
            pltpu.VMEM((THIRD, 256), BF16),
            pltpu.VMEM((THIRD, 256), BF16),
            pltpu.VMEM((3, 256, 256), F32),
            pltpu.VMEM((3, 256, 128), F32),
            state,
            state,
            state,
            pltpu.VMEM((256, 512), F32),
            pltpu.VMEM((256, 512), F32),
            pltpu.VMEM((256, 256), F32),
            pltpu.VMEM((256, 512), F32),
        ],
        compiler_params=params(),
    )(info, own, sib)


def backward_kernel(info, own, sib, dap, ap, lse, down, dsib, kvf, kc, vc, kt, qf, qc, qn, dc, dn, X, lt, k4, v4, kt4, q4, qn4, d4, dn4, lt4, k5, v5, kt5, q5, qn5, d5, dn5, lt5, dqt, dk, dv, dq, dk4, dv4, b1, b2, b3, b4):
    active = info[0] == 1
    b = info[1]
    offs = [info[2 + i] for i in range(PATTERNS)]
    df = dq

    @pl.when(active)
    def _():
        unpack_keys(own, sib, b, kvf)
        unpack_pairs(own, ROWS, qf, 1.0 / math.sqrt(HD))
        unpack_pairs(dap, 0, df, 1.0)

        def facts(m, carry):
            ci = lax.rem(m, 2)
            t = pl.multiple_of((m // 2) * ROWS, 32)
            prod = dap[m] * ap[m]
            low = lower_lanes(prod)
            d0 = jnp.sum(jnp.where(low, prod, 0.0), -1, keepdims=True)
            d1 = jnp.sum(jnp.where(low, 0.0, prod), -1, keepdims=True)
            for part, d in ((0, d0), (1, d1)):
                rows = pl.ds(t + HALF * part, HALF)
                l = lse[ci, rows, :]
                X[ci, rows, :] = jnp.where(low, l, jnp.broadcast_to(d, l.shape))
            return carry

        lax.fori_loop(0, HOMES, facts, 0)

        def prepare(i, carry):
            c, t = i // 12, pl.multiple_of(lax.rem(i, 12) * 128, 128)
            k2, v2 = keys_and_values(kvf[c, pl.ds(t, 128), :])
            kc[c, pl.ds(t, 128), :] = doubled(k2.astype(BF16))
            vc[c, pl.ds(t, 128), :] = doubled(v2.astype(BF16))
            kt[c, :, pl.ds(t, 128)] = k2.T.astype(BF16)
            dk[c, pl.ds(t, 128), :] = jnp.zeros((128, 128), F32)
            dv[c, pl.ds(t, 128), :] = jnp.zeros((128, 128), F32)
            return carry

        lax.fori_loop(0, 48, prepare, 0)

        def prepare_q(i, carry):
            c, t = i // 12, pl.multiple_of(lax.rem(i, 12) * 128, 128)
            rows = pl.ds(t, 128)
            qc[c, rows, :], qn[c, rows, :] = query_quads(qf[c, rows, :])
            dc[c, rows, :], dn[c, rows, :] = query_quads(df[c, rows, :])
            lt[i] = X[c, rows, :].T
            return carry

        lax.fori_loop(0, 24, prepare_q, 0)

        keys4, e4, (qc4, qv4), (kc5, kv5) = class_facts(offs, b)
        qi4, qi5 = qc4 - 2 * b, lax.rem(kc5, 2)
        for blk in range(4):
            r = slice(128 * blk, 128 * blk + 128)
            for e in range(2):
                c, v = keys4[e]
                k2, v2 = keys_and_values(kvf[c, pl.ds(v + 384 * blk, 128, stride=3), :])
                k4[e, r, :] = doubled(k2.astype(BF16))
                v4[e, r, :] = doubled(v2.astype(BF16))
                kt4[e, :, r] = k2.T.astype(BF16)
            rows = pl.ds(qv4 + 384 * blk, 128, stride=3)
            q4[r, :], qn4[r, :] = query_quads(qf[qi4, rows, :])
            d4[r, :], dn4[r, :] = query_quads(df[qi4, rows, :])
            lt4[blk] = X[qi4, rows, :].T
            rows = pl.ds(kv5 + 384 * blk, 128, stride=3)
            k2, v2 = keys_and_values(kvf[kc5, rows, :])
            k5[r, :] = doubled(k2.astype(BF16))
            v5[r, :] = doubled(v2.astype(BF16))
            kt5[:, r] = k2.T.astype(BF16)
            q5[r, :], qn5[r, :] = query_quads(qf[qi5, rows, :])
            d5[r, :], dn5[r, :] = query_quads(df[qi5, rows, :])
            lt5[blk] = X[qi5, rows, :].T

        b1[...] = key_bias((2, 128), (4, 128), 4, 1, 2 * b, True)
        b2[...] = key_bias((1, 256), (2, 256), 4, 2, 2 * b, True)
        b3[...] = key_bias((1, 256), (1, 256), 1, 1, 0, True)
        b4[...] = key_bias((1, 256), (2, 256), 12, 6, 6 * e4, True)

        def tile(g, k, v, kT, q, q2, d, d2, facts_pair, bias, first):
            s = dot_nt(k, q)
            if bias is not None:
                s = s + bias[...]
            l0, l1 = facts_pair
            row = jnp.concatenate([l0[0:1, :], l1[0:1, :]], 1)
            delta = jnp.concatenate([l0[HD : HD + 1, :], l1[HD : HD + 1, :]], 1)
            p = jnp.exp(s - row)
            ds = p * (dot_nt(v, d) - delta)
            hi, lo = split(p)
            dv_new = dot_nn(hi, d2) + dot_nn(lo, d2)
            hi, lo = split(ds)
            dk_new = dot_nn(hi, q2) + dot_nn(lo, q2)
            dq_new = dot_nn(kT, hi) + dot_nn(kT, lo)
            dqt[g] = dq_new if first else dqt[g] + dq_new
            return dk_new, dv_new

        def q1(qb, carry):
            def at(g, blk):
                return pl.ds(pl.multiple_of(512 * g + 128 * blk, 128), 128)

            def step(kb, bias, first):
                for g in range(3):
                    ks, qs = at(g, kb), at(g, qb)
                    kT = jnp.concatenate([kt[c, :, ks] for c in range(4)], 1)
                    a, c = tile(
                        g,
                        kc[:, ks, :].reshape(512, 256),
                        vc[:, ks, :].reshape(512, 256),
                        kT,
                        qc[:, qs, :].reshape(256, 256),
                        qn[:, qs, :].reshape(256, 128),
                        dc[:, qs, :].reshape(256, 256),
                        dn[:, qs, :].reshape(256, 128),
                        (lt.at[4 * g + qb], lt.at[12 + 4 * g + qb]),
                        bias,
                        first,
                    )
                    dk[:, ks, :] += a.reshape(4, 128, 128)
                    dv[:, ks, :] += c.reshape(4, 128, 128)

            step(qb, b1, True)

            def more(kb, inner):
                step(kb, None, False)
                return inner

            lax.fori_loop(0, qb, more, 0)
            for g in range(3):
                dq[:, at(g, qb), :] = dqt[g].T.reshape(2, 128, 128)
            return carry

        lax.fori_loop(0, 4, q1, 0)

        def at256(blk):
            return pl.ds(pl.multiple_of(256 * blk, 128), 256)

        par = offs[1]

        def q2(qb, carry):
            def step(kb, bias, first):
                ks, qs = at256(kb), at256(qb)
                a, c = tile(
                    0,
                    jnp.concatenate([kc[par, ks, :], kc[par + 2, ks, :]], 0),
                    jnp.concatenate([vc[par, ks, :], vc[par + 2, ks, :]], 0),
                    jnp.concatenate([kt[par, :, ks], kt[par + 2, :, ks]], 1),
                    qc[par, qs, :],
                    qn[par, qs, :],
                    dc[par, qs, :],
                    dn[par, qs, :],
                    (lt.at[12 * par + 2 * qb], lt.at[12 * par + 2 * qb + 1]),
                    bias,
                    first,
                )
                dk[par, ks, :] += a[:256]
                dk[par + 2, ks, :] += a[256:]
                dv[par, ks, :] += c[:256]
                dv[par + 2, ks, :] += c[256:]

            step(qb, b2, True)

            def more(kb, inner):
                step(kb, None, False)
                return inner

            lax.fori_loop(jnp.where(qb >= 4, 4, 0), qb, more, 0)
            dq[par, at256(qb), :] += dqt[0].T
            return carry

        lax.fori_loop(0, TOTAL // 256, q2, 0)

        o3 = offs[2]

        @pl.when(o3 // 2 == b)
        def _():
            ci = lax.rem(o3, 2)

            def q3(qb, carry):
                def step(kb, bias, first):
                    ks, qs = at256(kb), at256(qb)
                    a, c = tile(
                        0,
                        kc[o3, ks, :],
                        vc[o3, ks, :],
                        kt[o3, :, ks],
                        qc[ci, qs, :],
                        qn[ci, qs, :],
                        dc[ci, qs, :],
                        dn[ci, qs, :],
                        (lt.at[12 * ci + 2 * qb], lt.at[12 * ci + 2 * qb + 1]),
                        bias,
                        first,
                    )
                    dk[o3, ks, :] += a
                    dv[o3, ks, :] += c

                step(qb, b3, True)

                def more(kb, inner):
                    step(kb, None, False)
                    return inner

                lax.fori_loop(0, qb, more, 0)
                dq[ci, at256(qb), :] += dqt[0].T
                return carry

            lax.fori_loop(0, TOTAL // 256, q3, 0)

        dk4[...] = jnp.zeros_like(dk4)
        dv4[...] = jnp.zeros_like(dv4)
        for qb in range(2):
            qs = slice(256 * qb, 256 * qb + 256)
            for kb in range(qb, -1, -1):
                ks = slice(256 * kb, 256 * kb + 256)
                a, c = tile(
                    qb,
                    k4[:, ks, :].reshape(512, 256),
                    v4[:, ks, :].reshape(512, 256),
                    jnp.concatenate([kt4[0, :, ks], kt4[1, :, ks]], 1),
                    q4[qs, :],
                    qn4[qs, :],
                    d4[qs, :],
                    dn4[qs, :],
                    (lt4.at[2 * qb], lt4.at[2 * qb + 1]),
                    b4 if kb == qb else None,
                    kb == qb,
                )
                dk4[:, ks, :] += a.reshape(2, 256, 128)
                dv4[:, ks, :] += c.reshape(2, 256, 128)
            dq[qi4, pl.ds(qv4 + 768 * qb, 256, stride=3), :] += dqt[qb].T
        for e in range(2):
            c, v = keys4[e]
            rows = pl.ds(v, THIRD, stride=3)
            dk[c, rows, :] += dk4[e]
            dv[c, rows, :] += dv4[e]

        @pl.when(kc5 // 2 == b)
        def _():
            dk4[0] = jnp.zeros((THIRD, 128), F32)
            dv4[0] = jnp.zeros((THIRD, 128), F32)
            for qb in range(2):
                qs = slice(256 * qb, 256 * qb + 256)
                for kb in range(qb, -1, -1):
                    ks = slice(256 * kb, 256 * kb + 256)
                    a, c = tile(
                        qb,
                        k5[ks, :],
                        v5[ks, :],
                        kt5[:, ks],
                        q5[qs, :],
                        qn5[qs, :],
                        d5[qs, :],
                        dn5[qs, :],
                        (lt5.at[2 * qb], lt5.at[2 * qb + 1]),
                        b3 if kb == qb else None,
                        kb == qb,
                    )
                    dk4[0, ks, :] += a
                    dv4[0, ks, :] += c
                dq[qi5, pl.ds(kv5 + 768 * qb, 256, stride=3), :] += dqt[qb].T
            rows = pl.ds(kv5, THIRD, stride=3)
            dk[kc5, rows, :] += dk4[0]
            dv[kc5, rows, :] += dv4[0]

        def finish(m, carry):
            ci = lax.rem(m, 2)
            rows = pl.ds(pl.multiple_of((m // 2) * ROWS, 64), ROWS)

            def kv(c):
                k, v = dk[c, rows, :], dv[c, rows, :]
                return pick(k + swap(k), v + swap(v))

            down[m, 0:ROWS, :] = kv(2 * b + ci)
            dsib[m] = kv(2 * (1 - b) + ci)
            q = dq[ci, rows, :]
            q = (q + swap(q)) * (1.0 / math.sqrt(HD))
            down[m, ROWS:PACK, :] = pick(q[:HALF], q[HALF:])
            return carry

        lax.fori_loop(0, HOMES, finish, 0)


def attention_backward(info, own, sib, dap, ap, lse):
    big = pltpu.VMEM((4, TOTAL, 256), BF16)
    state = pltpu.VMEM((2, TOTAL, 128), F32)
    quad = pltpu.VMEM((2, TOTAL, 256), BF16)
    pair = pltpu.VMEM((2, TOTAL, 128), BF16)
    quad3 = pltpu.VMEM((THIRD, 256), BF16)
    pair3 = pltpu.VMEM((THIRD, 128), BF16)
    turned = pltpu.VMEM((4, 128, 128), F32)
    full = pltpu.VMEM((4, TOTAL, 128), F32)
    return pl.pallas_call(
        backward_kernel,
        out_shape=[
            jax.ShapeDtypeStruct((HOMES, PACK, 128), F32),
            jax.ShapeDtypeStruct((HOMES, ROWS, 128), F32),
        ],
        in_specs=[SM, VM, VM, VM, VM, VM],
        out_specs=[VM, VM],
        scratch_shapes=[
            full,
            big,
            big,
            pltpu.VMEM((4, 128, TOTAL), BF16),
            state,
            quad,
            pair,
            quad,
            pair,
            state,
            pltpu.VMEM((24, 128, 128), F32),
            pltpu.VMEM((2, THIRD, 256), BF16),
            pltpu.VMEM((2, THIRD, 256), BF16),
            pltpu.VMEM((2, 128, THIRD), BF16),
            quad3,
            pair3,
            quad3,
            pair3,
            turned,
            quad3,
            quad3,
            pltpu.VMEM((128, THIRD), BF16),
            quad3,
            pair3,
            quad3,
            pair3,
            turned,
            pltpu.VMEM((3, 128, 256), F32),
            full,
            full,
            state,
            pltpu.VMEM((2, THIRD, 128), F32),
            pltpu.VMEM((2, THIRD, 128), F32),
            pltpu.VMEM((512, 256), F32),
            pltpu.VMEM((512, 256), F32),
            pltpu.VMEM((256, 256), F32),
            pltpu.VMEM((512, 256), F32),
        ],
        compiler_params=params(),
    )(info, own, sib, dap, ap, lse)


def rows_from_pairs(rec, dst):
    for j in range(HEADS // 2):
        u, v = rec[2 * j], rec[2 * j + 1]
        cols = slice(128 * j, 128 * j + 128)
        dst[0:HALF, cols] = pick(u, swap(v))
        dst[HALF:ROWS, cols] = pick(swap(u), v)


def pairs_from_rows(src, dst):
    for j in range(HEADS // 2):
        top = src[0:HALF, 128 * j : 128 * j + 128]
        bottom = src[HALF:ROWS, 128 * j : 128 * j + 128]
        dst[2 * j] = pick(top, swap(bottom))
        dst[2 * j + 1] = pick(swap(top), bottom)


def halves_sum(r):
    return r[:ROWS] + r[ROWS:]


def norm_back(f, n, rs):
    return (f - jnp.mean(f, -1, keepdims=True) - n * jnp.mean(f * n, -1, keepdims=True)) * rs


def put_turned(hi_ref, lo_ref, v):
    for j in range(D // 128):
        t = v[:, 128 * j : 128 * j + 128].T
        hi, lo = split(t)
        hi_ref[128 * j : 128 * j + 128, :] = hi
        lo_ref[128 * j : 128 * j + 128, :] = lo


FT = 512


class Spill:
    def __init__(self, tiles, sem):
        self.tiles, self.sem, self.count, self.open = tiles, sem, 0, [[], []]

    def emit(self, fill, copies):
        k = self.count % 2
        for c in self.open[k]:
            c.wait()
        fill(self.tiles.at[k])
        self.open[k] = copies(self.tiles.at[k], self.sem.at[k])
        for c in self.open[k]:
            c.start()
        self.count += 1

    def close(self):
        for k in range(2):
            for c in self.open[k]:
                c.wait()
            self.open[k] = []


def product(hi, lo, r_hi, r_lo, tile):
    def one(i, carry):
        rows = pl.ds(pl.multiple_of(i * 128, 128), 128)
        h, l = hi[rows, :], lo[rows, :]
        tile[rows, :] = dot_nn(h, r_hi[...]) + dot_nn(h, r_lo[...]) + dot_nn(l, r_hi[...])
        return carry

    lax.fori_loop(0, D // 128, one, 0)


def column_copies(G, chunk):
    def make(tile, sem):
        return [
            pltpu.make_async_copy(
                tile.at[pl.ds(24 * d, 24), :], G.at[d // 16, (d // 8) % 2, (d % 8) // 2, d % 2, chunk], sem.at[d]
            )
            for d in range(32)
        ]

    return make


def row_copies(G, part, chunk):
    def make(tile, sem):
        return [
            pltpu.make_async_copy(
                tile.at[pl.ds(24 * d, 24), :], G.at[part // 2, part % 2, d // 8, (d // 4) % 2, chunk + d % 4], sem.at[d]
            )
            for d in range(32)
        ]

    return make


def ff_kernel(rec, x_ref, g_ref, wo, wu, wd, gi, gf, gh, out_ref, dap, dy1_ref, gi_g, gf_g, gh_g, G, lhs, lhs2, V, N1, U, GP, E, ACC, th, tl, r_hi, r_lo, tiles, sem):
    spill = Spill(tiles, sem)
    rows_from_pairs(rec, V)
    na, rs_a = normed(V[...])
    V[...] = na
    put_split(lhs, na * gi[...])
    for j in range(3):
        cols = slice(256 * j, 256 * j + 256)
        N1[:, cols] = x_ref[:, cols] + halves_sum(dot_nn(lhs[...], wo[:, cols]))
    y1 = N1[...]
    out_ref[...] = y1
    ny, rs_y = normed(y1)
    N1[...] = ny
    put_split(lhs, ny * gf[...])

    def up(j, su):
        cols = pl.ds(pl.multiple_of(j * FT, FT), FT)
        z = halves_sum(dot_nn(lhs[...], wu[:, cols]))
        phi = 0.5 * (1.0 + lax.erf(z * math.sqrt(0.5)))
        u = z * phi
        U[:, cols] = u
        GP[:, cols] = phi + z * jnp.exp(-0.5 * z * z) * (1.0 / math.sqrt(2.0 * math.pi))
        return su + jnp.sum(u, -1, keepdims=True)

    zero = jnp.zeros((ROWS, 1), F32)
    mean = lax.fori_loop(0, FF // FT, up, zero) * (1.0 / FF)

    def spread(j, sv):
        cols = pl.ds(pl.multiple_of(j * FT, FT), FT)
        c = U[:, cols] - mean
        return sv + jnp.sum(c * c, -1, keepdims=True)

    rs_u = lax.rsqrt(lax.fori_loop(0, FF // FT, spread, zero) * (1.0 / FF) + LN_EPSILON)
    ACC[...] = jnp.zeros_like(ACC)

    def lower(j, carry):
        cols = pl.ds(pl.multiple_of(j * FT, FT), FT)
        n = (U[:, cols] - mean) * rs_u
        U[:, cols] = n
        put_split(lhs2, n * gh[:, cols])
        ACC[...] += halves_sum(dot_nn(lhs2[...], wd[cols, :]))
        return carry

    lax.fori_loop(0, FF // FT, lower, 0)
    out_ref[...] += ACC[...]

    put_split(lhs, g_ref[...])

    def back_down(j, sums):
        cols = pl.ds(pl.multiple_of(j * FT, FT), FT)
        e = halves_sum(dot_nt(lhs[...], wd[cols, :]))
        n = U[:, cols]
        gh_g[:, cols] = jnp.sum(e * n, 0, keepdims=True)
        f = e * gh[:, cols]
        E[:, cols] = f
        return sums[0] + jnp.sum(f, -1, keepdims=True), sums[1] + jnp.sum(f * n, -1, keepdims=True)

    sf, sfn = lax.fori_loop(0, FF // FT, back_down, (zero, zero))
    mf, mfn = sf * (1.0 / FF), sfn * (1.0 / FF)
    ACC[...] = jnp.zeros_like(ACC)

    def back_up(j, carry):
        cols = pl.ds(pl.multiple_of(j * FT, FT), FT)
        dz = (E[:, cols] - mf - U[:, cols] * mfn) * rs_u * GP[:, cols]
        E[:, cols] = dz
        put_split(lhs2, dz)
        ACC[...] += halves_sum(dot_nt(lhs2[...], wu[:, cols]))
        return carry

    lax.fori_loop(0, FF // FT, back_up, 0)
    e = ACC[...]
    ny = N1[...]
    gf_g[...] = jnp.sum(e * ny, 0, keepdims=True)
    dy1 = g_ref[...] + norm_back(e * gf[...], ny, rs_y)
    dy1_ref[...] = dy1
    put_split(lhs, dy1)
    for j in range(3):
        cols = slice(256 * j, 256 * j + 256)
        ACC[:, cols] = halves_sum(dot_nt(lhs[...], wo[cols, :]))
    e = ACC[...]
    na = V[...]
    gi_g[...] = jnp.sum(e * na, 0, keepdims=True)
    ACC[...] = norm_back(e * gi[...], na, rs_a)
    pairs_from_rows(ACC, dap)

    put_turned(th, tl, na * gi[...])
    r_hi[...], r_lo[...] = split(dy1)
    spill.emit(lambda t: product(th, tl, r_hi, r_lo, t), column_copies(G, 3))
    put_turned(th, tl, ny * gf[...])
    for j in range(4):
        r_hi[...], r_lo[...] = split(E[:, D * j : D * j + D])
        spill.emit(lambda t: product(th, tl, r_hi, r_lo, t), column_copies(G, 4 + j))
    r_hi[...], r_lo[...] = split(g_ref[...])
    for j in range(4):
        cols = slice(D * j, D * j + D)
        put_turned(th, tl, U[:, cols] * gh[:, cols])
        spill.emit(lambda t: product(th, tl, r_hi, r_lo, t), row_copies(G, j, 8))
    spill.close()


CHUNKS = 12
PIECE = 24


def grad_shape():
    return jax.ShapeDtypeStruct((2, 2, 4, 2, CHUNKS, PIECE, D), F32)


def tile_scratch():
    return [
        pltpu.VMEM((D, ROWS), BF16),
        pltpu.VMEM((D, ROWS), BF16),
        pltpu.VMEM((ROWS, D), BF16),
        pltpu.VMEM((ROWS, D), BF16),
        pltpu.VMEM((2, D, D), F32),
        pltpu.SemaphoreType.DMA((2, 32)),
    ]


def feed_forward(rec, x, g, wo, wu, wd, gi, gf, gh):
    act = jax.ShapeDtypeStruct((ROWS, D), F32)
    wide = pltpu.VMEM((ROWS, FF), F32)
    thin = pltpu.VMEM((ROWS, D), F32)
    return pl.pallas_call(
        ff_kernel,
        out_shape=[
            act,
            jax.ShapeDtypeStruct((HEADS, HALF, 128), F32),
            act,
            jax.ShapeDtypeStruct((1, D), F32),
            jax.ShapeDtypeStruct((1, D), F32),
            jax.ShapeDtypeStruct((1, FF), F32),
            grad_shape(),
        ],
        in_specs=[VM] * 9,
        out_specs=[VM] * 6 + [ANY],
        scratch_shapes=[
            pltpu.VMEM((2 * ROWS, D), BF16),
            pltpu.VMEM((2 * ROWS, FT), BF16),
            thin,
            thin,
            wide,
            wide,
            wide,
            thin,
        ]
        + tile_scratch(),
        compiler_params=params(),
    )(rec, x, g, wo, wu, wd, gi.reshape(1, D), gf.reshape(1, D), gh.reshape(1, FF))


def last_kernel(rec, x_ref, dy1_ref, w, ga, gi_g, gf_g, gh_g, sums, G_in, gx, S, G, dqkv, lhs, th, tl, r_hi, r_lo, tiles, sem):
    spill = Spill(tiles, sem)
    for j in range(HEADS // 2):
        u, v = rec[2 * j, ROWS:PACK, :], rec[2 * j + 1, ROWS:PACK, :]
        cols = slice(128 * j, 128 * j + 128)
        dqkv[0:HALF, cols] = pick(u, swap(v))
        dqkv[HALF:ROWS, cols] = pick(swap(u), v)
        u, v = rec[2 * j, 0:ROWS, :], rec[2 * j + 1, 0:ROWS, :]
        dqkv[:, D + 128 * j : D + 128 * j + 128] = pick(u, swap(v))
        dqkv[:, 2 * D + 128 * j : 2 * D + 128 * j + 128] = pick(swap(u), v)
    n, rs = normed(x_ref[...])
    put_turned(th, tl, n * ga[...])
    e = None
    for j in range(3):
        cols = slice(D * j, D * j + D)
        part = dqkv[:, cols]
        hi, lo = split(part)
        r_hi[...], r_lo[...] = hi, lo
        lhs[0:ROWS, :], lhs[ROWS : 2 * ROWS, :] = hi, lo
        spill.emit(lambda t: product(th, tl, r_hi, r_lo, t), column_copies(G, j))
        more = halves_sum(dot_nt(lhs[...], w[:, cols]))
        e = more if e is None else e + more
    S[0:1, :] = jnp.sum(e * n, 0, keepdims=True)
    S[1:2, :] = gi_g[...]
    S[2:3, :] = gf_g[...]
    for j in range(4):
        S[3 + j : 4 + j, :] = gh_g[:, D * j : D * j + D]
    lane = lax.broadcasted_iota(jnp.int32, (1, 128), 1)
    S[7:8, :] = jnp.zeros((1, D), F32)
    S[7:8, 0:128] = sum(jnp.where(lane == i, sums[i : i + 1, :], 0.0) for i in range(PATTERNS))
    gx[...] = dy1_ref[...] + norm_back(e * ga[...], n, rs)
    spill.close()


def last(rec, x, dy1, w, ga, gi_g, gf_g, gh_g, sums, G):
    return pl.pallas_call(
        last_kernel,
        out_shape=[
            jax.ShapeDtypeStruct((ROWS, D), F32),
            jax.ShapeDtypeStruct((8, D), F32),
            grad_shape(),
        ],
        in_specs=[VM] * 9 + [ANY],
        out_specs=[VM, VM, ANY],
        scratch_shapes=[pltpu.VMEM((ROWS, 3 * D), F32), pltpu.VMEM((2 * ROWS, D), BF16)] + tile_scratch(),
        input_output_aliases={9: 2},
        compiler_params=params(),
    )(rec, x, dy1, w, ga.reshape(1, D), gi_g, gf_g, gh_g, sums, G)


class Place:
    def __init__(self):
        p, s = lax.axis_index("pat"), lax.axis_index("seq")
        self.p, self.s = p, s
        self.x, self.core, self.z, self.y = p // 2, lax.rem(p, 2), s // 2, lax.rem(s, 2)
        self.peer = to(self.x * 2 + 1 - self.core, s)
        self.xn = to((1 - self.x) * 2 + self.core, s)
        self.yn = to(p, self.z * 2 + 1 - self.y)
        self.left, self.right = to(p, s - 2), to(p, s + 2)

    def greet(self, barrier):
        for d in (self.peer, self.xn, self.yn):
            pl.semaphore_signal(barrier, inc=1, device_id=d, device_id_type=MESH)

        @pl.when(self.z > 0)
        def _():
            pl.semaphore_signal(barrier, inc=1, device_id=self.left, device_id_type=MESH)

        @pl.when(self.z < 3)
        def _():
            pl.semaphore_signal(barrier, inc=1, device_id=self.right, device_id_type=MESH)

        return 3 + (self.z > 0).astype(jnp.int32) + (self.z < 3).astype(jnp.int32)


def remote(src, dst, a, b, d):
    return pltpu.make_async_remote_copy(
        src_ref=src, dst_ref=dst, send_sem=a, recv_sem=b, device_id=d, device_id_type=MESH
    )


class Chunk:
    def __init__(self, place, k, group, slot, own, osem, bufs, sems, put, x_first):
        self.at, self.k, self.group, self.slot, self.own, self.osem = place, k, group, slot, own, osem
        self.b0, self.b1, self.b2, self.bl, self.br = bufs
        self.sc, self.rc, self.s1, self.r1, self.s2, self.r2, self.sl, self.rl, self.sr, self.rr = sems
        self.put, self.x_first = put, x_first

    def core(self):
        k, c = self.k, 1 - self.at.core
        return [
            remote(self.group(i, c), self.b0.at[i], self.sc.at[k, i], self.rc.at[k, i], self.at.peer)
            for i in range(2)
        ]

    def load(self):
        return [
            pltpu.make_async_copy(self.group(i, self.at.core), self.own.at[i], self.osem.at[self.slot, i])
            for i in range(2)
        ]

    def one(self):
        k, at = self.k, self.at
        if self.x_first:
            return remote(self.b0.at[1 - at.x], self.b1, self.s1.at[k], self.r1.at[k], at.xn)
        return remote(self.b0.at[:, :, 1 - at.y], self.b1, self.s1.at[k], self.r1.at[k], at.yn)

    def two(self):
        k, at = self.k, self.at
        if self.x_first:
            return remote(self.b1.at[:, 1 - at.y], self.b2, self.s2.at[k], self.r2.at[k], at.yn)
        return remote(self.b1.at[1 - at.x], self.b2, self.s2.at[k], self.r2.at[k], at.xn)

    def rightward(self, i):
        k, part = self.k, pl.ds(i + 1, 3 - i)
        src = self.b2 if i == 0 else self.bl
        return remote(src.at[part], self.bl.at[part], self.sr.at[k], self.rl.at[k], self.at.right)

    def leftward(self, i):
        k, part = self.k, pl.ds(0, i)
        src = self.b2 if i == 3 else self.br
        return remote(src.at[part], self.br.at[part], self.sl.at[k], self.rr.at[k], self.at.left)

    def stage1(self):
        for c in self.load():
            c.wait()
        for c in self.core():
            c.wait_recv()
        self.b0[...] += self.own[...]
        self.one().start()

    def stage2(self):
        self.one().wait_recv()
        mine = self.b0[self.at.x] if self.x_first else self.b0[:, :, self.at.y]
        self.b1[...] += mine
        self.two().start()

    def stage3(self):
        self.two().wait_recv()
        mine = self.b1[:, self.at.y] if self.x_first else self.b1[self.at.x]
        self.b2[...] += mine

        @pl.when(self.at.z == 0)
        def _():
            self.rightward(0).start()

        @pl.when(self.at.z == 3)
        def _():
            self.leftward(3).start()

    def stage4(self):
        @pl.when(self.at.z == 1)
        def _():
            self.rightward(0).wait_recv()
            self.bl[2:4] += self.b2[2:4]
            self.rightward(1).start()

        @pl.when(self.at.z == 2)
        def _():
            self.leftward(3).wait_recv()
            self.br[0:2] += self.b2[0:2]
            self.leftward(2).start()

    def stage5(self):
        @pl.when(self.at.z == 2)
        def _():
            self.rightward(1).wait_recv()
            self.bl[3:4] += self.b2[3:4]
            self.rightward(2).start()

        @pl.when(self.at.z == 1)
        def _():
            self.leftward(2).wait_recv()
            self.br[0:1] += self.b2[0:1]
            self.leftward(1).start()

    def stage6(self):
        @pl.when(self.at.z == 3)
        def _():
            self.rightward(2).wait_recv()
            self.put(self.b2[3] + self.bl[3])

        @pl.when(self.at.z == 0)
        def _():
            self.leftward(1).wait_recv()
            self.put(self.b2[0] + self.br[0])

        @pl.when(self.at.z == 1)
        def _():
            self.put(self.b2[1] + self.bl[1] + self.br[1])

        @pl.when(self.at.z == 2)
        def _():
            self.put(self.b2[2] + self.bl[2] + self.br[2])

    def sent(self):
        for c in self.core() + [self.one(), self.two()]:
            c.wait_send()
        for i in range(4):

            @pl.when(self.at.z == i)
            def _(i=i):
                if i < 3:
                    self.rightward(i).wait_send()
                if i > 0:
                    self.leftward(i).wait_send()


class Reducer:
    def __init__(self, place, n, G, scratch, put):
        self.place, self.n, self.G, self.put = place, n, G, put
        self.own, self.c0, self.c1a, self.c1b, self.c2, self.zl, self.zr, self.osem = scratch[:8]
        self.sems = scratch[8:18]
        self.pairs = (n + 1) // 2

    @staticmethod
    def scratch(n):
        dma = pltpu.SemaphoreType.DMA
        bufs = [(4, 2, 4, 2), (n, 2, 4, 2), ((n + 1) // 2, 4, 2), (max(n // 2, 1), 2, 4), (n, 4), (n, 4), (n, 4)]
        return (
            [pltpu.VMEM(b + (PIECE, D), F32) for b in bufs]
            + [dma((4, 2)), dma((n, 2)), dma((n, 2))]
            + [dma((n,)) for _ in range(8)]
        )

    def chunk(self, k, parity):
        slot = lax.rem(k, 4)
        b1 = (self.c1b if parity else self.c1a).at[k // 2]
        return Chunk(
            self.place,
            k,
            lambda i, c: self.G.at[i, c, :, :, k],
            slot,
            self.own.at[slot],
            self.osem,
            (self.c0.at[k], b1, self.c2.at[k], self.zl.at[k], self.zr.at[k]),
            self.sems,
            lambda v: self.put(k, v),
            parity == 0,
        )

    def begin(self):
        def one(k, carry):
            for c in self.chunk(k, 0).core():
                c.start()
            return carry

        lax.fori_loop(0, self.n, one, 0)
        for k in range(min(2, self.n)):
            for c in self.chunk(jnp.int32(k), 0).load():
                c.start()

    def step(self, tau, last=6):
        for stage in range(1, last + 1):
            for parity in range(2):
                k = 2 * (tau - stage) + parity

                @pl.when(jnp.logical_and(k >= 0, k < self.n))
                def _(k=k, stage=stage, parity=parity):
                    if stage == 1:

                        @pl.when(k + 2 < self.n)
                        def _():
                            for c in self.chunk(k + 2, 0).load():
                                c.start()

                    getattr(self.chunk(k, parity), f"stage{stage}")()

    def finish(self):
        def one(k, carry):
            for parity in range(2):

                @pl.when(lax.rem(k, 2) == parity)
                def _(parity=parity):
                    self.chunk(k, parity).sent()

            return carry

        lax.fori_loop(0, self.n, one, 0)


class SmallSum:
    def __init__(self, place, S, bufs, send, recv, put):
        self.at, self.S, self.send, self.recv, self.put = place, S, send, recv, put
        self.d0, self.d1, self.d2, self.dl, self.dr, self.t1, self.t2, self.t3, self.fl, self.fr = bufs

    @staticmethod
    def scratch():
        return [pltpu.VMEM((8, D), F32)] * 10 + [pltpu.SemaphoreType.DMA((5,)), pltpu.SemaphoreType.DMA((5,))]

    def hop(self, src, dst, i, d):
        return remote(src, dst, self.send.at[i], self.recv.at[i], d)

    def core(self):
        return self.hop(self.S, self.d0, 0, self.at.peer)

    def along_x(self):
        return self.hop(self.t1, self.d1, 1, self.at.xn)

    def along_y(self):
        return self.hop(self.t2, self.d2, 2, self.at.yn)

    def rightward(self, i):
        return self.hop(self.t3 if i == 0 else self.fl, self.dl, 3, self.at.right)

    def leftward(self, i):
        return self.hop(self.t3 if i == 3 else self.fr, self.dr, 4, self.at.left)

    def stage1(self):
        self.core().wait_recv()
        self.t1[...] = self.S[...] + self.d0[...]
        self.along_x().start()

    def stage2(self):
        self.along_x().wait_recv()
        self.t2[...] = self.t1[...] + self.d1[...]
        self.along_y().start()

    def stage3(self):
        self.along_y().wait_recv()
        self.t3[...] = self.t2[...] + self.d2[...]

        @pl.when(self.at.z == 0)
        def _():
            self.rightward(0).start()

        @pl.when(self.at.z == 3)
        def _():
            self.leftward(3).start()

    def from_left(self, i):
        self.rightward(i).wait_recv()
        self.fl[...] = self.dl[...] + self.t3[...]

    def from_right(self, i):
        self.leftward(i).wait_recv()
        self.fr[...] = self.dr[...] + self.t3[...]

    def stage4(self):
        @pl.when(self.at.z == 1)
        def _():
            self.from_left(0)
            self.rightward(1).start()

        @pl.when(self.at.z == 2)
        def _():
            self.from_right(3)
            self.leftward(2).start()

    def stage5(self):
        @pl.when(self.at.z == 2)
        def _():
            self.from_left(1)
            self.rightward(2).start()

        @pl.when(self.at.z == 1)
        def _():
            self.from_right(2)
            self.leftward(1).start()

    def stage6(self):
        @pl.when(self.at.z == 3)
        def _():
            self.from_left(2)
            self.put(self.fl[...])

        @pl.when(self.at.z == 0)
        def _():
            self.from_right(1)
            self.put(self.fr[...])

        @pl.when(jnp.logical_or(self.at.z == 1, self.at.z == 2))
        def _():
            self.put(self.fl[...] + self.dr[...])

    def finish(self):
        for c in (self.core(), self.along_x(), self.along_y()):
            c.wait_send()
        for i in range(4):

            @pl.when(self.at.z == i)
            def _(i=i):
                if i < 3:
                    self.rightward(i).wait_send()
                if i > 0:
                    self.leftward(i).wait_send()


def small_outputs(place, counts, outs, tot):
    ga, gi, gf, gh, means = outs

    def put(v):
        tot[...] = v
        d = place.p * RUNS + place.s
        for i, ref in enumerate((ga, gi, gf)):
            ref[...] = pltpu.roll(tot[i : i + 1, :], D - PIECE * d, 1)[:, :PIECE]
        row = tot[pl.ds(3 + d // 8, 1), :]
        gh[...] = pltpu.roll(row, D - 4 * PIECE * lax.rem(d, 8), 1)[:, : 4 * PIECE]
        lane = lax.broadcasted_iota(jnp.int32, (1, 128), 1)
        scale = jnp.full((1, 128), counts[0], F32)
        for i in range(1, PATTERNS):
            scale = jnp.where(lane == i, counts[i], scale)
        means[...] = (tot[7:8, :128] / scale)[:, :PATTERNS]

    return put


def small_shapes():
    return [jax.ShapeDtypeStruct((1, n), F32) for n in (PIECE, PIECE, PIECE, 4 * PIECE, PATTERNS)]


N_REDUCER = 18
N_SMALL = 12


def reduce_kernel(counts, G, S, qkv, wo, up, down, ga, gi, gf, gh, means, tot, *scratch):
    place = Place()
    barrier = pltpu.get_barrier_semaphore()
    pl.semaphore_wait(barrier, place.greet(barrier))

    def put(k, v):
        @pl.when(k < 3)
        def _():
            qkv[:, pl.ds(pl.multiple_of(k * D, D), D)] = v

        @pl.when(k == 3)
        def _():
            wo[...] = v

        @pl.when(jnp.logical_and(k > 3, k < 8))
        def _():
            up[:, pl.ds(pl.multiple_of((k - 4) * D, D), D)] = v

        @pl.when(k >= 8)
        def _():
            down[pl.ds(pl.multiple_of((k - 8) * PIECE, PIECE), PIECE), :] = v

    big = Reducer(place, CHUNKS, G, scratch[:N_REDUCER], put)
    rest = scratch[N_REDUCER:]
    small = SmallSum(
        place, S, rest[:10], rest[10], rest[11], small_outputs(place, counts, (ga, gi, gf, gh, means), tot)
    )
    small.core().start()
    big.begin()

    def step(tau, carry):
        for stage in range(1, 7):

            @pl.when(tau == stage)
            def _(stage=stage):
                getattr(small, f"stage{stage}")()

        big.step(tau)
        return carry

    lax.fori_loop(1, big.pairs + 6, step, 0)
    big.finish()
    small.finish()


def reduce_scatter(G, S, counts, cid):
    return pl.pallas_call(
        functools.partial(reduce_kernel, counts),
        out_shape=[
            jax.ShapeDtypeStruct((PIECE, 3 * D), F32),
            jax.ShapeDtypeStruct((PIECE, D), F32),
            jax.ShapeDtypeStruct((PIECE, FF), F32),
            jax.ShapeDtypeStruct((4 * PIECE, D), F32),
        ]
        + small_shapes(),
        in_specs=[ANY, VM],
        out_specs=[VM] * 9,
        scratch_shapes=[pltpu.VMEM((8, D), F32)] + Reducer.scratch(CHUNKS) + SmallSum.scratch(),
        compiler_params=params(collective_id=cid, has_side_effects=True),
    )(G, S)


SEG1, SEG2, SEG3, SEG4, SEG5 = SEGMENTS
DILATION_ONE, DILATION_TWO, DILATION_THREE, DILATION_FOUR, DILATION_FIVE = DILATIONS
MASK_VALUE = -1e30
MATMUL_ACCURACY = lax.Precision.HIGHEST


def passed_along(value, axis, by):
    length = lax.axis_size(axis)
    return lax.ppermute(value, axis, [(i, (i + by) % length) for i in range(length)])


def run_is_live(distance, anchor_point, sequence_width, segment_length):
    return (anchor_point - (distance - 1) * sequence_width - 1) // segment_length == anchor_point // segment_length


def layer_norm(x, gain_vec):
    average = jnp.mean(x, -1, keepdims=True)
    centred = x - average
    variance = jnp.mean(centred * centred, -1, keepdims=True)
    return centred * lax.rsqrt(variance + LN_EPSILON) * gain_vec


def select_table(offsets_row, dilation_rate):
    return (jnp.arange(dilation_rate, dtype=jnp.int32)[:, None] == offsets_row[None, :]).astype(
        jnp.float32
    )


def spread_apart(x, select_option, dilation_rate):
    shaped = x.reshape(x.shape[0] // dilation_rate, dilation_rate, x.shape[1], x.shape[2])
    return jnp.einsum("trhd,rh->thd", shaped, select_option, precision=MATMUL_ACCURACY)


def spread_scalar_rows(x, select_option, dilation_rate):
    shaped = x.reshape(x.shape[0] // dilation_rate, dilation_rate, x.shape[1])
    return jnp.einsum("trh,rh->th", shaped, select_option, precision=MATMUL_ACCURACY)


def spread_rows(x, select_option):
    return jnp.einsum("thd,rh->trhd", x, select_option, precision=MATMUL_ACCURACY).reshape(
        -1, x.shape[1], x.shape[2]
    )


def spread_scalars(x, select_option):
    return jnp.einsum("th,rh->trh", x, select_option, precision=MATMUL_ACCURACY).reshape(
        -1, x.shape[1]
    )


def masked_score_matrix(sparse_queries, key_portion, query_position, key_position, segment_length):
    score_matrix = jnp.einsum(
        "ozt,bzt->zob", sparse_queries, key_portion, precision=MATMUL_ACCURACY
    ) * (1.0 / math.sqrt(key_portion.shape[-1]))
    q_cols = query_position.T[:, :, None]
    k_cols = key_position.T[:, None, :]
    permitted_mask = (k_cols <= q_cols) & (k_cols // segment_length == q_cols // segment_length)
    return (jnp.where(permitted_mask, score_matrix, MASK_VALUE), permitted_mask)


def prepare_pattern(
    query_sequence, key_sequence, value_sequence, offsets_row, dilation_rate, anchor_point
):
    select_option = select_table(offsets_row, dilation_rate)
    sparse_queries = spread_apart(query_sequence, select_option, dilation_rate)
    sparse_key_value = jnp.stack(
        (
            spread_apart(key_sequence, select_option, dilation_rate),
            spread_apart(value_sequence, select_option, dilation_rate),
        )
    )
    query_position = (
        anchor_point
        + jnp.arange(sparse_queries.shape[0], dtype=jnp.int32)[:, None] * dilation_rate
        + offsets_row[None, :]
    )
    return (select_option, sparse_queries, sparse_key_value, query_position)


def pattern_forward_pass(
    sparse_queries,
    sparse_key_value,
    query_position,
    reach,
    segment_length,
    anchor_point,
    sequence_width,
):
    masked_logits, permitted_mask = masked_score_matrix(
        sparse_queries, sparse_key_value[0], query_position, query_position, segment_length
    )
    row_max = jnp.max(masked_logits, -1)
    softmax_weights = jnp.where(permitted_mask, jnp.exp(masked_logits - row_max[..., None]), 0.0)
    state = (
        row_max,
        jnp.sum(softmax_weights, -1),
        jnp.einsum("tlj,jtb->tlb", softmax_weights, sparse_key_value[1], precision=MATMUL_ACCURACY),
    )

    def one_run(distance, carry):
        remote_key_value, state = carry
        remote_key_value = passed_along(remote_key_value, "seq", 1)
        key_position = query_position - distance * sequence_width

        def update(state_in):
            old_max, old_sum, old_acc = state_in
            masked_remote, permitted_remote = masked_score_matrix(
                sparse_queries, remote_key_value[0], query_position, key_position, segment_length
            )
            new_max = jnp.maximum(old_max, jnp.max(masked_remote, -1))
            weights_far = jnp.where(
                permitted_remote, jnp.exp(masked_remote - new_max[..., None]), 0.0
            )
            factor = jnp.exp(old_max - new_max)
            added = jnp.einsum(
                "tlj,jtb->tlb", weights_far, remote_key_value[1], precision=MATMUL_ACCURACY
            )
            return (
                new_max,
                old_sum * factor + jnp.sum(weights_far, -1),
                old_acc * factor[..., None] + added,
            )

        def unchanged(state_in):
            return state_in

        is_live = run_is_live(distance, anchor_point, sequence_width, segment_length)
        return remote_key_value, lax.cond(is_live, update, unchanged, state)

    state = lax.fori_loop(1, reach + 1, one_run, (sparse_key_value, state))[1]
    row_max, row_sum, accumulated = state
    mixture = jnp.transpose(accumulated / row_sum[..., None], (1, 0, 2))
    log_sum = (row_max + jnp.log(row_sum)).T
    return (mixture, log_sum)


def merge_patterns(forwards, prepared_inputs):
    full_lse = []
    full_mix = []
    for pattern_spec in range(len(forwards)):
        mixture, log_sum = forwards[pattern_spec]
        select_option = prepared_inputs[pattern_spec][0]
        covered = spread_scalars(jnp.ones_like(log_sum), select_option)
        full_lse.append(spread_scalars(log_sum, select_option) + (covered - 1.0) * 1e30)
        full_mix.append(spread_rows(mixture, select_option))
    stacked = jnp.stack(full_lse)
    row_max = jnp.max(stacked, 0)
    softmax_weights = jnp.exp(stacked - row_max)
    row_sum = jnp.sum(softmax_weights, 0)
    attended = full_mix[0] * softmax_weights[0][..., None]
    for pattern_spec in range(1, len(full_mix)):
        attended = attended + full_mix[pattern_spec] * softmax_weights[pattern_spec][..., None]
    return (attended / row_sum[..., None], row_max + jnp.log(row_sum))


def pattern_backward(
    select_option,
    dilation_rate,
    segment_length,
    anchor_point,
    sparse_queries,
    sparse_key_value,
    query_position,
    reach,
    sequence_gradient,
    row_difference,
    combined_logsumexp,
):
    sequence_width = sequence_gradient.shape[0]
    sparse_gradient = spread_apart(sequence_gradient, select_option, dilation_rate)
    sparse_output_grad = spread_scalar_rows(row_difference, select_option, dilation_rate).T
    sparse_logsumexp = spread_scalar_rows(combined_logsumexp, select_option, dilation_rate).T
    inverse_square_root = 1.0 / math.sqrt(sparse_queries.shape[-1])

    def portion_gradients(key_portion, value_portion, key_position):
        masked_logits, permitted_mask = masked_score_matrix(
            sparse_queries, key_portion, query_position, key_position, segment_length
        )
        softmax_weights = jnp.where(
            permitted_mask, jnp.exp(masked_logits - sparse_logsumexp[..., None]), 0.0
        )
        value_gradient = jnp.einsum(
            "tui,utx->itx", softmax_weights, sparse_gradient, precision=MATMUL_ACCURACY
        )
        pattern_gradient = jnp.einsum(
            "ozt,bzt->zob", sparse_gradient, value_portion, precision=MATMUL_ACCURACY
        )
        score_gradient = (
            softmax_weights
            * (pattern_gradient - sparse_output_grad[..., None])
            * inverse_square_root
        )
        query_gradient = jnp.einsum(
            "hqk,khd->qhd", score_gradient, key_portion, precision=MATMUL_ACCURACY
        )
        key_gradient = jnp.einsum(
            "tui,utx->itx", score_gradient, sparse_queries, precision=MATMUL_ACCURACY
        )
        return (query_gradient, jnp.stack((key_gradient, value_gradient)))

    query_gradient, key_value_gradient = portion_gradients(
        sparse_key_value[0], sparse_key_value[1], query_position
    )

    def one_run(distance, carry):
        remote_key_value, remote_gradient, query_sum = carry
        remote_key_value = passed_along(remote_key_value, "seq", 1)
        remote_gradient = passed_along(remote_gradient, "seq", 1)
        key_position = query_position - distance * sequence_width

        def far_grads():
            part_q, part_kv = portion_gradients(remote_key_value[0], remote_key_value[1], key_position)
            return query_sum + part_q, remote_gradient + part_kv

        def no_grads():
            return query_sum, remote_gradient

        is_live = run_is_live(distance, anchor_point, sequence_width, segment_length)
        query_sum, remote_gradient = lax.cond(is_live, far_grads, no_grads)
        return remote_key_value, remote_gradient, query_sum

    _, travelled, query_gradient = lax.fori_loop(
        1, reach + 1, one_run, (sparse_key_value, key_value_gradient, query_gradient)
    )
    return (query_gradient, passed_along(travelled, "seq", -reach))


def front_part(own_rows, w_qkv, gain_attn):
    return jnp.dot(layer_norm(own_rows, gain_attn), w_qkv, precision=MATMUL_ACCURACY)


def after_part(attn_rows, own_rows, w_out, w_up, w_down, gain_inner, gain_ffn, gain_hidden):
    residual = own_rows + jnp.dot(
        layer_norm(attn_rows, gain_inner), w_out, precision=MATMUL_ACCURACY
    )
    hidden = jax.nn.gelu(
        jnp.dot(layer_norm(residual, gain_ffn), w_up, precision=MATMUL_ACCURACY), approximate=False
    )
    return residual + jnp.dot(layer_norm(hidden, gain_hidden), w_down, precision=MATMUL_ACCURACY)


def shards(
    tokens,
    w_qkv,
    w_out,
    w_up,
    w_down,
    gain_attn,
    gain_inner,
    gain_ffn,
    gain_hidden,
    offsets,
    grad_out,
):
    w_qkv = w_qkv.astype(jnp.float32)
    w_out = w_out.astype(jnp.float32)
    w_up = w_up.astype(jnp.float32)
    w_down = w_down.astype(jnp.float32)
    groups = lax.axis_size("pat")
    local_rows = tokens.shape[0]
    sequence_width = local_rows * groups
    heads_here = HEADS // groups
    own_rows = tokens.reshape(local_rows, D)
    qkv_rows, front_back = jax.vjp(front_part, own_rows, w_qkv, gain_attn)
    gathered_qkv = lax.all_to_all(
        qkv_rows.reshape(local_rows, 1, 3, HEADS, HD),
        "pat",
        split_axis=3,
        concat_axis=1,
        tiled=True,
    )
    gathered_qkv = gathered_qkv.reshape(sequence_width, 3, heads_here, HD)
    head_offsets = lax.dynamic_slice_in_dim(
        offsets, lax.axis_index("pat") * heads_here, heads_here, 1
    )
    anchor_point = lax.axis_index("seq") * sequence_width
    dilation_rates = (DILATION_ONE, DILATION_TWO, DILATION_THREE, DILATION_FOUR, DILATION_FIVE)
    segment_lengths = (SEG1, SEG2, SEG3, SEG4, SEG5)
    reaches = [
        min((segment_lengths[pattern_spec] - 2) // sequence_width + 1, lax.axis_size("seq") - 1)
        for pattern_spec in range(PATTERNS)
    ]
    prepared_inputs = []
    for pattern_spec in range(PATTERNS):
        prepared_inputs.append(
            prepare_pattern(
                gathered_qkv[:, 0],
                gathered_qkv[:, 1],
                gathered_qkv[:, 2],
                head_offsets[pattern_spec],
                dilation_rates[pattern_spec],
                anchor_point,
            )
        )
    forwards = []
    for pattern_spec in range(PATTERNS):
        select_option, sparse_queries, sparse_key_value, query_position = prepared_inputs[
            pattern_spec
        ]
        forwards.append(
            pattern_forward_pass(
                sparse_queries,
                sparse_key_value,
                query_position,
                reaches[pattern_spec],
                segment_lengths[pattern_spec],
                anchor_point,
                sequence_width,
            )
        )
    lse_sums = jnp.stack([jnp.sum(entry[1]) for entry in forwards])
    totals = lax.psum(lse_sums, ("pat", "seq"))
    full_length = sequence_width * lax.axis_size("seq")
    counts = jnp.array(
        [
            float(full_length // dilation_rates[pattern_spec] * HEADS)
            for pattern_spec in range(PATTERNS)
        ],
        jnp.float32,
    )
    log_means = totals / counts
    attended, combined_logsumexp = merge_patterns(forwards, prepared_inputs)
    returned_rows = lax.all_to_all(
        attended.reshape(local_rows, groups, heads_here, HD),
        "pat",
        split_axis=1,
        concat_axis=2,
        tiled=True,
    )
    attn_rows = returned_rows.reshape(local_rows, D)
    result, after_back = jax.vjp(
        after_part, attn_rows, own_rows, w_out, w_up, w_down, gain_inner, gain_ffn, gain_hidden
    )
    g_attn, g_resid, g_out, g_up, g_down, g_inner, g_ffn, g_hidden = after_back(
        grad_out.reshape(local_rows, D)
    )
    sequence_gradient = lax.all_to_all(
        g_attn.reshape(local_rows, 1, HEADS, HD), "pat", split_axis=2, concat_axis=1, tiled=True
    )
    sequence_gradient = sequence_gradient.reshape(sequence_width, heads_here, HD)
    row_difference = jnp.sum(sequence_gradient * attended, -1)
    q_grads = []
    kv_grads = []
    for pattern_spec in range(PATTERNS):
        select_option, sparse_queries, sparse_key_value, query_position = prepared_inputs[
            pattern_spec
        ]
        part_q, part_kv = pattern_backward(
            select_option,
            dilation_rates[pattern_spec],
            segment_lengths[pattern_spec],
            anchor_point,
            sparse_queries,
            sparse_key_value,
            query_position,
            reaches[pattern_spec],
            sequence_gradient,
            row_difference,
            combined_logsumexp,
        )
        q_grads.append(part_q)
        kv_grads.append(part_kv)
    grad_total = jnp.zeros((sequence_width, 3, heads_here, HD), jnp.float32)
    for pattern_spec in range(PATTERNS):
        select_option = prepared_inputs[pattern_spec][0]
        grad_total = grad_total + jnp.stack(
            (
                spread_rows(q_grads[pattern_spec], select_option),
                spread_rows(kv_grads[pattern_spec][0], select_option),
                spread_rows(kv_grads[pattern_spec][1], select_option),
            ),
            1,
        )
    grad_back = lax.all_to_all(
        grad_total.reshape(local_rows, groups, 3, heads_here, HD),
        "pat",
        split_axis=1,
        concat_axis=3,
        tiled=True,
    )
    g_tokens, g_qkv, g_attn_gain = front_back(grad_back.reshape(local_rows, 3 * D))
    grad_tokens = (g_resid + g_tokens).reshape(local_rows, 1, D)
    summed = (
        lax.psum_scatter(g_qkv, ("pat", "seq"), scatter_dimension=0, tiled=True),
        lax.psum_scatter(g_out, ("pat", "seq"), scatter_dimension=0, tiled=True),
        lax.psum_scatter(g_up, ("pat", "seq"), scatter_dimension=0, tiled=True),
        lax.psum_scatter(g_down, ("pat", "seq"), scatter_dimension=0, tiled=True),
        lax.psum_scatter(g_attn_gain, ("pat", "seq"), scatter_dimension=0, tiled=True),
        lax.psum_scatter(g_inner, ("pat", "seq"), scatter_dimension=0, tiled=True),
        lax.psum_scatter(g_ffn, ("pat", "seq"), scatter_dimension=0, tiled=True),
        lax.psum_scatter(g_hidden, ("pat", "seq"), scatter_dimension=0, tiled=True),
    )
    return (
        result.reshape(local_rows, 1, D),
        grad_tokens,
        summed[0],
        summed[1],
        summed[2],
        summed[3],
        summed[4],
        summed[5],
        summed[6],
        summed[7],
        log_means,
    )


def fast_shards(tokens, w_qkv, w_out, w_up, w_down, gain_attn, gain_inner, gain_ffn, gain_hidden, offsets, grad_out):
    x = tokens.reshape(ROWS, D)
    g = grad_out.reshape(ROWS, D)
    p, s = lax.axis_index("pat"), lax.axis_index("seq")
    active, head = head_here(p, s)
    mine = lax.dynamic_slice_in_dim(offsets, head, 1, 1)[:, 0]
    info = jnp.concatenate([jnp.stack([active.astype(jnp.int32), lax.rem(p, 2).astype(jnp.int32)]), mine])

    own, sib = to_heads(front(x, w_qkv, gain_attn), True, 0)
    ap, lse, sums = attention_forward(info, own, sib)
    rec = to_homes(ap, 1)
    mixed, dap, dy1, gi_g, gf_g, gh_g, G = feed_forward(
        rec, x, g, w_out, w_up, w_down, gain_inner, gain_ffn, gain_hidden
    )
    (drec,) = to_heads(dap, False, 2)
    down, dsib = attention_backward(info, own, sib, drec, ap, lse)
    grec = grads_to_homes(down, dsib, 3)
    gx, S, G = last(grec, x, dy1, w_qkv, gain_attn, gi_g, gf_g, gh_g, sums, G)
    counts = [float(TOTAL * 4 // r * HEADS) for r in DILATIONS]
    out = reduce_scatter(G, S, counts, 4)
    return (mixed.reshape(ROWS, 1, D), gx.reshape(ROWS, 1, D), *out[:4], *(v.reshape(-1) for v in out[4:]))


def fits(mesh):
    return mesh.shape["pat"] == 4 and mesh.shape["seq"] == RUNS


def solution(mesh):
    rows = P("seq", "pat", None)
    split_rows = P(("pat", "seq"), None)
    split_one = P(("pat", "seq"))
    planned = jax.shard_map(
        fast_shards,
        mesh=mesh,
        in_specs=(rows,) + (P(),) * 9 + (rows,),
        out_specs=(rows, rows) + (split_rows,) * 4 + (split_one,) * 4 + (P(),),
        check_vma=False,
    )
    general = jax.shard_map(
        shards,
        mesh=mesh,
        in_specs=(rows,) + (P(),) * 9 + (rows,),
        out_specs=(rows, rows) + (split_rows,) * 4 + (split_one,) * 4 + (P(),),
        check_vma=False,
    )

    def layer(tokens, *rest):
        if fits(mesh) and tokens.shape[0] == TOTAL:
            return planned(tokens, *rest)
        return general(tokens, *rest)

    return layer
```

```python
import functools
import math

import jax
import jax.numpy as jnp
from jax import lax
from jax.experimental import pallas as pl
from jax.experimental.pallas import tpu as pltpu
from jax.sharding import PartitionSpec as P

D = 768
HEADS = 12
HD = 64
FF = 3072
PATTERNS = 5
SEGMENTS = (2048, 4096, 8192, 16384, 32768)
DILATIONS = (1, 2, 4, 6, 12)
LN_EPSILON = 1e-05
NEG = -1e30
F32 = jnp.float32
BF16 = jnp.bfloat16
HIGHEST = lax.Precision.HIGHEST
VMEM_LIMIT = 58 * 1024 * 1024

ROWS = 192
HALF = ROWS // 2
RUNS = 8
TOTAL = ROWS * RUNS
PACK = ROWS + HALF
HOMES = 16
THIRD = TOTAL // 3
MESH = pl.DeviceIdType.MESH


def dot_nn(a, b):
    return lax.dot_general(a, b, (((1,), (0,)), ((), ())), preferred_element_type=F32)


def dot_nt(a, b):
    return lax.dot_general(a, b, (((1,), (1,)), ((), ())), preferred_element_type=F32)


def split(v):
    hi = v.astype(BF16)
    return hi, (v - hi.astype(F32)).astype(BF16)


def split32(v):
    hi = v.astype(BF16).astype(F32)
    return hi, v - hi


def lower_lanes(v):
    return lax.broadcasted_iota(jnp.int32, v.shape, v.ndim - 1) < HD


def swap(v):
    return pltpu.roll(v, HD, v.ndim - 1)


def pick(a, b):
    return jnp.where(lower_lanes(a), a, b)


def head_place(h):
    z = h // 3
    column = lax.rem(lax.rem(h, 3) + z + 1, 4)
    return column // 2, z * 2 + lax.rem(column, 2)


def head_here(p, s):
    z = s // 2
    column = (p // 2) * 2 + lax.rem(s, 2)
    k = lax.rem(column - z + 7, 4)
    return k < 3, z * 3 + jnp.minimum(k, 2)


def whole(*_):
    return pl.BlockSpec(memory_space=pltpu.VMEM)


VM = pl.BlockSpec(memory_space=pltpu.VMEM)
ANY = pl.BlockSpec(memory_space=pl.ANY)
SM = pl.BlockSpec(memory_space=pltpu.SMEM)


def params(**kw):
    return pltpu.CompilerParams(vmem_limit_bytes=VMEM_LIMIT, **kw)


def normed(v):
    centred = v - jnp.mean(v, -1, keepdims=True)
    rs = lax.rsqrt(jnp.mean(centred * centred, -1, keepdims=True) + LN_EPSILON)
    return centred * rs, rs


def put_split(ref, v):
    hi, lo = split(v)
    n = v.shape[0]
    ref[0:n, :] = hi
    ref[n : 2 * n, :] = lo


def front_kernel(x3, w_ref, gain_ref, pk_ref, x_ref, lhs):
    x = x3[...].reshape(ROWS, D)
    x_ref[...] = x
    n, _ = normed(x)
    put_split(lhs, n * gain_ref[...][None, :])
    for jj in range(3):
        parts = []
        for kind in range(3):
            c0 = kind * D + 256 * jj
            r = dot_nn(lhs[...], w_ref[:, c0 : c0 + 256])
            parts.append(r[:ROWS] + r[ROWS:])
        for half in range(2):
            q, k, v = (a[:, 128 * half : 128 * half + 128] for a in parts)
            h = 4 * jj + 2 * half
            pk_ref[h, 0:ROWS, :] = pick(k, swap(v))
            pk_ref[h + 1, 0:ROWS, :] = pick(swap(k), v)
            top, bottom = q[:HALF], q[HALF:]
            pk_ref[h, ROWS:PACK, :] = pick(top, swap(bottom))
            pk_ref[h + 1, ROWS:PACK, :] = pick(swap(top), bottom)


def front(x, w, gain):
    return pl.pallas_call(
        front_kernel,
        out_shape=[jax.ShapeDtypeStruct((HEADS, PACK, 128), F32), jax.ShapeDtypeStruct((ROWS, D), F32)],
        in_specs=[VM] * 3,
        out_specs=[VM, VM],
        scratch_shapes=[pltpu.VMEM((2 * ROWS, D), BF16)],
        compiler_params=params(),
    )(x, w, gain)


def place_facts():
    p, s = lax.axis_index("pat"), lax.axis_index("seq")
    x, core = p // 2, lax.rem(p, 2)
    active, head = head_here(p, s)
    return p, s, x, core, active, head


def home_device(core, m):
    return core * 2 + lax.rem(m, 2), m // 2


def head_device(h, b):
    hx, hs = head_place(h)
    return hx * 2 + b, hs


def same(p, s, q, t):
    return jnp.logical_and(p == q, s == t)


def to(p, s):
    return {"pat": p, "seq": s}


def scatter_kernel(forward, pk, own, *rest):
    if forward:
        sib, send, recv, fsend, frecv = rest
    else:
        send, recv = rest
    p, s, x, core, active, head = place_facts()
    slot = s * 2 + core
    barrier = pltpu.get_barrier_semaphore()

    @pl.when(active)
    def _():
        def greet(m, carry):
            q, t = home_device(core, m)

            @pl.when(jnp.logical_not(same(p, s, q, t)))
            def _():
                pl.semaphore_signal(barrier, inc=1, device_id=to(q, t), device_id_type=MESH)

            return carry

        lax.fori_loop(0, HOMES, greet, 0)
        if forward:
            pl.semaphore_signal(barrier, inc=1, device_id=to(x * 2 + 1 - core, s), device_id_type=MESH)

    mine = jnp.logical_and(active, core == x)
    waits = HEADS - mine.astype(jnp.int32)
    if forward:
        waits = waits + active.astype(jnp.int32)
    pl.semaphore_wait(barrier, waits)

    def copy(h):
        q, t = head_device(h, x)
        return q, t, pltpu.make_async_remote_copy(
            src_ref=pk.at[h],
            dst_ref=own.at[slot],
            send_sem=send.at[h],
            recv_sem=recv.at[slot],
            device_id=to(q, t),
            device_id_type=MESH,
        )

    def start(j, carry):
        h = lax.rem(j + 3 * (s // 2) + 2 * p, HEADS)
        q, t, remote = copy(h)

        @pl.when(same(p, s, q, t))
        def _():
            pltpu.make_async_copy(pk.at[h], own.at[slot], recv.at[slot]).start()

        @pl.when(jnp.logical_not(same(p, s, q, t)))
        def _():
            remote.start()

        return carry

    lax.fori_loop(0, HEADS, start, 0)

    def passed(m):
        return pltpu.make_async_remote_copy(
            src_ref=own.at[m, pl.ds(0, ROWS), :],
            dst_ref=sib.at[m],
            send_sem=fsend.at[m],
            recv_sem=frecv.at[m],
            device_id=to(x * 2 + 1 - core, s),
            device_id_type=MESH,
        )

    @pl.when(active)
    def _():
        def arrive(m, carry):
            pltpu.make_async_copy(own.at[m], own.at[m], recv.at[m]).wait()
            if forward:
                passed(m).start()
            return carry

        lax.fori_loop(0, HOMES, arrive, 0)
        if forward:

            def finish(m, carry):
                passed(m).wait()
                return carry

            lax.fori_loop(0, HOMES, finish, 0)

    def sent(h, carry):
        q, t, remote = copy(h)

        @pl.when(jnp.logical_not(same(p, s, q, t)))
        def _():
            remote.wait_send()

        return carry

    lax.fori_loop(0, HEADS, sent, 0)


def to_heads(packets, forward, cid):
    rows = packets.shape[1]
    shapes = [jax.ShapeDtypeStruct((HOMES, rows, 128), F32)]
    sems = [pltpu.SemaphoreType.DMA((HEADS,)), pltpu.SemaphoreType.DMA((HOMES,))]
    if forward:
        shapes.append(jax.ShapeDtypeStruct((HOMES, ROWS, 128), F32))
        sems += [pltpu.SemaphoreType.DMA((HOMES,)), pltpu.SemaphoreType.DMA((HOMES,))]
    return pl.pallas_call(
        functools.partial(scatter_kernel, forward),
        out_shape=shapes,
        in_specs=[ANY],
        out_specs=[ANY] * len(shapes),
        scratch_shapes=sems,
        compiler_params=params(collective_id=cid, has_side_effects=True),
    )(packets)


def home_barrier(p, s, x, core, active, barrier, also_sibling):
    def greet(h, carry):
        q, t = head_device(h, x)

        @pl.when(jnp.logical_not(same(p, s, q, t)))
        def _():
            pl.semaphore_signal(barrier, inc=1, device_id=to(q, t), device_id_type=MESH)

        return carry

    lax.fori_loop(0, HEADS, greet, 0)

    @pl.when(active)
    def _():
        if also_sibling:
            pl.semaphore_signal(barrier, inc=1, device_id=to(x * 2 + 1 - core, s), device_id_type=MESH)
        mine = (core == x).astype(jnp.int32)
        pl.semaphore_wait(barrier, HOMES - mine + (1 if also_sibling else 0))


def gather_kernel(pk, rec, send, recv):
    p, s, x, core, active, head = place_facts()
    barrier = pltpu.get_barrier_semaphore()
    home_barrier(p, s, x, core, active, barrier, False)

    def copy(m):
        q, t = home_device(core, m)
        return q, t, pltpu.make_async_remote_copy(
            src_ref=pk.at[m],
            dst_ref=rec.at[head],
            send_sem=send.at[m],
            recv_sem=recv.at[head],
            device_id=to(q, t),
            device_id_type=MESH,
        )

    @pl.when(active)
    def _():
        def start(j, carry):
            m = lax.rem(j + 2 * s + 1, HOMES)
            q, t, remote = copy(m)

            @pl.when(same(p, s, q, t))
            def _():
                pltpu.make_async_copy(pk.at[m], rec.at[head], recv.at[head]).start()

            @pl.when(jnp.logical_not(same(p, s, q, t)))
            def _():
                remote.start()

            return carry

        lax.fori_loop(0, HOMES, start, 0)

    def arrive(h, carry):
        pltpu.make_async_copy(rec.at[h], rec.at[h], recv.at[h]).wait()
        return carry

    lax.fori_loop(0, HEADS, arrive, 0)

    @pl.when(active)
    def _():
        def sent(m, carry):
            q, t, remote = copy(m)

            @pl.when(jnp.logical_not(same(p, s, q, t)))
            def _():
                remote.wait_send()

            return carry

        lax.fori_loop(0, HOMES, sent, 0)


def to_homes(packets, cid):
    rows = packets.shape[1]
    return pl.pallas_call(
        gather_kernel,
        out_shape=jax.ShapeDtypeStruct((HEADS, rows, 128), F32),
        in_specs=[ANY],
        out_specs=ANY,
        scratch_shapes=[pltpu.SemaphoreType.DMA((HOMES,)), pltpu.SemaphoreType.DMA((HEADS,))],
        compiler_params=params(collective_id=cid, has_side_effects=True),
    )(packets)


def tile_positions(rows, columns, row_classes, column_classes, t_step, class_step):
    r = lax.broadcasted_iota(jnp.int32, (rows, columns), 0)
    q = lax.broadcasted_iota(jnp.int32, (rows, columns), 1)
    rn, qn = rows // row_classes, columns // column_classes
    return (r % rn) * t_step + (r // rn) * class_step, (q % qn) * t_step + (q // qn) * class_step


def key_bias(q_shape, k_shape, t_step, class_step, shift, keys_first):
    nq, nk = q_shape[0] * q_shape[1], k_shape[0] * k_shape[1]
    if keys_first:
        kp, qp = tile_positions(nk, nq, k_shape[0], q_shape[0], t_step, class_step)
    else:
        qp, kp = tile_positions(nq, nk, q_shape[0], k_shape[0], t_step, class_step)
    return jnp.where(kp - qp <= shift, 0.0, NEG).astype(F32)


def unpack_keys(own, sib, b, kvf):
    def one(m, carry):
        c = 2 * b + lax.rem(m, 2)
        d = 2 * (1 - b) + lax.rem(m, 2)
        t = pl.multiple_of((m // 2) * ROWS, 64)
        kvf[c, pl.ds(t, ROWS), :] = own[m, 0:ROWS, :]
        kvf[d, pl.ds(t, ROWS), :] = sib[m]
        return carry

    lax.fori_loop(0, HOMES, one, 0)


def unpack_pairs(src, first, dst, scale):
    def one(m, carry):
        t = pl.multiple_of((m // 2) * ROWS, 32)
        v = src[m, first : first + HALF, :] * scale
        w = swap(v)
        dst[lax.rem(m, 2), pl.ds(t, HALF), :] = pick(v, w)
        dst[lax.rem(m, 2), pl.ds(t + HALF, HALF), :] = pick(w, v)
        return carry

    lax.fori_loop(0, HOMES, one, 0)


def keys_and_values(kv):
    hi, lo = split32(kv)
    k2 = pick(hi, swap(lo))
    v2 = pick(swap(hi), lo)
    return k2, v2


def doubled(v):
    return jnp.concatenate([v, v], 1)


def query_quads(qq):
    hi, lo = split32(qq)
    return jnp.concatenate([hi.astype(BF16), lo.astype(BF16)], 1)


def class_facts4(o4, b):
    keys = ((lax.rem(o4, 4), o4 // 4), (lax.rem(o4 + 6, 4), (o4 + 6) // 4))
    first = (keys[0][0] // 2) == b
    query = (jnp.where(first, keys[0][0], keys[1][0]), jnp.where(first, keys[0][1], keys[1][1]))
    return keys, jnp.where(first, 0, 1), query


def forward_kernel(info, own, sib, ap, lse, sums, kvf, kc, vc, qf, qc, k4, v4, q4, k5, v5, q5, acc, mx, A, L, M, b1, b2, b3, b4):
    active = info[0] == 1
    b = info[1]
    offs = [info[2 + i] for i in range(PATTERNS)]
    sums[...] = jnp.zeros_like(sums)

    @pl.when(active)
    def _():
        ones = jnp.ones((128, 128), BF16)
        unpack_keys(own, sib, b, kvf)
        unpack_pairs(own, ROWS, qf, 1.0 / math.sqrt(HD))

        def prepare(i, carry):
            c, t = i // 12, pl.multiple_of(lax.rem(i, 12) * 128, 128)
            k2, v2 = keys_and_values(kvf[c, pl.ds(t, 128), :])
            kc[c, pl.ds(t, 128), :] = doubled(k2.astype(BF16))
            vc[c, pl.ds(t, 128), :] = jnp.concatenate([v2.astype(BF16), ones], 1)
            return carry

        lax.fori_loop(0, 48, prepare, 0)

        def prepare_q(i, carry):
            c, t = i // 12, pl.multiple_of(lax.rem(i, 12) * 128, 128)
            qc[c, pl.ds(t, 128), :] = query_quads(qf[c, pl.ds(t, 128), :])
            return carry

        lax.fori_loop(0, 24, prepare_q, 0)

        keys4, e4, (qc4, qv4) = class_facts4(offs[3], b)
        kc5, kv5 = lax.rem(offs[4], 4), offs[4] // 4
        for blk in range(4):
            r = slice(128 * blk, 128 * blk + 128)
            for e in range(2):
                c, v = keys4[e]
                k2, v2 = keys_and_values(kvf[c, pl.ds(v + 384 * blk, 128, stride=3), :])
                k4[e, r, :] = doubled(k2.astype(BF16))
                v4[e, r, :] = jnp.concatenate([v2.astype(BF16), ones], 1)
            q4[r, :] = query_quads(qf[qc4 - 2 * b, pl.ds(qv4 + 384 * blk, 128, stride=3), :])
            k2, v2 = keys_and_values(kvf[kc5, pl.ds(kv5 + 384 * blk, 128, stride=3), :])
            k5[r, :] = doubled(k2.astype(BF16))
            v5[r, :] = jnp.concatenate([v2.astype(BF16), ones], 1)
            q5[r, :] = query_quads(qf[lax.rem(kc5, 2), pl.ds(kv5 + 384 * blk, 128, stride=3), :])

        b1[...] = key_bias((2, 128), (4, 128), 4, 1, 2 * b, False)
        b2[...] = key_bias((1, 256), (2, 256), 4, 2, 2 * b, False)
        b3[...] = key_bias((1, 256), (1, 256), 1, 1, 0, False)
        b4[...] = key_bias((1, 256), (2, 256), 12, 6, 6 * e4, False)

        def tile(g, q, k, v, bias, first):
            s = dot_nt(q, k)
            if bias is not None:
                s = s + bias[...]
            top = jnp.max(s, -1, keepdims=True)
            n = k.shape[0] // 128
            if first:
                m = jnp.broadcast_to(top, (256, 128))
            else:
                old = mx[g]
                m = jnp.maximum(old, top)
            mx[g] = m
            p = jnp.exp(s - jnp.concatenate([m] * n, 1))
            hi, lo = split(p)
            new = dot_nn(hi, v) + dot_nn(lo, v)
            if first:
                acc[g] = new
            else:
                alpha = jnp.exp(old - m)
                acc[g] = acc[g] * doubled(alpha) + new

        def note(pattern, g):
            rows = mx[g] + jnp.log(acc[g][:, 128:])
            sums[pattern : pattern + 1, :] += jnp.sum(rows, 0, keepdims=True)

        def q1(qb, carry):
            def at(g, blk):
                return pl.ds(pl.multiple_of(512 * g + 128 * blk, 128), 128)

            def load_q(g):
                return qc[:, at(g, qb), :].reshape(256, 256)

            def step(kb, bias, first):
                for g in range(3):
                    k = kc[:, at(g, kb), :].reshape(512, 256)
                    v = vc[:, at(g, kb), :].reshape(512, 256)
                    tile(g, load_q(g), k, v, bias, first)

            step(qb, b1, True)

            def more(kb, inner):
                step(kb, None, False)
                return inner

            lax.fori_loop(0, qb, more, 0)
            for g in range(3):
                note(0, g)
                A[:, at(g, qb), :] = acc[g][:, :128].reshape(2, 128, 128)
                L[:, at(g, qb), :] = acc[g][:, 128:].reshape(2, 128, 128)
                M[:, at(g, qb), :] = mx[g].reshape(2, 128, 128)
            return carry

        lax.fori_loop(0, 4, q1, 0)

        def merge(g, ci, rows):
            m0, m1 = M[ci, rows, :], mx[g]
            m = jnp.maximum(m0, m1)
            w0, w1 = jnp.exp(m0 - m), jnp.exp(m1 - m)
            A[ci, rows, :] = A[ci, rows, :] * w0 + acc[g][:, :128] * w1
            L[ci, rows, :] = L[ci, rows, :] * w0 + acc[g][:, 128:] * w1
            M[ci, rows, :] = m

        def at256(blk):
            return pl.ds(pl.multiple_of(256 * blk, 128), 256)

        par = offs[1]

        def keys2(ref, blk):
            return jnp.concatenate([ref[par, at256(blk), :], ref[par + 2, at256(blk), :]], 0)

        def q2(qb, carry):
            q = qc[par, at256(qb), :]
            tile(0, q, keys2(kc, qb), keys2(vc, qb), b2, True)

            def more(kb, inner):
                tile(0, q, keys2(kc, kb), keys2(vc, kb), None, False)
                return inner

            lax.fori_loop(jnp.where(qb >= 4, 4, 0), qb, more, 0)
            note(1, 0)
            merge(0, par, at256(qb))
            return carry

        lax.fori_loop(0, TOTAL // 256, q2, 0)

        o3 = offs[2]

        @pl.when(o3 // 2 == b)
        def _():
            ci = lax.rem(o3, 2)

            def q3(qb, carry):
                q = qc[ci, at256(qb), :]
                tile(0, q, kc[o3, at256(qb), :], vc[o3, at256(qb), :], b3, True)

                def more(kb, inner):
                    tile(0, q, kc[o3, at256(kb), :], vc[o3, at256(kb), :], None, False)
                    return inner

                lax.fori_loop(0, qb, more, 0)
                note(2, 0)
                merge(0, ci, at256(qb))
                return carry

            lax.fori_loop(0, TOTAL // 256, q3, 0)

        for qb in range(2):
            q = q4[256 * qb : 256 * qb + 256, :]
            for kb in range(qb, -1, -1):
                ks = slice(256 * kb, 256 * kb + 256)
                k = k4[:, ks, :].reshape(512, 256)
                v = v4[:, ks, :].reshape(512, 256)
                tile(qb, q, k, v, b4 if kb == qb else None, kb == qb)
            note(3, qb)
            merge(qb, qc4 - 2 * b, pl.ds(qv4 + 768 * qb, 256, stride=3))

        @pl.when(kc5 // 2 == b)
        def _():
            for qb in range(2):
                q = q5[256 * qb : 256 * qb + 256, :]
                for kb in range(qb, -1, -1):
                    ks = slice(256 * kb, 256 * kb + 256)
                    tile(qb, q, k5[ks, :], v5[ks, :], b3 if kb == qb else None, kb == qb)
                note(4, qb)
                merge(qb, lax.rem(kc5, 2), pl.ds(kv5 + 768 * qb, 256, stride=3))

        def finish(m, carry):
            ci = lax.rem(m, 2)
            t = pl.multiple_of((m // 2) * ROWS, 64)
            rows = pl.ds(t, ROWS)
            a, l = A[ci, rows, :], L[ci, rows, :]
            out = (a + swap(a)) / l
            ap[m] = pick(out[:HALF], out[HALF:])
            lse[ci, rows, :] = M[ci, rows, :] + jnp.log(l)
            return carry

        lax.fori_loop(0, HOMES, finish, 0)


def attention_forward(info, own, sib):
    big = pltpu.VMEM((4, TOTAL, 256), BF16)
    state = pltpu.VMEM((2, TOTAL, 128), F32)
    return pl.pallas_call(
        forward_kernel,
        out_shape=[
            jax.ShapeDtypeStruct((HOMES, HALF, 128), F32),
            jax.ShapeDtypeStruct((2, TOTAL, 128), F32),
            jax.ShapeDtypeStruct((8, 128), F32),
        ],
        in_specs=[SM, VM, VM],
        out_specs=[VM, VM, VM],
        scratch_shapes=[
            pltpu.VMEM((4, TOTAL, 128), F32),
            big,
            big,
            state,
            pltpu.VMEM((2, TOTAL, 256), BF16),
            pltpu.VMEM((2, THIRD, 256), BF16),
            pltpu.VMEM((2, THIRD, 256), BF16),
            pltpu.VMEM((THIRD, 256), BF16),
            pltpu.VMEM((THIRD, 256), BF16),
            pltpu.VMEM((THIRD, 256), BF16),
            pltpu.VMEM((THIRD, 256), BF16),
            pltpu.VMEM((3, 256, 256), F32),
            pltpu.VMEM((3, 256, 128), F32),
            state,
            state,
            state,
            pltpu.VMEM((256, 512), F32),
            pltpu.VMEM((256, 512), F32),
            pltpu.VMEM((256, 256), F32),
            pltpu.VMEM((256, 512), F32),
        ],
        compiler_params=params(),
    )(info, own, sib)


def rows_from_pairs(rec, dst):
    for j in range(HEADS // 2):
        u, v = rec[2 * j], rec[2 * j + 1]
        cols = slice(128 * j, 128 * j + 128)
        dst[0:HALF, cols] = pick(u, swap(v))
        dst[HALF:ROWS, cols] = pick(swap(u), v)


def pairs_from_rows(src, dst):
    for j in range(HEADS // 2):
        top = src[0:HALF, 128 * j : 128 * j + 128]
        bottom = src[HALF:ROWS, 128 * j : 128 * j + 128]
        dst[2 * j] = pick(top, swap(bottom))
        dst[2 * j + 1] = pick(swap(top), bottom)


def halves_sum(r):
    return r[:ROWS] + r[ROWS:]


def norm_back(f, n, rs):
    return (f - jnp.mean(f, -1, keepdims=True) - n * jnp.mean(f * n, -1, keepdims=True)) * rs


def put_turned(hi_ref, lo_ref, v):
    for j in range(D // 128):
        t = v[:, 128 * j : 128 * j + 128].T
        hi, lo = split(t)
        hi_ref[128 * j : 128 * j + 128, :] = hi
        lo_ref[128 * j : 128 * j + 128, :] = lo


FT = 512


class Spill:
    def __init__(self, tiles, sem):
        self.tiles, self.sem, self.count, self.open = tiles, sem, 0, [[], []]

    def emit(self, fill, copies):
        k = self.count % 2
        for c in self.open[k]:
            c.wait()
        fill(self.tiles.at[k])
        self.open[k] = copies(self.tiles.at[k], self.sem.at[k])
        for c in self.open[k]:
            c.start()
        self.count += 1

    def close(self):
        for k in range(2):
            for c in self.open[k]:
                c.wait()
            self.open[k] = []


def product(hi, lo, r_hi, r_lo, tile):
    def one(i, carry):
        rows = pl.ds(pl.multiple_of(i * 128, 128), 128)
        h, l = hi[rows, :], lo[rows, :]
        tile[rows, :] = dot_nn(h, r_hi[...]) + dot_nn(h, r_lo[...]) + dot_nn(l, r_hi[...])
        return carry

    lax.fori_loop(0, D // 128, one, 0)


def column_copies(G, chunk):
    def make(tile, sem):
        return [
            pltpu.make_async_copy(
                tile.at[pl.ds(24 * d, 24), :], G.at[d // 16, (d // 8) % 2, (d % 8) // 2, d % 2, chunk], sem.at[d]
            )
            for d in range(32)
        ]

    return make


def row_copies(G, part, chunk):
    def make(tile, sem):
        return [
            pltpu.make_async_copy(
                tile.at[pl.ds(24 * d, 24), :], G.at[part // 2, part % 2, d // 8, (d // 4) % 2, chunk + d % 4], sem.at[d]
            )
            for d in range(32)
        ]

    return make


def ff_kernel(rec, x_ref, g3, wo, wu, wd, gi1, gf1, gh1, out3,  dap, dy1_ref, gi_g, gf_g, gh_g, G, lhs, lhs2, gi, gf, gh, g_ref, out_ref, V, N1, U, GP, E, ACC, th, tl, r_hi, r_lo, tiles, sem):
    spill = Spill(tiles, sem)
    for wide, flat in ((gi, gi1), (gf, gf1), (gh, gh1)):
        wide[...] = flat[...][None, :]
    g_ref[...] = g3[...].reshape(ROWS, D)
    rows_from_pairs(rec, V)
    na, rs_a = normed(V[...])
    V[...] = na
    put_split(lhs, na * gi[...])
    for j in range(3):
        cols = slice(256 * j, 256 * j + 256)
        N1[:, cols] = x_ref[:, cols] + halves_sum(dot_nn(lhs[...], wo[:, cols]))
    y1 = N1[...]
    out_ref[...] = y1
    ny, rs_y = normed(y1)
    N1[...] = ny
    put_split(lhs, ny * gf[...])

    def up(j, su):
        cols = pl.ds(pl.multiple_of(j * FT, FT), FT)
        z = halves_sum(dot_nn(lhs[...], wu[:, cols]))
        phi = 0.5 * (1.0 + lax.erf(z * math.sqrt(0.5)))
        u = z * phi
        U[:, cols] = u
        GP[:, cols] = phi + z * jnp.exp(-0.5 * z * z) * (1.0 / math.sqrt(2.0 * math.pi))
        return su + jnp.sum(u, -1, keepdims=True)

    zero = jnp.zeros((ROWS, 1), F32)
    mean = lax.fori_loop(0, FF // FT, up, zero) * (1.0 / FF)

    def spread(j, sv):
        cols = pl.ds(pl.multiple_of(j * FT, FT), FT)
        c = U[:, cols] - mean
        return sv + jnp.sum(c * c, -1, keepdims=True)

    rs_u = lax.rsqrt(lax.fori_loop(0, FF // FT, spread, zero) * (1.0 / FF) + LN_EPSILON)
    ACC[...] = jnp.zeros_like(ACC)

    def lower(j, carry):
        cols = pl.ds(pl.multiple_of(j * FT, FT), FT)
        n = (U[:, cols] - mean) * rs_u
        U[:, cols] = n
        put_split(lhs2, n * gh[:, cols])
        ACC[...] += halves_sum(dot_nn(lhs2[...], wd[cols, :]))
        return carry

    lax.fori_loop(0, FF // FT, lower, 0)
    out3[...] = (out_ref[...] + ACC[...]).reshape(ROWS, 1, D)

    put_split(lhs, g_ref[...])

    def back_down(j, sums):
        cols = pl.ds(pl.multiple_of(j * FT, FT), FT)
        e = halves_sum(dot_nt(lhs[...], wd[cols, :]))
        n = U[:, cols]
        gh_g[:, cols] = jnp.sum(e * n, 0, keepdims=True)
        f = e * gh[:, cols]
        E[:, cols] = f
        return sums[0] + jnp.sum(f, -1, keepdims=True), sums[1] + jnp.sum(f * n, -1, keepdims=True)

    sf, sfn = lax.fori_loop(0, FF // FT, back_down, (zero, zero))
    mf, mfn = sf * (1.0 / FF), sfn * (1.0 / FF)
    ACC[...] = jnp.zeros_like(ACC)

    def back_up(j, carry):
        cols = pl.ds(pl.multiple_of(j * FT, FT), FT)
        dz = (E[:, cols] - mf - U[:, cols] * mfn) * rs_u * GP[:, cols]
        E[:, cols] = dz
        put_split(lhs2, dz)
        ACC[...] += halves_sum(dot_nt(lhs2[...], wu[:, cols]))
        return carry

    lax.fori_loop(0, FF // FT, back_up, 0)
    e = ACC[...]
    ny = N1[...]
    gf_g[...] = jnp.sum(e * ny, 0, keepdims=True)
    dy1 = g_ref[...] + norm_back(e * gf[...], ny, rs_y)
    dy1_ref[...] = dy1
    put_split(lhs, dy1)
    for j in range(3):
        cols = slice(256 * j, 256 * j + 256)
        ACC[:, cols] = halves_sum(dot_nt(lhs[...], wo[cols, :]))
    e = ACC[...]
    na = V[...]
    gi_g[...] = jnp.sum(e * na, 0, keepdims=True)
    ACC[...] = norm_back(e * gi[...], na, rs_a)
    pairs_from_rows(ACC, dap)

    put_turned(th, tl, na * gi[...])
    r_hi[...], r_lo[...] = split(dy1)
    spill.emit(lambda t: product(th, tl, r_hi, r_lo, t), column_copies(G, 0))
    put_turned(th, tl, ny * gf[...])
    for j in range(4):
        r_hi[...], r_lo[...] = split(E[:, D * j : D * j + D])
        spill.emit(lambda t: product(th, tl, r_hi, r_lo, t), column_copies(G, 1 + j))
    r_hi[...], r_lo[...] = split(g_ref[...])
    for j in range(4):
        cols = slice(D * j, D * j + D)
        put_turned(th, tl, U[:, cols] * gh[:, cols])
        spill.emit(lambda t: product(th, tl, r_hi, r_lo, t), row_copies(G, j, 5))
    spill.close()


PIECE = 24


def grad_shape(n):
    return jax.ShapeDtypeStruct((2, 2, 4, 2, n, PIECE, D), F32)


def tile_scratch():
    return [
        pltpu.VMEM((D, ROWS), BF16),
        pltpu.VMEM((D, ROWS), BF16),
        pltpu.VMEM((ROWS, D), BF16),
        pltpu.VMEM((ROWS, D), BF16),
        pltpu.VMEM((2, D, D), F32),
        pltpu.SemaphoreType.DMA((2, 32)),
    ]


def feed_forward(rec, x, g, wo, wu, wd, gi, gf, gh):
    act = jax.ShapeDtypeStruct((ROWS, D), F32)
    wide = pltpu.VMEM((ROWS, FF), F32)
    thin = pltpu.VMEM((ROWS, D), F32)
    return pl.pallas_call(
        ff_kernel,
        out_shape=[
            jax.ShapeDtypeStruct((ROWS, 1, D), F32),
            jax.ShapeDtypeStruct((HEADS, HALF, 128), F32),
            act,
            jax.ShapeDtypeStruct((1, D), F32),
            jax.ShapeDtypeStruct((1, D), F32),
            jax.ShapeDtypeStruct((1, FF), F32),
            grad_shape(9),
        ],
        in_specs=[VM] * 9,
        out_specs=[VM] * 6 + [ANY],
        scratch_shapes=[
            pltpu.VMEM((2 * ROWS, D), BF16),
            pltpu.VMEM((2 * ROWS, FT), BF16),
            pltpu.VMEM((1, D), F32),
            pltpu.VMEM((1, D), F32),
            pltpu.VMEM((1, FF), F32),
            thin,
            thin,
            thin,
            thin,
            wide,
            wide,
            wide,
            thin,
        ]
        + tile_scratch(),
        compiler_params=params(),
    )(rec, x, g, wo, wu, wd, gi, gf, gh)


def last_kernel(rec, x_ref, dy1_ref, w, ga1, gi_g, gf_g, gh_g, sums, gx, S, G, dqkv, lhs, th, tl, r_hi, r_lo, tiles, sem):
    spill = Spill(tiles, sem)
    for j in range(HEADS // 2):
        u, v = rec[2 * j, ROWS:PACK, :], rec[2 * j + 1, ROWS:PACK, :]
        cols = slice(128 * j, 128 * j + 128)
        dqkv[0:HALF, cols] = pick(u, swap(v))
        dqkv[HALF:ROWS, cols] = pick(swap(u), v)
        u, v = rec[2 * j, 0:ROWS, :], rec[2 * j + 1, 0:ROWS, :]
        dqkv[:, D + 128 * j : D + 128 * j + 128] = pick(u, swap(v))
        dqkv[:, 2 * D + 128 * j : 2 * D + 128 * j + 128] = pick(swap(u), v)
    ga = ga1[...][None, :]
    n, rs = normed(x_ref[...])
    put_turned(th, tl, n * ga)
    e = None
    for j in range(3):
        cols = slice(D * j, D * j + D)
        part = dqkv[:, cols]
        hi, lo = split(part)
        r_hi[...], r_lo[...] = hi, lo
        lhs[0:ROWS, :], lhs[ROWS : 2 * ROWS, :] = hi, lo
        spill.emit(lambda t: product(th, tl, r_hi, r_lo, t), column_copies(G, j))
        more = halves_sum(dot_nt(lhs[...], w[:, cols]))
        e = more if e is None else e + more
    S[0:1, :] = jnp.sum(e * n, 0, keepdims=True)
    S[1:2, :] = gi_g[...]
    S[2:3, :] = gf_g[...]
    for j in range(4):
        S[3 + j : 4 + j, :] = gh_g[:, D * j : D * j + D]
    lane = lax.broadcasted_iota(jnp.int32, (1, 128), 1)
    S[7:8, :] = jnp.zeros((1, D), F32)
    S[7:8, 0:128] = sum(jnp.where(lane == i, sums[i : i + 1, :], 0.0) for i in range(PATTERNS))
    gx[...] = (dy1_ref[...] + norm_back(e * ga, n, rs)).reshape(ROWS, 1, D)
    spill.close()


def last(rec, x, dy1, w, ga, gi_g, gf_g, gh_g, sums):
    return pl.pallas_call(
        last_kernel,
        out_shape=[
            jax.ShapeDtypeStruct((ROWS, 1, D), F32),
            jax.ShapeDtypeStruct((8, D), F32),
            grad_shape(3),
        ],
        in_specs=[VM] * 9,
        out_specs=[VM, VM, ANY],
        scratch_shapes=[pltpu.VMEM((ROWS, 3 * D), F32), pltpu.VMEM((2 * ROWS, D), BF16)] + tile_scratch(),
        compiler_params=params(),
    )(rec, x, dy1, w, ga, gi_g, gf_g, gh_g, sums)


class Place:
    def __init__(self):
        p, s = lax.axis_index("pat"), lax.axis_index("seq")
        self.p, self.s = p, s
        self.x, self.core, self.z, self.y = p // 2, lax.rem(p, 2), s // 2, lax.rem(s, 2)
        self.peer = to(self.x * 2 + 1 - self.core, s)
        self.xn = to((1 - self.x) * 2 + self.core, s)
        self.yn = to(p, self.z * 2 + 1 - self.y)
        self.left, self.right = to(p, s - 2), to(p, s + 2)

    def greet(self, barrier):
        for d in (self.peer, self.xn, self.yn):
            pl.semaphore_signal(barrier, inc=1, device_id=d, device_id_type=MESH)

        @pl.when(self.z > 0)
        def _():
            pl.semaphore_signal(barrier, inc=1, device_id=self.left, device_id_type=MESH)

        @pl.when(self.z < 3)
        def _():
            pl.semaphore_signal(barrier, inc=1, device_id=self.right, device_id_type=MESH)

        return 3 + (self.z > 0).astype(jnp.int32) + (self.z < 3).astype(jnp.int32)


def remote(src, dst, a, b, d):
    return pltpu.make_async_remote_copy(
        src_ref=src, dst_ref=dst, send_sem=a, recv_sem=b, device_id=d, device_id_type=MESH
    )


class Chunk:
    def __init__(self, place, k, group, slot, own, osem, bufs, sems, put, x_first):
        self.at, self.k, self.group, self.slot, self.own, self.osem = place, k, group, slot, own, osem
        self.b0, self.b1, self.b2, self.bl, self.br = bufs
        self.sc, self.rc, self.s1, self.r1, self.s2, self.r2, self.sl, self.rl, self.sr, self.rr = sems
        self.put, self.x_first = put, x_first

    def core(self):
        k, c = self.k, 1 - self.at.core
        return [
            remote(self.group(i, c), self.b0.at[i], self.sc.at[k, i], self.rc.at[k, i], self.at.peer)
            for i in range(2)
        ]

    def load(self):
        return [
            pltpu.make_async_copy(self.group(i, self.at.core), self.own.at[i], self.osem.at[self.slot, i])
            for i in range(2)
        ]

    def one(self):
        k, at = self.k, self.at
        if self.x_first:
            return remote(self.b0.at[1 - at.x], self.b1, self.s1.at[k], self.r1.at[k], at.xn)
        return remote(self.b0.at[:, :, 1 - at.y], self.b1, self.s1.at[k], self.r1.at[k], at.yn)

    def two(self):
        k, at = self.k, self.at
        if self.x_first:
            return remote(self.b1.at[:, 1 - at.y], self.b2, self.s2.at[k], self.r2.at[k], at.yn)
        return remote(self.b1.at[1 - at.x], self.b2, self.s2.at[k], self.r2.at[k], at.xn)

    def rightward(self, i):
        k, part = self.k, pl.ds(i + 1, 3 - i)
        src = self.b2 if i == 0 else self.bl
        return remote(src.at[part], self.bl.at[part], self.sr.at[k], self.rl.at[k], self.at.right)

    def leftward(self, i):
        k, part = self.k, pl.ds(0, i)
        src = self.b2 if i == 3 else self.br
        return remote(src.at[part], self.br.at[part], self.sl.at[k], self.rr.at[k], self.at.left)

    def stage1(self):
        for c in self.load():
            c.wait()
        for c in self.core():
            c.wait_recv()
        self.b0[...] += self.own[...]
        self.one().start()

    def stage2(self):
        self.one().wait_recv()
        mine = self.b0[self.at.x] if self.x_first else self.b0[:, :, self.at.y]
        self.b1[...] += mine
        self.two().start()

    def stage3(self):
        self.two().wait_recv()
        mine = self.b1[:, self.at.y] if self.x_first else self.b1[self.at.x]
        self.b2[...] += mine

        @pl.when(self.at.z == 0)
        def _():
            self.rightward(0).start()

        @pl.when(self.at.z == 3)
        def _():
            self.leftward(3).start()

    def stage4(self):
        @pl.when(self.at.z == 1)
        def _():
            self.rightward(0).wait_recv()
            self.bl[2:4] += self.b2[2:4]
            self.rightward(1).start()

        @pl.when(self.at.z == 2)
        def _():
            self.leftward(3).wait_recv()
            self.br[0:2] += self.b2[0:2]
            self.leftward(2).start()

    def stage5(self):
        @pl.when(self.at.z == 2)
        def _():
            self.rightward(1).wait_recv()
            self.bl[3:4] += self.b2[3:4]
            self.rightward(2).start()

        @pl.when(self.at.z == 1)
        def _():
            self.leftward(2).wait_recv()
            self.br[0:1] += self.b2[0:1]
            self.leftward(1).start()

    def stage6(self):
        @pl.when(self.at.z == 3)
        def _():
            self.rightward(2).wait_recv()
            self.put(self.b2[3] + self.bl[3])

        @pl.when(self.at.z == 0)
        def _():
            self.leftward(1).wait_recv()
            self.put(self.b2[0] + self.br[0])

        @pl.when(self.at.z == 1)
        def _():
            self.put(self.b2[1] + self.bl[1] + self.br[1])

        @pl.when(self.at.z == 2)
        def _():
            self.put(self.b2[2] + self.bl[2] + self.br[2])

    def sent(self):
        for c in self.core() + [self.one(), self.two()]:
            c.wait_send()
        for i in range(4):

            @pl.when(self.at.z == i)
            def _(i=i):
                if i < 3:
                    self.rightward(i).wait_send()
                if i > 0:
                    self.leftward(i).wait_send()


class Reducer:
    def __init__(self, place, n, G, scratch, put):
        self.place, self.n, self.G, self.put = place, n, G, put
        self.own, self.c0, self.c1a, self.c1b, self.c2, self.zl, self.zr, self.osem = scratch[:8]
        self.sems = scratch[8:18]
        self.pairs = (n + 1) // 2

    @staticmethod
    def scratch(n):
        dma = pltpu.SemaphoreType.DMA
        bufs = [(4, 2, 4, 2), (n, 2, 4, 2), ((n + 1) // 2, 4, 2), (max(n // 2, 1), 2, 4), (n, 4), (n, 4), (n, 4)]
        return (
            [pltpu.VMEM(b + (PIECE, D), F32) for b in bufs]
            + [dma((4, 2)), dma((n, 2)), dma((n, 2))]
            + [dma((n,)) for _ in range(8)]
        )

    def chunk(self, k, parity):
        slot = lax.rem(k, 4)
        b1 = (self.c1b if parity else self.c1a).at[k // 2]
        return Chunk(
            self.place,
            k,
            lambda i, c: self.G.at[i, c, :, :, k],
            slot,
            self.own.at[slot],
            self.osem,
            (self.c0.at[k], b1, self.c2.at[k], self.zl.at[k], self.zr.at[k]),
            self.sems,
            lambda v: self.put(k, v),
            parity == 0,
        )

    def begin(self):
        def one(k, carry):
            for c in self.chunk(k, 0).core():
                c.start()
            return carry

        lax.fori_loop(0, self.n, one, 0)
        for k in range(min(2, self.n)):
            for c in self.chunk(jnp.int32(k), 0).load():
                c.start()

    def one(self, stage, pair):
        for parity in range(2):
            k = jnp.int32(2 * pair + parity)

            @pl.when(jnp.logical_and(k >= 0, k < self.n))
            def _(k=k, parity=parity):
                if stage == 1:

                    @pl.when(k + 2 < self.n)
                    def _():
                        for c in self.chunk(k + 2, 0).load():
                            c.start()

                getattr(self.chunk(k, parity), f"stage{stage}")()

    def early(self, pair):
        self.one(1, pair)

    def step(self, tau):
        self.one(1, tau)
        for stage in range(2, 7):
            self.one(stage, tau - stage)

    def finish(self):
        def one(k, carry):
            for parity in range(2):

                @pl.when(lax.rem(k, 2) == parity)
                def _(parity=parity):
                    self.chunk(k, parity).sent()

            return carry

        lax.fori_loop(0, self.n, one, 0)


class SmallSum:
    def __init__(self, place, S, bufs, send, recv, put):
        self.at, self.S, self.send, self.recv, self.put = place, S, send, recv, put
        self.d0, self.d1, self.d2, self.dl, self.dr, self.t1, self.t2, self.t3, self.fl, self.fr = bufs

    @staticmethod
    def scratch():
        return [pltpu.VMEM((8, D), F32)] * 10 + [pltpu.SemaphoreType.DMA((5,)), pltpu.SemaphoreType.DMA((5,))]

    def hop(self, src, dst, i, d):
        return remote(src, dst, self.send.at[i], self.recv.at[i], d)

    def core(self):
        return self.hop(self.S, self.d0, 0, self.at.peer)

    def along_x(self):
        return self.hop(self.t1, self.d1, 1, self.at.xn)

    def along_y(self):
        return self.hop(self.t2, self.d2, 2, self.at.yn)

    def rightward(self, i):
        return self.hop(self.t3 if i == 0 else self.fl, self.dl, 3, self.at.right)

    def leftward(self, i):
        return self.hop(self.t3 if i == 3 else self.fr, self.dr, 4, self.at.left)

    def stage1(self):
        self.core().wait_recv()
        self.t1[...] = self.S[...] + self.d0[...]
        self.along_x().start()

    def stage2(self):
        self.along_x().wait_recv()
        self.t2[...] = self.t1[...] + self.d1[...]
        self.along_y().start()

    def stage3(self):
        self.along_y().wait_recv()
        self.t3[...] = self.t2[...] + self.d2[...]

        @pl.when(self.at.z == 0)
        def _():
            self.rightward(0).start()

        @pl.when(self.at.z == 3)
        def _():
            self.leftward(3).start()

    def from_left(self, i):
        self.rightward(i).wait_recv()
        self.fl[...] = self.dl[...] + self.t3[...]

    def from_right(self, i):
        self.leftward(i).wait_recv()
        self.fr[...] = self.dr[...] + self.t3[...]

    def stage4(self):
        @pl.when(self.at.z == 1)
        def _():
            self.from_left(0)
            self.rightward(1).start()

        @pl.when(self.at.z == 2)
        def _():
            self.from_right(3)
            self.leftward(2).start()

    def stage5(self):
        @pl.when(self.at.z == 2)
        def _():
            self.from_left(1)
            self.rightward(2).start()

        @pl.when(self.at.z == 1)
        def _():
            self.from_right(2)
            self.leftward(1).start()

    def stage6(self):
        @pl.when(self.at.z == 3)
        def _():
            self.from_left(2)
            self.put(self.fl[...])

        @pl.when(self.at.z == 0)
        def _():
            self.from_right(1)
            self.put(self.fr[...])

        @pl.when(jnp.logical_or(self.at.z == 1, self.at.z == 2))
        def _():
            self.put(self.fl[...] + self.dr[...])

    def finish(self):
        for c in (self.core(), self.along_x(), self.along_y()):
            c.wait_send()
        for i in range(4):

            @pl.when(self.at.z == i)
            def _(i=i):
                if i < 3:
                    self.rightward(i).wait_send()
                if i > 0:
                    self.leftward(i).wait_send()


def small_outputs(place, counts, outs, tot):
    ga, gi, gf, gh, means = outs

    def put(v):
        tot[...] = v
        d = place.p * RUNS + place.s
        for i, ref in enumerate((ga, gi, gf)):
            ref[...] = pltpu.roll(tot[i : i + 1, :], D - PIECE * d, 1)[:, :PIECE]
        row = tot[pl.ds(3 + d // 8, 1), :]
        gh[...] = pltpu.roll(row, D - 4 * PIECE * lax.rem(d, 8), 1)[:, : 4 * PIECE]
        lane = lax.broadcasted_iota(jnp.int32, (1, 128), 1)
        scale = jnp.full((1, 128), counts[0], F32)
        for i in range(1, PATTERNS):
            scale = jnp.where(lane == i, counts[i], scale)
        means[...] = (tot[7:8, :128] / scale)[:, :PATTERNS]

    return put


def small_shapes():
    return [jax.ShapeDtypeStruct((1, n), F32) for n in (PIECE, PIECE, PIECE, 4 * PIECE, PATTERNS)]


N_REDUCER = 18
N_QKV = 3
N_SMALL = 12


def reduce_kernel(counts, G, S, qkv, ga, gi, gf, gh, means, tot, *scratch):
    place = Place()
    barrier = pltpu.get_barrier_semaphore()
    pl.semaphore_wait(barrier, place.greet(barrier))

    def put(k, v):
        qkv[:, pl.ds(pl.multiple_of(k * D, D), D)] = v

    big = Reducer(place, N_QKV, G, scratch[:N_REDUCER], put)
    rest = scratch[N_REDUCER:]
    small = SmallSum(
        place, S, rest[:10], rest[10], rest[11], small_outputs(place, counts, (ga, gi, gf, gh, means), tot)
    )
    small.core().start()
    big.begin()

    big.early(0)
    big.early(1)
    small.stage1()

    def step(tau, carry):
        for stage in range(2, 7):

            @pl.when(tau == stage)
            def _(stage=stage):
                getattr(small, f"stage{stage}")()

        big.step(tau)
        return carry

    lax.fori_loop(2, max(big.pairs + 6, 7), step, 0)
    big.finish()
    small.finish()


def reduce_scatter(G, S, counts, cid):
    return pl.pallas_call(
        functools.partial(reduce_kernel, counts),
        out_shape=[
            jax.ShapeDtypeStruct((PIECE, 3 * D), F32),
        ]
        + small_shapes(),
        in_specs=[ANY, VM],
        out_specs=[VM] * 6,
        scratch_shapes=[pltpu.VMEM((8, D), F32)] + Reducer.scratch(N_QKV) + SmallSum.scratch(),
        compiler_params=params(collective_id=cid, has_side_effects=True),
    )(G, S)


def deliver_kernel(*refs):
    n = len(refs) // 2
    for src, dst in zip(refs[:n], refs[n:]):
        dst[...] = src[...]


def deliver(*arrays):
    return pl.pallas_call(
        deliver_kernel,
        out_shape=[jax.ShapeDtypeStruct(v.shape, v.dtype) for v in arrays],
        in_specs=[VM] * len(arrays),
        out_specs=[VM] * len(arrays),
        compiler_params=params(),
    )(*arrays)


N_FF = 9


def back_all_kernel(offs, dap, own, sib, ap, lse, G, grec, wo_g, up_g, down_g, drec, qst, kc, vc, kt, qc, dc, lt, k4, v4, kt4, q4, d4, lt4, k5, v5, kt5, q5, d5, lt5, dqt, dk, dv, dq, dk4, dv4, dk5, dv5, dq4, dq5, b1, b2, b3, b4, ds_out, came, lsem, dsend, drecv, send, recv, qsend, qrecv, fsend, frecv, *scratch):
    place = Place()
    p, s, x, core, active, head = place_facts()
    b = core
    o2, o3, o4, o5 = offs[1], offs[2], offs[3], offs[4]
    kvf, qf, X, df = dk, dv.at[0:2], dv.at[2:4], dq
    dqp = qst

    barrier = pltpu.get_barrier_semaphore()
    expected = place.greet(barrier)
    expected = expected + HEADS - jnp.logical_and(active, core == x).astype(jnp.int32)

    @pl.when(active)
    def _():
        def greet(m, carry):
            q, t = home_device(core, m)

            @pl.when(jnp.logical_not(same(p, s, q, t)))
            def _():
                pl.semaphore_signal(barrier, inc=1, device_id=to(q, t), device_id_type=MESH)

            return carry

        lax.fori_loop(0, HOMES, greet, 0)

    def greet_heads(h, carry):
        q, t = head_device(h, x)

        @pl.when(jnp.logical_not(same(p, s, q, t)))
        def _():
            pl.semaphore_signal(barrier, inc=1, device_id=to(q, t), device_id_type=MESH)

        return carry

    lax.fori_loop(0, HEADS, greet_heads, 0)
    from_homes = HOMES - (core == x).astype(jnp.int32)
    pl.semaphore_wait(barrier, expected + active.astype(jnp.int32) * from_homes)

    slot = s * 2 + core

    def da_copy(h):
        q, t = head_device(h, x)
        return q, t, remote(dap.at[h], drec.at[slot], dsend.at[h], drecv.at[slot], to(q, t))

    def da_start(j, carry):
        h = lax.rem(j + 3 * (s // 2) + 2 * p, HEADS)
        q, t, far = da_copy(h)

        @pl.when(same(p, s, q, t))
        def _():
            pltpu.make_async_copy(dap.at[h], drec.at[slot], drecv.at[slot]).start()

        @pl.when(jnp.logical_not(same(p, s, q, t)))
        def _():
            far.start()

        return carry

    lax.fori_loop(0, HEADS, da_start, 0)

    def put(k, v):
        @pl.when(k == 0)
        def _():
            wo_g[...] = v

        @pl.when(jnp.logical_and(k > 0, k < 5))
        def _():
            up_g[:, pl.ds(pl.multiple_of((k - 1) * D, D), D)] = v

        @pl.when(k >= 5)
        def _():
            down_g[pl.ds(pl.multiple_of((k - 5) * PIECE, PIECE), PIECE), :] = v

    big = Reducer(place, N_FF, G, scratch, put)
    big.begin()

    def local_copies(m):
        t = pl.multiple_of((m // 2) * ROWS, 64)
        c, d = 2 * b + lax.rem(m, 2), 2 * (1 - b) + lax.rem(m, 2)
        return [
            pltpu.make_async_copy(own.at[m, pl.ds(0, ROWS), :], kvf.at[c, pl.ds(t, ROWS), :], lsem.at[m, 0]),
            pltpu.make_async_copy(sib.at[m], kvf.at[d, pl.ds(t, ROWS), :], lsem.at[m, 1]),
            pltpu.make_async_copy(own.at[m, pl.ds(ROWS, HALF), :], qst.at[m], lsem.at[m, 2]),
        ]

    lse_copy = pltpu.make_async_copy(lse, X, lsem.at[HOMES, 0])

    @pl.when(active)
    def _():
        lse_copy.start()

        def start(m, carry):
            for c in local_copies(m):
                c.start()
            return carry

        lax.fori_loop(0, HOMES, start, 0)
        b1[...] = key_bias((2, 128), (4, 128), 4, 1, 2 * b, True)
        b2[...] = key_bias((1, 256), (2, 256), 4, 2, 2 * b, True)
        b3[...] = key_bias((1, 256), (1, 256), 1, 1, 0, True)
        e4 = class_facts4(o4, b)[1]
        b4[...] = key_bias((1, 256), (2, 256), 12, 6, 6 * e4, True)

        def wait(m, carry):
            for c in local_copies(m):
                c.wait()
            return carry

        lax.fori_loop(0, HOMES, wait, 0)
        lse_copy.wait()
        unpack_pairs(qst, 0, qf, 1.0 / math.sqrt(HD))

        def prepare(i, carry):
            c, t = i // 12, pl.multiple_of(lax.rem(i, 12) * 128, 128)
            k2, v2 = keys_and_values(kvf[c, pl.ds(t, 128), :])
            kc[c, pl.ds(t, 128), :] = k2.astype(BF16)
            vc[c, pl.ds(t, 128), :] = v2.astype(BF16)
            kt[c, :, pl.ds(t, 128)] = k2.T.astype(BF16)
            return carry

        lax.fori_loop(0, 48, prepare, 0)

        def prepare_q(i, carry):
            c, t = i // 12, pl.multiple_of(lax.rem(i, 12) * 128, 128)
            qc[c, pl.ds(t, 128), :] = query_quads(qf[c, pl.ds(t, 128), :])
            return carry

        lax.fori_loop(0, 24, prepare_q, 0)

    keys4, e4, (qc4, qv4) = class_facts4(o4, b)
    kc5, kv5 = lax.rem(o5, 4), o5 // 4
    qi4, qi5 = qc4 - 2 * b, lax.rem(kc5, 2)

    @pl.when(active)
    def _():
        for blk in range(4):
            r = slice(128 * blk, 128 * blk + 128)
            for e in range(2):
                c, v = keys4[e]
                k2, v2 = keys_and_values(kvf[c, pl.ds(v + 384 * blk, 128, stride=3), :])
                k4[e, r, :] = k2.astype(BF16)
                v4[e, r, :] = v2.astype(BF16)
                kt4[e, :, r] = k2.T.astype(BF16)
            q4[r, :] = query_quads(qf[qi4, pl.ds(qv4 + 384 * blk, 128, stride=3), :])
            rows = pl.ds(kv5 + 384 * blk, 128, stride=3)
            k2, v2 = keys_and_values(kvf[kc5, rows, :])
            k5[r, :] = k2.astype(BF16)
            v5[r, :] = v2.astype(BF16)
            kt5[:, r] = k2.T.astype(BF16)
            q5[r, :] = query_quads(qf[qi5, rows, :])
        dk[...] = jnp.zeros_like(dk)

    big.early(0)
    big.early(1)

    @pl.when(active)
    def _():
        def arrive(m, carry):
            pltpu.make_async_copy(drec.at[m], drec.at[m], drecv.at[m]).wait()
            return carry

        lax.fori_loop(0, HOMES, arrive, 0)
        unpack_pairs(drec, 0, df, 1.0)

        def facts(m, carry):
            ci = lax.rem(m, 2)
            t = pl.multiple_of((m // 2) * ROWS, 32)
            prod = drec[m] * ap[m]
            low = lower_lanes(prod)
            d0 = jnp.sum(jnp.where(low, prod, 0.0), -1, keepdims=True)
            d1 = jnp.sum(jnp.where(low, 0.0, prod), -1, keepdims=True)
            for part, d in ((0, d0), (1, d1)):
                rows = pl.ds(t + HALF * part, HALF)
                l = X[ci, rows, :]
                X[ci, rows, :] = jnp.where(low, l, jnp.broadcast_to(d, l.shape))
            return carry

        lax.fori_loop(0, HOMES, facts, 0)

        def turned(v):
            w = v.T
            return jnp.concatenate([w[0:1, :], w[HD : HD + 1, :]], 0)

        def prepare_d(i, carry):
            c, t = i // 12, pl.multiple_of(lax.rem(i, 12) * 128, 128)
            rows = pl.ds(t, 128)
            dc[c, rows, :] = query_quads(df[c, rows, :])
            lt[i] = turned(X[c, rows, :])
            return carry

        lax.fori_loop(0, 24, prepare_d, 0)
        for blk in range(4):
            r = slice(128 * blk, 128 * blk + 128)
            rows = pl.ds(qv4 + 384 * blk, 128, stride=3)
            d4[r, :] = query_quads(df[qi4, rows, :])
            lt4[blk] = turned(X[qi4, rows, :])
            rows = pl.ds(kv5 + 384 * blk, 128, stride=3)
            d5[r, :] = query_quads(df[qi5, rows, :])
            lt5[blk] = turned(X[qi5, rows, :])
        dv[...] = jnp.zeros_like(dv)

    big.step(2)

    def tile(g, k, v, kT, q, d, facts_pair, bias, first):
        s_ = dot_nt(doubled(k), q)
        if bias is not None:
            s_ = s_ + bias[...]
        l0, l1 = facts_pair
        row = jnp.concatenate([l0[0:1, :], l1[0:1, :]], 1)
        delta = jnp.concatenate([l0[1:2, :], l1[1:2, :]], 1)
        pr = jnp.exp(s_ - row)
        ds = pr * (dot_nt(doubled(v), d) - delta)
        hi, lo = split(pr)
        dv_new = dot_nn(hi, d) + dot_nn(lo, d)
        hi, lo = split(ds)
        dk_new = dot_nn(hi, q) + dot_nn(lo, q)
        dq_new = dot_nn(kT, hi) + dot_nn(kT, lo)
        dqt[g] = dq_new if first else dqt[g] + dq_new
        return dk_new[:, :128] + dk_new[:, 128:], dv_new[:, :128] + dv_new[:, 128:]

    def q1(qb, carry):
        def at(g, blk):
            return pl.ds(pl.multiple_of(512 * g + 128 * blk, 128), 128)

        def step(kb, bias, first):
            for g in range(3):
                ks, qs = at(g, kb), at(g, qb)
                kT = jnp.concatenate([kt[c, :, ks] for c in range(4)], 1)
                a, c = tile(
                    g,
                    kc[:, ks, :].reshape(512, 128),
                    vc[:, ks, :].reshape(512, 128),
                    kT,
                    qc[:, qs, :].reshape(256, 256),
                    dc[:, qs, :].reshape(256, 256),
                    (lt.at[4 * g + qb], lt.at[12 + 4 * g + qb]),
                    bias,
                    first,
                )
                dk[:, ks, :] += a.reshape(4, 128, 128)
                dv[:, ks, :] += c.reshape(4, 128, 128)

        step(qb, b1, True)

        def more(kb, inner):
            step(kb, None, False)
            return inner

        lax.fori_loop(0, qb, more, 0)
        for g in range(3):
            dq[:, at(g, qb), :] = dqt[g].T.reshape(2, 128, 128)
        return carry

    @pl.when(active)
    def _():
        lax.fori_loop(0, 3, q1, 0)

    big.step(3)

    @pl.when(active)
    def _():
        lax.fori_loop(3, 4, q1, 0)

    def at256(blk):
        return pl.ds(pl.multiple_of(256 * blk, 128), 256)

    def kept(flag, v):
        return jnp.where(flag, v, 0.0)

    def q2(qb, carry):
        def step(kb, bias, first):
            ks, qs = at256(kb), at256(qb)
            a, c = tile(
                0,
                jnp.concatenate([kc[o2, ks, :], kc[o2 + 2, ks, :]], 0),
                jnp.concatenate([vc[o2, ks, :], vc[o2 + 2, ks, :]], 0),
                jnp.concatenate([kt[o2, :, ks], kt[o2 + 2, :, ks]], 1),
                qc[o2, qs, :],
                dc[o2, qs, :],
                (lt.at[12 * o2 + 2 * qb], lt.at[12 * o2 + 2 * qb + 1]),
                bias,
                first,
            )
            for par in range(2):
                f = o2 == par
                dk[par, ks, :] += kept(f, a[:256])
                dk[par + 2, ks, :] += kept(f, a[256:])
                dv[par, ks, :] += kept(f, c[:256])
                dv[par + 2, ks, :] += kept(f, c[256:])

        step(qb, b2, True)

        def more(kb, inner):
            step(kb, None, False)
            return inner

        lax.fori_loop(jnp.where(qb >= 4, 4, 0), qb, more, 0)
        for par in range(2):
            dq[par, at256(qb), :] += kept(o2 == par, dqt[0].T)
        return carry

    @pl.when(active)
    def _():
        lax.fori_loop(0, TOTAL // 256, q2, 0)

    big.step(4)

    def q3(qb, carry):
        ci = lax.rem(o3, 2)

        def step(kb, bias, first):
            ks, qs = at256(kb), at256(qb)
            a, c = tile(
                0,
                kc[o3, ks, :],
                vc[o3, ks, :],
                kt[o3, :, ks],
                qc[ci, qs, :],
                dc[ci, qs, :],
                (lt.at[12 * ci + 2 * qb], lt.at[12 * ci + 2 * qb + 1]),
                bias,
                first,
            )
            for i in range(2):
                f = o3 == 2 * b + i
                dk[2 * b + i, ks, :] += kept(f, a)
                dv[2 * b + i, ks, :] += kept(f, c)

        step(qb, b3, True)

        def more(kb, inner):
            step(kb, None, False)
            return inner

        lax.fori_loop(0, qb, more, 0)
        for i in range(2):
            dq[i, at256(qb), :] += kept(o3 == 2 * b + i, dqt[0].T)
        return carry

    @pl.when(active)
    def _():
        lax.fori_loop(0, TOTAL // 256, q3, 0)

    big.step(5)

    @pl.when(active)
    def _():
        for ref in (dk4, dv4, dk5, dv5):
            ref[...] = jnp.zeros_like(ref)
        for qb in range(2):
            qs = slice(256 * qb, 256 * qb + 256)
            for kb in range(qb, -1, -1):
                ks = slice(256 * kb, 256 * kb + 256)
                a, c = tile(
                    0,
                    k4[:, ks, :].reshape(512, 128),
                    v4[:, ks, :].reshape(512, 128),
                    jnp.concatenate([kt4[0, :, ks], kt4[1, :, ks]], 1),
                    q4[qs, :],
                    d4[qs, :],
                    (lt4.at[2 * qb], lt4.at[2 * qb + 1]),
                    b4 if kb == qb else None,
                    kb == qb,
                )
                dk4[:, ks, :] += a.reshape(2, 256, 128)
                dv4[:, ks, :] += c.reshape(2, 256, 128)
                a, c = tile(
                    1,
                    k5[ks, :],
                    v5[ks, :],
                    kt5[:, ks],
                    q5[qs, :],
                    d5[qs, :],
                    (lt5.at[2 * qb], lt5.at[2 * qb + 1]),
                    b3 if kb == qb else None,
                    kb == qb,
                )
                dk5[ks, :] += a
                dv5[ks, :] += c
            dq4[qs, :] = dqt[0].T
            dq5[qs, :] = dqt[1].T
        mine5 = kc5 // 2 == b
        for kind in range(12):
            c, rows = kind % 4, pl.ds(kind // 4, THIRD, stride=3)
            f0, f1, f5 = o4 == kind, o4 + 6 == kind, jnp.logical_and(o5 == kind, mine5)
            dk[c, rows, :] += kept(f0, dk4[0]) + kept(f1, dk4[1]) + kept(f5, dk5[...])
            dv[c, rows, :] += kept(f0, dv4[0]) + kept(f1, dv4[1]) + kept(f5, dv5[...])
        for ci in range(2):
            for v in range(3):
                rows = pl.ds(v, THIRD, stride=3)
                f4 = jnp.logical_and(qi4 == ci, qv4 == v)
                f5 = jnp.logical_and(jnp.logical_and(qi5 == ci, kv5 == v), mine5)
                dq[ci, rows, :] += kept(f4, dq4[...]) + kept(f5, dq5[...])

    def passed(m):
        return remote(ds_out.at[m], came.at[m], fsend.at[m], frecv.at[m], place.peer)

    def home_copies(m):
        q, t = home_device(core, m)
        kv = remote(came.at[m], grec.at[head, pl.ds(0, ROWS), :], send.at[m], recv.at[head], to(q, t))
        dq_ = remote(dqp.at[m], grec.at[head, pl.ds(ROWS, HALF), :], qsend.at[m], qrecv.at[head], to(q, t))
        return q, t, kv, dq_

    @pl.when(active)
    def _():
        def rows_of(m):
            return pl.ds(pl.multiple_of((m // 2) * ROWS, 64), ROWS)

        def kv(c, m):
            return pick(dk[c, rows_of(m), :], dv[c, rows_of(m), :])

        def share(m, carry):
            ds_out[m] = kv(2 * (1 - b) + lax.rem(m, 2), m)
            passed(m).start()
            return carry

        lax.fori_loop(0, HOMES, share, 0)

        def add(m, carry):
            q, t, far_kv, far_q = home_copies(m)
            ci = lax.rem(m, 2)
            v = dq[ci, rows_of(m), :]
            v = (v + swap(v)) * (1.0 / math.sqrt(HD))
            dqp[m] = pick(v[:HALF], v[HALF:])
            passed(m).wait_recv()
            came[m] += kv(2 * b + ci, m)

            @pl.when(same(p, s, q, t))
            def _():
                pltpu.make_async_copy(came.at[m], grec.at[head, pl.ds(0, ROWS), :], recv.at[head]).start()
                pltpu.make_async_copy(dqp.at[m], grec.at[head, pl.ds(ROWS, HALF), :], qrecv.at[head]).start()

            @pl.when(jnp.logical_not(same(p, s, q, t)))
            def _():
                far_kv.start()
                far_q.start()

            return carry

        lax.fori_loop(0, HOMES, add, 0)

    for tau in range(6, big.pairs + 6):
        big.step(tau)

    def from_head(h, carry):
        a = grec.at[h, pl.ds(0, ROWS), :]
        c = grec.at[h, pl.ds(ROWS, HALF), :]
        pltpu.make_async_copy(a, a, recv.at[h]).wait()
        pltpu.make_async_copy(c, c, qrecv.at[h]).wait()
        return carry

    lax.fori_loop(0, HEADS, from_head, 0)
    big.finish()

    @pl.when(active)
    def _():
        def sent(m, carry):
            q, t, far_kv, far_q = home_copies(m)
            passed(m).wait_send()

            @pl.when(jnp.logical_not(same(p, s, q, t)))
            def _():
                far_kv.wait_send()
                far_q.wait_send()

            return carry

        lax.fori_loop(0, HOMES, sent, 0)

    def da_sent(h, carry):
        q, t, far = da_copy(h)

        @pl.when(jnp.logical_not(same(p, s, q, t)))
        def _():
            far.wait_send()

        return carry

    lax.fori_loop(0, HEADS, da_sent, 0)


def backward_all(offs, dap, own, sib, ap, lse, G, cid):
    dma = pltpu.SemaphoreType.DMA
    keys = pltpu.VMEM((4, TOTAL, 128), BF16)
    full = pltpu.VMEM((4, TOTAL, 128), F32)
    quad = pltpu.VMEM((2, TOTAL, 256), BF16)
    quad3 = pltpu.VMEM((THIRD, 256), BF16)
    pair3 = pltpu.VMEM((THIRD, 128), BF16)
    turned = pltpu.VMEM((128, THIRD), BF16)
    facts3 = pltpu.VMEM((4, 2, 128), F32)
    out3 = pltpu.VMEM((THIRD, 128), F32)
    packs = pltpu.VMEM((HOMES, ROWS, 128), F32)
    halves = pltpu.VMEM((HOMES, HALF, 128), F32)
    return pl.pallas_call(
        back_all_kernel,
        out_shape=[
            jax.ShapeDtypeStruct((HEADS, PACK, 128), F32),
            jax.ShapeDtypeStruct((PIECE, D), F32),
            jax.ShapeDtypeStruct((PIECE, FF), F32),
            jax.ShapeDtypeStruct((4 * PIECE, D), F32),
        ],
        in_specs=[SM, ANY, ANY, ANY, VM, ANY, ANY],
        out_specs=[ANY, VM, VM, VM],
        scratch_shapes=[
            halves,
            halves,
            keys,
            keys,
            pltpu.VMEM((4, 128, TOTAL), BF16),
            quad,
            quad,
            pltpu.VMEM((24, 2, 128), F32),
            pltpu.VMEM((2, THIRD, 128), BF16),
            pltpu.VMEM((2, THIRD, 128), BF16),
            pltpu.VMEM((2, 128, THIRD), BF16),
            quad3,
            quad3,
            facts3,
            pair3,
            pair3,
            turned,
            quad3,
            quad3,
            facts3,
            pltpu.VMEM((3, 128, 256), F32),
            full,
            full,
            pltpu.VMEM((2, TOTAL, 128), F32),
            pltpu.VMEM((2, THIRD, 128), F32),
            pltpu.VMEM((2, THIRD, 128), F32),
            out3,
            out3,
            out3,
            out3,
            pltpu.VMEM((512, 256), F32),
            pltpu.VMEM((512, 256), F32),
            pltpu.VMEM((256, 256), F32),
            pltpu.VMEM((512, 256), F32),
            packs,
            packs,
            dma((HOMES + 1, 3)),
            dma((HEADS,)),
            dma((HOMES,)),
            dma((HOMES,)),
            dma((HEADS,)),
            dma((HOMES,)),
            dma((HEADS,)),
            dma((HOMES,)),
            dma((HOMES,)),
        ]
        + Reducer.scratch(N_FF),
        compiler_params=params(collective_id=cid, has_side_effects=True),
    )(offs, dap, own, sib, ap, lse, G)


SEG1, SEG2, SEG3, SEG4, SEG5 = SEGMENTS
DILATION_ONE, DILATION_TWO, DILATION_THREE, DILATION_FOUR, DILATION_FIVE = DILATIONS
MASK_VALUE = -1e30
MATMUL_ACCURACY = lax.Precision.HIGHEST


def passed_along(value, axis, by):
    length = lax.axis_size(axis)
    return lax.ppermute(value, axis, [(i, (i + by) % length) for i in range(length)])


def run_is_live(distance, anchor_point, sequence_width, segment_length):
    return (anchor_point - (distance - 1) * sequence_width - 1) // segment_length == anchor_point // segment_length


def layer_norm(x, gain_vec):
    average = jnp.mean(x, -1, keepdims=True)
    centred = x - average
    variance = jnp.mean(centred * centred, -1, keepdims=True)
    return centred * lax.rsqrt(variance + LN_EPSILON) * gain_vec


def select_table(offsets_row, dilation_rate):
    return (jnp.arange(dilation_rate, dtype=jnp.int32)[:, None] == offsets_row[None, :]).astype(
        jnp.float32
    )


def spread_apart(x, select_option, dilation_rate):
    shaped = x.reshape(x.shape[0] // dilation_rate, dilation_rate, x.shape[1], x.shape[2])
    return jnp.einsum("trhd,rh->thd", shaped, select_option, precision=MATMUL_ACCURACY)


def spread_scalar_rows(x, select_option, dilation_rate):
    shaped = x.reshape(x.shape[0] // dilation_rate, dilation_rate, x.shape[1])
    return jnp.einsum("trh,rh->th", shaped, select_option, precision=MATMUL_ACCURACY)


def spread_rows(x, select_option):
    return jnp.einsum("thd,rh->trhd", x, select_option, precision=MATMUL_ACCURACY).reshape(
        -1, x.shape[1], x.shape[2]
    )


def spread_scalars(x, select_option):
    return jnp.einsum("th,rh->trh", x, select_option, precision=MATMUL_ACCURACY).reshape(
        -1, x.shape[1]
    )


def masked_score_matrix(sparse_queries, key_portion, query_position, key_position, segment_length):
    score_matrix = jnp.einsum(
        "ozt,bzt->zob", sparse_queries, key_portion, precision=MATMUL_ACCURACY
    ) * (1.0 / math.sqrt(key_portion.shape[-1]))
    q_cols = query_position.T[:, :, None]
    k_cols = key_position.T[:, None, :]
    permitted_mask = (k_cols <= q_cols) & (k_cols // segment_length == q_cols // segment_length)
    return (jnp.where(permitted_mask, score_matrix, MASK_VALUE), permitted_mask)


def prepare_pattern(
    query_sequence, key_sequence, value_sequence, offsets_row, dilation_rate, anchor_point
):
    select_option = select_table(offsets_row, dilation_rate)
    sparse_queries = spread_apart(query_sequence, select_option, dilation_rate)
    sparse_key_value = jnp.stack(
        (
            spread_apart(key_sequence, select_option, dilation_rate),
            spread_apart(value_sequence, select_option, dilation_rate),
        )
    )
    query_position = (
        anchor_point
        + jnp.arange(sparse_queries.shape[0], dtype=jnp.int32)[:, None] * dilation_rate
        + offsets_row[None, :]
    )
    return (select_option, sparse_queries, sparse_key_value, query_position)


def pattern_forward_pass(
    sparse_queries,
    sparse_key_value,
    query_position,
    reach,
    segment_length,
    anchor_point,
    sequence_width,
):
    masked_logits, permitted_mask = masked_score_matrix(
        sparse_queries, sparse_key_value[0], query_position, query_position, segment_length
    )
    row_max = jnp.max(masked_logits, -1)
    softmax_weights = jnp.where(permitted_mask, jnp.exp(masked_logits - row_max[..., None]), 0.0)
    state = (
        row_max,
        jnp.sum(softmax_weights, -1),
        jnp.einsum("tlj,jtb->tlb", softmax_weights, sparse_key_value[1], precision=MATMUL_ACCURACY),
    )

    def one_run(distance, carry):
        remote_key_value, state = carry
        remote_key_value = passed_along(remote_key_value, "seq", 1)
        key_position = query_position - distance * sequence_width

        def update(state_in):
            old_max, old_sum, old_acc = state_in
            masked_remote, permitted_remote = masked_score_matrix(
                sparse_queries, remote_key_value[0], query_position, key_position, segment_length
            )
            new_max = jnp.maximum(old_max, jnp.max(masked_remote, -1))
            weights_far = jnp.where(
                permitted_remote, jnp.exp(masked_remote - new_max[..., None]), 0.0
            )
            factor = jnp.exp(old_max - new_max)
            added = jnp.einsum(
                "tlj,jtb->tlb", weights_far, remote_key_value[1], precision=MATMUL_ACCURACY
            )
            return (
                new_max,
                old_sum * factor + jnp.sum(weights_far, -1),
                old_acc * factor[..., None] + added,
            )

        def unchanged(state_in):
            return state_in

        is_live = run_is_live(distance, anchor_point, sequence_width, segment_length)
        return remote_key_value, lax.cond(is_live, update, unchanged, state)

    state = lax.fori_loop(1, reach + 1, one_run, (sparse_key_value, state))[1]
    row_max, row_sum, accumulated = state
    mixture = jnp.transpose(accumulated / row_sum[..., None], (1, 0, 2))
    log_sum = (row_max + jnp.log(row_sum)).T
    return (mixture, log_sum)


def merge_patterns(forwards, prepared_inputs):
    full_lse = []
    full_mix = []
    for pattern_spec in range(len(forwards)):
        mixture, log_sum = forwards[pattern_spec]
        select_option = prepared_inputs[pattern_spec][0]
        covered = spread_scalars(jnp.ones_like(log_sum), select_option)
        full_lse.append(spread_scalars(log_sum, select_option) + (covered - 1.0) * 1e30)
        full_mix.append(spread_rows(mixture, select_option))
    stacked = jnp.stack(full_lse)
    row_max = jnp.max(stacked, 0)
    softmax_weights = jnp.exp(stacked - row_max)
    row_sum = jnp.sum(softmax_weights, 0)
    attended = full_mix[0] * softmax_weights[0][..., None]
    for pattern_spec in range(1, len(full_mix)):
        attended = attended + full_mix[pattern_spec] * softmax_weights[pattern_spec][..., None]
    return (attended / row_sum[..., None], row_max + jnp.log(row_sum))


def pattern_backward(
    select_option,
    dilation_rate,
    segment_length,
    anchor_point,
    sparse_queries,
    sparse_key_value,
    query_position,
    reach,
    sequence_gradient,
    row_difference,
    combined_logsumexp,
):
    sequence_width = sequence_gradient.shape[0]
    sparse_gradient = spread_apart(sequence_gradient, select_option, dilation_rate)
    sparse_output_grad = spread_scalar_rows(row_difference, select_option, dilation_rate).T
    sparse_logsumexp = spread_scalar_rows(combined_logsumexp, select_option, dilation_rate).T
    inverse_square_root = 1.0 / math.sqrt(sparse_queries.shape[-1])

    def portion_gradients(key_portion, value_portion, key_position):
        masked_logits, permitted_mask = masked_score_matrix(
            sparse_queries, key_portion, query_position, key_position, segment_length
        )
        softmax_weights = jnp.where(
            permitted_mask, jnp.exp(masked_logits - sparse_logsumexp[..., None]), 0.0
        )
        value_gradient = jnp.einsum(
            "tui,utx->itx", softmax_weights, sparse_gradient, precision=MATMUL_ACCURACY
        )
        pattern_gradient = jnp.einsum(
            "ozt,bzt->zob", sparse_gradient, value_portion, precision=MATMUL_ACCURACY
        )
        score_gradient = (
            softmax_weights
            * (pattern_gradient - sparse_output_grad[..., None])
            * inverse_square_root
        )
        query_gradient = jnp.einsum(
            "hqk,khd->qhd", score_gradient, key_portion, precision=MATMUL_ACCURACY
        )
        key_gradient = jnp.einsum(
            "tui,utx->itx", score_gradient, sparse_queries, precision=MATMUL_ACCURACY
        )
        return (query_gradient, jnp.stack((key_gradient, value_gradient)))

    query_gradient, key_value_gradient = portion_gradients(
        sparse_key_value[0], sparse_key_value[1], query_position
    )

    def one_run(distance, carry):
        remote_key_value, remote_gradient, query_sum = carry
        remote_key_value = passed_along(remote_key_value, "seq", 1)
        remote_gradient = passed_along(remote_gradient, "seq", 1)
        key_position = query_position - distance * sequence_width

        def far_grads():
            part_q, part_kv = portion_gradients(remote_key_value[0], remote_key_value[1], key_position)
            return query_sum + part_q, remote_gradient + part_kv

        def no_grads():
            return query_sum, remote_gradient

        is_live = run_is_live(distance, anchor_point, sequence_width, segment_length)
        query_sum, remote_gradient = lax.cond(is_live, far_grads, no_grads)
        return remote_key_value, remote_gradient, query_sum

    _, travelled, query_gradient = lax.fori_loop(
        1, reach + 1, one_run, (sparse_key_value, key_value_gradient, query_gradient)
    )
    return (query_gradient, passed_along(travelled, "seq", -reach))


def front_part(own_rows, w_qkv, gain_attn):
    return jnp.dot(layer_norm(own_rows, gain_attn), w_qkv, precision=MATMUL_ACCURACY)


def after_part(attn_rows, own_rows, w_out, w_up, w_down, gain_inner, gain_ffn, gain_hidden):
    residual = own_rows + jnp.dot(
        layer_norm(attn_rows, gain_inner), w_out, precision=MATMUL_ACCURACY
    )
    hidden = jax.nn.gelu(
        jnp.dot(layer_norm(residual, gain_ffn), w_up, precision=MATMUL_ACCURACY), approximate=False
    )
    return residual + jnp.dot(layer_norm(hidden, gain_hidden), w_down, precision=MATMUL_ACCURACY)


def shards(
    tokens,
    w_qkv,
    w_out,
    w_up,
    w_down,
    gain_attn,
    gain_inner,
    gain_ffn,
    gain_hidden,
    offsets,
    grad_out,
):
    w_qkv = w_qkv.astype(jnp.float32)
    w_out = w_out.astype(jnp.float32)
    w_up = w_up.astype(jnp.float32)
    w_down = w_down.astype(jnp.float32)
    groups = lax.axis_size("pat")
    local_rows = tokens.shape[0]
    sequence_width = local_rows * groups
    heads_here = HEADS // groups
    own_rows = tokens.reshape(local_rows, D)
    qkv_rows, front_back = jax.vjp(front_part, own_rows, w_qkv, gain_attn)
    gathered_qkv = lax.all_to_all(
        qkv_rows.reshape(local_rows, 1, 3, HEADS, HD),
        "pat",
        split_axis=3,
        concat_axis=1,
        tiled=True,
    )
    gathered_qkv = gathered_qkv.reshape(sequence_width, 3, heads_here, HD)
    head_offsets = lax.dynamic_slice_in_dim(
        offsets, lax.axis_index("pat") * heads_here, heads_here, 1
    )
    anchor_point = lax.axis_index("seq") * sequence_width
    dilation_rates = (DILATION_ONE, DILATION_TWO, DILATION_THREE, DILATION_FOUR, DILATION_FIVE)
    segment_lengths = (SEG1, SEG2, SEG3, SEG4, SEG5)
    reaches = [
        min((segment_lengths[pattern_spec] - 2) // sequence_width + 1, lax.axis_size("seq") - 1)
        for pattern_spec in range(PATTERNS)
    ]
    prepared_inputs = []
    for pattern_spec in range(PATTERNS):
        prepared_inputs.append(
            prepare_pattern(
                gathered_qkv[:, 0],
                gathered_qkv[:, 1],
                gathered_qkv[:, 2],
                head_offsets[pattern_spec],
                dilation_rates[pattern_spec],
                anchor_point,
            )
        )
    forwards = []
    for pattern_spec in range(PATTERNS):
        select_option, sparse_queries, sparse_key_value, query_position = prepared_inputs[
            pattern_spec
        ]
        forwards.append(
            pattern_forward_pass(
                sparse_queries,
                sparse_key_value,
                query_position,
                reaches[pattern_spec],
                segment_lengths[pattern_spec],
                anchor_point,
                sequence_width,
            )
        )
    lse_sums = jnp.stack([jnp.sum(entry[1]) for entry in forwards])
    totals = lax.psum(lse_sums, ("pat", "seq"))
    full_length = sequence_width * lax.axis_size("seq")
    counts = jnp.array(
        [
            float(full_length // dilation_rates[pattern_spec] * HEADS)
            for pattern_spec in range(PATTERNS)
        ],
        jnp.float32,
    )
    log_means = totals / counts
    attended, combined_logsumexp = merge_patterns(forwards, prepared_inputs)
    returned_rows = lax.all_to_all(
        attended.reshape(local_rows, groups, heads_here, HD),
        "pat",
        split_axis=1,
        concat_axis=2,
        tiled=True,
    )
    attn_rows = returned_rows.reshape(local_rows, D)
    result, after_back = jax.vjp(
        after_part, attn_rows, own_rows, w_out, w_up, w_down, gain_inner, gain_ffn, gain_hidden
    )
    g_attn, g_resid, g_out, g_up, g_down, g_inner, g_ffn, g_hidden = after_back(
        grad_out.reshape(local_rows, D)
    )
    sequence_gradient = lax.all_to_all(
        g_attn.reshape(local_rows, 1, HEADS, HD), "pat", split_axis=2, concat_axis=1, tiled=True
    )
    sequence_gradient = sequence_gradient.reshape(sequence_width, heads_here, HD)
    row_difference = jnp.sum(sequence_gradient * attended, -1)
    q_grads = []
    kv_grads = []
    for pattern_spec in range(PATTERNS):
        select_option, sparse_queries, sparse_key_value, query_position = prepared_inputs[
            pattern_spec
        ]
        part_q, part_kv = pattern_backward(
            select_option,
            dilation_rates[pattern_spec],
            segment_lengths[pattern_spec],
            anchor_point,
            sparse_queries,
            sparse_key_value,
            query_position,
            reaches[pattern_spec],
            sequence_gradient,
            row_difference,
            combined_logsumexp,
        )
        q_grads.append(part_q)
        kv_grads.append(part_kv)
    grad_total = jnp.zeros((sequence_width, 3, heads_here, HD), jnp.float32)
    for pattern_spec in range(PATTERNS):
        select_option = prepared_inputs[pattern_spec][0]
        grad_total = grad_total + jnp.stack(
            (
                spread_rows(q_grads[pattern_spec], select_option),
                spread_rows(kv_grads[pattern_spec][0], select_option),
                spread_rows(kv_grads[pattern_spec][1], select_option),
            ),
            1,
        )
    grad_back = lax.all_to_all(
        grad_total.reshape(local_rows, groups, 3, heads_here, HD),
        "pat",
        split_axis=1,
        concat_axis=3,
        tiled=True,
    )
    g_tokens, g_qkv, g_attn_gain = front_back(grad_back.reshape(local_rows, 3 * D))
    grad_tokens = (g_resid + g_tokens).reshape(local_rows, 1, D)
    summed = (
        lax.psum_scatter(g_qkv, ("pat", "seq"), scatter_dimension=0, tiled=True),
        lax.psum_scatter(g_out, ("pat", "seq"), scatter_dimension=0, tiled=True),
        lax.psum_scatter(g_up, ("pat", "seq"), scatter_dimension=0, tiled=True),
        lax.psum_scatter(g_down, ("pat", "seq"), scatter_dimension=0, tiled=True),
        lax.psum_scatter(g_attn_gain, ("pat", "seq"), scatter_dimension=0, tiled=True),
        lax.psum_scatter(g_inner, ("pat", "seq"), scatter_dimension=0, tiled=True),
        lax.psum_scatter(g_ffn, ("pat", "seq"), scatter_dimension=0, tiled=True),
        lax.psum_scatter(g_hidden, ("pat", "seq"), scatter_dimension=0, tiled=True),
    )
    return (
        result.reshape(local_rows, 1, D),
        grad_tokens,
        summed[0],
        summed[1],
        summed[2],
        summed[3],
        summed[4],
        summed[5],
        summed[6],
        summed[7],
        log_means,
    )


def fast_shards(tokens, w_qkv, w_out, w_up, w_down, gain_attn, gain_inner, gain_ffn, gain_hidden, offsets, grad_out):
    p, s = lax.axis_index("pat"), lax.axis_index("seq")
    active, head = head_here(p, s)
    mine = lax.dynamic_slice_in_dim(offsets, head, 1, 1)[:, 0]
    info = jnp.concatenate([jnp.stack([active.astype(jnp.int32), lax.rem(p, 2).astype(jnp.int32)]), mine])

    pk, x = front(tokens, w_qkv, gain_attn)
    own, sib = to_heads(pk, True, 0)
    ap, lse, sums = attention_forward(info, own, sib)
    rec = to_homes(ap, 1)
    mixed, dap, dy1, gi_g, gf_g, gh_g, G = feed_forward(
        rec, x, grad_out, w_out, w_up, w_down, gain_inner, gain_ffn, gain_hidden
    )
    grec, g_out, g_up, g_down = backward_all(mine, dap, own, sib, ap, lse, G, 2)
    gx, S, Gq = last(grec, x, dy1, w_qkv, gain_attn, gi_g, gf_g, gh_g, sums)
    counts = [float(TOTAL * 4 // r * HEADS) for r in DILATIONS]
    g_qkv, *small = reduce_scatter(Gq, S, counts, 3)
    done = deliver(g_qkv, g_out, g_up, g_down, *small)
    return (mixed, gx, *done[:4], *(v.reshape(-1) for v in done[4:]))


def fits(mesh):
    return mesh.shape["pat"] == 4 and mesh.shape["seq"] == RUNS


def solution(mesh):
    rows = P("seq", "pat", None)
    split_rows = P(("pat", "seq"), None)
    split_one = P(("pat", "seq"))
    planned = jax.shard_map(
        fast_shards,
        mesh=mesh,
        in_specs=(rows,) + (P(),) * 9 + (rows,),
        out_specs=(rows, rows) + (split_rows,) * 4 + (split_one,) * 4 + (P(),),
        check_vma=False,
    )
    general = jax.shard_map(
        shards,
        mesh=mesh,
        in_specs=(rows,) + (P(),) * 9 + (rows,),
        out_specs=(rows, rows) + (split_rows,) * 4 + (split_one,) * 4 + (P(),),
        check_vma=False,
    )

    def layer(tokens, *rest):
        if fits(mesh) and tokens.shape[0] == TOTAL:
            return planned(tokens, *rest)
        return general(tokens, *rest)

    return layer
```

```python
import functools
import math

import jax
import jax.numpy as jnp
from jax import lax
from jax.experimental import pallas as pl
from jax.experimental.pallas import tpu as pltpu
from jax.sharding import PartitionSpec as P

D = 768
HEADS = 12
HD = 64
FF = 3072
PATTERNS = 5
SEGMENTS = (2048, 4096, 8192, 16384, 32768)
DILATIONS = (1, 2, 4, 6, 12)
LN_EPSILON = 1e-05
NEG = -1e30
F32 = jnp.float32
BF16 = jnp.bfloat16
HIGHEST = lax.Precision.HIGHEST
VMEM_LIMIT = 60 * 1024 * 1024

ROWS = 192
HALF = ROWS // 2
RUNS = 8
TOTAL = ROWS * RUNS
PACK = ROWS + HALF
HOMES = 16
THIRD = TOTAL // 3
MESH = pl.DeviceIdType.MESH


def dot_nn(a, b):
    return lax.dot_general(a, b, (((1,), (0,)), ((), ())), preferred_element_type=F32)


def dot_nt(a, b):
    return lax.dot_general(a, b, (((1,), (1,)), ((), ())), preferred_element_type=F32)


def split(v):
    hi = v.astype(BF16)
    return hi, (v - hi.astype(F32)).astype(BF16)


def split32(v):
    hi = v.astype(BF16).astype(F32)
    return hi, v - hi


def lower_lanes(v):
    return lax.broadcasted_iota(jnp.int32, v.shape, v.ndim - 1) < HD


def swap(v):
    return pltpu.roll(v, HD, v.ndim - 1)


def pick(a, b):
    return jnp.where(lower_lanes(a), a, b)


def head_place(h):
    z = h // 3
    column = lax.rem(lax.rem(h, 3) + z + 1, 4)
    return column // 2, z * 2 + lax.rem(column, 2)


def head_here(p, s):
    z = s // 2
    column = (p // 2) * 2 + lax.rem(s, 2)
    k = lax.rem(column - z + 7, 4)
    return k < 3, z * 3 + jnp.minimum(k, 2)


def whole(*_):
    return pl.BlockSpec(memory_space=pltpu.VMEM)


VM = pl.BlockSpec(memory_space=pltpu.VMEM)
ANY = pl.BlockSpec(memory_space=pl.ANY)
SM = pl.BlockSpec(memory_space=pltpu.SMEM)


def params(**kw):
    return pltpu.CompilerParams(vmem_limit_bytes=VMEM_LIMIT, **kw)


def normed(v):
    centred = v - jnp.mean(v, -1, keepdims=True)
    rs = lax.rsqrt(jnp.mean(centred * centred, -1, keepdims=True) + LN_EPSILON)
    return centred * rs, rs


def put_split(ref, v):
    hi, lo = split(v)
    n = v.shape[0]
    ref[0:n, :] = hi
    ref[n : 2 * n, :] = lo


def front_kernel(x3, w_ref, gain_ref, pk_ref, x_ref, n_ref, lhs):
    x = x3[...].reshape(ROWS, D)
    x_ref[...] = x
    n, _ = normed(x)
    n_ref[...] = n
    put_split(lhs, n * gain_ref[...][None, :])
    for jj in range(3):
        parts = []
        for kind in range(3):
            c0 = kind * D + 256 * jj
            r = dot_nn(lhs[...], w_ref[:, c0 : c0 + 256])
            parts.append(r[:ROWS] + r[ROWS:])
        for half in range(2):
            q, k, v = (a[:, 128 * half : 128 * half + 128] for a in parts)
            h = 4 * jj + 2 * half
            pk_ref[h, 0:ROWS, :] = pick(k, swap(v))
            pk_ref[h + 1, 0:ROWS, :] = pick(swap(k), v)
            top, bottom = q[:HALF], q[HALF:]
            pk_ref[h, ROWS:PACK, :] = pick(top, swap(bottom))
            pk_ref[h + 1, ROWS:PACK, :] = pick(swap(top), bottom)


def front(x, w, gain):
    return pl.pallas_call(
        front_kernel,
        out_shape=[jax.ShapeDtypeStruct((HEADS, PACK, 128), F32)] + [jax.ShapeDtypeStruct((ROWS, D), F32)] * 2,
        in_specs=[VM] * 3,
        out_specs=[VM] * 3,
        scratch_shapes=[pltpu.VMEM((2 * ROWS, D), BF16)],
        compiler_params=params(),
    )(x, w, gain)


def place_facts():
    p, s = lax.axis_index("pat"), lax.axis_index("seq")
    x, core = p // 2, lax.rem(p, 2)
    active, head = head_here(p, s)
    return p, s, x, core, active, head


def home_device(core, m):
    return core * 2 + lax.rem(m, 2), m // 2


def head_device(h, b):
    hx, hs = head_place(h)
    return hx * 2 + b, hs


def same(p, s, q, t):
    return jnp.logical_and(p == q, s == t)


def to(p, s):
    return {"pat": p, "seq": s}


def scatter_kernel(forward, pk, own, *rest):
    if forward:
        sib, send, recv, fsend, frecv = rest
    else:
        send, recv = rest
    p, s, x, core, active, head = place_facts()
    slot = s * 2 + core
    barrier = pltpu.get_barrier_semaphore()

    @pl.when(active)
    def _():
        def greet(m, carry):
            q, t = home_device(core, m)

            @pl.when(jnp.logical_not(same(p, s, q, t)))
            def _():
                pl.semaphore_signal(barrier, inc=1, device_id=to(q, t), device_id_type=MESH)

            return carry

        lax.fori_loop(0, HOMES, greet, 0)
        if forward:
            pl.semaphore_signal(barrier, inc=1, device_id=to(x * 2 + 1 - core, s), device_id_type=MESH)

    mine = jnp.logical_and(active, core == x)
    waits = HEADS - mine.astype(jnp.int32)
    if forward:
        waits = waits + active.astype(jnp.int32)
    pl.semaphore_wait(barrier, waits)

    def copy(h):
        q, t = head_device(h, x)
        return q, t, pltpu.make_async_remote_copy(
            src_ref=pk.at[h],
            dst_ref=own.at[slot],
            send_sem=send.at[h],
            recv_sem=recv.at[slot],
            device_id=to(q, t),
            device_id_type=MESH,
        )

    def start(j, carry):
        h = lax.rem(j + 3 * (s // 2) + 2 * p, HEADS)
        q, t, remote = copy(h)

        @pl.when(same(p, s, q, t))
        def _():
            pltpu.make_async_copy(pk.at[h], own.at[slot], recv.at[slot]).start()

        @pl.when(jnp.logical_not(same(p, s, q, t)))
        def _():
            remote.start()

        return carry

    lax.fori_loop(0, HEADS, start, 0)

    def passed(m):
        return pltpu.make_async_remote_copy(
            src_ref=own.at[m, pl.ds(0, ROWS), :],
            dst_ref=sib.at[m],
            send_sem=fsend.at[m],
            recv_sem=frecv.at[m],
            device_id=to(x * 2 + 1 - core, s),
            device_id_type=MESH,
        )

    @pl.when(active)
    def _():
        def arrive(m, carry):
            pltpu.make_async_copy(own.at[m], own.at[m], recv.at[m]).wait()
            if forward:
                passed(m).start()
            return carry

        lax.fori_loop(0, HOMES, arrive, 0)
        if forward:

            def finish(m, carry):
                passed(m).wait()
                return carry

            lax.fori_loop(0, HOMES, finish, 0)

    def sent(h, carry):
        q, t, remote = copy(h)

        @pl.when(jnp.logical_not(same(p, s, q, t)))
        def _():
            remote.wait_send()

        return carry

    lax.fori_loop(0, HEADS, sent, 0)


def to_heads(packets, forward, cid):
    rows = packets.shape[1]
    shapes = [jax.ShapeDtypeStruct((HOMES, rows, 128), F32)]
    sems = [pltpu.SemaphoreType.DMA((HEADS,)), pltpu.SemaphoreType.DMA((HOMES,))]
    if forward:
        shapes.append(jax.ShapeDtypeStruct((HOMES, ROWS, 128), F32))
        sems += [pltpu.SemaphoreType.DMA((HOMES,)), pltpu.SemaphoreType.DMA((HOMES,))]
    return pl.pallas_call(
        functools.partial(scatter_kernel, forward),
        out_shape=shapes,
        in_specs=[ANY],
        out_specs=[ANY] * len(shapes),
        scratch_shapes=sems,
        compiler_params=params(collective_id=cid, has_side_effects=True),
    )(packets)


def home_barrier(p, s, x, core, active, barrier, also_sibling):
    def greet(h, carry):
        q, t = head_device(h, x)

        @pl.when(jnp.logical_not(same(p, s, q, t)))
        def _():
            pl.semaphore_signal(barrier, inc=1, device_id=to(q, t), device_id_type=MESH)

        return carry

    lax.fori_loop(0, HEADS, greet, 0)

    @pl.when(active)
    def _():
        if also_sibling:
            pl.semaphore_signal(barrier, inc=1, device_id=to(x * 2 + 1 - core, s), device_id_type=MESH)
        mine = (core == x).astype(jnp.int32)
        pl.semaphore_wait(barrier, HOMES - mine + (1 if also_sibling else 0))


def gather_kernel(pk, rec, send, recv):
    p, s, x, core, active, head = place_facts()
    barrier = pltpu.get_barrier_semaphore()
    home_barrier(p, s, x, core, active, barrier, False)

    def copy(m):
        q, t = home_device(core, m)
        return q, t, pltpu.make_async_remote_copy(
            src_ref=pk.at[m],
            dst_ref=rec.at[head],
            send_sem=send.at[m],
            recv_sem=recv.at[head],
            device_id=to(q, t),
            device_id_type=MESH,
        )

    @pl.when(active)
    def _():
        def start(j, carry):
            m = lax.rem(j + 2 * s + 1, HOMES)
            q, t, remote = copy(m)

            @pl.when(same(p, s, q, t))
            def _():
                pltpu.make_async_copy(pk.at[m], rec.at[head], recv.at[head]).start()

            @pl.when(jnp.logical_not(same(p, s, q, t)))
            def _():
                remote.start()

            return carry

        lax.fori_loop(0, HOMES, start, 0)

    def arrive(h, carry):
        pltpu.make_async_copy(rec.at[h], rec.at[h], recv.at[h]).wait()
        return carry

    lax.fori_loop(0, HEADS, arrive, 0)

    @pl.when(active)
    def _():
        def sent(m, carry):
            q, t, remote = copy(m)

            @pl.when(jnp.logical_not(same(p, s, q, t)))
            def _():
                remote.wait_send()

            return carry

        lax.fori_loop(0, HOMES, sent, 0)


def to_homes(packets, cid):
    rows = packets.shape[1]
    return pl.pallas_call(
        gather_kernel,
        out_shape=jax.ShapeDtypeStruct((HEADS, rows, 128), F32),
        in_specs=[ANY],
        out_specs=ANY,
        scratch_shapes=[pltpu.SemaphoreType.DMA((HOMES,)), pltpu.SemaphoreType.DMA((HEADS,))],
        compiler_params=params(collective_id=cid, has_side_effects=True),
    )(packets)


def tile_positions(rows, columns, row_classes, column_classes, t_step, class_step):
    r = lax.broadcasted_iota(jnp.int32, (rows, columns), 0)
    q = lax.broadcasted_iota(jnp.int32, (rows, columns), 1)
    rn, qn = rows // row_classes, columns // column_classes
    return (r % rn) * t_step + (r // rn) * class_step, (q % qn) * t_step + (q // qn) * class_step


def key_bias(q_shape, k_shape, t_step, class_step, shift, keys_first):
    nq, nk = q_shape[0] * q_shape[1], k_shape[0] * k_shape[1]
    if keys_first:
        kp, qp = tile_positions(nk, nq, k_shape[0], q_shape[0], t_step, class_step)
    else:
        qp, kp = tile_positions(nq, nk, q_shape[0], k_shape[0], t_step, class_step)
    return jnp.where(kp - qp <= shift, 0.0, NEG).astype(F32)


def unpack_keys(own, sib, b, kvf):
    def one(m, carry):
        c = 2 * b + lax.rem(m, 2)
        d = 2 * (1 - b) + lax.rem(m, 2)
        t = pl.multiple_of((m // 2) * ROWS, 64)
        kvf[c, pl.ds(t, ROWS), :] = own[m, 0:ROWS, :]
        kvf[d, pl.ds(t, ROWS), :] = sib[m]
        return carry

    lax.fori_loop(0, HOMES, one, 0)


def unpack_pairs(src, first, dst, scale):
    def one(m, carry):
        t = pl.multiple_of((m // 2) * ROWS, 32)
        v = src[m, first : first + HALF, :] * scale
        w = swap(v)
        dst[lax.rem(m, 2), pl.ds(t, HALF), :] = pick(v, w)
        dst[lax.rem(m, 2), pl.ds(t + HALF, HALF), :] = pick(w, v)
        return carry

    lax.fori_loop(0, HOMES, one, 0)


def keys_and_values(kv):
    hi, lo = split32(kv)
    k2 = pick(hi, swap(lo))
    v2 = pick(swap(hi), lo)
    return k2, v2


def doubled(v):
    return jnp.concatenate([v, v], 1)


def query_quads(qq):
    hi, lo = split32(qq)
    return jnp.concatenate([hi.astype(BF16), lo.astype(BF16)], 1)


def class_facts4(o4, b):
    keys = ((lax.rem(o4, 4), o4 // 4), (lax.rem(o4 + 6, 4), (o4 + 6) // 4))
    first = (keys[0][0] // 2) == b
    query = (jnp.where(first, keys[0][0], keys[1][0]), jnp.where(first, keys[0][1], keys[1][1]))
    return keys, jnp.where(first, 0, 1), query


def forward_kernel(info, own, sib, ap, lse, sums, kvf, kc, vc, qf, qc, k4, v4, q4, k5, v5, q5, acc, mx, A, L, M, b1, b2, b3, b4):
    active = info[0] == 1
    b = info[1]
    offs = [info[2 + i] for i in range(PATTERNS)]
    sums[...] = jnp.zeros_like(sums)

    @pl.when(active)
    def _():
        ones = jnp.ones((128, 128), BF16)
        unpack_keys(own, sib, b, kvf)
        unpack_pairs(own, ROWS, qf, 1.0 / math.sqrt(HD))

        def prepare(i, carry):
            c, t = i // 12, pl.multiple_of(lax.rem(i, 12) * 128, 128)
            k2, v2 = keys_and_values(kvf[c, pl.ds(t, 128), :])
            kc[c, pl.ds(t, 128), :] = doubled(k2.astype(BF16))
            vc[c, pl.ds(t, 128), :] = jnp.concatenate([v2.astype(BF16), ones], 1)
            return carry

        lax.fori_loop(0, 48, prepare, 0)

        def prepare_q(i, carry):
            c, t = i // 12, pl.multiple_of(lax.rem(i, 12) * 128, 128)
            qc[c, pl.ds(t, 128), :] = query_quads(qf[c, pl.ds(t, 128), :])
            return carry

        lax.fori_loop(0, 24, prepare_q, 0)

        keys4, e4, (qc4, qv4) = class_facts4(offs[3], b)
        kc5, kv5 = lax.rem(offs[4], 4), offs[4] // 4
        for blk in range(4):
            r = slice(128 * blk, 128 * blk + 128)
            for e in range(2):
                c, v = keys4[e]
                k2, v2 = keys_and_values(kvf[c, pl.ds(v + 384 * blk, 128, stride=3), :])
                k4[e, r, :] = doubled(k2.astype(BF16))
                v4[e, r, :] = jnp.concatenate([v2.astype(BF16), ones], 1)
            q4[r, :] = query_quads(qf[qc4 - 2 * b, pl.ds(qv4 + 384 * blk, 128, stride=3), :])
            k2, v2 = keys_and_values(kvf[kc5, pl.ds(kv5 + 384 * blk, 128, stride=3), :])
            k5[r, :] = doubled(k2.astype(BF16))
            v5[r, :] = jnp.concatenate([v2.astype(BF16), ones], 1)
            q5[r, :] = query_quads(qf[lax.rem(kc5, 2), pl.ds(kv5 + 384 * blk, 128, stride=3), :])

        b1[...] = key_bias((2, 128), (4, 128), 4, 1, 2 * b, False)
        b2[...] = key_bias((1, 256), (2, 256), 4, 2, 2 * b, False)
        b3[...] = key_bias((1, 256), (1, 256), 1, 1, 0, False)
        b4[...] = key_bias((1, 256), (2, 256), 12, 6, 6 * e4, False)

        def tile(g, q, k, v, bias, first):
            s = dot_nt(q, k)
            if bias is not None:
                s = s + bias[...]
            top = jnp.max(s, -1, keepdims=True)
            n = k.shape[0] // 128
            if first:
                m = jnp.broadcast_to(top, (256, 128))
            else:
                old = mx[g]
                m = jnp.maximum(old, top)
            mx[g] = m
            p = jnp.exp(s - jnp.concatenate([m] * n, 1))
            hi, lo = split(p)
            new = dot_nn(hi, v) + dot_nn(lo, v)
            if first:
                acc[g] = new
            else:
                alpha = jnp.exp(old - m)
                acc[g] = acc[g] * doubled(alpha) + new

        def note(pattern, g):
            rows = mx[g] + jnp.log(acc[g][:, 128:])
            sums[pattern : pattern + 1, :] += jnp.sum(rows, 0, keepdims=True)

        def q1(qb, carry):
            def at(g, blk):
                return pl.ds(pl.multiple_of(512 * g + 128 * blk, 128), 128)

            def load_q(g):
                return qc[:, at(g, qb), :].reshape(256, 256)

            def step(kb, bias, first):
                for g in range(3):
                    k = kc[:, at(g, kb), :].reshape(512, 256)
                    v = vc[:, at(g, kb), :].reshape(512, 256)
                    tile(g, load_q(g), k, v, bias, first)

            step(qb, b1, True)

            def more(kb, inner):
                step(kb, None, False)
                return inner

            lax.fori_loop(0, qb, more, 0)
            for g in range(3):
                note(0, g)
                A[:, at(g, qb), :] = acc[g][:, :128].reshape(2, 128, 128)
                L[:, at(g, qb), :] = acc[g][:, 128:].reshape(2, 128, 128)
                M[:, at(g, qb), :] = mx[g].reshape(2, 128, 128)
            return carry

        lax.fori_loop(0, 4, q1, 0)

        def merge(g, ci, rows):
            m0, m1 = M[ci, rows, :], mx[g]
            m = jnp.maximum(m0, m1)
            w0, w1 = jnp.exp(m0 - m), jnp.exp(m1 - m)
            A[ci, rows, :] = A[ci, rows, :] * w0 + acc[g][:, :128] * w1
            L[ci, rows, :] = L[ci, rows, :] * w0 + acc[g][:, 128:] * w1
            M[ci, rows, :] = m

        def at256(blk):
            return pl.ds(pl.multiple_of(256 * blk, 128), 256)

        par = offs[1]

        def keys2(ref, blk):
            return jnp.concatenate([ref[par, at256(blk), :], ref[par + 2, at256(blk), :]], 0)

        def q2(qb, carry):
            q = qc[par, at256(qb), :]
            tile(0, q, keys2(kc, qb), keys2(vc, qb), b2, True)

            def more(kb, inner):
                tile(0, q, keys2(kc, kb), keys2(vc, kb), None, False)
                return inner

            lax.fori_loop(jnp.where(qb >= 4, 4, 0), qb, more, 0)
            note(1, 0)
            merge(0, par, at256(qb))
            return carry

        lax.fori_loop(0, TOTAL // 256, q2, 0)

        o3 = offs[2]

        @pl.when(o3 // 2 == b)
        def _():
            ci = lax.rem(o3, 2)

            def q3(qb, carry):
                q = qc[ci, at256(qb), :]
                tile(0, q, kc[o3, at256(qb), :], vc[o3, at256(qb), :], b3, True)

                def more(kb, inner):
                    tile(0, q, kc[o3, at256(kb), :], vc[o3, at256(kb), :], None, False)
                    return inner

                lax.fori_loop(0, qb, more, 0)
                note(2, 0)
                merge(0, ci, at256(qb))
                return carry

            lax.fori_loop(0, TOTAL // 256, q3, 0)

        for qb in range(2):
            q = q4[256 * qb : 256 * qb + 256, :]
            for kb in range(qb, -1, -1):
                ks = slice(256 * kb, 256 * kb + 256)
                k = k4[:, ks, :].reshape(512, 256)
                v = v4[:, ks, :].reshape(512, 256)
                tile(qb, q, k, v, b4 if kb == qb else None, kb == qb)
            note(3, qb)
            merge(qb, qc4 - 2 * b, pl.ds(qv4 + 768 * qb, 256, stride=3))

        @pl.when(kc5 // 2 == b)
        def _():
            for qb in range(2):
                q = q5[256 * qb : 256 * qb + 256, :]
                for kb in range(qb, -1, -1):
                    ks = slice(256 * kb, 256 * kb + 256)
                    tile(qb, q, k5[ks, :], v5[ks, :], b3 if kb == qb else None, kb == qb)
                note(4, qb)
                merge(qb, lax.rem(kc5, 2), pl.ds(kv5 + 768 * qb, 256, stride=3))

        def finish(m, carry):
            ci = lax.rem(m, 2)
            t = pl.multiple_of((m // 2) * ROWS, 64)
            rows = pl.ds(t, ROWS)
            a, l = A[ci, rows, :], L[ci, rows, :]
            out = (a + swap(a)) / l
            ap[m] = pick(out[:HALF], out[HALF:])
            lse[ci, rows, :] = M[ci, rows, :] + jnp.log(l)
            return carry

        lax.fori_loop(0, HOMES, finish, 0)


def attention_forward(info, own, sib):
    big = pltpu.VMEM((4, TOTAL, 256), BF16)
    state = pltpu.VMEM((2, TOTAL, 128), F32)
    return pl.pallas_call(
        forward_kernel,
        out_shape=[
            jax.ShapeDtypeStruct((HOMES, HALF, 128), F32),
            jax.ShapeDtypeStruct((2, TOTAL, 128), F32),
            jax.ShapeDtypeStruct((8, 128), F32),
        ],
        in_specs=[SM, VM, VM],
        out_specs=[VM, VM, VM],
        scratch_shapes=[
            pltpu.VMEM((4, TOTAL, 128), F32),
            big,
            big,
            state,
            pltpu.VMEM((2, TOTAL, 256), BF16),
            pltpu.VMEM((2, THIRD, 256), BF16),
            pltpu.VMEM((2, THIRD, 256), BF16),
            pltpu.VMEM((THIRD, 256), BF16),
            pltpu.VMEM((THIRD, 256), BF16),
            pltpu.VMEM((THIRD, 256), BF16),
            pltpu.VMEM((THIRD, 256), BF16),
            pltpu.VMEM((3, 256, 256), F32),
            pltpu.VMEM((3, 256, 128), F32),
            state,
            state,
            state,
            pltpu.VMEM((256, 512), F32),
            pltpu.VMEM((256, 512), F32),
            pltpu.VMEM((256, 256), F32),
            pltpu.VMEM((256, 512), F32),
        ],
        compiler_params=params(),
    )(info, own, sib)


def rows_from_pairs(rec, dst):
    for j in range(HEADS // 2):
        u, v = rec[2 * j], rec[2 * j + 1]
        cols = slice(128 * j, 128 * j + 128)
        dst[0:HALF, cols] = pick(u, swap(v))
        dst[HALF:ROWS, cols] = pick(swap(u), v)


def pairs_from_rows(src, dst):
    for j in range(HEADS // 2):
        top = src[0:HALF, 128 * j : 128 * j + 128]
        bottom = src[HALF:ROWS, 128 * j : 128 * j + 128]
        dst[2 * j] = pick(top, swap(bottom))
        dst[2 * j + 1] = pick(swap(top), bottom)


def halves_sum(r):
    return r[:ROWS] + r[ROWS:]


def norm_back(f, n, rs):
    return (f - jnp.mean(f, -1, keepdims=True) - n * jnp.mean(f * n, -1, keepdims=True)) * rs


def put_turned(hi_ref, lo_ref, v):
    for j in range(D // 128):
        t = v[:, 128 * j : 128 * j + 128].T
        hi, lo = split(t)
        hi_ref[128 * j : 128 * j + 128, :] = hi
        lo_ref[128 * j : 128 * j + 128, :] = lo


FT = 512


class Spill:
    def __init__(self, tiles, sem):
        self.tiles, self.sem, self.count, self.open = tiles, sem, 0, [[], []]

    def emit(self, fill, copies):
        k = self.count % 2
        for c in self.open[k]:
            c.wait()
        fill(self.tiles.at[k])
        self.open[k] = copies(self.tiles.at[k], self.sem.at[k])
        for c in self.open[k]:
            c.start()
        self.count += 1

    def close(self):
        for k in range(2):
            for c in self.open[k]:
                c.wait()
            self.open[k] = []


def product(hi, lo, r_hi, r_lo, tile):
    def one(i, carry):
        rows = pl.ds(pl.multiple_of(i * 128, 128), 128)
        h, l = hi[rows, :], lo[rows, :]
        tile[rows, :] = dot_nn(h, r_hi[...]) + dot_nn(h, r_lo[...]) + dot_nn(l, r_hi[...])
        return carry

    lax.fori_loop(0, D // 128, one, 0)


def column_copies(G, chunk):
    def make(tile, sem):
        return [
            pltpu.make_async_copy(
                tile.at[pl.ds(24 * d, 24), :], G.at[d // 16, (d // 8) % 2, (d % 8) // 2, d % 2, chunk], sem.at[d]
            )
            for d in range(32)
        ]

    return make


def row_copies(G, part, chunk):
    def make(tile, sem):
        return [
            pltpu.make_async_copy(
                tile.at[pl.ds(24 * d, 24), :], G.at[part // 2, part % 2, d // 8, (d // 4) % 2, chunk + d % 4], sem.at[d]
            )
            for d in range(32)
        ]

    return make


def ff_kernel(rec, x_ref, g3, wo, wu, wd, gi1, gf1, gh1, sums, out3, dap, dy1_ref, S, G, lhs, lhs2, gi, gf, gh, gh_g, g_ref, out_ref, V, N1, U, GP, E, ACC, th, tl, r_hi, r_lo, tiles, sem):
    spill = Spill(tiles, sem)
    for wide, flat in ((gi, gi1), (gf, gf1), (gh, gh1)):
        wide[...] = flat[...][None, :]
    g_ref[...] = g3[...].reshape(ROWS, D)
    rows_from_pairs(rec, V)
    na, rs_a = normed(V[...])
    V[...] = na
    put_split(lhs, na * gi[...])
    for j in range(3):
        cols = slice(256 * j, 256 * j + 256)
        N1[:, cols] = x_ref[:, cols] + halves_sum(dot_nn(lhs[...], wo[:, cols]))
    y1 = N1[...]
    out_ref[...] = y1
    ny, rs_y = normed(y1)
    N1[...] = ny
    put_split(lhs, ny * gf[...])

    def up(j, su):
        cols = pl.ds(pl.multiple_of(j * FT, FT), FT)
        z = halves_sum(dot_nn(lhs[...], wu[:, cols]))
        phi = 0.5 * (1.0 + lax.erf(z * math.sqrt(0.5)))
        u = z * phi
        U[:, cols] = u
        GP[:, cols] = phi + z * jnp.exp(-0.5 * z * z) * (1.0 / math.sqrt(2.0 * math.pi))
        return su + jnp.sum(u, -1, keepdims=True)

    zero = jnp.zeros((ROWS, 1), F32)
    mean = lax.fori_loop(0, FF // FT, up, zero) * (1.0 / FF)

    def spread(j, sv):
        cols = pl.ds(pl.multiple_of(j * FT, FT), FT)
        c = U[:, cols] - mean
        return sv + jnp.sum(c * c, -1, keepdims=True)

    rs_u = lax.rsqrt(lax.fori_loop(0, FF // FT, spread, zero) * (1.0 / FF) + LN_EPSILON)
    ACC[...] = jnp.zeros_like(ACC)

    def lower(j, carry):
        cols = pl.ds(pl.multiple_of(j * FT, FT), FT)
        n = (U[:, cols] - mean) * rs_u
        U[:, cols] = n
        put_split(lhs2, n * gh[:, cols])
        ACC[...] += halves_sum(dot_nn(lhs2[...], wd[cols, :]))
        return carry

    lax.fori_loop(0, FF // FT, lower, 0)
    out3[...] = (out_ref[...] + ACC[...]).reshape(ROWS, 1, D)

    put_split(lhs, g_ref[...])

    def back_down(j, sums):
        cols = pl.ds(pl.multiple_of(j * FT, FT), FT)
        e = halves_sum(dot_nt(lhs[...], wd[cols, :]))
        n = U[:, cols]
        gh_g[:, cols] = jnp.sum(e * n, 0, keepdims=True)
        f = e * gh[:, cols]
        E[:, cols] = f
        return sums[0] + jnp.sum(f, -1, keepdims=True), sums[1] + jnp.sum(f * n, -1, keepdims=True)

    sf, sfn = lax.fori_loop(0, FF // FT, back_down, (zero, zero))
    mf, mfn = sf * (1.0 / FF), sfn * (1.0 / FF)
    ACC[...] = jnp.zeros_like(ACC)

    def back_up(j, carry):
        cols = pl.ds(pl.multiple_of(j * FT, FT), FT)
        dz = (E[:, cols] - mf - U[:, cols] * mfn) * rs_u * GP[:, cols]
        E[:, cols] = dz
        put_split(lhs2, dz)
        ACC[...] += halves_sum(dot_nt(lhs2[...], wu[:, cols]))
        return carry

    lax.fori_loop(0, FF // FT, back_up, 0)
    e = ACC[...]
    ny = N1[...]
    S[2:3, :] = jnp.sum(e * ny, 0, keepdims=True)
    dy1 = g_ref[...] + norm_back(e * gf[...], ny, rs_y)
    dy1_ref[...] = dy1
    put_split(lhs, dy1)
    for j in range(3):
        cols = slice(256 * j, 256 * j + 256)
        ACC[:, cols] = halves_sum(dot_nt(lhs[...], wo[cols, :]))
    e = ACC[...]
    na = V[...]
    S[1:2, :] = jnp.sum(e * na, 0, keepdims=True)
    S[0:1, :] = jnp.zeros((1, D), F32)
    for j in range(4):
        S[3 + j : 4 + j, :] = gh_g[:, D * j : D * j + D]
    lane = lax.broadcasted_iota(jnp.int32, (1, 128), 1)
    S[7:8, :] = jnp.zeros((1, D), F32)
    S[7:8, 0:128] = sum(jnp.where(lane == i, sums[i : i + 1, :], 0.0) for i in range(PATTERNS))
    ACC[...] = norm_back(e * gi[...], na, rs_a)
    pairs_from_rows(ACC, dap)

    put_turned(th, tl, na * gi[...])
    r_hi[...], r_lo[...] = split(dy1)
    spill.emit(lambda t: product(th, tl, r_hi, r_lo, t), column_copies(G, 0))
    put_turned(th, tl, ny * gf[...])
    for j in range(4):
        r_hi[...], r_lo[...] = split(E[:, D * j : D * j + D])
        spill.emit(lambda t: product(th, tl, r_hi, r_lo, t), column_copies(G, 1 + j))
    r_hi[...], r_lo[...] = split(g_ref[...])
    for j in range(4):
        cols = slice(D * j, D * j + D)
        put_turned(th, tl, U[:, cols] * gh[:, cols])
        spill.emit(lambda t: product(th, tl, r_hi, r_lo, t), row_copies(G, j, 5))
    spill.close()


PIECE = 24


def grad_shape(n):
    return jax.ShapeDtypeStruct((2, 2, 4, 2, n, PIECE, D), F32)


def tile_scratch():
    return [
        pltpu.VMEM((D, ROWS), BF16),
        pltpu.VMEM((D, ROWS), BF16),
        pltpu.VMEM((ROWS, D), BF16),
        pltpu.VMEM((ROWS, D), BF16),
        pltpu.VMEM((2, D, D), F32),
        pltpu.SemaphoreType.DMA((2, 32)),
    ]


def feed_forward(rec, x, g, wo, wu, wd, gi, gf, gh, sums):
    act = jax.ShapeDtypeStruct((ROWS, D), F32)
    wide = pltpu.VMEM((ROWS, FF), F32)
    thin = pltpu.VMEM((ROWS, D), F32)
    return pl.pallas_call(
        ff_kernel,
        out_shape=[
            jax.ShapeDtypeStruct((ROWS, 1, D), F32),
            jax.ShapeDtypeStruct((HEADS, HALF, 128), F32),
            act,
            jax.ShapeDtypeStruct((8, D), F32),
            grad_shape(9),
        ],
        in_specs=[VM] * 10,
        out_specs=[VM] * 4 + [ANY],
        scratch_shapes=[
            pltpu.VMEM((2 * ROWS, D), BF16),
            pltpu.VMEM((2 * ROWS, FT), BF16),
            pltpu.VMEM((1, D), F32),
            pltpu.VMEM((1, D), F32),
            pltpu.VMEM((1, FF), F32),
            pltpu.VMEM((1, FF), F32),
            thin,
            thin,
            thin,
            thin,
            wide,
            wide,
            wide,
            thin,
        ]
        + tile_scratch(),
        compiler_params=params(),
    )(rec, x, g, wo, wu, wd, gi, gf, gh, sums)


def last_kernel(rec, zrec, x_ref, dy1_ref, w, ga1, *refs):
    n_same = 7
    same_in, (gx, g_qkv, ga_g), same_out = refs[:n_same], refs[n_same : n_same + 3], refs[n_same + 3 : 2 * n_same + 3]
    dqkv, lhs, rows32 = refs[2 * n_same + 3 :]
    for src, dst in zip(same_in, same_out):
        dst[...] = src[...]
    for j in range(HEADS // 2):
        u, v = rec[2 * j, ROWS:PACK, :], rec[2 * j + 1, ROWS:PACK, :]
        cols = slice(128 * j, 128 * j + 128)
        dqkv[0:HALF, cols] = pick(u, swap(v))
        dqkv[HALF:ROWS, cols] = pick(swap(u), v)
        u, v = rec[2 * j, 0:ROWS, :], rec[2 * j + 1, 0:ROWS, :]
        dqkv[:, D + 128 * j : D + 128 * j + 128] = pick(u, swap(v))
        dqkv[:, 2 * D + 128 * j : 2 * D + 128 * j + 128] = pick(swap(u), v)
    ga = ga1[...][None, :]
    n, rs = normed(x_ref[...])
    e = None
    for j in range(3):
        cols = slice(D * j, D * j + D)
        put_split(lhs, dqkv[:, cols])
        more = halves_sum(dot_nt(lhs[...], w[:, cols]))
        e = more if e is None else e + more
    gx[...] = (dy1_ref[...] + norm_back(e * ga, n, rs)).reshape(ROWS, 1, D)

    d = lax.axis_index("pat") * RUNS + lax.axis_index("seq")
    first = d * PIECE - 8 * lax.rem(d, 2)
    rows32[...] = w[pl.ds(pl.multiple_of(first, 16), 32), :].astype(F32)
    w_rows = rows32.at[pl.ds(pl.multiple_of(8 * lax.rem(d, 2), 8), PIECE), :]
    own = pltpu.roll(ga, D - PIECE * d, 1)[:, :128]
    gain = jnp.broadcast_to(own, (128, 128)).T[:PIECE]
    total = jnp.zeros((PIECE, 128), F32)
    for j in range(HEADS // 2):
        u, v = zrec[2 * j, 0], zrec[2 * j + 1, 0]
        a, c = zrec[2 * j, 1], zrec[2 * j + 1, 1]
        for kind, z in enumerate((pick(u, swap(v)), pick(swap(u), v), pick(a, swap(c)))):
            cols = slice(kind * D + 128 * j, kind * D + 128 * j + 128)
            total += w_rows[:, cols] * z
            g_qkv[:, cols] = gain * z
    column = jnp.broadcast_to(jnp.sum(total, -1, keepdims=True), (PIECE, 128))
    ga_g[...] = jnp.concatenate([column, jnp.zeros((128 - PIECE, 128), F32)], 0).T[0:1, :PIECE]


def last(rec, zrec, x, dy1, w, ga, *done):
    return pl.pallas_call(
        last_kernel,
        out_shape=[
            jax.ShapeDtypeStruct((ROWS, 1, D), F32),
            jax.ShapeDtypeStruct((PIECE, 3 * D), F32),
            jax.ShapeDtypeStruct((1, PIECE), F32),
        ]
        + [jax.ShapeDtypeStruct(v.shape, v.dtype) for v in done],
        in_specs=[VM] * (6 + len(done)),
        out_specs=[VM] * (3 + len(done)),
        scratch_shapes=[
            pltpu.VMEM((ROWS, 3 * D), F32),
            pltpu.VMEM((2 * ROWS, D), BF16),
            pltpu.VMEM((32, 3 * D), F32),
        ],
        compiler_params=params(),
    )(rec, zrec, x, dy1, w, ga, *done)


class Place:
    def __init__(self):
        p, s = lax.axis_index("pat"), lax.axis_index("seq")
        self.p, self.s = p, s
        self.x, self.core, self.z, self.y = p // 2, lax.rem(p, 2), s // 2, lax.rem(s, 2)
        self.peer = to(self.x * 2 + 1 - self.core, s)
        self.xn = to((1 - self.x) * 2 + self.core, s)
        self.yn = to(p, self.z * 2 + 1 - self.y)
        self.left, self.right = to(p, s - 2), to(p, s + 2)

    def greet(self, barrier):
        for d in (self.peer, self.xn, self.yn):
            pl.semaphore_signal(barrier, inc=1, device_id=d, device_id_type=MESH)

        @pl.when(self.z > 0)
        def _():
            pl.semaphore_signal(barrier, inc=1, device_id=self.left, device_id_type=MESH)

        @pl.when(self.z < 3)
        def _():
            pl.semaphore_signal(barrier, inc=1, device_id=self.right, device_id_type=MESH)

        return 3 + (self.z > 0).astype(jnp.int32) + (self.z < 3).astype(jnp.int32)


def remote(src, dst, a, b, d):
    return pltpu.make_async_remote_copy(
        src_ref=src, dst_ref=dst, send_sem=a, recv_sem=b, device_id=d, device_id_type=MESH
    )


class Chunk:
    def __init__(self, place, k, group, slot, own, osem, bufs, sems, put, x_first):
        self.at, self.k, self.group, self.slot, self.own, self.osem = place, k, group, slot, own, osem
        self.b0, self.b1, self.b2, self.bl, self.br = bufs
        self.sc, self.rc, self.s1, self.r1, self.s2, self.r2, self.sl, self.rl, self.sr, self.rr = sems
        self.put, self.x_first = put, x_first

    def core(self):
        k, c = self.k, 1 - self.at.core
        return [
            remote(self.group(i, c), self.b0.at[i], self.sc.at[k, i], self.rc.at[k, i], self.at.peer)
            for i in range(2)
        ]

    def load(self):
        return [
            pltpu.make_async_copy(self.group(i, self.at.core), self.own.at[i], self.osem.at[self.slot, i])
            for i in range(2)
        ]

    def one(self):
        k, at = self.k, self.at
        if self.x_first:
            return remote(self.b0.at[1 - at.x], self.b1, self.s1.at[k], self.r1.at[k], at.xn)
        return remote(self.b0.at[:, :, 1 - at.y], self.b1, self.s1.at[k], self.r1.at[k], at.yn)

    def two(self):
        k, at = self.k, self.at
        if self.x_first:
            return remote(self.b1.at[:, 1 - at.y], self.b2, self.s2.at[k], self.r2.at[k], at.yn)
        return remote(self.b1.at[1 - at.x], self.b2, self.s2.at[k], self.r2.at[k], at.xn)

    def rightward(self, i):
        k, part = self.k, pl.ds(i + 1, 3 - i)
        src = self.b2 if i == 0 else self.bl
        return remote(src.at[part], self.bl.at[part], self.sr.at[k], self.rl.at[k], self.at.right)

    def leftward(self, i):
        k, part = self.k, pl.ds(0, i)
        src = self.b2 if i == 3 else self.br
        return remote(src.at[part], self.br.at[part], self.sl.at[k], self.rr.at[k], self.at.left)

    def stage1(self):
        for c in self.load():
            c.wait()
        for c in self.core():
            c.wait_recv()
        self.b0[...] += self.own[...]
        self.one().start()

    def stage2(self):
        self.one().wait_recv()
        mine = self.b0[self.at.x] if self.x_first else self.b0[:, :, self.at.y]
        self.b1[...] += mine
        self.two().start()

    def stage3(self):
        self.two().wait_recv()
        mine = self.b1[:, self.at.y] if self.x_first else self.b1[self.at.x]
        self.b2[...] += mine

        @pl.when(self.at.z == 0)
        def _():
            self.rightward(0).start()

        @pl.when(self.at.z == 3)
        def _():
            self.leftward(3).start()

    def stage4(self):
        @pl.when(self.at.z == 1)
        def _():
            self.rightward(0).wait_recv()
            self.bl[2:4] += self.b2[2:4]
            self.rightward(1).start()

        @pl.when(self.at.z == 2)
        def _():
            self.leftward(3).wait_recv()
            self.br[0:2] += self.b2[0:2]
            self.leftward(2).start()

    def stage5(self):
        @pl.when(self.at.z == 2)
        def _():
            self.rightward(1).wait_recv()
            self.bl[3:4] += self.b2[3:4]
            self.rightward(2).start()

        @pl.when(self.at.z == 1)
        def _():
            self.leftward(2).wait_recv()
            self.br[0:1] += self.b2[0:1]
            self.leftward(1).start()

    def stage6(self):
        @pl.when(self.at.z == 3)
        def _():
            self.rightward(2).wait_recv()
            self.put(self.b2[3] + self.bl[3])

        @pl.when(self.at.z == 0)
        def _():
            self.leftward(1).wait_recv()
            self.put(self.b2[0] + self.br[0])

        @pl.when(self.at.z == 1)
        def _():
            self.put(self.b2[1] + self.bl[1] + self.br[1])

        @pl.when(self.at.z == 2)
        def _():
            self.put(self.b2[2] + self.bl[2] + self.br[2])

    def sent(self):
        for c in self.core() + [self.one(), self.two()]:
            c.wait_send()
        for i in range(4):

            @pl.when(self.at.z == i)
            def _(i=i):
                if i < 3:
                    self.rightward(i).wait_send()
                if i > 0:
                    self.leftward(i).wait_send()


class Reducer:
    def __init__(self, place, n, G, scratch, put):
        self.place, self.n, self.G, self.put = place, n, G, put
        self.own, self.c0, self.c1a, self.c1b, self.c2, self.zl, self.zr, self.osem = scratch[:8]
        self.sems = scratch[8:18]
        self.pairs = (n + 1) // 2

    @staticmethod
    def scratch(n):
        dma = pltpu.SemaphoreType.DMA
        bufs = [(4, 2, 4, 2), (n, 2, 4, 2), ((n + 1) // 2, 4, 2), (max(n // 2, 1), 2, 4), (n, 4), (n, 4), (n, 4)]
        return (
            [pltpu.VMEM(b + (PIECE, D), F32) for b in bufs]
            + [dma((4, 2)), dma((n, 2)), dma((n, 2))]
            + [dma((n,)) for _ in range(8)]
        )

    def chunk(self, k, parity):
        slot = lax.rem(k, 4)
        b1 = (self.c1b if parity else self.c1a).at[k // 2]
        return Chunk(
            self.place,
            k,
            lambda i, c: self.G.at[i, c, :, :, k],
            slot,
            self.own.at[slot],
            self.osem,
            (self.c0.at[k], b1, self.c2.at[k], self.zl.at[k], self.zr.at[k]),
            self.sems,
            lambda v: self.put(k, v),
            parity == 0,
        )

    def begin(self):
        def one(k, carry):
            for c in self.chunk(k, 0).core():
                c.start()
            return carry

        lax.fori_loop(0, self.n, one, 0)
        for k in range(min(2, self.n)):
            for c in self.chunk(jnp.int32(k), 0).load():
                c.start()

    def one(self, stage, pair):
        for parity in range(2):
            k = jnp.int32(2 * pair + parity)

            @pl.when(jnp.logical_and(k >= 0, k < self.n))
            def _(k=k, parity=parity):
                if stage == 1:

                    @pl.when(k + 2 < self.n)
                    def _():
                        for c in self.chunk(k + 2, 0).load():
                            c.start()

                getattr(self.chunk(k, parity), f"stage{stage}")()

    def early(self, pair):
        self.one(1, pair)

    def step(self, tau):
        self.one(1, tau)
        for stage in range(2, 7):
            self.one(stage, tau - stage)

    def finish(self):
        def one(k, carry):
            for parity in range(2):

                @pl.when(lax.rem(k, 2) == parity)
                def _(parity=parity):
                    self.chunk(k, parity).sent()

            return carry

        lax.fori_loop(0, self.n, one, 0)


class SmallSum:
    def __init__(self, place, S, bufs, send, recv, put):
        self.at, self.S, self.send, self.recv, self.put = place, S, send, recv, put
        self.d0, self.d1, self.d2, self.dl, self.dr, self.t1, self.t2, self.t3, self.fl, self.fr = bufs

    @staticmethod
    def scratch():
        return [pltpu.VMEM((8, D), F32)] * 10 + [pltpu.SemaphoreType.DMA((5,)), pltpu.SemaphoreType.DMA((5,))]

    def hop(self, src, dst, i, d):
        return remote(src, dst, self.send.at[i], self.recv.at[i], d)

    def core(self):
        return self.hop(self.S, self.d0, 0, self.at.peer)

    def along_x(self):
        return self.hop(self.t1, self.d1, 1, self.at.xn)

    def along_y(self):
        return self.hop(self.t2, self.d2, 2, self.at.yn)

    def rightward(self, i):
        return self.hop(self.t3 if i == 0 else self.fl, self.dl, 3, self.at.right)

    def leftward(self, i):
        return self.hop(self.t3 if i == 3 else self.fr, self.dr, 4, self.at.left)

    def stage1(self):
        self.core().wait_recv()
        self.t1[...] = self.S[...] + self.d0[...]
        self.along_x().start()

    def stage2(self):
        self.along_x().wait_recv()
        self.t2[...] = self.t1[...] + self.d1[...]
        self.along_y().start()

    def stage3(self):
        self.along_y().wait_recv()
        self.t3[...] = self.t2[...] + self.d2[...]

        @pl.when(self.at.z == 0)
        def _():
            self.rightward(0).start()

        @pl.when(self.at.z == 3)
        def _():
            self.leftward(3).start()

    def from_left(self, i):
        self.rightward(i).wait_recv()
        self.fl[...] = self.dl[...] + self.t3[...]

    def from_right(self, i):
        self.leftward(i).wait_recv()
        self.fr[...] = self.dr[...] + self.t3[...]

    def stage4(self):
        @pl.when(self.at.z == 1)
        def _():
            self.from_left(0)
            self.rightward(1).start()

        @pl.when(self.at.z == 2)
        def _():
            self.from_right(3)
            self.leftward(2).start()

    def stage5(self):
        @pl.when(self.at.z == 2)
        def _():
            self.from_left(1)
            self.rightward(2).start()

        @pl.when(self.at.z == 1)
        def _():
            self.from_right(2)
            self.leftward(1).start()

    def stage6(self):
        @pl.when(self.at.z == 3)
        def _():
            self.from_left(2)
            self.put(self.fl[...])

        @pl.when(self.at.z == 0)
        def _():
            self.from_right(1)
            self.put(self.fr[...])

        @pl.when(jnp.logical_or(self.at.z == 1, self.at.z == 2))
        def _():
            self.put(self.fl[...] + self.dr[...])

    def finish(self):
        for c in (self.core(), self.along_x(), self.along_y()):
            c.wait_send()
        for i in range(4):

            @pl.when(self.at.z == i)
            def _(i=i):
                if i < 3:
                    self.rightward(i).wait_send()
                if i > 0:
                    self.leftward(i).wait_send()


def small_outputs(place, counts, outs, tot):
    gi, gf, gh, means = outs

    def put(v):
        tot[...] = v
        d = place.p * RUNS + place.s
        for i, ref in enumerate((gi, gf)):
            ref[...] = pltpu.roll(tot[i + 1 : i + 2, :], D - PIECE * d, 1)[:, :PIECE]
        row = tot[pl.ds(3 + d // 8, 1), :]
        gh[...] = pltpu.roll(row, D - 4 * PIECE * lax.rem(d, 8), 1)[:, : 4 * PIECE]
        lane = lax.broadcasted_iota(jnp.int32, (1, 128), 1)
        scale = jnp.full((1, 128), counts[0], F32)
        for i in range(1, PATTERNS):
            scale = jnp.where(lane == i, counts[i], scale)
        means[...] = (tot[7:8, :128] / scale)[:, :PATTERNS]

    return put


N_REDUCER = 18


N_FF = 9


def back_all_kernel(counts, offs, dap, own, sib, ap, lse, G, N, S, grec, zrec, wo_g, up_g, down_g, gi_o, gf_o, gh_o, means, drec, qst, kc, vc, kt, qc, dc, lt, k4, v4, kt4, q4, d4, lt4, k5, v5, kt5, q5, d5, lt5, dqt, dk, dv, dq, dk4, dv4, dk5, dv5, dq4, dq5, b1, b2, b3, b4, ds_out, came, zc, tot, lsem, dsend, drecv, send, recv, qsend, qrecv, fsend, frecv, nsem, zsend, zrecv, osend, orecv, *scratch):
    place = Place()
    p, s, x, core, active, head = place_facts()
    b = core
    o2, o3, o4, o5 = offs[1], offs[2], offs[3], offs[4]
    kvf, qf, X, df = dk, dv.at[0:2], dv.at[2:4], dq
    dqp = qst

    barrier = pltpu.get_barrier_semaphore()
    expected = place.greet(barrier)
    expected = expected + HEADS - jnp.logical_and(active, core == x).astype(jnp.int32)

    def greet_owners(h, carry):
        q, t = head_device(h, core)

        @pl.when(jnp.logical_not(same(p, s, q, t)))
        def _():
            pl.semaphore_signal(barrier, inc=1, device_id=to(q, t), device_id_type=MESH)

        return carry

    lax.fori_loop(0, HEADS, greet_owners, 0)

    @pl.when(active)
    def _():
        def greet(m, carry):
            q, t = home_device(core, m)

            @pl.when(jnp.logical_not(same(p, s, q, t)))
            def _():
                pl.semaphore_signal(barrier, inc=1, device_id=to(q, t), device_id_type=MESH)

            return carry

        lax.fori_loop(0, HOMES, greet, 0)

    def greet_heads(h, carry):
        q, t = head_device(h, x)

        @pl.when(jnp.logical_not(same(p, s, q, t)))
        def _():
            pl.semaphore_signal(barrier, inc=1, device_id=to(q, t), device_id_type=MESH)

        return carry

    lax.fori_loop(0, HEADS, greet_heads, 0)
    from_homes = HOMES - (core == x).astype(jnp.int32)
    pl.semaphore_wait(barrier, expected + active.astype(jnp.int32) * (from_homes + HOMES - 1))

    slot = s * 2 + core

    def da_copy(h):
        q, t = head_device(h, x)
        return q, t, remote(dap.at[h], drec.at[slot], dsend.at[h], drecv.at[slot], to(q, t))

    def da_start(j, carry):
        h = lax.rem(j + 3 * (s // 2) + 2 * p, HEADS)
        q, t, far = da_copy(h)

        @pl.when(same(p, s, q, t))
        def _():
            pltpu.make_async_copy(dap.at[h], drec.at[slot], drecv.at[slot]).start()

        @pl.when(jnp.logical_not(same(p, s, q, t)))
        def _():
            far.start()

        return carry

    lax.fori_loop(0, HEADS, da_start, 0)

    def put(k, v):
        @pl.when(k == 0)
        def _():
            wo_g[...] = v

        @pl.when(jnp.logical_and(k > 0, k < 5))
        def _():
            up_g[:, pl.ds(pl.multiple_of((k - 1) * D, D), D)] = v

        @pl.when(k >= 5)
        def _():
            down_g[pl.ds(pl.multiple_of((k - 5) * PIECE, PIECE), PIECE), :] = v

    big = Reducer(place, N_FF, G, scratch[:N_REDUCER], put)
    rest = scratch[N_REDUCER:]
    small = SmallSum(
        place, S, rest[:10], rest[10], rest[11], small_outputs(place, counts, (gi_o, gf_o, gh_o, means), tot)
    )
    small.core().start()
    big.begin()

    def local_copies(m):
        t = pl.multiple_of((m // 2) * ROWS, 64)
        c, d = 2 * b + lax.rem(m, 2), 2 * (1 - b) + lax.rem(m, 2)
        return [
            pltpu.make_async_copy(own.at[m, pl.ds(0, ROWS), :], kvf.at[c, pl.ds(t, ROWS), :], lsem.at[m, 0]),
            pltpu.make_async_copy(sib.at[m], kvf.at[d, pl.ds(t, ROWS), :], lsem.at[m, 1]),
            pltpu.make_async_copy(own.at[m, pl.ds(ROWS, HALF), :], qst.at[m], lsem.at[m, 2]),
        ]

    lse_copy = pltpu.make_async_copy(lse, X, lsem.at[HOMES, 0])

    @pl.when(active)
    def _():
        lse_copy.start()

        def start(m, carry):
            for c in local_copies(m):
                c.start()
            return carry

        lax.fori_loop(0, HOMES, start, 0)
        b1[...] = key_bias((2, 128), (4, 128), 4, 1, 2 * b, True)
        b2[...] = key_bias((1, 256), (2, 256), 4, 2, 2 * b, True)
        b3[...] = key_bias((1, 256), (1, 256), 1, 1, 0, True)
        e4 = class_facts4(o4, b)[1]
        b4[...] = key_bias((1, 256), (2, 256), 12, 6, 6 * e4, True)

        def wait(m, carry):
            for c in local_copies(m):
                c.wait()
            return carry

        lax.fori_loop(0, HOMES, wait, 0)
        lse_copy.wait()
        unpack_pairs(qst, 0, qf, 1.0 / math.sqrt(HD))

        def prepare(i, carry):
            c, t = i // 12, pl.multiple_of(lax.rem(i, 12) * 128, 128)
            k2, v2 = keys_and_values(kvf[c, pl.ds(t, 128), :])
            kc[c, pl.ds(t, 128), :] = k2.astype(BF16)
            vc[c, pl.ds(t, 128), :] = v2.astype(BF16)
            kt[c, :, pl.ds(t, 128)] = k2.T.astype(BF16)
            return carry

        lax.fori_loop(0, 48, prepare, 0)

        def prepare_q(i, carry):
            c, t = i // 12, pl.multiple_of(lax.rem(i, 12) * 128, 128)
            qc[c, pl.ds(t, 128), :] = query_quads(qf[c, pl.ds(t, 128), :])
            return carry

        lax.fori_loop(0, 24, prepare_q, 0)

    keys4, e4, (qc4, qv4) = class_facts4(o4, b)
    kc5, kv5 = lax.rem(o5, 4), o5 // 4
    qi4, qi5 = qc4 - 2 * b, lax.rem(kc5, 2)

    @pl.when(active)
    def _():
        for blk in range(4):
            r = slice(128 * blk, 128 * blk + 128)
            for e in range(2):
                c, v = keys4[e]
                k2, v2 = keys_and_values(kvf[c, pl.ds(v + 384 * blk, 128, stride=3), :])
                k4[e, r, :] = k2.astype(BF16)
                v4[e, r, :] = v2.astype(BF16)
                kt4[e, :, r] = k2.T.astype(BF16)
            q4[r, :] = query_quads(qf[qi4, pl.ds(qv4 + 384 * blk, 128, stride=3), :])
            rows = pl.ds(kv5 + 384 * blk, 128, stride=3)
            k2, v2 = keys_and_values(kvf[kc5, rows, :])
            k5[r, :] = k2.astype(BF16)
            v5[r, :] = v2.astype(BF16)
            kt5[:, r] = k2.T.astype(BF16)
            q5[r, :] = query_quads(qf[qi5, rows, :])
        dk[...] = jnp.zeros_like(dk)

    small.stage1()
    big.early(0)
    big.early(1)

    @pl.when(active)
    def _():
        def arrive(m, carry):
            pltpu.make_async_copy(drec.at[m], drec.at[m], drecv.at[m]).wait()
            return carry

        lax.fori_loop(0, HOMES, arrive, 0)
        unpack_pairs(drec, 0, df, 1.0)

        def facts(m, carry):
            ci = lax.rem(m, 2)
            t = pl.multiple_of((m // 2) * ROWS, 32)
            prod = drec[m] * ap[m]
            low = lower_lanes(prod)
            d0 = jnp.sum(jnp.where(low, prod, 0.0), -1, keepdims=True)
            d1 = jnp.sum(jnp.where(low, 0.0, prod), -1, keepdims=True)
            for part, d in ((0, d0), (1, d1)):
                rows = pl.ds(t + HALF * part, HALF)
                l = X[ci, rows, :]
                X[ci, rows, :] = jnp.where(low, l, jnp.broadcast_to(d, l.shape))
            return carry

        lax.fori_loop(0, HOMES, facts, 0)

        def turned(v):
            w = v.T
            return jnp.concatenate([w[0:1, :], w[HD : HD + 1, :]], 0)

        def prepare_d(i, carry):
            c, t = i // 12, pl.multiple_of(lax.rem(i, 12) * 128, 128)
            rows = pl.ds(t, 128)
            dc[c, rows, :] = query_quads(df[c, rows, :])
            lt[i] = turned(X[c, rows, :])
            return carry

        lax.fori_loop(0, 24, prepare_d, 0)
        for blk in range(4):
            r = slice(128 * blk, 128 * blk + 128)
            rows = pl.ds(qv4 + 384 * blk, 128, stride=3)
            d4[r, :] = query_quads(df[qi4, rows, :])
            lt4[blk] = turned(X[qi4, rows, :])
            rows = pl.ds(kv5 + 384 * blk, 128, stride=3)
            d5[r, :] = query_quads(df[qi5, rows, :])
            lt5[blk] = turned(X[qi5, rows, :])
        dv[...] = jnp.zeros_like(dv)

    small.stage2()
    big.step(2)

    def tile(g, k, v, kT, q, d, facts_pair, bias, first):
        s_ = dot_nt(doubled(k), q)
        if bias is not None:
            s_ = s_ + bias[...]
        l0, l1 = facts_pair
        row = jnp.concatenate([l0[0:1, :], l1[0:1, :]], 1)
        delta = jnp.concatenate([l0[1:2, :], l1[1:2, :]], 1)
        pr = jnp.exp(s_ - row)
        ds = pr * (dot_nt(doubled(v), d) - delta)
        hi, lo = split(pr)
        dv_new = dot_nn(hi, d) + dot_nn(lo, d)
        hi, lo = split(ds)
        dk_new = dot_nn(hi, q) + dot_nn(lo, q)
        dq_new = dot_nn(kT, hi) + dot_nn(kT, lo)
        dqt[g] = dq_new if first else dqt[g] + dq_new
        return dk_new[:, :128] + dk_new[:, 128:], dv_new[:, :128] + dv_new[:, 128:]

    def q1(qb, carry):
        def at(g, blk):
            return pl.ds(pl.multiple_of(512 * g + 128 * blk, 128), 128)

        def step(kb, bias, first):
            for g in range(3):
                ks, qs = at(g, kb), at(g, qb)
                kT = jnp.concatenate([kt[c, :, ks] for c in range(4)], 1)
                a, c = tile(
                    g,
                    kc[:, ks, :].reshape(512, 128),
                    vc[:, ks, :].reshape(512, 128),
                    kT,
                    qc[:, qs, :].reshape(256, 256),
                    dc[:, qs, :].reshape(256, 256),
                    (lt.at[4 * g + qb], lt.at[12 + 4 * g + qb]),
                    bias,
                    first,
                )
                dk[:, ks, :] += a.reshape(4, 128, 128)
                dv[:, ks, :] += c.reshape(4, 128, 128)

        step(qb, b1, True)

        def more(kb, inner):
            step(kb, None, False)
            return inner

        lax.fori_loop(0, qb, more, 0)
        for g in range(3):
            dq[:, at(g, qb), :] = dqt[g].T.reshape(2, 128, 128)
        return carry

    for first, after, tau in ((0, 2, 3), (2, 3, 4), (3, 4, 5)):

        @pl.when(active)
        def _(first=first, after=after):
            lax.fori_loop(first, after, q1, 0)

        getattr(small, f"stage{tau}")()
        big.step(tau)

    def at256(blk):
        return pl.ds(pl.multiple_of(256 * blk, 128), 256)

    def kept(flag, v):
        return jnp.where(flag, v, 0.0)

    def q2(qb, carry):
        def step(kb, bias, first):
            ks, qs = at256(kb), at256(qb)
            a, c = tile(
                0,
                jnp.concatenate([kc[o2, ks, :], kc[o2 + 2, ks, :]], 0),
                jnp.concatenate([vc[o2, ks, :], vc[o2 + 2, ks, :]], 0),
                jnp.concatenate([kt[o2, :, ks], kt[o2 + 2, :, ks]], 1),
                qc[o2, qs, :],
                dc[o2, qs, :],
                (lt.at[12 * o2 + 2 * qb], lt.at[12 * o2 + 2 * qb + 1]),
                bias,
                first,
            )
            for par in range(2):
                f = o2 == par
                dk[par, ks, :] += kept(f, a[:256])
                dk[par + 2, ks, :] += kept(f, a[256:])
                dv[par, ks, :] += kept(f, c[:256])
                dv[par + 2, ks, :] += kept(f, c[256:])

        step(qb, b2, True)

        def more(kb, inner):
            step(kb, None, False)
            return inner

        lax.fori_loop(jnp.where(qb >= 4, 4, 0), qb, more, 0)
        for par in range(2):
            dq[par, at256(qb), :] += kept(o2 == par, dqt[0].T)
        return carry

    @pl.when(active)
    def _():
        lax.fori_loop(0, TOTAL // 256, q2, 0)

    small.stage6()
    big.step(6)

    def q3(qb, carry):
        ci = lax.rem(o3, 2)

        def step(kb, bias, first):
            ks, qs = at256(kb), at256(qb)
            a, c = tile(
                0,
                kc[o3, ks, :],
                vc[o3, ks, :],
                kt[o3, :, ks],
                qc[ci, qs, :],
                dc[ci, qs, :],
                (lt.at[12 * ci + 2 * qb], lt.at[12 * ci + 2 * qb + 1]),
                bias,
                first,
            )
            for i in range(2):
                f = o3 == 2 * b + i
                dk[2 * b + i, ks, :] += kept(f, a)
                dv[2 * b + i, ks, :] += kept(f, c)

        step(qb, b3, True)

        def more(kb, inner):
            step(kb, None, False)
            return inner

        lax.fori_loop(0, qb, more, 0)
        for i in range(2):
            dq[i, at256(qb), :] += kept(o3 == 2 * b + i, dqt[0].T)
        return carry

    for first, after, tau in ((0, 4, 7), (4, 6, 8)):

        @pl.when(active)
        def _(first=first, after=after):
            lax.fori_loop(first, after, q3, 0)

        big.step(tau)

    @pl.when(active)
    def _():
        for ref in (dk4, dv4, dk5, dv5):
            ref[...] = jnp.zeros_like(ref)
        for qb in range(2):
            qs = slice(256 * qb, 256 * qb + 256)
            for kb in range(qb, -1, -1):
                ks = slice(256 * kb, 256 * kb + 256)
                a, c = tile(
                    0,
                    k4[:, ks, :].reshape(512, 128),
                    v4[:, ks, :].reshape(512, 128),
                    jnp.concatenate([kt4[0, :, ks], kt4[1, :, ks]], 1),
                    q4[qs, :],
                    d4[qs, :],
                    (lt4.at[2 * qb], lt4.at[2 * qb + 1]),
                    b4 if kb == qb else None,
                    kb == qb,
                )
                dk4[:, ks, :] += a.reshape(2, 256, 128)
                dv4[:, ks, :] += c.reshape(2, 256, 128)
                a, c = tile(
                    1,
                    k5[ks, :],
                    v5[ks, :],
                    kt5[:, ks],
                    q5[qs, :],
                    d5[qs, :],
                    (lt5.at[2 * qb], lt5.at[2 * qb + 1]),
                    b3 if kb == qb else None,
                    kb == qb,
                )
                dk5[ks, :] += a
                dv5[ks, :] += c
            dq4[qs, :] = dqt[0].T
            dq5[qs, :] = dqt[1].T
        mine5 = kc5 // 2 == b
        for kind in range(12):
            c, rows = kind % 4, pl.ds(kind // 4, THIRD, stride=3)
            f0, f1, f5 = o4 == kind, o4 + 6 == kind, jnp.logical_and(o5 == kind, mine5)
            dk[c, rows, :] += kept(f0, dk4[0]) + kept(f1, dk4[1]) + kept(f5, dk5[...])
            dv[c, rows, :] += kept(f0, dv4[0]) + kept(f1, dv4[1]) + kept(f5, dv5[...])
        for ci in range(2):
            for v in range(3):
                rows = pl.ds(v, THIRD, stride=3)
                f4 = jnp.logical_and(qi4 == ci, qv4 == v)
                f5 = jnp.logical_and(jnp.logical_and(qi5 == ci, kv5 == v), mine5)
                dq[ci, rows, :] += kept(f4, dq4[...]) + kept(f5, dq5[...])

    big.step(9)

    def passed(m):
        return remote(ds_out.at[m], came.at[m], fsend.at[m], frecv.at[m], place.peer)

    def home_copies(m):
        q, t = home_device(core, m)
        kv = remote(came.at[m], grec.at[head, pl.ds(0, ROWS), :], send.at[m], recv.at[head], to(q, t))
        dq_ = remote(dqp.at[m], grec.at[head, pl.ds(ROWS, HALF), :], qsend.at[m], qrecv.at[head], to(q, t))
        return q, t, kv, dq_

    @pl.when(active)
    def _():
        def rows_of(m):
            return pl.ds(pl.multiple_of((m // 2) * ROWS, 64), ROWS)

        def kv(c, m):
            return pick(dk[c, rows_of(m), :], dv[c, rows_of(m), :])

        def share(m, carry):
            ds_out[m] = kv(2 * (1 - b) + lax.rem(m, 2), m)
            passed(m).start()
            return carry

        lax.fori_loop(0, HOMES, share, 0)

        def add(m, carry):
            q, t, far_kv, far_q = home_copies(m)
            ci = lax.rem(m, 2)
            v = dq[ci, rows_of(m), :]
            v = (v + swap(v)) * (1.0 / math.sqrt(HD))
            dqp[m] = pick(v[:HALF], v[HALF:])
            passed(m).wait_recv()
            came[m] += kv(2 * b + ci, m)

            @pl.when(same(p, s, q, t))
            def _():
                pltpu.make_async_copy(came.at[m], grec.at[head, pl.ds(0, ROWS), :], recv.at[head]).start()
                pltpu.make_async_copy(dqp.at[m], grec.at[head, pl.ds(ROWS, HALF), :], qrecv.at[head]).start()

            @pl.when(jnp.logical_not(same(p, s, q, t)))
            def _():
                far_kv.start()
                far_q.start()

            return carry

        lax.fori_loop(0, HOMES, add, 0)

    big.step(10)

    def n_copies(m, slot):
        q, t = home_device(core, m)
        return [
            pltpu.make_async_copy(
                N.at[q * RUNS + t, :, pl.ds(128 * j, 128)],
                dv.at[slot, pl.ds(ROWS * j, ROWS), :],
                nsem.at[slot, j],
            )
            for j in range(6)
        ]

    def z_rows(i, c, half):
        return dq.at[1, pl.ds(D * half + (i * 16 + c * 8) * PIECE, ROWS), :]

    def z_swap():
        return [
            remote(z_rows(i, 1 - b, half), zc.at[i, half], zsend.at[i, half], zrecv.at[i, half], place.peer)
            for i in range(2)
            for half in range(2)
        ]

    def owner_copies(m):
        i, t = m // RUNS, lax.rem(m, RUNS)
        first = (i * 16 + b * 8 + t) * PIECE
        return [
            (
                dq.at[1, pl.ds(D * half + first, PIECE), :],
                zrec.at[head, half],
                osend.at[m, half],
                orecv.at[head, half],
            )
            for half in range(2)
        ], to(i * 2 + b, t), same(p, s, i * 2 + b, t)

    @pl.when(active)
    def _():
        for c in n_copies(jnp.int32(0), 0):
            c.start()
        dq[0] = jnp.zeros((TOTAL, 128), F32)

        def one(m, carry):
            slot = lax.rem(m, 2)

            @pl.when(m + 1 < HOMES)
            def _():
                for c in n_copies(m + 1, 1 - slot):
                    c.start()

            v = dqp[m]
            w = swap(v)
            dq_t = jnp.concatenate([pick(v, w), pick(w, v)], 0).T[:HD]
            hi, lo = split(jnp.concatenate([dq_t, came[m].T], 0))
            for c in n_copies(m, slot):
                c.wait()
            for j in range(6):
                blk = pl.ds(ROWS * j, ROWS)
                n_hi, n_lo = split(dv[slot, blk, :])
                dq[0, blk, :] += dot_nn(hi, n_hi) + dot_nn(hi, n_lo) + dot_nn(lo, n_hi)
            return carry

        lax.fori_loop(0, HOMES, one, 0)
        for j in range(6):
            w = dq[0, ROWS * j : ROWS * j + ROWS, :].T
            dq[1, 128 * j : 128 * j + 128, :] = w[:, :128]
            dq[1, D + 128 * j : D + 128 * j + 128, 0:HD] = w[:, 128:ROWS]
        for c in z_swap():
            c.start()
        for c in z_swap():
            c.wait_recv()
        for i in range(2):
            for half in range(2):
                mine = z_rows(i, b, half)
                mine[...] += zc[i, half]

        def hand_out(m, carry):
            parts, there, here = owner_copies(m)
            for src, dst, a, c in parts:

                @pl.when(here)
                def _(src=src, dst=dst, c=c):
                    pltpu.make_async_copy(src, dst, c).start()

                @pl.when(jnp.logical_not(here))
                def _(src=src, dst=dst, a=a, c=c):
                    remote(src, dst, a, c, there).start()

            return carry

        lax.fori_loop(0, HOMES, hand_out, 0)

    def from_head(h, carry):
        a = grec.at[h, pl.ds(0, ROWS), :]
        c = grec.at[h, pl.ds(ROWS, HALF), :]
        pltpu.make_async_copy(a, a, recv.at[h]).wait()
        pltpu.make_async_copy(c, c, qrecv.at[h]).wait()
        return carry

    lax.fori_loop(0, HEADS, from_head, 0)

    def from_owner(h, carry):
        for half in range(2):
            pltpu.make_async_copy(zrec.at[h, half], zrec.at[h, half], orecv.at[h, half]).wait()
        return carry

    lax.fori_loop(0, HEADS, from_owner, 0)
    big.finish()
    small.finish()

    @pl.when(active)
    def _():
        def sent(m, carry):
            q, t, far_kv, far_q = home_copies(m)
            passed(m).wait_send()

            @pl.when(jnp.logical_not(same(p, s, q, t)))
            def _():
                far_kv.wait_send()
                far_q.wait_send()

            parts, there, here = owner_copies(m)
            for src, dst, a, c in parts:

                @pl.when(jnp.logical_not(here))
                def _(src=src, dst=dst, a=a, c=c):
                    remote(src, dst, a, c, there).wait_send()

            return carry

        lax.fori_loop(0, HOMES, sent, 0)
        for c in z_swap():
            c.wait_send()

    def da_sent(h, carry):
        q, t, far = da_copy(h)

        @pl.when(jnp.logical_not(same(p, s, q, t)))
        def _():
            far.wait_send()

        return carry

    lax.fori_loop(0, HEADS, da_sent, 0)


def backward_all(offs, dap, own, sib, ap, lse, G, N, S, counts, cid):
    dma = pltpu.SemaphoreType.DMA
    keys = pltpu.VMEM((4, TOTAL, 128), BF16)
    full = pltpu.VMEM((4, TOTAL, 128), F32)
    quad = pltpu.VMEM((2, TOTAL, 256), BF16)
    quad3 = pltpu.VMEM((THIRD, 256), BF16)
    pair3 = pltpu.VMEM((THIRD, 128), BF16)
    turned = pltpu.VMEM((128, THIRD), BF16)
    facts3 = pltpu.VMEM((4, 2, 128), F32)
    out3 = pltpu.VMEM((THIRD, 128), F32)
    packs = pltpu.VMEM((HOMES, ROWS, 128), F32)
    halves = pltpu.VMEM((HOMES, HALF, 128), F32)
    return pl.pallas_call(
        functools.partial(back_all_kernel, counts),
        out_shape=[
            jax.ShapeDtypeStruct((HEADS, PACK, 128), F32),
            jax.ShapeDtypeStruct((HEADS, 2, PIECE, 128), F32),
            jax.ShapeDtypeStruct((PIECE, D), F32),
            jax.ShapeDtypeStruct((PIECE, FF), F32),
            jax.ShapeDtypeStruct((4 * PIECE, D), F32),
        ]
        + [jax.ShapeDtypeStruct((1, n), F32) for n in (PIECE, PIECE, 4 * PIECE, PATTERNS)],
        in_specs=[SM, ANY, ANY, ANY, VM, ANY, ANY, ANY, VM],
        out_specs=[ANY, ANY] + [VM] * 7,
        scratch_shapes=[
            halves,
            halves,
            keys,
            keys,
            pltpu.VMEM((4, 128, TOTAL), BF16),
            quad,
            quad,
            pltpu.VMEM((24, 2, 128), F32),
            pltpu.VMEM((2, THIRD, 128), BF16),
            pltpu.VMEM((2, THIRD, 128), BF16),
            pltpu.VMEM((2, 128, THIRD), BF16),
            quad3,
            quad3,
            facts3,
            pair3,
            pair3,
            turned,
            quad3,
            quad3,
            facts3,
            pltpu.VMEM((3, 128, 256), F32),
            full,
            full,
            pltpu.VMEM((2, TOTAL, 128), F32),
            pltpu.VMEM((2, THIRD, 128), F32),
            pltpu.VMEM((2, THIRD, 128), F32),
            out3,
            out3,
            out3,
            out3,
            pltpu.VMEM((512, 256), F32),
            pltpu.VMEM((512, 256), F32),
            pltpu.VMEM((256, 256), F32),
            pltpu.VMEM((512, 256), F32),
            packs,
            packs,
            pltpu.VMEM((2, 2, ROWS, 128), F32),
            pltpu.VMEM((8, D), F32),
            dma((HOMES + 1, 3)),
            dma((HEADS,)),
            dma((HOMES,)),
            dma((HOMES,)),
            dma((HEADS,)),
            dma((HOMES,)),
            dma((HEADS,)),
            dma((HOMES,)),
            dma((HOMES,)),
            dma((2, 6)),
            dma((2, 2)),
            dma((2, 2)),
            dma((HOMES, 2)),
            dma((HEADS, 2)),
        ]
        + Reducer.scratch(N_FF)
        + SmallSum.scratch(),
        compiler_params=params(collective_id=cid, has_side_effects=True),
    )(offs, dap, own, sib, ap, lse, G, N, S)


SEG1, SEG2, SEG3, SEG4, SEG5 = SEGMENTS
DILATION_ONE, DILATION_TWO, DILATION_THREE, DILATION_FOUR, DILATION_FIVE = DILATIONS
MASK_VALUE = -1e30
MATMUL_ACCURACY = lax.Precision.HIGHEST


def passed_along(value, axis, by):
    length = lax.axis_size(axis)
    return lax.ppermute(value, axis, [(i, (i + by) % length) for i in range(length)])


def run_is_live(distance, anchor_point, sequence_width, segment_length):
    return (anchor_point - (distance - 1) * sequence_width - 1) // segment_length == anchor_point // segment_length


def layer_norm(x, gain_vec):
    average = jnp.mean(x, -1, keepdims=True)
    centred = x - average
    variance = jnp.mean(centred * centred, -1, keepdims=True)
    return centred * lax.rsqrt(variance + LN_EPSILON) * gain_vec


def select_table(offsets_row, dilation_rate):
    return (jnp.arange(dilation_rate, dtype=jnp.int32)[:, None] == offsets_row[None, :]).astype(
        jnp.float32
    )


def spread_apart(x, select_option, dilation_rate):
    shaped = x.reshape(x.shape[0] // dilation_rate, dilation_rate, x.shape[1], x.shape[2])
    return jnp.einsum("trhd,rh->thd", shaped, select_option, precision=MATMUL_ACCURACY)


def spread_scalar_rows(x, select_option, dilation_rate):
    shaped = x.reshape(x.shape[0] // dilation_rate, dilation_rate, x.shape[1])
    return jnp.einsum("trh,rh->th", shaped, select_option, precision=MATMUL_ACCURACY)


def spread_rows(x, select_option):
    return jnp.einsum("thd,rh->trhd", x, select_option, precision=MATMUL_ACCURACY).reshape(
        -1, x.shape[1], x.shape[2]
    )


def spread_scalars(x, select_option):
    return jnp.einsum("th,rh->trh", x, select_option, precision=MATMUL_ACCURACY).reshape(
        -1, x.shape[1]
    )


def masked_score_matrix(sparse_queries, key_portion, query_position, key_position, segment_length):
    score_matrix = jnp.einsum(
        "ozt,bzt->zob", sparse_queries, key_portion, precision=MATMUL_ACCURACY
    ) * (1.0 / math.sqrt(key_portion.shape[-1]))
    q_cols = query_position.T[:, :, None]
    k_cols = key_position.T[:, None, :]
    permitted_mask = (k_cols <= q_cols) & (k_cols // segment_length == q_cols // segment_length)
    return (jnp.where(permitted_mask, score_matrix, MASK_VALUE), permitted_mask)


def prepare_pattern(
    query_sequence, key_sequence, value_sequence, offsets_row, dilation_rate, anchor_point
):
    select_option = select_table(offsets_row, dilation_rate)
    sparse_queries = spread_apart(query_sequence, select_option, dilation_rate)
    sparse_key_value = jnp.stack(
        (
            spread_apart(key_sequence, select_option, dilation_rate),
            spread_apart(value_sequence, select_option, dilation_rate),
        )
    )
    query_position = (
        anchor_point
        + jnp.arange(sparse_queries.shape[0], dtype=jnp.int32)[:, None] * dilation_rate
        + offsets_row[None, :]
    )
    return (select_option, sparse_queries, sparse_key_value, query_position)


def pattern_forward_pass(
    sparse_queries,
    sparse_key_value,
    query_position,
    reach,
    segment_length,
    anchor_point,
    sequence_width,
):
    masked_logits, permitted_mask = masked_score_matrix(
        sparse_queries, sparse_key_value[0], query_position, query_position, segment_length
    )
    row_max = jnp.max(masked_logits, -1)
    softmax_weights = jnp.where(permitted_mask, jnp.exp(masked_logits - row_max[..., None]), 0.0)
    state = (
        row_max,
        jnp.sum(softmax_weights, -1),
        jnp.einsum("tlj,jtb->tlb", softmax_weights, sparse_key_value[1], precision=MATMUL_ACCURACY),
    )

    def one_run(distance, carry):
        remote_key_value, state = carry
        remote_key_value = passed_along(remote_key_value, "seq", 1)
        key_position = query_position - distance * sequence_width

        def update(state_in):
            old_max, old_sum, old_acc = state_in
            masked_remote, permitted_remote = masked_score_matrix(
                sparse_queries, remote_key_value[0], query_position, key_position, segment_length
            )
            new_max = jnp.maximum(old_max, jnp.max(masked_remote, -1))
            weights_far = jnp.where(
                permitted_remote, jnp.exp(masked_remote - new_max[..., None]), 0.0
            )
            factor = jnp.exp(old_max - new_max)
            added = jnp.einsum(
                "tlj,jtb->tlb", weights_far, remote_key_value[1], precision=MATMUL_ACCURACY
            )
            return (
                new_max,
                old_sum * factor + jnp.sum(weights_far, -1),
                old_acc * factor[..., None] + added,
            )

        def unchanged(state_in):
            return state_in

        is_live = run_is_live(distance, anchor_point, sequence_width, segment_length)
        return remote_key_value, lax.cond(is_live, update, unchanged, state)

    state = lax.fori_loop(1, reach + 1, one_run, (sparse_key_value, state))[1]
    row_max, row_sum, accumulated = state
    mixture = jnp.transpose(accumulated / row_sum[..., None], (1, 0, 2))
    log_sum = (row_max + jnp.log(row_sum)).T
    return (mixture, log_sum)


def merge_patterns(forwards, prepared_inputs):
    full_lse = []
    full_mix = []
    for pattern_spec in range(len(forwards)):
        mixture, log_sum = forwards[pattern_spec]
        select_option = prepared_inputs[pattern_spec][0]
        covered = spread_scalars(jnp.ones_like(log_sum), select_option)
        full_lse.append(spread_scalars(log_sum, select_option) + (covered - 1.0) * 1e30)
        full_mix.append(spread_rows(mixture, select_option))
    stacked = jnp.stack(full_lse)
    row_max = jnp.max(stacked, 0)
    softmax_weights = jnp.exp(stacked - row_max)
    row_sum = jnp.sum(softmax_weights, 0)
    attended = full_mix[0] * softmax_weights[0][..., None]
    for pattern_spec in range(1, len(full_mix)):
        attended = attended + full_mix[pattern_spec] * softmax_weights[pattern_spec][..., None]
    return (attended / row_sum[..., None], row_max + jnp.log(row_sum))


def pattern_backward(
    select_option,
    dilation_rate,
    segment_length,
    anchor_point,
    sparse_queries,
    sparse_key_value,
    query_position,
    reach,
    sequence_gradient,
    row_difference,
    combined_logsumexp,
):
    sequence_width = sequence_gradient.shape[0]
    sparse_gradient = spread_apart(sequence_gradient, select_option, dilation_rate)
    sparse_output_grad = spread_scalar_rows(row_difference, select_option, dilation_rate).T
    sparse_logsumexp = spread_scalar_rows(combined_logsumexp, select_option, dilation_rate).T
    inverse_square_root = 1.0 / math.sqrt(sparse_queries.shape[-1])

    def portion_gradients(key_portion, value_portion, key_position):
        masked_logits, permitted_mask = masked_score_matrix(
            sparse_queries, key_portion, query_position, key_position, segment_length
        )
        softmax_weights = jnp.where(
            permitted_mask, jnp.exp(masked_logits - sparse_logsumexp[..., None]), 0.0
        )
        value_gradient = jnp.einsum(
            "tui,utx->itx", softmax_weights, sparse_gradient, precision=MATMUL_ACCURACY
        )
        pattern_gradient = jnp.einsum(
            "ozt,bzt->zob", sparse_gradient, value_portion, precision=MATMUL_ACCURACY
        )
        score_gradient = (
            softmax_weights
            * (pattern_gradient - sparse_output_grad[..., None])
            * inverse_square_root
        )
        query_gradient = jnp.einsum(
            "hqk,khd->qhd", score_gradient, key_portion, precision=MATMUL_ACCURACY
        )
        key_gradient = jnp.einsum(
            "tui,utx->itx", score_gradient, sparse_queries, precision=MATMUL_ACCURACY
        )
        return (query_gradient, jnp.stack((key_gradient, value_gradient)))

    query_gradient, key_value_gradient = portion_gradients(
        sparse_key_value[0], sparse_key_value[1], query_position
    )

    def one_run(distance, carry):
        remote_key_value, remote_gradient, query_sum = carry
        remote_key_value = passed_along(remote_key_value, "seq", 1)
        remote_gradient = passed_along(remote_gradient, "seq", 1)
        key_position = query_position - distance * sequence_width

        def far_grads():
            part_q, part_kv = portion_gradients(remote_key_value[0], remote_key_value[1], key_position)
            return query_sum + part_q, remote_gradient + part_kv

        def no_grads():
            return query_sum, remote_gradient

        is_live = run_is_live(distance, anchor_point, sequence_width, segment_length)
        query_sum, remote_gradient = lax.cond(is_live, far_grads, no_grads)
        return remote_key_value, remote_gradient, query_sum

    _, travelled, query_gradient = lax.fori_loop(
        1, reach + 1, one_run, (sparse_key_value, key_value_gradient, query_gradient)
    )
    return (query_gradient, passed_along(travelled, "seq", -reach))


def front_part(own_rows, w_qkv, gain_attn):
    return jnp.dot(layer_norm(own_rows, gain_attn), w_qkv, precision=MATMUL_ACCURACY)


def after_part(attn_rows, own_rows, w_out, w_up, w_down, gain_inner, gain_ffn, gain_hidden):
    residual = own_rows + jnp.dot(
        layer_norm(attn_rows, gain_inner), w_out, precision=MATMUL_ACCURACY
    )
    hidden = jax.nn.gelu(
        jnp.dot(layer_norm(residual, gain_ffn), w_up, precision=MATMUL_ACCURACY), approximate=False
    )
    return residual + jnp.dot(layer_norm(hidden, gain_hidden), w_down, precision=MATMUL_ACCURACY)


def shards(
    tokens,
    w_qkv,
    w_out,
    w_up,
    w_down,
    gain_attn,
    gain_inner,
    gain_ffn,
    gain_hidden,
    offsets,
    grad_out,
):
    w_qkv = w_qkv.astype(jnp.float32)
    w_out = w_out.astype(jnp.float32)
    w_up = w_up.astype(jnp.float32)
    w_down = w_down.astype(jnp.float32)
    groups = lax.axis_size("pat")
    local_rows = tokens.shape[0]
    sequence_width = local_rows * groups
    heads_here = HEADS // groups
    own_rows = tokens.reshape(local_rows, D)
    qkv_rows, front_back = jax.vjp(front_part, own_rows, w_qkv, gain_attn)
    gathered_qkv = lax.all_to_all(
        qkv_rows.reshape(local_rows, 1, 3, HEADS, HD),
        "pat",
        split_axis=3,
        concat_axis=1,
        tiled=True,
    )
    gathered_qkv = gathered_qkv.reshape(sequence_width, 3, heads_here, HD)
    head_offsets = lax.dynamic_slice_in_dim(
        offsets, lax.axis_index("pat") * heads_here, heads_here, 1
    )
    anchor_point = lax.axis_index("seq") * sequence_width
    dilation_rates = (DILATION_ONE, DILATION_TWO, DILATION_THREE, DILATION_FOUR, DILATION_FIVE)
    segment_lengths = (SEG1, SEG2, SEG3, SEG4, SEG5)
    reaches = [
        min((segment_lengths[pattern_spec] - 2) // sequence_width + 1, lax.axis_size("seq") - 1)
        for pattern_spec in range(PATTERNS)
    ]
    prepared_inputs = []
    for pattern_spec in range(PATTERNS):
        prepared_inputs.append(
            prepare_pattern(
                gathered_qkv[:, 0],
                gathered_qkv[:, 1],
                gathered_qkv[:, 2],
                head_offsets[pattern_spec],
                dilation_rates[pattern_spec],
                anchor_point,
            )
        )
    forwards = []
    for pattern_spec in range(PATTERNS):
        select_option, sparse_queries, sparse_key_value, query_position = prepared_inputs[
            pattern_spec
        ]
        forwards.append(
            pattern_forward_pass(
                sparse_queries,
                sparse_key_value,
                query_position,
                reaches[pattern_spec],
                segment_lengths[pattern_spec],
                anchor_point,
                sequence_width,
            )
        )
    lse_sums = jnp.stack([jnp.sum(entry[1]) for entry in forwards])
    totals = lax.psum(lse_sums, ("pat", "seq"))
    full_length = sequence_width * lax.axis_size("seq")
    counts = jnp.array(
        [
            float(full_length // dilation_rates[pattern_spec] * HEADS)
            for pattern_spec in range(PATTERNS)
        ],
        jnp.float32,
    )
    log_means = totals / counts
    attended, combined_logsumexp = merge_patterns(forwards, prepared_inputs)
    returned_rows = lax.all_to_all(
        attended.reshape(local_rows, groups, heads_here, HD),
        "pat",
        split_axis=1,
        concat_axis=2,
        tiled=True,
    )
    attn_rows = returned_rows.reshape(local_rows, D)
    result, after_back = jax.vjp(
        after_part, attn_rows, own_rows, w_out, w_up, w_down, gain_inner, gain_ffn, gain_hidden
    )
    g_attn, g_resid, g_out, g_up, g_down, g_inner, g_ffn, g_hidden = after_back(
        grad_out.reshape(local_rows, D)
    )
    sequence_gradient = lax.all_to_all(
        g_attn.reshape(local_rows, 1, HEADS, HD), "pat", split_axis=2, concat_axis=1, tiled=True
    )
    sequence_gradient = sequence_gradient.reshape(sequence_width, heads_here, HD)
    row_difference = jnp.sum(sequence_gradient * attended, -1)
    q_grads = []
    kv_grads = []
    for pattern_spec in range(PATTERNS):
        select_option, sparse_queries, sparse_key_value, query_position = prepared_inputs[
            pattern_spec
        ]
        part_q, part_kv = pattern_backward(
            select_option,
            dilation_rates[pattern_spec],
            segment_lengths[pattern_spec],
            anchor_point,
            sparse_queries,
            sparse_key_value,
            query_position,
            reaches[pattern_spec],
            sequence_gradient,
            row_difference,
            combined_logsumexp,
        )
        q_grads.append(part_q)
        kv_grads.append(part_kv)
    grad_total = jnp.zeros((sequence_width, 3, heads_here, HD), jnp.float32)
    for pattern_spec in range(PATTERNS):
        select_option = prepared_inputs[pattern_spec][0]
        grad_total = grad_total + jnp.stack(
            (
                spread_rows(q_grads[pattern_spec], select_option),
                spread_rows(kv_grads[pattern_spec][0], select_option),
                spread_rows(kv_grads[pattern_spec][1], select_option),
            ),
            1,
        )
    grad_back = lax.all_to_all(
        grad_total.reshape(local_rows, groups, 3, heads_here, HD),
        "pat",
        split_axis=1,
        concat_axis=3,
        tiled=True,
    )
    g_tokens, g_qkv, g_attn_gain = front_back(grad_back.reshape(local_rows, 3 * D))
    grad_tokens = (g_resid + g_tokens).reshape(local_rows, 1, D)
    summed = (
        lax.psum_scatter(g_qkv, ("pat", "seq"), scatter_dimension=0, tiled=True),
        lax.psum_scatter(g_out, ("pat", "seq"), scatter_dimension=0, tiled=True),
        lax.psum_scatter(g_up, ("pat", "seq"), scatter_dimension=0, tiled=True),
        lax.psum_scatter(g_down, ("pat", "seq"), scatter_dimension=0, tiled=True),
        lax.psum_scatter(g_attn_gain, ("pat", "seq"), scatter_dimension=0, tiled=True),
        lax.psum_scatter(g_inner, ("pat", "seq"), scatter_dimension=0, tiled=True),
        lax.psum_scatter(g_ffn, ("pat", "seq"), scatter_dimension=0, tiled=True),
        lax.psum_scatter(g_hidden, ("pat", "seq"), scatter_dimension=0, tiled=True),
    )
    return (
        result.reshape(local_rows, 1, D),
        grad_tokens,
        summed[0],
        summed[1],
        summed[2],
        summed[3],
        summed[4],
        summed[5],
        summed[6],
        summed[7],
        log_means,
    )


def fast_shards(tokens, w_qkv, w_out, w_up, w_down, gain_attn, gain_inner, gain_ffn, gain_hidden, offsets, grad_out):
    p, s = lax.axis_index("pat"), lax.axis_index("seq")
    active, head = head_here(p, s)
    mine = lax.dynamic_slice_in_dim(offsets, head, 1, 1)[:, 0]
    info = jnp.concatenate([jnp.stack([active.astype(jnp.int32), lax.rem(p, 2).astype(jnp.int32)]), mine])

    counts = [float(TOTAL * 4 // r * HEADS) for r in DILATIONS]
    pk, x, n = front(tokens, w_qkv, gain_attn)
    N = lax.all_gather(n, ("pat", "seq"))
    own, sib = to_heads(pk, True, 0)
    ap, lse, sums = attention_forward(info, own, sib)
    rec = to_homes(ap, 1)
    mixed, dap, dy1, S, G = feed_forward(
        rec, x, grad_out, w_out, w_up, w_down, gain_inner, gain_ffn, gain_hidden, sums
    )
    grec, zrec, *done = backward_all(mine, dap, own, sib, ap, lse, G, N, S, counts, 2)
    gx, g_qkv, ga, g_out, g_up, g_down, gi, gf, gh, means = last(grec, zrec, x, dy1, w_qkv, gain_attn, *done)
    return (mixed, gx, g_qkv, g_out, g_up, g_down, *(v.reshape(-1) for v in (ga, gi, gf, gh, means)))


def fits(mesh):
    return mesh.shape["pat"] == 4 and mesh.shape["seq"] == RUNS


def solution(mesh):
    rows = P("seq", "pat", None)
    split_rows = P(("pat", "seq"), None)
    split_one = P(("pat", "seq"))
    planned = jax.shard_map(
        fast_shards,
        mesh=mesh,
        in_specs=(rows,) + (P(),) * 9 + (rows,),
        out_specs=(rows, rows) + (split_rows,) * 4 + (split_one,) * 4 + (P(),),
        check_vma=False,
    )
    general = jax.shard_map(
        shards,
        mesh=mesh,
        in_specs=(rows,) + (P(),) * 9 + (rows,),
        out_specs=(rows, rows) + (split_rows,) * 4 + (split_one,) * 4 + (P(),),
        check_vma=False,
    )

    def layer(tokens, *rest):
        if fits(mesh) and tokens.shape[0] == TOTAL:
            return planned(tokens, *rest)
        return general(tokens, *rest)

    return layer
```

```python
import functools
import math

import jax
import jax.numpy as jnp
from jax import lax
from jax.experimental import pallas as pl
from jax.experimental.pallas import tpu as pltpu
from jax.sharding import PartitionSpec as P

D = 768
HEADS = 12
HD = 64
FF = 3072
PATTERNS = 5
SEGMENTS = (2048, 4096, 8192, 16384, 32768)
DILATIONS = (1, 2, 4, 6, 12)
LN_EPSILON = 1e-05
NEG = -1e30
F32 = jnp.float32
BF16 = jnp.bfloat16
HIGHEST = lax.Precision.HIGHEST
VMEM_LIMIT = 60 * 1024 * 1024

ROWS = 192
HALF = ROWS // 2
RUNS = 8
TOTAL = ROWS * RUNS
PACK = ROWS + HALF
HOMES = 16
THIRD = TOTAL // 3
MESH = pl.DeviceIdType.MESH


def dot_nn(a, b):
    return lax.dot_general(a, b, (((1,), (0,)), ((), ())), preferred_element_type=F32)


def dot_nt(a, b):
    return lax.dot_general(a, b, (((1,), (1,)), ((), ())), preferred_element_type=F32)


def split(v):
    hi = v.astype(BF16)
    return hi, (v - hi.astype(F32)).astype(BF16)


def split32(v):
    hi = v.astype(BF16).astype(F32)
    return hi, v - hi


def lower_lanes(v):
    return lax.broadcasted_iota(jnp.int32, v.shape, v.ndim - 1) < HD


def swap(v):
    return pltpu.roll(v, HD, v.ndim - 1)


def pick(a, b):
    return jnp.where(lower_lanes(a), a, b)


def head_place(h):
    z = h // 3
    column = lax.rem(lax.rem(h, 3) + z + 1, 4)
    return column // 2, z * 2 + lax.rem(column, 2)


def head_here(p, s):
    z = s // 2
    column = (p // 2) * 2 + lax.rem(s, 2)
    k = lax.rem(column - z + 7, 4)
    return k < 3, z * 3 + jnp.minimum(k, 2)


def whole(*_):
    return pl.BlockSpec(memory_space=pltpu.VMEM)


VM = pl.BlockSpec(memory_space=pltpu.VMEM)
ANY = pl.BlockSpec(memory_space=pl.ANY)
SM = pl.BlockSpec(memory_space=pltpu.SMEM)


def params(**kw):
    return pltpu.CompilerParams(vmem_limit_bytes=VMEM_LIMIT, **kw)


def normed(v):
    centred = v - jnp.mean(v, -1, keepdims=True)
    rs = lax.rsqrt(jnp.mean(centred * centred, -1, keepdims=True) + LN_EPSILON)
    return centred * rs, rs


def put_split(ref, v):
    hi, lo = split(v)
    n = v.shape[0]
    ref[0:n, :] = hi
    ref[n : 2 * n, :] = lo


def front_kernel(x3, w_ref, gain_ref, pk_ref, x_ref, lhs):
    x = x3[...].reshape(ROWS, D)
    x_ref[...] = x
    n, _ = normed(x)
    put_split(lhs, n * gain_ref[...][None, :])
    for jj in range(3):
        parts = []
        for kind in range(3):
            c0 = kind * D + 256 * jj
            r = dot_nn(lhs[...], w_ref[:, c0 : c0 + 256])
            parts.append(r[:ROWS] + r[ROWS:])
        for half in range(2):
            q, k, v = (a[:, 128 * half : 128 * half + 128] for a in parts)
            h = 4 * jj + 2 * half
            pk_ref[h, 0:ROWS, :] = pick(k, swap(v))
            pk_ref[h + 1, 0:ROWS, :] = pick(swap(k), v)
            top, bottom = q[:HALF], q[HALF:]
            pk_ref[h, ROWS:PACK, :] = pick(top, swap(bottom))
            pk_ref[h + 1, ROWS:PACK, :] = pick(swap(top), bottom)


def front(x, w, gain):
    return pl.pallas_call(
        front_kernel,
        out_shape=[jax.ShapeDtypeStruct((HEADS, PACK, 128), F32)] + [jax.ShapeDtypeStruct((ROWS, D), F32)],
        in_specs=[VM] * 3,
        out_specs=[VM] * 2,
        scratch_shapes=[pltpu.VMEM((2 * ROWS, D), BF16)],
        compiler_params=params(),
    )(x, w, gain)


def place_facts():
    p, s = lax.axis_index("pat"), lax.axis_index("seq")
    x, core = p // 2, lax.rem(p, 2)
    active, head = head_here(p, s)
    return p, s, x, core, active, head


def home_device(core, m):
    return core * 2 + lax.rem(m, 2), m // 2


def head_device(h, b):
    hx, hs = head_place(h)
    return hx * 2 + b, hs


def same(p, s, q, t):
    return jnp.logical_and(p == q, s == t)


def to(p, s):
    return {"pat": p, "seq": s}


def scatter_kernel(forward, pk, own, *rest):
    if forward:
        sib, send, recv, fsend, frecv = rest
    else:
        send, recv = rest
    p, s, x, core, active, head = place_facts()
    slot = s * 2 + core
    barrier = pltpu.get_barrier_semaphore()

    @pl.when(active)
    def _():
        def greet(m, carry):
            q, t = home_device(core, m)

            @pl.when(jnp.logical_not(same(p, s, q, t)))
            def _():
                pl.semaphore_signal(barrier, inc=1, device_id=to(q, t), device_id_type=MESH)

            return carry

        lax.fori_loop(0, HOMES, greet, 0)
        if forward:
            pl.semaphore_signal(barrier, inc=1, device_id=to(x * 2 + 1 - core, s), device_id_type=MESH)

    mine = jnp.logical_and(active, core == x)
    waits = HEADS - mine.astype(jnp.int32)
    if forward:
        waits = waits + active.astype(jnp.int32)
    pl.semaphore_wait(barrier, waits)

    def copy(h):
        q, t = head_device(h, x)
        return q, t, pltpu.make_async_remote_copy(
            src_ref=pk.at[h],
            dst_ref=own.at[slot],
            send_sem=send.at[h],
            recv_sem=recv.at[slot],
            device_id=to(q, t),
            device_id_type=MESH,
        )

    def start(j, carry):
        h = lax.rem(j + 3 * (s // 2) + 2 * p, HEADS)
        q, t, remote = copy(h)

        @pl.when(same(p, s, q, t))
        def _():
            pltpu.make_async_copy(pk.at[h], own.at[slot], recv.at[slot]).start()

        @pl.when(jnp.logical_not(same(p, s, q, t)))
        def _():
            remote.start()

        return carry

    lax.fori_loop(0, HEADS, start, 0)

    def passed(m):
        return pltpu.make_async_remote_copy(
            src_ref=own.at[m, pl.ds(0, ROWS), :],
            dst_ref=sib.at[m],
            send_sem=fsend.at[m],
            recv_sem=frecv.at[m],
            device_id=to(x * 2 + 1 - core, s),
            device_id_type=MESH,
        )

    @pl.when(active)
    def _():
        def arrive(m, carry):
            pltpu.make_async_copy(own.at[m], own.at[m], recv.at[m]).wait()
            if forward:
                passed(m).start()
            return carry

        lax.fori_loop(0, HOMES, arrive, 0)
        if forward:

            def finish(m, carry):
                passed(m).wait()
                return carry

            lax.fori_loop(0, HOMES, finish, 0)

    def sent(h, carry):
        q, t, remote = copy(h)

        @pl.when(jnp.logical_not(same(p, s, q, t)))
        def _():
            remote.wait_send()

        return carry

    lax.fori_loop(0, HEADS, sent, 0)


def to_heads(packets, forward, cid):
    rows = packets.shape[1]
    shapes = [jax.ShapeDtypeStruct((HOMES, rows, 128), F32)]
    sems = [pltpu.SemaphoreType.DMA((HEADS,)), pltpu.SemaphoreType.DMA((HOMES,))]
    if forward:
        shapes.append(jax.ShapeDtypeStruct((HOMES, ROWS, 128), F32))
        sems += [pltpu.SemaphoreType.DMA((HOMES,)), pltpu.SemaphoreType.DMA((HOMES,))]
    return pl.pallas_call(
        functools.partial(scatter_kernel, forward),
        out_shape=shapes,
        in_specs=[ANY],
        out_specs=[ANY] * len(shapes),
        scratch_shapes=sems,
        compiler_params=params(collective_id=cid, has_side_effects=True),
    )(packets)


def home_barrier(p, s, x, core, active, barrier, also_sibling):
    def greet(h, carry):
        q, t = head_device(h, x)

        @pl.when(jnp.logical_not(same(p, s, q, t)))
        def _():
            pl.semaphore_signal(barrier, inc=1, device_id=to(q, t), device_id_type=MESH)

        return carry

    lax.fori_loop(0, HEADS, greet, 0)

    @pl.when(active)
    def _():
        if also_sibling:
            pl.semaphore_signal(barrier, inc=1, device_id=to(x * 2 + 1 - core, s), device_id_type=MESH)
        mine = (core == x).astype(jnp.int32)
        pl.semaphore_wait(barrier, HOMES - mine + (1 if also_sibling else 0))


def gather_kernel(pk, rec, send, recv):
    p, s, x, core, active, head = place_facts()
    barrier = pltpu.get_barrier_semaphore()
    home_barrier(p, s, x, core, active, barrier, False)

    def copy(m):
        q, t = home_device(core, m)
        return q, t, pltpu.make_async_remote_copy(
            src_ref=pk.at[m],
            dst_ref=rec.at[head],
            send_sem=send.at[m],
            recv_sem=recv.at[head],
            device_id=to(q, t),
            device_id_type=MESH,
        )

    @pl.when(active)
    def _():
        def start(j, carry):
            m = lax.rem(j + 2 * s + 1, HOMES)
            q, t, remote = copy(m)

            @pl.when(same(p, s, q, t))
            def _():
                pltpu.make_async_copy(pk.at[m], rec.at[head], recv.at[head]).start()

            @pl.when(jnp.logical_not(same(p, s, q, t)))
            def _():
                remote.start()

            return carry

        lax.fori_loop(0, HOMES, start, 0)

    def arrive(h, carry):
        pltpu.make_async_copy(rec.at[h], rec.at[h], recv.at[h]).wait()
        return carry

    lax.fori_loop(0, HEADS, arrive, 0)

    @pl.when(active)
    def _():
        def sent(m, carry):
            q, t, remote = copy(m)

            @pl.when(jnp.logical_not(same(p, s, q, t)))
            def _():
                remote.wait_send()

            return carry

        lax.fori_loop(0, HOMES, sent, 0)


def to_homes(packets, cid):
    rows = packets.shape[1]
    return pl.pallas_call(
        gather_kernel,
        out_shape=jax.ShapeDtypeStruct((HEADS, rows, 128), F32),
        in_specs=[ANY],
        out_specs=ANY,
        scratch_shapes=[pltpu.SemaphoreType.DMA((HOMES,)), pltpu.SemaphoreType.DMA((HEADS,))],
        compiler_params=params(collective_id=cid, has_side_effects=True),
    )(packets)


def tile_positions(rows, columns, row_classes, column_classes, t_step, class_step):
    r = lax.broadcasted_iota(jnp.int32, (rows, columns), 0)
    q = lax.broadcasted_iota(jnp.int32, (rows, columns), 1)
    rn, qn = rows // row_classes, columns // column_classes
    return (r % rn) * t_step + (r // rn) * class_step, (q % qn) * t_step + (q // qn) * class_step


def key_bias(q_shape, k_shape, t_step, class_step, shift, keys_first):
    nq, nk = q_shape[0] * q_shape[1], k_shape[0] * k_shape[1]
    if keys_first:
        kp, qp = tile_positions(nk, nq, k_shape[0], q_shape[0], t_step, class_step)
    else:
        qp, kp = tile_positions(nq, nk, q_shape[0], k_shape[0], t_step, class_step)
    return jnp.where(kp - qp <= shift, 0.0, NEG).astype(F32)


def unpack_keys(own, sib, b, kvf):
    def one(m, carry):
        c = 2 * b + lax.rem(m, 2)
        d = 2 * (1 - b) + lax.rem(m, 2)
        t = pl.multiple_of((m // 2) * ROWS, 64)
        kvf[c, pl.ds(t, ROWS), :] = own[m, 0:ROWS, :]
        kvf[d, pl.ds(t, ROWS), :] = sib[m]
        return carry

    lax.fori_loop(0, HOMES, one, 0)


def unpack_pairs(src, first, dst, scale):
    def one(m, carry):
        t = pl.multiple_of((m // 2) * ROWS, 32)
        v = src[m, first : first + HALF, :] * scale
        w = swap(v)
        dst[lax.rem(m, 2), pl.ds(t, HALF), :] = pick(v, w)
        dst[lax.rem(m, 2), pl.ds(t + HALF, HALF), :] = pick(w, v)
        return carry

    lax.fori_loop(0, HOMES, one, 0)


def keys_and_values(kv):
    hi, lo = split32(kv)
    k2 = pick(hi, swap(lo))
    v2 = pick(swap(hi), lo)
    return k2, v2


def doubled(v):
    return jnp.concatenate([v, v], 1)


def query_quads(qq):
    hi, lo = split32(qq)
    return jnp.concatenate([pick(hi, lo).astype(BF16), pick(lo, hi).astype(BF16)], 1)


def class_facts4(o4, b):
    keys = ((lax.rem(o4, 4), o4 // 4), (lax.rem(o4 + 6, 4), (o4 + 6) // 4))
    first = (keys[0][0] // 2) == b
    query = (jnp.where(first, keys[0][0], keys[1][0]), jnp.where(first, keys[0][1], keys[1][1]))
    return keys, jnp.where(first, 0, 1), query


def forward_kernel(info, own, sib, ap, lse, sums, kvf, kc, vt, qf, qc, k4, vt4, q4, k5, vt5, q5, acc, ml, R, b1, b2, b3, b4):
    active = info[0] == 1
    b = info[1]
    offs = [info[2 + i] for i in range(PATTERNS)]
    sums[...] = jnp.zeros_like(sums)

    @pl.when(active)
    def _():
        unpack_keys(own, sib, b, kvf)
        unpack_pairs(own, ROWS, qf, 1.0 / math.sqrt(HD))

        def prepare(i, carry):
            c, t = i // 12, pl.multiple_of(lax.rem(i, 12) * 128, 128)
            k2, v2 = keys_and_values(kvf[c, pl.ds(t, 128), :])
            kc[c, pl.ds(t, 128), :] = k2.astype(BF16)
            vt[c, :, pl.ds(t, 128)] = v2.T.astype(BF16)
            return carry

        lax.fori_loop(0, 48, prepare, 0, unroll=2)

        def prepare_q(i, carry):
            c, t = i // 12, pl.multiple_of(lax.rem(i, 12) * 128, 128)
            qc[c, pl.ds(t, 128), :] = query_quads(qf[c, pl.ds(t, 128), :])
            return carry

        lax.fori_loop(0, 24, prepare_q, 0, unroll=2)

        keys4, e4, (qc4, qv4) = class_facts4(offs[3], b)
        kc5, kv5 = lax.rem(offs[4], 4), offs[4] // 4
        for blk in range(4):
            r = slice(128 * blk, 128 * blk + 128)
            for e in range(2):
                c, v = keys4[e]
                k2, v2 = keys_and_values(kvf[c, pl.ds(v + 384 * blk, 128, stride=3), :])
                k4[e, r, :] = k2.astype(BF16)
                vt4[e, :, r] = v2.T.astype(BF16)
            q4[r, :] = query_quads(qf[qc4 - 2 * b, pl.ds(qv4 + 384 * blk, 128, stride=3), :])
            k2, v2 = keys_and_values(kvf[kc5, pl.ds(kv5 + 384 * blk, 128, stride=3), :])
            k5[r, :] = k2.astype(BF16)
            vt5[:, r] = v2.T.astype(BF16)
            q5[r, :] = query_quads(qf[lax.rem(kc5, 2), pl.ds(kv5 + 384 * blk, 128, stride=3), :])

        b1[...] = key_bias((2, 128), (4, 128), 4, 1, 2 * b, True)
        b2[...] = key_bias((1, 256), (2, 256), 4, 2, 2 * b, True)
        b3[...] = key_bias((1, 256), (1, 256), 1, 1, 0, True)
        b4[...] = key_bias((1, 256), (2, 256), 12, 6, 6 * e4, True)

        def tile(g, q, k, vT, bias, first):
            s = dot_nt(doubled(k), q)
            if bias is not None:
                s = s + bias[...]
            m = jnp.max(s, 0, keepdims=True)
            if not first:
                old = ml[g, 0:1, :]
                m = jnp.maximum(old, m)
            p = jnp.exp(s - m)
            total = jnp.sum(p, 0, keepdims=True)
            hi, lo = split(p)
            new = dot_nn(doubled(vT), jnp.concatenate([hi, lo], 0))
            if first:
                acc[g] = new
            else:
                alpha = jnp.exp(old - m)
                acc[g] = acc[g] * alpha + new
                total = ml[g, 1:2, :] * alpha + total
            ml[g, 0:1, :] = m
            ml[g, 1:2, :] = total

        def closed(pattern, g):
            m, l = ml[g, 0:1, :], ml[g, 1:2, :]
            rows = m + jnp.log(l)
            sums[pattern : pattern + 1, :] += rows[:, :128] + rows[:, 128:]
            o = acc[g]
            return jnp.concatenate(
                [o[:HD] + o[HD:], jnp.broadcast_to(l, (32, 256)), jnp.broadcast_to(m, (32, 256))], 0
            ).T

        def q1(qb, carry):
            def at(g, blk):
                return pl.ds(pl.multiple_of(512 * g + 128 * blk, 128), 128)

            def step(kb, bias, first):
                for g in range(3):
                    ks = at(g, kb)
                    vT = jnp.concatenate([vt[c, :, ks] for c in range(4)], 1)
                    tile(g, qc[:, at(g, qb), :].reshape(256, 256), kc[:, ks, :].reshape(512, 128), vT, bias, first)

            step(qb, b1, True)

            def more(kb, inner):
                step(kb, None, False)
                return inner

            lax.fori_loop(0, qb, more, 0)
            for g in range(3):
                R[:, at(g, qb), :] = closed(0, g).reshape(2, 128, 128)
            return carry

        lax.fori_loop(0, 4, q1, 0)

        def merge(pattern, g, ci, rows):
            r0, r1 = R[ci, rows, :], closed(pattern, g)
            m0 = jnp.broadcast_to(r0[:, 96:97], r0.shape)
            m1 = jnp.broadcast_to(r1[:, 96:97], r1.shape)
            m = jnp.maximum(m0, m1)
            both = r0 * jnp.exp(m0 - m) + r1 * jnp.exp(m1 - m)
            lane = lax.broadcasted_iota(jnp.int32, r0.shape, 1)
            R[ci, rows, :] = jnp.where(lane < 96, both, m)

        def at256(blk):
            return pl.ds(pl.multiple_of(256 * blk, 128), 256)

        par = offs[1]

        def step2(g, q, kb, bias, first):
            ks = at256(kb)
            k = jnp.concatenate([kc[par, ks, :], kc[par + 2, ks, :]], 0)
            vT = jnp.concatenate([vt[par, :, ks], vt[par + 2, :, ks]], 1)
            tile(g, q, k, vT, bias, first)

        def q2(qb, carry):
            q = qc[par, at256(qb), :]
            step2(0, q, qb, b2, True)

            def more(kb, inner):
                step2(0, q, kb, None, False)
                return inner

            lax.fori_loop(jnp.where(qb >= 4, 4, 0), qb, more, 0)
            merge(1, 0, par, at256(qb))
            return carry

        lax.fori_loop(0, TOTAL // 256, q2, 0)

        o3 = offs[2]

        @pl.when(o3 // 2 == b)
        def _():
            ci = lax.rem(o3, 2)

            def step3(g, qb, kb, bias, first):
                tile(g, qc[ci, at256(qb), :], kc[o3, at256(kb), :], vt[o3, :, at256(kb)], bias, first)

            def q3(pair, carry):
                q0, q1_ = 2 * pair, 2 * pair + 1
                step3(0, q0, q0, b3, True)
                step3(1, q1_, q1_, b3, True)

                def more(kb, inner):
                    step3(0, q0, kb, None, False)
                    step3(1, q1_, kb, None, False)
                    return inner

                lax.fori_loop(0, q0, more, 0)
                step3(1, q1_, q0, None, False)
                merge(2, 0, ci, at256(q0))
                merge(2, 1, ci, at256(q1_))
                return carry

            lax.fori_loop(0, TOTAL // 512, q3, 0)

        for kb in range(2):
            for qb in range(kb, 2):
                order = qb - kb
                ks = slice(256 * order, 256 * order + 256)
                tile(
                    qb,
                    q4[256 * qb : 256 * qb + 256, :],
                    k4[:, ks, :].reshape(512, 128),
                    jnp.concatenate([vt4[0, :, ks], vt4[1, :, ks]], 1),
                    b4 if order == qb else None,
                    kb == 0,
                )
        for qb in range(2):
            merge(3, qb, qc4 - 2 * b, pl.ds(qv4 + 768 * qb, 256, stride=3))

        @pl.when(kc5 // 2 == b)
        def _():
            for kb in range(2):
                for qb in range(kb, 2):
                    order = qb - kb
                    ks = slice(256 * order, 256 * order + 256)
                    tile(
                        qb,
                        q5[256 * qb : 256 * qb + 256, :],
                        k5[ks, :],
                        vt5[:, ks],
                        b3 if order == qb else None,
                        kb == 0,
                    )
            for qb in range(2):
                merge(4, qb, lax.rem(kc5, 2), pl.ds(kv5 + 768 * qb, 256, stride=3))

        def finish(m, carry):
            ci = lax.rem(m, 2)
            rows = pl.ds(pl.multiple_of((m // 2) * ROWS, 64), ROWS)
            r = R[ci, rows, :]
            l = jnp.broadcast_to(r[:, HD : HD + 1], r.shape)
            out = r / l
            ap[m] = pick(out[:HALF], swap(out[HALF:]))
            lse[ci, rows, :] = jnp.broadcast_to(r[:, 96:97], r.shape) + jnp.log(l)
            return carry

        lax.fori_loop(0, HOMES, finish, 0, unroll=2)
        sums[...] = jnp.broadcast_to(jnp.sum(sums[...], -1, keepdims=True), (8, 128))


def attention_forward(info, own, sib):
    keys = pltpu.VMEM((4, TOTAL, 128), BF16)
    turned = pltpu.VMEM((4, 128, TOTAL), BF16)
    state = pltpu.VMEM((2, TOTAL, 128), F32)
    return pl.pallas_call(
        forward_kernel,
        out_shape=[
            jax.ShapeDtypeStruct((HOMES, HALF, 128), F32),
            jax.ShapeDtypeStruct((2, TOTAL, 128), F32),
            jax.ShapeDtypeStruct((8, 128), F32),
        ],
        in_specs=[SM, VM, VM],
        out_specs=[VM, VM, VM],
        scratch_shapes=[
            pltpu.VMEM((4, TOTAL, 128), F32),
            keys,
            turned,
            state,
            pltpu.VMEM((2, TOTAL, 256), BF16),
            pltpu.VMEM((2, THIRD, 128), BF16),
            pltpu.VMEM((2, 128, THIRD), BF16),
            pltpu.VMEM((THIRD, 256), BF16),
            pltpu.VMEM((THIRD, 128), BF16),
            pltpu.VMEM((128, THIRD), BF16),
            pltpu.VMEM((THIRD, 256), BF16),
            pltpu.VMEM((3, 128, 256), F32),
            pltpu.VMEM((3, 8, 256), F32),
            state,
            pltpu.VMEM((512, 256), F32),
            pltpu.VMEM((512, 256), F32),
            pltpu.VMEM((256, 256), F32),
            pltpu.VMEM((512, 256), F32),
        ],
        compiler_params=params(),
    )(info, own, sib)


def rows_from_pairs(rec, dst):
    for j in range(HEADS // 2):
        u, v = rec[2 * j], rec[2 * j + 1]
        cols = slice(128 * j, 128 * j + 128)
        dst[0:HALF, cols] = pick(u, swap(v))
        dst[HALF:ROWS, cols] = pick(swap(u), v)


def pairs_from_rows(src, dst):
    for j in range(HEADS // 2):
        top = src[0:HALF, 128 * j : 128 * j + 128]
        bottom = src[HALF:ROWS, 128 * j : 128 * j + 128]
        dst[2 * j] = pick(top, swap(bottom))
        dst[2 * j + 1] = pick(swap(top), bottom)


def halves_sum(r):
    return r[:ROWS] + r[ROWS:]


def norm_back(f, n, rs):
    return (f - jnp.mean(f, -1, keepdims=True) - n * jnp.mean(f * n, -1, keepdims=True)) * rs


def put_turned(hi_ref, lo_ref, v):
    for j in range(D // 128):
        t = v[:, 128 * j : 128 * j + 128].T
        hi, lo = split(t)
        hi_ref[128 * j : 128 * j + 128, :] = hi
        lo_ref[128 * j : 128 * j + 128, :] = lo


FT = 512


class Spill:
    def __init__(self, tiles, sem):
        self.tiles, self.sem, self.count, self.open = tiles, sem, 0, [[], []]

    def emit(self, fill, copies):
        k = self.count % 2
        for c in self.open[k]:
            c.wait()
        fill(self.tiles.at[k])
        self.open[k] = copies(self.tiles.at[k], self.sem.at[k])
        for c in self.open[k]:
            c.start()
        self.count += 1

    def close(self):
        for k in range(2):
            for c in self.open[k]:
                c.wait()
            self.open[k] = []


def product(hi, lo, r_hi, r_lo, tile):
    def one(i, carry):
        rows = pl.ds(pl.multiple_of(i * 128, 128), 128)
        h, l = hi[rows, :], lo[rows, :]
        tile[rows, :] = dot_nn(h, r_hi[...]) + dot_nn(h, r_lo[...]) + dot_nn(l, r_hi[...])
        return carry

    lax.fori_loop(0, D // 128, one, 0)


def column_copies(G, chunk):
    def make(tile, sem):
        return [
            pltpu.make_async_copy(
                tile.at[pl.ds(24 * d, 24), :], G.at[d // 16, (d // 8) % 2, (d % 8) // 2, d % 2, chunk], sem.at[d]
            )
            for d in range(32)
        ]

    return make


def row_copies(G, part, chunk):
    def make(tile, sem):
        return [
            pltpu.make_async_copy(
                tile.at[pl.ds(24 * d, 24), :], G.at[part // 2, part % 2, d // 8, (d // 4) % 2, chunk + d % 4], sem.at[d]
            )
            for d in range(32)
        ]

    return make


def ff_kernel(rec, x_ref, g3, wo, wu, wd, gi1, gf1, gh1, sums, out3, dap, dy1_ref, S, G, lhs, lhs2, gi, gf, gh, gh_g, g_ref, out_ref, V, N1, U, GP, E, ACC, th, tl, r_hi, r_lo, tiles, sem):
    spill = Spill(tiles, sem)
    for wide, flat in ((gi, gi1), (gf, gf1), (gh, gh1)):
        wide[...] = flat[...][None, :]
    g_ref[...] = g3[...].reshape(ROWS, D)
    rows_from_pairs(rec, V)
    na, rs_a = normed(V[...])
    V[...] = na
    put_split(lhs, na * gi[...])
    for j in range(3):
        cols = slice(256 * j, 256 * j + 256)
        N1[:, cols] = x_ref[:, cols] + halves_sum(dot_nn(lhs[...], wo[:, cols]))
    y1 = N1[...]
    out_ref[...] = y1
    ny, rs_y = normed(y1)
    N1[...] = ny
    put_split(lhs, ny * gf[...])

    def up(j, su):
        cols = pl.ds(pl.multiple_of(j * FT, FT), FT)
        z = halves_sum(dot_nn(lhs[...], wu[:, cols]))
        phi = 0.5 * (1.0 + lax.erf(z * math.sqrt(0.5)))
        u = z * phi
        U[:, cols] = u
        GP[:, cols] = phi + z * jnp.exp(-0.5 * z * z) * (1.0 / math.sqrt(2.0 * math.pi))
        return su + jnp.sum(u, -1, keepdims=True)

    zero = jnp.zeros((ROWS, 1), F32)
    mean = lax.fori_loop(0, FF // FT, up, zero) * (1.0 / FF)

    def spread(j, sv):
        cols = pl.ds(pl.multiple_of(j * FT, FT), FT)
        c = U[:, cols] - mean
        return sv + jnp.sum(c * c, -1, keepdims=True)

    rs_u = lax.rsqrt(lax.fori_loop(0, FF // FT, spread, zero) * (1.0 / FF) + LN_EPSILON)
    ACC[...] = jnp.zeros_like(ACC)

    def lower(j, carry):
        cols = pl.ds(pl.multiple_of(j * FT, FT), FT)
        n = (U[:, cols] - mean) * rs_u
        U[:, cols] = n
        put_split(lhs2, n * gh[:, cols])
        ACC[...] += halves_sum(dot_nn(lhs2[...], wd[cols, :]))
        return carry

    lax.fori_loop(0, FF // FT, lower, 0)
    out3[...] = (out_ref[...] + ACC[...]).reshape(ROWS, 1, D)

    put_split(lhs, g_ref[...])

    def back_down(j, sums):
        cols = pl.ds(pl.multiple_of(j * FT, FT), FT)
        e = halves_sum(dot_nt(lhs[...], wd[cols, :]))
        n = U[:, cols]
        gh_g[:, cols] = jnp.sum(e * n, 0, keepdims=True)
        f = e * gh[:, cols]
        E[:, cols] = f
        return sums[0] + jnp.sum(f, -1, keepdims=True), sums[1] + jnp.sum(f * n, -1, keepdims=True)

    sf, sfn = lax.fori_loop(0, FF // FT, back_down, (zero, zero))
    mf, mfn = sf * (1.0 / FF), sfn * (1.0 / FF)
    ACC[...] = jnp.zeros_like(ACC)

    def back_up(j, carry):
        cols = pl.ds(pl.multiple_of(j * FT, FT), FT)
        dz = (E[:, cols] - mf - U[:, cols] * mfn) * rs_u * GP[:, cols]
        E[:, cols] = dz
        put_split(lhs2, dz)
        ACC[...] += halves_sum(dot_nt(lhs2[...], wu[:, cols]))
        return carry

    lax.fori_loop(0, FF // FT, back_up, 0)
    e = ACC[...]
    ny = N1[...]
    S[2:3, :] = jnp.sum(e * ny, 0, keepdims=True)
    dy1 = g_ref[...] + norm_back(e * gf[...], ny, rs_y)
    dy1_ref[...] = dy1
    put_split(lhs, dy1)
    for j in range(3):
        cols = slice(256 * j, 256 * j + 256)
        ACC[:, cols] = halves_sum(dot_nt(lhs[...], wo[cols, :]))
    e = ACC[...]
    na = V[...]
    S[1:2, :] = jnp.sum(e * na, 0, keepdims=True)
    S[0:1, :] = jnp.zeros((1, D), F32)
    for j in range(4):
        S[3 + j : 4 + j, :] = gh_g[:, D * j : D * j + D]
    lane = lax.broadcasted_iota(jnp.int32, (1, 128), 1)
    S[7:8, :] = jnp.zeros((1, D), F32)
    S[7:8, 0:128] = sum(jnp.where(lane == i, sums[i : i + 1, :], 0.0) for i in range(PATTERNS))
    ACC[...] = norm_back(e * gi[...], na, rs_a)
    pairs_from_rows(ACC, dap)

    put_turned(th, tl, na * gi[...])
    r_hi[...], r_lo[...] = split(dy1)
    spill.emit(lambda t: product(th, tl, r_hi, r_lo, t), column_copies(G, 0))
    put_turned(th, tl, ny * gf[...])
    for j in range(4):
        r_hi[...], r_lo[...] = split(E[:, D * j : D * j + D])
        spill.emit(lambda t: product(th, tl, r_hi, r_lo, t), column_copies(G, 1 + j))
    r_hi[...], r_lo[...] = split(g_ref[...])
    for j in range(4):
        cols = slice(D * j, D * j + D)
        put_turned(th, tl, U[:, cols] * gh[:, cols])
        spill.emit(lambda t: product(th, tl, r_hi, r_lo, t), row_copies(G, j, 5))
    spill.close()


PIECE = 24


def grad_shape(n):
    return jax.ShapeDtypeStruct((2, 2, 4, 2, n, PIECE, D), F32)


def tile_scratch():
    return [
        pltpu.VMEM((D, ROWS), BF16),
        pltpu.VMEM((D, ROWS), BF16),
        pltpu.VMEM((ROWS, D), BF16),
        pltpu.VMEM((ROWS, D), BF16),
        pltpu.VMEM((2, D, D), F32),
        pltpu.SemaphoreType.DMA((2, 32)),
    ]


def feed_forward(rec, x, g, wo, wu, wd, gi, gf, gh, sums):
    act = jax.ShapeDtypeStruct((ROWS, D), F32)
    wide = pltpu.VMEM((ROWS, FF), F32)
    thin = pltpu.VMEM((ROWS, D), F32)
    return pl.pallas_call(
        ff_kernel,
        out_shape=[
            jax.ShapeDtypeStruct((ROWS, 1, D), F32),
            jax.ShapeDtypeStruct((HEADS, HALF, 128), F32),
            act,
            jax.ShapeDtypeStruct((8, D), F32),
            grad_shape(9),
        ],
        in_specs=[VM] * 10,
        out_specs=[VM] * 4 + [ANY],
        scratch_shapes=[
            pltpu.VMEM((2 * ROWS, D), BF16),
            pltpu.VMEM((2 * ROWS, FT), BF16),
            pltpu.VMEM((1, D), F32),
            pltpu.VMEM((1, D), F32),
            pltpu.VMEM((1, FF), F32),
            pltpu.VMEM((1, FF), F32),
            thin,
            thin,
            thin,
            thin,
            wide,
            wide,
            wide,
            thin,
        ]
        + tile_scratch(),
        compiler_params=params(),
    )(rec, x, g, wo, wu, wd, gi, gf, gh, sums)


class Place:
    def __init__(self):
        p, s = lax.axis_index("pat"), lax.axis_index("seq")
        self.p, self.s = p, s
        self.x, self.core, self.z, self.y = p // 2, lax.rem(p, 2), s // 2, lax.rem(s, 2)
        self.peer = to(self.x * 2 + 1 - self.core, s)
        self.xn = to((1 - self.x) * 2 + self.core, s)
        self.yn = to(p, self.z * 2 + 1 - self.y)
        self.left, self.right = to(p, s - 2), to(p, s + 2)

    def greet(self, barrier):
        for d in (self.peer, self.xn, self.yn):
            pl.semaphore_signal(barrier, inc=1, device_id=d, device_id_type=MESH)

        @pl.when(self.z > 0)
        def _():
            pl.semaphore_signal(barrier, inc=1, device_id=self.left, device_id_type=MESH)

        @pl.when(self.z < 3)
        def _():
            pl.semaphore_signal(barrier, inc=1, device_id=self.right, device_id_type=MESH)

        return 3 + (self.z > 0).astype(jnp.int32) + (self.z < 3).astype(jnp.int32)


def remote(src, dst, a, b, d):
    return pltpu.make_async_remote_copy(
        src_ref=src, dst_ref=dst, send_sem=a, recv_sem=b, device_id=d, device_id_type=MESH
    )


class Chunk:
    def __init__(self, place, k, group, slot, own, osem, bufs, sems, put, x_first):
        self.at, self.k, self.group, self.slot, self.own, self.osem = place, k, group, slot, own, osem
        self.b0, self.b1, self.b2, self.bl, self.br = bufs
        self.sc, self.rc, self.s1, self.r1, self.s2, self.r2, self.sl, self.rl, self.sr, self.rr = sems
        self.put, self.x_first = put, x_first

    def core(self):
        k, c = self.k, 1 - self.at.core
        return [
            remote(self.group(i, c), self.b0.at[i], self.sc.at[k, i], self.rc.at[k, i], self.at.peer)
            for i in range(2)
        ]

    def load(self):
        return [
            pltpu.make_async_copy(self.group(i, self.at.core), self.own.at[i], self.osem.at[self.slot, i])
            for i in range(2)
        ]

    def one(self):
        k, at = self.k, self.at
        if self.x_first:
            return remote(self.b0.at[1 - at.x], self.b1, self.s1.at[k], self.r1.at[k], at.xn)
        return remote(self.b0.at[:, :, 1 - at.y], self.b1, self.s1.at[k], self.r1.at[k], at.yn)

    def two(self):
        k, at = self.k, self.at
        if self.x_first:
            return remote(self.b1.at[:, 1 - at.y], self.b2, self.s2.at[k], self.r2.at[k], at.yn)
        return remote(self.b1.at[1 - at.x], self.b2, self.s2.at[k], self.r2.at[k], at.xn)

    def rightward(self, i):
        k, part = self.k, pl.ds(i + 1, 3 - i)
        src = self.b2 if i == 0 else self.bl
        return remote(src.at[part], self.bl.at[part], self.sr.at[k], self.rl.at[k], self.at.right)

    def leftward(self, i):
        k, part = self.k, pl.ds(0, i)
        src = self.b2 if i == 3 else self.br
        return remote(src.at[part], self.br.at[part], self.sl.at[k], self.rr.at[k], self.at.left)

    def stage1(self):
        if self.own is not None:
            for c in self.load():
                c.wait()
        for c in self.core():
            c.wait_recv()
        if self.own is not None:
            self.b0[...] += self.own[...]
        else:
            for i in range(2):
                self.b0[i] += self.group(i, self.at.core)[...]
        self.one().start()

    def stage2(self):
        self.one().wait_recv()
        mine = self.b0[self.at.x] if self.x_first else self.b0[:, :, self.at.y]
        self.b1[...] += mine
        self.two().start()

    def stage3(self):
        self.two().wait_recv()
        mine = self.b1[:, self.at.y] if self.x_first else self.b1[self.at.x]
        self.b2[...] += mine

        @pl.when(self.at.z == 0)
        def _():
            self.rightward(0).start()

        @pl.when(self.at.z == 3)
        def _():
            self.leftward(3).start()

    def stage4(self):
        @pl.when(self.at.z == 1)
        def _():
            self.rightward(0).wait_recv()
            self.bl[2:4] += self.b2[2:4]
            self.rightward(1).start()

        @pl.when(self.at.z == 2)
        def _():
            self.leftward(3).wait_recv()
            self.br[0:2] += self.b2[0:2]
            self.leftward(2).start()

    def stage5(self):
        @pl.when(self.at.z == 2)
        def _():
            self.rightward(1).wait_recv()
            self.bl[3:4] += self.b2[3:4]
            self.rightward(2).start()

        @pl.when(self.at.z == 1)
        def _():
            self.leftward(2).wait_recv()
            self.br[0:1] += self.b2[0:1]
            self.leftward(1).start()

    def stage6(self):
        @pl.when(self.at.z == 3)
        def _():
            self.rightward(2).wait_recv()
            self.put(self.b2[3] + self.bl[3])

        @pl.when(self.at.z == 0)
        def _():
            self.leftward(1).wait_recv()
            self.put(self.b2[0] + self.br[0])

        @pl.when(self.at.z == 1)
        def _():
            self.put(self.b2[1] + self.bl[1] + self.br[1])

        @pl.when(self.at.z == 2)
        def _():
            self.put(self.b2[2] + self.bl[2] + self.br[2])

    def sent(self):
        for c in self.core() + [self.one(), self.two()]:
            c.wait_send()
        for i in range(4):

            @pl.when(self.at.z == i)
            def _(i=i):
                if i < 3:
                    self.rightward(i).wait_send()
                if i > 0:
                    self.leftward(i).wait_send()


class Reducer:
    def __init__(self, place, n, rows, parts, scratch, put, staged):
        self.place, self.n, self.parts, self.put, self.staged = place, n, parts, put, staged
        scratch = list(scratch)
        self.own = scratch.pop(0) if staged else None
        self.osem = scratch.pop(0) if staged else None
        self.c0, self.c1a, self.c1b, self.c2, self.zl, self.zr = scratch[:6]
        self.sems = scratch[6:16]
        self.pairs = (n + 1) // 2

    @staticmethod
    def scratch(n, rows, staged):
        dma = pltpu.SemaphoreType.DMA
        bufs = [(n, 2, 4, 2), ((n + 1) // 2, 4, 2), (max(n // 2, 1), 2, 4), (n, 4), (n, 4), (n, 4)]
        return (
            ([pltpu.VMEM((4, 2, 4, 2, rows, D), F32), dma((4, 2))] if staged else [])
            + [pltpu.VMEM(b + (rows, D), F32) for b in bufs]
            + [dma((n, 2)), dma((n, 2))]
            + [dma((n,)) for _ in range(8)]
        )

    def chunk(self, k, parity):
        slot = lax.rem(k, 4)
        b1 = (self.c1b if parity else self.c1a).at[k // 2]
        return Chunk(
            self.place,
            k,
            lambda i, c: self.parts(k).at[i, c],
            slot,
            self.own.at[slot] if self.staged else None,
            self.osem,
            (self.c0.at[k], b1, self.c2.at[k], self.zl.at[k], self.zr.at[k]),
            self.sems,
            lambda v: self.put(k, v),
            parity == 0,
        )

    def begin(self):
        def one(k, carry):
            for c in self.chunk(k, 0).core():
                c.start()
            return carry

        lax.fori_loop(0, self.n, one, 0)
        for k in range(min(2, self.n)):
            for c in self.chunk(jnp.int32(k), 0).load():
                c.start()

    def send(self, first, after):
        for k in range(first, after):
            for c in self.chunk(jnp.int32(k), 0).core():
                c.start()

    def one(self, stage, pair):
        for parity in range(2):
            k = jnp.int32(2 * pair + parity)

            @pl.when(jnp.logical_and(k >= 0, k < self.n))
            def _(k=k, parity=parity):
                if stage == 1 and self.staged:

                    @pl.when(k + 2 < self.n)
                    def _():
                        for c in self.chunk(k + 2, 0).load():
                            c.start()

                getattr(self.chunk(k, parity), f"stage{stage}")()

    def early(self, pair):
        self.one(1, pair)

    def step(self, tau):
        self.one(1, tau)
        for stage in range(2, 7):
            self.one(stage, tau - stage)

    def finish(self):
        def one(k, carry):
            for parity in range(2):

                @pl.when(lax.rem(k, 2) == parity)
                def _(parity=parity):
                    self.chunk(k, parity).sent()

            return carry

        lax.fori_loop(0, self.n, one, 0)


class SmallSum:
    def __init__(self, place, S, bufs, send, recv, put):
        self.at, self.S, self.send, self.recv, self.put = place, S, send, recv, put
        self.d0, self.d1, self.d2, self.dl, self.dr, self.t1, self.t2, self.t3, self.fl, self.fr = bufs

    @staticmethod
    def scratch():
        return [pltpu.VMEM((8, D), F32)] * 10 + [pltpu.SemaphoreType.DMA((5,)), pltpu.SemaphoreType.DMA((5,))]

    def hop(self, src, dst, i, d):
        return remote(src, dst, self.send.at[i], self.recv.at[i], d)

    def core(self):
        return self.hop(self.S, self.d0, 0, self.at.peer)

    def along_x(self):
        return self.hop(self.t1, self.d1, 1, self.at.xn)

    def along_y(self):
        return self.hop(self.t2, self.d2, 2, self.at.yn)

    def rightward(self, i):
        return self.hop(self.t3 if i == 0 else self.fl, self.dl, 3, self.at.right)

    def leftward(self, i):
        return self.hop(self.t3 if i == 3 else self.fr, self.dr, 4, self.at.left)

    def stage1(self):
        self.core().wait_recv()
        self.t1[...] = self.S[...] + self.d0[...]
        self.along_x().start()

    def stage2(self):
        self.along_x().wait_recv()
        self.t2[...] = self.t1[...] + self.d1[...]
        self.along_y().start()

    def stage3(self):
        self.along_y().wait_recv()
        self.t3[...] = self.t2[...] + self.d2[...]

        @pl.when(self.at.z == 0)
        def _():
            self.rightward(0).start()

        @pl.when(self.at.z == 3)
        def _():
            self.leftward(3).start()

    def from_left(self, i):
        self.rightward(i).wait_recv()
        self.fl[...] = self.dl[...] + self.t3[...]

    def from_right(self, i):
        self.leftward(i).wait_recv()
        self.fr[...] = self.dr[...] + self.t3[...]

    def stage4(self):
        @pl.when(self.at.z == 1)
        def _():
            self.from_left(0)
            self.rightward(1).start()

        @pl.when(self.at.z == 2)
        def _():
            self.from_right(3)
            self.leftward(2).start()

    def stage5(self):
        @pl.when(self.at.z == 2)
        def _():
            self.from_left(1)
            self.rightward(2).start()

        @pl.when(self.at.z == 1)
        def _():
            self.from_right(2)
            self.leftward(1).start()

    def stage6(self):
        @pl.when(self.at.z == 3)
        def _():
            self.from_left(2)
            self.put(self.fl[...])

        @pl.when(self.at.z == 0)
        def _():
            self.from_right(1)
            self.put(self.fr[...])

        @pl.when(jnp.logical_or(self.at.z == 1, self.at.z == 2))
        def _():
            self.put(self.fl[...] + self.dr[...])

    def finish(self):
        for c in (self.core(), self.along_x(), self.along_y()):
            c.wait_send()
        for i in range(4):

            @pl.when(self.at.z == i)
            def _(i=i):
                if i < 3:
                    self.rightward(i).wait_send()
                if i > 0:
                    self.leftward(i).wait_send()


def small_outputs(place, counts, outs, tot):
    ga, gi, gf, gh, means = outs

    def put(v):
        tot[...] = v
        d = place.p * RUNS + place.s
        for i, ref in enumerate((ga, gi, gf)):
            ref[...] = pltpu.roll(tot[i : i + 1, :], D - PIECE * d, 1)[:, :PIECE]
        row = tot[pl.ds(3 + d // 8, 1), :]
        gh[...] = pltpu.roll(row, D - 4 * PIECE * lax.rem(d, 8), 1)[:, : 4 * PIECE]
        lane = lax.broadcasted_iota(jnp.int32, (1, 128), 1)
        scale = jnp.full((1, 128), counts[0], F32)
        for i in range(1, PATTERNS):
            scale = jnp.where(lane == i, counts[i], scale)
        means[...] = (tot[7:8, :128] / scale)[:, :PATTERNS]

    return put


N_PIECES = 9
SUB = 8


def finish_kernel(counts, rec, x_ref, dy1_ref, w, ga1, S_in, gx, g_qkv, ga, gi, gf, gh, means, dqkv, lhs, th, tl, r_hi, r_lo, tiles, S, tot, *scratch):
    place = Place()
    barrier = pltpu.get_barrier_semaphore()
    expected = place.greet(barrier)
    for j in range(HEADS // 2):
        u, v = rec[2 * j, ROWS:PACK, :], rec[2 * j + 1, ROWS:PACK, :]
        cols = slice(128 * j, 128 * j + 128)
        dqkv[0:HALF, cols] = pick(u, swap(v))
        dqkv[HALF:ROWS, cols] = pick(swap(u), v)
        u, v = rec[2 * j, 0:ROWS, :], rec[2 * j + 1, 0:ROWS, :]
        dqkv[:, D + 128 * j : D + 128 * j + 128] = pick(u, swap(v))
        dqkv[:, 2 * D + 128 * j : 2 * D + 128 * j + 128] = pick(swap(u), v)
    gain = ga1[...][None, :]
    n, rs = normed(x_ref[...])
    put_turned(th, tl, n * gain)

    def parts(k):
        return tiles.at[k // 3, :, :, :, :, pl.ds(pl.multiple_of(lax.rem(k, 3) * SUB, SUB), SUB), :]

    def put(k, v):
        g_qkv[
            pl.ds(pl.multiple_of(lax.rem(k, 3) * SUB, SUB), SUB), pl.ds(pl.multiple_of((k // 3) * D, D), D)
        ] = v

    n_r = 16
    big = Reducer(place, N_PIECES, SUB, parts, scratch[:n_r], put, False)
    rest = scratch[n_r:]
    small = SmallSum(
        place, S, rest[:10], rest[10], rest[11], small_outputs(place, counts, (ga, gi, gf, gh, means), tot)
    )
    for j in range(3):
        r_hi[...], r_lo[...] = split(dqkv[:, D * j : D * j + D])

        def one(i, carry):
            rows = pl.ds(pl.multiple_of(i * ROWS, 64), ROWS)
            h, l = th[rows, :], tl[rows, :]
            v = dot_nn(h, r_hi[...]) + dot_nn(h, r_lo[...]) + dot_nn(l, r_hi[...])
            tiles[j, i // 2, lax.rem(i, 2)] = v.reshape(4, 2, PIECE, D)
            return carry

        lax.fori_loop(0, 4, one, 0)
        if j == 0:
            pl.semaphore_wait(barrier, expected)
        big.send(3 * j, 3 * j + 3)
    big.early(0)
    big.early(1)
    e = None
    for j in range(3):
        cols = slice(D * j, D * j + D)
        put_split(lhs, dqkv[:, cols])
        more = halves_sum(dot_nt(lhs[...], w[:, cols]))
        e = more if e is None else e + more
        if j == 0:
            big.step(2)
    S[...] = S_in[...]
    S[0:1, :] = jnp.sum(e * n, 0, keepdims=True)
    small.core().start()
    gx[...] = (dy1_ref[...] + norm_back(e * gain, n, rs)).reshape(ROWS, 1, D)
    small.stage1()

    def step(tau, carry):
        for stage in range(2, 7):

            @pl.when(tau == stage + 1)
            def _(stage=stage):
                getattr(small, f"stage{stage}")()

        big.step(tau)
        return carry

    lax.fori_loop(3, big.pairs + 6, step, 0)

    def close(k, carry):
        for parity in range(2):

            @pl.when(lax.rem(k, 2) == parity)
            def _(parity=parity):
                big.chunk(k, parity).sent()

        return carry

    lax.fori_loop(0, N_PIECES, close, 0)
    small.finish()


def finish(rec, x, dy1, w, ga, S, counts, cid):
    return pl.pallas_call(
        functools.partial(finish_kernel, counts),
        out_shape=[jax.ShapeDtypeStruct((ROWS, 1, D), F32), jax.ShapeDtypeStruct((PIECE, 3 * D), F32)]
        + [jax.ShapeDtypeStruct((1, n), F32) for n in (PIECE, PIECE, PIECE, 4 * PIECE, PATTERNS)],
        in_specs=[VM] * 6,
        out_specs=[VM] * 7,
        scratch_shapes=[
            pltpu.VMEM((ROWS, 3 * D), F32),
            pltpu.VMEM((2 * ROWS, D), BF16),
            pltpu.VMEM((D, ROWS), BF16),
            pltpu.VMEM((D, ROWS), BF16),
            pltpu.VMEM((ROWS, D), BF16),
            pltpu.VMEM((ROWS, D), BF16),
            pltpu.VMEM((3, 2, 2, 4, 2, PIECE, D), F32),
            pltpu.VMEM((8, D), F32),
            pltpu.VMEM((8, D), F32),
        ]
        + Reducer.scratch(N_PIECES, SUB, False)
        + SmallSum.scratch(),
        compiler_params=params(collective_id=cid, has_side_effects=True),
    )(rec, x, dy1, w, ga, S)


def deliver_kernel(*refs):
    n = len(refs) // 2
    for src, dst in zip(refs[:n], refs[n:]):
        dst[...] = src[...]


def deliver(*arrays):
    return pl.pallas_call(
        deliver_kernel,
        out_shape=[jax.ShapeDtypeStruct(v.shape, v.dtype) for v in arrays],
        in_specs=[VM] * len(arrays),
        out_specs=[VM] * len(arrays),
        compiler_params=params(),
    )(*arrays)


N_FF = 9


def back_all_kernel(offs, dap, own, sib, ap, lse, G, grec, wo_g, up_g, down_g, drec, qst, kc, vc, kt, qc, dc, lt, k4, v4, kt4, q4, d4, lt4, k5, v5, kt5, q5, d5, lt5, dqt, dk, dv, dq, dk4, dv4, dk5, dv5, dq4, dq5, b1, b2, b3, b4, ds_out, came, lsem, dsend, drecv, send, recv, qsend, qrecv, fsend, frecv, *scratch):
    place = Place()
    p, s, x, core, active, head = place_facts()
    b = core
    o2, o3, o4, o5 = offs[1], offs[2], offs[3], offs[4]
    kvf, qf, X, df = dk, dv.at[0:2], dv.at[2:4], dq
    dqp = qst

    barrier = pltpu.get_barrier_semaphore()
    expected = place.greet(barrier)
    expected = expected + HEADS - jnp.logical_and(active, core == x).astype(jnp.int32)

    @pl.when(active)
    def _():
        def greet(m, carry):
            q, t = home_device(core, m)

            @pl.when(jnp.logical_not(same(p, s, q, t)))
            def _():
                pl.semaphore_signal(barrier, inc=1, device_id=to(q, t), device_id_type=MESH)

            return carry

        lax.fori_loop(0, HOMES, greet, 0)

    def greet_heads(h, carry):
        q, t = head_device(h, x)

        @pl.when(jnp.logical_not(same(p, s, q, t)))
        def _():
            pl.semaphore_signal(barrier, inc=1, device_id=to(q, t), device_id_type=MESH)

        return carry

    lax.fori_loop(0, HEADS, greet_heads, 0)
    from_homes = HOMES - (core == x).astype(jnp.int32)
    pl.semaphore_wait(barrier, expected + active.astype(jnp.int32) * from_homes)

    slot = s * 2 + core

    def da_copy(h):
        q, t = head_device(h, x)
        return q, t, remote(dap.at[h], drec.at[slot], dsend.at[h], drecv.at[slot], to(q, t))

    def da_start(j, carry):
        h = lax.rem(j + 3 * (s // 2) + 2 * p, HEADS)
        q, t, far = da_copy(h)

        @pl.when(same(p, s, q, t))
        def _():
            pltpu.make_async_copy(dap.at[h], drec.at[slot], drecv.at[slot]).start()

        @pl.when(jnp.logical_not(same(p, s, q, t)))
        def _():
            far.start()

        return carry

    lax.fori_loop(0, HEADS, da_start, 0)

    def put(k, v):
        @pl.when(k == 0)
        def _():
            wo_g[...] = v

        @pl.when(jnp.logical_and(k > 0, k < 5))
        def _():
            up_g[:, pl.ds(pl.multiple_of((k - 1) * D, D), D)] = v

        @pl.when(k >= 5)
        def _():
            down_g[pl.ds(pl.multiple_of((k - 5) * PIECE, PIECE), PIECE), :] = v

    big = Reducer(place, N_FF, PIECE, lambda k: G.at[:, :, :, :, k], scratch, put, True)
    big.begin()

    def local_copies(m):
        t = pl.multiple_of((m // 2) * ROWS, 64)
        c, d = 2 * b + lax.rem(m, 2), 2 * (1 - b) + lax.rem(m, 2)
        return [
            pltpu.make_async_copy(own.at[m, pl.ds(0, ROWS), :], kvf.at[c, pl.ds(t, ROWS), :], lsem.at[m, 0]),
            pltpu.make_async_copy(sib.at[m], kvf.at[d, pl.ds(t, ROWS), :], lsem.at[m, 1]),
            pltpu.make_async_copy(own.at[m, pl.ds(ROWS, HALF), :], qst.at[m], lsem.at[m, 2]),
        ]

    lse_copy = pltpu.make_async_copy(lse, X, lsem.at[HOMES, 0])

    @pl.when(active)
    def _():
        lse_copy.start()

        def start(m, carry):
            for c in local_copies(m):
                c.start()
            return carry

        lax.fori_loop(0, HOMES, start, 0)
        b1[...] = key_bias((2, 128), (4, 128), 4, 1, 2 * b, True)
        b2[...] = key_bias((1, 256), (2, 256), 4, 2, 2 * b, True)
        b3[...] = key_bias((1, 256), (1, 256), 1, 1, 0, True)
        e4 = class_facts4(o4, b)[1]
        b4[...] = key_bias((1, 256), (2, 256), 12, 6, 6 * e4, True)

        def wait(m, carry):
            for c in local_copies(m):
                c.wait()
            return carry

        lax.fori_loop(0, HOMES, wait, 0)
        lse_copy.wait()
        unpack_pairs(qst, 0, qf, 1.0 / math.sqrt(HD))

        def prepare(i, carry):
            c, t = i // 12, pl.multiple_of(lax.rem(i, 12) * 128, 128)
            k2, v2 = keys_and_values(kvf[c, pl.ds(t, 128), :])
            kc[c, pl.ds(t, 128), :] = k2.astype(BF16)
            vc[c, pl.ds(t, 128), :] = v2.astype(BF16)
            kt[c, :, pl.ds(t, 128)] = k2.T.astype(BF16)
            return carry

        lax.fori_loop(0, 48, prepare, 0)

        def prepare_q(i, carry):
            c, t = i // 12, pl.multiple_of(lax.rem(i, 12) * 128, 128)
            qc[c, pl.ds(t, 128), :] = query_quads(qf[c, pl.ds(t, 128), :])
            return carry

        lax.fori_loop(0, 24, prepare_q, 0)

    keys4, e4, (qc4, qv4) = class_facts4(o4, b)
    kc5, kv5 = lax.rem(o5, 4), o5 // 4
    qi4, qi5 = qc4 - 2 * b, lax.rem(kc5, 2)

    @pl.when(active)
    def _():
        for blk in range(4):
            r = slice(128 * blk, 128 * blk + 128)
            for e in range(2):
                c, v = keys4[e]
                k2, v2 = keys_and_values(kvf[c, pl.ds(v + 384 * blk, 128, stride=3), :])
                k4[e, r, :] = k2.astype(BF16)
                v4[e, r, :] = v2.astype(BF16)
                kt4[e, :, r] = k2.T.astype(BF16)
            q4[r, :] = query_quads(qf[qi4, pl.ds(qv4 + 384 * blk, 128, stride=3), :])
            rows = pl.ds(kv5 + 384 * blk, 128, stride=3)
            k2, v2 = keys_and_values(kvf[kc5, rows, :])
            k5[r, :] = k2.astype(BF16)
            v5[r, :] = v2.astype(BF16)
            kt5[:, r] = k2.T.astype(BF16)
            q5[r, :] = query_quads(qf[qi5, rows, :])
        dk[...] = jnp.zeros_like(dk)

    big.early(0)
    big.early(1)

    @pl.when(active)
    def _():
        def arrive(m, carry):
            pltpu.make_async_copy(drec.at[m], drec.at[m], drecv.at[m]).wait()
            return carry

        lax.fori_loop(0, HOMES, arrive, 0)
        unpack_pairs(drec, 0, df, 1.0)

        def facts(m, carry):
            ci = lax.rem(m, 2)
            t = pl.multiple_of((m // 2) * ROWS, 32)
            prod = drec[m] * ap[m]
            low = lower_lanes(prod)
            d0 = jnp.sum(jnp.where(low, prod, 0.0), -1, keepdims=True)
            d1 = jnp.sum(jnp.where(low, 0.0, prod), -1, keepdims=True)
            for part, d in ((0, d0), (1, d1)):
                rows = pl.ds(t + HALF * part, HALF)
                l = X[ci, rows, :]
                X[ci, rows, :] = jnp.where(low, l, jnp.broadcast_to(d, l.shape))
            return carry

        lax.fori_loop(0, HOMES, facts, 0)

        def turned(v):
            w = v.T
            return jnp.concatenate([w[0:1, :], w[HD : HD + 1, :]], 0)

        def prepare_d(i, carry):
            c, t = i // 12, pl.multiple_of(lax.rem(i, 12) * 128, 128)
            rows = pl.ds(t, 128)
            dc[c, rows, :] = query_quads(df[c, rows, :])
            lt[i] = turned(X[c, rows, :])
            return carry

        lax.fori_loop(0, 24, prepare_d, 0)
        for blk in range(4):
            r = slice(128 * blk, 128 * blk + 128)
            rows = pl.ds(qv4 + 384 * blk, 128, stride=3)
            d4[r, :] = query_quads(df[qi4, rows, :])
            lt4[blk] = turned(X[qi4, rows, :])
            rows = pl.ds(kv5 + 384 * blk, 128, stride=3)
            d5[r, :] = query_quads(df[qi5, rows, :])
            lt5[blk] = turned(X[qi5, rows, :])
        dv[...] = jnp.zeros_like(dv)

    big.step(2)

    def tile(g, k, v, kT, q, d, facts_pair, bias, first):
        s_ = dot_nt(doubled(k), q)
        if bias is not None:
            s_ = s_ + bias[...]
        l0, l1 = facts_pair
        row = jnp.concatenate([l0[0:1, :], l1[0:1, :]], 1)
        delta = jnp.concatenate([l0[1:2, :], l1[1:2, :]], 1)
        pr = jnp.exp(s_ - row)
        ds = pr * (dot_nt(doubled(v), d) - delta)
        hi, lo = split(pr)
        d2, q2_ = d[:, :128], q[:, :128]
        dv_new = dot_nn(jnp.concatenate([hi, lo], 1), jnp.concatenate([d2, d2], 0))
        hi, lo = split(ds)
        dk_new = dot_nn(jnp.concatenate([hi, lo], 1), jnp.concatenate([q2_, q2_], 0))
        dq_new = dot_nn(doubled(kT), jnp.concatenate([hi, lo], 0))
        dqt[g] = dq_new if first else dqt[g] + dq_new
        return dk_new, dv_new

    def q1(qb, carry):
        def at(g, blk):
            return pl.ds(pl.multiple_of(512 * g + 128 * blk, 128), 128)

        def step(kb, bias, first):
            for g in range(3):
                ks, qs = at(g, kb), at(g, qb)
                kT = jnp.concatenate([kt[c, :, ks] for c in range(4)], 1)
                a, c = tile(
                    g,
                    kc[:, ks, :].reshape(512, 128),
                    vc[:, ks, :].reshape(512, 128),
                    kT,
                    qc[:, qs, :].reshape(256, 256),
                    dc[:, qs, :].reshape(256, 256),
                    (lt.at[4 * g + qb], lt.at[12 + 4 * g + qb]),
                    bias,
                    first,
                )
                dk[:, ks, :] += a.reshape(4, 128, 128)
                dv[:, ks, :] += c.reshape(4, 128, 128)

        step(qb, b1, True)

        def more(kb, inner):
            step(kb, None, False)
            return inner

        lax.fori_loop(0, qb, more, 0)
        for g in range(3):
            dq[:, at(g, qb), :] = dqt[g].T.reshape(2, 128, 128)
        return carry

    for first, after, tau in ((0, 2, 3), (2, 3, 4), (3, 4, 5)):

        @pl.when(active)
        def _(first=first, after=after):
            lax.fori_loop(first, after, q1, 0)

        big.step(tau)

    def at256(blk):
        return pl.ds(pl.multiple_of(256 * blk, 128), 256)

    def kept(flag, v):
        return jnp.where(flag, v, 0.0)

    def q2(qb, carry):
        def step(kb, bias, first):
            ks, qs = at256(kb), at256(qb)
            a, c = tile(
                0,
                jnp.concatenate([kc[o2, ks, :], kc[o2 + 2, ks, :]], 0),
                jnp.concatenate([vc[o2, ks, :], vc[o2 + 2, ks, :]], 0),
                jnp.concatenate([kt[o2, :, ks], kt[o2 + 2, :, ks]], 1),
                qc[o2, qs, :],
                dc[o2, qs, :],
                (lt.at[12 * o2 + 2 * qb], lt.at[12 * o2 + 2 * qb + 1]),
                bias,
                first,
            )
            for par in range(2):
                f = o2 == par
                dk[par, ks, :] += kept(f, a[:256])
                dk[par + 2, ks, :] += kept(f, a[256:])
                dv[par, ks, :] += kept(f, c[:256])
                dv[par + 2, ks, :] += kept(f, c[256:])

        step(qb, b2, True)

        def more(kb, inner):
            step(kb, None, False)
            return inner

        lax.fori_loop(jnp.where(qb >= 4, 4, 0), qb, more, 0)
        for par in range(2):
            dq[par, at256(qb), :] += kept(o2 == par, dqt[0].T)
        return carry

    @pl.when(active)
    def _():
        lax.fori_loop(0, TOTAL // 256, q2, 0)

    big.step(6)

    def q3(qb, carry):
        ci = lax.rem(o3, 2)

        def step(kb, bias, first):
            ks, qs = at256(kb), at256(qb)
            a, c = tile(
                0,
                kc[o3, ks, :],
                vc[o3, ks, :],
                kt[o3, :, ks],
                qc[ci, qs, :],
                dc[ci, qs, :],
                (lt.at[12 * ci + 2 * qb], lt.at[12 * ci + 2 * qb + 1]),
                bias,
                first,
            )
            for i in range(2):
                f = o3 == 2 * b + i
                dk[2 * b + i, ks, :] += kept(f, a)
                dv[2 * b + i, ks, :] += kept(f, c)

        step(qb, b3, True)

        def more(kb, inner):
            step(kb, None, False)
            return inner

        lax.fori_loop(0, qb, more, 0)
        for i in range(2):
            dq[i, at256(qb), :] += kept(o3 == 2 * b + i, dqt[0].T)
        return carry

    for first, after, tau in ((0, 4, 7), (4, 6, 8)):

        @pl.when(active)
        def _(first=first, after=after):
            lax.fori_loop(first, after, q3, 0)

        big.step(tau)

    @pl.when(active)
    def _():
        for ref in (dk4, dv4, dk5, dv5):
            ref[...] = jnp.zeros_like(ref)
        for qb in range(2):
            qs = slice(256 * qb, 256 * qb + 256)
            for kb in range(qb, -1, -1):
                ks = slice(256 * kb, 256 * kb + 256)
                a, c = tile(
                    0,
                    k4[:, ks, :].reshape(512, 128),
                    v4[:, ks, :].reshape(512, 128),
                    jnp.concatenate([kt4[0, :, ks], kt4[1, :, ks]], 1),
                    q4[qs, :],
                    d4[qs, :],
                    (lt4.at[2 * qb], lt4.at[2 * qb + 1]),
                    b4 if kb == qb else None,
                    kb == qb,
                )
                dk4[:, ks, :] += a.reshape(2, 256, 128)
                dv4[:, ks, :] += c.reshape(2, 256, 128)
                a, c = tile(
                    1,
                    k5[ks, :],
                    v5[ks, :],
                    kt5[:, ks],
                    q5[qs, :],
                    d5[qs, :],
                    (lt5.at[2 * qb], lt5.at[2 * qb + 1]),
                    b3 if kb == qb else None,
                    kb == qb,
                )
                dk5[ks, :] += a
                dv5[ks, :] += c
            dq4[qs, :] = dqt[0].T
            dq5[qs, :] = dqt[1].T
        mine5 = kc5 // 2 == b
        for kind in range(12):
            c, rows = kind % 4, pl.ds(kind // 4, THIRD, stride=3)
            f0, f1, f5 = o4 == kind, o4 + 6 == kind, jnp.logical_and(o5 == kind, mine5)
            dk[c, rows, :] += kept(f0, dk4[0]) + kept(f1, dk4[1]) + kept(f5, dk5[...])
            dv[c, rows, :] += kept(f0, dv4[0]) + kept(f1, dv4[1]) + kept(f5, dv5[...])
        for ci in range(2):
            for v in range(3):
                rows = pl.ds(v, THIRD, stride=3)
                f4 = jnp.logical_and(qi4 == ci, qv4 == v)
                f5 = jnp.logical_and(jnp.logical_and(qi5 == ci, kv5 == v), mine5)
                dq[ci, rows, :] += kept(f4, dq4[...]) + kept(f5, dq5[...])

    big.step(9)

    def passed(m):
        return remote(ds_out.at[m], came.at[m], fsend.at[m], frecv.at[m], place.peer)

    def home_copies(m):
        q, t = home_device(core, m)
        kv = remote(came.at[m], grec.at[head, pl.ds(0, ROWS), :], send.at[m], recv.at[head], to(q, t))
        dq_ = remote(dqp.at[m], grec.at[head, pl.ds(ROWS, HALF), :], qsend.at[m], qrecv.at[head], to(q, t))
        return q, t, kv, dq_

    @pl.when(active)
    def _():
        def rows_of(m):
            return pl.ds(pl.multiple_of((m // 2) * ROWS, 64), ROWS)

        def kv(c, m):
            k, v = dk[c, rows_of(m), :], dv[c, rows_of(m), :]
            return pick(k + swap(k), v + swap(v))

        def share(m, carry):
            ds_out[m] = kv(2 * (1 - b) + lax.rem(m, 2), m)
            passed(m).start()
            return carry

        lax.fori_loop(0, HOMES, share, 0)

        def add(m, carry):
            q, t, far_kv, far_q = home_copies(m)
            ci = lax.rem(m, 2)
            v = dq[ci, rows_of(m), :]
            v = (v + swap(v)) * (1.0 / math.sqrt(HD))
            dqp[m] = pick(v[:HALF], v[HALF:])
            passed(m).wait_recv()
            came[m] += kv(2 * b + ci, m)

            @pl.when(same(p, s, q, t))
            def _():
                pltpu.make_async_copy(came.at[m], grec.at[head, pl.ds(0, ROWS), :], recv.at[head]).start()
                pltpu.make_async_copy(dqp.at[m], grec.at[head, pl.ds(ROWS, HALF), :], qrecv.at[head]).start()

            @pl.when(jnp.logical_not(same(p, s, q, t)))
            def _():
                far_kv.start()
                far_q.start()

            return carry

        lax.fori_loop(0, HOMES, add, 0)

    big.step(10)

    def from_head(h, carry):
        a = grec.at[h, pl.ds(0, ROWS), :]
        c = grec.at[h, pl.ds(ROWS, HALF), :]
        pltpu.make_async_copy(a, a, recv.at[h]).wait()
        pltpu.make_async_copy(c, c, qrecv.at[h]).wait()
        return carry

    lax.fori_loop(0, HEADS, from_head, 0)
    big.finish()

    @pl.when(active)
    def _():
        def sent(m, carry):
            q, t, far_kv, far_q = home_copies(m)
            passed(m).wait_send()

            @pl.when(jnp.logical_not(same(p, s, q, t)))
            def _():
                far_kv.wait_send()
                far_q.wait_send()

            return carry

        lax.fori_loop(0, HOMES, sent, 0)

    def da_sent(h, carry):
        q, t, far = da_copy(h)

        @pl.when(jnp.logical_not(same(p, s, q, t)))
        def _():
            far.wait_send()

        return carry

    lax.fori_loop(0, HEADS, da_sent, 0)


def backward_all(offs, dap, own, sib, ap, lse, G, cid):
    dma = pltpu.SemaphoreType.DMA
    keys = pltpu.VMEM((4, TOTAL, 128), BF16)
    full = pltpu.VMEM((4, TOTAL, 128), F32)
    quad = pltpu.VMEM((2, TOTAL, 256), BF16)
    quad3 = pltpu.VMEM((THIRD, 256), BF16)
    pair3 = pltpu.VMEM((THIRD, 128), BF16)
    turned = pltpu.VMEM((128, THIRD), BF16)
    facts3 = pltpu.VMEM((4, 2, 128), F32)
    out3 = pltpu.VMEM((THIRD, 128), F32)
    packs = pltpu.VMEM((HOMES, ROWS, 128), F32)
    halves = pltpu.VMEM((HOMES, HALF, 128), F32)
    return pl.pallas_call(
        back_all_kernel,
        out_shape=[
            jax.ShapeDtypeStruct((HEADS, PACK, 128), F32),
            jax.ShapeDtypeStruct((PIECE, D), F32),
            jax.ShapeDtypeStruct((PIECE, FF), F32),
            jax.ShapeDtypeStruct((4 * PIECE, D), F32),
        ],
        in_specs=[SM, ANY, ANY, ANY, VM, ANY, ANY],
        out_specs=[ANY, VM, VM, VM],
        scratch_shapes=[
            halves,
            halves,
            keys,
            keys,
            pltpu.VMEM((4, 128, TOTAL), BF16),
            quad,
            quad,
            pltpu.VMEM((24, 2, 128), F32),
            pltpu.VMEM((2, THIRD, 128), BF16),
            pltpu.VMEM((2, THIRD, 128), BF16),
            pltpu.VMEM((2, 128, THIRD), BF16),
            quad3,
            quad3,
            facts3,
            pair3,
            pair3,
            turned,
            quad3,
            quad3,
            facts3,
            pltpu.VMEM((3, 128, 256), F32),
            full,
            full,
            pltpu.VMEM((2, TOTAL, 128), F32),
            pltpu.VMEM((2, THIRD, 128), F32),
            pltpu.VMEM((2, THIRD, 128), F32),
            out3,
            out3,
            out3,
            out3,
            pltpu.VMEM((512, 256), F32),
            pltpu.VMEM((512, 256), F32),
            pltpu.VMEM((256, 256), F32),
            pltpu.VMEM((512, 256), F32),
            packs,
            packs,
            dma((HOMES + 1, 3)),
            dma((HEADS,)),
            dma((HOMES,)),
            dma((HOMES,)),
            dma((HEADS,)),
            dma((HOMES,)),
            dma((HEADS,)),
            dma((HOMES,)),
            dma((HOMES,)),
        ]
        + Reducer.scratch(N_FF, PIECE, True),
        compiler_params=params(collective_id=cid, has_side_effects=True),
    )(offs, dap, own, sib, ap, lse, G)


SEG1, SEG2, SEG3, SEG4, SEG5 = SEGMENTS
DILATION_ONE, DILATION_TWO, DILATION_THREE, DILATION_FOUR, DILATION_FIVE = DILATIONS
MASK_VALUE = -1e30
MATMUL_ACCURACY = lax.Precision.HIGHEST


def passed_along(value, axis, by):
    length = lax.axis_size(axis)
    return lax.ppermute(value, axis, [(i, (i + by) % length) for i in range(length)])


def run_is_live(distance, anchor_point, sequence_width, segment_length):
    return (anchor_point - (distance - 1) * sequence_width - 1) // segment_length == anchor_point // segment_length


def layer_norm(x, gain_vec):
    average = jnp.mean(x, -1, keepdims=True)
    centred = x - average
    variance = jnp.mean(centred * centred, -1, keepdims=True)
    return centred * lax.rsqrt(variance + LN_EPSILON) * gain_vec


def select_table(offsets_row, dilation_rate):
    return (jnp.arange(dilation_rate, dtype=jnp.int32)[:, None] == offsets_row[None, :]).astype(
        jnp.float32
    )


def spread_apart(x, select_option, dilation_rate):
    shaped = x.reshape(x.shape[0] // dilation_rate, dilation_rate, x.shape[1], x.shape[2])
    return jnp.einsum("trhd,rh->thd", shaped, select_option, precision=MATMUL_ACCURACY)


def spread_scalar_rows(x, select_option, dilation_rate):
    shaped = x.reshape(x.shape[0] // dilation_rate, dilation_rate, x.shape[1])
    return jnp.einsum("trh,rh->th", shaped, select_option, precision=MATMUL_ACCURACY)


def spread_rows(x, select_option):
    return jnp.einsum("thd,rh->trhd", x, select_option, precision=MATMUL_ACCURACY).reshape(
        -1, x.shape[1], x.shape[2]
    )


def spread_scalars(x, select_option):
    return jnp.einsum("th,rh->trh", x, select_option, precision=MATMUL_ACCURACY).reshape(
        -1, x.shape[1]
    )


def masked_score_matrix(sparse_queries, key_portion, query_position, key_position, segment_length):
    score_matrix = jnp.einsum(
        "ozt,bzt->zob", sparse_queries, key_portion, precision=MATMUL_ACCURACY
    ) * (1.0 / math.sqrt(key_portion.shape[-1]))
    q_cols = query_position.T[:, :, None]
    k_cols = key_position.T[:, None, :]
    permitted_mask = (k_cols <= q_cols) & (k_cols // segment_length == q_cols // segment_length)
    return (jnp.where(permitted_mask, score_matrix, MASK_VALUE), permitted_mask)


def prepare_pattern(
    query_sequence, key_sequence, value_sequence, offsets_row, dilation_rate, anchor_point
):
    select_option = select_table(offsets_row, dilation_rate)
    sparse_queries = spread_apart(query_sequence, select_option, dilation_rate)
    sparse_key_value = jnp.stack(
        (
            spread_apart(key_sequence, select_option, dilation_rate),
            spread_apart(value_sequence, select_option, dilation_rate),
        )
    )
    query_position = (
        anchor_point
        + jnp.arange(sparse_queries.shape[0], dtype=jnp.int32)[:, None] * dilation_rate
        + offsets_row[None, :]
    )
    return (select_option, sparse_queries, sparse_key_value, query_position)


def pattern_forward_pass(
    sparse_queries,
    sparse_key_value,
    query_position,
    reach,
    segment_length,
    anchor_point,
    sequence_width,
):
    masked_logits, permitted_mask = masked_score_matrix(
        sparse_queries, sparse_key_value[0], query_position, query_position, segment_length
    )
    row_max = jnp.max(masked_logits, -1)
    softmax_weights = jnp.where(permitted_mask, jnp.exp(masked_logits - row_max[..., None]), 0.0)
    state = (
        row_max,
        jnp.sum(softmax_weights, -1),
        jnp.einsum("tlj,jtb->tlb", softmax_weights, sparse_key_value[1], precision=MATMUL_ACCURACY),
    )

    def one_run(distance, carry):
        remote_key_value, state = carry
        remote_key_value = passed_along(remote_key_value, "seq", 1)
        key_position = query_position - distance * sequence_width

        def update(state_in):
            old_max, old_sum, old_acc = state_in
            masked_remote, permitted_remote = masked_score_matrix(
                sparse_queries, remote_key_value[0], query_position, key_position, segment_length
            )
            new_max = jnp.maximum(old_max, jnp.max(masked_remote, -1))
            weights_far = jnp.where(
                permitted_remote, jnp.exp(masked_remote - new_max[..., None]), 0.0
            )
            factor = jnp.exp(old_max - new_max)
            added = jnp.einsum(
                "tlj,jtb->tlb", weights_far, remote_key_value[1], precision=MATMUL_ACCURACY
            )
            return (
                new_max,
                old_sum * factor + jnp.sum(weights_far, -1),
                old_acc * factor[..., None] + added,
            )

        def unchanged(state_in):
            return state_in

        is_live = run_is_live(distance, anchor_point, sequence_width, segment_length)
        return remote_key_value, lax.cond(is_live, update, unchanged, state)

    state = lax.fori_loop(1, reach + 1, one_run, (sparse_key_value, state))[1]
    row_max, row_sum, accumulated = state
    mixture = jnp.transpose(accumulated / row_sum[..., None], (1, 0, 2))
    log_sum = (row_max + jnp.log(row_sum)).T
    return (mixture, log_sum)


def merge_patterns(forwards, prepared_inputs):
    full_lse = []
    full_mix = []
    for pattern_spec in range(len(forwards)):
        mixture, log_sum = forwards[pattern_spec]
        select_option = prepared_inputs[pattern_spec][0]
        covered = spread_scalars(jnp.ones_like(log_sum), select_option)
        full_lse.append(spread_scalars(log_sum, select_option) + (covered - 1.0) * 1e30)
        full_mix.append(spread_rows(mixture, select_option))
    stacked = jnp.stack(full_lse)
    row_max = jnp.max(stacked, 0)
    softmax_weights = jnp.exp(stacked - row_max)
    row_sum = jnp.sum(softmax_weights, 0)
    attended = full_mix[0] * softmax_weights[0][..., None]
    for pattern_spec in range(1, len(full_mix)):
        attended = attended + full_mix[pattern_spec] * softmax_weights[pattern_spec][..., None]
    return (attended / row_sum[..., None], row_max + jnp.log(row_sum))


def pattern_backward(
    select_option,
    dilation_rate,
    segment_length,
    anchor_point,
    sparse_queries,
    sparse_key_value,
    query_position,
    reach,
    sequence_gradient,
    row_difference,
    combined_logsumexp,
):
    sequence_width = sequence_gradient.shape[0]
    sparse_gradient = spread_apart(sequence_gradient, select_option, dilation_rate)
    sparse_output_grad = spread_scalar_rows(row_difference, select_option, dilation_rate).T
    sparse_logsumexp = spread_scalar_rows(combined_logsumexp, select_option, dilation_rate).T
    inverse_square_root = 1.0 / math.sqrt(sparse_queries.shape[-1])

    def portion_gradients(key_portion, value_portion, key_position):
        masked_logits, permitted_mask = masked_score_matrix(
            sparse_queries, key_portion, query_position, key_position, segment_length
        )
        softmax_weights = jnp.where(
            permitted_mask, jnp.exp(masked_logits - sparse_logsumexp[..., None]), 0.0
        )
        value_gradient = jnp.einsum(
            "tui,utx->itx", softmax_weights, sparse_gradient, precision=MATMUL_ACCURACY
        )
        pattern_gradient = jnp.einsum(
            "ozt,bzt->zob", sparse_gradient, value_portion, precision=MATMUL_ACCURACY
        )
        score_gradient = (
            softmax_weights
            * (pattern_gradient - sparse_output_grad[..., None])
            * inverse_square_root
        )
        query_gradient = jnp.einsum(
            "hqk,khd->qhd", score_gradient, key_portion, precision=MATMUL_ACCURACY
        )
        key_gradient = jnp.einsum(
            "tui,utx->itx", score_gradient, sparse_queries, precision=MATMUL_ACCURACY
        )
        return (query_gradient, jnp.stack((key_gradient, value_gradient)))

    query_gradient, key_value_gradient = portion_gradients(
        sparse_key_value[0], sparse_key_value[1], query_position
    )

    def one_run(distance, carry):
        remote_key_value, remote_gradient, query_sum = carry
        remote_key_value = passed_along(remote_key_value, "seq", 1)
        remote_gradient = passed_along(remote_gradient, "seq", 1)
        key_position = query_position - distance * sequence_width

        def far_grads():
            part_q, part_kv = portion_gradients(remote_key_value[0], remote_key_value[1], key_position)
            return query_sum + part_q, remote_gradient + part_kv

        def no_grads():
            return query_sum, remote_gradient

        is_live = run_is_live(distance, anchor_point, sequence_width, segment_length)
        query_sum, remote_gradient = lax.cond(is_live, far_grads, no_grads)
        return remote_key_value, remote_gradient, query_sum

    _, travelled, query_gradient = lax.fori_loop(
        1, reach + 1, one_run, (sparse_key_value, key_value_gradient, query_gradient)
    )
    return (query_gradient, passed_along(travelled, "seq", -reach))


def front_part(own_rows, w_qkv, gain_attn):
    return jnp.dot(layer_norm(own_rows, gain_attn), w_qkv, precision=MATMUL_ACCURACY)


def after_part(attn_rows, own_rows, w_out, w_up, w_down, gain_inner, gain_ffn, gain_hidden):
    residual = own_rows + jnp.dot(
        layer_norm(attn_rows, gain_inner), w_out, precision=MATMUL_ACCURACY
    )
    hidden = jax.nn.gelu(
        jnp.dot(layer_norm(residual, gain_ffn), w_up, precision=MATMUL_ACCURACY), approximate=False
    )
    return residual + jnp.dot(layer_norm(hidden, gain_hidden), w_down, precision=MATMUL_ACCURACY)


def shards(
    tokens,
    w_qkv,
    w_out,
    w_up,
    w_down,
    gain_attn,
    gain_inner,
    gain_ffn,
    gain_hidden,
    offsets,
    grad_out,
):
    w_qkv = w_qkv.astype(jnp.float32)
    w_out = w_out.astype(jnp.float32)
    w_up = w_up.astype(jnp.float32)
    w_down = w_down.astype(jnp.float32)
    groups = lax.axis_size("pat")
    local_rows = tokens.shape[0]
    sequence_width = local_rows * groups
    heads_here = HEADS // groups
    own_rows = tokens.reshape(local_rows, D)
    qkv_rows, front_back = jax.vjp(front_part, own_rows, w_qkv, gain_attn)
    gathered_qkv = lax.all_to_all(
        qkv_rows.reshape(local_rows, 1, 3, HEADS, HD),
        "pat",
        split_axis=3,
        concat_axis=1,
        tiled=True,
    )
    gathered_qkv = gathered_qkv.reshape(sequence_width, 3, heads_here, HD)
    head_offsets = lax.dynamic_slice_in_dim(
        offsets, lax.axis_index("pat") * heads_here, heads_here, 1
    )
    anchor_point = lax.axis_index("seq") * sequence_width
    dilation_rates = (DILATION_ONE, DILATION_TWO, DILATION_THREE, DILATION_FOUR, DILATION_FIVE)
    segment_lengths = (SEG1, SEG2, SEG3, SEG4, SEG5)
    reaches = [
        min((segment_lengths[pattern_spec] - 2) // sequence_width + 1, lax.axis_size("seq") - 1)
        for pattern_spec in range(PATTERNS)
    ]
    prepared_inputs = []
    for pattern_spec in range(PATTERNS):
        prepared_inputs.append(
            prepare_pattern(
                gathered_qkv[:, 0],
                gathered_qkv[:, 1],
                gathered_qkv[:, 2],
                head_offsets[pattern_spec],
                dilation_rates[pattern_spec],
                anchor_point,
            )
        )
    forwards = []
    for pattern_spec in range(PATTERNS):
        select_option, sparse_queries, sparse_key_value, query_position = prepared_inputs[
            pattern_spec
        ]
        forwards.append(
            pattern_forward_pass(
                sparse_queries,
                sparse_key_value,
                query_position,
                reaches[pattern_spec],
                segment_lengths[pattern_spec],
                anchor_point,
                sequence_width,
            )
        )
    lse_sums = jnp.stack([jnp.sum(entry[1]) for entry in forwards])
    totals = lax.psum(lse_sums, ("pat", "seq"))
    full_length = sequence_width * lax.axis_size("seq")
    counts = jnp.array(
        [
            float(full_length // dilation_rates[pattern_spec] * HEADS)
            for pattern_spec in range(PATTERNS)
        ],
        jnp.float32,
    )
    log_means = totals / counts
    attended, combined_logsumexp = merge_patterns(forwards, prepared_inputs)
    returned_rows = lax.all_to_all(
        attended.reshape(local_rows, groups, heads_here, HD),
        "pat",
        split_axis=1,
        concat_axis=2,
        tiled=True,
    )
    attn_rows = returned_rows.reshape(local_rows, D)
    result, after_back = jax.vjp(
        after_part, attn_rows, own_rows, w_out, w_up, w_down, gain_inner, gain_ffn, gain_hidden
    )
    g_attn, g_resid, g_out, g_up, g_down, g_inner, g_ffn, g_hidden = after_back(
        grad_out.reshape(local_rows, D)
    )
    sequence_gradient = lax.all_to_all(
        g_attn.reshape(local_rows, 1, HEADS, HD), "pat", split_axis=2, concat_axis=1, tiled=True
    )
    sequence_gradient = sequence_gradient.reshape(sequence_width, heads_here, HD)
    row_difference = jnp.sum(sequence_gradient * attended, -1)
    q_grads = []
    kv_grads = []
    for pattern_spec in range(PATTERNS):
        select_option, sparse_queries, sparse_key_value, query_position = prepared_inputs[
            pattern_spec
        ]
        part_q, part_kv = pattern_backward(
            select_option,
            dilation_rates[pattern_spec],
            segment_lengths[pattern_spec],
            anchor_point,
            sparse_queries,
            sparse_key_value,
            query_position,
            reaches[pattern_spec],
            sequence_gradient,
            row_difference,
            combined_logsumexp,
        )
        q_grads.append(part_q)
        kv_grads.append(part_kv)
    grad_total = jnp.zeros((sequence_width, 3, heads_here, HD), jnp.float32)
    for pattern_spec in range(PATTERNS):
        select_option = prepared_inputs[pattern_spec][0]
        grad_total = grad_total + jnp.stack(
            (
                spread_rows(q_grads[pattern_spec], select_option),
                spread_rows(kv_grads[pattern_spec][0], select_option),
                spread_rows(kv_grads[pattern_spec][1], select_option),
            ),
            1,
        )
    grad_back = lax.all_to_all(
        grad_total.reshape(local_rows, groups, 3, heads_here, HD),
        "pat",
        split_axis=1,
        concat_axis=3,
        tiled=True,
    )
    g_tokens, g_qkv, g_attn_gain = front_back(grad_back.reshape(local_rows, 3 * D))
    grad_tokens = (g_resid + g_tokens).reshape(local_rows, 1, D)
    summed = (
        lax.psum_scatter(g_qkv, ("pat", "seq"), scatter_dimension=0, tiled=True),
        lax.psum_scatter(g_out, ("pat", "seq"), scatter_dimension=0, tiled=True),
        lax.psum_scatter(g_up, ("pat", "seq"), scatter_dimension=0, tiled=True),
        lax.psum_scatter(g_down, ("pat", "seq"), scatter_dimension=0, tiled=True),
        lax.psum_scatter(g_attn_gain, ("pat", "seq"), scatter_dimension=0, tiled=True),
        lax.psum_scatter(g_inner, ("pat", "seq"), scatter_dimension=0, tiled=True),
        lax.psum_scatter(g_ffn, ("pat", "seq"), scatter_dimension=0, tiled=True),
        lax.psum_scatter(g_hidden, ("pat", "seq"), scatter_dimension=0, tiled=True),
    )
    return (
        result.reshape(local_rows, 1, D),
        grad_tokens,
        summed[0],
        summed[1],
        summed[2],
        summed[3],
        summed[4],
        summed[5],
        summed[6],
        summed[7],
        log_means,
    )


def fast_shards(tokens, w_qkv, w_out, w_up, w_down, gain_attn, gain_inner, gain_ffn, gain_hidden, offsets, grad_out):
    p, s = lax.axis_index("pat"), lax.axis_index("seq")
    active, head = head_here(p, s)
    mine = lax.dynamic_slice_in_dim(offsets, head, 1, 1)[:, 0]
    info = jnp.concatenate([jnp.stack([active.astype(jnp.int32), lax.rem(p, 2).astype(jnp.int32)]), mine])

    counts = [float(TOTAL * 4 // r * HEADS) for r in DILATIONS]
    pk, x = front(tokens, w_qkv, gain_attn)
    own, sib = to_heads(pk, True, 0)
    ap, lse, sums = attention_forward(info, own, sib)
    rec = to_homes(ap, 1)
    mixed, dap, dy1, S, G = feed_forward(
        rec, x, grad_out, w_out, w_up, w_down, gain_inner, gain_ffn, gain_hidden, sums
    )
    grec, g_out, g_up, g_down = backward_all(mine, dap, own, sib, ap, lse, G, 2)
    gx, g_qkv, *small = finish(grec, x, dy1, w_qkv, gain_attn, S, counts, 3)
    gx, g_qkv, g_out, g_up, g_down, *small = deliver(gx, g_qkv, g_out, g_up, g_down, *small)
    return (mixed, gx, g_qkv, g_out, g_up, g_down, *(v.reshape(-1) for v in small))


def fits(mesh):
    return mesh.shape["pat"] == 4 and mesh.shape["seq"] == RUNS


def solution(mesh):
    rows = P("seq", "pat", None)
    split_rows = P(("pat", "seq"), None)
    split_one = P(("pat", "seq"))
    planned = jax.shard_map(
        fast_shards,
        mesh=mesh,
        in_specs=(rows,) + (P(),) * 9 + (rows,),
        out_specs=(rows, rows) + (split_rows,) * 4 + (split_one,) * 4 + (P(),),
        check_vma=False,
    )
    general = jax.shard_map(
        shards,
        mesh=mesh,
        in_specs=(rows,) + (P(),) * 9 + (rows,),
        out_specs=(rows, rows) + (split_rows,) * 4 + (split_one,) * 4 + (P(),),
        check_vma=False,
    )

    def layer(tokens, *rest):
        if fits(mesh) and tokens.shape[0] == TOTAL:
            return planned(tokens, *rest)
        return general(tokens, *rest)

    return layer
```

```python
import functools
import math

import jax
import jax.numpy as jnp
from jax import lax
from jax.experimental import pallas as pl
from jax.experimental.pallas import tpu as pltpu
from jax.sharding import PartitionSpec as P

D = 768
HEADS = 12
HD = 64
FF = 3072
PATTERNS = 5
SEGMENTS = (2048, 4096, 8192, 16384, 32768)
DILATIONS = (1, 2, 4, 6, 12)
LN_EPSILON = 1e-05
NEG = -1e30
F32 = jnp.float32
BF16 = jnp.bfloat16
HIGHEST = lax.Precision.HIGHEST
VMEM_LIMIT = 60 * 1024 * 1024

ROWS = 192
HALF = ROWS // 2
RUNS = 8
TOTAL = ROWS * RUNS
PACK = ROWS + HALF
HOMES = 16
THIRD = TOTAL // 3
MESH = pl.DeviceIdType.MESH


def dot_nn(a, b):
    return lax.dot_general(a, b, (((1,), (0,)), ((), ())), preferred_element_type=F32)


def dot_nt(a, b):
    return lax.dot_general(a, b, (((1,), (1,)), ((), ())), preferred_element_type=F32)


def split(v):
    hi = v.astype(BF16)
    return hi, (v - hi.astype(F32)).astype(BF16)


def split32(v):
    hi = v.astype(BF16).astype(F32)
    return hi, v - hi


def lower_lanes(v):
    return lax.broadcasted_iota(jnp.int32, v.shape, v.ndim - 1) < HD


def swap(v):
    return pltpu.roll(v, HD, v.ndim - 1)


def pick(a, b):
    return jnp.where(lower_lanes(a), a, b)


def head_place(h):
    z = h // 3
    column = lax.rem(lax.rem(h, 3) + z + 1, 4)
    return column // 2, z * 2 + lax.rem(column, 2)


def head_here(p, s):
    z = s // 2
    column = (p // 2) * 2 + lax.rem(s, 2)
    k = lax.rem(column - z + 7, 4)
    return k < 3, z * 3 + jnp.minimum(k, 2)


def whole(*_):
    return pl.BlockSpec(memory_space=pltpu.VMEM)


VM = pl.BlockSpec(memory_space=pltpu.VMEM)
ANY = pl.BlockSpec(memory_space=pl.ANY)
SM = pl.BlockSpec(memory_space=pltpu.SMEM)


def params(**kw):
    return pltpu.CompilerParams(vmem_limit_bytes=VMEM_LIMIT, **kw)


def normed(v):
    centred = v - jnp.mean(v, -1, keepdims=True)
    rs = lax.rsqrt(jnp.mean(centred * centred, -1, keepdims=True) + LN_EPSILON)
    return centred * rs, rs


def put_split(ref, v):
    hi, lo = split(v)
    n = v.shape[0]
    ref[0:n, :] = hi
    ref[n : 2 * n, :] = lo


def front_kernel(x3, w_ref, gain_ref, pk_ref, x_ref, lhs):
    x = x3[...].reshape(ROWS, D)
    x_ref[...] = x
    n, _ = normed(x)
    put_split(lhs, n * gain_ref[...][None, :])
    for jj in range(3):
        parts = []
        for kind in range(3):
            c0 = kind * D + 256 * jj
            r = dot_nn(lhs[...], w_ref[:, c0 : c0 + 256])
            parts.append(r[:ROWS] + r[ROWS:])
        for half in range(2):
            q, k, v = (a[:, 128 * half : 128 * half + 128] for a in parts)
            h = 4 * jj + 2 * half
            pk_ref[h, 0:ROWS, :] = pick(k, swap(v))
            pk_ref[h + 1, 0:ROWS, :] = pick(swap(k), v)
            top, bottom = q[:HALF], q[HALF:]
            pk_ref[h, ROWS:PACK, :] = pick(top, swap(bottom))
            pk_ref[h + 1, ROWS:PACK, :] = pick(swap(top), bottom)


def front(x, w, gain):
    return pl.pallas_call(
        front_kernel,
        out_shape=[jax.ShapeDtypeStruct((HEADS, PACK, 128), F32)] + [jax.ShapeDtypeStruct((ROWS, D), F32)],
        in_specs=[VM] * 3,
        out_specs=[VM] * 2,
        scratch_shapes=[pltpu.VMEM((2 * ROWS, D), BF16)],
        compiler_params=params(),
    )(x, w, gain)


def place_facts():
    p, s = lax.axis_index("pat"), lax.axis_index("seq")
    x, core = p // 2, lax.rem(p, 2)
    active, head = head_here(p, s)
    return p, s, x, core, active, head


def home_device(core, m):
    return core * 2 + lax.rem(m, 2), m // 2


def head_device(h, b):
    hx, hs = head_place(h)
    return hx * 2 + b, hs


def same(p, s, q, t):
    return jnp.logical_and(p == q, s == t)


def to(p, s):
    return {"pat": p, "seq": s}


def scatter_kernel(forward, pk, own, *rest):
    if forward:
        sib, send, recv, fsend, frecv = rest
    else:
        send, recv = rest
    p, s, x, core, active, head = place_facts()
    slot = s * 2 + core
    barrier = pltpu.get_barrier_semaphore()

    @pl.when(active)
    def _():
        def greet(m, carry):
            q, t = home_device(core, m)

            @pl.when(jnp.logical_not(same(p, s, q, t)))
            def _():
                pl.semaphore_signal(barrier, inc=1, device_id=to(q, t), device_id_type=MESH)

            return carry

        lax.fori_loop(0, HOMES, greet, 0)
        if forward:
            pl.semaphore_signal(barrier, inc=1, device_id=to(x * 2 + 1 - core, s), device_id_type=MESH)

    mine = jnp.logical_and(active, core == x)
    waits = HEADS - mine.astype(jnp.int32)
    if forward:
        waits = waits + active.astype(jnp.int32)
    pl.semaphore_wait(barrier, waits)

    def copy(h):
        q, t = head_device(h, x)
        return q, t, pltpu.make_async_remote_copy(
            src_ref=pk.at[h],
            dst_ref=own.at[slot],
            send_sem=send.at[h],
            recv_sem=recv.at[slot],
            device_id=to(q, t),
            device_id_type=MESH,
        )

    def start(j, carry):
        h = lax.rem(j + 3 * (s // 2) + 2 * p, HEADS)
        q, t, remote = copy(h)

        @pl.when(same(p, s, q, t))
        def _():
            pltpu.make_async_copy(pk.at[h], own.at[slot], recv.at[slot]).start()

        @pl.when(jnp.logical_not(same(p, s, q, t)))
        def _():
            remote.start()

        return carry

    lax.fori_loop(0, HEADS, start, 0)

    def passed(m):
        return pltpu.make_async_remote_copy(
            src_ref=own.at[m, pl.ds(0, ROWS), :],
            dst_ref=sib.at[m],
            send_sem=fsend.at[m],
            recv_sem=frecv.at[m],
            device_id=to(x * 2 + 1 - core, s),
            device_id_type=MESH,
        )

    @pl.when(active)
    def _():
        def arrive(m, carry):
            pltpu.make_async_copy(own.at[m], own.at[m], recv.at[m]).wait()
            if forward:
                passed(m).start()
            return carry

        lax.fori_loop(0, HOMES, arrive, 0)
        if forward:

            def finish(m, carry):
                passed(m).wait()
                return carry

            lax.fori_loop(0, HOMES, finish, 0)

    def sent(h, carry):
        q, t, remote = copy(h)

        @pl.when(jnp.logical_not(same(p, s, q, t)))
        def _():
            remote.wait_send()

        return carry

    lax.fori_loop(0, HEADS, sent, 0)


def to_heads(packets, forward, cid):
    rows = packets.shape[1]
    shapes = [jax.ShapeDtypeStruct((HOMES, rows, 128), F32)]
    sems = [pltpu.SemaphoreType.DMA((HEADS,)), pltpu.SemaphoreType.DMA((HOMES,))]
    if forward:
        shapes.append(jax.ShapeDtypeStruct((HOMES, ROWS, 128), F32))
        sems += [pltpu.SemaphoreType.DMA((HOMES,)), pltpu.SemaphoreType.DMA((HOMES,))]
    return pl.pallas_call(
        functools.partial(scatter_kernel, forward),
        out_shape=shapes,
        in_specs=[ANY],
        out_specs=[ANY] * len(shapes),
        scratch_shapes=sems,
        compiler_params=params(collective_id=cid, has_side_effects=True),
    )(packets)


def home_barrier(p, s, x, core, active, barrier, also_sibling):
    def greet(h, carry):
        q, t = head_device(h, x)

        @pl.when(jnp.logical_not(same(p, s, q, t)))
        def _():
            pl.semaphore_signal(barrier, inc=1, device_id=to(q, t), device_id_type=MESH)

        return carry

    lax.fori_loop(0, HEADS, greet, 0)

    @pl.when(active)
    def _():
        if also_sibling:
            pl.semaphore_signal(barrier, inc=1, device_id=to(x * 2 + 1 - core, s), device_id_type=MESH)
        mine = (core == x).astype(jnp.int32)
        pl.semaphore_wait(barrier, HOMES - mine + (1 if also_sibling else 0))


def gather_kernel(pk, rec, send, recv):
    p, s, x, core, active, head = place_facts()
    barrier = pltpu.get_barrier_semaphore()
    home_barrier(p, s, x, core, active, barrier, False)

    def copy(m):
        q, t = home_device(core, m)
        return q, t, pltpu.make_async_remote_copy(
            src_ref=pk.at[m],
            dst_ref=rec.at[head],
            send_sem=send.at[m],
            recv_sem=recv.at[head],
            device_id=to(q, t),
            device_id_type=MESH,
        )

    @pl.when(active)
    def _():
        def start(j, carry):
            m = lax.rem(j + 2 * s + 1, HOMES)
            q, t, remote = copy(m)

            @pl.when(same(p, s, q, t))
            def _():
                pltpu.make_async_copy(pk.at[m], rec.at[head], recv.at[head]).start()

            @pl.when(jnp.logical_not(same(p, s, q, t)))
            def _():
                remote.start()

            return carry

        lax.fori_loop(0, HOMES, start, 0)

    def arrive(h, carry):
        pltpu.make_async_copy(rec.at[h], rec.at[h], recv.at[h]).wait()
        return carry

    lax.fori_loop(0, HEADS, arrive, 0)

    @pl.when(active)
    def _():
        def sent(m, carry):
            q, t, remote = copy(m)

            @pl.when(jnp.logical_not(same(p, s, q, t)))
            def _():
                remote.wait_send()

            return carry

        lax.fori_loop(0, HOMES, sent, 0)


def to_homes(packets, cid):
    rows = packets.shape[1]
    return pl.pallas_call(
        gather_kernel,
        out_shape=jax.ShapeDtypeStruct((HEADS, rows, 128), F32),
        in_specs=[ANY],
        out_specs=ANY,
        scratch_shapes=[pltpu.SemaphoreType.DMA((HOMES,)), pltpu.SemaphoreType.DMA((HEADS,))],
        compiler_params=params(collective_id=cid, has_side_effects=True),
    )(packets)


def tile_positions(rows, columns, row_classes, column_classes, t_step, class_step):
    r = lax.broadcasted_iota(jnp.int32, (rows, columns), 0)
    q = lax.broadcasted_iota(jnp.int32, (rows, columns), 1)
    rn, qn = rows // row_classes, columns // column_classes
    return (r % rn) * t_step + (r // rn) * class_step, (q % qn) * t_step + (q // qn) * class_step


def key_bias(q_shape, k_shape, t_step, class_step, shift, keys_first):
    nq, nk = q_shape[0] * q_shape[1], k_shape[0] * k_shape[1]
    if keys_first:
        kp, qp = tile_positions(nk, nq, k_shape[0], q_shape[0], t_step, class_step)
    else:
        qp, kp = tile_positions(nq, nk, q_shape[0], k_shape[0], t_step, class_step)
    return jnp.where(kp - qp <= shift, 0.0, NEG).astype(F32)


def unpack_keys(own, sib, b, kvf):
    def one(m, carry):
        c = 2 * b + lax.rem(m, 2)
        d = 2 * (1 - b) + lax.rem(m, 2)
        t = pl.multiple_of((m // 2) * ROWS, 64)
        kvf[c, pl.ds(t, ROWS), :] = own[m, 0:ROWS, :]
        kvf[d, pl.ds(t, ROWS), :] = sib[m]
        return carry

    lax.fori_loop(0, HOMES, one, 0)


def unpack_pairs(src, first, dst, scale):
    def one(m, carry):
        t = pl.multiple_of((m // 2) * ROWS, 32)
        v = src[m, first : first + HALF, :] * scale
        w = swap(v)
        dst[lax.rem(m, 2), pl.ds(t, HALF), :] = pick(v, w)
        dst[lax.rem(m, 2), pl.ds(t + HALF, HALF), :] = pick(w, v)
        return carry

    lax.fori_loop(0, HOMES, one, 0)


def keys_and_values(kv):
    hi, lo = split32(kv)
    k2 = pick(hi, swap(lo))
    v2 = pick(swap(hi), lo)
    return k2, v2


def doubled(v):
    return jnp.concatenate([v, v], 1)


def query_quads(qq):
    hi, lo = split32(qq)
    return jnp.concatenate([pick(hi, lo).astype(BF16), pick(lo, hi).astype(BF16)], 1)


def class_facts4(o4, b):
    keys = ((lax.rem(o4, 4), o4 // 4), (lax.rem(o4 + 6, 4), (o4 + 6) // 4))
    first = (keys[0][0] // 2) == b
    query = (jnp.where(first, keys[0][0], keys[1][0]), jnp.where(first, keys[0][1], keys[1][1]))
    return keys, jnp.where(first, 0, 1), query


def forward_kernel(info, own, sib, ap, lse, sums, kvf, kc, vt, qf, qc, k4, vt4, q4, k5, vt5, q5, acc, ml, sc, pc, R, b1, b2, b3, b4):
    active = info[0] == 1
    b = info[1]
    offs = [info[2 + i] for i in range(PATTERNS)]
    sums[...] = jnp.zeros_like(sums)

    @pl.when(active)
    def _():
        unpack_keys(own, sib, b, kvf)
        unpack_pairs(own, ROWS, qf, 1.0 / math.sqrt(HD))

        def prepare(i, carry):
            c, t = i // 12, pl.multiple_of(lax.rem(i, 12) * 128, 128)
            k2, v2 = keys_and_values(kvf[c, pl.ds(t, 128), :])
            kc[c, pl.ds(t, 128), :] = k2.astype(BF16)
            vt[c, :, pl.ds(t, 128)] = v2.T.astype(BF16)
            return carry

        lax.fori_loop(0, 48, prepare, 0, unroll=2)

        def prepare_q(i, carry):
            c, t = i // 12, pl.multiple_of(lax.rem(i, 12) * 128, 128)
            qc[c, pl.ds(t, 128), :] = query_quads(qf[c, pl.ds(t, 128), :])
            return carry

        lax.fori_loop(0, 24, prepare_q, 0, unroll=2)

        keys4, e4, (qc4, qv4) = class_facts4(offs[3], b)
        kc5, kv5 = lax.rem(offs[4], 4), offs[4] // 4
        for blk in range(4):
            r = slice(128 * blk, 128 * blk + 128)
            for e in range(2):
                c, v = keys4[e]
                k2, v2 = keys_and_values(kvf[c, pl.ds(v + 384 * blk, 128, stride=3), :])
                k4[e, r, :] = k2.astype(BF16)
                vt4[e, :, r] = v2.T.astype(BF16)
            q4[r, :] = query_quads(qf[qc4 - 2 * b, pl.ds(qv4 + 384 * blk, 128, stride=3), :])
            k2, v2 = keys_and_values(kvf[kc5, pl.ds(kv5 + 384 * blk, 128, stride=3), :])
            k5[r, :] = k2.astype(BF16)
            vt5[:, r] = v2.T.astype(BF16)
            q5[r, :] = query_quads(qf[lax.rem(kc5, 2), pl.ds(kv5 + 384 * blk, 128, stride=3), :])

        b1[...] = key_bias((2, 128), (4, 128), 4, 1, 2 * b, True)
        b2[...] = key_bias((1, 256), (2, 256), 4, 2, 2 * b, True)
        b3[...] = key_bias((1, 256), (1, 256), 1, 1, 0, True)
        b4[...] = key_bias((1, 256), (2, 256), 12, 6, 6 * e4, True)

        def tile(g, q, k, vT, bias, first):
            n = k.shape[0] // 128
            kk = doubled(k)
            m = None
            for i in range(n):
                piece = slice(128 * i, 128 * i + 128)
                s = dot_nt(kk[piece], q)
                if bias is not None:
                    s = s + bias[piece, :]
                sc[g, piece, :] = s
                top = jnp.max(s.reshape(16, 8, 256), 0)
                m = top if m is None else jnp.maximum(m, top)
            m = jnp.max(m, 0, keepdims=True)
            if not first:
                old = ml[g, 0:1, :]
                m = jnp.maximum(old, m)
            total = None
            for i in range(n):
                piece = slice(128 * i, 128 * i + 128)
                p = jnp.exp(sc[g, piece, :] - m)
                part = jnp.sum(p.reshape(16, 8, 256), 0)
                total = part if total is None else total + part
                hi, lo = split(p)
                pc[g, piece, :] = hi
                pc[g, 128 * (n + i) : 128 * (n + i) + 128, :] = lo
            total = jnp.sum(total, 0, keepdims=True)
            new = dot_nn(doubled(vT), pc[g, : 256 * n, :])
            if first:
                acc[g] = new
            else:
                alpha = jnp.exp(old - m)
                acc[g] = acc[g] * alpha + new
                total = ml[g, 1:2, :] * alpha + total
            ml[g, 0:1, :] = m
            ml[g, 1:2, :] = total

        def closed(pattern, g):
            m, l = ml[g, 0:1, :], ml[g, 1:2, :]
            rows = m + jnp.log(l)
            sums[pattern : pattern + 1, :] += rows[:, :128] + rows[:, 128:]
            o = acc[g]
            return jnp.concatenate(
                [o[:HD] + o[HD:], jnp.broadcast_to(l, (32, 256)), jnp.broadcast_to(m, (32, 256))], 0
            ).T

        def q1(qb, carry):
            def at(g, blk):
                return pl.ds(pl.multiple_of(512 * g + 128 * blk, 128), 128)

            def step(kb, bias, first):
                for g in range(3):
                    ks = at(g, kb)
                    vT = jnp.concatenate([vt[c, :, ks] for c in range(4)], 1)
                    tile(g, qc[:, at(g, qb), :].reshape(256, 256), kc[:, ks, :].reshape(512, 128), vT, bias, first)

            step(qb, b1, True)

            def more(kb, inner):
                step(kb, None, False)
                return inner

            lax.fori_loop(0, qb, more, 0)
            for g in range(3):
                R[:, at(g, qb), :] = closed(0, g).reshape(2, 128, 128)
            return carry

        lax.fori_loop(0, 4, q1, 0)

        def merge(pattern, g, ci, rows):
            r0, r1 = R[ci, rows, :], closed(pattern, g)
            m0 = jnp.broadcast_to(r0[:, 96:97], r0.shape)
            m1 = jnp.broadcast_to(r1[:, 96:97], r1.shape)
            m = jnp.maximum(m0, m1)
            both = r0 * jnp.exp(m0 - m) + r1 * jnp.exp(m1 - m)
            lane = lax.broadcasted_iota(jnp.int32, r0.shape, 1)
            R[ci, rows, :] = jnp.where(lane < 96, both, m)

        def at256(blk):
            return pl.ds(pl.multiple_of(256 * blk, 128), 256)

        par = offs[1]

        def step2(g, q, kb, bias, first):
            ks = at256(kb)
            k = jnp.concatenate([kc[par, ks, :], kc[par + 2, ks, :]], 0)
            vT = jnp.concatenate([vt[par, :, ks], vt[par + 2, :, ks]], 1)
            tile(g, q, k, vT, bias, first)

        def q2(qb, carry):
            q = qc[par, at256(qb), :]
            step2(0, q, qb, b2, True)

            def more(kb, inner):
                step2(0, q, kb, None, False)
                return inner

            lax.fori_loop(jnp.where(qb >= 4, 4, 0), qb, more, 0)
            merge(1, 0, par, at256(qb))
            return carry

        lax.fori_loop(0, TOTAL // 256, q2, 0)

        o3 = offs[2]

        @pl.when(o3 // 2 == b)
        def _():
            ci = lax.rem(o3, 2)

            def step3(g, qb, kb, bias, first):
                tile(g, qc[ci, at256(qb), :], kc[o3, at256(kb), :], vt[o3, :, at256(kb)], bias, first)

            def q3(pair, carry):
                q0, q1_ = 2 * pair, 2 * pair + 1
                step3(0, q0, q0, b3, True)
                step3(1, q1_, q1_, b3, True)

                def more(kb, inner):
                    step3(0, q0, kb, None, False)
                    step3(1, q1_, kb, None, False)
                    return inner

                lax.fori_loop(0, q0, more, 0)
                step3(1, q1_, q0, None, False)
                merge(2, 0, ci, at256(q0))
                merge(2, 1, ci, at256(q1_))
                return carry

            lax.fori_loop(0, TOTAL // 512, q3, 0)

        for kb in range(2):
            for qb in range(kb, 2):
                order = qb - kb
                ks = slice(256 * order, 256 * order + 256)
                tile(
                    qb,
                    q4[256 * qb : 256 * qb + 256, :],
                    k4[:, ks, :].reshape(512, 128),
                    jnp.concatenate([vt4[0, :, ks], vt4[1, :, ks]], 1),
                    b4 if order == qb else None,
                    kb == 0,
                )
        for qb in range(2):
            merge(3, qb, qc4 - 2 * b, pl.ds(qv4 + 768 * qb, 256, stride=3))

        @pl.when(kc5 // 2 == b)
        def _():
            for kb in range(2):
                for qb in range(kb, 2):
                    order = qb - kb
                    ks = slice(256 * order, 256 * order + 256)
                    tile(
                        qb,
                        q5[256 * qb : 256 * qb + 256, :],
                        k5[ks, :],
                        vt5[:, ks],
                        b3 if order == qb else None,
                        kb == 0,
                    )
            for qb in range(2):
                merge(4, qb, lax.rem(kc5, 2), pl.ds(kv5 + 768 * qb, 256, stride=3))

        def finish(m, carry):
            ci = lax.rem(m, 2)
            rows = pl.ds(pl.multiple_of((m // 2) * ROWS, 64), ROWS)
            r = R[ci, rows, :]
            l = jnp.broadcast_to(r[:, HD : HD + 1], r.shape)
            out = r / l
            ap[m] = pick(out[:HALF], swap(out[HALF:]))
            lse[ci, rows, :] = jnp.broadcast_to(r[:, 96:97], r.shape) + jnp.log(l)
            return carry

        lax.fori_loop(0, HOMES, finish, 0, unroll=2)
        sums[...] = jnp.broadcast_to(jnp.sum(sums[...], -1, keepdims=True), (8, 128))


def attention_forward(info, own, sib):
    keys = pltpu.VMEM((4, TOTAL, 128), BF16)
    turned = pltpu.VMEM((4, 128, TOTAL), BF16)
    state = pltpu.VMEM((2, TOTAL, 128), F32)
    return pl.pallas_call(
        forward_kernel,
        out_shape=[
            jax.ShapeDtypeStruct((HOMES, HALF, 128), F32),
            jax.ShapeDtypeStruct((2, TOTAL, 128), F32),
            jax.ShapeDtypeStruct((8, 128), F32),
        ],
        in_specs=[SM, VM, VM],
        out_specs=[VM, VM, VM],
        scratch_shapes=[
            pltpu.VMEM((4, TOTAL, 128), F32),
            keys,
            turned,
            state,
            pltpu.VMEM((2, TOTAL, 256), BF16),
            pltpu.VMEM((2, THIRD, 128), BF16),
            pltpu.VMEM((2, 128, THIRD), BF16),
            pltpu.VMEM((THIRD, 256), BF16),
            pltpu.VMEM((THIRD, 128), BF16),
            pltpu.VMEM((128, THIRD), BF16),
            pltpu.VMEM((THIRD, 256), BF16),
            pltpu.VMEM((3, 128, 256), F32),
            pltpu.VMEM((3, 8, 256), F32),
            pltpu.VMEM((3, 512, 256), F32),
            pltpu.VMEM((3, 1024, 256), BF16),
            state,
            pltpu.VMEM((512, 256), F32),
            pltpu.VMEM((512, 256), F32),
            pltpu.VMEM((256, 256), F32),
            pltpu.VMEM((512, 256), F32),
        ],
        compiler_params=params(),
    )(info, own, sib)


def rows_from_pairs(rec, dst):
    for j in range(HEADS // 2):
        u, v = rec[2 * j], rec[2 * j + 1]
        cols = slice(128 * j, 128 * j + 128)
        dst[0:HALF, cols] = pick(u, swap(v))
        dst[HALF:ROWS, cols] = pick(swap(u), v)


def pairs_from_rows(src, dst):
    for j in range(HEADS // 2):
        top = src[0:HALF, 128 * j : 128 * j + 128]
        bottom = src[HALF:ROWS, 128 * j : 128 * j + 128]
        dst[2 * j] = pick(top, swap(bottom))
        dst[2 * j + 1] = pick(swap(top), bottom)


def halves_sum(r):
    return r[:ROWS] + r[ROWS:]


def norm_back(f, n, rs):
    return (f - jnp.mean(f, -1, keepdims=True) - n * jnp.mean(f * n, -1, keepdims=True)) * rs


def put_turned(hi_ref, lo_ref, v):
    for j in range(D // 128):
        t = v[:, 128 * j : 128 * j + 128].T
        hi, lo = split(t)
        hi_ref[128 * j : 128 * j + 128, :] = hi
        lo_ref[128 * j : 128 * j + 128, :] = lo


class ToHeads:
    def __init__(self, pk, rec, send, recv):
        self.pk, self.rec, self.send, self.recv = pk, rec, send, recv
        self.facts = place_facts()

    def greet(self):
        p, s, x, core, active, head = self.facts
        barrier = pltpu.get_barrier_semaphore()

        @pl.when(active)
        def _():
            def one(m, carry):
                q, t = home_device(core, m)

                @pl.when(jnp.logical_not(same(p, s, q, t)))
                def _():
                    pl.semaphore_signal(barrier, inc=1, device_id=to(q, t), device_id_type=MESH)

                return carry

            lax.fori_loop(0, HOMES, one, 0)

    def copy(self, h):
        p, s, x, core, active, head = self.facts
        slot = s * 2 + core
        q, t = head_device(h, x)
        far = pltpu.make_async_remote_copy(
            src_ref=self.pk.at[h],
            dst_ref=self.rec.at[slot],
            send_sem=self.send.at[h],
            recv_sem=self.recv.at[slot],
            device_id=to(q, t),
            device_id_type=MESH,
        )
        return same(p, s, q, t), lambda: pltpu.make_async_copy(self.pk.at[h], self.rec.at[slot], self.recv.at[slot]), far

    def start(self):
        p, s, x, core, active, head = self.facts
        mine = jnp.logical_and(active, core == x).astype(jnp.int32)
        pl.semaphore_wait(pltpu.get_barrier_semaphore(), HEADS - mine)

        def one(j, carry):
            here, near, far = self.copy(lax.rem(j + 3 * (s // 2) + 2 * p, HEADS))

            @pl.when(here)
            def _():
                near().start()

            @pl.when(jnp.logical_not(here))
            def _():
                far.start()

            return carry

        lax.fori_loop(0, HEADS, one, 0)

    def finish(self):
        active = self.facts[4]

        @pl.when(active)
        def _():
            def arrive(m, carry):
                pltpu.make_async_copy(self.rec.at[m], self.rec.at[m], self.recv.at[m]).wait()
                return carry

            lax.fori_loop(0, HOMES, arrive, 0)

        def sent(h, carry):
            here, near, far = self.copy(h)

            @pl.when(jnp.logical_not(here))
            def _():
                far.wait_send()

            return carry

        lax.fori_loop(0, HEADS, sent, 0)


FT = 512


class Spill:
    def __init__(self, tiles, sem):
        self.tiles, self.sem, self.count, self.open = tiles, sem, 0, [[], []]

    def emit(self, fill, copies):
        k = self.count % 2
        for c in self.open[k]:
            c.wait()
        fill(self.tiles.at[k])
        self.open[k] = copies(self.tiles.at[k], self.sem.at[k])
        for c in self.open[k]:
            c.start()
        self.count += 1

    def close(self):
        for k in range(2):
            for c in self.open[k]:
                c.wait()
            self.open[k] = []


def product(hi, lo, r_hi, r_lo, tile):
    def one(i, carry):
        rows = pl.ds(pl.multiple_of(i * 128, 128), 128)
        h, l = hi[rows, :], lo[rows, :]
        tile[rows, :] = dot_nn(h, r_hi[...]) + dot_nn(h, r_lo[...]) + dot_nn(l, r_hi[...])
        return carry

    lax.fori_loop(0, D // 128, one, 0)


def column_copies(G, chunk):
    def make(tile, sem):
        return [
            pltpu.make_async_copy(
                tile.at[pl.ds(24 * d, 24), :], G.at[d // 16, (d // 8) % 2, (d % 8) // 2, d % 2, chunk], sem.at[d]
            )
            for d in range(32)
        ]

    return make


def row_copies(G, part, chunk):
    def make(tile, sem):
        return [
            pltpu.make_async_copy(
                tile.at[pl.ds(24 * d, 24), :], G.at[part // 2, part % 2, d // 8, (d // 4) % 2, chunk + d % 4], sem.at[d]
            )
            for d in range(32)
        ]

    return make


def ff_kernel(rec, x_ref, g3, wo, wu, wd, gi1, gf1, gh1, sums, out3, drec, dy1_ref, S, G, dap, lhs, lhs2, gi, gf, gh, gh_g, g_ref, out_ref, V, N1, U, GP, E, ACC, th, tl, r_hi, r_lo, tiles, sem, dsend, drecv):
    spill = Spill(tiles, sem)
    travel = ToHeads(dap, drec, dsend, drecv)
    travel.greet()
    for wide, flat in ((gi, gi1), (gf, gf1), (gh, gh1)):
        wide[...] = flat[...][None, :]
    g_ref[...] = g3[...].reshape(ROWS, D)
    rows_from_pairs(rec, V)
    na, rs_a = normed(V[...])
    V[...] = na
    put_split(lhs, na * gi[...])
    for j in range(3):
        cols = slice(256 * j, 256 * j + 256)
        N1[:, cols] = x_ref[:, cols] + halves_sum(dot_nn(lhs[...], wo[:, cols]))
    y1 = N1[...]
    out_ref[...] = y1
    ny, rs_y = normed(y1)
    N1[...] = ny
    put_split(lhs, ny * gf[...])

    def up(j, su):
        cols = pl.ds(pl.multiple_of(j * FT, FT), FT)
        z = halves_sum(dot_nn(lhs[...], wu[:, cols]))
        phi = 0.5 * (1.0 + lax.erf(z * math.sqrt(0.5)))
        u = z * phi
        U[:, cols] = u
        GP[:, cols] = phi + z * jnp.exp(-0.5 * z * z) * (1.0 / math.sqrt(2.0 * math.pi))
        return su + jnp.sum(u, -1, keepdims=True)

    zero = jnp.zeros((ROWS, 1), F32)
    mean = lax.fori_loop(0, FF // FT, up, zero) * (1.0 / FF)

    def spread(j, sv):
        cols = pl.ds(pl.multiple_of(j * FT, FT), FT)
        c = U[:, cols] - mean
        return sv + jnp.sum(c * c, -1, keepdims=True)

    rs_u = lax.rsqrt(lax.fori_loop(0, FF // FT, spread, zero) * (1.0 / FF) + LN_EPSILON)
    ACC[...] = jnp.zeros_like(ACC)

    def lower(j, carry):
        cols = pl.ds(pl.multiple_of(j * FT, FT), FT)
        n = (U[:, cols] - mean) * rs_u
        U[:, cols] = n
        put_split(lhs2, n * gh[:, cols])
        ACC[...] += halves_sum(dot_nn(lhs2[...], wd[cols, :]))
        return carry

    lax.fori_loop(0, FF // FT, lower, 0)
    out3[...] = (out_ref[...] + ACC[...]).reshape(ROWS, 1, D)

    put_split(lhs, g_ref[...])

    def back_down(j, sums):
        cols = pl.ds(pl.multiple_of(j * FT, FT), FT)
        e = halves_sum(dot_nt(lhs[...], wd[cols, :]))
        n = U[:, cols]
        gh_g[:, cols] = jnp.sum(e * n, 0, keepdims=True)
        f = e * gh[:, cols]
        E[:, cols] = f
        return sums[0] + jnp.sum(f, -1, keepdims=True), sums[1] + jnp.sum(f * n, -1, keepdims=True)

    sf, sfn = lax.fori_loop(0, FF // FT, back_down, (zero, zero))
    mf, mfn = sf * (1.0 / FF), sfn * (1.0 / FF)
    ACC[...] = jnp.zeros_like(ACC)

    def back_up(j, carry):
        cols = pl.ds(pl.multiple_of(j * FT, FT), FT)
        dz = (E[:, cols] - mf - U[:, cols] * mfn) * rs_u * GP[:, cols]
        E[:, cols] = dz
        put_split(lhs2, dz)
        ACC[...] += halves_sum(dot_nt(lhs2[...], wu[:, cols]))
        return carry

    lax.fori_loop(0, FF // FT, back_up, 0)
    e = ACC[...]
    ny = N1[...]
    S[2:3, :] = jnp.sum(e * ny, 0, keepdims=True)
    dy1 = g_ref[...] + norm_back(e * gf[...], ny, rs_y)
    dy1_ref[...] = dy1
    put_split(lhs, dy1)
    for j in range(3):
        cols = slice(256 * j, 256 * j + 256)
        ACC[:, cols] = halves_sum(dot_nt(lhs[...], wo[cols, :]))
    e = ACC[...]
    na = V[...]
    S[1:2, :] = jnp.sum(e * na, 0, keepdims=True)
    S[0:1, :] = jnp.zeros((1, D), F32)
    for j in range(4):
        S[3 + j : 4 + j, :] = gh_g[:, D * j : D * j + D]
    lane = lax.broadcasted_iota(jnp.int32, (1, 128), 1)
    S[7:8, :] = jnp.zeros((1, D), F32)
    S[7:8, 0:128] = sum(jnp.where(lane == i, sums[i : i + 1, :], 0.0) for i in range(PATTERNS))
    ACC[...] = norm_back(e * gi[...], na, rs_a)
    pairs_from_rows(ACC, dap)
    travel.start()

    put_turned(th, tl, na * gi[...])
    r_hi[...], r_lo[...] = split(dy1)
    spill.emit(lambda t: product(th, tl, r_hi, r_lo, t), column_copies(G, 0))
    put_turned(th, tl, ny * gf[...])
    for j in range(4):
        r_hi[...], r_lo[...] = split(E[:, D * j : D * j + D])
        spill.emit(lambda t: product(th, tl, r_hi, r_lo, t), column_copies(G, 1 + j))
    r_hi[...], r_lo[...] = split(g_ref[...])
    for j in range(4):
        cols = slice(D * j, D * j + D)
        put_turned(th, tl, U[:, cols] * gh[:, cols])
        spill.emit(lambda t: product(th, tl, r_hi, r_lo, t), row_copies(G, j, 5))
    spill.close()
    travel.finish()


PIECE = 24


def grad_shape(n):
    return jax.ShapeDtypeStruct((2, 2, 4, 2, n, PIECE, D), F32)


def tile_scratch():
    return [
        pltpu.VMEM((D, ROWS), BF16),
        pltpu.VMEM((D, ROWS), BF16),
        pltpu.VMEM((ROWS, D), BF16),
        pltpu.VMEM((ROWS, D), BF16),
        pltpu.VMEM((2, D, D), F32),
        pltpu.SemaphoreType.DMA((2, 32)),
    ]


def feed_forward(rec, x, g, wo, wu, wd, gi, gf, gh, sums):
    act = jax.ShapeDtypeStruct((ROWS, D), F32)
    wide = pltpu.VMEM((ROWS, FF), F32)
    thin = pltpu.VMEM((ROWS, D), F32)
    return pl.pallas_call(
        ff_kernel,
        out_shape=[
            jax.ShapeDtypeStruct((ROWS, 1, D), F32),
            jax.ShapeDtypeStruct((HOMES, HALF, 128), F32),
            act,
            jax.ShapeDtypeStruct((8, D), F32),
            grad_shape(9),
        ],
        in_specs=[VM] * 10,
        out_specs=[VM, ANY, VM, VM, ANY],
        scratch_shapes=[
            pltpu.VMEM((HEADS, HALF, 128), F32),
            pltpu.VMEM((2 * ROWS, D), BF16),
            pltpu.VMEM((2 * ROWS, FT), BF16),
            pltpu.VMEM((1, D), F32),
            pltpu.VMEM((1, D), F32),
            pltpu.VMEM((1, FF), F32),
            pltpu.VMEM((1, FF), F32),
            thin,
            thin,
            thin,
            thin,
            wide,
            wide,
            wide,
            thin,
        ]
        + tile_scratch()
        + [pltpu.SemaphoreType.DMA((HEADS,)), pltpu.SemaphoreType.DMA((HOMES,))],
        compiler_params=params(collective_id=4, has_side_effects=True),
    )(rec, x, g, wo, wu, wd, gi, gf, gh, sums)


class Place:
    def __init__(self):
        p, s = lax.axis_index("pat"), lax.axis_index("seq")
        self.p, self.s = p, s
        self.x, self.core, self.z, self.y = p // 2, lax.rem(p, 2), s // 2, lax.rem(s, 2)
        self.peer = to(self.x * 2 + 1 - self.core, s)
        self.xn = to((1 - self.x) * 2 + self.core, s)
        self.yn = to(p, self.z * 2 + 1 - self.y)
        self.left, self.right = to(p, s - 2), to(p, s + 2)

    def greet(self, barrier):
        for d in (self.peer, self.xn, self.yn):
            pl.semaphore_signal(barrier, inc=1, device_id=d, device_id_type=MESH)

        @pl.when(self.z > 0)
        def _():
            pl.semaphore_signal(barrier, inc=1, device_id=self.left, device_id_type=MESH)

        @pl.when(self.z < 3)
        def _():
            pl.semaphore_signal(barrier, inc=1, device_id=self.right, device_id_type=MESH)

        return 3 + (self.z > 0).astype(jnp.int32) + (self.z < 3).astype(jnp.int32)


def remote(src, dst, a, b, d):
    return pltpu.make_async_remote_copy(
        src_ref=src, dst_ref=dst, send_sem=a, recv_sem=b, device_id=d, device_id_type=MESH
    )


class Chunk:
    def __init__(self, place, k, group, slot, own, osem, bufs, sems, put, x_first):
        self.at, self.k, self.group, self.slot, self.own, self.osem = place, k, group, slot, own, osem
        self.b0, self.b1, self.b2, self.bl, self.br = bufs
        self.sc, self.rc, self.s1, self.r1, self.s2, self.r2, self.sl, self.rl, self.sr, self.rr = sems
        self.put, self.x_first = put, x_first

    def core(self):
        k, c = self.k, 1 - self.at.core
        return [
            remote(self.group(i, c), self.b0.at[i], self.sc.at[k, i], self.rc.at[k, i], self.at.peer)
            for i in range(2)
        ]

    def load(self):
        return [
            pltpu.make_async_copy(self.group(i, self.at.core), self.own.at[i], self.osem.at[self.slot, i])
            for i in range(2)
        ]

    def one(self):
        k, at = self.k, self.at
        if self.x_first:
            return remote(self.b0.at[1 - at.x], self.b1, self.s1.at[k], self.r1.at[k], at.xn)
        return remote(self.b0.at[:, :, 1 - at.y], self.b1, self.s1.at[k], self.r1.at[k], at.yn)

    def two(self):
        k, at = self.k, self.at
        if self.x_first:
            return remote(self.b1.at[:, 1 - at.y], self.b2, self.s2.at[k], self.r2.at[k], at.yn)
        return remote(self.b1.at[1 - at.x], self.b2, self.s2.at[k], self.r2.at[k], at.xn)

    def rightward(self, i):
        k, part = self.k, pl.ds(i + 1, 3 - i)
        src = self.b2 if i == 0 else self.bl
        return remote(src.at[part], self.bl.at[part], self.sr.at[k], self.rl.at[k], self.at.right)

    def leftward(self, i):
        k, part = self.k, pl.ds(0, i)
        src = self.b2 if i == 3 else self.br
        return remote(src.at[part], self.br.at[part], self.sl.at[k], self.rr.at[k], self.at.left)

    def stage1(self):
        if self.own is not None:
            for c in self.load():
                c.wait()
        for c in self.core():
            c.wait_recv()
        if self.own is not None:
            self.b0[...] += self.own[...]
        else:
            for i in range(2):
                self.b0[i] += self.group(i, self.at.core)[...]
        self.one().start()

    def stage2(self):
        self.one().wait_recv()
        mine = self.b0[self.at.x] if self.x_first else self.b0[:, :, self.at.y]
        self.b1[...] += mine
        self.two().start()

    def stage3(self):
        self.two().wait_recv()
        mine = self.b1[:, self.at.y] if self.x_first else self.b1[self.at.x]
        self.b2[...] += mine

        @pl.when(self.at.z == 0)
        def _():
            self.rightward(0).start()

        @pl.when(self.at.z == 3)
        def _():
            self.leftward(3).start()

    def stage4(self):
        @pl.when(self.at.z == 1)
        def _():
            self.rightward(0).wait_recv()
            self.bl[2:4] += self.b2[2:4]
            self.rightward(1).start()

        @pl.when(self.at.z == 2)
        def _():
            self.leftward(3).wait_recv()
            self.br[0:2] += self.b2[0:2]
            self.leftward(2).start()

    def stage5(self):
        @pl.when(self.at.z == 2)
        def _():
            self.rightward(1).wait_recv()
            self.bl[3:4] += self.b2[3:4]
            self.rightward(2).start()

        @pl.when(self.at.z == 1)
        def _():
            self.leftward(2).wait_recv()
            self.br[0:1] += self.b2[0:1]
            self.leftward(1).start()

    def stage6(self):
        @pl.when(self.at.z == 3)
        def _():
            self.rightward(2).wait_recv()
            self.put(self.b2[3] + self.bl[3])

        @pl.when(self.at.z == 0)
        def _():
            self.leftward(1).wait_recv()
            self.put(self.b2[0] + self.br[0])

        @pl.when(self.at.z == 1)
        def _():
            self.put(self.b2[1] + self.bl[1] + self.br[1])

        @pl.when(self.at.z == 2)
        def _():
            self.put(self.b2[2] + self.bl[2] + self.br[2])

    def sent(self):
        for c in self.core() + [self.one(), self.two()]:
            c.wait_send()
        for i in range(4):

            @pl.when(self.at.z == i)
            def _(i=i):
                if i < 3:
                    self.rightward(i).wait_send()
                if i > 0:
                    self.leftward(i).wait_send()


class Reducer:
    def __init__(self, place, n, rows, parts, scratch, put, staged):
        self.place, self.n, self.parts, self.put, self.staged = place, n, parts, put, staged
        scratch = list(scratch)
        self.own = scratch.pop(0) if staged else None
        self.osem = scratch.pop(0) if staged else None
        self.c0, self.c1a, self.c1b, self.c2, self.zl, self.zr = scratch[:6]
        self.sems = scratch[6:16]
        self.pairs = (n + 1) // 2

    @staticmethod
    def scratch(n, rows, staged):
        dma = pltpu.SemaphoreType.DMA
        bufs = [(n, 2, 4, 2), ((n + 1) // 2, 4, 2), (max(n // 2, 1), 2, 4), (n, 4), (n, 4), (n, 4)]
        return (
            ([pltpu.VMEM((4, 2, 4, 2, rows, D), F32), dma((4, 2))] if staged else [])
            + [pltpu.VMEM(b + (rows, D), F32) for b in bufs]
            + [dma((n, 2)), dma((n, 2))]
            + [dma((n,)) for _ in range(8)]
        )

    def chunk(self, k, parity):
        slot = lax.rem(k, 4)
        b1 = (self.c1b if parity else self.c1a).at[k // 2]
        return Chunk(
            self.place,
            k,
            lambda i, c: self.parts(k).at[i, c],
            slot,
            self.own.at[slot] if self.staged else None,
            self.osem,
            (self.c0.at[k], b1, self.c2.at[k], self.zl.at[k], self.zr.at[k]),
            self.sems,
            lambda v: self.put(k, v),
            parity == 0,
        )

    def begin(self):
        def one(k, carry):
            for c in self.chunk(k, 0).core():
                c.start()
            return carry

        lax.fori_loop(0, self.n, one, 0)
        for k in range(min(2, self.n)):
            for c in self.chunk(jnp.int32(k), 0).load():
                c.start()

    def send(self, first, after):
        for k in range(first, after):
            for c in self.chunk(jnp.int32(k), 0).core():
                c.start()

    def one(self, stage, pair):
        for parity in range(2):
            k = jnp.int32(2 * pair + parity)

            @pl.when(jnp.logical_and(k >= 0, k < self.n))
            def _(k=k, parity=parity):
                if stage == 1 and self.staged:

                    @pl.when(k + 2 < self.n)
                    def _():
                        for c in self.chunk(k + 2, 0).load():
                            c.start()

                getattr(self.chunk(k, parity), f"stage{stage}")()

    def early(self, pair):
        self.one(1, pair)

    def step(self, tau):
        self.one(1, tau)
        for stage in range(2, 7):
            self.one(stage, tau - stage)

    def finish(self):
        def one(k, carry):
            for parity in range(2):

                @pl.when(lax.rem(k, 2) == parity)
                def _(parity=parity):
                    self.chunk(k, parity).sent()

            return carry

        lax.fori_loop(0, self.n, one, 0)


class SmallSum:
    def __init__(self, place, S, bufs, send, recv, put):
        self.at, self.S, self.send, self.recv, self.put = place, S, send, recv, put
        self.d0, self.d1, self.d2, self.dl, self.dr, self.t1, self.t2, self.t3, self.fl, self.fr = bufs

    @staticmethod
    def scratch():
        return [pltpu.VMEM((8, D), F32)] * 10 + [pltpu.SemaphoreType.DMA((5,)), pltpu.SemaphoreType.DMA((5,))]

    def hop(self, src, dst, i, d):
        return remote(src, dst, self.send.at[i], self.recv.at[i], d)

    def core(self):
        return self.hop(self.S, self.d0, 0, self.at.peer)

    def along_x(self):
        return self.hop(self.t1, self.d1, 1, self.at.xn)

    def along_y(self):
        return self.hop(self.t2, self.d2, 2, self.at.yn)

    def rightward(self, i):
        return self.hop(self.t3 if i == 0 else self.fl, self.dl, 3, self.at.right)

    def leftward(self, i):
        return self.hop(self.t3 if i == 3 else self.fr, self.dr, 4, self.at.left)

    def stage1(self):
        self.core().wait_recv()
        self.t1[...] = self.S[...] + self.d0[...]
        self.along_x().start()

    def stage2(self):
        self.along_x().wait_recv()
        self.t2[...] = self.t1[...] + self.d1[...]
        self.along_y().start()

    def stage3(self):
        self.along_y().wait_recv()
        self.t3[...] = self.t2[...] + self.d2[...]

        @pl.when(self.at.z == 0)
        def _():
            self.rightward(0).start()

        @pl.when(self.at.z == 3)
        def _():
            self.leftward(3).start()

    def from_left(self, i):
        self.rightward(i).wait_recv()
        self.fl[...] = self.dl[...] + self.t3[...]

    def from_right(self, i):
        self.leftward(i).wait_recv()
        self.fr[...] = self.dr[...] + self.t3[...]

    def stage4(self):
        @pl.when(self.at.z == 1)
        def _():
            self.from_left(0)
            self.rightward(1).start()

        @pl.when(self.at.z == 2)
        def _():
            self.from_right(3)
            self.leftward(2).start()

    def stage5(self):
        @pl.when(self.at.z == 2)
        def _():
            self.from_left(1)
            self.rightward(2).start()

        @pl.when(self.at.z == 1)
        def _():
            self.from_right(2)
            self.leftward(1).start()

    def stage6(self):
        @pl.when(self.at.z == 3)
        def _():
            self.from_left(2)
            self.put(self.fl[...])

        @pl.when(self.at.z == 0)
        def _():
            self.from_right(1)
            self.put(self.fr[...])

        @pl.when(jnp.logical_or(self.at.z == 1, self.at.z == 2))
        def _():
            self.put(self.fl[...] + self.dr[...])

    def finish(self):
        for c in (self.core(), self.along_x(), self.along_y()):
            c.wait_send()
        for i in range(4):

            @pl.when(self.at.z == i)
            def _(i=i):
                if i < 3:
                    self.rightward(i).wait_send()
                if i > 0:
                    self.leftward(i).wait_send()


def small_outputs(place, counts, outs, tot):
    ga, gi, gf, gh, means = outs

    def put(v):
        tot[...] = v
        d = place.p * RUNS + place.s
        for i, ref in enumerate((ga, gi, gf)):
            ref[...] = pltpu.roll(tot[i : i + 1, :], D - PIECE * d, 1)[:, :PIECE]
        row = tot[pl.ds(3 + d // 8, 1), :]
        gh[...] = pltpu.roll(row, D - 4 * PIECE * lax.rem(d, 8), 1)[:, : 4 * PIECE]
        lane = lax.broadcasted_iota(jnp.int32, (1, 128), 1)
        scale = jnp.full((1, 128), counts[0], F32)
        for i in range(1, PATTERNS):
            scale = jnp.where(lane == i, counts[i], scale)
        means[...] = (tot[7:8, :128] / scale)[:, :PATTERNS]

    return put


N_PIECES = 9
SUB = 8


def finish_kernel(counts, rec, x_ref, dy1_ref, w, ga1, S_in, gx, g_qkv, ga, gi, gf, gh, means, dqkv, lhs, th, tl, r_hi, r_lo, tiles, S, tot, *scratch):
    place = Place()
    barrier = pltpu.get_barrier_semaphore()
    expected = place.greet(barrier)
    for j in range(HEADS // 2):
        u, v = rec[2 * j, ROWS:PACK, :], rec[2 * j + 1, ROWS:PACK, :]
        cols = slice(128 * j, 128 * j + 128)
        dqkv[0:HALF, cols] = pick(u, swap(v))
        dqkv[HALF:ROWS, cols] = pick(swap(u), v)
        u, v = rec[2 * j, 0:ROWS, :], rec[2 * j + 1, 0:ROWS, :]
        dqkv[:, D + 128 * j : D + 128 * j + 128] = pick(u, swap(v))
        dqkv[:, 2 * D + 128 * j : 2 * D + 128 * j + 128] = pick(swap(u), v)
    gain = ga1[...][None, :]
    n, rs = normed(x_ref[...])
    put_turned(th, tl, n * gain)

    def parts(k):
        return tiles.at[k // 3, :, :, :, :, pl.ds(pl.multiple_of(lax.rem(k, 3) * SUB, SUB), SUB), :]

    def put(k, v):
        g_qkv[
            pl.ds(pl.multiple_of(lax.rem(k, 3) * SUB, SUB), SUB), pl.ds(pl.multiple_of((k // 3) * D, D), D)
        ] = v

    n_r = 16
    big = Reducer(place, N_PIECES, SUB, parts, scratch[:n_r], put, False)
    rest = scratch[n_r:]
    small = SmallSum(
        place, S, rest[:10], rest[10], rest[11], small_outputs(place, counts, (ga, gi, gf, gh, means), tot)
    )
    for j in range(3):
        r_hi[...], r_lo[...] = split(dqkv[:, D * j : D * j + D])

        def one(i, carry):
            rows = pl.ds(pl.multiple_of(i * ROWS, 64), ROWS)
            h, l = th[rows, :], tl[rows, :]
            v = dot_nn(h, r_hi[...]) + dot_nn(h, r_lo[...]) + dot_nn(l, r_hi[...])
            tiles[j, i // 2, lax.rem(i, 2)] = v.reshape(4, 2, PIECE, D)
            return carry

        lax.fori_loop(0, 4, one, 0)
        if j == 0:
            pl.semaphore_wait(barrier, expected)
        big.send(3 * j, 3 * j + 3)
    big.early(0)
    big.early(1)
    e = None
    for j in range(3):
        cols = slice(D * j, D * j + D)
        put_split(lhs, dqkv[:, cols])
        more = halves_sum(dot_nt(lhs[...], w[:, cols]))
        e = more if e is None else e + more
        if j == 0:
            big.step(2)
    S[...] = S_in[...]
    S[0:1, :] = jnp.sum(e * n, 0, keepdims=True)
    small.core().start()
    gx[...] = (dy1_ref[...] + norm_back(e * gain, n, rs)).reshape(ROWS, 1, D)
    small.stage1()

    def step(tau, carry):
        for stage in range(2, 7):

            @pl.when(tau == stage + 1)
            def _(stage=stage):
                getattr(small, f"stage{stage}")()

        big.step(tau)
        return carry

    lax.fori_loop(3, big.pairs + 6, step, 0)

    def close(k, carry):
        for parity in range(2):

            @pl.when(lax.rem(k, 2) == parity)
            def _(parity=parity):
                big.chunk(k, parity).sent()

        return carry

    lax.fori_loop(0, N_PIECES, close, 0)
    small.finish()


def finish(rec, x, dy1, w, ga, S, counts, cid):
    return pl.pallas_call(
        functools.partial(finish_kernel, counts),
        out_shape=[jax.ShapeDtypeStruct((ROWS, 1, D), F32), jax.ShapeDtypeStruct((PIECE, 3 * D), F32)]
        + [jax.ShapeDtypeStruct((1, n), F32) for n in (PIECE, PIECE, PIECE, 4 * PIECE, PATTERNS)],
        in_specs=[VM] * 6,
        out_specs=[VM] * 7,
        scratch_shapes=[
            pltpu.VMEM((ROWS, 3 * D), F32),
            pltpu.VMEM((2 * ROWS, D), BF16),
            pltpu.VMEM((D, ROWS), BF16),
            pltpu.VMEM((D, ROWS), BF16),
            pltpu.VMEM((ROWS, D), BF16),
            pltpu.VMEM((ROWS, D), BF16),
            pltpu.VMEM((3, 2, 2, 4, 2, PIECE, D), F32),
            pltpu.VMEM((8, D), F32),
            pltpu.VMEM((8, D), F32),
        ]
        + Reducer.scratch(N_PIECES, SUB, False)
        + SmallSum.scratch(),
        compiler_params=params(collective_id=cid, has_side_effects=True),
    )(rec, x, dy1, w, ga, S)


def deliver_kernel(*refs):
    n = len(refs) // 2
    for src, dst in zip(refs[:n], refs[n:]):
        dst[...] = src[...]


def deliver(*arrays):
    return pl.pallas_call(
        deliver_kernel,
        out_shape=[jax.ShapeDtypeStruct(v.shape, v.dtype) for v in arrays],
        in_specs=[VM] * len(arrays),
        out_specs=[VM] * len(arrays),
        compiler_params=params(),
    )(*arrays)


N_FF = 9


def back_all_kernel(offs, drec, own, sib, ap, lse, G, grec, wo_g, up_g, down_g, qst, kc, vc, kt, qc, dc, lt, k4, v4, kt4, q4, d4, lt4, k5, v5, kt5, q5, d5, lt5, pp, sp, dqt, dk, dv, dq, dk4, dv4, dk5, dv5, dq4, dq5, b1, b2, b3, b4, ds_out, came, lsem, send, recv, qsend, qrecv, fsend, frecv, *scratch):
    place = Place()
    p, s, x, core, active, head = place_facts()
    b = core
    o2, o3, o4, o5 = offs[1], offs[2], offs[3], offs[4]
    kvf, qf, X, df = dk, dv.at[0:2], dv.at[2:4], dq
    dqp = qst

    barrier = pltpu.get_barrier_semaphore()
    expected = place.greet(barrier)

    def greet_heads(h, carry):
        q, t = head_device(h, x)

        @pl.when(jnp.logical_not(same(p, s, q, t)))
        def _():
            pl.semaphore_signal(barrier, inc=1, device_id=to(q, t), device_id_type=MESH)

        return carry

    lax.fori_loop(0, HEADS, greet_heads, 0)
    from_homes = HOMES - (core == x).astype(jnp.int32)
    pl.semaphore_wait(barrier, expected + active.astype(jnp.int32) * from_homes)

    def put(k, v):
        @pl.when(k == 0)
        def _():
            wo_g[...] = v

        @pl.when(jnp.logical_and(k > 0, k < 5))
        def _():
            up_g[:, pl.ds(pl.multiple_of((k - 1) * D, D), D)] = v

        @pl.when(k >= 5)
        def _():
            down_g[pl.ds(pl.multiple_of((k - 5) * PIECE, PIECE), PIECE), :] = v

    big = Reducer(place, N_FF, PIECE, lambda k: G.at[:, :, :, :, k], scratch, put, True)
    big.begin()

    def local_copies(m):
        t = pl.multiple_of((m // 2) * ROWS, 64)
        c, d = 2 * b + lax.rem(m, 2), 2 * (1 - b) + lax.rem(m, 2)
        return [
            pltpu.make_async_copy(own.at[m, pl.ds(0, ROWS), :], kvf.at[c, pl.ds(t, ROWS), :], lsem.at[m, 0]),
            pltpu.make_async_copy(sib.at[m], kvf.at[d, pl.ds(t, ROWS), :], lsem.at[m, 1]),
            pltpu.make_async_copy(own.at[m, pl.ds(ROWS, HALF), :], qst.at[m], lsem.at[m, 2]),
        ]

    lse_copy = pltpu.make_async_copy(lse, X, lsem.at[HOMES, 0])

    @pl.when(active)
    def _():
        lse_copy.start()

        def start(m, carry):
            for c in local_copies(m):
                c.start()
            return carry

        lax.fori_loop(0, HOMES, start, 0)
        b1[...] = key_bias((2, 128), (4, 128), 4, 1, 2 * b, True)
        b2[...] = key_bias((1, 256), (2, 256), 4, 2, 2 * b, True)
        b3[...] = key_bias((1, 256), (1, 256), 1, 1, 0, True)
        e4 = class_facts4(o4, b)[1]
        b4[...] = key_bias((1, 256), (2, 256), 12, 6, 6 * e4, True)

        def wait(m, carry):
            for c in local_copies(m):
                c.wait()
            return carry

        lax.fori_loop(0, HOMES, wait, 0)
        lse_copy.wait()
        unpack_pairs(qst, 0, qf, 1.0 / math.sqrt(HD))

        def prepare(i, carry):
            c, t = i // 12, pl.multiple_of(lax.rem(i, 12) * 128, 128)
            k2, v2 = keys_and_values(kvf[c, pl.ds(t, 128), :])
            kc[c, pl.ds(t, 128), :] = k2.astype(BF16)
            vc[c, pl.ds(t, 128), :] = v2.astype(BF16)
            kt[c, :, pl.ds(t, 128)] = k2.T.astype(BF16)
            return carry

        lax.fori_loop(0, 48, prepare, 0)

        def prepare_q(i, carry):
            c, t = i // 12, pl.multiple_of(lax.rem(i, 12) * 128, 128)
            qc[c, pl.ds(t, 128), :] = query_quads(qf[c, pl.ds(t, 128), :])
            return carry

        lax.fori_loop(0, 24, prepare_q, 0)

    keys4, e4, (qc4, qv4) = class_facts4(o4, b)
    kc5, kv5 = lax.rem(o5, 4), o5 // 4
    qi4, qi5 = qc4 - 2 * b, lax.rem(kc5, 2)

    @pl.when(active)
    def _():
        for blk in range(4):
            r = slice(128 * blk, 128 * blk + 128)
            for e in range(2):
                c, v = keys4[e]
                k2, v2 = keys_and_values(kvf[c, pl.ds(v + 384 * blk, 128, stride=3), :])
                k4[e, r, :] = k2.astype(BF16)
                v4[e, r, :] = v2.astype(BF16)
                kt4[e, :, r] = k2.T.astype(BF16)
            q4[r, :] = query_quads(qf[qi4, pl.ds(qv4 + 384 * blk, 128, stride=3), :])
            rows = pl.ds(kv5 + 384 * blk, 128, stride=3)
            k2, v2 = keys_and_values(kvf[kc5, rows, :])
            k5[r, :] = k2.astype(BF16)
            v5[r, :] = v2.astype(BF16)
            kt5[:, r] = k2.T.astype(BF16)
            q5[r, :] = query_quads(qf[qi5, rows, :])
        dk[...] = jnp.zeros_like(dk)

    big.early(0)
    big.early(1)

    @pl.when(active)
    def _():
        unpack_pairs(drec, 0, df, 1.0)

        def facts(m, carry):
            ci = lax.rem(m, 2)
            t = pl.multiple_of((m // 2) * ROWS, 32)
            prod = drec[m] * ap[m]
            low = lower_lanes(prod)
            d0 = jnp.sum(jnp.where(low, prod, 0.0), -1, keepdims=True)
            d1 = jnp.sum(jnp.where(low, 0.0, prod), -1, keepdims=True)
            for part, d in ((0, d0), (1, d1)):
                rows = pl.ds(t + HALF * part, HALF)
                l = X[ci, rows, :]
                X[ci, rows, :] = jnp.where(low, l, jnp.broadcast_to(d, l.shape))
            return carry

        lax.fori_loop(0, HOMES, facts, 0)

        def turned(v):
            w = v.T
            return jnp.concatenate([w[0:1, :], w[HD : HD + 1, :]], 0)

        def prepare_d(i, carry):
            c, t = i // 12, pl.multiple_of(lax.rem(i, 12) * 128, 128)
            rows = pl.ds(t, 128)
            dc[c, rows, :] = query_quads(df[c, rows, :])
            lt[i] = turned(X[c, rows, :])
            return carry

        lax.fori_loop(0, 24, prepare_d, 0)
        for blk in range(4):
            r = slice(128 * blk, 128 * blk + 128)
            rows = pl.ds(qv4 + 384 * blk, 128, stride=3)
            d4[r, :] = query_quads(df[qi4, rows, :])
            lt4[blk] = turned(X[qi4, rows, :])
            rows = pl.ds(kv5 + 384 * blk, 128, stride=3)
            d5[r, :] = query_quads(df[qi5, rows, :])
            lt5[blk] = turned(X[qi5, rows, :])
        dv[...] = jnp.zeros_like(dv)

    big.step(2)

    def tile(g, k, v, kT, q, d, facts_pair, bias, first):
        l0, l1 = facts_pair
        row = jnp.concatenate([l0[0:1, :], l1[0:1, :]], 1)
        delta = jnp.concatenate([l0[1:2, :], l1[1:2, :]], 1)
        n = k.shape[0] // 128
        kk, vv = doubled(k), doubled(v)
        for i in range(n):
            piece = slice(128 * i, 128 * i + 128)
            s_ = dot_nt(kk[piece], q)
            if bias is not None:
                s_ = s_ + bias[piece, :]
            pr = jnp.exp(s_ - row)
            ds = pr * (dot_nt(vv[piece], d) - delta)
            hi, lo = split(pr)
            pp[g, piece, 0:256] = hi
            pp[g, piece, 256:512] = lo
            hi, lo = split(ds)
            sp[g, piece, 0:256] = hi
            sp[g, piece, 256:512] = lo
        d2, q2_ = d[:, :128], q[:, :128]
        rows = slice(0, 128 * n)
        dv_new = dot_nn(pp[g, rows, :], jnp.concatenate([d2, d2], 0))
        dk_new = dot_nn(sp[g, rows, :], jnp.concatenate([q2_, q2_], 0))
        dq_new = dot_nn(kT, sp[g, rows, 0:256]) + dot_nn(kT, sp[g, rows, 256:512])
        dqt[g] = dq_new if first else dqt[g] + dq_new
        return dk_new, dv_new

    def q1(qb, carry):
        def at(g, blk):
            return pl.ds(pl.multiple_of(512 * g + 128 * blk, 128), 128)

        def step(kb, bias, first):
            for g in range(3):
                ks, qs = at(g, kb), at(g, qb)
                kT = jnp.concatenate([kt[c, :, ks] for c in range(4)], 1)
                a, c = tile(
                    g,
                    kc[:, ks, :].reshape(512, 128),
                    vc[:, ks, :].reshape(512, 128),
                    kT,
                    qc[:, qs, :].reshape(256, 256),
                    dc[:, qs, :].reshape(256, 256),
                    (lt.at[4 * g + qb], lt.at[12 + 4 * g + qb]),
                    bias,
                    first,
                )
                dk[:, ks, :] += a.reshape(4, 128, 128)
                dv[:, ks, :] += c.reshape(4, 128, 128)

        step(qb, b1, True)

        def more(kb, inner):
            step(kb, None, False)
            return inner

        lax.fori_loop(0, qb, more, 0)
        for g in range(3):
            dq[:, at(g, qb), :] = dqt[g].T.reshape(2, 128, 128)
        return carry

    for first, after, tau in ((0, 2, 3), (2, 3, 4), (3, 4, 5)):

        @pl.when(active)
        def _(first=first, after=after):
            lax.fori_loop(first, after, q1, 0)

        big.step(tau)

    def at256(blk):
        return pl.ds(pl.multiple_of(256 * blk, 128), 256)

    def kept(flag, v):
        return jnp.where(flag, v, 0.0)

    def q2(qb, carry):
        def step(kb, bias, first):
            ks, qs = at256(kb), at256(qb)
            a, c = tile(
                0,
                jnp.concatenate([kc[o2, ks, :], kc[o2 + 2, ks, :]], 0),
                jnp.concatenate([vc[o2, ks, :], vc[o2 + 2, ks, :]], 0),
                jnp.concatenate([kt[o2, :, ks], kt[o2 + 2, :, ks]], 1),
                qc[o2, qs, :],
                dc[o2, qs, :],
                (lt.at[12 * o2 + 2 * qb], lt.at[12 * o2 + 2 * qb + 1]),
                bias,
                first,
            )
            for par in range(2):
                f = o2 == par
                dk[par, ks, :] += kept(f, a[:256])
                dk[par + 2, ks, :] += kept(f, a[256:])
                dv[par, ks, :] += kept(f, c[:256])
                dv[par + 2, ks, :] += kept(f, c[256:])

        step(qb, b2, True)

        def more(kb, inner):
            step(kb, None, False)
            return inner

        lax.fori_loop(jnp.where(qb >= 4, 4, 0), qb, more, 0)
        for par in range(2):
            dq[par, at256(qb), :] += kept(o2 == par, dqt[0].T)
        return carry

    @pl.when(active)
    def _():
        lax.fori_loop(0, TOTAL // 256, q2, 0)

    big.step(6)

    def q3(qb, carry):
        ci = lax.rem(o3, 2)

        def step(kb, bias, first):
            ks, qs = at256(kb), at256(qb)
            a, c = tile(
                0,
                kc[o3, ks, :],
                vc[o3, ks, :],
                kt[o3, :, ks],
                qc[ci, qs, :],
                dc[ci, qs, :],
                (lt.at[12 * ci + 2 * qb], lt.at[12 * ci + 2 * qb + 1]),
                bias,
                first,
            )
            for i in range(2):
                f = o3 == 2 * b + i
                dk[2 * b + i, ks, :] += kept(f, a)
                dv[2 * b + i, ks, :] += kept(f, c)

        step(qb, b3, True)

        def more(kb, inner):
            step(kb, None, False)
            return inner

        lax.fori_loop(0, qb, more, 0)
        for i in range(2):
            dq[i, at256(qb), :] += kept(o3 == 2 * b + i, dqt[0].T)
        return carry

    for first, after, tau in ((0, 4, 7), (4, 6, 8)):

        @pl.when(active)
        def _(first=first, after=after):
            lax.fori_loop(first, after, q3, 0)

        big.step(tau)

    @pl.when(active)
    def _():
        for ref in (dk4, dv4, dk5, dv5):
            ref[...] = jnp.zeros_like(ref)
        for qb in range(2):
            qs = slice(256 * qb, 256 * qb + 256)
            for kb in range(qb, -1, -1):
                ks = slice(256 * kb, 256 * kb + 256)
                a, c = tile(
                    0,
                    k4[:, ks, :].reshape(512, 128),
                    v4[:, ks, :].reshape(512, 128),
                    jnp.concatenate([kt4[0, :, ks], kt4[1, :, ks]], 1),
                    q4[qs, :],
                    d4[qs, :],
                    (lt4.at[2 * qb], lt4.at[2 * qb + 1]),
                    b4 if kb == qb else None,
                    kb == qb,
                )
                dk4[:, ks, :] += a.reshape(2, 256, 128)
                dv4[:, ks, :] += c.reshape(2, 256, 128)
                a, c = tile(
                    1,
                    k5[ks, :],
                    v5[ks, :],
                    kt5[:, ks],
                    q5[qs, :],
                    d5[qs, :],
                    (lt5.at[2 * qb], lt5.at[2 * qb + 1]),
                    b3 if kb == qb else None,
                    kb == qb,
                )
                dk5[ks, :] += a
                dv5[ks, :] += c
            dq4[qs, :] = dqt[0].T
            dq5[qs, :] = dqt[1].T
        mine5 = kc5 // 2 == b
        for kind in range(12):
            c, rows = kind % 4, pl.ds(kind // 4, THIRD, stride=3)
            f0, f1, f5 = o4 == kind, o4 + 6 == kind, jnp.logical_and(o5 == kind, mine5)
            dk[c, rows, :] += kept(f0, dk4[0]) + kept(f1, dk4[1]) + kept(f5, dk5[...])
            dv[c, rows, :] += kept(f0, dv4[0]) + kept(f1, dv4[1]) + kept(f5, dv5[...])
        for ci in range(2):
            for v in range(3):
                rows = pl.ds(v, THIRD, stride=3)
                f4 = jnp.logical_and(qi4 == ci, qv4 == v)
                f5 = jnp.logical_and(jnp.logical_and(qi5 == ci, kv5 == v), mine5)
                dq[ci, rows, :] += kept(f4, dq4[...]) + kept(f5, dq5[...])

    big.step(9)

    def passed(m):
        return remote(ds_out.at[m], came.at[m], fsend.at[m], frecv.at[m], place.peer)

    def home_copies(m):
        q, t = home_device(core, m)
        kv = remote(came.at[m], grec.at[head, pl.ds(0, ROWS), :], send.at[m], recv.at[head], to(q, t))
        dq_ = remote(dqp.at[m], grec.at[head, pl.ds(ROWS, HALF), :], qsend.at[m], qrecv.at[head], to(q, t))
        return q, t, kv, dq_

    @pl.when(active)
    def _():
        def rows_of(m):
            return pl.ds(pl.multiple_of((m // 2) * ROWS, 64), ROWS)

        def kv(c, m):
            k, v = dk[c, rows_of(m), :], dv[c, rows_of(m), :]
            return pick(k + swap(k), v + swap(v))

        def share(m, carry):
            ds_out[m] = kv(2 * (1 - b) + lax.rem(m, 2), m)
            passed(m).start()
            return carry

        lax.fori_loop(0, HOMES, share, 0)

        def add(m, carry):
            q, t, far_kv, far_q = home_copies(m)
            ci = lax.rem(m, 2)
            v = dq[ci, rows_of(m), :]
            v = (v + swap(v)) * (1.0 / math.sqrt(HD))
            dqp[m] = pick(v[:HALF], v[HALF:])
            passed(m).wait_recv()
            came[m] += kv(2 * b + ci, m)

            @pl.when(same(p, s, q, t))
            def _():
                pltpu.make_async_copy(came.at[m], grec.at[head, pl.ds(0, ROWS), :], recv.at[head]).start()
                pltpu.make_async_copy(dqp.at[m], grec.at[head, pl.ds(ROWS, HALF), :], qrecv.at[head]).start()

            @pl.when(jnp.logical_not(same(p, s, q, t)))
            def _():
                far_kv.start()
                far_q.start()

            return carry

        lax.fori_loop(0, HOMES, add, 0)

    big.step(10)

    def from_head(h, carry):
        a = grec.at[h, pl.ds(0, ROWS), :]
        c = grec.at[h, pl.ds(ROWS, HALF), :]
        pltpu.make_async_copy(a, a, recv.at[h]).wait()
        pltpu.make_async_copy(c, c, qrecv.at[h]).wait()
        return carry

    lax.fori_loop(0, HEADS, from_head, 0)
    big.finish()

    @pl.when(active)
    def _():
        def sent(m, carry):
            q, t, far_kv, far_q = home_copies(m)
            passed(m).wait_send()

            @pl.when(jnp.logical_not(same(p, s, q, t)))
            def _():
                far_kv.wait_send()
                far_q.wait_send()

            return carry

        lax.fori_loop(0, HOMES, sent, 0)


def backward_all(offs, drec, own, sib, ap, lse, G, cid):
    dma = pltpu.SemaphoreType.DMA
    keys = pltpu.VMEM((4, TOTAL, 128), BF16)
    full = pltpu.VMEM((4, TOTAL, 128), F32)
    quad = pltpu.VMEM((2, TOTAL, 256), BF16)
    quad3 = pltpu.VMEM((THIRD, 256), BF16)
    pair3 = pltpu.VMEM((THIRD, 128), BF16)
    turned = pltpu.VMEM((128, THIRD), BF16)
    facts3 = pltpu.VMEM((4, 2, 128), F32)
    out3 = pltpu.VMEM((THIRD, 128), F32)
    packs = pltpu.VMEM((HOMES, ROWS, 128), F32)
    halves = pltpu.VMEM((HOMES, HALF, 128), F32)
    return pl.pallas_call(
        back_all_kernel,
        out_shape=[
            jax.ShapeDtypeStruct((HEADS, PACK, 128), F32),
            jax.ShapeDtypeStruct((PIECE, D), F32),
            jax.ShapeDtypeStruct((PIECE, FF), F32),
            jax.ShapeDtypeStruct((4 * PIECE, D), F32),
        ],
        in_specs=[SM, VM, ANY, ANY, VM, ANY, ANY],
        out_specs=[ANY, VM, VM, VM],
        scratch_shapes=[
            halves,
            keys,
            keys,
            pltpu.VMEM((4, 128, TOTAL), BF16),
            quad,
            quad,
            pltpu.VMEM((24, 2, 128), F32),
            pltpu.VMEM((2, THIRD, 128), BF16),
            pltpu.VMEM((2, THIRD, 128), BF16),
            pltpu.VMEM((2, 128, THIRD), BF16),
            quad3,
            quad3,
            facts3,
            pair3,
            pair3,
            turned,
            quad3,
            quad3,
            facts3,
            pltpu.VMEM((3, 512, 512), BF16),
            pltpu.VMEM((3, 512, 512), BF16),
            pltpu.VMEM((3, 128, 256), F32),
            full,
            full,
            pltpu.VMEM((2, TOTAL, 128), F32),
            pltpu.VMEM((2, THIRD, 128), F32),
            pltpu.VMEM((2, THIRD, 128), F32),
            out3,
            out3,
            out3,
            out3,
            pltpu.VMEM((512, 256), F32),
            pltpu.VMEM((512, 256), F32),
            pltpu.VMEM((256, 256), F32),
            pltpu.VMEM((512, 256), F32),
            packs,
            packs,
            dma((HOMES + 1, 3)),
            dma((HOMES,)),
            dma((HEADS,)),
            dma((HOMES,)),
            dma((HEADS,)),
            dma((HOMES,)),
            dma((HOMES,)),
        ]
        + Reducer.scratch(N_FF, PIECE, True),
        compiler_params=params(collective_id=cid, has_side_effects=True),
    )(offs, drec, own, sib, ap, lse, G)


SEG1, SEG2, SEG3, SEG4, SEG5 = SEGMENTS
DILATION_ONE, DILATION_TWO, DILATION_THREE, DILATION_FOUR, DILATION_FIVE = DILATIONS
MASK_VALUE = -1e30
MATMUL_ACCURACY = lax.Precision.HIGHEST


def passed_along(value, axis, by):
    length = lax.axis_size(axis)
    return lax.ppermute(value, axis, [(i, (i + by) % length) for i in range(length)])


def run_is_live(distance, anchor_point, sequence_width, segment_length):
    return (anchor_point - (distance - 1) * sequence_width - 1) // segment_length == anchor_point // segment_length


def layer_norm(x, gain_vec):
    average = jnp.mean(x, -1, keepdims=True)
    centred = x - average
    variance = jnp.mean(centred * centred, -1, keepdims=True)
    return centred * lax.rsqrt(variance + LN_EPSILON) * gain_vec


def select_table(offsets_row, dilation_rate):
    return (jnp.arange(dilation_rate, dtype=jnp.int32)[:, None] == offsets_row[None, :]).astype(
        jnp.float32
    )


def spread_apart(x, select_option, dilation_rate):
    shaped = x.reshape(x.shape[0] // dilation_rate, dilation_rate, x.shape[1], x.shape[2])
    return jnp.einsum("trhd,rh->thd", shaped, select_option, precision=MATMUL_ACCURACY)


def spread_scalar_rows(x, select_option, dilation_rate):
    shaped = x.reshape(x.shape[0] // dilation_rate, dilation_rate, x.shape[1])
    return jnp.einsum("trh,rh->th", shaped, select_option, precision=MATMUL_ACCURACY)


def spread_rows(x, select_option):
    return jnp.einsum("thd,rh->trhd", x, select_option, precision=MATMUL_ACCURACY).reshape(
        -1, x.shape[1], x.shape[2]
    )


def spread_scalars(x, select_option):
    return jnp.einsum("th,rh->trh", x, select_option, precision=MATMUL_ACCURACY).reshape(
        -1, x.shape[1]
    )


def masked_score_matrix(sparse_queries, key_portion, query_position, key_position, segment_length):
    score_matrix = jnp.einsum(
        "ozt,bzt->zob", sparse_queries, key_portion, precision=MATMUL_ACCURACY
    ) * (1.0 / math.sqrt(key_portion.shape[-1]))
    q_cols = query_position.T[:, :, None]
    k_cols = key_position.T[:, None, :]
    permitted_mask = (k_cols <= q_cols) & (k_cols // segment_length == q_cols // segment_length)
    return (jnp.where(permitted_mask, score_matrix, MASK_VALUE), permitted_mask)


def prepare_pattern(
    query_sequence, key_sequence, value_sequence, offsets_row, dilation_rate, anchor_point
):
    select_option = select_table(offsets_row, dilation_rate)
    sparse_queries = spread_apart(query_sequence, select_option, dilation_rate)
    sparse_key_value = jnp.stack(
        (
            spread_apart(key_sequence, select_option, dilation_rate),
            spread_apart(value_sequence, select_option, dilation_rate),
        )
    )
    query_position = (
        anchor_point
        + jnp.arange(sparse_queries.shape[0], dtype=jnp.int32)[:, None] * dilation_rate
        + offsets_row[None, :]
    )
    return (select_option, sparse_queries, sparse_key_value, query_position)


def pattern_forward_pass(
    sparse_queries,
    sparse_key_value,
    query_position,
    reach,
    segment_length,
    anchor_point,
    sequence_width,
):
    masked_logits, permitted_mask = masked_score_matrix(
        sparse_queries, sparse_key_value[0], query_position, query_position, segment_length
    )
    row_max = jnp.max(masked_logits, -1)
    softmax_weights = jnp.where(permitted_mask, jnp.exp(masked_logits - row_max[..., None]), 0.0)
    state = (
        row_max,
        jnp.sum(softmax_weights, -1),
        jnp.einsum("tlj,jtb->tlb", softmax_weights, sparse_key_value[1], precision=MATMUL_ACCURACY),
    )

    def one_run(distance, carry):
        remote_key_value, state = carry
        remote_key_value = passed_along(remote_key_value, "seq", 1)
        key_position = query_position - distance * sequence_width

        def update(state_in):
            old_max, old_sum, old_acc = state_in
            masked_remote, permitted_remote = masked_score_matrix(
                sparse_queries, remote_key_value[0], query_position, key_position, segment_length
            )
            new_max = jnp.maximum(old_max, jnp.max(masked_remote, -1))
            weights_far = jnp.where(
                permitted_remote, jnp.exp(masked_remote - new_max[..., None]), 0.0
            )
            factor = jnp.exp(old_max - new_max)
            added = jnp.einsum(
                "tlj,jtb->tlb", weights_far, remote_key_value[1], precision=MATMUL_ACCURACY
            )
            return (
                new_max,
                old_sum * factor + jnp.sum(weights_far, -1),
                old_acc * factor[..., None] + added,
            )

        def unchanged(state_in):
            return state_in

        is_live = run_is_live(distance, anchor_point, sequence_width, segment_length)
        return remote_key_value, lax.cond(is_live, update, unchanged, state)

    state = lax.fori_loop(1, reach + 1, one_run, (sparse_key_value, state))[1]
    row_max, row_sum, accumulated = state
    mixture = jnp.transpose(accumulated / row_sum[..., None], (1, 0, 2))
    log_sum = (row_max + jnp.log(row_sum)).T
    return (mixture, log_sum)


def merge_patterns(forwards, prepared_inputs):
    full_lse = []
    full_mix = []
    for pattern_spec in range(len(forwards)):
        mixture, log_sum = forwards[pattern_spec]
        select_option = prepared_inputs[pattern_spec][0]
        covered = spread_scalars(jnp.ones_like(log_sum), select_option)
        full_lse.append(spread_scalars(log_sum, select_option) + (covered - 1.0) * 1e30)
        full_mix.append(spread_rows(mixture, select_option))
    stacked = jnp.stack(full_lse)
    row_max = jnp.max(stacked, 0)
    softmax_weights = jnp.exp(stacked - row_max)
    row_sum = jnp.sum(softmax_weights, 0)
    attended = full_mix[0] * softmax_weights[0][..., None]
    for pattern_spec in range(1, len(full_mix)):
        attended = attended + full_mix[pattern_spec] * softmax_weights[pattern_spec][..., None]
    return (attended / row_sum[..., None], row_max + jnp.log(row_sum))


def pattern_backward(
    select_option,
    dilation_rate,
    segment_length,
    anchor_point,
    sparse_queries,
    sparse_key_value,
    query_position,
    reach,
    sequence_gradient,
    row_difference,
    combined_logsumexp,
):
    sequence_width = sequence_gradient.shape[0]
    sparse_gradient = spread_apart(sequence_gradient, select_option, dilation_rate)
    sparse_output_grad = spread_scalar_rows(row_difference, select_option, dilation_rate).T
    sparse_logsumexp = spread_scalar_rows(combined_logsumexp, select_option, dilation_rate).T
    inverse_square_root = 1.0 / math.sqrt(sparse_queries.shape[-1])

    def portion_gradients(key_portion, value_portion, key_position):
        masked_logits, permitted_mask = masked_score_matrix(
            sparse_queries, key_portion, query_position, key_position, segment_length
        )
        softmax_weights = jnp.where(
            permitted_mask, jnp.exp(masked_logits - sparse_logsumexp[..., None]), 0.0
        )
        value_gradient = jnp.einsum(
            "tui,utx->itx", softmax_weights, sparse_gradient, precision=MATMUL_ACCURACY
        )
        pattern_gradient = jnp.einsum(
            "ozt,bzt->zob", sparse_gradient, value_portion, precision=MATMUL_ACCURACY
        )
        score_gradient = (
            softmax_weights
            * (pattern_gradient - sparse_output_grad[..., None])
            * inverse_square_root
        )
        query_gradient = jnp.einsum(
            "hqk,khd->qhd", score_gradient, key_portion, precision=MATMUL_ACCURACY
        )
        key_gradient = jnp.einsum(
            "tui,utx->itx", score_gradient, sparse_queries, precision=MATMUL_ACCURACY
        )
        return (query_gradient, jnp.stack((key_gradient, value_gradient)))

    query_gradient, key_value_gradient = portion_gradients(
        sparse_key_value[0], sparse_key_value[1], query_position
    )

    def one_run(distance, carry):
        remote_key_value, remote_gradient, query_sum = carry
        remote_key_value = passed_along(remote_key_value, "seq", 1)
        remote_gradient = passed_along(remote_gradient, "seq", 1)
        key_position = query_position - distance * sequence_width

        def far_grads():
            part_q, part_kv = portion_gradients(remote_key_value[0], remote_key_value[1], key_position)
            return query_sum + part_q, remote_gradient + part_kv

        def no_grads():
            return query_sum, remote_gradient

        is_live = run_is_live(distance, anchor_point, sequence_width, segment_length)
        query_sum, remote_gradient = lax.cond(is_live, far_grads, no_grads)
        return remote_key_value, remote_gradient, query_sum

    _, travelled, query_gradient = lax.fori_loop(
        1, reach + 1, one_run, (sparse_key_value, key_value_gradient, query_gradient)
    )
    return (query_gradient, passed_along(travelled, "seq", -reach))


def front_part(own_rows, w_qkv, gain_attn):
    return jnp.dot(layer_norm(own_rows, gain_attn), w_qkv, precision=MATMUL_ACCURACY)


def after_part(attn_rows, own_rows, w_out, w_up, w_down, gain_inner, gain_ffn, gain_hidden):
    residual = own_rows + jnp.dot(
        layer_norm(attn_rows, gain_inner), w_out, precision=MATMUL_ACCURACY
    )
    hidden = jax.nn.gelu(
        jnp.dot(layer_norm(residual, gain_ffn), w_up, precision=MATMUL_ACCURACY), approximate=False
    )
    return residual + jnp.dot(layer_norm(hidden, gain_hidden), w_down, precision=MATMUL_ACCURACY)


def shards(
    tokens,
    w_qkv,
    w_out,
    w_up,
    w_down,
    gain_attn,
    gain_inner,
    gain_ffn,
    gain_hidden,
    offsets,
    grad_out,
):
    w_qkv = w_qkv.astype(jnp.float32)
    w_out = w_out.astype(jnp.float32)
    w_up = w_up.astype(jnp.float32)
    w_down = w_down.astype(jnp.float32)
    groups = lax.axis_size("pat")
    local_rows = tokens.shape[0]
    sequence_width = local_rows * groups
    heads_here = HEADS // groups
    own_rows = tokens.reshape(local_rows, D)
    qkv_rows, front_back = jax.vjp(front_part, own_rows, w_qkv, gain_attn)
    gathered_qkv = lax.all_to_all(
        qkv_rows.reshape(local_rows, 1, 3, HEADS, HD),
        "pat",
        split_axis=3,
        concat_axis=1,
        tiled=True,
    )
    gathered_qkv = gathered_qkv.reshape(sequence_width, 3, heads_here, HD)
    head_offsets = lax.dynamic_slice_in_dim(
        offsets, lax.axis_index("pat") * heads_here, heads_here, 1
    )
    anchor_point = lax.axis_index("seq") * sequence_width
    dilation_rates = (DILATION_ONE, DILATION_TWO, DILATION_THREE, DILATION_FOUR, DILATION_FIVE)
    segment_lengths = (SEG1, SEG2, SEG3, SEG4, SEG5)
    reaches = [
        min((segment_lengths[pattern_spec] - 2) // sequence_width + 1, lax.axis_size("seq") - 1)
        for pattern_spec in range(PATTERNS)
    ]
    prepared_inputs = []
    for pattern_spec in range(PATTERNS):
        prepared_inputs.append(
            prepare_pattern(
                gathered_qkv[:, 0],
                gathered_qkv[:, 1],
                gathered_qkv[:, 2],
                head_offsets[pattern_spec],
                dilation_rates[pattern_spec],
                anchor_point,
            )
        )
    forwards = []
    for pattern_spec in range(PATTERNS):
        select_option, sparse_queries, sparse_key_value, query_position = prepared_inputs[
            pattern_spec
        ]
        forwards.append(
            pattern_forward_pass(
                sparse_queries,
                sparse_key_value,
                query_position,
                reaches[pattern_spec],
                segment_lengths[pattern_spec],
                anchor_point,
                sequence_width,
            )
        )
    lse_sums = jnp.stack([jnp.sum(entry[1]) for entry in forwards])
    totals = lax.psum(lse_sums, ("pat", "seq"))
    full_length = sequence_width * lax.axis_size("seq")
    counts = jnp.array(
        [
            float(full_length // dilation_rates[pattern_spec] * HEADS)
            for pattern_spec in range(PATTERNS)
        ],
        jnp.float32,
    )
    log_means = totals / counts
    attended, combined_logsumexp = merge_patterns(forwards, prepared_inputs)
    returned_rows = lax.all_to_all(
        attended.reshape(local_rows, groups, heads_here, HD),
        "pat",
        split_axis=1,
        concat_axis=2,
        tiled=True,
    )
    attn_rows = returned_rows.reshape(local_rows, D)
    result, after_back = jax.vjp(
        after_part, attn_rows, own_rows, w_out, w_up, w_down, gain_inner, gain_ffn, gain_hidden
    )
    g_attn, g_resid, g_out, g_up, g_down, g_inner, g_ffn, g_hidden = after_back(
        grad_out.reshape(local_rows, D)
    )
    sequence_gradient = lax.all_to_all(
        g_attn.reshape(local_rows, 1, HEADS, HD), "pat", split_axis=2, concat_axis=1, tiled=True
    )
    sequence_gradient = sequence_gradient.reshape(sequence_width, heads_here, HD)
    row_difference = jnp.sum(sequence_gradient * attended, -1)
    q_grads = []
    kv_grads = []
    for pattern_spec in range(PATTERNS):
        select_option, sparse_queries, sparse_key_value, query_position = prepared_inputs[
            pattern_spec
        ]
        part_q, part_kv = pattern_backward(
            select_option,
            dilation_rates[pattern_spec],
            segment_lengths[pattern_spec],
            anchor_point,
            sparse_queries,
            sparse_key_value,
            query_position,
            reaches[pattern_spec],
            sequence_gradient,
            row_difference,
            combined_logsumexp,
        )
        q_grads.append(part_q)
        kv_grads.append(part_kv)
    grad_total = jnp.zeros((sequence_width, 3, heads_here, HD), jnp.float32)
    for pattern_spec in range(PATTERNS):
        select_option = prepared_inputs[pattern_spec][0]
        grad_total = grad_total + jnp.stack(
            (
                spread_rows(q_grads[pattern_spec], select_option),
                spread_rows(kv_grads[pattern_spec][0], select_option),
                spread_rows(kv_grads[pattern_spec][1], select_option),
            ),
            1,
        )
    grad_back = lax.all_to_all(
        grad_total.reshape(local_rows, groups, 3, heads_here, HD),
        "pat",
        split_axis=1,
        concat_axis=3,
        tiled=True,
    )
    g_tokens, g_qkv, g_attn_gain = front_back(grad_back.reshape(local_rows, 3 * D))
    grad_tokens = (g_resid + g_tokens).reshape(local_rows, 1, D)
    summed = (
        lax.psum_scatter(g_qkv, ("pat", "seq"), scatter_dimension=0, tiled=True),
        lax.psum_scatter(g_out, ("pat", "seq"), scatter_dimension=0, tiled=True),
        lax.psum_scatter(g_up, ("pat", "seq"), scatter_dimension=0, tiled=True),
        lax.psum_scatter(g_down, ("pat", "seq"), scatter_dimension=0, tiled=True),
        lax.psum_scatter(g_attn_gain, ("pat", "seq"), scatter_dimension=0, tiled=True),
        lax.psum_scatter(g_inner, ("pat", "seq"), scatter_dimension=0, tiled=True),
        lax.psum_scatter(g_ffn, ("pat", "seq"), scatter_dimension=0, tiled=True),
        lax.psum_scatter(g_hidden, ("pat", "seq"), scatter_dimension=0, tiled=True),
    )
    return (
        result.reshape(local_rows, 1, D),
        grad_tokens,
        summed[0],
        summed[1],
        summed[2],
        summed[3],
        summed[4],
        summed[5],
        summed[6],
        summed[7],
        log_means,
    )


def fast_shards(tokens, w_qkv, w_out, w_up, w_down, gain_attn, gain_inner, gain_ffn, gain_hidden, offsets, grad_out):
    p, s = lax.axis_index("pat"), lax.axis_index("seq")
    active, head = head_here(p, s)
    mine = lax.dynamic_slice_in_dim(offsets, head, 1, 1)[:, 0]
    info = jnp.concatenate([jnp.stack([active.astype(jnp.int32), lax.rem(p, 2).astype(jnp.int32)]), mine])

    counts = [float(TOTAL * 4 // r * HEADS) for r in DILATIONS]
    pk, x = front(tokens, w_qkv, gain_attn)
    own, sib = to_heads(pk, True, 0)
    ap, lse, sums = attention_forward(info, own, sib)
    rec = to_homes(ap, 1)
    mixed, drec, dy1, S, G = feed_forward(
        rec, x, grad_out, w_out, w_up, w_down, gain_inner, gain_ffn, gain_hidden, sums
    )
    grec, g_out, g_up, g_down = backward_all(mine, drec, own, sib, ap, lse, G, 2)
    gx, g_qkv, *small = finish(grec, x, dy1, w_qkv, gain_attn, S, counts, 3)
    mixed, gx, g_qkv, g_out, g_up, g_down, *small = deliver(mixed, gx, g_qkv, g_out, g_up, g_down, *small)
    return (mixed, gx, g_qkv, g_out, g_up, g_down, *(v.reshape(-1) for v in small))


def fits(mesh):
    return mesh.shape["pat"] == 4 and mesh.shape["seq"] == RUNS


def solution(mesh):
    rows = P("seq", "pat", None)
    split_rows = P(("pat", "seq"), None)
    split_one = P(("pat", "seq"))
    planned = jax.shard_map(
        fast_shards,
        mesh=mesh,
        in_specs=(rows,) + (P(),) * 9 + (rows,),
        out_specs=(rows, rows) + (split_rows,) * 4 + (split_one,) * 4 + (P(),),
        check_vma=False,
    )
    general = jax.shard_map(
        shards,
        mesh=mesh,
        in_specs=(rows,) + (P(),) * 9 + (rows,),
        out_specs=(rows, rows) + (split_rows,) * 4 + (split_one,) * 4 + (P(),),
        check_vma=False,
    )

    def layer(tokens, *rest):
        if fits(mesh) and tokens.shape[0] == TOTAL:
            return planned(tokens, *rest)
        return general(tokens, *rest)

    return layer
```

```python
import functools
import math

import jax
import jax.numpy as jnp
from jax import lax
from jax.experimental import pallas as pl
from jax.experimental.pallas import tpu as pltpu
from jax.sharding import PartitionSpec as P

D = 768
HEADS = 12
HD = 64
FF = 3072
PATTERNS = 5
SEGMENTS = (2048, 4096, 8192, 16384, 32768)
DILATIONS = (1, 2, 4, 6, 12)
LN_EPSILON = 1e-05
NEG = -1e30
F32 = jnp.float32
BF16 = jnp.bfloat16
HIGHEST = lax.Precision.HIGHEST
VMEM_LIMIT = 60 * 1024 * 1024

ROWS = 192
HALF = ROWS // 2
RUNS = 8
TOTAL = ROWS * RUNS
PACK = ROWS + HALF
HOMES = 16
THIRD = TOTAL // 3
MESH = pl.DeviceIdType.MESH


def dot_nn(a, b):
    return lax.dot_general(a, b, (((1,), (0,)), ((), ())), preferred_element_type=F32)


def dot_nt(a, b):
    return lax.dot_general(a, b, (((1,), (1,)), ((), ())), preferred_element_type=F32)


def split(v):
    hi = v.astype(BF16)
    return hi, (v - hi.astype(F32)).astype(BF16)


def split32(v):
    hi = v.astype(BF16).astype(F32)
    return hi, v - hi


def lower_lanes(v):
    return lax.broadcasted_iota(jnp.int32, v.shape, v.ndim - 1) < HD


def swap(v):
    return pltpu.roll(v, HD, v.ndim - 1)


def pick(a, b):
    return jnp.where(lower_lanes(a), a, b)


def head_place(h):
    z = h // 3
    column = lax.rem(lax.rem(h, 3) + z + 1, 4)
    return column // 2, z * 2 + lax.rem(column, 2)


def head_here(p, s):
    z = s // 2
    column = (p // 2) * 2 + lax.rem(s, 2)
    k = lax.rem(column - z + 7, 4)
    return k < 3, z * 3 + jnp.minimum(k, 2)


def whole(*_):
    return pl.BlockSpec(memory_space=pltpu.VMEM)


VM = pl.BlockSpec(memory_space=pltpu.VMEM)
ANY = pl.BlockSpec(memory_space=pl.ANY)
SM = pl.BlockSpec(memory_space=pltpu.SMEM)


def params(**kw):
    return pltpu.CompilerParams(vmem_limit_bytes=VMEM_LIMIT, **kw)


def normed(v):
    centred = v - jnp.mean(v, -1, keepdims=True)
    rs = lax.rsqrt(jnp.mean(centred * centred, -1, keepdims=True) + LN_EPSILON)
    return centred * rs, rs


def put_split(ref, v):
    hi, lo = split(v)
    n = v.shape[0]
    ref[0:n, :] = hi
    ref[n : 2 * n, :] = lo


def front_kernel(x3, w_ref, gain_ref, pk_ref, x_ref, lhs):
    x = x3[...].reshape(ROWS, D)
    x_ref[...] = x
    n, _ = normed(x)
    put_split(lhs, n * gain_ref[...][None, :])
    for jj in range(3):
        parts = []
        for kind in range(3):
            c0 = kind * D + 256 * jj
            r = dot_nn(lhs[...], w_ref[:, c0 : c0 + 256])
            parts.append(r[:ROWS] + r[ROWS:])
        for half in range(2):
            q, k, v = (a[:, 128 * half : 128 * half + 128] for a in parts)
            h = 4 * jj + 2 * half
            pk_ref[h, 0:ROWS, :] = pick(k, swap(v))
            pk_ref[h + 1, 0:ROWS, :] = pick(swap(k), v)
            top, bottom = q[:HALF], q[HALF:]
            pk_ref[h, ROWS:PACK, :] = pick(top, swap(bottom))
            pk_ref[h + 1, ROWS:PACK, :] = pick(swap(top), bottom)


def front(x, w, gain):
    return pl.pallas_call(
        front_kernel,
        out_shape=[jax.ShapeDtypeStruct((HEADS, PACK, 128), F32)] + [jax.ShapeDtypeStruct((ROWS, D), F32)],
        in_specs=[VM] * 3,
        out_specs=[VM] * 2,
        scratch_shapes=[pltpu.VMEM((2 * ROWS, D), BF16)],
        compiler_params=params(),
    )(x, w, gain)


def place_facts():
    p, s = lax.axis_index("pat"), lax.axis_index("seq")
    x, core = p // 2, lax.rem(p, 2)
    active, head = head_here(p, s)
    return p, s, x, core, active, head


def home_device(core, m):
    return core * 2 + lax.rem(m, 2), m // 2


def head_device(h, b):
    hx, hs = head_place(h)
    return hx * 2 + b, hs


def same(p, s, q, t):
    return jnp.logical_and(p == q, s == t)


def to(p, s):
    return {"pat": p, "seq": s}


def scatter_kernel(forward, pk, own, *rest):
    if forward:
        sib, send, recv, fsend, frecv = rest
    else:
        send, recv = rest
    p, s, x, core, active, head = place_facts()
    slot = s * 2 + core
    barrier = pltpu.get_barrier_semaphore()

    @pl.when(active)
    def _():
        def greet(m, carry):
            q, t = home_device(core, m)

            @pl.when(jnp.logical_not(same(p, s, q, t)))
            def _():
                pl.semaphore_signal(barrier, inc=1, device_id=to(q, t), device_id_type=MESH)

            return carry

        lax.fori_loop(0, HOMES, greet, 0)
        if forward:
            pl.semaphore_signal(barrier, inc=1, device_id=to(x * 2 + 1 - core, s), device_id_type=MESH)

    mine = jnp.logical_and(active, core == x)
    waits = HEADS - mine.astype(jnp.int32)
    if forward:
        waits = waits + active.astype(jnp.int32)
    pl.semaphore_wait(barrier, waits)

    def copy(h):
        q, t = head_device(h, x)
        return q, t, pltpu.make_async_remote_copy(
            src_ref=pk.at[h],
            dst_ref=own.at[slot],
            send_sem=send.at[h],
            recv_sem=recv.at[slot],
            device_id=to(q, t),
            device_id_type=MESH,
        )

    def start(j, carry):
        h = lax.rem(j + 3 * (s // 2) + 2 * p, HEADS)
        q, t, remote = copy(h)

        @pl.when(same(p, s, q, t))
        def _():
            pltpu.make_async_copy(pk.at[h], own.at[slot], recv.at[slot]).start()

        @pl.when(jnp.logical_not(same(p, s, q, t)))
        def _():
            remote.start()

        return carry

    lax.fori_loop(0, HEADS, start, 0)

    def passed(m):
        return pltpu.make_async_remote_copy(
            src_ref=own.at[m, pl.ds(0, ROWS), :],
            dst_ref=sib.at[m],
            send_sem=fsend.at[m],
            recv_sem=frecv.at[m],
            device_id=to(x * 2 + 1 - core, s),
            device_id_type=MESH,
        )

    @pl.when(active)
    def _():
        def arrive(m, carry):
            pltpu.make_async_copy(own.at[m], own.at[m], recv.at[m]).wait()
            if forward:
                passed(m).start()
            return carry

        lax.fori_loop(0, HOMES, arrive, 0)
        if forward:

            def finish(m, carry):
                passed(m).wait()
                return carry

            lax.fori_loop(0, HOMES, finish, 0)

    def sent(h, carry):
        q, t, remote = copy(h)

        @pl.when(jnp.logical_not(same(p, s, q, t)))
        def _():
            remote.wait_send()

        return carry

    lax.fori_loop(0, HEADS, sent, 0)


def to_heads(packets, forward, cid):
    rows = packets.shape[1]
    shapes = [jax.ShapeDtypeStruct((HOMES, rows, 128), F32)]
    sems = [pltpu.SemaphoreType.DMA((HEADS,)), pltpu.SemaphoreType.DMA((HOMES,))]
    if forward:
        shapes.append(jax.ShapeDtypeStruct((HOMES, ROWS, 128), F32))
        sems += [pltpu.SemaphoreType.DMA((HOMES,)), pltpu.SemaphoreType.DMA((HOMES,))]
    return pl.pallas_call(
        functools.partial(scatter_kernel, forward),
        out_shape=shapes,
        in_specs=[ANY],
        out_specs=[ANY] * len(shapes),
        scratch_shapes=sems,
        compiler_params=params(collective_id=cid, has_side_effects=True),
    )(packets)


def home_barrier(p, s, x, core, active, barrier, also_sibling):
    def greet(h, carry):
        q, t = head_device(h, x)

        @pl.when(jnp.logical_not(same(p, s, q, t)))
        def _():
            pl.semaphore_signal(barrier, inc=1, device_id=to(q, t), device_id_type=MESH)

        return carry

    lax.fori_loop(0, HEADS, greet, 0)

    @pl.when(active)
    def _():
        if also_sibling:
            pl.semaphore_signal(barrier, inc=1, device_id=to(x * 2 + 1 - core, s), device_id_type=MESH)
        mine = (core == x).astype(jnp.int32)
        pl.semaphore_wait(barrier, HOMES - mine + (1 if also_sibling else 0))


def gather_kernel(pk, rec, send, recv):
    p, s, x, core, active, head = place_facts()
    barrier = pltpu.get_barrier_semaphore()
    home_barrier(p, s, x, core, active, barrier, False)

    def copy(m):
        q, t = home_device(core, m)
        return q, t, pltpu.make_async_remote_copy(
            src_ref=pk.at[m],
            dst_ref=rec.at[head],
            send_sem=send.at[m],
            recv_sem=recv.at[head],
            device_id=to(q, t),
            device_id_type=MESH,
        )

    @pl.when(active)
    def _():
        def start(j, carry):
            m = lax.rem(j + 2 * s + 1, HOMES)
            q, t, remote = copy(m)

            @pl.when(same(p, s, q, t))
            def _():
                pltpu.make_async_copy(pk.at[m], rec.at[head], recv.at[head]).start()

            @pl.when(jnp.logical_not(same(p, s, q, t)))
            def _():
                remote.start()

            return carry

        lax.fori_loop(0, HOMES, start, 0)

    def arrive(h, carry):
        pltpu.make_async_copy(rec.at[h], rec.at[h], recv.at[h]).wait()
        return carry

    lax.fori_loop(0, HEADS, arrive, 0)

    @pl.when(active)
    def _():
        def sent(m, carry):
            q, t, remote = copy(m)

            @pl.when(jnp.logical_not(same(p, s, q, t)))
            def _():
                remote.wait_send()

            return carry

        lax.fori_loop(0, HOMES, sent, 0)


def to_homes(packets, cid):
    rows = packets.shape[1]
    return pl.pallas_call(
        gather_kernel,
        out_shape=jax.ShapeDtypeStruct((HEADS, rows, 128), F32),
        in_specs=[ANY],
        out_specs=ANY,
        scratch_shapes=[pltpu.SemaphoreType.DMA((HOMES,)), pltpu.SemaphoreType.DMA((HEADS,))],
        compiler_params=params(collective_id=cid, has_side_effects=True),
    )(packets)


def tile_positions(rows, columns, row_classes, column_classes, t_step, class_step):
    r = lax.broadcasted_iota(jnp.int32, (rows, columns), 0)
    q = lax.broadcasted_iota(jnp.int32, (rows, columns), 1)
    rn, qn = rows // row_classes, columns // column_classes
    return (r % rn) * t_step + (r // rn) * class_step, (q % qn) * t_step + (q // qn) * class_step


def key_bias(q_shape, k_shape, t_step, class_step, shift, keys_first):
    nq, nk = q_shape[0] * q_shape[1], k_shape[0] * k_shape[1]
    if keys_first:
        kp, qp = tile_positions(nk, nq, k_shape[0], q_shape[0], t_step, class_step)
    else:
        qp, kp = tile_positions(nq, nk, q_shape[0], k_shape[0], t_step, class_step)
    return jnp.where(kp - qp <= shift, 0.0, NEG).astype(F32)


def unpack_keys(own, sib, b, kvf):
    def one(m, carry):
        c = 2 * b + lax.rem(m, 2)
        d = 2 * (1 - b) + lax.rem(m, 2)
        t = pl.multiple_of((m // 2) * ROWS, 64)
        kvf[c, pl.ds(t, ROWS), :] = own[m, 0:ROWS, :]
        kvf[d, pl.ds(t, ROWS), :] = sib[m]
        return carry

    lax.fori_loop(0, HOMES, one, 0)


def unpack_pairs(src, first, dst, scale):
    def one(m, carry):
        t = pl.multiple_of((m // 2) * ROWS, 32)
        v = src[m, first : first + HALF, :] * scale
        w = swap(v)
        dst[lax.rem(m, 2), pl.ds(t, HALF), :] = pick(v, w)
        dst[lax.rem(m, 2), pl.ds(t + HALF, HALF), :] = pick(w, v)
        return carry

    lax.fori_loop(0, HOMES, one, 0)


def keys_and_values(kv):
    hi, lo = split32(kv)
    k2 = pick(hi, swap(lo))
    v2 = pick(swap(hi), lo)
    return k2, v2


def doubled(v):
    return jnp.concatenate([v, v], 1)


def query_quads(qq):
    hi, lo = split32(qq)
    return jnp.concatenate([pick(hi, lo).astype(BF16), pick(lo, hi).astype(BF16)], 1)


def class_facts4(o4, b):
    keys = ((lax.rem(o4, 4), o4 // 4), (lax.rem(o4 + 6, 4), (o4 + 6) // 4))
    first = (keys[0][0] // 2) == b
    query = (jnp.where(first, keys[0][0], keys[1][0]), jnp.where(first, keys[0][1], keys[1][1]))
    return keys, jnp.where(first, 0, 1), query


def forward_kernel(info, own, sib, ap, lse, sums, kvf, kc, vt, qf, qc, k4, vt4, q4, k5, vt5, q5, acc, ml, R, b1, b2, b3, b4):
    active = info[0] == 1
    b = info[1]
    offs = [info[2 + i] for i in range(PATTERNS)]
    sums[...] = jnp.zeros_like(sums)

    @pl.when(active)
    def _():
        unpack_keys(own, sib, b, kvf)
        unpack_pairs(own, ROWS, qf, 1.0 / math.sqrt(HD))

        def prepare(i, carry):
            c, t = i // 12, pl.multiple_of(lax.rem(i, 12) * 128, 128)
            k2, v2 = keys_and_values(kvf[c, pl.ds(t, 128), :])
            kc[c, pl.ds(t, 128), :] = k2.astype(BF16)
            vt[c, :, pl.ds(t, 128)] = v2.T.astype(BF16)
            return carry

        lax.fori_loop(0, 48, prepare, 0, unroll=2)

        def prepare_q(i, carry):
            c, t = i // 12, pl.multiple_of(lax.rem(i, 12) * 128, 128)
            qc[c, pl.ds(t, 128), :] = query_quads(qf[c, pl.ds(t, 128), :])
            return carry

        lax.fori_loop(0, 24, prepare_q, 0, unroll=2)

        keys4, e4, (qc4, qv4) = class_facts4(offs[3], b)
        kc5, kv5 = lax.rem(offs[4], 4), offs[4] // 4
        for blk in range(4):
            r = slice(128 * blk, 128 * blk + 128)
            for e in range(2):
                c, v = keys4[e]
                k2, v2 = keys_and_values(kvf[c, pl.ds(v + 384 * blk, 128, stride=3), :])
                k4[e, r, :] = k2.astype(BF16)
                vt4[e, :, r] = v2.T.astype(BF16)
            q4[r, :] = query_quads(qf[qc4 - 2 * b, pl.ds(qv4 + 384 * blk, 128, stride=3), :])
            k2, v2 = keys_and_values(kvf[kc5, pl.ds(kv5 + 384 * blk, 128, stride=3), :])
            k5[r, :] = k2.astype(BF16)
            vt5[:, r] = v2.T.astype(BF16)
            q5[r, :] = query_quads(qf[lax.rem(kc5, 2), pl.ds(kv5 + 384 * blk, 128, stride=3), :])

        b1[...] = key_bias((2, 128), (4, 128), 4, 1, 2 * b, True)
        b2[...] = key_bias((1, 256), (2, 256), 4, 2, 2 * b, True)
        b3[...] = key_bias((1, 256), (1, 256), 1, 1, 0, True)
        b4[...] = key_bias((1, 256), (2, 256), 12, 6, 6 * e4, True)

        def tile(g, q, k, vT, bias, first):
            s = dot_nt(doubled(k), q)
            if bias is not None:
                s = s + bias[...]
            m = jnp.max(s, 0, keepdims=True)
            if not first:
                old = ml[g, 0:1, :]
                m = jnp.maximum(old, m)
            p = jnp.exp(s - m)
            total = jnp.sum(p, 0, keepdims=True)
            hi, lo = split(p)
            new = dot_nn(doubled(vT), jnp.concatenate([hi, lo], 0))
            if first:
                acc[g] = new
            else:
                alpha = jnp.exp(old - m)
                acc[g] = acc[g] * alpha + new
                total = ml[g, 1:2, :] * alpha + total
            ml[g, 0:1, :] = m
            ml[g, 1:2, :] = total

        def closed(pattern, g):
            m, l = ml[g, 0:1, :], ml[g, 1:2, :]
            rows = m + jnp.log(l)
            sums[pattern : pattern + 1, :] += rows[:, :128] + rows[:, 128:]
            o = acc[g]
            return jnp.concatenate(
                [o[:HD] + o[HD:], jnp.broadcast_to(l, (32, 256)), jnp.broadcast_to(m, (32, 256))], 0
            ).T

        def q1(qb, carry):
            def at(g, blk):
                return pl.ds(pl.multiple_of(512 * g + 128 * blk, 128), 128)

            def step(kb, bias, first):
                for g in range(3):
                    ks = at(g, kb)
                    vT = jnp.concatenate([vt[c, :, ks] for c in range(4)], 1)
                    tile(g, qc[:, at(g, qb), :].reshape(256, 256), kc[:, ks, :].reshape(512, 128), vT, bias, first)

            step(qb, b1, True)

            def more(kb, inner):
                step(kb, None, False)
                return inner

            lax.fori_loop(0, qb, more, 0)
            for g in range(3):
                R[:, at(g, qb), :] = closed(0, g).reshape(2, 128, 128)
            return carry

        lax.fori_loop(0, 4, q1, 0)

        def merge(pattern, g, ci, rows):
            r0, r1 = R[ci, rows, :], closed(pattern, g)
            m0 = jnp.broadcast_to(r0[:, 96:97], r0.shape)
            m1 = jnp.broadcast_to(r1[:, 96:97], r1.shape)
            m = jnp.maximum(m0, m1)
            both = r0 * jnp.exp(m0 - m) + r1 * jnp.exp(m1 - m)
            lane = lax.broadcasted_iota(jnp.int32, r0.shape, 1)
            R[ci, rows, :] = jnp.where(lane < 96, both, m)

        def at256(blk):
            return pl.ds(pl.multiple_of(256 * blk, 128), 256)

        par = offs[1]

        def step2(g, q, kb, bias, first):
            ks = at256(kb)
            k = jnp.concatenate([kc[par, ks, :], kc[par + 2, ks, :]], 0)
            vT = jnp.concatenate([vt[par, :, ks], vt[par + 2, :, ks]], 1)
            tile(g, q, k, vT, bias, first)

        def q2(qb, carry):
            q = qc[par, at256(qb), :]
            step2(0, q, qb, b2, True)

            def more(kb, inner):
                step2(0, q, kb, None, False)
                return inner

            lax.fori_loop(jnp.where(qb >= 4, 4, 0), qb, more, 0)
            merge(1, 0, par, at256(qb))
            return carry

        lax.fori_loop(0, TOTAL // 256, q2, 0)

        o3 = offs[2]

        @pl.when(o3 // 2 == b)
        def _():
            ci = lax.rem(o3, 2)

            def step3(g, qb, kb, bias, first):
                tile(g, qc[ci, at256(qb), :], kc[o3, at256(kb), :], vt[o3, :, at256(kb)], bias, first)

            def q3(pair, carry):
                q0, q1_ = 2 * pair, 2 * pair + 1
                step3(0, q0, q0, b3, True)
                step3(1, q1_, q1_, b3, True)

                def more(kb, inner):
                    step3(0, q0, kb, None, False)
                    step3(1, q1_, kb, None, False)
                    return inner

                lax.fori_loop(0, q0, more, 0)
                step3(1, q1_, q0, None, False)
                merge(2, 0, ci, at256(q0))
                merge(2, 1, ci, at256(q1_))
                return carry

            lax.fori_loop(0, TOTAL // 512, q3, 0)

        for kb in range(2):
            for qb in range(kb, 2):
                order = qb - kb
                ks = slice(256 * order, 256 * order + 256)
                tile(
                    qb,
                    q4[256 * qb : 256 * qb + 256, :],
                    k4[:, ks, :].reshape(512, 128),
                    jnp.concatenate([vt4[0, :, ks], vt4[1, :, ks]], 1),
                    b4 if order == qb else None,
                    kb == 0,
                )
        for qb in range(2):
            merge(3, qb, qc4 - 2 * b, pl.ds(qv4 + 768 * qb, 256, stride=3))

        @pl.when(kc5 // 2 == b)
        def _():
            for kb in range(2):
                for qb in range(kb, 2):
                    order = qb - kb
                    ks = slice(256 * order, 256 * order + 256)
                    tile(
                        qb,
                        q5[256 * qb : 256 * qb + 256, :],
                        k5[ks, :],
                        vt5[:, ks],
                        b3 if order == qb else None,
                        kb == 0,
                    )
            for qb in range(2):
                merge(4, qb, lax.rem(kc5, 2), pl.ds(kv5 + 768 * qb, 256, stride=3))

        def finish(m, carry):
            ci = lax.rem(m, 2)
            rows = pl.ds(pl.multiple_of((m // 2) * ROWS, 64), ROWS)
            r = R[ci, rows, :]
            l = jnp.broadcast_to(r[:, HD : HD + 1], r.shape)
            out = r / l
            ap[m] = pick(out[:HALF], swap(out[HALF:]))
            lse[ci, rows, :] = jnp.broadcast_to(r[:, 96:97], r.shape) + jnp.log(l)
            return carry

        lax.fori_loop(0, HOMES, finish, 0, unroll=2)
        sums[...] = jnp.broadcast_to(jnp.sum(sums[...], -1, keepdims=True), (8, 128))


def attention_forward(info, own, sib):
    keys = pltpu.VMEM((4, TOTAL, 128), BF16)
    turned = pltpu.VMEM((4, 128, TOTAL), BF16)
    state = pltpu.VMEM((2, TOTAL, 128), F32)
    return pl.pallas_call(
        forward_kernel,
        out_shape=[
            jax.ShapeDtypeStruct((HOMES, HALF, 128), F32),
            jax.ShapeDtypeStruct((2, TOTAL, 128), F32),
            jax.ShapeDtypeStruct((8, 128), F32),
        ],
        in_specs=[SM, VM, VM],
        out_specs=[VM, VM, VM],
        scratch_shapes=[
            pltpu.VMEM((4, TOTAL, 128), F32),
            keys,
            turned,
            state,
            pltpu.VMEM((2, TOTAL, 256), BF16),
            pltpu.VMEM((2, THIRD, 128), BF16),
            pltpu.VMEM((2, 128, THIRD), BF16),
            pltpu.VMEM((THIRD, 256), BF16),
            pltpu.VMEM((THIRD, 128), BF16),
            pltpu.VMEM((128, THIRD), BF16),
            pltpu.VMEM((THIRD, 256), BF16),
            pltpu.VMEM((3, 128, 256), F32),
            pltpu.VMEM((3, 8, 256), F32),
            state,
            pltpu.VMEM((512, 256), F32),
            pltpu.VMEM((512, 256), F32),
            pltpu.VMEM((256, 256), F32),
            pltpu.VMEM((512, 256), F32),
        ],
        compiler_params=params(),
    )(info, own, sib)


def rows_from_pairs(rec, dst):
    for j in range(HEADS // 2):
        u, v = rec[2 * j], rec[2 * j + 1]
        cols = slice(128 * j, 128 * j + 128)
        dst[0:HALF, cols] = pick(u, swap(v))
        dst[HALF:ROWS, cols] = pick(swap(u), v)


def pairs_from_rows(src, dst):
    for j in range(HEADS // 2):
        top = src[0:HALF, 128 * j : 128 * j + 128]
        bottom = src[HALF:ROWS, 128 * j : 128 * j + 128]
        dst[2 * j] = pick(top, swap(bottom))
        dst[2 * j + 1] = pick(swap(top), bottom)


def halves_sum(r):
    return r[:ROWS] + r[ROWS:]


def norm_back(f, n, rs):
    return (f - jnp.mean(f, -1, keepdims=True) - n * jnp.mean(f * n, -1, keepdims=True)) * rs


def put_turned(hi_ref, lo_ref, v):
    for j in range(D // 128):
        t = v[:, 128 * j : 128 * j + 128].T
        hi, lo = split(t)
        hi_ref[128 * j : 128 * j + 128, :] = hi
        lo_ref[128 * j : 128 * j + 128, :] = lo


class ToHeads:
    def __init__(self, pk, rec, send, recv):
        self.pk, self.rec, self.send, self.recv = pk, rec, send, recv
        self.facts = place_facts()

    def greet(self):
        p, s, x, core, active, head = self.facts
        barrier = pltpu.get_barrier_semaphore()

        @pl.when(active)
        def _():
            def one(m, carry):
                q, t = home_device(core, m)

                @pl.when(jnp.logical_not(same(p, s, q, t)))
                def _():
                    pl.semaphore_signal(barrier, inc=1, device_id=to(q, t), device_id_type=MESH)

                return carry

            lax.fori_loop(0, HOMES, one, 0)

    def copy(self, h):
        p, s, x, core, active, head = self.facts
        slot = s * 2 + core
        q, t = head_device(h, x)
        far = pltpu.make_async_remote_copy(
            src_ref=self.pk.at[h],
            dst_ref=self.rec.at[slot],
            send_sem=self.send.at[h],
            recv_sem=self.recv.at[slot],
            device_id=to(q, t),
            device_id_type=MESH,
        )
        return same(p, s, q, t), lambda: pltpu.make_async_copy(self.pk.at[h], self.rec.at[slot], self.recv.at[slot]), far

    def start(self):
        p, s, x, core, active, head = self.facts
        mine = jnp.logical_and(active, core == x).astype(jnp.int32)
        pl.semaphore_wait(pltpu.get_barrier_semaphore(), HEADS - mine)

        def one(j, carry):
            here, near, far = self.copy(lax.rem(j + 3 * (s // 2) + 2 * p, HEADS))

            @pl.when(here)
            def _():
                near().start()

            @pl.when(jnp.logical_not(here))
            def _():
                far.start()

            return carry

        lax.fori_loop(0, HEADS, one, 0)

    def finish(self):
        active = self.facts[4]

        @pl.when(active)
        def _():
            def arrive(m, carry):
                pltpu.make_async_copy(self.rec.at[m], self.rec.at[m], self.recv.at[m]).wait()
                return carry

            lax.fori_loop(0, HOMES, arrive, 0)

        def sent(h, carry):
            here, near, far = self.copy(h)

            @pl.when(jnp.logical_not(here))
            def _():
                far.wait_send()

            return carry

        lax.fori_loop(0, HEADS, sent, 0)


FT = 512


class Spill:
    def __init__(self, tiles, sem):
        self.tiles, self.sem, self.count, self.open = tiles, sem, 0, [[], []]

    def emit(self, fill, copies):
        k = self.count % 2
        for c in self.open[k]:
            c.wait()
        fill(self.tiles.at[k])
        self.open[k] = copies(self.tiles.at[k], self.sem.at[k])
        for c in self.open[k]:
            c.start()
        self.count += 1

    def close(self):
        for k in range(2):
            for c in self.open[k]:
                c.wait()
            self.open[k] = []


def product(hi, lo, r_hi, r_lo, tile):
    def one(i, carry):
        rows = pl.ds(pl.multiple_of(i * 128, 128), 128)
        h, l = hi[rows, :], lo[rows, :]
        tile[rows, :] = dot_nn(h, r_hi[...]) + dot_nn(h, r_lo[...]) + dot_nn(l, r_hi[...])
        return carry

    lax.fori_loop(0, D // 128, one, 0)


def column_copies(G, chunk):
    def make(tile, sem):
        return [
            pltpu.make_async_copy(
                tile.at[pl.ds(24 * d, 24), :], G.at[d // 16, (d // 8) % 2, (d % 8) // 2, d % 2, chunk], sem.at[d]
            )
            for d in range(32)
        ]

    return make


def row_copies(G, part, chunk):
    def make(tile, sem):
        return [
            pltpu.make_async_copy(
                tile.at[pl.ds(24 * d, 24), :], G.at[part // 2, part % 2, d // 8, (d // 4) % 2, chunk + d % 4], sem.at[d]
            )
            for d in range(32)
        ]

    return make


def ff_kernel(rec, x_ref, g3, wo, wu, wd, gi1, gf1, gh1, sums, out3, drec, dy1_ref, S, G, dap, lhs, lhs2, gi, gf, gh, gh_g, g_ref, out_ref, V, N1, U, GP, E, ACC, th, tl, r_hi, r_lo, tiles, sem, dsend, drecv):
    spill = Spill(tiles, sem)
    travel = ToHeads(dap, drec, dsend, drecv)
    travel.greet()
    for wide, flat in ((gi, gi1), (gf, gf1), (gh, gh1)):
        wide[...] = flat[...][None, :]
    g_ref[...] = g3[...].reshape(ROWS, D)
    rows_from_pairs(rec, V)
    na, rs_a = normed(V[...])
    V[...] = na
    put_split(lhs, na * gi[...])
    for j in range(3):
        cols = slice(256 * j, 256 * j + 256)
        N1[:, cols] = x_ref[:, cols] + halves_sum(dot_nn(lhs[...], wo[:, cols]))
    y1 = N1[...]
    out_ref[...] = y1
    ny, rs_y = normed(y1)
    N1[...] = ny
    put_split(lhs, ny * gf[...])

    def up(j, su):
        cols = pl.ds(pl.multiple_of(j * FT, FT), FT)
        z = halves_sum(dot_nn(lhs[...], wu[:, cols]))
        phi = 0.5 * (1.0 + lax.erf(z * math.sqrt(0.5)))
        u = z * phi
        U[:, cols] = u
        GP[:, cols] = phi + z * jnp.exp(-0.5 * z * z) * (1.0 / math.sqrt(2.0 * math.pi))
        return su + jnp.sum(u, -1, keepdims=True)

    zero = jnp.zeros((ROWS, 1), F32)
    mean = lax.fori_loop(0, FF // FT, up, zero) * (1.0 / FF)

    def spread(j, sv):
        cols = pl.ds(pl.multiple_of(j * FT, FT), FT)
        c = U[:, cols] - mean
        return sv + jnp.sum(c * c, -1, keepdims=True)

    rs_u = lax.rsqrt(lax.fori_loop(0, FF // FT, spread, zero) * (1.0 / FF) + LN_EPSILON)
    ACC[...] = jnp.zeros_like(ACC)

    def lower(j, carry):
        cols = pl.ds(pl.multiple_of(j * FT, FT), FT)
        n = (U[:, cols] - mean) * rs_u
        U[:, cols] = n
        put_split(lhs2, n * gh[:, cols])
        ACC[...] += halves_sum(dot_nn(lhs2[...], wd[cols, :]))
        return carry

    lax.fori_loop(0, FF // FT, lower, 0)
    out3[...] = (out_ref[...] + ACC[...]).reshape(ROWS, 1, D)

    put_split(lhs, g_ref[...])

    def back_down(j, sums):
        cols = pl.ds(pl.multiple_of(j * FT, FT), FT)
        e = halves_sum(dot_nt(lhs[...], wd[cols, :]))
        n = U[:, cols]
        gh_g[:, cols] = jnp.sum(e * n, 0, keepdims=True)
        f = e * gh[:, cols]
        E[:, cols] = f
        return sums[0] + jnp.sum(f, -1, keepdims=True), sums[1] + jnp.sum(f * n, -1, keepdims=True)

    sf, sfn = lax.fori_loop(0, FF // FT, back_down, (zero, zero))
    mf, mfn = sf * (1.0 / FF), sfn * (1.0 / FF)
    ACC[...] = jnp.zeros_like(ACC)

    def back_up(j, carry):
        cols = pl.ds(pl.multiple_of(j * FT, FT), FT)
        dz = (E[:, cols] - mf - U[:, cols] * mfn) * rs_u * GP[:, cols]
        E[:, cols] = dz
        put_split(lhs2, dz)
        ACC[...] += halves_sum(dot_nt(lhs2[...], wu[:, cols]))
        return carry

    lax.fori_loop(0, FF // FT, back_up, 0)
    e = ACC[...]
    ny = N1[...]
    S[2:3, :] = jnp.sum(e * ny, 0, keepdims=True)
    dy1 = g_ref[...] + norm_back(e * gf[...], ny, rs_y)
    dy1_ref[...] = dy1
    put_split(lhs, dy1)
    for j in range(3):
        cols = slice(256 * j, 256 * j + 256)
        ACC[:, cols] = halves_sum(dot_nt(lhs[...], wo[cols, :]))
    e = ACC[...]
    na = V[...]
    S[1:2, :] = jnp.sum(e * na, 0, keepdims=True)
    S[0:1, :] = jnp.zeros((1, D), F32)
    for j in range(4):
        S[3 + j : 4 + j, :] = gh_g[:, D * j : D * j + D]
    lane = lax.broadcasted_iota(jnp.int32, (1, 128), 1)
    S[7:8, :] = jnp.zeros((1, D), F32)
    S[7:8, 0:128] = sum(jnp.where(lane == i, sums[i : i + 1, :], 0.0) for i in range(PATTERNS))
    ACC[...] = norm_back(e * gi[...], na, rs_a)
    pairs_from_rows(ACC, dap)
    travel.start()

    put_turned(th, tl, na * gi[...])
    r_hi[...], r_lo[...] = split(dy1)
    spill.emit(lambda t: product(th, tl, r_hi, r_lo, t), column_copies(G, 0))
    put_turned(th, tl, ny * gf[...])
    for j in range(4):
        r_hi[...], r_lo[...] = split(E[:, D * j : D * j + D])
        spill.emit(lambda t: product(th, tl, r_hi, r_lo, t), column_copies(G, 1 + j))
    r_hi[...], r_lo[...] = split(g_ref[...])
    for j in range(4):
        cols = slice(D * j, D * j + D)
        put_turned(th, tl, U[:, cols] * gh[:, cols])
        spill.emit(lambda t: product(th, tl, r_hi, r_lo, t), row_copies(G, j, 5))
    spill.close()
    travel.finish()


PIECE = 24


def grad_shape(n):
    return jax.ShapeDtypeStruct((2, 2, 4, 2, n, PIECE, D), F32)


def tile_scratch():
    return [
        pltpu.VMEM((D, ROWS), BF16),
        pltpu.VMEM((D, ROWS), BF16),
        pltpu.VMEM((ROWS, D), BF16),
        pltpu.VMEM((ROWS, D), BF16),
        pltpu.VMEM((2, D, D), F32),
        pltpu.SemaphoreType.DMA((2, 32)),
    ]


def feed_forward(rec, x, g, wo, wu, wd, gi, gf, gh, sums):
    act = jax.ShapeDtypeStruct((ROWS, D), F32)
    wide = pltpu.VMEM((ROWS, FF), F32)
    thin = pltpu.VMEM((ROWS, D), F32)
    return pl.pallas_call(
        ff_kernel,
        out_shape=[
            jax.ShapeDtypeStruct((ROWS, 1, D), F32),
            jax.ShapeDtypeStruct((HOMES, HALF, 128), F32),
            act,
            jax.ShapeDtypeStruct((8, D), F32),
            grad_shape(9),
        ],
        in_specs=[VM] * 10,
        out_specs=[VM, ANY, VM, VM, ANY],
        scratch_shapes=[
            pltpu.VMEM((HEADS, HALF, 128), F32),
            pltpu.VMEM((2 * ROWS, D), BF16),
            pltpu.VMEM((2 * ROWS, FT), BF16),
            pltpu.VMEM((1, D), F32),
            pltpu.VMEM((1, D), F32),
            pltpu.VMEM((1, FF), F32),
            pltpu.VMEM((1, FF), F32),
            thin,
            thin,
            thin,
            thin,
            wide,
            wide,
            wide,
            thin,
        ]
        + tile_scratch()
        + [pltpu.SemaphoreType.DMA((HEADS,)), pltpu.SemaphoreType.DMA((HOMES,))],
        compiler_params=params(collective_id=4, has_side_effects=True),
    )(rec, x, g, wo, wu, wd, gi, gf, gh, sums)


class Place:
    def __init__(self):
        p, s = lax.axis_index("pat"), lax.axis_index("seq")
        self.p, self.s = p, s
        self.x, self.core, self.z, self.y = p // 2, lax.rem(p, 2), s // 2, lax.rem(s, 2)
        self.peer = to(self.x * 2 + 1 - self.core, s)
        self.xn = to((1 - self.x) * 2 + self.core, s)
        self.yn = to(p, self.z * 2 + 1 - self.y)
        self.left, self.right = to(p, s - 2), to(p, s + 2)

    def greet(self, barrier):
        for d in (self.peer, self.xn, self.yn):
            pl.semaphore_signal(barrier, inc=1, device_id=d, device_id_type=MESH)

        @pl.when(self.z > 0)
        def _():
            pl.semaphore_signal(barrier, inc=1, device_id=self.left, device_id_type=MESH)

        @pl.when(self.z < 3)
        def _():
            pl.semaphore_signal(barrier, inc=1, device_id=self.right, device_id_type=MESH)

        return 3 + (self.z > 0).astype(jnp.int32) + (self.z < 3).astype(jnp.int32)


def remote(src, dst, a, b, d):
    return pltpu.make_async_remote_copy(
        src_ref=src, dst_ref=dst, send_sem=a, recv_sem=b, device_id=d, device_id_type=MESH
    )


class Chunk:
    def __init__(self, place, k, group, slot, own, osem, bufs, sems, put, x_first):
        self.at, self.k, self.group, self.slot, self.own, self.osem = place, k, group, slot, own, osem
        self.b0, self.b1, self.b2, self.bl, self.br = bufs
        self.sc, self.rc, self.s1, self.r1, self.s2, self.r2, self.sl, self.rl, self.sr, self.rr = sems
        self.put, self.x_first = put, x_first

    def core(self):
        k, c = self.k, 1 - self.at.core
        return [
            remote(self.group(i, c), self.b0.at[i], self.sc.at[k, i], self.rc.at[k, i], self.at.peer)
            for i in range(2)
        ]

    def load(self):
        return [
            pltpu.make_async_copy(self.group(i, self.at.core), self.own.at[i], self.osem.at[self.slot, i])
            for i in range(2)
        ]

    def one(self):
        k, at = self.k, self.at
        if self.x_first:
            return remote(self.b0.at[1 - at.x], self.b1, self.s1.at[k], self.r1.at[k], at.xn)
        return remote(self.b0.at[:, :, 1 - at.y], self.b1, self.s1.at[k], self.r1.at[k], at.yn)

    def two(self):
        k, at = self.k, self.at
        if self.x_first:
            return remote(self.b1.at[:, 1 - at.y], self.b2, self.s2.at[k], self.r2.at[k], at.yn)
        return remote(self.b1.at[1 - at.x], self.b2, self.s2.at[k], self.r2.at[k], at.xn)

    def rightward(self, i):
        k, part = self.k, pl.ds(i + 1, 3 - i)
        src = self.b2 if i == 0 else self.bl
        return remote(src.at[part], self.bl.at[part], self.sr.at[k], self.rl.at[k], self.at.right)

    def leftward(self, i):
        k, part = self.k, pl.ds(0, i)
        src = self.b2 if i == 3 else self.br
        return remote(src.at[part], self.br.at[part], self.sl.at[k], self.rr.at[k], self.at.left)

    def stage1(self):
        if self.own is not None:
            for c in self.load():
                c.wait()
        for c in self.core():
            c.wait_recv()
        if self.own is not None:
            self.b0[...] += self.own[...]
        else:
            for i in range(2):
                self.b0[i] += self.group(i, self.at.core)[...]
        self.one().start()

    def stage2(self):
        self.one().wait_recv()
        mine = self.b0[self.at.x] if self.x_first else self.b0[:, :, self.at.y]
        self.b1[...] += mine
        self.two().start()

    def stage3(self):
        self.two().wait_recv()
        mine = self.b1[:, self.at.y] if self.x_first else self.b1[self.at.x]
        self.b2[...] += mine

        @pl.when(self.at.z == 0)
        def _():
            self.rightward(0).start()

        @pl.when(self.at.z == 3)
        def _():
            self.leftward(3).start()

    def stage4(self):
        @pl.when(self.at.z == 1)
        def _():
            self.rightward(0).wait_recv()
            self.bl[2:4] += self.b2[2:4]
            self.rightward(1).start()

        @pl.when(self.at.z == 2)
        def _():
            self.leftward(3).wait_recv()
            self.br[0:2] += self.b2[0:2]
            self.leftward(2).start()

    def stage5(self):
        @pl.when(self.at.z == 2)
        def _():
            self.rightward(1).wait_recv()
            self.bl[3:4] += self.b2[3:4]
            self.rightward(2).start()

        @pl.when(self.at.z == 1)
        def _():
            self.leftward(2).wait_recv()
            self.br[0:1] += self.b2[0:1]
            self.leftward(1).start()

    def stage6(self):
        @pl.when(self.at.z == 3)
        def _():
            self.rightward(2).wait_recv()
            self.put(self.b2[3] + self.bl[3])

        @pl.when(self.at.z == 0)
        def _():
            self.leftward(1).wait_recv()
            self.put(self.b2[0] + self.br[0])

        @pl.when(self.at.z == 1)
        def _():
            self.put(self.b2[1] + self.bl[1] + self.br[1])

        @pl.when(self.at.z == 2)
        def _():
            self.put(self.b2[2] + self.bl[2] + self.br[2])

    def sent(self):
        for c in self.core() + [self.one(), self.two()]:
            c.wait_send()
        for i in range(4):

            @pl.when(self.at.z == i)
            def _(i=i):
                if i < 3:
                    self.rightward(i).wait_send()
                if i > 0:
                    self.leftward(i).wait_send()


class Reducer:
    def __init__(self, place, n, rows, parts, scratch, put, staged):
        self.place, self.n, self.parts, self.put, self.staged = place, n, parts, put, staged
        scratch = list(scratch)
        self.own = scratch.pop(0) if staged else None
        self.osem = scratch.pop(0) if staged else None
        self.c0, self.c1a, self.c1b, self.c2, self.zl, self.zr = scratch[:6]
        self.sems = scratch[6:16]
        self.pairs = (n + 1) // 2

    @staticmethod
    def scratch(n, rows, staged):
        dma = pltpu.SemaphoreType.DMA
        bufs = [(n, 2, 4, 2), ((n + 1) // 2, 4, 2), (max(n // 2, 1), 2, 4), (n, 4), (n, 4), (n, 4)]
        return (
            ([pltpu.VMEM((4, 2, 4, 2, rows, D), F32), dma((4, 2))] if staged else [])
            + [pltpu.VMEM(b + (rows, D), F32) for b in bufs]
            + [dma((n, 2)), dma((n, 2))]
            + [dma((n,)) for _ in range(8)]
        )

    def chunk(self, k, parity):
        slot = lax.rem(k, 4)
        b1 = (self.c1b if parity else self.c1a).at[k // 2]
        return Chunk(
            self.place,
            k,
            lambda i, c: self.parts(k).at[i, c],
            slot,
            self.own.at[slot] if self.staged else None,
            self.osem,
            (self.c0.at[k], b1, self.c2.at[k], self.zl.at[k], self.zr.at[k]),
            self.sems,
            lambda v: self.put(k, v),
            parity == 0,
        )

    def begin(self):
        def one(k, carry):
            for c in self.chunk(k, 0).core():
                c.start()
            return carry

        lax.fori_loop(0, self.n, one, 0)
        for k in range(min(2, self.n)):
            for c in self.chunk(jnp.int32(k), 0).load():
                c.start()

    def send(self, first, after):
        for k in range(first, after):
            for c in self.chunk(jnp.int32(k), 0).core():
                c.start()

    def one(self, stage, pair):
        for parity in range(2):
            k = jnp.int32(2 * pair + parity)

            @pl.when(jnp.logical_and(k >= 0, k < self.n))
            def _(k=k, parity=parity):
                if stage == 1 and self.staged:

                    @pl.when(k + 2 < self.n)
                    def _():
                        for c in self.chunk(k + 2, 0).load():
                            c.start()

                getattr(self.chunk(k, parity), f"stage{stage}")()

    def early(self, pair):
        self.one(1, pair)

    def step(self, tau):
        self.one(1, tau)
        for stage in range(2, 7):
            self.one(stage, tau - stage)

    def finish(self):
        def one(k, carry):
            for parity in range(2):

                @pl.when(lax.rem(k, 2) == parity)
                def _(parity=parity):
                    self.chunk(k, parity).sent()

            return carry

        lax.fori_loop(0, self.n, one, 0)


class SmallSum:
    def __init__(self, place, S, bufs, send, recv, put):
        self.at, self.S, self.send, self.recv, self.put = place, S, send, recv, put
        self.d0, self.d1, self.d2, self.dl, self.dr, self.t1, self.t2, self.t3, self.fl, self.fr = bufs

    @staticmethod
    def scratch():
        return [pltpu.VMEM((8, D), F32)] * 10 + [pltpu.SemaphoreType.DMA((5,)), pltpu.SemaphoreType.DMA((5,))]

    def hop(self, src, dst, i, d):
        return remote(src, dst, self.send.at[i], self.recv.at[i], d)

    def core(self):
        return self.hop(self.S, self.d0, 0, self.at.peer)

    def along_x(self):
        return self.hop(self.t1, self.d1, 1, self.at.xn)

    def along_y(self):
        return self.hop(self.t2, self.d2, 2, self.at.yn)

    def rightward(self, i):
        return self.hop(self.t3 if i == 0 else self.fl, self.dl, 3, self.at.right)

    def leftward(self, i):
        return self.hop(self.t3 if i == 3 else self.fr, self.dr, 4, self.at.left)

    def stage1(self):
        self.core().wait_recv()
        self.t1[...] = self.S[...] + self.d0[...]
        self.along_x().start()

    def stage2(self):
        self.along_x().wait_recv()
        self.t2[...] = self.t1[...] + self.d1[...]
        self.along_y().start()

    def stage3(self):
        self.along_y().wait_recv()
        self.t3[...] = self.t2[...] + self.d2[...]

        @pl.when(self.at.z == 0)
        def _():
            self.rightward(0).start()

        @pl.when(self.at.z == 3)
        def _():
            self.leftward(3).start()

    def from_left(self, i):
        self.rightward(i).wait_recv()
        self.fl[...] = self.dl[...] + self.t3[...]

    def from_right(self, i):
        self.leftward(i).wait_recv()
        self.fr[...] = self.dr[...] + self.t3[...]

    def stage4(self):
        @pl.when(self.at.z == 1)
        def _():
            self.from_left(0)
            self.rightward(1).start()

        @pl.when(self.at.z == 2)
        def _():
            self.from_right(3)
            self.leftward(2).start()

    def stage5(self):
        @pl.when(self.at.z == 2)
        def _():
            self.from_left(1)
            self.rightward(2).start()

        @pl.when(self.at.z == 1)
        def _():
            self.from_right(2)
            self.leftward(1).start()

    def stage6(self):
        @pl.when(self.at.z == 3)
        def _():
            self.from_left(2)
            self.put(self.fl[...])

        @pl.when(self.at.z == 0)
        def _():
            self.from_right(1)
            self.put(self.fr[...])

        @pl.when(jnp.logical_or(self.at.z == 1, self.at.z == 2))
        def _():
            self.put(self.fl[...] + self.dr[...])

    def finish(self):
        for c in (self.core(), self.along_x(), self.along_y()):
            c.wait_send()
        for i in range(4):

            @pl.when(self.at.z == i)
            def _(i=i):
                if i < 3:
                    self.rightward(i).wait_send()
                if i > 0:
                    self.leftward(i).wait_send()


def small_outputs(place, counts, outs, tot):
    ga, gi, gf, gh, means = outs

    def put(v):
        tot[...] = v
        d = place.p * RUNS + place.s
        for i, ref in enumerate((ga, gi, gf)):
            ref[...] = pltpu.roll(tot[i : i + 1, :], D - PIECE * d, 1)[:, :PIECE]
        row = tot[pl.ds(3 + d // 8, 1), :]
        gh[...] = pltpu.roll(row, D - 4 * PIECE * lax.rem(d, 8), 1)[:, : 4 * PIECE]
        lane = lax.broadcasted_iota(jnp.int32, (1, 128), 1)
        scale = jnp.full((1, 128), counts[0], F32)
        for i in range(1, PATTERNS):
            scale = jnp.where(lane == i, counts[i], scale)
        means[...] = (tot[7:8, :128] / scale)[:, :PATTERNS]

    return put


N_PIECES = 9
SUB = 8


def finish_kernel(counts, rec, x_ref, dy1_ref, w, ga1, S_in, gx, g_qkv, ga, gi, gf, gh, means, dqkv, lhs, th, tl, r_hi, r_lo, tiles, S, tot, *scratch):
    place = Place()
    barrier = pltpu.get_barrier_semaphore()
    expected = place.greet(barrier)
    for j in range(HEADS // 2):
        u, v = rec[2 * j, ROWS:PACK, :], rec[2 * j + 1, ROWS:PACK, :]
        cols = slice(128 * j, 128 * j + 128)
        dqkv[0:HALF, cols] = pick(u, swap(v))
        dqkv[HALF:ROWS, cols] = pick(swap(u), v)
        u, v = rec[2 * j, 0:ROWS, :], rec[2 * j + 1, 0:ROWS, :]
        dqkv[:, D + 128 * j : D + 128 * j + 128] = pick(u, swap(v))
        dqkv[:, 2 * D + 128 * j : 2 * D + 128 * j + 128] = pick(swap(u), v)
    gain = ga1[...][None, :]
    n, rs = normed(x_ref[...])
    put_turned(th, tl, n * gain)

    def parts(k):
        return tiles.at[k // 3, :, :, :, :, pl.ds(pl.multiple_of(lax.rem(k, 3) * SUB, SUB), SUB), :]

    def put(k, v):
        g_qkv[
            pl.ds(pl.multiple_of(lax.rem(k, 3) * SUB, SUB), SUB), pl.ds(pl.multiple_of((k // 3) * D, D), D)
        ] = v

    n_r = 16
    big = Reducer(place, N_PIECES, SUB, parts, scratch[:n_r], put, False)
    rest = scratch[n_r:]
    small = SmallSum(
        place, S, rest[:10], rest[10], rest[11], small_outputs(place, counts, (ga, gi, gf, gh, means), tot)
    )
    for j in range(3):
        r_hi[...], r_lo[...] = split(dqkv[:, D * j : D * j + D])

        def one(i, carry):
            rows = pl.ds(pl.multiple_of(i * ROWS, 64), ROWS)
            h, l = th[rows, :], tl[rows, :]
            v = dot_nn(h, r_hi[...]) + dot_nn(h, r_lo[...]) + dot_nn(l, r_hi[...])
            tiles[j, i // 2, lax.rem(i, 2)] = v.reshape(4, 2, PIECE, D)
            return carry

        lax.fori_loop(0, 4, one, 0)
        if j == 0:
            pl.semaphore_wait(barrier, expected)
        big.send(3 * j, 3 * j + 3)
    big.early(0)
    big.early(1)
    e = None
    for j in range(3):
        cols = slice(D * j, D * j + D)
        put_split(lhs, dqkv[:, cols])
        more = halves_sum(dot_nt(lhs[...], w[:, cols]))
        e = more if e is None else e + more
        if j == 0:
            big.step(2)
    S[...] = S_in[...]
    S[0:1, :] = jnp.sum(e * n, 0, keepdims=True)
    small.core().start()
    gx[...] = (dy1_ref[...] + norm_back(e * gain, n, rs)).reshape(ROWS, 1, D)
    small.stage1()

    def step(tau, carry):
        for stage in range(2, 7):

            @pl.when(tau == stage + 1)
            def _(stage=stage):
                getattr(small, f"stage{stage}")()

        big.step(tau)
        return carry

    lax.fori_loop(3, big.pairs + 6, step, 0)

    def close(k, carry):
        for parity in range(2):

            @pl.when(lax.rem(k, 2) == parity)
            def _(parity=parity):
                big.chunk(k, parity).sent()

        return carry

    lax.fori_loop(0, N_PIECES, close, 0)
    small.finish()


def finish(rec, x, dy1, w, ga, S, counts, cid):
    return pl.pallas_call(
        functools.partial(finish_kernel, counts),
        out_shape=[jax.ShapeDtypeStruct((ROWS, 1, D), F32), jax.ShapeDtypeStruct((PIECE, 3 * D), F32)]
        + [jax.ShapeDtypeStruct((1, n), F32) for n in (PIECE, PIECE, PIECE, 4 * PIECE, PATTERNS)],
        in_specs=[VM] * 6,
        out_specs=[VM] * 7,
        scratch_shapes=[
            pltpu.VMEM((ROWS, 3 * D), F32),
            pltpu.VMEM((2 * ROWS, D), BF16),
            pltpu.VMEM((D, ROWS), BF16),
            pltpu.VMEM((D, ROWS), BF16),
            pltpu.VMEM((ROWS, D), BF16),
            pltpu.VMEM((ROWS, D), BF16),
            pltpu.VMEM((3, 2, 2, 4, 2, PIECE, D), F32),
            pltpu.VMEM((8, D), F32),
            pltpu.VMEM((8, D), F32),
        ]
        + Reducer.scratch(N_PIECES, SUB, False)
        + SmallSum.scratch(),
        compiler_params=params(collective_id=cid, has_side_effects=True),
    )(rec, x, dy1, w, ga, S)


def deliver_kernel(*refs):
    n = len(refs) // 2
    for src, dst in zip(refs[:n], refs[n:]):
        dst[...] = src[...]


def deliver(*arrays):
    return pl.pallas_call(
        deliver_kernel,
        out_shape=[jax.ShapeDtypeStruct(v.shape, v.dtype) for v in arrays],
        in_specs=[VM] * len(arrays),
        out_specs=[VM] * len(arrays),
        compiler_params=params(),
    )(*arrays)


N_FF = 9


def back_all_kernel(offs, drec, own, sib, ap, lse, G, grec, wo_g, up_g, down_g, qst, kc, vc, kt, qc, dc, lt, k4, v4, kt4, q4, d4, lt4, k5, v5, kt5, q5, d5, lt5, dqt, dk, dv, dq, dk4, dv4, dk5, dv5, dq4, dq5, b1, b2, b3, b4, ds_out, came, lsem, send, recv, qsend, qrecv, fsend, frecv, *scratch):
    place = Place()
    p, s, x, core, active, head = place_facts()
    b = core
    o2, o3, o4, o5 = offs[1], offs[2], offs[3], offs[4]
    kvf, qf, X, df = dk, dv.at[0:2], dv.at[2:4], dq
    dqp = qst

    barrier = pltpu.get_barrier_semaphore()
    expected = place.greet(barrier)

    def greet_heads(h, carry):
        q, t = head_device(h, x)

        @pl.when(jnp.logical_not(same(p, s, q, t)))
        def _():
            pl.semaphore_signal(barrier, inc=1, device_id=to(q, t), device_id_type=MESH)

        return carry

    lax.fori_loop(0, HEADS, greet_heads, 0)
    from_homes = HOMES - (core == x).astype(jnp.int32)
    pl.semaphore_wait(barrier, expected + active.astype(jnp.int32) * from_homes)

    def put(k, v):
        @pl.when(k == 0)
        def _():
            wo_g[...] = v

        @pl.when(jnp.logical_and(k > 0, k < 5))
        def _():
            up_g[:, pl.ds(pl.multiple_of((k - 1) * D, D), D)] = v

        @pl.when(k >= 5)
        def _():
            down_g[pl.ds(pl.multiple_of((k - 5) * PIECE, PIECE), PIECE), :] = v

    big = Reducer(place, N_FF, PIECE, lambda k: G.at[:, :, :, :, k], scratch, put, True)

    def local_copies(m):
        t = pl.multiple_of((m // 2) * ROWS, 64)
        c, d = 2 * b + lax.rem(m, 2), 2 * (1 - b) + lax.rem(m, 2)
        return [
            pltpu.make_async_copy(own.at[m, pl.ds(0, ROWS), :], kvf.at[c, pl.ds(t, ROWS), :], lsem.at[m, 0]),
            pltpu.make_async_copy(sib.at[m], kvf.at[d, pl.ds(t, ROWS), :], lsem.at[m, 1]),
            pltpu.make_async_copy(own.at[m, pl.ds(ROWS, HALF), :], qst.at[m], lsem.at[m, 2]),
        ]

    lse_copy = pltpu.make_async_copy(lse, X, lsem.at[HOMES, 0])

    @pl.when(active)
    def _():
        lse_copy.start()

        def start(m, carry):
            for c in local_copies(m):
                c.start()
            return carry

        lax.fori_loop(0, HOMES, start, 0)

    big.begin()

    @pl.when(active)
    def _():
        b1[...] = key_bias((2, 128), (4, 128), 4, 1, 2 * b, True)
        b2[...] = key_bias((1, 256), (2, 256), 4, 2, 2 * b, True)
        b3[...] = key_bias((1, 256), (1, 256), 1, 1, 0, True)
        e4 = class_facts4(o4, b)[1]
        b4[...] = key_bias((1, 256), (2, 256), 12, 6, 6 * e4, True)

        def wait(m, carry):
            for c in local_copies(m):
                c.wait()
            return carry

        lax.fori_loop(0, HOMES, wait, 0)
        lse_copy.wait()
        unpack_pairs(qst, 0, qf, 1.0 / math.sqrt(HD))

        def prepare(i, carry):
            c, t = i // 12, pl.multiple_of(lax.rem(i, 12) * 128, 128)
            k2, v2 = keys_and_values(kvf[c, pl.ds(t, 128), :])
            kc[c, pl.ds(t, 128), :] = k2.astype(BF16)
            vc[c, pl.ds(t, 128), :] = v2.astype(BF16)
            kt[c, :, pl.ds(t, 128)] = k2.T.astype(BF16)
            return carry

        lax.fori_loop(0, 48, prepare, 0)

        def prepare_q(i, carry):
            c, t = i // 12, pl.multiple_of(lax.rem(i, 12) * 128, 128)
            qc[c, pl.ds(t, 128), :] = query_quads(qf[c, pl.ds(t, 128), :])
            return carry

        lax.fori_loop(0, 24, prepare_q, 0)

    keys4, e4, (qc4, qv4) = class_facts4(o4, b)
    kc5, kv5 = lax.rem(o5, 4), o5 // 4
    qi4, qi5 = qc4 - 2 * b, lax.rem(kc5, 2)

    @pl.when(active)
    def _():
        for blk in range(4):
            r = slice(128 * blk, 128 * blk + 128)
            for e in range(2):
                c, v = keys4[e]
                k2, v2 = keys_and_values(kvf[c, pl.ds(v + 384 * blk, 128, stride=3), :])
                k4[e, r, :] = k2.astype(BF16)
                v4[e, r, :] = v2.astype(BF16)
                kt4[e, :, r] = k2.T.astype(BF16)
            q4[r, :] = query_quads(qf[qi4, pl.ds(qv4 + 384 * blk, 128, stride=3), :])
            rows = pl.ds(kv5 + 384 * blk, 128, stride=3)
            k2, v2 = keys_and_values(kvf[kc5, rows, :])
            k5[r, :] = k2.astype(BF16)
            v5[r, :] = v2.astype(BF16)
            kt5[:, r] = k2.T.astype(BF16)
            q5[r, :] = query_quads(qf[qi5, rows, :])
        dk[...] = jnp.zeros_like(dk)

    big.early(0)
    big.early(1)

    @pl.when(active)
    def _():
        unpack_pairs(drec, 0, df, 1.0)

        def facts(m, carry):
            ci = lax.rem(m, 2)
            t = pl.multiple_of((m // 2) * ROWS, 32)
            prod = drec[m] * ap[m]
            low = lower_lanes(prod)
            d0 = jnp.sum(jnp.where(low, prod, 0.0), -1, keepdims=True)
            d1 = jnp.sum(jnp.where(low, 0.0, prod), -1, keepdims=True)
            for part, d in ((0, d0), (1, d1)):
                rows = pl.ds(t + HALF * part, HALF)
                l = X[ci, rows, :]
                X[ci, rows, :] = jnp.where(low, l, jnp.broadcast_to(d, l.shape))
            return carry

        lax.fori_loop(0, HOMES, facts, 0)

        def turned(v):
            w = v.T
            return jnp.concatenate([w[0:1, :], w[HD : HD + 1, :]], 0)

        def prepare_d(i, carry):
            c, t = i // 12, pl.multiple_of(lax.rem(i, 12) * 128, 128)
            rows = pl.ds(t, 128)
            dc[c, rows, :] = query_quads(df[c, rows, :])
            lt[i] = turned(X[c, rows, :])
            return carry

        lax.fori_loop(0, 24, prepare_d, 0)
        for blk in range(4):
            r = slice(128 * blk, 128 * blk + 128)
            rows = pl.ds(qv4 + 384 * blk, 128, stride=3)
            d4[r, :] = query_quads(df[qi4, rows, :])
            lt4[blk] = turned(X[qi4, rows, :])
            rows = pl.ds(kv5 + 384 * blk, 128, stride=3)
            d5[r, :] = query_quads(df[qi5, rows, :])
            lt5[blk] = turned(X[qi5, rows, :])
        dv[...] = jnp.zeros_like(dv)
        dq[...] = jnp.zeros_like(dq)

    def tile(g, k, v, kT, q, d, facts_pair, bias, first):
        s_ = dot_nt(doubled(k), q)
        if bias is not None:
            s_ = s_ + bias[...]
        l0, l1 = facts_pair
        row = jnp.concatenate([l0[0:1, :], l1[0:1, :]], 1)
        delta = jnp.concatenate([l0[1:2, :], l1[1:2, :]], 1)
        pr = jnp.exp(s_ - row)
        ds = pr * (dot_nt(doubled(v), d) - delta)
        hi, lo = split(pr)
        d2, q2_ = d[:, :128], q[:, :128]
        dv_new = dot_nn(jnp.concatenate([hi, lo], 1), jnp.concatenate([d2, d2], 0))
        hi, lo = split(ds)
        dk_new = dot_nn(jnp.concatenate([hi, lo], 1), jnp.concatenate([q2_, q2_], 0))
        dq_new = dot_nn(doubled(kT), jnp.concatenate([hi, lo], 0))
        dqt[g] = dq_new if first else dqt[g] + dq_new
        return dk_new, dv_new

    def at256(blk):
        return pl.ds(pl.multiple_of(256 * blk, 128), 256)

    def kept(flag, v):
        return jnp.where(flag, v, 0.0)

    def q2(qb, carry):
        def step(kb, bias, first):
            ks, qs = at256(kb), at256(qb)
            a, c = tile(
                0,
                jnp.concatenate([kc[o2, ks, :], kc[o2 + 2, ks, :]], 0),
                jnp.concatenate([vc[o2, ks, :], vc[o2 + 2, ks, :]], 0),
                jnp.concatenate([kt[o2, :, ks], kt[o2 + 2, :, ks]], 1),
                qc[o2, qs, :],
                dc[o2, qs, :],
                (lt.at[12 * o2 + 2 * qb], lt.at[12 * o2 + 2 * qb + 1]),
                bias,
                first,
            )
            for par in range(2):
                f = o2 == par
                dk[par, ks, :] += kept(f, a[:256])
                dk[par + 2, ks, :] += kept(f, a[256:])
                dv[par, ks, :] += kept(f, c[:256])
                dv[par + 2, ks, :] += kept(f, c[256:])

        step(qb, b2, True)

        def more(kb, inner):
            step(kb, None, False)
            return inner

        lax.fori_loop(jnp.where(qb >= 4, 4, 0), qb, more, 0)
        for par in range(2):
            dq[par, at256(qb), :] += kept(o2 == par, dqt[0].T)
        return carry

    @pl.when(active)
    def _():
        lax.fori_loop(0, TOTAL // 256, q2, 0)

    big.step(2)

    def q3(qb, carry):
        ci = lax.rem(o3, 2)

        def step(kb, bias, first):
            ks, qs = at256(kb), at256(qb)
            a, c = tile(
                0,
                kc[o3, ks, :],
                vc[o3, ks, :],
                kt[o3, :, ks],
                qc[ci, qs, :],
                dc[ci, qs, :],
                (lt.at[12 * ci + 2 * qb], lt.at[12 * ci + 2 * qb + 1]),
                bias,
                first,
            )
            for i in range(2):
                f = o3 == 2 * b + i
                dk[2 * b + i, ks, :] += kept(f, a)
                dv[2 * b + i, ks, :] += kept(f, c)

        step(qb, b3, True)

        def more(kb, inner):
            step(kb, None, False)
            return inner

        lax.fori_loop(0, qb, more, 0)
        for i in range(2):
            dq[i, at256(qb), :] += kept(o3 == 2 * b + i, dqt[0].T)
        return carry

    @pl.when(active)
    def _():
        lax.fori_loop(0, TOTAL // 256, q3, 0)

    @pl.when(active)
    def _():
        for ref in (dk4, dv4, dk5, dv5):
            ref[...] = jnp.zeros_like(ref)
        for qb in range(2):
            qs = slice(256 * qb, 256 * qb + 256)
            for kb in range(qb, -1, -1):
                ks = slice(256 * kb, 256 * kb + 256)
                a, c = tile(
                    0,
                    k4[:, ks, :].reshape(512, 128),
                    v4[:, ks, :].reshape(512, 128),
                    jnp.concatenate([kt4[0, :, ks], kt4[1, :, ks]], 1),
                    q4[qs, :],
                    d4[qs, :],
                    (lt4.at[2 * qb], lt4.at[2 * qb + 1]),
                    b4 if kb == qb else None,
                    kb == qb,
                )
                dk4[:, ks, :] += a.reshape(2, 256, 128)
                dv4[:, ks, :] += c.reshape(2, 256, 128)
                a, c = tile(
                    1,
                    k5[ks, :],
                    v5[ks, :],
                    kt5[:, ks],
                    q5[qs, :],
                    d5[qs, :],
                    (lt5.at[2 * qb], lt5.at[2 * qb + 1]),
                    b3 if kb == qb else None,
                    kb == qb,
                )
                dk5[ks, :] += a
                dv5[ks, :] += c
            dq4[qs, :] = dqt[0].T
            dq5[qs, :] = dqt[1].T
        mine5 = kc5 // 2 == b
        for kind in range(12):
            c, rows = kind % 4, pl.ds(kind // 4, THIRD, stride=3)
            f0, f1, f5 = o4 == kind, o4 + 6 == kind, jnp.logical_and(o5 == kind, mine5)
            dk[c, rows, :] += kept(f0, dk4[0]) + kept(f1, dk4[1]) + kept(f5, dk5[...])
            dv[c, rows, :] += kept(f0, dv4[0]) + kept(f1, dv4[1]) + kept(f5, dv5[...])
        for ci in range(2):
            for v in range(3):
                rows = pl.ds(v, THIRD, stride=3)
                f4 = jnp.logical_and(qi4 == ci, qv4 == v)
                f5 = jnp.logical_and(jnp.logical_and(qi5 == ci, kv5 == v), mine5)
                dq[ci, rows, :] += kept(f4, dq4[...]) + kept(f5, dq5[...])

    big.step(3)

    def segment(g):
        def at(blk):
            return pl.ds(pl.multiple_of(512 * g + 128 * blk, 128), 128)

        def step(i, qb, kb, bias, first):
            ks, qs = at(kb), at(qb)
            kT = jnp.concatenate([kt[c, :, ks] for c in range(4)], 1)
            a, c = tile(
                i,
                kc[:, ks, :].reshape(512, 128),
                vc[:, ks, :].reshape(512, 128),
                kT,
                qc[:, qs, :].reshape(256, 256),
                dc[:, qs, :].reshape(256, 256),
                (lt.at[4 * g + qb], lt.at[12 + 4 * g + qb]),
                bias,
                first,
            )
            dk[:, ks, :] += a.reshape(4, 128, 128)
            dv[:, ks, :] += c.reshape(4, 128, 128)

        def pair(j, carry):
            q0, q1_ = 2 * j, 2 * j + 1
            step(0, q0, q0, b1, True)
            step(1, q1_, q1_, b1, True)

            def more(kb, inner):
                step(0, q0, kb, None, False)
                step(1, q1_, kb, None, False)
                return inner

            lax.fori_loop(0, q0, more, 0)
            step(1, q1_, q0, None, False)
            for i, qb in ((0, q0), (1, q1_)):
                dq[:, at(qb), :] += dqt[i].T.reshape(2, 128, 128)
            return carry

        lax.fori_loop(0, 2, pair, 0)

    def passed(m):
        return remote(ds_out.at[m], came.at[m], fsend.at[m], frecv.at[m], place.peer)

    def home_copies(m):
        q, t = home_device(core, m)
        kv = remote(came.at[m], grec.at[head, pl.ds(0, ROWS), :], send.at[m], recv.at[head], to(q, t))
        dq_ = remote(dqp.at[m], grec.at[head, pl.ds(ROWS, HALF), :], qsend.at[m], qrecv.at[head], to(q, t))
        return q, t, kv, dq_

    def rows_of(m):
        return pl.ds(pl.multiple_of((m // 2) * ROWS, 64), ROWS)

    def kv(c, m):
        k, v = dk[c, rows_of(m), :], dv[c, rows_of(m), :]
        return pick(k + swap(k), v + swap(v))

    def share(m, carry):
        ds_out[m] = kv(2 * (1 - b) + lax.rem(m, 2), m)
        passed(m).start()
        return carry

    def add(m, carry):
        q, t, far_kv, far_q = home_copies(m)
        ci = lax.rem(m, 2)
        v = dq[ci, rows_of(m), :]
        v = (v + swap(v)) * (1.0 / math.sqrt(HD))
        dqp[m] = pick(v[:HALF], v[HALF:])
        passed(m).wait_recv()
        came[m] += kv(2 * b + ci, m)

        @pl.when(same(p, s, q, t))
        def _():
            pltpu.make_async_copy(came.at[m], grec.at[head, pl.ds(0, ROWS), :], recv.at[head]).start()
            pltpu.make_async_copy(dqp.at[m], grec.at[head, pl.ds(ROWS, HALF), :], qrecv.at[head]).start()

        @pl.when(jnp.logical_not(same(p, s, q, t)))
        def _():
            far_kv.start()
            far_q.start()

        return carry

    @pl.when(active)
    def _():
        segment(0)
        lax.fori_loop(0, 4, share, 0)
        segment(2)
        lax.fori_loop(12, HOMES, share, 0)
        lax.fori_loop(0, 4, add, 0)

    big.step(4)

    @pl.when(active)
    def _():
        segment(1)
        lax.fori_loop(4, 12, share, 0)
        lax.fori_loop(12, HOMES, add, 0)
        lax.fori_loop(4, 12, add, 0)

    for tau in range(5, big.pairs + 6):
        big.step(tau)

    def from_head(h, carry):
        a = grec.at[h, pl.ds(0, ROWS), :]
        c = grec.at[h, pl.ds(ROWS, HALF), :]
        pltpu.make_async_copy(a, a, recv.at[h]).wait()
        pltpu.make_async_copy(c, c, qrecv.at[h]).wait()
        return carry

    lax.fori_loop(0, HEADS, from_head, 0)
    big.finish()

    @pl.when(active)
    def _():
        def sent(m, carry):
            q, t, far_kv, far_q = home_copies(m)
            passed(m).wait_send()

            @pl.when(jnp.logical_not(same(p, s, q, t)))
            def _():
                far_kv.wait_send()
                far_q.wait_send()

            return carry

        lax.fori_loop(0, HOMES, sent, 0)


def backward_all(offs, drec, own, sib, ap, lse, G, cid):
    dma = pltpu.SemaphoreType.DMA
    keys = pltpu.VMEM((4, TOTAL, 128), BF16)
    full = pltpu.VMEM((4, TOTAL, 128), F32)
    quad = pltpu.VMEM((2, TOTAL, 256), BF16)
    quad3 = pltpu.VMEM((THIRD, 256), BF16)
    pair3 = pltpu.VMEM((THIRD, 128), BF16)
    turned = pltpu.VMEM((128, THIRD), BF16)
    facts3 = pltpu.VMEM((4, 2, 128), F32)
    out3 = pltpu.VMEM((THIRD, 128), F32)
    packs = pltpu.VMEM((HOMES, ROWS, 128), F32)
    halves = pltpu.VMEM((HOMES, HALF, 128), F32)
    return pl.pallas_call(
        back_all_kernel,
        out_shape=[
            jax.ShapeDtypeStruct((HEADS, PACK, 128), F32),
            jax.ShapeDtypeStruct((PIECE, D), F32),
            jax.ShapeDtypeStruct((PIECE, FF), F32),
            jax.ShapeDtypeStruct((4 * PIECE, D), F32),
        ],
        in_specs=[SM, VM, ANY, ANY, VM, ANY, ANY],
        out_specs=[ANY, VM, VM, VM],
        scratch_shapes=[
            halves,
            keys,
            keys,
            pltpu.VMEM((4, 128, TOTAL), BF16),
            quad,
            quad,
            pltpu.VMEM((24, 2, 128), F32),
            pltpu.VMEM((2, THIRD, 128), BF16),
            pltpu.VMEM((2, THIRD, 128), BF16),
            pltpu.VMEM((2, 128, THIRD), BF16),
            quad3,
            quad3,
            facts3,
            pair3,
            pair3,
            turned,
            quad3,
            quad3,
            facts3,
            pltpu.VMEM((3, 128, 256), F32),
            full,
            full,
            pltpu.VMEM((2, TOTAL, 128), F32),
            pltpu.VMEM((2, THIRD, 128), F32),
            pltpu.VMEM((2, THIRD, 128), F32),
            out3,
            out3,
            out3,
            out3,
            pltpu.VMEM((512, 256), F32),
            pltpu.VMEM((512, 256), F32),
            pltpu.VMEM((256, 256), F32),
            pltpu.VMEM((512, 256), F32),
            packs,
            packs,
            dma((HOMES + 1, 3)),
            dma((HOMES,)),
            dma((HEADS,)),
            dma((HOMES,)),
            dma((HEADS,)),
            dma((HOMES,)),
            dma((HOMES,)),
        ]
        + Reducer.scratch(N_FF, PIECE, True),
        compiler_params=params(collective_id=cid, has_side_effects=True),
    )(offs, drec, own, sib, ap, lse, G)


SEG1, SEG2, SEG3, SEG4, SEG5 = SEGMENTS
DILATION_ONE, DILATION_TWO, DILATION_THREE, DILATION_FOUR, DILATION_FIVE = DILATIONS
MASK_VALUE = -1e30
MATMUL_ACCURACY = lax.Precision.HIGHEST


def passed_along(value, axis, by):
    length = lax.axis_size(axis)
    return lax.ppermute(value, axis, [(i, (i + by) % length) for i in range(length)])


def run_is_live(distance, anchor_point, sequence_width, segment_length):
    return (anchor_point - (distance - 1) * sequence_width - 1) // segment_length == anchor_point // segment_length


def layer_norm(x, gain_vec):
    average = jnp.mean(x, -1, keepdims=True)
    centred = x - average
    variance = jnp.mean(centred * centred, -1, keepdims=True)
    return centred * lax.rsqrt(variance + LN_EPSILON) * gain_vec


def select_table(offsets_row, dilation_rate):
    return (jnp.arange(dilation_rate, dtype=jnp.int32)[:, None] == offsets_row[None, :]).astype(
        jnp.float32
    )


def spread_apart(x, select_option, dilation_rate):
    shaped = x.reshape(x.shape[0] // dilation_rate, dilation_rate, x.shape[1], x.shape[2])
    return jnp.einsum("trhd,rh->thd", shaped, select_option, precision=MATMUL_ACCURACY)


def spread_scalar_rows(x, select_option, dilation_rate):
    shaped = x.reshape(x.shape[0] // dilation_rate, dilation_rate, x.shape[1])
    return jnp.einsum("trh,rh->th", shaped, select_option, precision=MATMUL_ACCURACY)


def spread_rows(x, select_option):
    return jnp.einsum("thd,rh->trhd", x, select_option, precision=MATMUL_ACCURACY).reshape(
        -1, x.shape[1], x.shape[2]
    )


def spread_scalars(x, select_option):
    return jnp.einsum("th,rh->trh", x, select_option, precision=MATMUL_ACCURACY).reshape(
        -1, x.shape[1]
    )


def masked_score_matrix(sparse_queries, key_portion, query_position, key_position, segment_length):
    score_matrix = jnp.einsum(
        "ozt,bzt->zob", sparse_queries, key_portion, precision=MATMUL_ACCURACY
    ) * (1.0 / math.sqrt(key_portion.shape[-1]))
    q_cols = query_position.T[:, :, None]
    k_cols = key_position.T[:, None, :]
    permitted_mask = (k_cols <= q_cols) & (k_cols // segment_length == q_cols // segment_length)
    return (jnp.where(permitted_mask, score_matrix, MASK_VALUE), permitted_mask)


def prepare_pattern(
    query_sequence, key_sequence, value_sequence, offsets_row, dilation_rate, anchor_point
):
    select_option = select_table(offsets_row, dilation_rate)
    sparse_queries = spread_apart(query_sequence, select_option, dilation_rate)
    sparse_key_value = jnp.stack(
        (
            spread_apart(key_sequence, select_option, dilation_rate),
            spread_apart(value_sequence, select_option, dilation_rate),
        )
    )
    query_position = (
        anchor_point
        + jnp.arange(sparse_queries.shape[0], dtype=jnp.int32)[:, None] * dilation_rate
        + offsets_row[None, :]
    )
    return (select_option, sparse_queries, sparse_key_value, query_position)


def pattern_forward_pass(
    sparse_queries,
    sparse_key_value,
    query_position,
    reach,
    segment_length,
    anchor_point,
    sequence_width,
):
    masked_logits, permitted_mask = masked_score_matrix(
        sparse_queries, sparse_key_value[0], query_position, query_position, segment_length
    )
    row_max = jnp.max(masked_logits, -1)
    softmax_weights = jnp.where(permitted_mask, jnp.exp(masked_logits - row_max[..., None]), 0.0)
    state = (
        row_max,
        jnp.sum(softmax_weights, -1),
        jnp.einsum("tlj,jtb->tlb", softmax_weights, sparse_key_value[1], precision=MATMUL_ACCURACY),
    )

    def one_run(distance, carry):
        remote_key_value, state = carry
        remote_key_value = passed_along(remote_key_value, "seq", 1)
        key_position = query_position - distance * sequence_width

        def update(state_in):
            old_max, old_sum, old_acc = state_in
            masked_remote, permitted_remote = masked_score_matrix(
                sparse_queries, remote_key_value[0], query_position, key_position, segment_length
            )
            new_max = jnp.maximum(old_max, jnp.max(masked_remote, -1))
            weights_far = jnp.where(
                permitted_remote, jnp.exp(masked_remote - new_max[..., None]), 0.0
            )
            factor = jnp.exp(old_max - new_max)
            added = jnp.einsum(
                "tlj,jtb->tlb", weights_far, remote_key_value[1], precision=MATMUL_ACCURACY
            )
            return (
                new_max,
                old_sum * factor + jnp.sum(weights_far, -1),
                old_acc * factor[..., None] + added,
            )

        def unchanged(state_in):
            return state_in

        is_live = run_is_live(distance, anchor_point, sequence_width, segment_length)
        return remote_key_value, lax.cond(is_live, update, unchanged, state)

    state = lax.fori_loop(1, reach + 1, one_run, (sparse_key_value, state))[1]
    row_max, row_sum, accumulated = state
    mixture = jnp.transpose(accumulated / row_sum[..., None], (1, 0, 2))
    log_sum = (row_max + jnp.log(row_sum)).T
    return (mixture, log_sum)


def merge_patterns(forwards, prepared_inputs):
    full_lse = []
    full_mix = []
    for pattern_spec in range(len(forwards)):
        mixture, log_sum = forwards[pattern_spec]
        select_option = prepared_inputs[pattern_spec][0]
        covered = spread_scalars(jnp.ones_like(log_sum), select_option)
        full_lse.append(spread_scalars(log_sum, select_option) + (covered - 1.0) * 1e30)
        full_mix.append(spread_rows(mixture, select_option))
    stacked = jnp.stack(full_lse)
    row_max = jnp.max(stacked, 0)
    softmax_weights = jnp.exp(stacked - row_max)
    row_sum = jnp.sum(softmax_weights, 0)
    attended = full_mix[0] * softmax_weights[0][..., None]
    for pattern_spec in range(1, len(full_mix)):
        attended = attended + full_mix[pattern_spec] * softmax_weights[pattern_spec][..., None]
    return (attended / row_sum[..., None], row_max + jnp.log(row_sum))


def pattern_backward(
    select_option,
    dilation_rate,
    segment_length,
    anchor_point,
    sparse_queries,
    sparse_key_value,
    query_position,
    reach,
    sequence_gradient,
    row_difference,
    combined_logsumexp,
):
    sequence_width = sequence_gradient.shape[0]
    sparse_gradient = spread_apart(sequence_gradient, select_option, dilation_rate)
    sparse_output_grad = spread_scalar_rows(row_difference, select_option, dilation_rate).T
    sparse_logsumexp = spread_scalar_rows(combined_logsumexp, select_option, dilation_rate).T
    inverse_square_root = 1.0 / math.sqrt(sparse_queries.shape[-1])

    def portion_gradients(key_portion, value_portion, key_position):
        masked_logits, permitted_mask = masked_score_matrix(
            sparse_queries, key_portion, query_position, key_position, segment_length
        )
        softmax_weights = jnp.where(
            permitted_mask, jnp.exp(masked_logits - sparse_logsumexp[..., None]), 0.0
        )
        value_gradient = jnp.einsum(
            "tui,utx->itx", softmax_weights, sparse_gradient, precision=MATMUL_ACCURACY
        )
        pattern_gradient = jnp.einsum(
            "ozt,bzt->zob", sparse_gradient, value_portion, precision=MATMUL_ACCURACY
        )
        score_gradient = (
            softmax_weights
            * (pattern_gradient - sparse_output_grad[..., None])
            * inverse_square_root
        )
        query_gradient = jnp.einsum(
            "hqk,khd->qhd", score_gradient, key_portion, precision=MATMUL_ACCURACY
        )
        key_gradient = jnp.einsum(
            "tui,utx->itx", score_gradient, sparse_queries, precision=MATMUL_ACCURACY
        )
        return (query_gradient, jnp.stack((key_gradient, value_gradient)))

    query_gradient, key_value_gradient = portion_gradients(
        sparse_key_value[0], sparse_key_value[1], query_position
    )

    def one_run(distance, carry):
        remote_key_value, remote_gradient, query_sum = carry
        remote_key_value = passed_along(remote_key_value, "seq", 1)
        remote_gradient = passed_along(remote_gradient, "seq", 1)
        key_position = query_position - distance * sequence_width

        def far_grads():
            part_q, part_kv = portion_gradients(remote_key_value[0], remote_key_value[1], key_position)
            return query_sum + part_q, remote_gradient + part_kv

        def no_grads():
            return query_sum, remote_gradient

        is_live = run_is_live(distance, anchor_point, sequence_width, segment_length)
        query_sum, remote_gradient = lax.cond(is_live, far_grads, no_grads)
        return remote_key_value, remote_gradient, query_sum

    _, travelled, query_gradient = lax.fori_loop(
        1, reach + 1, one_run, (sparse_key_value, key_value_gradient, query_gradient)
    )
    return (query_gradient, passed_along(travelled, "seq", -reach))


def front_part(own_rows, w_qkv, gain_attn):
    return jnp.dot(layer_norm(own_rows, gain_attn), w_qkv, precision=MATMUL_ACCURACY)


def after_part(attn_rows, own_rows, w_out, w_up, w_down, gain_inner, gain_ffn, gain_hidden):
    residual = own_rows + jnp.dot(
        layer_norm(attn_rows, gain_inner), w_out, precision=MATMUL_ACCURACY
    )
    hidden = jax.nn.gelu(
        jnp.dot(layer_norm(residual, gain_ffn), w_up, precision=MATMUL_ACCURACY), approximate=False
    )
    return residual + jnp.dot(layer_norm(hidden, gain_hidden), w_down, precision=MATMUL_ACCURACY)


def shards(
    tokens,
    w_qkv,
    w_out,
    w_up,
    w_down,
    gain_attn,
    gain_inner,
    gain_ffn,
    gain_hidden,
    offsets,
    grad_out,
):
    w_qkv = w_qkv.astype(jnp.float32)
    w_out = w_out.astype(jnp.float32)
    w_up = w_up.astype(jnp.float32)
    w_down = w_down.astype(jnp.float32)
    groups = lax.axis_size("pat")
    local_rows = tokens.shape[0]
    sequence_width = local_rows * groups
    heads_here = HEADS // groups
    own_rows = tokens.reshape(local_rows, D)
    qkv_rows, front_back = jax.vjp(front_part, own_rows, w_qkv, gain_attn)
    gathered_qkv = lax.all_to_all(
        qkv_rows.reshape(local_rows, 1, 3, HEADS, HD),
        "pat",
        split_axis=3,
        concat_axis=1,
        tiled=True,
    )
    gathered_qkv = gathered_qkv.reshape(sequence_width, 3, heads_here, HD)
    head_offsets = lax.dynamic_slice_in_dim(
        offsets, lax.axis_index("pat") * heads_here, heads_here, 1
    )
    anchor_point = lax.axis_index("seq") * sequence_width
    dilation_rates = (DILATION_ONE, DILATION_TWO, DILATION_THREE, DILATION_FOUR, DILATION_FIVE)
    segment_lengths = (SEG1, SEG2, SEG3, SEG4, SEG5)
    reaches = [
        min((segment_lengths[pattern_spec] - 2) // sequence_width + 1, lax.axis_size("seq") - 1)
        for pattern_spec in range(PATTERNS)
    ]
    prepared_inputs = []
    for pattern_spec in range(PATTERNS):
        prepared_inputs.append(
            prepare_pattern(
                gathered_qkv[:, 0],
                gathered_qkv[:, 1],
                gathered_qkv[:, 2],
                head_offsets[pattern_spec],
                dilation_rates[pattern_spec],
                anchor_point,
            )
        )
    forwards = []
    for pattern_spec in range(PATTERNS):
        select_option, sparse_queries, sparse_key_value, query_position = prepared_inputs[
            pattern_spec
        ]
        forwards.append(
            pattern_forward_pass(
                sparse_queries,
                sparse_key_value,
                query_position,
                reaches[pattern_spec],
                segment_lengths[pattern_spec],
                anchor_point,
                sequence_width,
            )
        )
    lse_sums = jnp.stack([jnp.sum(entry[1]) for entry in forwards])
    totals = lax.psum(lse_sums, ("pat", "seq"))
    full_length = sequence_width * lax.axis_size("seq")
    counts = jnp.array(
        [
            float(full_length // dilation_rates[pattern_spec] * HEADS)
            for pattern_spec in range(PATTERNS)
        ],
        jnp.float32,
    )
    log_means = totals / counts
    attended, combined_logsumexp = merge_patterns(forwards, prepared_inputs)
    returned_rows = lax.all_to_all(
        attended.reshape(local_rows, groups, heads_here, HD),
        "pat",
        split_axis=1,
        concat_axis=2,
        tiled=True,
    )
    attn_rows = returned_rows.reshape(local_rows, D)
    result, after_back = jax.vjp(
        after_part, attn_rows, own_rows, w_out, w_up, w_down, gain_inner, gain_ffn, gain_hidden
    )
    g_attn, g_resid, g_out, g_up, g_down, g_inner, g_ffn, g_hidden = after_back(
        grad_out.reshape(local_rows, D)
    )
    sequence_gradient = lax.all_to_all(
        g_attn.reshape(local_rows, 1, HEADS, HD), "pat", split_axis=2, concat_axis=1, tiled=True
    )
    sequence_gradient = sequence_gradient.reshape(sequence_width, heads_here, HD)
    row_difference = jnp.sum(sequence_gradient * attended, -1)
    q_grads = []
    kv_grads = []
    for pattern_spec in range(PATTERNS):
        select_option, sparse_queries, sparse_key_value, query_position = prepared_inputs[
            pattern_spec
        ]
        part_q, part_kv = pattern_backward(
            select_option,
            dilation_rates[pattern_spec],
            segment_lengths[pattern_spec],
            anchor_point,
            sparse_queries,
            sparse_key_value,
            query_position,
            reaches[pattern_spec],
            sequence_gradient,
            row_difference,
            combined_logsumexp,
        )
        q_grads.append(part_q)
        kv_grads.append(part_kv)
    grad_total = jnp.zeros((sequence_width, 3, heads_here, HD), jnp.float32)
    for pattern_spec in range(PATTERNS):
        select_option = prepared_inputs[pattern_spec][0]
        grad_total = grad_total + jnp.stack(
            (
                spread_rows(q_grads[pattern_spec], select_option),
                spread_rows(kv_grads[pattern_spec][0], select_option),
                spread_rows(kv_grads[pattern_spec][1], select_option),
            ),
            1,
        )
    grad_back = lax.all_to_all(
        grad_total.reshape(local_rows, groups, 3, heads_here, HD),
        "pat",
        split_axis=1,
        concat_axis=3,
        tiled=True,
    )
    g_tokens, g_qkv, g_attn_gain = front_back(grad_back.reshape(local_rows, 3 * D))
    grad_tokens = (g_resid + g_tokens).reshape(local_rows, 1, D)
    summed = (
        lax.psum_scatter(g_qkv, ("pat", "seq"), scatter_dimension=0, tiled=True),
        lax.psum_scatter(g_out, ("pat", "seq"), scatter_dimension=0, tiled=True),
        lax.psum_scatter(g_up, ("pat", "seq"), scatter_dimension=0, tiled=True),
        lax.psum_scatter(g_down, ("pat", "seq"), scatter_dimension=0, tiled=True),
        lax.psum_scatter(g_attn_gain, ("pat", "seq"), scatter_dimension=0, tiled=True),
        lax.psum_scatter(g_inner, ("pat", "seq"), scatter_dimension=0, tiled=True),
        lax.psum_scatter(g_ffn, ("pat", "seq"), scatter_dimension=0, tiled=True),
        lax.psum_scatter(g_hidden, ("pat", "seq"), scatter_dimension=0, tiled=True),
    )
    return (
        result.reshape(local_rows, 1, D),
        grad_tokens,
        summed[0],
        summed[1],
        summed[2],
        summed[3],
        summed[4],
        summed[5],
        summed[6],
        summed[7],
        log_means,
    )


def fast_shards(tokens, w_qkv, w_out, w_up, w_down, gain_attn, gain_inner, gain_ffn, gain_hidden, offsets, grad_out):
    p, s = lax.axis_index("pat"), lax.axis_index("seq")
    active, head = head_here(p, s)
    mine = lax.dynamic_slice_in_dim(offsets, head, 1, 1)[:, 0]
    info = jnp.concatenate([jnp.stack([active.astype(jnp.int32), lax.rem(p, 2).astype(jnp.int32)]), mine])

    counts = [float(TOTAL * 4 // r * HEADS) for r in DILATIONS]
    pk, x = front(tokens, w_qkv, gain_attn)
    own, sib = to_heads(pk, True, 0)
    ap, lse, sums = attention_forward(info, own, sib)
    rec = to_homes(ap, 1)
    mixed, drec, dy1, S, G = feed_forward(
        rec, x, grad_out, w_out, w_up, w_down, gain_inner, gain_ffn, gain_hidden, sums
    )
    grec, g_out, g_up, g_down = backward_all(mine, drec, own, sib, ap, lse, G, 2)
    gx, g_qkv, *small = finish(grec, x, dy1, w_qkv, gain_attn, S, counts, 3)
    mixed, gx, g_qkv, g_out, g_up, g_down, *small = deliver(mixed, gx, g_qkv, g_out, g_up, g_down, *small)
    return (mixed, gx, g_qkv, g_out, g_up, g_down, *(v.reshape(-1) for v in small))


def fits(mesh):
    return mesh.shape["pat"] == 4 and mesh.shape["seq"] == RUNS


def solution(mesh):
    rows = P("seq", "pat", None)
    split_rows = P(("pat", "seq"), None)
    split_one = P(("pat", "seq"))
    planned = jax.shard_map(
        fast_shards,
        mesh=mesh,
        in_specs=(rows,) + (P(),) * 9 + (rows,),
        out_specs=(rows, rows) + (split_rows,) * 4 + (split_one,) * 4 + (P(),),
        check_vma=False,
    )
    general = jax.shard_map(
        shards,
        mesh=mesh,
        in_specs=(rows,) + (P(),) * 9 + (rows,),
        out_specs=(rows, rows) + (split_rows,) * 4 + (split_one,) * 4 + (P(),),
        check_vma=False,
    )

    def layer(tokens, *rest):
        if fits(mesh) and tokens.shape[0] == TOTAL:
            return planned(tokens, *rest)
        return general(tokens, *rest)

    return layer
```

```python
import functools
import math

import jax
import jax.numpy as jnp
from jax import lax
from jax.experimental import pallas as pl
from jax.experimental.pallas import tpu as pltpu
from jax.sharding import PartitionSpec as P

D = 768
HEADS = 12
HD = 64
FF = 3072
PATTERNS = 5
SEGMENTS = (2048, 4096, 8192, 16384, 32768)
DILATIONS = (1, 2, 4, 6, 12)
LN_EPSILON = 1e-05
NEG = -1e30
F32 = jnp.float32
BF16 = jnp.bfloat16
HIGHEST = lax.Precision.HIGHEST
VMEM_LIMIT = 60 * 1024 * 1024

ROWS = 192
HALF = ROWS // 2
RUNS = 8
TOTAL = ROWS * RUNS
PACK = ROWS + HALF
HOMES = 16
THIRD = TOTAL // 3
PIECE = 24
MESH = pl.DeviceIdType.MESH


def dot_nn(a, b):
    return lax.dot_general(a, b, (((1,), (0,)), ((), ())), preferred_element_type=F32)


def dot_nt(a, b):
    return lax.dot_general(a, b, (((1,), (1,)), ((), ())), preferred_element_type=F32)


def split(v):
    hi = v.astype(BF16)
    return hi, (v - hi.astype(F32)).astype(BF16)


def split32(v):
    hi = v.astype(BF16).astype(F32)
    return hi, v - hi


def lower_lanes(v):
    return lax.broadcasted_iota(jnp.int32, v.shape, v.ndim - 1) < HD


def swap(v):
    return pltpu.roll(v, HD, v.ndim - 1)


def pick(a, b):
    return jnp.where(lower_lanes(a), a, b)


def head_place(h):
    z = h // 3
    column = lax.rem(lax.rem(h, 3) + z + 1, 4)
    return column // 2, z * 2 + lax.rem(column, 2)


def head_here(p, s):
    z = s // 2
    column = (p // 2) * 2 + lax.rem(s, 2)
    k = lax.rem(column - z + 7, 4)
    return k < 3, z * 3 + jnp.minimum(k, 2)


def whole(*_):
    return pl.BlockSpec(memory_space=pltpu.VMEM)


VM = pl.BlockSpec(memory_space=pltpu.VMEM)
ANY = pl.BlockSpec(memory_space=pl.ANY)
SM = pl.BlockSpec(memory_space=pltpu.SMEM)


def params(**kw):
    return pltpu.CompilerParams(vmem_limit_bytes=VMEM_LIMIT, **kw)


def normed(v):
    centred = v - jnp.mean(v, -1, keepdims=True)
    rs = lax.rsqrt(jnp.mean(centred * centred, -1, keepdims=True) + LN_EPSILON)
    return centred * rs, rs


def put_split(ref, v):
    hi, lo = split(v)
    n = v.shape[0]
    ref[0:n, :] = hi
    ref[n : 2 * n, :] = lo


def front_kernel(x3, w_ref, gain_ref, pk_ref, x_ref, lhs):
    x = x3[...].reshape(ROWS, D)
    x_ref[...] = x
    n, _ = normed(x)
    put_split(lhs, n * gain_ref[...][None, :])
    for jj in range(3):
        parts = []
        for kind in range(3):
            c0 = kind * D + 256 * jj
            r = dot_nn(lhs[...], w_ref[:, c0 : c0 + 256])
            parts.append(r[:ROWS] + r[ROWS:])
        for half in range(2):
            q, k, v = (a[:, 128 * half : 128 * half + 128] for a in parts)
            h = 4 * jj + 2 * half
            pk_ref[h, 0:ROWS, :] = pick(k, swap(v))
            pk_ref[h + 1, 0:ROWS, :] = pick(swap(k), v)
            top, bottom = q[:HALF], q[HALF:]
            pk_ref[h, ROWS:PACK, :] = pick(top, swap(bottom))
            pk_ref[h + 1, ROWS:PACK, :] = pick(swap(top), bottom)


def front(x, w, gain):
    return pl.pallas_call(
        front_kernel,
        out_shape=[jax.ShapeDtypeStruct((HEADS, PACK, 128), F32)] + [jax.ShapeDtypeStruct((ROWS, D), F32)],
        in_specs=[VM] * 3,
        out_specs=[VM] * 2,
        scratch_shapes=[pltpu.VMEM((2 * ROWS, D), BF16)],
        compiler_params=params(),
    )(x, w, gain)


def place_facts():
    p, s = lax.axis_index("pat"), lax.axis_index("seq")
    x, core = p // 2, lax.rem(p, 2)
    active, head = head_here(p, s)
    return p, s, x, core, active, head


def home_device(core, m):
    return core * 2 + lax.rem(m, 2), m // 2


def head_device(h, b):
    hx, hs = head_place(h)
    return hx * 2 + b, hs


def same(p, s, q, t):
    return jnp.logical_and(p == q, s == t)


def to(p, s):
    return {"pat": p, "seq": s}


def scatter_kernel(forward, pk, own, *rest):
    if forward:
        sib, send, recv, fsend, frecv = rest
    else:
        send, recv = rest
    p, s, x, core, active, head = place_facts()
    slot = s * 2 + core
    barrier = pltpu.get_barrier_semaphore()

    @pl.when(active)
    def _():
        def greet(m, carry):
            q, t = home_device(core, m)

            @pl.when(jnp.logical_not(same(p, s, q, t)))
            def _():
                pl.semaphore_signal(barrier, inc=1, device_id=to(q, t), device_id_type=MESH)

            return carry

        lax.fori_loop(0, HOMES, greet, 0)
        if forward:
            pl.semaphore_signal(barrier, inc=1, device_id=to(x * 2 + 1 - core, s), device_id_type=MESH)

    mine = jnp.logical_and(active, core == x)
    waits = HEADS - mine.astype(jnp.int32)
    if forward:
        waits = waits + active.astype(jnp.int32)
    pl.semaphore_wait(barrier, waits)

    def copy(h):
        q, t = head_device(h, x)
        return q, t, pltpu.make_async_remote_copy(
            src_ref=pk.at[h],
            dst_ref=own.at[slot],
            send_sem=send.at[h],
            recv_sem=recv.at[slot],
            device_id=to(q, t),
            device_id_type=MESH,
        )

    def start(j, carry):
        h = lax.rem(j + 3 * (s // 2) + 2 * p, HEADS)
        q, t, remote = copy(h)

        @pl.when(same(p, s, q, t))
        def _():
            pltpu.make_async_copy(pk.at[h], own.at[slot], recv.at[slot]).start()

        @pl.when(jnp.logical_not(same(p, s, q, t)))
        def _():
            remote.start()

        return carry

    lax.fori_loop(0, HEADS, start, 0)

    def passed(m):
        return pltpu.make_async_remote_copy(
            src_ref=own.at[m, pl.ds(0, ROWS), :],
            dst_ref=sib.at[m],
            send_sem=fsend.at[m],
            recv_sem=frecv.at[m],
            device_id=to(x * 2 + 1 - core, s),
            device_id_type=MESH,
        )

    @pl.when(active)
    def _():
        def arrive(m, carry):
            pltpu.make_async_copy(own.at[m], own.at[m], recv.at[m]).wait()
            if forward:
                passed(m).start()
            return carry

        lax.fori_loop(0, HOMES, arrive, 0)
        if forward:

            def finish(m, carry):
                passed(m).wait()
                return carry

            lax.fori_loop(0, HOMES, finish, 0)

    def sent(h, carry):
        q, t, remote = copy(h)

        @pl.when(jnp.logical_not(same(p, s, q, t)))
        def _():
            remote.wait_send()

        return carry

    lax.fori_loop(0, HEADS, sent, 0)


def to_heads(packets, forward, cid):
    rows = packets.shape[1]
    shapes = [jax.ShapeDtypeStruct((HOMES, rows, 128), F32)]
    sems = [pltpu.SemaphoreType.DMA((HEADS,)), pltpu.SemaphoreType.DMA((HOMES,))]
    if forward:
        shapes.append(jax.ShapeDtypeStruct((HOMES, ROWS, 128), F32))
        sems += [pltpu.SemaphoreType.DMA((HOMES,)), pltpu.SemaphoreType.DMA((HOMES,))]
    return pl.pallas_call(
        functools.partial(scatter_kernel, forward),
        out_shape=shapes,
        in_specs=[ANY],
        out_specs=[ANY] * len(shapes),
        scratch_shapes=sems,
        compiler_params=params(collective_id=cid, has_side_effects=True),
    )(packets)


def home_barrier(p, s, x, core, active, barrier, also_sibling):
    def greet(h, carry):
        q, t = head_device(h, x)

        @pl.when(jnp.logical_not(same(p, s, q, t)))
        def _():
            pl.semaphore_signal(barrier, inc=1, device_id=to(q, t), device_id_type=MESH)

        return carry

    lax.fori_loop(0, HEADS, greet, 0)

    @pl.when(active)
    def _():
        if also_sibling:
            pl.semaphore_signal(barrier, inc=1, device_id=to(x * 2 + 1 - core, s), device_id_type=MESH)
        mine = (core == x).astype(jnp.int32)
        pl.semaphore_wait(barrier, HOMES - mine + (1 if also_sibling else 0))


def gather_kernel(pk, rec, send, recv):
    p, s, x, core, active, head = place_facts()
    barrier = pltpu.get_barrier_semaphore()
    home_barrier(p, s, x, core, active, barrier, False)

    def copy(m):
        q, t = home_device(core, m)
        return q, t, pltpu.make_async_remote_copy(
            src_ref=pk.at[m],
            dst_ref=rec.at[head],
            send_sem=send.at[m],
            recv_sem=recv.at[head],
            device_id=to(q, t),
            device_id_type=MESH,
        )

    @pl.when(active)
    def _():
        def start(j, carry):
            m = lax.rem(j + 2 * s + 1, HOMES)
            q, t, remote = copy(m)

            @pl.when(same(p, s, q, t))
            def _():
                pltpu.make_async_copy(pk.at[m], rec.at[head], recv.at[head]).start()

            @pl.when(jnp.logical_not(same(p, s, q, t)))
            def _():
                remote.start()

            return carry

        lax.fori_loop(0, HOMES, start, 0)

    def arrive(h, carry):
        pltpu.make_async_copy(rec.at[h], rec.at[h], recv.at[h]).wait()
        return carry

    lax.fori_loop(0, HEADS, arrive, 0)

    @pl.when(active)
    def _():
        def sent(m, carry):
            q, t, remote = copy(m)

            @pl.when(jnp.logical_not(same(p, s, q, t)))
            def _():
                remote.wait_send()

            return carry

        lax.fori_loop(0, HOMES, sent, 0)


def to_homes(packets, cid):
    rows = packets.shape[1]
    return pl.pallas_call(
        gather_kernel,
        out_shape=jax.ShapeDtypeStruct((HEADS, rows, 128), F32),
        in_specs=[ANY],
        out_specs=ANY,
        scratch_shapes=[pltpu.SemaphoreType.DMA((HOMES,)), pltpu.SemaphoreType.DMA((HEADS,))],
        compiler_params=params(collective_id=cid, has_side_effects=True),
    )(packets)


def tile_positions(rows, columns, row_classes, column_classes, t_step, class_step):
    r = lax.broadcasted_iota(jnp.int32, (rows, columns), 0)
    q = lax.broadcasted_iota(jnp.int32, (rows, columns), 1)
    rn, qn = rows // row_classes, columns // column_classes
    return (r % rn) * t_step + (r // rn) * class_step, (q % qn) * t_step + (q // qn) * class_step


def key_bias(q_shape, k_shape, t_step, class_step, shift, keys_first):
    nq, nk = q_shape[0] * q_shape[1], k_shape[0] * k_shape[1]
    if keys_first:
        kp, qp = tile_positions(nk, nq, k_shape[0], q_shape[0], t_step, class_step)
    else:
        qp, kp = tile_positions(nq, nk, q_shape[0], k_shape[0], t_step, class_step)
    return jnp.where(kp - qp <= shift, 0.0, NEG).astype(F32)


def unpack_keys(own, sib, b, kvf):
    def one(m, carry):
        c = 2 * b + lax.rem(m, 2)
        d = 2 * (1 - b) + lax.rem(m, 2)
        t = pl.multiple_of((m // 2) * ROWS, 64)
        kvf[c, pl.ds(t, ROWS), :] = own[m, 0:ROWS, :]
        kvf[d, pl.ds(t, ROWS), :] = sib[m]
        return carry

    lax.fori_loop(0, HOMES, one, 0)


def unpack_pairs(src, first, dst, scale):
    def one(m, carry):
        t = pl.multiple_of((m // 2) * ROWS, 32)
        v = src[m, first : first + HALF, :] * scale
        w = swap(v)
        dst[lax.rem(m, 2), pl.ds(t, HALF), :] = pick(v, w)
        dst[lax.rem(m, 2), pl.ds(t + HALF, HALF), :] = pick(w, v)
        return carry

    lax.fori_loop(0, HOMES, one, 0)


def keys_and_values(kv):
    hi, lo = split32(kv)
    k2 = pick(hi, swap(lo))
    v2 = pick(swap(hi), lo)
    return k2, v2


def doubled(v):
    return jnp.concatenate([v, v], 1)


def query_quads(qq):
    hi, lo = split32(qq)
    return jnp.concatenate([pick(hi, lo).astype(BF16), pick(lo, hi).astype(BF16)], 1)


def class_facts4(o4, b):
    keys = ((lax.rem(o4, 4), o4 // 4), (lax.rem(o4 + 6, 4), (o4 + 6) // 4))
    first = (keys[0][0] // 2) == b
    query = (jnp.where(first, keys[0][0], keys[1][0]), jnp.where(first, keys[0][1], keys[1][1]))
    return keys, jnp.where(first, 0, 1), query


def forward_kernel(info, own, sib, ap, lse, sums, kvf, kc, vt, qf, qc, k4, vt4, q4, k5, vt5, q5, acc, ml, R, b1, b2, b3, b4):
    active = info[0] == 1
    b = info[1]
    offs = [info[2 + i] for i in range(PATTERNS)]
    sums[...] = jnp.zeros_like(sums)

    @pl.when(active)
    def _():
        unpack_keys(own, sib, b, kvf)
        unpack_pairs(own, ROWS, qf, 1.0 / math.sqrt(HD))

        def prepare(i, carry):
            c, t = i // 12, pl.multiple_of(lax.rem(i, 12) * 128, 128)
            k2, v2 = keys_and_values(kvf[c, pl.ds(t, 128), :])
            kc[c, pl.ds(t, 128), :] = k2.astype(BF16)
            vt[c, :, pl.ds(t, 128)] = v2.T.astype(BF16)
            return carry

        lax.fori_loop(0, 48, prepare, 0, unroll=2)

        def prepare_q(i, carry):
            c, t = i // 12, pl.multiple_of(lax.rem(i, 12) * 128, 128)
            qc[c, pl.ds(t, 128), :] = query_quads(qf[c, pl.ds(t, 128), :])
            return carry

        lax.fori_loop(0, 24, prepare_q, 0, unroll=2)

        keys4, e4, (qc4, qv4) = class_facts4(offs[3], b)
        kc5, kv5 = lax.rem(offs[4], 4), offs[4] // 4
        for blk in range(4):
            r = slice(128 * blk, 128 * blk + 128)
            for e in range(2):
                c, v = keys4[e]
                k2, v2 = keys_and_values(kvf[c, pl.ds(v + 384 * blk, 128, stride=3), :])
                k4[e, r, :] = k2.astype(BF16)
                vt4[e, :, r] = v2.T.astype(BF16)
            q4[r, :] = query_quads(qf[qc4 - 2 * b, pl.ds(qv4 + 384 * blk, 128, stride=3), :])
            k2, v2 = keys_and_values(kvf[kc5, pl.ds(kv5 + 384 * blk, 128, stride=3), :])
            k5[r, :] = k2.astype(BF16)
            vt5[:, r] = v2.T.astype(BF16)
            q5[r, :] = query_quads(qf[lax.rem(kc5, 2), pl.ds(kv5 + 384 * blk, 128, stride=3), :])

        b1[...] = key_bias((2, 128), (4, 128), 4, 1, 2 * b, True)
        b2[...] = key_bias((1, 256), (2, 256), 4, 2, 2 * b, True)
        b3[...] = key_bias((1, 256), (1, 256), 1, 1, 0, True)
        b4[...] = key_bias((1, 256), (2, 256), 12, 6, 6 * e4, True)

        def tile(g, q, k, vT, bias, first):
            s = dot_nt(doubled(k), q)
            if bias is not None:
                s = s + bias[...]
            m = jnp.max(s, 0, keepdims=True)
            if not first:
                old = ml[g, 0:1, :]
                m = jnp.maximum(old, m)
            p = jnp.exp(s - m)
            total = jnp.sum(p, 0, keepdims=True)
            hi, lo = split(p)
            new = dot_nn(doubled(vT), jnp.concatenate([hi, lo], 0))
            if first:
                acc[g] = new
            else:
                alpha = jnp.exp(old - m)
                acc[g] = acc[g] * alpha + new
                total = ml[g, 1:2, :] * alpha + total
            ml[g, 0:1, :] = m
            ml[g, 1:2, :] = total

        def closed(pattern, g):
            m, l = ml[g, 0:1, :], ml[g, 1:2, :]
            rows = m + jnp.log(l)
            sums[pattern : pattern + 1, :] += rows[:, :128] + rows[:, 128:]
            o = acc[g]
            return jnp.concatenate(
                [o[:HD] + o[HD:], jnp.broadcast_to(l, (32, 256)), jnp.broadcast_to(m, (32, 256))], 0
            ).T

        def q1(qb, carry):
            def at(g, blk):
                return pl.ds(pl.multiple_of(512 * g + 128 * blk, 128), 128)

            def step(kb, bias, first):
                for g in range(3):
                    ks = at(g, kb)
                    vT = jnp.concatenate([vt[c, :, ks] for c in range(4)], 1)
                    tile(g, qc[:, at(g, qb), :].reshape(256, 256), kc[:, ks, :].reshape(512, 128), vT, bias, first)

            step(qb, b1, True)

            def more(kb, inner):
                step(kb, None, False)
                return inner

            lax.fori_loop(0, qb, more, 0)
            for g in range(3):
                R[:, at(g, qb), :] = closed(0, g).reshape(2, 128, 128)
            return carry

        lax.fori_loop(0, 4, q1, 0)

        def merge(pattern, g, ci, rows):
            r0, r1 = R[ci, rows, :], closed(pattern, g)
            m0 = jnp.broadcast_to(r0[:, 96:97], r0.shape)
            m1 = jnp.broadcast_to(r1[:, 96:97], r1.shape)
            m = jnp.maximum(m0, m1)
            both = r0 * jnp.exp(m0 - m) + r1 * jnp.exp(m1 - m)
            lane = lax.broadcasted_iota(jnp.int32, r0.shape, 1)
            R[ci, rows, :] = jnp.where(lane < 96, both, m)

        def at256(blk):
            return pl.ds(pl.multiple_of(256 * blk, 128), 256)

        par = offs[1]

        def step2(g, q, kb, bias, first):
            ks = at256(kb)
            k = jnp.concatenate([kc[par, ks, :], kc[par + 2, ks, :]], 0)
            vT = jnp.concatenate([vt[par, :, ks], vt[par + 2, :, ks]], 1)
            tile(g, q, k, vT, bias, first)

        def q2(qb, carry):
            q = qc[par, at256(qb), :]
            step2(0, q, qb, b2, True)

            def more(kb, inner):
                step2(0, q, kb, None, False)
                return inner

            lax.fori_loop(jnp.where(qb >= 4, 4, 0), qb, more, 0)
            merge(1, 0, par, at256(qb))
            return carry

        lax.fori_loop(0, TOTAL // 256, q2, 0)

        o3 = offs[2]

        @pl.when(o3 // 2 == b)
        def _():
            ci = lax.rem(o3, 2)

            def step3(g, qb, kb, bias, first):
                tile(g, qc[ci, at256(qb), :], kc[o3, at256(kb), :], vt[o3, :, at256(kb)], bias, first)

            def q3(pair, carry):
                q0, q1_ = 2 * pair, 2 * pair + 1
                step3(0, q0, q0, b3, True)
                step3(1, q1_, q1_, b3, True)

                def more(kb, inner):
                    step3(0, q0, kb, None, False)
                    step3(1, q1_, kb, None, False)
                    return inner

                lax.fori_loop(0, q0, more, 0)
                step3(1, q1_, q0, None, False)
                merge(2, 0, ci, at256(q0))
                merge(2, 1, ci, at256(q1_))
                return carry

            lax.fori_loop(0, TOTAL // 512, q3, 0)

        for kb in range(2):
            for qb in range(kb, 2):
                order = qb - kb
                ks = slice(256 * order, 256 * order + 256)
                tile(
                    qb,
                    q4[256 * qb : 256 * qb + 256, :],
                    k4[:, ks, :].reshape(512, 128),
                    jnp.concatenate([vt4[0, :, ks], vt4[1, :, ks]], 1),
                    b4 if order == qb else None,
                    kb == 0,
                )
        for qb in range(2):
            merge(3, qb, qc4 - 2 * b, pl.ds(qv4 + 768 * qb, 256, stride=3))

        @pl.when(kc5 // 2 == b)
        def _():
            for kb in range(2):
                for qb in range(kb, 2):
                    order = qb - kb
                    ks = slice(256 * order, 256 * order + 256)
                    tile(
                        qb,
                        q5[256 * qb : 256 * qb + 256, :],
                        k5[ks, :],
                        vt5[:, ks],
                        b3 if order == qb else None,
                        kb == 0,
                    )
            for qb in range(2):
                merge(4, qb, lax.rem(kc5, 2), pl.ds(kv5 + 768 * qb, 256, stride=3))

        def finish(m, carry):
            ci = lax.rem(m, 2)
            rows = pl.ds(pl.multiple_of((m // 2) * ROWS, 64), ROWS)
            r = R[ci, rows, :]
            l = jnp.broadcast_to(r[:, HD : HD + 1], r.shape)
            out = r / l
            ap[m] = pick(out[:HALF], swap(out[HALF:]))
            lse[ci, rows, :] = jnp.broadcast_to(r[:, 96:97], r.shape) + jnp.log(l)
            return carry

        lax.fori_loop(0, HOMES, finish, 0, unroll=2)
        sums[...] = jnp.broadcast_to(jnp.sum(sums[...], -1, keepdims=True), (8, 128))


def attention_forward(info, own, sib):
    keys = pltpu.VMEM((4, TOTAL, 128), BF16)
    turned = pltpu.VMEM((4, 128, TOTAL), BF16)
    state = pltpu.VMEM((2, TOTAL, 128), F32)
    return pl.pallas_call(
        forward_kernel,
        out_shape=[
            jax.ShapeDtypeStruct((HOMES, HALF, 128), F32),
            jax.ShapeDtypeStruct((2, TOTAL, 128), F32),
            jax.ShapeDtypeStruct((8, 128), F32),
        ],
        in_specs=[SM, VM, VM],
        out_specs=[VM, VM, VM],
        scratch_shapes=[
            pltpu.VMEM((4, TOTAL, 128), F32),
            keys,
            turned,
            state,
            pltpu.VMEM((2, TOTAL, 256), BF16),
            pltpu.VMEM((2, THIRD, 128), BF16),
            pltpu.VMEM((2, 128, THIRD), BF16),
            pltpu.VMEM((THIRD, 256), BF16),
            pltpu.VMEM((THIRD, 128), BF16),
            pltpu.VMEM((128, THIRD), BF16),
            pltpu.VMEM((THIRD, 256), BF16),
            pltpu.VMEM((3, 128, 256), F32),
            pltpu.VMEM((3, 8, 256), F32),
            state,
            pltpu.VMEM((512, 256), F32),
            pltpu.VMEM((512, 256), F32),
            pltpu.VMEM((256, 256), F32),
            pltpu.VMEM((512, 256), F32),
        ],
        compiler_params=params(),
    )(info, own, sib)


class Place:
    def __init__(self):
        p, s = lax.axis_index("pat"), lax.axis_index("seq")
        self.p, self.s = p, s
        self.x, self.core, self.z, self.y = p // 2, lax.rem(p, 2), s // 2, lax.rem(s, 2)
        self.peer = to(self.x * 2 + 1 - self.core, s)
        self.xn = to((1 - self.x) * 2 + self.core, s)
        self.yn = to(p, self.z * 2 + 1 - self.y)
        self.left, self.right = to(p, s - 2), to(p, s + 2)

    def greet(self, barrier, line=True):
        for d in (self.peer, self.xn, self.yn):
            pl.semaphore_signal(barrier, inc=1, device_id=d, device_id_type=MESH)
        if not line:
            return 3

        @pl.when(self.z > 0)
        def _():
            pl.semaphore_signal(barrier, inc=1, device_id=self.left, device_id_type=MESH)

        @pl.when(self.z < 3)
        def _():
            pl.semaphore_signal(barrier, inc=1, device_id=self.right, device_id_type=MESH)

        return 3 + (self.z > 0).astype(jnp.int32) + (self.z < 3).astype(jnp.int32)


def remote(src, dst, a, b, d):
    return pltpu.make_async_remote_copy(
        src_ref=src, dst_ref=dst, send_sem=a, recv_sem=b, device_id=d, device_id_type=MESH
    )


def add_in(dst, src):
    lead = dst.shape[:-2]

    def one(i, carry):
        index = []
        for d in reversed(lead):
            index.insert(0, lax.rem(i, d))
            i = i // d
        dst[tuple(index)] += src[tuple(index)]
        return carry

    lax.fori_loop(0, math.prod(lead), one, 0)


class Sems:
    NAMES = ("sc", "rc", "s1", "r1", "s2", "r2", "sl", "rl", "sr", "rr")

    def __init__(self, refs):
        for name, ref in zip(self.NAMES, refs):
            setattr(self, name, ref)

    @staticmethod
    def scratch(n):
        dma = pltpu.SemaphoreType.DMA
        return [dma((n, 2)), dma((n, 2))] + [dma((n,)) for _ in range(8)]


class Chunk:
    def __init__(self, place, k, x_first, sems, b0=None, b1=None, b2=None, bl=None, br=None, part=None, put=None):
        self.at, self.k, self.x_first, self.sems = place, k, x_first, sems
        self.b0, self.b1, self.b2, self.bl, self.br = b0, b1, b2, bl, br
        self.part, self.put = part, put

    def core(self, i):
        k, m = self.k, self.sems
        return remote(self.part(i, 1 - self.at.core), self.b0.at[i], m.sc.at[k, i], m.rc.at[k, i], self.at.peer)

    def one(self):
        k, at, m = self.k, self.at, self.sems
        if self.x_first:
            return remote(self.b0.at[1 - at.x], self.b1, m.s1.at[k], m.r1.at[k], at.xn)
        return remote(self.b0.at[:, :, 1 - at.y], self.b1, m.s1.at[k], m.r1.at[k], at.yn)

    def two(self):
        k, at, m = self.k, self.at, self.sems
        if self.x_first:
            return remote(self.b1.at[:, 1 - at.y], self.b2, m.s2.at[k], m.r2.at[k], at.yn)
        return remote(self.b1.at[1 - at.x], self.b2, m.s2.at[k], m.r2.at[k], at.xn)

    def rightward(self, i):
        k, part, m = self.k, pl.ds(i + 1, 3 - i), self.sems
        src = self.b2 if i == 0 else self.bl
        return remote(src.at[part], self.bl.at[part], m.sr.at[k], m.rl.at[k], self.at.right)

    def leftward(self, i):
        k, part, m = self.k, pl.ds(0, i), self.sems
        src = self.b2 if i == 3 else self.br
        return remote(src.at[part], self.br.at[part], m.sl.at[k], m.rr.at[k], self.at.left)

    def own_core(self, i):
        self.core(i).wait_recv()
        add_in(self.b0.at[i], self.part(i, self.at.core))

    def stage1(self):
        for i in range(2):
            self.own_core(i)
        self.one().start()

    def arrived(self):
        self.one().wait_recv()
        add_in(self.b1, self.b0.at[self.at.x] if self.x_first else self.b0.at[:, :, self.at.y])

    def stage2(self):
        self.arrived()
        self.two().start()

    def stage3(self):
        self.two().wait_recv()
        add_in(self.b2, self.b1.at[:, self.at.y] if self.x_first else self.b1.at[self.at.x])

        @pl.when(self.at.z == 0)
        def _():
            self.rightward(0).start()

        @pl.when(self.at.z == 3)
        def _():
            self.leftward(3).start()

    def stage4(self):
        @pl.when(self.at.z == 1)
        def _():
            self.rightward(0).wait_recv()
            self.bl[2:4] += self.b2[2:4]
            self.rightward(1).start()

        @pl.when(self.at.z == 2)
        def _():
            self.leftward(3).wait_recv()
            self.br[0:2] += self.b2[0:2]
            self.leftward(2).start()

    def stage5(self):
        @pl.when(self.at.z == 2)
        def _():
            self.rightward(1).wait_recv()
            self.bl[3:4] += self.b2[3:4]
            self.rightward(2).start()

        @pl.when(self.at.z == 1)
        def _():
            self.leftward(2).wait_recv()
            self.br[0:1] += self.b2[0:1]
            self.leftward(1).start()

    def stage6(self):
        @pl.when(self.at.z == 3)
        def _():
            self.rightward(2).wait_recv()
            self.put(self.b2[3] + self.bl[3])

        @pl.when(self.at.z == 0)
        def _():
            self.leftward(1).wait_recv()
            self.put(self.b2[0] + self.br[0])

        @pl.when(self.at.z == 1)
        def _():
            self.put(self.b2[1] + self.bl[1] + self.br[1])

        @pl.when(self.at.z == 2)
        def _():
            self.put(self.b2[2] + self.bl[2] + self.br[2])

    def line_sent(self):
        for i in range(4):

            @pl.when(self.at.z == i)
            def _(i=i):
                if i < 3:
                    self.rightward(i).wait_send()
                if i > 0:
                    self.leftward(i).wait_send()


class Reducer:
    def __init__(self, place, n, part, scratch, put):
        self.place, self.n, self.part, self.put = place, n, part, put
        self.c0, self.c1a, self.c1b, self.c2, self.zl, self.zr = scratch[:6]
        self.sems = Sems(scratch[6:16])
        self.pairs = (n + 1) // 2

    @staticmethod
    def scratch(n, rows):
        bufs = [(n, 2, 4, 2), ((n + 1) // 2, 4, 2), (max(n // 2, 1), 2, 4), (n, 4), (n, 4), (n, 4)]
        return [pltpu.VMEM(b + (rows, D), F32) for b in bufs] + Sems.scratch(n)

    def chunk(self, k, parity):
        return Chunk(
            self.place,
            k,
            parity == 0,
            self.sems,
            self.c0.at[k],
            (self.c1b if parity else self.c1a).at[k // 2],
            self.c2.at[k],
            self.zl.at[k],
            self.zr.at[k],
            self.part(k),
            lambda v: self.put(k, v),
        )

    def send(self, first, after):
        for k in range(first, after):
            for i in range(2):
                self.chunk(jnp.int32(k), 0).core(i).start()

    def one(self, stage, pair):
        for parity in range(2):
            k = jnp.int32(2 * pair + parity)

            @pl.when(jnp.logical_and(k >= 0, k < self.n))
            def _(k=k, parity=parity):
                getattr(self.chunk(k, parity), f"stage{stage}")()

    def early(self, pair):
        self.one(1, pair)

    def step(self, tau):
        self.one(1, tau)
        for stage in range(2, 7):
            self.one(stage, tau - stage)

    def finish(self):
        def one(k, carry):
            for parity in range(2):

                @pl.when(lax.rem(k, 2) == parity)
                def _(parity=parity):
                    c = self.chunk(k, parity)
                    for i in range(2):
                        c.core(i).wait_send()
                    c.one().wait_send()
                    c.two().wait_send()
                    c.line_sent()

            return carry

        lax.fori_loop(0, self.n, one, 0)


class SmallSum:
    def __init__(self, place, S, bufs, send, recv, put):
        self.at, self.S, self.send, self.recv, self.put = place, S, send, recv, put
        self.d0, self.d1, self.d2, self.dl, self.dr, self.t1, self.t2, self.t3, self.fl, self.fr = bufs

    @staticmethod
    def scratch():
        return [pltpu.VMEM((8, D), F32)] * 10 + [pltpu.SemaphoreType.DMA((5,)), pltpu.SemaphoreType.DMA((5,))]

    def hop(self, src, dst, i, d):
        return remote(src, dst, self.send.at[i], self.recv.at[i], d)

    def core(self):
        return self.hop(self.S, self.d0, 0, self.at.peer)

    def along_x(self):
        return self.hop(self.t1, self.d1, 1, self.at.xn)

    def along_y(self):
        return self.hop(self.t2, self.d2, 2, self.at.yn)

    def rightward(self, i):
        return self.hop(self.t3 if i == 0 else self.fl, self.dl, 3, self.at.right)

    def leftward(self, i):
        return self.hop(self.t3 if i == 3 else self.fr, self.dr, 4, self.at.left)

    def stage1(self):
        self.core().wait_recv()
        self.t1[...] = self.S[...] + self.d0[...]
        self.along_x().start()

    def stage2(self):
        self.along_x().wait_recv()
        self.t2[...] = self.t1[...] + self.d1[...]
        self.along_y().start()

    def stage3(self):
        self.along_y().wait_recv()
        self.t3[...] = self.t2[...] + self.d2[...]

        @pl.when(self.at.z == 0)
        def _():
            self.rightward(0).start()

        @pl.when(self.at.z == 3)
        def _():
            self.leftward(3).start()

    def from_left(self, i):
        self.rightward(i).wait_recv()
        self.fl[...] = self.dl[...] + self.t3[...]

    def from_right(self, i):
        self.leftward(i).wait_recv()
        self.fr[...] = self.dr[...] + self.t3[...]

    def stage4(self):
        @pl.when(self.at.z == 1)
        def _():
            self.from_left(0)
            self.rightward(1).start()

        @pl.when(self.at.z == 2)
        def _():
            self.from_right(3)
            self.leftward(2).start()

    def stage5(self):
        @pl.when(self.at.z == 2)
        def _():
            self.from_left(1)
            self.rightward(2).start()

        @pl.when(self.at.z == 1)
        def _():
            self.from_right(2)
            self.leftward(1).start()

    def stage6(self):
        @pl.when(self.at.z == 3)
        def _():
            self.from_left(2)
            self.put(self.fl[...])

        @pl.when(self.at.z == 0)
        def _():
            self.from_right(1)
            self.put(self.fr[...])

        @pl.when(jnp.logical_or(self.at.z == 1, self.at.z == 2))
        def _():
            self.put(self.fl[...] + self.dr[...])

    def finish(self):
        for c in (self.core(), self.along_x(), self.along_y()):
            c.wait_send()
        for i in range(4):

            @pl.when(self.at.z == i)
            def _(i=i):
                if i < 3:
                    self.rightward(i).wait_send()
                if i > 0:
                    self.leftward(i).wait_send()


def small_outputs(place, counts, outs, tot):
    ga, gi, gf, gh, means = outs

    def put(v):
        tot[...] = v
        d = place.p * RUNS + place.s
        for i, ref in enumerate((ga, gi, gf)):
            ref[...] = pltpu.roll(tot[i : i + 1, :], D - PIECE * d, 1)[:, :PIECE]
        row = tot[pl.ds(3 + d // 8, 1), :]
        gh[...] = pltpu.roll(row, D - 4 * PIECE * lax.rem(d, 8), 1)[:, : 4 * PIECE]
        lane = lax.broadcasted_iota(jnp.int32, (1, 128), 1)
        scale = jnp.full((1, 128), counts[0], F32)
        for i in range(1, PATTERNS):
            scale = jnp.where(lane == i, counts[i], scale)
        means[...] = (tot[7:8, :128] / scale)[:, :PATTERNS]

    return put


N_PIECES = 9
SUB = 8


def finish_kernel(counts, rec, x_ref, dy1_ref, w, ga1, S_in, gx, g_qkv, ga, gi, gf, gh, means, dqkv, lhs, th, tl, r_hi, r_lo, tiles, S, tot, *scratch):
    place = Place()
    barrier = pltpu.get_barrier_semaphore()
    expected = place.greet(barrier)
    for j in range(HEADS // 2):
        u, v = rec[2 * j, ROWS:PACK, :], rec[2 * j + 1, ROWS:PACK, :]
        cols = slice(128 * j, 128 * j + 128)
        dqkv[0:HALF, cols] = pick(u, swap(v))
        dqkv[HALF:ROWS, cols] = pick(swap(u), v)
        u, v = rec[2 * j, 0:ROWS, :], rec[2 * j + 1, 0:ROWS, :]
        dqkv[:, D + 128 * j : D + 128 * j + 128] = pick(u, swap(v))
        dqkv[:, 2 * D + 128 * j : 2 * D + 128 * j + 128] = pick(swap(u), v)
    gain = ga1[...][None, :]
    n, rs = normed(x_ref[...])
    put_turned(th, tl, n * gain)

    def part(k):
        rows = pl.ds(pl.multiple_of(lax.rem(k, 3) * SUB, SUB), SUB)
        return lambda i, c: tiles.at[k // 3, i, c, :, :, rows, :]

    def put(k, v):
        g_qkv[
            pl.ds(pl.multiple_of(lax.rem(k, 3) * SUB, SUB), SUB), pl.ds(pl.multiple_of((k // 3) * D, D), D)
        ] = v

    n_r = 16
    big = Reducer(place, N_PIECES, part, scratch[:n_r], put)
    rest = scratch[n_r:]
    small = SmallSum(
        place, S, rest[:10], rest[10], rest[11], small_outputs(place, counts, (ga, gi, gf, gh, means), tot)
    )
    for j in range(3):
        r_hi[...], r_lo[...] = split(dqkv[:, D * j : D * j + D])

        def one(i, carry):
            rows = pl.ds(pl.multiple_of(i * 2 * ROWS, 128), 2 * ROWS)
            h, l = th[rows, :], tl[rows, :]
            v = dot_nn(h, r_hi[...]) + dot_nn(h, r_lo[...]) + dot_nn(l, r_hi[...])
            tiles[j, i] = v.reshape(2, 4, 2, PIECE, D)
            return carry

        lax.fori_loop(0, 2, one, 0)
        if j == 0:
            pl.semaphore_wait(barrier, expected)
        big.send(3 * j, 3 * j + 3)
        if j > 0:
            big.early(j - 1)
    e = None
    for j in range(3):
        cols = slice(D * j, D * j + D)
        put_split(lhs, dqkv[:, cols])
        more = halves_sum(dot_nt(lhs[...], w[:, cols]))
        e = more if e is None else e + more
        if j == 0:
            big.step(2)
    S[...] = S_in[...]
    S[0:1, :] = jnp.sum(e * n, 0, keepdims=True)
    small.core().start()
    gx[...] = (dy1_ref[...] + norm_back(e * gain, n, rs)).reshape(ROWS, 1, D)
    small.stage1()

    def step(tau, carry):
        for stage in range(2, 7):

            @pl.when(tau == stage + 1)
            def _(stage=stage):
                getattr(small, f"stage{stage}")()

        big.step(tau)
        return carry

    lax.fori_loop(3, big.pairs + 6, step, 0)

    big.finish()
    small.finish()


def finish(rec, x, dy1, w, ga, S, counts, cid):
    return pl.pallas_call(
        functools.partial(finish_kernel, counts),
        out_shape=[jax.ShapeDtypeStruct((ROWS, 1, D), F32), jax.ShapeDtypeStruct((PIECE, 3 * D), F32)]
        + [jax.ShapeDtypeStruct((1, n), F32) for n in (PIECE, PIECE, PIECE, 4 * PIECE, PATTERNS)],
        in_specs=[VM] * 6,
        out_specs=[VM] * 7,
        scratch_shapes=[
            pltpu.VMEM((ROWS, 3 * D), F32),
            pltpu.VMEM((2 * ROWS, D), BF16),
            pltpu.VMEM((D, ROWS), BF16),
            pltpu.VMEM((D, ROWS), BF16),
            pltpu.VMEM((ROWS, D), BF16),
            pltpu.VMEM((ROWS, D), BF16),
            pltpu.VMEM((3, 2, 2, 4, 2, PIECE, D), F32),
            pltpu.VMEM((8, D), F32),
            pltpu.VMEM((8, D), F32),
        ]
        + Reducer.scratch(N_PIECES, SUB)
        + SmallSum.scratch(),
        compiler_params=params(collective_id=cid, has_side_effects=True),
    )(rec, x, dy1, w, ga, S)


def deliver_kernel(*refs):
    n = len(refs) // 2
    for src, dst in zip(refs[:n], refs[n:]):
        dst[...] = src[...]


def deliver(*arrays):
    return pl.pallas_call(
        deliver_kernel,
        out_shape=[jax.ShapeDtypeStruct(v.shape, v.dtype) for v in arrays],
        in_specs=[VM] * len(arrays),
        out_specs=[VM] * len(arrays),
        compiler_params=params(),
    )(*arrays)


def rows_from_pairs(rec, dst):
    for j in range(HEADS // 2):
        u, v = rec[2 * j], rec[2 * j + 1]
        cols = slice(128 * j, 128 * j + 128)
        dst[0:HALF, cols] = pick(u, swap(v))
        dst[HALF:ROWS, cols] = pick(swap(u), v)


def pairs_from_rows(src, dst):
    for j in range(HEADS // 2):
        top = src[0:HALF, 128 * j : 128 * j + 128]
        bottom = src[HALF:ROWS, 128 * j : 128 * j + 128]
        dst[2 * j] = pick(top, swap(bottom))
        dst[2 * j + 1] = pick(swap(top), bottom)


def halves_sum(r):
    return r[:ROWS] + r[ROWS:]


def norm_back(f, n, rs):
    return (f - jnp.mean(f, -1, keepdims=True) - n * jnp.mean(f * n, -1, keepdims=True)) * rs


def put_turned(hi_ref, lo_ref, v):
    for j in range(D // 128):
        t = v[:, 128 * j : 128 * j + 128].T
        hi, lo = split(t)
        hi_ref[128 * j : 128 * j + 128, :] = hi
        lo_ref[128 * j : 128 * j + 128, :] = lo


class ToHeads:
    def __init__(self, pk, rec, send, recv):
        self.pk, self.rec, self.send, self.recv = pk, rec, send, recv
        self.facts = place_facts()

    def greet(self):
        p, s, x, core, active, head = self.facts
        barrier = pltpu.get_barrier_semaphore()

        @pl.when(active)
        def _():
            def one(m, carry):
                q, t = home_device(core, m)

                @pl.when(jnp.logical_not(same(p, s, q, t)))
                def _():
                    pl.semaphore_signal(barrier, inc=1, device_id=to(q, t), device_id_type=MESH)

                return carry

            lax.fori_loop(0, HOMES, one, 0)

    def copy(self, h):
        p, s, x, core, active, head = self.facts
        slot = s * 2 + core
        q, t = head_device(h, x)
        far = pltpu.make_async_remote_copy(
            src_ref=self.pk.at[h],
            dst_ref=self.rec.at[slot],
            send_sem=self.send.at[h],
            recv_sem=self.recv.at[slot],
            device_id=to(q, t),
            device_id_type=MESH,
        )
        return same(p, s, q, t), lambda: pltpu.make_async_copy(self.pk.at[h], self.rec.at[slot], self.recv.at[slot]), far

    def wait(self, others):
        p, s, x, core, active, head = self.facts
        mine = jnp.logical_and(active, core == x).astype(jnp.int32)
        pl.semaphore_wait(pltpu.get_barrier_semaphore(), HEADS + others - mine)

    def start(self):
        p, s, x, core, active, head = self.facts

        def one(j, carry):
            here, near, far = self.copy(lax.rem(j + 3 * (s // 2) + 2 * p, HEADS))

            @pl.when(here)
            def _():
                near().start()

            @pl.when(jnp.logical_not(here))
            def _():
                far.start()

            return carry

        lax.fori_loop(0, HEADS, one, 0)

    def finish(self):
        active = self.facts[4]

        @pl.when(active)
        def _():
            def arrive(m, carry):
                pltpu.make_async_copy(self.rec.at[m], self.rec.at[m], self.recv.at[m]).wait()
                return carry

            lax.fori_loop(0, HOMES, arrive, 0)

        def sent(h, carry):
            here, near, far = self.copy(h)

            @pl.when(jnp.logical_not(here))
            def _():
                far.wait_send()

            return carry

        lax.fori_loop(0, HEADS, sent, 0)


FT = 512


def product(hi, lo, r_hi, r_lo, put):
    def one(i, carry):
        rows = pl.ds(pl.multiple_of(i * 2 * ROWS, 128), 2 * ROWS)
        h, l = hi[rows, :], lo[rows, :]
        put(i, dot_nn(h, r_hi[...]) + dot_nn(h, r_lo[...]) + dot_nn(l, r_hi[...]))
        return carry

    lax.fori_loop(0, 2, one, 0)


N_FF = 9
N_COLS = 5


def ff_kernel(rec, x_ref, g3, wo, wu, wd, gi1, gf1, gh1, sums, out3, drec, dy1_ref, S, C0, C1a, C1b, dap, lhs, lhs2, gi, gf, gh, gh_g, g_ref, out_ref, V, N1, U, GP, E, ACC, th, tl, r_hi, r_lo, cols_t, rows_t, c0, c1a, c1b, osem, dsend, drecv, *rsems):
    place = Place()
    sems = Sems(rsems)
    travel = ToHeads(dap, drec, dsend, drecv)
    travel.greet()
    place.greet(pltpu.get_barrier_semaphore(), False)

    def chunk(k, part=None):
        x_first = k % 2 == 0
        b1 = None if k < N_COLS else (c1a if x_first else c1b).at[(k - N_COLS) // 2]
        return Chunk(place, k, x_first, sems, c0.at[k], b1, part=part)

    for wide, flat in ((gi, gi1), (gf, gf1), (gh, gh1)):
        wide[...] = flat[...][None, :]
    g_ref[...] = g3[...].reshape(ROWS, D)
    rows_from_pairs(rec, V)
    na, rs_a = normed(V[...])
    V[...] = na
    put_split(lhs, na * gi[...])
    for j in range(3):
        cols = slice(256 * j, 256 * j + 256)
        N1[:, cols] = x_ref[:, cols] + halves_sum(dot_nn(lhs[...], wo[:, cols]))
    y1 = N1[...]
    out_ref[...] = y1
    ny, rs_y = normed(y1)
    N1[...] = ny
    put_split(lhs, ny * gf[...])

    def up(j, su):
        cols = pl.ds(pl.multiple_of(j * FT, FT), FT)
        z = halves_sum(dot_nn(lhs[...], wu[:, cols]))
        phi = 0.5 * (1.0 + lax.erf(z * math.sqrt(0.5)))
        u = z * phi
        U[:, cols] = u
        GP[:, cols] = phi + z * jnp.exp(-0.5 * z * z) * (1.0 / math.sqrt(2.0 * math.pi))
        return su + jnp.sum(u, -1, keepdims=True)

    zero = jnp.zeros((ROWS, 1), F32)
    mean = lax.fori_loop(0, FF // FT, up, zero) * (1.0 / FF)

    def spread(j, sv):
        cols = pl.ds(pl.multiple_of(j * FT, FT), FT)
        c = U[:, cols] - mean
        return sv + jnp.sum(c * c, -1, keepdims=True)

    rs_u = lax.rsqrt(lax.fori_loop(0, FF // FT, spread, zero) * (1.0 / FF) + LN_EPSILON)
    ACC[...] = jnp.zeros_like(ACC)

    def lower(j, carry):
        cols = pl.ds(pl.multiple_of(j * FT, FT), FT)
        n = (U[:, cols] - mean) * rs_u
        U[:, cols] = n
        put_split(lhs2, n * gh[:, cols])
        ACC[...] += halves_sum(dot_nn(lhs2[...], wd[cols, :]))
        return carry

    lax.fori_loop(0, FF // FT, lower, 0)
    out3[...] = (out_ref[...] + ACC[...]).reshape(ROWS, 1, D)

    travel.wait(3)
    r_hi[...], r_lo[...] = split(g_ref[...])

    def down(j, q):
        return chunk(N_COLS + q, lambda i, c: rows_t.at[j % 2, :, :, q])

    for j in range(5):
        if j < 4:
            cols = slice(D * j, D * j + D)
            put_turned(th, tl, U[:, cols] * gh[:, cols])
            if j >= 2:

                @pl.when(place.core != j % 2)
                def _(j=j):
                    for q in range(4):
                        down(j - 2, q).core(j // 2 - 1).wait_send()

            def put(i, v, j=j):
                rows_t[j % 2, pl.ds(2 * i, 2)] = v.reshape(2, 2, 4, PIECE, D)

            product(th, tl, r_hi, r_lo, put)

            @pl.when(place.core != j % 2)
            def _(j=j):
                for q in range(4):
                    down(j, q).core(j // 2).start()

        if j > 0:

            @pl.when(place.core == (j - 1) % 2)
            def _(j=j - 1):
                for q in range(4):
                    down(j, q).own_core(j // 2)

    for k in range(N_COLS, N_FF):
        chunk(k).one().start()

    put_split(lhs, g_ref[...])

    def back_down(j, sums):
        cols = pl.ds(pl.multiple_of(j * FT, FT), FT)
        e = halves_sum(dot_nt(lhs[...], wd[cols, :]))
        n = U[:, cols]
        gh_g[:, cols] = jnp.sum(e * n, 0, keepdims=True)
        f = e * gh[:, cols]
        E[:, cols] = f
        return sums[0] + jnp.sum(f, -1, keepdims=True), sums[1] + jnp.sum(f * n, -1, keepdims=True)

    sf, sfn = lax.fori_loop(0, FF // FT, back_down, (zero, zero))
    mf, mfn = sf * (1.0 / FF), sfn * (1.0 / FF)
    ACC[...] = jnp.zeros_like(ACC)

    def back_up(j, carry):
        cols = pl.ds(pl.multiple_of(j * FT, FT), FT)
        dz = (E[:, cols] - mf - U[:, cols] * mfn) * rs_u * GP[:, cols]
        E[:, cols] = dz
        put_split(lhs2, dz)
        ACC[...] += halves_sum(dot_nt(lhs2[...], wu[:, cols]))
        return carry

    lax.fori_loop(0, FF // FT, back_up, 0)
    e = ACC[...]
    ny = N1[...]
    S[2:3, :] = jnp.sum(e * ny, 0, keepdims=True)
    dy1 = g_ref[...] + norm_back(e * gf[...], ny, rs_y)
    dy1_ref[...] = dy1
    put_split(lhs, dy1)
    for j in range(3):
        cols = slice(256 * j, 256 * j + 256)
        ACC[:, cols] = halves_sum(dot_nt(lhs[...], wo[cols, :]))
    e = ACC[...]
    na = V[...]
    S[1:2, :] = jnp.sum(e * na, 0, keepdims=True)
    S[0:1, :] = jnp.zeros((1, D), F32)
    for j in range(4):
        S[3 + j : 4 + j, :] = gh_g[:, D * j : D * j + D]
    lane = lax.broadcasted_iota(jnp.int32, (1, 128), 1)
    S[7:8, :] = jnp.zeros((1, D), F32)
    S[7:8, 0:128] = sum(jnp.where(lane == i, sums[i : i + 1, :], 0.0) for i in range(PATTERNS))
    ACC[...] = norm_back(e * gi[...], na, rs_a)
    pairs_from_rows(ACC, dap)
    travel.start()

    def column(k):
        return chunk(k, lambda i, c: cols_t.at[k % 2, i, c])

    def out_copy(k):
        return pltpu.make_async_copy(c0.at[k], C0.at[k], osem.at[k])

    put_turned(th, tl, na * gi[...])
    r_hi[...], r_lo[...] = split(dy1)
    for k in range(N_COLS + 1):
        if k < N_COLS:
            if k >= 2:
                for i in range(2):
                    column(k - 2).core(i).wait_send()

            def put(i, v, k=k):
                cols_t[k % 2, i] = v.reshape(2, 4, 2, PIECE, D)

            product(th, tl, r_hi, r_lo, put)
            for i in range(2):
                column(k).core(i).start()
            if k == 0:
                put_turned(th, tl, ny * gf[...])
            if k + 1 < N_COLS:
                r_hi[...], r_lo[...] = split(E[:, D * k : D * k + D])
        if k > 0:
            for i in range(2):
                column(k - 1).own_core(i)
            out_copy(k - 1).start()

    def c1_copy(k):
        b1, out = (c1a, C1a) if k % 2 == 0 else (c1b, C1b)
        i = (k - N_COLS) // 2
        return pltpu.make_async_copy(b1.at[i], out.at[i], osem.at[k])

    for k in range(N_COLS, N_FF):
        chunk(k).arrived()
        c1_copy(k).start()
    travel.finish()
    for k in range(N_COLS - 2, N_COLS):
        for i in range(2):
            column(k).core(i).wait_send()
    for j in range(2, 4):

        @pl.when(place.core != j % 2)
        def _(j=j):
            for q in range(4):
                down(j, q).core(j // 2).wait_send()

    for k in range(N_COLS):
        out_copy(k).wait()
    for k in range(N_COLS, N_FF):
        chunk(k).one().wait_send()
        c1_copy(k).wait()


def feed_forward(rec, x, g, wo, wu, wd, gi, gf, gh, sums):
    act = jax.ShapeDtypeStruct((ROWS, D), F32)
    wide = pltpu.VMEM((ROWS, FF), F32)
    thin = pltpu.VMEM((ROWS, D), F32)
    return pl.pallas_call(
        ff_kernel,
        out_shape=[
            jax.ShapeDtypeStruct((ROWS, 1, D), F32),
            jax.ShapeDtypeStruct((HOMES, HALF, 128), F32),
            act,
            jax.ShapeDtypeStruct((8, D), F32),
            jax.ShapeDtypeStruct((N_COLS, 2, 4, 2, PIECE, D), F32),
            jax.ShapeDtypeStruct((2, 4, 2, PIECE, D), F32),
            jax.ShapeDtypeStruct((2, 2, 4, PIECE, D), F32),
        ],
        in_specs=[VM] * 10,
        out_specs=[VM, ANY, VM, VM, ANY, ANY, ANY],
        scratch_shapes=[
            pltpu.VMEM((HEADS, HALF, 128), F32),
            pltpu.VMEM((2 * ROWS, D), BF16),
            pltpu.VMEM((2 * ROWS, FT), BF16),
            pltpu.VMEM((1, D), F32),
            pltpu.VMEM((1, D), F32),
            pltpu.VMEM((1, FF), F32),
            pltpu.VMEM((1, FF), F32),
            thin,
            thin,
            thin,
            thin,
            wide,
            wide,
            wide,
            thin,
        ]
        + [
            pltpu.VMEM((D, ROWS), BF16),
            pltpu.VMEM((D, ROWS), BF16),
            pltpu.VMEM((ROWS, D), BF16),
            pltpu.VMEM((ROWS, D), BF16),
            pltpu.VMEM((2, 2, 2, 4, 2, PIECE, D), F32),
            pltpu.VMEM((2, 4, 2, 4, PIECE, D), F32),
            pltpu.VMEM((N_FF, 2, 4, 2, PIECE, D), F32),
            pltpu.VMEM((2, 4, 2, PIECE, D), F32),
            pltpu.VMEM((2, 2, 4, PIECE, D), F32),
            pltpu.SemaphoreType.DMA((N_FF,)),
            pltpu.SemaphoreType.DMA((HEADS,)),
            pltpu.SemaphoreType.DMA((HOMES,)),
        ]
        + Sems.scratch(N_FF),
        compiler_params=params(collective_id=4, has_side_effects=True),
    )(rec, x, g, wo, wu, wd, gi, gf, gh, sums)


def back_all_kernel(offs, drec, own, sib, ap, lse, C0, C1a, C1b, grec, wo_g, up_g, down_g, qst, kc, vc, kt, qc, dc, lt, k4, v4, kt4, q4, d4, lt4, k5, v5, kt5, q5, d5, lt5, dqt, dk, dv, dq, dk4, dv4, dk5, dv5, dq4, dq5, b1, b2, b3, b4, ds_out, came, lsem, send, recv, qsend, qrecv, fsend, frecv, c0, c1a, c1b, c2, zl, zr, csem, *rsems):
    place = Place()
    p, s, x, core, active, head = place_facts()
    b = core
    o2, o3, o4, o5 = offs[1], offs[2], offs[3], offs[4]
    kvf, qf, X, df = dk, dv.at[0:2], dv.at[2:4], dq
    dqp = qst

    barrier = pltpu.get_barrier_semaphore()
    expected = place.greet(barrier)

    def greet_heads(h, carry):
        q, t = head_device(h, x)

        @pl.when(jnp.logical_not(same(p, s, q, t)))
        def _():
            pl.semaphore_signal(barrier, inc=1, device_id=to(q, t), device_id_type=MESH)

        return carry

    lax.fori_loop(0, HEADS, greet_heads, 0)
    from_homes = HOMES - (core == x).astype(jnp.int32)
    pl.semaphore_wait(barrier, expected + active.astype(jnp.int32) * from_homes)

    def put(k, v):
        @pl.when(k == 0)
        def _():
            wo_g[...] = v

        @pl.when(jnp.logical_and(k > 0, k < 5))
        def _():
            up_g[:, pl.ds(pl.multiple_of((k - 1) * D, D), D)] = v

        @pl.when(k >= 5)
        def _():
            down_g[pl.ds(pl.multiple_of((k - 5) * PIECE, PIECE), PIECE), :] = v

    sems = Sems(rsems)

    def chunk(k):
        x_first = k % 2 == 0
        b0 = c0.at[k] if k < N_COLS else None
        b1 = (c1a if x_first else c1b).at[k // 2]
        return Chunk(
            place, k, x_first, sems, b0, b1, c2.at[k], zl.at[k], zr.at[k], put=lambda v: put(jnp.int32(k), v)
        )

    def load(k):
        if k < N_COLS:
            return pltpu.make_async_copy(C0.at[k], c0.at[k], csem.at[k])
        src, dst = (C1a, c1a) if k % 2 == 0 else (C1b, c1b)
        return pltpu.make_async_copy(src.at[(k - N_COLS) // 2], dst.at[k // 2], csem.at[k])

    PAIRS = ((5, 6), (7, 8), (0, 1), (2, 3), (4,))

    def reduction(*todo):
        for stage, pair in todo:
            for k in PAIRS[pair]:
                if stage == 1:
                    load(k).wait()
                    chunk(k).one().start()
                elif stage == 2 and k >= N_COLS:
                    load(k).wait()
                    chunk(k).two().start()
                else:
                    getattr(chunk(k), f"stage{stage}")()


    def local_copies(m):
        t = pl.multiple_of((m // 2) * ROWS, 64)
        c, d = 2 * b + lax.rem(m, 2), 2 * (1 - b) + lax.rem(m, 2)
        return [
            pltpu.make_async_copy(own.at[m, pl.ds(0, ROWS), :], kvf.at[c, pl.ds(t, ROWS), :], lsem.at[m, 0]),
            pltpu.make_async_copy(sib.at[m], kvf.at[d, pl.ds(t, ROWS), :], lsem.at[m, 1]),
            pltpu.make_async_copy(own.at[m, pl.ds(ROWS, HALF), :], qst.at[m], lsem.at[m, 2]),
        ]

    lse_copy = pltpu.make_async_copy(lse, X, lsem.at[HOMES, 0])

    @pl.when(active)
    def _():
        lse_copy.start()

        def start(m, carry):
            for c in local_copies(m):
                c.start()
            return carry

        lax.fori_loop(0, HOMES, start, 0)

    for pair in PAIRS:
        for k in pair:
            load(k).start()
    reduction((2, 0), (1, 2), (2, 1))

    @pl.when(active)
    def _():
        b1[...] = key_bias((2, 128), (4, 128), 4, 1, 2 * b, True)
        b2[...] = key_bias((1, 256), (2, 256), 4, 2, 2 * b, True)
        b3[...] = key_bias((1, 256), (1, 256), 1, 1, 0, True)
        e4 = class_facts4(o4, b)[1]
        b4[...] = key_bias((1, 256), (2, 256), 12, 6, 6 * e4, True)

        def wait(m, carry):
            for c in local_copies(m):
                c.wait()
            return carry

        lax.fori_loop(0, HOMES, wait, 0)
        lse_copy.wait()
        unpack_pairs(qst, 0, qf, 1.0 / math.sqrt(HD))

        def prepare(i, carry):
            c, t = i // 12, pl.multiple_of(lax.rem(i, 12) * 128, 128)
            k2, v2 = keys_and_values(kvf[c, pl.ds(t, 128), :])
            kc[c, pl.ds(t, 128), :] = k2.astype(BF16)
            vc[c, pl.ds(t, 128), :] = v2.astype(BF16)
            kt[c, :, pl.ds(t, 128)] = k2.T.astype(BF16)
            return carry

        lax.fori_loop(0, 48, prepare, 0)

        def prepare_q(i, carry):
            c, t = i // 12, pl.multiple_of(lax.rem(i, 12) * 128, 128)
            qc[c, pl.ds(t, 128), :] = query_quads(qf[c, pl.ds(t, 128), :])
            return carry

        lax.fori_loop(0, 24, prepare_q, 0)

    keys4, e4, (qc4, qv4) = class_facts4(o4, b)
    kc5, kv5 = lax.rem(o5, 4), o5 // 4
    qi4, qi5 = qc4 - 2 * b, lax.rem(kc5, 2)

    @pl.when(active)
    def _():
        for blk in range(4):
            r = slice(128 * blk, 128 * blk + 128)
            for e in range(2):
                c, v = keys4[e]
                k2, v2 = keys_and_values(kvf[c, pl.ds(v + 384 * blk, 128, stride=3), :])
                k4[e, r, :] = k2.astype(BF16)
                v4[e, r, :] = v2.astype(BF16)
                kt4[e, :, r] = k2.T.astype(BF16)
            q4[r, :] = query_quads(qf[qi4, pl.ds(qv4 + 384 * blk, 128, stride=3), :])
            rows = pl.ds(kv5 + 384 * blk, 128, stride=3)
            k2, v2 = keys_and_values(kvf[kc5, rows, :])
            k5[r, :] = k2.astype(BF16)
            v5[r, :] = v2.astype(BF16)
            kt5[:, r] = k2.T.astype(BF16)
            q5[r, :] = query_quads(qf[qi5, rows, :])
        dk[...] = jnp.zeros_like(dk)

    reduction((1, 3))

    @pl.when(active)
    def _():
        unpack_pairs(drec, 0, df, 1.0)

        def facts(m, carry):
            ci = lax.rem(m, 2)
            t = pl.multiple_of((m // 2) * ROWS, 32)
            prod = drec[m] * ap[m]
            low = lower_lanes(prod)
            d0 = jnp.sum(jnp.where(low, prod, 0.0), -1, keepdims=True)
            d1 = jnp.sum(jnp.where(low, 0.0, prod), -1, keepdims=True)
            for part, d in ((0, d0), (1, d1)):
                rows = pl.ds(t + HALF * part, HALF)
                l = X[ci, rows, :]
                X[ci, rows, :] = jnp.where(low, l, jnp.broadcast_to(d, l.shape))
            return carry

        lax.fori_loop(0, HOMES, facts, 0)

        def turned(v):
            w = v.T
            return jnp.concatenate([w[0:1, :], w[HD : HD + 1, :]], 0)

        def prepare_d(i, carry):
            c, t = i // 12, pl.multiple_of(lax.rem(i, 12) * 128, 128)
            rows = pl.ds(t, 128)
            dc[c, rows, :] = query_quads(df[c, rows, :])
            lt[i] = turned(X[c, rows, :])
            return carry

        lax.fori_loop(0, 24, prepare_d, 0)
        for blk in range(4):
            r = slice(128 * blk, 128 * blk + 128)
            rows = pl.ds(qv4 + 384 * blk, 128, stride=3)
            d4[r, :] = query_quads(df[qi4, rows, :])
            lt4[blk] = turned(X[qi4, rows, :])
            rows = pl.ds(kv5 + 384 * blk, 128, stride=3)
            d5[r, :] = query_quads(df[qi5, rows, :])
            lt5[blk] = turned(X[qi5, rows, :])
        dv[...] = jnp.zeros_like(dv)
        dq[...] = jnp.zeros_like(dq)

    def tile(g, k, v, kT, q, d, facts_pair, bias, first):
        s_ = dot_nt(doubled(k), q)
        if bias is not None:
            s_ = s_ + bias[...]
        l0, l1 = facts_pair
        row = jnp.concatenate([l0[0:1, :], l1[0:1, :]], 1)
        delta = jnp.concatenate([l0[1:2, :], l1[1:2, :]], 1)
        pr = jnp.exp(s_ - row)
        ds = pr * (dot_nt(doubled(v), d) - delta)
        hi, lo = split(pr)
        d2, q2_ = d[:, :128], q[:, :128]
        dv_new = dot_nn(jnp.concatenate([hi, lo], 1), jnp.concatenate([d2, d2], 0))
        hi, lo = split(ds)
        dk_new = dot_nn(jnp.concatenate([hi, lo], 1), jnp.concatenate([q2_, q2_], 0))
        dq_new = dot_nn(doubled(kT), jnp.concatenate([hi, lo], 0))
        dqt[g] = dq_new if first else dqt[g] + dq_new
        return dk_new, dv_new

    def at256(blk):
        return pl.ds(pl.multiple_of(256 * blk, 128), 256)

    def kept(flag, v):
        return jnp.where(flag, v, 0.0)

    def q2(qb, carry):
        def step(kb, bias, first):
            ks, qs = at256(kb), at256(qb)
            a, c = tile(
                0,
                jnp.concatenate([kc[o2, ks, :], kc[o2 + 2, ks, :]], 0),
                jnp.concatenate([vc[o2, ks, :], vc[o2 + 2, ks, :]], 0),
                jnp.concatenate([kt[o2, :, ks], kt[o2 + 2, :, ks]], 1),
                qc[o2, qs, :],
                dc[o2, qs, :],
                (lt.at[12 * o2 + 2 * qb], lt.at[12 * o2 + 2 * qb + 1]),
                bias,
                first,
            )
            for par in range(2):
                f = o2 == par
                dk[par, ks, :] += kept(f, a[:256])
                dk[par + 2, ks, :] += kept(f, a[256:])
                dv[par, ks, :] += kept(f, c[:256])
                dv[par + 2, ks, :] += kept(f, c[256:])

        step(qb, b2, True)

        def more(kb, inner):
            step(kb, None, False)
            return inner

        lax.fori_loop(jnp.where(qb >= 4, 4, 0), qb, more, 0)
        for par in range(2):
            dq[par, at256(qb), :] += kept(o2 == par, dqt[0].T)
        return carry

    @pl.when(active)
    def _():
        lax.fori_loop(0, TOTAL // 256, q2, 0)

    reduction((3, 0), (2, 2), (3, 1), (1, 4))

    def q3(qb, carry):
        ci = lax.rem(o3, 2)

        def step(kb, bias, first):
            ks, qs = at256(kb), at256(qb)
            a, c = tile(
                0,
                kc[o3, ks, :],
                vc[o3, ks, :],
                kt[o3, :, ks],
                qc[ci, qs, :],
                dc[ci, qs, :],
                (lt.at[12 * ci + 2 * qb], lt.at[12 * ci + 2 * qb + 1]),
                bias,
                first,
            )
            for i in range(2):
                f = o3 == 2 * b + i
                dk[2 * b + i, ks, :] += kept(f, a)
                dv[2 * b + i, ks, :] += kept(f, c)

        step(qb, b3, True)

        def more(kb, inner):
            step(kb, None, False)
            return inner

        lax.fori_loop(0, qb, more, 0)
        for i in range(2):
            dq[i, at256(qb), :] += kept(o3 == 2 * b + i, dqt[0].T)
        return carry

    @pl.when(active)
    def _():
        lax.fori_loop(0, TOTAL // 256, q3, 0)

    @pl.when(active)
    def _():
        for ref in (dk4, dv4, dk5, dv5):
            ref[...] = jnp.zeros_like(ref)
        for qb in range(2):
            qs = slice(256 * qb, 256 * qb + 256)
            for kb in range(qb, -1, -1):
                ks = slice(256 * kb, 256 * kb + 256)
                a, c = tile(
                    0,
                    k4[:, ks, :].reshape(512, 128),
                    v4[:, ks, :].reshape(512, 128),
                    jnp.concatenate([kt4[0, :, ks], kt4[1, :, ks]], 1),
                    q4[qs, :],
                    d4[qs, :],
                    (lt4.at[2 * qb], lt4.at[2 * qb + 1]),
                    b4 if kb == qb else None,
                    kb == qb,
                )
                dk4[:, ks, :] += a.reshape(2, 256, 128)
                dv4[:, ks, :] += c.reshape(2, 256, 128)
                a, c = tile(
                    1,
                    k5[ks, :],
                    v5[ks, :],
                    kt5[:, ks],
                    q5[qs, :],
                    d5[qs, :],
                    (lt5.at[2 * qb], lt5.at[2 * qb + 1]),
                    b3 if kb == qb else None,
                    kb == qb,
                )
                dk5[ks, :] += a
                dv5[ks, :] += c
            dq4[qs, :] = dqt[0].T
            dq5[qs, :] = dqt[1].T
        mine5 = kc5 // 2 == b
        for kind in range(12):
            c, rows = kind % 4, pl.ds(kind // 4, THIRD, stride=3)
            f0, f1, f5 = o4 == kind, o4 + 6 == kind, jnp.logical_and(o5 == kind, mine5)
            dk[c, rows, :] += kept(f0, dk4[0]) + kept(f1, dk4[1]) + kept(f5, dk5[...])
            dv[c, rows, :] += kept(f0, dv4[0]) + kept(f1, dv4[1]) + kept(f5, dv5[...])
        for ci in range(2):
            for v in range(3):
                rows = pl.ds(v, THIRD, stride=3)
                f4 = jnp.logical_and(qi4 == ci, qv4 == v)
                f5 = jnp.logical_and(jnp.logical_and(qi5 == ci, kv5 == v), mine5)
                dq[ci, rows, :] += kept(f4, dq4[...]) + kept(f5, dq5[...])

    reduction((4, 0), (4, 1), (2, 3), (3, 2))

    def segment(g):
        def at(blk):
            return pl.ds(pl.multiple_of(512 * g + 128 * blk, 128), 128)

        def step(i, qb, kb, bias, first):
            ks, qs = at(kb), at(qb)
            kT = jnp.concatenate([kt[c, :, ks] for c in range(4)], 1)
            a, c = tile(
                i,
                kc[:, ks, :].reshape(512, 128),
                vc[:, ks, :].reshape(512, 128),
                kT,
                qc[:, qs, :].reshape(256, 256),
                dc[:, qs, :].reshape(256, 256),
                (lt.at[4 * g + qb], lt.at[12 + 4 * g + qb]),
                bias,
                first,
            )
            dk[:, ks, :] += a.reshape(4, 128, 128)
            dv[:, ks, :] += c.reshape(4, 128, 128)

        def pair(j, carry):
            q0, q1_ = 2 * j, 2 * j + 1
            step(0, q0, q0, b1, True)
            step(1, q1_, q1_, b1, True)

            def more(kb, inner):
                step(0, q0, kb, None, False)
                step(1, q1_, kb, None, False)
                return inner

            lax.fori_loop(0, q0, more, 0)
            step(1, q1_, q0, None, False)
            for i, qb in ((0, q0), (1, q1_)):
                dq[:, at(qb), :] += dqt[i].T.reshape(2, 128, 128)
            return carry

        lax.fori_loop(0, 2, pair, 0)

    def passed(m):
        return remote(ds_out.at[m], came.at[m], fsend.at[m], frecv.at[m], place.peer)

    def home_copies(m):
        q, t = home_device(core, m)
        kv = remote(came.at[m], grec.at[head, pl.ds(0, ROWS), :], send.at[m], recv.at[head], to(q, t))
        dq_ = remote(dqp.at[m], grec.at[head, pl.ds(ROWS, HALF), :], qsend.at[m], qrecv.at[head], to(q, t))
        return q, t, kv, dq_

    def rows_of(m):
        return pl.ds(pl.multiple_of((m // 2) * ROWS, 64), ROWS)

    def kv(c, m):
        k, v = dk[c, rows_of(m), :], dv[c, rows_of(m), :]
        return pick(k + swap(k), v + swap(v))

    def share(m, carry):
        ds_out[m] = kv(2 * (1 - b) + lax.rem(m, 2), m)
        passed(m).start()
        return carry

    def add(m, carry):
        q, t, far_kv, far_q = home_copies(m)
        ci = lax.rem(m, 2)
        v = dq[ci, rows_of(m), :]
        v = (v + swap(v)) * (1.0 / math.sqrt(HD))
        dqp[m] = pick(v[:HALF], v[HALF:])
        passed(m).wait_recv()
        came[m] += kv(2 * b + ci, m)

        @pl.when(same(p, s, q, t))
        def _():
            pltpu.make_async_copy(came.at[m], grec.at[head, pl.ds(0, ROWS), :], recv.at[head]).start()
            pltpu.make_async_copy(dqp.at[m], grec.at[head, pl.ds(ROWS, HALF), :], qrecv.at[head]).start()

        @pl.when(jnp.logical_not(same(p, s, q, t)))
        def _():
            far_kv.start()
            far_q.start()

        return carry

    @pl.when(active)
    def _():
        segment(0)
        lax.fori_loop(0, 4, share, 0)
        segment(2)
        lax.fori_loop(12, HOMES, share, 0)
        lax.fori_loop(0, 4, add, 0)

    reduction((5, 0), (5, 1), (2, 4), (3, 3), (4, 2))

    @pl.when(active)
    def _():
        segment(1)
        lax.fori_loop(4, 12, share, 0)
        lax.fori_loop(12, HOMES, add, 0)
        lax.fori_loop(4, 12, add, 0)

    reduction((6, 0), (6, 1), (3, 4), (4, 3), (5, 2))
    reduction((4, 4), (5, 3), (6, 2))
    reduction((5, 4), (6, 3))
    reduction((6, 4))

    def from_head(h, carry):
        a = grec.at[h, pl.ds(0, ROWS), :]
        c = grec.at[h, pl.ds(ROWS, HALF), :]
        pltpu.make_async_copy(a, a, recv.at[h]).wait()
        pltpu.make_async_copy(c, c, qrecv.at[h]).wait()
        return carry

    lax.fori_loop(0, HEADS, from_head, 0)
    for k in range(N_FF):
        if k < N_COLS:
            chunk(k).one().wait_send()
        chunk(k).two().wait_send()
        chunk(k).line_sent()

    @pl.when(active)
    def _():
        def sent(m, carry):
            q, t, far_kv, far_q = home_copies(m)
            passed(m).wait_send()

            @pl.when(jnp.logical_not(same(p, s, q, t)))
            def _():
                far_kv.wait_send()
                far_q.wait_send()

            return carry

        lax.fori_loop(0, HOMES, sent, 0)


def backward_all(offs, drec, own, sib, ap, lse, C0, C1a, C1b, cid):
    dma = pltpu.SemaphoreType.DMA
    keys = pltpu.VMEM((4, TOTAL, 128), BF16)
    full = pltpu.VMEM((4, TOTAL, 128), F32)
    quad = pltpu.VMEM((2, TOTAL, 256), BF16)
    quad3 = pltpu.VMEM((THIRD, 256), BF16)
    pair3 = pltpu.VMEM((THIRD, 128), BF16)
    turned = pltpu.VMEM((128, THIRD), BF16)
    facts3 = pltpu.VMEM((4, 2, 128), F32)
    out3 = pltpu.VMEM((THIRD, 128), F32)
    packs = pltpu.VMEM((HOMES, ROWS, 128), F32)
    halves = pltpu.VMEM((HOMES, HALF, 128), F32)
    return pl.pallas_call(
        back_all_kernel,
        out_shape=[
            jax.ShapeDtypeStruct((HEADS, PACK, 128), F32),
            jax.ShapeDtypeStruct((PIECE, D), F32),
            jax.ShapeDtypeStruct((PIECE, FF), F32),
            jax.ShapeDtypeStruct((4 * PIECE, D), F32),
        ],
        in_specs=[SM, VM, ANY, ANY, VM, ANY, ANY, ANY, ANY],
        out_specs=[ANY, VM, VM, VM],
        scratch_shapes=[
            halves,
            keys,
            keys,
            pltpu.VMEM((4, 128, TOTAL), BF16),
            quad,
            quad,
            pltpu.VMEM((24, 2, 128), F32),
            pltpu.VMEM((2, THIRD, 128), BF16),
            pltpu.VMEM((2, THIRD, 128), BF16),
            pltpu.VMEM((2, 128, THIRD), BF16),
            quad3,
            quad3,
            facts3,
            pair3,
            pair3,
            turned,
            quad3,
            quad3,
            facts3,
            pltpu.VMEM((3, 128, 256), F32),
            full,
            full,
            pltpu.VMEM((2, TOTAL, 128), F32),
            pltpu.VMEM((2, THIRD, 128), F32),
            pltpu.VMEM((2, THIRD, 128), F32),
            out3,
            out3,
            out3,
            out3,
            pltpu.VMEM((512, 256), F32),
            pltpu.VMEM((512, 256), F32),
            pltpu.VMEM((256, 256), F32),
            pltpu.VMEM((512, 256), F32),
            packs,
            packs,
            dma((HOMES + 1, 3)),
            dma((HOMES,)),
            dma((HEADS,)),
            dma((HOMES,)),
            dma((HEADS,)),
            dma((HOMES,)),
            dma((HOMES,)),
            pltpu.VMEM((N_COLS, 2, 4, 2, PIECE, D), F32),
            pltpu.VMEM((5, 4, 2, PIECE, D), F32),
            pltpu.VMEM((4, 2, 4, PIECE, D), F32),
            pltpu.VMEM((N_FF, 4, PIECE, D), F32),
            pltpu.VMEM((N_FF, 4, PIECE, D), F32),
            pltpu.VMEM((N_FF, 4, PIECE, D), F32),
            dma((N_FF,)),
        ]
        + Sems.scratch(N_FF),
        compiler_params=params(collective_id=cid, has_side_effects=True),
    )(offs, drec, own, sib, ap, lse, C0, C1a, C1b)


SEG1, SEG2, SEG3, SEG4, SEG5 = SEGMENTS
DILATION_ONE, DILATION_TWO, DILATION_THREE, DILATION_FOUR, DILATION_FIVE = DILATIONS
MASK_VALUE = -1e30
MATMUL_ACCURACY = lax.Precision.HIGHEST


def passed_along(value, axis, by):
    length = lax.axis_size(axis)
    return lax.ppermute(value, axis, [(i, (i + by) % length) for i in range(length)])


def run_is_live(distance, anchor_point, sequence_width, segment_length):
    return (anchor_point - (distance - 1) * sequence_width - 1) // segment_length == anchor_point // segment_length


def layer_norm(x, gain_vec):
    average = jnp.mean(x, -1, keepdims=True)
    centred = x - average
    variance = jnp.mean(centred * centred, -1, keepdims=True)
    return centred * lax.rsqrt(variance + LN_EPSILON) * gain_vec


def select_table(offsets_row, dilation_rate):
    return (jnp.arange(dilation_rate, dtype=jnp.int32)[:, None] == offsets_row[None, :]).astype(
        jnp.float32
    )


def spread_apart(x, select_option, dilation_rate):
    shaped = x.reshape(x.shape[0] // dilation_rate, dilation_rate, x.shape[1], x.shape[2])
    return jnp.einsum("trhd,rh->thd", shaped, select_option, precision=MATMUL_ACCURACY)


def spread_scalar_rows(x, select_option, dilation_rate):
    shaped = x.reshape(x.shape[0] // dilation_rate, dilation_rate, x.shape[1])
    return jnp.einsum("trh,rh->th", shaped, select_option, precision=MATMUL_ACCURACY)


def spread_rows(x, select_option):
    return jnp.einsum("thd,rh->trhd", x, select_option, precision=MATMUL_ACCURACY).reshape(
        -1, x.shape[1], x.shape[2]
    )


def spread_scalars(x, select_option):
    return jnp.einsum("th,rh->trh", x, select_option, precision=MATMUL_ACCURACY).reshape(
        -1, x.shape[1]
    )


def masked_score_matrix(sparse_queries, key_portion, query_position, key_position, segment_length):
    score_matrix = jnp.einsum(
        "ozt,bzt->zob", sparse_queries, key_portion, precision=MATMUL_ACCURACY
    ) * (1.0 / math.sqrt(key_portion.shape[-1]))
    q_cols = query_position.T[:, :, None]
    k_cols = key_position.T[:, None, :]
    permitted_mask = (k_cols <= q_cols) & (k_cols // segment_length == q_cols // segment_length)
    return (jnp.where(permitted_mask, score_matrix, MASK_VALUE), permitted_mask)


def prepare_pattern(
    query_sequence, key_sequence, value_sequence, offsets_row, dilation_rate, anchor_point
):
    select_option = select_table(offsets_row, dilation_rate)
    sparse_queries = spread_apart(query_sequence, select_option, dilation_rate)
    sparse_key_value = jnp.stack(
        (
            spread_apart(key_sequence, select_option, dilation_rate),
            spread_apart(value_sequence, select_option, dilation_rate),
        )
    )
    query_position = (
        anchor_point
        + jnp.arange(sparse_queries.shape[0], dtype=jnp.int32)[:, None] * dilation_rate
        + offsets_row[None, :]
    )
    return (select_option, sparse_queries, sparse_key_value, query_position)


def pattern_forward_pass(
    sparse_queries,
    sparse_key_value,
    query_position,
    reach,
    segment_length,
    anchor_point,
    sequence_width,
):
    masked_logits, permitted_mask = masked_score_matrix(
        sparse_queries, sparse_key_value[0], query_position, query_position, segment_length
    )
    row_max = jnp.max(masked_logits, -1)
    softmax_weights = jnp.where(permitted_mask, jnp.exp(masked_logits - row_max[..., None]), 0.0)
    state = (
        row_max,
        jnp.sum(softmax_weights, -1),
        jnp.einsum("tlj,jtb->tlb", softmax_weights, sparse_key_value[1], precision=MATMUL_ACCURACY),
    )

    def one_run(distance, carry):
        remote_key_value, state = carry
        remote_key_value = passed_along(remote_key_value, "seq", 1)
        key_position = query_position - distance * sequence_width

        def update(state_in):
            old_max, old_sum, old_acc = state_in
            masked_remote, permitted_remote = masked_score_matrix(
                sparse_queries, remote_key_value[0], query_position, key_position, segment_length
            )
            new_max = jnp.maximum(old_max, jnp.max(masked_remote, -1))
            weights_far = jnp.where(
                permitted_remote, jnp.exp(masked_remote - new_max[..., None]), 0.0
            )
            factor = jnp.exp(old_max - new_max)
            added = jnp.einsum(
                "tlj,jtb->tlb", weights_far, remote_key_value[1], precision=MATMUL_ACCURACY
            )
            return (
                new_max,
                old_sum * factor + jnp.sum(weights_far, -1),
                old_acc * factor[..., None] + added,
            )

        def unchanged(state_in):
            return state_in

        is_live = run_is_live(distance, anchor_point, sequence_width, segment_length)
        return remote_key_value, lax.cond(is_live, update, unchanged, state)

    state = lax.fori_loop(1, reach + 1, one_run, (sparse_key_value, state))[1]
    row_max, row_sum, accumulated = state
    mixture = jnp.transpose(accumulated / row_sum[..., None], (1, 0, 2))
    log_sum = (row_max + jnp.log(row_sum)).T
    return (mixture, log_sum)


def merge_patterns(forwards, prepared_inputs):
    full_lse = []
    full_mix = []
    for pattern_spec in range(len(forwards)):
        mixture, log_sum = forwards[pattern_spec]
        select_option = prepared_inputs[pattern_spec][0]
        covered = spread_scalars(jnp.ones_like(log_sum), select_option)
        full_lse.append(spread_scalars(log_sum, select_option) + (covered - 1.0) * 1e30)
        full_mix.append(spread_rows(mixture, select_option))
    stacked = jnp.stack(full_lse)
    row_max = jnp.max(stacked, 0)
    softmax_weights = jnp.exp(stacked - row_max)
    row_sum = jnp.sum(softmax_weights, 0)
    attended = full_mix[0] * softmax_weights[0][..., None]
    for pattern_spec in range(1, len(full_mix)):
        attended = attended + full_mix[pattern_spec] * softmax_weights[pattern_spec][..., None]
    return (attended / row_sum[..., None], row_max + jnp.log(row_sum))


def pattern_backward(
    select_option,
    dilation_rate,
    segment_length,
    anchor_point,
    sparse_queries,
    sparse_key_value,
    query_position,
    reach,
    sequence_gradient,
    row_difference,
    combined_logsumexp,
):
    sequence_width = sequence_gradient.shape[0]
    sparse_gradient = spread_apart(sequence_gradient, select_option, dilation_rate)
    sparse_output_grad = spread_scalar_rows(row_difference, select_option, dilation_rate).T
    sparse_logsumexp = spread_scalar_rows(combined_logsumexp, select_option, dilation_rate).T
    inverse_square_root = 1.0 / math.sqrt(sparse_queries.shape[-1])

    def portion_gradients(key_portion, value_portion, key_position):
        masked_logits, permitted_mask = masked_score_matrix(
            sparse_queries, key_portion, query_position, key_position, segment_length
        )
        softmax_weights = jnp.where(
            permitted_mask, jnp.exp(masked_logits - sparse_logsumexp[..., None]), 0.0
        )
        value_gradient = jnp.einsum(
            "tui,utx->itx", softmax_weights, sparse_gradient, precision=MATMUL_ACCURACY
        )
        pattern_gradient = jnp.einsum(
            "ozt,bzt->zob", sparse_gradient, value_portion, precision=MATMUL_ACCURACY
        )
        score_gradient = (
            softmax_weights
            * (pattern_gradient - sparse_output_grad[..., None])
            * inverse_square_root
        )
        query_gradient = jnp.einsum(
            "hqk,khd->qhd", score_gradient, key_portion, precision=MATMUL_ACCURACY
        )
        key_gradient = jnp.einsum(
            "tui,utx->itx", score_gradient, sparse_queries, precision=MATMUL_ACCURACY
        )
        return (query_gradient, jnp.stack((key_gradient, value_gradient)))

    query_gradient, key_value_gradient = portion_gradients(
        sparse_key_value[0], sparse_key_value[1], query_position
    )

    def one_run(distance, carry):
        remote_key_value, remote_gradient, query_sum = carry
        remote_key_value = passed_along(remote_key_value, "seq", 1)
        remote_gradient = passed_along(remote_gradient, "seq", 1)
        key_position = query_position - distance * sequence_width

        def far_grads():
            part_q, part_kv = portion_gradients(remote_key_value[0], remote_key_value[1], key_position)
            return query_sum + part_q, remote_gradient + part_kv

        def no_grads():
            return query_sum, remote_gradient

        is_live = run_is_live(distance, anchor_point, sequence_width, segment_length)
        query_sum, remote_gradient = lax.cond(is_live, far_grads, no_grads)
        return remote_key_value, remote_gradient, query_sum

    _, travelled, query_gradient = lax.fori_loop(
        1, reach + 1, one_run, (sparse_key_value, key_value_gradient, query_gradient)
    )
    return (query_gradient, passed_along(travelled, "seq", -reach))


def front_part(own_rows, w_qkv, gain_attn):
    return jnp.dot(layer_norm(own_rows, gain_attn), w_qkv, precision=MATMUL_ACCURACY)


def after_part(attn_rows, own_rows, w_out, w_up, w_down, gain_inner, gain_ffn, gain_hidden):
    residual = own_rows + jnp.dot(
        layer_norm(attn_rows, gain_inner), w_out, precision=MATMUL_ACCURACY
    )
    hidden = jax.nn.gelu(
        jnp.dot(layer_norm(residual, gain_ffn), w_up, precision=MATMUL_ACCURACY), approximate=False
    )
    return residual + jnp.dot(layer_norm(hidden, gain_hidden), w_down, precision=MATMUL_ACCURACY)


def shards(
    tokens,
    w_qkv,
    w_out,
    w_up,
    w_down,
    gain_attn,
    gain_inner,
    gain_ffn,
    gain_hidden,
    offsets,
    grad_out,
):
    w_qkv = w_qkv.astype(jnp.float32)
    w_out = w_out.astype(jnp.float32)
    w_up = w_up.astype(jnp.float32)
    w_down = w_down.astype(jnp.float32)
    groups = lax.axis_size("pat")
    local_rows = tokens.shape[0]
    sequence_width = local_rows * groups
    heads_here = HEADS // groups
    own_rows = tokens.reshape(local_rows, D)
    qkv_rows, front_back = jax.vjp(front_part, own_rows, w_qkv, gain_attn)
    gathered_qkv = lax.all_to_all(
        qkv_rows.reshape(local_rows, 1, 3, HEADS, HD),
        "pat",
        split_axis=3,
        concat_axis=1,
        tiled=True,
    )
    gathered_qkv = gathered_qkv.reshape(sequence_width, 3, heads_here, HD)
    head_offsets = lax.dynamic_slice_in_dim(
        offsets, lax.axis_index("pat") * heads_here, heads_here, 1
    )
    anchor_point = lax.axis_index("seq") * sequence_width
    dilation_rates = (DILATION_ONE, DILATION_TWO, DILATION_THREE, DILATION_FOUR, DILATION_FIVE)
    segment_lengths = (SEG1, SEG2, SEG3, SEG4, SEG5)
    reaches = [
        min((segment_lengths[pattern_spec] - 2) // sequence_width + 1, lax.axis_size("seq") - 1)
        for pattern_spec in range(PATTERNS)
    ]
    prepared_inputs = []
    for pattern_spec in range(PATTERNS):
        prepared_inputs.append(
            prepare_pattern(
                gathered_qkv[:, 0],
                gathered_qkv[:, 1],
                gathered_qkv[:, 2],
                head_offsets[pattern_spec],
                dilation_rates[pattern_spec],
                anchor_point,
            )
        )
    forwards = []
    for pattern_spec in range(PATTERNS):
        select_option, sparse_queries, sparse_key_value, query_position = prepared_inputs[
            pattern_spec
        ]
        forwards.append(
            pattern_forward_pass(
                sparse_queries,
                sparse_key_value,
                query_position,
                reaches[pattern_spec],
                segment_lengths[pattern_spec],
                anchor_point,
                sequence_width,
            )
        )
    lse_sums = jnp.stack([jnp.sum(entry[1]) for entry in forwards])
    totals = lax.psum(lse_sums, ("pat", "seq"))
    full_length = sequence_width * lax.axis_size("seq")
    counts = jnp.array(
        [
            float(full_length // dilation_rates[pattern_spec] * HEADS)
            for pattern_spec in range(PATTERNS)
        ],
        jnp.float32,
    )
    log_means = totals / counts
    attended, combined_logsumexp = merge_patterns(forwards, prepared_inputs)
    returned_rows = lax.all_to_all(
        attended.reshape(local_rows, groups, heads_here, HD),
        "pat",
        split_axis=1,
        concat_axis=2,
        tiled=True,
    )
    attn_rows = returned_rows.reshape(local_rows, D)
    result, after_back = jax.vjp(
        after_part, attn_rows, own_rows, w_out, w_up, w_down, gain_inner, gain_ffn, gain_hidden
    )
    g_attn, g_resid, g_out, g_up, g_down, g_inner, g_ffn, g_hidden = after_back(
        grad_out.reshape(local_rows, D)
    )
    sequence_gradient = lax.all_to_all(
        g_attn.reshape(local_rows, 1, HEADS, HD), "pat", split_axis=2, concat_axis=1, tiled=True
    )
    sequence_gradient = sequence_gradient.reshape(sequence_width, heads_here, HD)
    row_difference = jnp.sum(sequence_gradient * attended, -1)
    q_grads = []
    kv_grads = []
    for pattern_spec in range(PATTERNS):
        select_option, sparse_queries, sparse_key_value, query_position = prepared_inputs[
            pattern_spec
        ]
        part_q, part_kv = pattern_backward(
            select_option,
            dilation_rates[pattern_spec],
            segment_lengths[pattern_spec],
            anchor_point,
            sparse_queries,
            sparse_key_value,
            query_position,
            reaches[pattern_spec],
            sequence_gradient,
            row_difference,
            combined_logsumexp,
        )
        q_grads.append(part_q)
        kv_grads.append(part_kv)
    grad_total = jnp.zeros((sequence_width, 3, heads_here, HD), jnp.float32)
    for pattern_spec in range(PATTERNS):
        select_option = prepared_inputs[pattern_spec][0]
        grad_total = grad_total + jnp.stack(
            (
                spread_rows(q_grads[pattern_spec], select_option),
                spread_rows(kv_grads[pattern_spec][0], select_option),
                spread_rows(kv_grads[pattern_spec][1], select_option),
            ),
            1,
        )
    grad_back = lax.all_to_all(
        grad_total.reshape(local_rows, groups, 3, heads_here, HD),
        "pat",
        split_axis=1,
        concat_axis=3,
        tiled=True,
    )
    g_tokens, g_qkv, g_attn_gain = front_back(grad_back.reshape(local_rows, 3 * D))
    grad_tokens = (g_resid + g_tokens).reshape(local_rows, 1, D)
    summed = (
        lax.psum_scatter(g_qkv, ("pat", "seq"), scatter_dimension=0, tiled=True),
        lax.psum_scatter(g_out, ("pat", "seq"), scatter_dimension=0, tiled=True),
        lax.psum_scatter(g_up, ("pat", "seq"), scatter_dimension=0, tiled=True),
        lax.psum_scatter(g_down, ("pat", "seq"), scatter_dimension=0, tiled=True),
        lax.psum_scatter(g_attn_gain, ("pat", "seq"), scatter_dimension=0, tiled=True),
        lax.psum_scatter(g_inner, ("pat", "seq"), scatter_dimension=0, tiled=True),
        lax.psum_scatter(g_ffn, ("pat", "seq"), scatter_dimension=0, tiled=True),
        lax.psum_scatter(g_hidden, ("pat", "seq"), scatter_dimension=0, tiled=True),
    )
    return (
        result.reshape(local_rows, 1, D),
        grad_tokens,
        summed[0],
        summed[1],
        summed[2],
        summed[3],
        summed[4],
        summed[5],
        summed[6],
        summed[7],
        log_means,
    )


def fast_shards(tokens, w_qkv, w_out, w_up, w_down, gain_attn, gain_inner, gain_ffn, gain_hidden, offsets, grad_out):
    p, s = lax.axis_index("pat"), lax.axis_index("seq")
    active, head = head_here(p, s)
    mine = lax.dynamic_slice_in_dim(offsets, head, 1, 1)[:, 0]
    info = jnp.concatenate([jnp.stack([active.astype(jnp.int32), lax.rem(p, 2).astype(jnp.int32)]), mine])

    counts = [float(TOTAL * 4 // r * HEADS) for r in DILATIONS]
    pk, x = front(tokens, w_qkv, gain_attn)
    own, sib = to_heads(pk, True, 0)
    ap, lse, sums = attention_forward(info, own, sib)
    rec = to_homes(ap, 1)
    mixed, drec, dy1, S, C0, C1a, C1b = feed_forward(
        rec, x, grad_out, w_out, w_up, w_down, gain_inner, gain_ffn, gain_hidden, sums
    )
    grec, g_out, g_up, g_down = backward_all(mine, drec, own, sib, ap, lse, C0, C1a, C1b, 2)
    gx, g_qkv, *small = finish(grec, x, dy1, w_qkv, gain_attn, S, counts, 3)
    mixed, gx, g_qkv, g_out, g_up, g_down, *small = deliver(mixed, gx, g_qkv, g_out, g_up, g_down, *small)
    return (mixed, gx, g_qkv, g_out, g_up, g_down, *(v.reshape(-1) for v in small))


def fits(mesh):
    return mesh.shape["pat"] == 4 and mesh.shape["seq"] == RUNS


def solution(mesh):
    rows = P("seq", "pat", None)
    split_rows = P(("pat", "seq"), None)
    split_one = P(("pat", "seq"))
    planned = jax.shard_map(
        fast_shards,
        mesh=mesh,
        in_specs=(rows,) + (P(),) * 9 + (rows,),
        out_specs=(rows, rows) + (split_rows,) * 4 + (split_one,) * 4 + (P(),),
        check_vma=False,
    )
    general = jax.shard_map(
        shards,
        mesh=mesh,
        in_specs=(rows,) + (P(),) * 9 + (rows,),
        out_specs=(rows, rows) + (split_rows,) * 4 + (split_one,) * 4 + (P(),),
        check_vma=False,
    )

    def layer(tokens, *rest):
        if fits(mesh) and tokens.shape[0] == TOTAL:
            return planned(tokens, *rest)
        return general(tokens, *rest)

    return layer
```

```python
import functools
import math

import jax
import jax.numpy as jnp
from jax import lax
from jax.experimental import pallas as pl
from jax.experimental.pallas import tpu as pltpu
from jax.sharding import PartitionSpec as P

D = 768
HEADS = 12
HD = 64
FF = 3072
PATTERNS = 5
SEGMENTS = (2048, 4096, 8192, 16384, 32768)
DILATIONS = (1, 2, 4, 6, 12)
LN_EPSILON = 1e-05
NEG = -1e30
F32 = jnp.float32
BF16 = jnp.bfloat16
HIGHEST = lax.Precision.HIGHEST
VMEM_LIMIT = 60 * 1024 * 1024

ROWS = 192
HALF = ROWS // 2
RUNS = 8
TOTAL = ROWS * RUNS
PACK = ROWS + HALF
HOMES = 16
THIRD = TOTAL // 3
PIECE = 24
MESH = pl.DeviceIdType.MESH


def dot_nn(a, b):
    return lax.dot_general(a, b, (((1,), (0,)), ((), ())), preferred_element_type=F32)


def dot_nt(a, b):
    return lax.dot_general(a, b, (((1,), (1,)), ((), ())), preferred_element_type=F32)


def split(v):
    hi = v.astype(BF16)
    return hi, (v - hi.astype(F32)).astype(BF16)


def split32(v):
    hi = v.astype(BF16).astype(F32)
    return hi, v - hi


def lower_lanes(v):
    return lax.broadcasted_iota(jnp.int32, v.shape, v.ndim - 1) < HD


def swap(v):
    return pltpu.roll(v, HD, v.ndim - 1)


def pick(a, b):
    return jnp.where(lower_lanes(a), a, b)


def head_place(h):
    z = h // 3
    column = lax.rem(lax.rem(h, 3) + z + 1, 4)
    return column // 2, z * 2 + lax.rem(column, 2)


def head_here(p, s):
    z = s // 2
    column = (p // 2) * 2 + lax.rem(s, 2)
    k = lax.rem(column - z + 7, 4)
    return k < 3, z * 3 + jnp.minimum(k, 2)


def whole(*_):
    return pl.BlockSpec(memory_space=pltpu.VMEM)


VM = pl.BlockSpec(memory_space=pltpu.VMEM)
ANY = pl.BlockSpec(memory_space=pl.ANY)
SM = pl.BlockSpec(memory_space=pltpu.SMEM)


def params(**kw):
    return pltpu.CompilerParams(vmem_limit_bytes=VMEM_LIMIT, **kw)


def normed(v):
    centred = v - jnp.mean(v, -1, keepdims=True)
    rs = lax.rsqrt(jnp.mean(centred * centred, -1, keepdims=True) + LN_EPSILON)
    return centred * rs, rs


def put_split(ref, v):
    hi, lo = split(v)
    n = v.shape[0]
    ref[0:n, :] = hi
    ref[n : 2 * n, :] = lo


def front_kernel(x3, w_ref, gain_ref, pk_ref, x_ref, lhs):
    x = x3[...].reshape(ROWS, D)
    x_ref[...] = x
    n, _ = normed(x)
    put_split(lhs, n * gain_ref[...][None, :])
    for jj in range(3):
        parts = []
        for kind in range(3):
            c0 = kind * D + 256 * jj
            r = dot_nn(lhs[...], w_ref[:, c0 : c0 + 256])
            parts.append(r[:ROWS] + r[ROWS:])
        for half in range(2):
            q, k, v = (a[:, 128 * half : 128 * half + 128] for a in parts)
            h = 4 * jj + 2 * half
            pk_ref[h, 0:ROWS, :] = pick(k, swap(v))
            pk_ref[h + 1, 0:ROWS, :] = pick(swap(k), v)
            top, bottom = q[:HALF], q[HALF:]
            pk_ref[h, ROWS:PACK, :] = pick(top, swap(bottom))
            pk_ref[h + 1, ROWS:PACK, :] = pick(swap(top), bottom)


def front(x, w, gain):
    return pl.pallas_call(
        front_kernel,
        out_shape=[jax.ShapeDtypeStruct((HEADS, PACK, 128), F32)] + [jax.ShapeDtypeStruct((ROWS, D), F32)],
        in_specs=[VM] * 3,
        out_specs=[VM] * 2,
        scratch_shapes=[pltpu.VMEM((2 * ROWS, D), BF16)],
        compiler_params=params(),
    )(x, w, gain)


def place_facts():
    p, s = lax.axis_index("pat"), lax.axis_index("seq")
    x, core = p // 2, lax.rem(p, 2)
    active, head = head_here(p, s)
    return p, s, x, core, active, head


def home_device(core, m):
    return core * 2 + lax.rem(m, 2), m // 2


def head_device(h, b):
    hx, hs = head_place(h)
    return hx * 2 + b, hs


def same(p, s, q, t):
    return jnp.logical_and(p == q, s == t)


def to(p, s):
    return {"pat": p, "seq": s}


def scatter_kernel(forward, pk, own, *rest):
    if forward:
        sib, send, recv, fsend, frecv = rest
    else:
        send, recv = rest
    p, s, x, core, active, head = place_facts()
    slot = s * 2 + core
    barrier = pltpu.get_barrier_semaphore()

    @pl.when(active)
    def _():
        def greet(m, carry):
            q, t = home_device(core, m)

            @pl.when(jnp.logical_not(same(p, s, q, t)))
            def _():
                pl.semaphore_signal(barrier, inc=1, device_id=to(q, t), device_id_type=MESH)

            return carry

        lax.fori_loop(0, HOMES, greet, 0)
        if forward:
            pl.semaphore_signal(barrier, inc=1, device_id=to(x * 2 + 1 - core, s), device_id_type=MESH)

    mine = jnp.logical_and(active, core == x)
    waits = HEADS - mine.astype(jnp.int32)
    if forward:
        waits = waits + active.astype(jnp.int32)
    pl.semaphore_wait(barrier, waits)

    def copy(h):
        q, t = head_device(h, x)
        return q, t, pltpu.make_async_remote_copy(
            src_ref=pk.at[h],
            dst_ref=own.at[slot],
            send_sem=send.at[h],
            recv_sem=recv.at[slot],
            device_id=to(q, t),
            device_id_type=MESH,
        )

    def start(j, carry):
        h = lax.rem(j + 3 * (s // 2) + 2 * p, HEADS)
        q, t, remote = copy(h)

        @pl.when(same(p, s, q, t))
        def _():
            pltpu.make_async_copy(pk.at[h], own.at[slot], recv.at[slot]).start()

        @pl.when(jnp.logical_not(same(p, s, q, t)))
        def _():
            remote.start()

        return carry

    lax.fori_loop(0, HEADS, start, 0)

    def passed(m):
        return pltpu.make_async_remote_copy(
            src_ref=own.at[m, pl.ds(0, ROWS), :],
            dst_ref=sib.at[m],
            send_sem=fsend.at[m],
            recv_sem=frecv.at[m],
            device_id=to(x * 2 + 1 - core, s),
            device_id_type=MESH,
        )

    @pl.when(active)
    def _():
        def arrive(m, carry):
            pltpu.make_async_copy(own.at[m], own.at[m], recv.at[m]).wait()
            if forward:
                passed(m).start()
            return carry

        lax.fori_loop(0, HOMES, arrive, 0)
        if forward:

            def finish(m, carry):
                passed(m).wait()
                return carry

            lax.fori_loop(0, HOMES, finish, 0)

    def sent(h, carry):
        q, t, remote = copy(h)

        @pl.when(jnp.logical_not(same(p, s, q, t)))
        def _():
            remote.wait_send()

        return carry

    lax.fori_loop(0, HEADS, sent, 0)


def to_heads(packets, forward, cid):
    rows = packets.shape[1]
    shapes = [jax.ShapeDtypeStruct((HOMES, rows, 128), F32)]
    sems = [pltpu.SemaphoreType.DMA((HEADS,)), pltpu.SemaphoreType.DMA((HOMES,))]
    if forward:
        shapes.append(jax.ShapeDtypeStruct((HOMES, ROWS, 128), F32))
        sems += [pltpu.SemaphoreType.DMA((HOMES,)), pltpu.SemaphoreType.DMA((HOMES,))]
    return pl.pallas_call(
        functools.partial(scatter_kernel, forward),
        out_shape=shapes,
        in_specs=[ANY],
        out_specs=[ANY] * len(shapes),
        scratch_shapes=sems,
        compiler_params=params(collective_id=cid, has_side_effects=True),
    )(packets)


def home_barrier(p, s, x, core, active, barrier, also_sibling):
    def greet(h, carry):
        q, t = head_device(h, x)

        @pl.when(jnp.logical_not(same(p, s, q, t)))
        def _():
            pl.semaphore_signal(barrier, inc=1, device_id=to(q, t), device_id_type=MESH)

        return carry

    lax.fori_loop(0, HEADS, greet, 0)

    @pl.when(active)
    def _():
        if also_sibling:
            pl.semaphore_signal(barrier, inc=1, device_id=to(x * 2 + 1 - core, s), device_id_type=MESH)
        mine = (core == x).astype(jnp.int32)
        pl.semaphore_wait(barrier, HOMES - mine + (1 if also_sibling else 0))


def gather_kernel(pk, rec, send, recv):
    p, s, x, core, active, head = place_facts()
    barrier = pltpu.get_barrier_semaphore()
    home_barrier(p, s, x, core, active, barrier, False)

    def copy(m):
        q, t = home_device(core, m)
        return q, t, pltpu.make_async_remote_copy(
            src_ref=pk.at[m],
            dst_ref=rec.at[head],
            send_sem=send.at[m],
            recv_sem=recv.at[head],
            device_id=to(q, t),
            device_id_type=MESH,
        )

    @pl.when(active)
    def _():
        def start(j, carry):
            m = lax.rem(j + 2 * s + 1, HOMES)
            q, t, remote = copy(m)

            @pl.when(same(p, s, q, t))
            def _():
                pltpu.make_async_copy(pk.at[m], rec.at[head], recv.at[head]).start()

            @pl.when(jnp.logical_not(same(p, s, q, t)))
            def _():
                remote.start()

            return carry

        lax.fori_loop(0, HOMES, start, 0)

    def arrive(h, carry):
        pltpu.make_async_copy(rec.at[h], rec.at[h], recv.at[h]).wait()
        return carry

    lax.fori_loop(0, HEADS, arrive, 0)

    @pl.when(active)
    def _():
        def sent(m, carry):
            q, t, remote = copy(m)

            @pl.when(jnp.logical_not(same(p, s, q, t)))
            def _():
                remote.wait_send()

            return carry

        lax.fori_loop(0, HOMES, sent, 0)


def to_homes(packets, cid):
    rows = packets.shape[1]
    return pl.pallas_call(
        gather_kernel,
        out_shape=jax.ShapeDtypeStruct((HEADS, rows, 128), F32),
        in_specs=[ANY],
        out_specs=ANY,
        scratch_shapes=[pltpu.SemaphoreType.DMA((HOMES,)), pltpu.SemaphoreType.DMA((HEADS,))],
        compiler_params=params(collective_id=cid, has_side_effects=True),
    )(packets)


def tile_positions(rows, columns, row_classes, column_classes, t_step, class_step):
    r = lax.broadcasted_iota(jnp.int32, (rows, columns), 0)
    q = lax.broadcasted_iota(jnp.int32, (rows, columns), 1)
    rn, qn = rows // row_classes, columns // column_classes
    return (r % rn) * t_step + (r // rn) * class_step, (q % qn) * t_step + (q // qn) * class_step


def key_bias(q_shape, k_shape, t_step, class_step, shift, keys_first):
    nq, nk = q_shape[0] * q_shape[1], k_shape[0] * k_shape[1]
    if keys_first:
        kp, qp = tile_positions(nk, nq, k_shape[0], q_shape[0], t_step, class_step)
    else:
        qp, kp = tile_positions(nq, nk, q_shape[0], k_shape[0], t_step, class_step)
    return jnp.where(kp - qp <= shift, 0.0, NEG).astype(F32)


def unpack_keys(own, sib, b, kvf):
    def one(m, carry):
        c = 2 * b + lax.rem(m, 2)
        d = 2 * (1 - b) + lax.rem(m, 2)
        t = pl.multiple_of((m // 2) * ROWS, 64)
        kvf[c, pl.ds(t, ROWS), :] = own[m, 0:ROWS, :]
        kvf[d, pl.ds(t, ROWS), :] = sib[m]
        return carry

    lax.fori_loop(0, HOMES, one, 0)


def unpack_pairs(src, first, dst, scale):
    def one(m, carry):
        t = pl.multiple_of((m // 2) * ROWS, 32)
        v = src[m, first : first + HALF, :] * scale
        w = swap(v)
        dst[lax.rem(m, 2), pl.ds(t, HALF), :] = pick(v, w)
        dst[lax.rem(m, 2), pl.ds(t + HALF, HALF), :] = pick(w, v)
        return carry

    lax.fori_loop(0, HOMES, one, 0)


def keys_and_values(kv):
    hi, lo = split32(kv)
    k2 = pick(hi, swap(lo))
    v2 = pick(swap(hi), lo)
    return k2, v2


def doubled(v):
    return jnp.concatenate([v, v], 1)


def query_quads(qq):
    hi, lo = split32(qq)
    return jnp.concatenate([pick(hi, lo).astype(BF16), pick(lo, hi).astype(BF16)], 1)


def class_facts4(o4, b):
    keys = ((lax.rem(o4, 4), o4 // 4), (lax.rem(o4 + 6, 4), (o4 + 6) // 4))
    first = (keys[0][0] // 2) == b
    query = (jnp.where(first, keys[0][0], keys[1][0]), jnp.where(first, keys[0][1], keys[1][1]))
    return keys, jnp.where(first, 0, 1), query


def forward_kernel(info, own, sib, ap, lse, sums, kvf, kc, vc, qf, qc, k4, v4, q4, k5, v5, q5, acc, mx, R, b1, b2, b3, b4):
    active = info[0] == 1
    b = info[1]
    offs = [info[2 + i] for i in range(PATTERNS)]
    sums[...] = jnp.zeros_like(sums)

    @pl.when(active)
    def _():
        ones = jnp.ones((128, 128), BF16)
        unpack_keys(own, sib, b, kvf)
        unpack_pairs(own, ROWS, qf, 1.0 / math.sqrt(HD))

        def with_ones(v2):
            return jnp.concatenate([v2.astype(BF16), ones], 1)

        def prepare(i, carry):
            c, t = i // 12, pl.multiple_of(lax.rem(i, 12) * 128, 128)
            k2, v2 = keys_and_values(kvf[c, pl.ds(t, 128), :])
            kc[c, pl.ds(t, 128), :] = k2.astype(BF16)
            vc[c, pl.ds(t, 128), :] = with_ones(v2)
            return carry

        lax.fori_loop(0, 48, prepare, 0, unroll=2)

        def prepare_q(i, carry):
            c, t = i // 12, pl.multiple_of(lax.rem(i, 12) * 128, 128)
            qc[c, pl.ds(t, 128), :] = query_quads(qf[c, pl.ds(t, 128), :])
            return carry

        lax.fori_loop(0, 24, prepare_q, 0, unroll=2)

        keys4, e4, (qc4, qv4) = class_facts4(offs[3], b)
        kc5, kv5 = lax.rem(offs[4], 4), offs[4] // 4
        for blk in range(4):
            r = slice(128 * blk, 128 * blk + 128)
            for e in range(2):
                c, v = keys4[e]
                k2, v2 = keys_and_values(kvf[c, pl.ds(v + 384 * blk, 128, stride=3), :])
                k4[e, r, :] = k2.astype(BF16)
                v4[e, r, :] = with_ones(v2)
            q4[r, :] = query_quads(qf[qc4 - 2 * b, pl.ds(qv4 + 384 * blk, 128, stride=3), :])
            k2, v2 = keys_and_values(kvf[kc5, pl.ds(kv5 + 384 * blk, 128, stride=3), :])
            k5[r, :] = k2.astype(BF16)
            v5[r, :] = with_ones(v2)
            q5[r, :] = query_quads(qf[lax.rem(kc5, 2), pl.ds(kv5 + 384 * blk, 128, stride=3), :])

        b1[...] = key_bias((2, 128), (4, 128), 4, 1, 2 * b, False)
        b2[...] = key_bias((1, 256), (2, 256), 4, 2, 2 * b, False)
        b3[...] = key_bias((1, 512), (1, 512), 1, 1, 0, False)
        b4[...] = key_bias((1, 256), (2, 256), 12, 6, 6 * e4, False)

        def tile(start, q, k, v, bias, classes, first):
            n = q.shape[0]
            each = n // classes
            per = 1536 // classes if classes == 1 else 512
            s = dot_nt(q, doubled(k))
            wide = s.shape[1]
            own_rows = bias.shape[0] // classes
            s = s.reshape(classes, each, wide)
            edge = s[:, :own_rows] + bias[...].reshape(classes, own_rows, wide)
            s = edge if each == own_rows else jnp.concatenate([edge, s[:, own_rows:]], 1)
            s = s.reshape(n, wide)
            top = jnp.max(s, -1, keepdims=True)

            def where(c):
                return pl.ds(c * per + start, each)

            def load(ref):
                return jnp.concatenate([ref[where(c), :] for c in range(classes)], 0)

            def store(ref, value):
                for c in range(classes):
                    ref[where(c), :] = value[c * each : c * each + each]

            if first:
                m = jnp.broadcast_to(top, (n, 128))
            else:
                old = load(mx)
                m = jnp.maximum(old, top)
            p = jnp.exp(s - jnp.concatenate([m] * (wide // 128), 1))
            hi, lo = split(p)
            new = dot_nn(jnp.concatenate([hi, lo], 0), v)
            new = new[:n] + new[n:]
            if not first:
                new = load(acc) * doubled(jnp.exp(old - m)) + new
            store(acc, new)
            store(mx, m)

        def closed(pattern, rows):
            value, m = acc[rows, :], mx[rows, :]
            o, l = value[:, :128], value[:, 128:]
            sums[pattern : pattern + 1, :] += jnp.sum(m + jnp.log(l), 0, keepdims=True)
            lane = lax.broadcasted_iota(jnp.int32, m.shape, 1)
            return jnp.where(lane < HD, o + swap(o), jnp.where(lane < 96, l, m))

        def merge(pattern, ci, rows, of):
            r0, r1 = R[ci, rows, :], closed(pattern, of)
            m0 = jnp.broadcast_to(r0[:, 96:97], r0.shape)
            m1 = jnp.broadcast_to(r1[:, 96:97], r1.shape)
            m = jnp.maximum(m0, m1)
            both = r0 * jnp.exp(m0 - m) + r1 * jnp.exp(m1 - m)
            lane = lax.broadcasted_iota(jnp.int32, r0.shape, 1)
            R[ci, rows, :] = jnp.where(lane < 96, both, m)

        def q1(g, carry):
            base = 512 * g

            def at(t, n):
                return pl.ds(pl.multiple_of(base + t, 128), n)

            for kb in range(4):
                start = 128 * kb
                each = 512 - start
                ks = at(start, 128)
                tile(
                    start,
                    qc[:, at(start, each), :].reshape(2 * each, 256),
                    kc[:, ks, :].reshape(512, 128),
                    vc[:, ks, :].reshape(512, 256),
                    b1,
                    2,
                    kb == 0,
                )
            for c in range(2):
                for i in range(2):
                    R[c, at(256 * i, 256), :] = closed(0, pl.ds(512 * c + 256 * i, 256))
            return carry

        lax.fori_loop(0, 3, q1, 0)

        par = offs[1]
        for base, length in ((0, 1024), (1024, 512)):
            for start in range(0, length, 256):
                ks = slice(base + start, base + start + 256)
                tile(
                    start,
                    qc[par, base + start : base + length, :],
                    jnp.concatenate([kc[par, ks, :], kc[par + 2, ks, :]], 0),
                    jnp.concatenate([vc[par, ks, :], vc[par + 2, ks, :]], 0),
                    b2,
                    1,
                    start == 0,
                )

            def join2(i, carry, base=base):
                t = pl.multiple_of(i * 256, 256)
                merge(1, par, pl.ds(base + t, 256), pl.ds(t, 256))
                return carry

            lax.fori_loop(0, length // 256, join2, 0)

        o3 = offs[2]

        @pl.when(o3 // 2 == b)
        def _():
            ci = lax.rem(o3, 2)
            for start in range(0, TOTAL, 512):
                ks = slice(start, start + 512)
                tile(start, qc[ci, start:TOTAL, :], kc[o3, ks, :], vc[o3, ks, :], b3, 1, start == 0)

            def join3(i, carry):
                t = pl.multiple_of(i * 256, 256)
                merge(2, ci, pl.ds(t, 256), pl.ds(t, 256))
                return carry

            lax.fori_loop(0, TOTAL // 256, join3, 0)

        for start in range(0, THIRD, 256):
            ks = slice(start, start + 256)
            tile(
                start, q4[start:THIRD, :], k4[:, ks, :].reshape(512, 128), v4[:, ks, :].reshape(512, 256), b4, 1, start == 0
            )
        for i in range(2):
            merge(3, qc4 - 2 * b, pl.ds(qv4 + 768 * i, 256, stride=3), pl.ds(256 * i, 256))

        @pl.when(kc5 // 2 == b)
        def _():
            tile(0, q5[...], k5[...], v5[...], b3, 1, True)
            for i in range(2):
                merge(4, lax.rem(kc5, 2), pl.ds(kv5 + 768 * i, 256, stride=3), pl.ds(256 * i, 256))

        def finish(m, carry):
            ci = lax.rem(m, 2)
            rows = pl.ds(pl.multiple_of((m // 2) * ROWS, 64), ROWS)
            r = R[ci, rows, :]
            l = jnp.broadcast_to(r[:, HD : HD + 1], r.shape)
            out = r / l
            ap[m] = pick(out[:HALF], swap(out[HALF:]))
            lse[ci, rows, :] = jnp.broadcast_to(r[:, 96:97], r.shape) + jnp.log(l)
            return carry

        lax.fori_loop(0, HOMES, finish, 0, unroll=2)


def attention_forward(info, own, sib):
    state = pltpu.VMEM((2, TOTAL, 128), F32)
    return pl.pallas_call(
        forward_kernel,
        out_shape=[
            jax.ShapeDtypeStruct((HOMES, HALF, 128), F32),
            jax.ShapeDtypeStruct((2, TOTAL, 128), F32),
            jax.ShapeDtypeStruct((8, 128), F32),
        ],
        in_specs=[SM, VM, VM],
        out_specs=[VM, VM, VM],
        scratch_shapes=[
            pltpu.VMEM((4, TOTAL, 128), F32),
            pltpu.VMEM((4, TOTAL, 128), BF16),
            pltpu.VMEM((4, TOTAL, 256), BF16),
            state,
            pltpu.VMEM((2, TOTAL, 256), BF16),
            pltpu.VMEM((2, THIRD, 128), BF16),
            pltpu.VMEM((2, THIRD, 256), BF16),
            pltpu.VMEM((THIRD, 256), BF16),
            pltpu.VMEM((THIRD, 128), BF16),
            pltpu.VMEM((THIRD, 256), BF16),
            pltpu.VMEM((THIRD, 256), BF16),
            pltpu.VMEM((TOTAL, 256), F32),
            pltpu.VMEM((TOTAL, 128), F32),
            state,
            pltpu.VMEM((256, 512), F32),
            pltpu.VMEM((256, 512), F32),
            pltpu.VMEM((512, 512), F32),
            pltpu.VMEM((256, 512), F32),
        ],
        compiler_params=params(),
    )(info, own, sib)


class Place:
    def __init__(self):
        p, s = lax.axis_index("pat"), lax.axis_index("seq")
        self.p, self.s = p, s
        self.x, self.core, self.z, self.y = p // 2, lax.rem(p, 2), s // 2, lax.rem(s, 2)
        self.peer = to(self.x * 2 + 1 - self.core, s)
        self.xn = to((1 - self.x) * 2 + self.core, s)
        self.yn = to(p, self.z * 2 + 1 - self.y)
        self.left, self.right = to(p, s - 2), to(p, s + 2)

    def greet(self, barrier, line=True):
        for d in (self.peer, self.xn, self.yn):
            pl.semaphore_signal(barrier, inc=1, device_id=d, device_id_type=MESH)
        if not line:
            return 3

        @pl.when(self.z > 0)
        def _():
            pl.semaphore_signal(barrier, inc=1, device_id=self.left, device_id_type=MESH)

        @pl.when(self.z < 3)
        def _():
            pl.semaphore_signal(barrier, inc=1, device_id=self.right, device_id_type=MESH)

        return 3 + (self.z > 0).astype(jnp.int32) + (self.z < 3).astype(jnp.int32)


def remote(src, dst, a, b, d):
    return pltpu.make_async_remote_copy(
        src_ref=src, dst_ref=dst, send_sem=a, recv_sem=b, device_id=d, device_id_type=MESH
    )


def add_in(dst, src):
    lead = dst.shape[:-2]

    def one(i, carry):
        index = []
        for d in reversed(lead):
            index.insert(0, lax.rem(i, d))
            i = i // d
        dst[tuple(index)] += src[tuple(index)]
        return carry

    lax.fori_loop(0, math.prod(lead), one, 0)


class Sems:
    NAMES = ("sc", "rc", "s1", "r1", "s2", "r2", "sl", "rl", "sr", "rr")

    def __init__(self, refs):
        for name, ref in zip(self.NAMES, refs):
            setattr(self, name, ref)

    @staticmethod
    def scratch(n):
        dma = pltpu.SemaphoreType.DMA
        return [dma((n, 2)), dma((n, 2))] + [dma((n,)) for _ in range(8)]


class Chunk:
    def __init__(self, place, k, x_first, sems, b0=None, b1=None, b2=None, bl=None, br=None, part=None, put=None):
        self.at, self.k, self.x_first, self.sems = place, k, x_first, sems
        self.b0, self.b1, self.b2, self.bl, self.br = b0, b1, b2, bl, br
        self.part, self.put = part, put

    def core(self, i):
        k, m = self.k, self.sems
        return remote(self.part(i, 1 - self.at.core), self.b0.at[i], m.sc.at[k, i], m.rc.at[k, i], self.at.peer)

    def one(self):
        k, at, m = self.k, self.at, self.sems
        if self.x_first:
            return remote(self.b0.at[1 - at.x], self.b1, m.s1.at[k], m.r1.at[k], at.xn)
        return remote(self.b0.at[:, :, 1 - at.y], self.b1, m.s1.at[k], m.r1.at[k], at.yn)

    def two(self):
        k, at, m = self.k, self.at, self.sems
        if self.x_first:
            return remote(self.b1.at[:, 1 - at.y], self.b2, m.s2.at[k], m.r2.at[k], at.yn)
        return remote(self.b1.at[1 - at.x], self.b2, m.s2.at[k], m.r2.at[k], at.xn)

    def rightward(self, i):
        k, part, m = self.k, pl.ds(i + 1, 3 - i), self.sems
        src = self.b2 if i == 0 else self.bl
        return remote(src.at[part], self.bl.at[part], m.sr.at[k], m.rl.at[k], self.at.right)

    def leftward(self, i):
        k, part, m = self.k, pl.ds(0, i), self.sems
        src = self.b2 if i == 3 else self.br
        return remote(src.at[part], self.br.at[part], m.sl.at[k], m.rr.at[k], self.at.left)

    def own_core(self, i):
        self.core(i).wait_recv()
        add_in(self.b0.at[i], self.part(i, self.at.core))

    def stage1(self):
        for i in range(2):
            self.own_core(i)
        self.one().start()

    def arrived(self):
        self.one().wait_recv()
        add_in(self.b1, self.b0.at[self.at.x] if self.x_first else self.b0.at[:, :, self.at.y])

    def stage2(self):
        self.arrived()
        self.two().start()

    def stage3(self):
        self.two().wait_recv()
        add_in(self.b2, self.b1.at[:, self.at.y] if self.x_first else self.b1.at[self.at.x])

        @pl.when(self.at.z == 0)
        def _():
            self.rightward(0).start()

        @pl.when(self.at.z == 3)
        def _():
            self.leftward(3).start()

    def stage4(self):
        @pl.when(self.at.z == 1)
        def _():
            self.rightward(0).wait_recv()
            self.bl[2:4] += self.b2[2:4]
            self.rightward(1).start()

        @pl.when(self.at.z == 2)
        def _():
            self.leftward(3).wait_recv()
            self.br[0:2] += self.b2[0:2]
            self.leftward(2).start()

    def stage5(self):
        @pl.when(self.at.z == 2)
        def _():
            self.rightward(1).wait_recv()
            self.bl[3:4] += self.b2[3:4]
            self.rightward(2).start()

        @pl.when(self.at.z == 1)
        def _():
            self.leftward(2).wait_recv()
            self.br[0:1] += self.b2[0:1]
            self.leftward(1).start()

    def stage6(self):
        @pl.when(self.at.z == 3)
        def _():
            self.rightward(2).wait_recv()
            self.put(self.b2[3] + self.bl[3])

        @pl.when(self.at.z == 0)
        def _():
            self.leftward(1).wait_recv()
            self.put(self.b2[0] + self.br[0])

        @pl.when(self.at.z == 1)
        def _():
            self.put(self.b2[1] + self.bl[1] + self.br[1])

        @pl.when(self.at.z == 2)
        def _():
            self.put(self.b2[2] + self.bl[2] + self.br[2])

    def line_sent(self):
        for i in range(4):

            @pl.when(self.at.z == i)
            def _(i=i):
                if i < 3:
                    self.rightward(i).wait_send()
                if i > 0:
                    self.leftward(i).wait_send()


class Reducer:
    def __init__(self, place, n, part, scratch, put):
        self.place, self.n, self.part, self.put = place, n, part, put
        self.c0, self.c1a, self.c1b, self.c2, self.zl, self.zr = scratch[:6]
        self.sems = Sems(scratch[6:16])
        self.pairs = (n + 1) // 2

    @staticmethod
    def scratch(n, rows):
        bufs = [(n, 2, 4, 2), ((n + 1) // 2, 4, 2), (max(n // 2, 1), 2, 4), (n, 4), (n, 4), (n, 4)]
        return [pltpu.VMEM(b + (rows, D), F32) for b in bufs] + Sems.scratch(n)

    def chunk(self, k, parity):
        return Chunk(
            self.place,
            k,
            parity == 0,
            self.sems,
            self.c0.at[k],
            (self.c1b if parity else self.c1a).at[k // 2],
            self.c2.at[k],
            self.zl.at[k],
            self.zr.at[k],
            self.part(k),
            lambda v: self.put(k, v),
        )

    def send(self, first, after):
        for k in range(first, after):
            for i in range(2):
                self.chunk(jnp.int32(k), 0).core(i).start()

    def one(self, stage, pair):
        for parity in range(2):
            k = jnp.int32(2 * pair + parity)

            @pl.when(jnp.logical_and(k >= 0, k < self.n))
            def _(k=k, parity=parity):
                getattr(self.chunk(k, parity), f"stage{stage}")()

    def early(self, pair):
        self.one(1, pair)

    def step(self, tau):
        self.one(1, tau)
        for stage in range(2, 7):
            self.one(stage, tau - stage)

    def finish(self):
        def one(k, carry):
            for parity in range(2):

                @pl.when(lax.rem(k, 2) == parity)
                def _(parity=parity):
                    c = self.chunk(k, parity)
                    for i in range(2):
                        c.core(i).wait_send()
                    c.one().wait_send()
                    c.two().wait_send()
                    c.line_sent()

            return carry

        lax.fori_loop(0, self.n, one, 0)


class SmallSum:
    def __init__(self, place, S, bufs, send, recv, put):
        self.at, self.S, self.send, self.recv, self.put = place, S, send, recv, put
        self.d0, self.d1, self.d2, self.dl, self.dr, self.t1, self.t2, self.t3, self.fl, self.fr = bufs

    @staticmethod
    def scratch():
        return [pltpu.VMEM((8, D), F32)] * 10 + [pltpu.SemaphoreType.DMA((5,)), pltpu.SemaphoreType.DMA((5,))]

    def hop(self, src, dst, i, d):
        return remote(src, dst, self.send.at[i], self.recv.at[i], d)

    def core(self):
        return self.hop(self.S, self.d0, 0, self.at.peer)

    def along_x(self):
        return self.hop(self.t1, self.d1, 1, self.at.xn)

    def along_y(self):
        return self.hop(self.t2, self.d2, 2, self.at.yn)

    def rightward(self, i):
        return self.hop(self.t3 if i == 0 else self.fl, self.dl, 3, self.at.right)

    def leftward(self, i):
        return self.hop(self.t3 if i == 3 else self.fr, self.dr, 4, self.at.left)

    def stage1(self):
        self.core().wait_recv()
        self.t1[...] = self.S[...] + self.d0[...]
        self.along_x().start()

    def stage2(self):
        self.along_x().wait_recv()
        self.t2[...] = self.t1[...] + self.d1[...]
        self.along_y().start()

    def stage3(self):
        self.along_y().wait_recv()
        self.t3[...] = self.t2[...] + self.d2[...]

        @pl.when(self.at.z == 0)
        def _():
            self.rightward(0).start()

        @pl.when(self.at.z == 3)
        def _():
            self.leftward(3).start()

    def from_left(self, i):
        self.rightward(i).wait_recv()
        self.fl[...] = self.dl[...] + self.t3[...]

    def from_right(self, i):
        self.leftward(i).wait_recv()
        self.fr[...] = self.dr[...] + self.t3[...]

    def stage4(self):
        @pl.when(self.at.z == 1)
        def _():
            self.from_left(0)
            self.rightward(1).start()

        @pl.when(self.at.z == 2)
        def _():
            self.from_right(3)
            self.leftward(2).start()

    def stage5(self):
        @pl.when(self.at.z == 2)
        def _():
            self.from_left(1)
            self.rightward(2).start()

        @pl.when(self.at.z == 1)
        def _():
            self.from_right(2)
            self.leftward(1).start()

    def stage6(self):
        @pl.when(self.at.z == 3)
        def _():
            self.from_left(2)
            self.put(self.fl[...])

        @pl.when(self.at.z == 0)
        def _():
            self.from_right(1)
            self.put(self.fr[...])

        @pl.when(jnp.logical_or(self.at.z == 1, self.at.z == 2))
        def _():
            self.put(self.fl[...] + self.dr[...])

    def finish(self):
        for c in (self.core(), self.along_x(), self.along_y()):
            c.wait_send()
        for i in range(4):

            @pl.when(self.at.z == i)
            def _(i=i):
                if i < 3:
                    self.rightward(i).wait_send()
                if i > 0:
                    self.leftward(i).wait_send()


def small_outputs(place, counts, outs, tot):
    ga, gi, gf, gh, means = outs

    def put(v):
        tot[...] = v
        d = place.p * RUNS + place.s
        for i, ref in enumerate((ga, gi, gf)):
            ref[...] = pltpu.roll(tot[i : i + 1, :], D - PIECE * d, 1)[:, :PIECE]
        row = tot[pl.ds(3 + d // 8, 1), :]
        gh[...] = pltpu.roll(row, D - 4 * PIECE * lax.rem(d, 8), 1)[:, : 4 * PIECE]
        lane = lax.broadcasted_iota(jnp.int32, (1, 128), 1)
        scale = jnp.full((1, 128), counts[0], F32)
        for i in range(1, PATTERNS):
            scale = jnp.where(lane == i, counts[i], scale)
        means[...] = (tot[7:8, :128] / scale)[:, :PATTERNS]

    return put


N_PIECES = 9
SUB = 8


def finish_kernel(counts, rec, x_ref, dy1_ref, w, ga1, S_in, gx, g_qkv, ga, gi, gf, gh, means, dqkv, lhs, th, tl, r_hi, r_lo, tiles, S, tot, *scratch):
    place = Place()
    barrier = pltpu.get_barrier_semaphore()
    expected = place.greet(barrier)
    for j in range(HEADS // 2):
        u, v = rec[2 * j, ROWS:PACK, :], rec[2 * j + 1, ROWS:PACK, :]
        cols = slice(128 * j, 128 * j + 128)
        dqkv[0:HALF, cols] = pick(u, swap(v))
        dqkv[HALF:ROWS, cols] = pick(swap(u), v)
        u, v = rec[2 * j, 0:ROWS, :], rec[2 * j + 1, 0:ROWS, :]
        dqkv[:, D + 128 * j : D + 128 * j + 128] = pick(u, swap(v))
        dqkv[:, 2 * D + 128 * j : 2 * D + 128 * j + 128] = pick(swap(u), v)
    gain = ga1[...][None, :]
    n, rs = normed(x_ref[...])
    put_turned(th, tl, n * gain)

    def part(k):
        rows = pl.ds(pl.multiple_of(lax.rem(k, 3) * SUB, SUB), SUB)
        return lambda i, c: tiles.at[k // 3, i, c, :, :, rows, :]

    def put(k, v):
        g_qkv[
            pl.ds(pl.multiple_of(lax.rem(k, 3) * SUB, SUB), SUB), pl.ds(pl.multiple_of((k // 3) * D, D), D)
        ] = v

    n_r = 16
    big = Reducer(place, N_PIECES, part, scratch[:n_r], put)
    rest = scratch[n_r:]
    small = SmallSum(
        place, S, rest[:10], rest[10], rest[11], small_outputs(place, counts, (ga, gi, gf, gh, means), tot)
    )
    for j in range(3):
        r_hi[...], r_lo[...] = split(dqkv[:, D * j : D * j + D])

        def one(i, carry):
            rows = pl.ds(pl.multiple_of(i * 2 * ROWS, 128), 2 * ROWS)
            h, l = th[rows, :], tl[rows, :]
            v = dot_nn(h, r_hi[...]) + dot_nn(h, r_lo[...]) + dot_nn(l, r_hi[...])
            tiles[j, i] = v.reshape(2, 4, 2, PIECE, D)
            return carry

        lax.fori_loop(0, 2, one, 0)
        if j == 0:
            pl.semaphore_wait(barrier, expected)
        big.send(3 * j, 3 * j + 3)
        if j > 0:
            big.early(j - 1)
    e = None
    for j in range(3):
        cols = slice(D * j, D * j + D)
        put_split(lhs, dqkv[:, cols])
        more = halves_sum(dot_nt(lhs[...], w[:, cols]))
        e = more if e is None else e + more
        if j == 0:
            big.step(2)
    S[...] = S_in[...]
    S[0:1, :] = jnp.sum(e * n, 0, keepdims=True)
    small.core().start()
    gx[...] = (dy1_ref[...] + norm_back(e * gain, n, rs)).reshape(ROWS, 1, D)
    small.stage1()

    def step(tau, carry):
        for stage in range(2, 7):

            @pl.when(tau == stage + 1)
            def _(stage=stage):
                getattr(small, f"stage{stage}")()

        big.step(tau)
        return carry

    lax.fori_loop(3, big.pairs + 6, step, 0)

    big.finish()
    small.finish()


def finish(rec, x, dy1, w, ga, S, counts, cid):
    return pl.pallas_call(
        functools.partial(finish_kernel, counts),
        out_shape=[jax.ShapeDtypeStruct((ROWS, 1, D), F32), jax.ShapeDtypeStruct((PIECE, 3 * D), F32)]
        + [jax.ShapeDtypeStruct((1, n), F32) for n in (PIECE, PIECE, PIECE, 4 * PIECE, PATTERNS)],
        in_specs=[VM] * 6,
        out_specs=[VM] * 7,
        scratch_shapes=[
            pltpu.VMEM((ROWS, 3 * D), F32),
            pltpu.VMEM((2 * ROWS, D), BF16),
            pltpu.VMEM((D, ROWS), BF16),
            pltpu.VMEM((D, ROWS), BF16),
            pltpu.VMEM((ROWS, D), BF16),
            pltpu.VMEM((ROWS, D), BF16),
            pltpu.VMEM((3, 2, 2, 4, 2, PIECE, D), F32),
            pltpu.VMEM((8, D), F32),
            pltpu.VMEM((8, D), F32),
        ]
        + Reducer.scratch(N_PIECES, SUB)
        + SmallSum.scratch(),
        compiler_params=params(collective_id=cid, has_side_effects=True),
    )(rec, x, dy1, w, ga, S)


def deliver_kernel(*refs):
    n = len(refs) // 2
    for src, dst in zip(refs[:n], refs[n:]):
        dst[...] = src[...]


def deliver(*arrays):
    return pl.pallas_call(
        deliver_kernel,
        out_shape=[jax.ShapeDtypeStruct(v.shape, v.dtype) for v in arrays],
        in_specs=[VM] * len(arrays),
        out_specs=[VM] * len(arrays),
        compiler_params=params(),
    )(*arrays)


def rows_from_pairs(rec, dst):
    for j in range(HEADS // 2):
        u, v = rec[2 * j], rec[2 * j + 1]
        cols = slice(128 * j, 128 * j + 128)
        dst[0:HALF, cols] = pick(u, swap(v))
        dst[HALF:ROWS, cols] = pick(swap(u), v)


def pairs_from_rows(src, dst):
    for j in range(HEADS // 2):
        top = src[0:HALF, 128 * j : 128 * j + 128]
        bottom = src[HALF:ROWS, 128 * j : 128 * j + 128]
        dst[2 * j] = pick(top, swap(bottom))
        dst[2 * j + 1] = pick(swap(top), bottom)


def halves_sum(r):
    return r[:ROWS] + r[ROWS:]


def norm_back(f, n, rs):
    return (f - jnp.mean(f, -1, keepdims=True) - n * jnp.mean(f * n, -1, keepdims=True)) * rs


def put_turned(hi_ref, lo_ref, v):
    for j in range(D // 128):
        t = v[:, 128 * j : 128 * j + 128].T
        hi, lo = split(t)
        hi_ref[128 * j : 128 * j + 128, :] = hi
        lo_ref[128 * j : 128 * j + 128, :] = lo


class ToHeads:
    def __init__(self, pk, rec, send, recv):
        self.pk, self.rec, self.send, self.recv = pk, rec, send, recv
        self.facts = place_facts()

    def greet(self):
        p, s, x, core, active, head = self.facts
        barrier = pltpu.get_barrier_semaphore()

        @pl.when(active)
        def _():
            def one(m, carry):
                q, t = home_device(core, m)

                @pl.when(jnp.logical_not(same(p, s, q, t)))
                def _():
                    pl.semaphore_signal(barrier, inc=1, device_id=to(q, t), device_id_type=MESH)

                return carry

            lax.fori_loop(0, HOMES, one, 0)

    def copy(self, h):
        p, s, x, core, active, head = self.facts
        slot = s * 2 + core
        q, t = head_device(h, x)
        far = pltpu.make_async_remote_copy(
            src_ref=self.pk.at[h],
            dst_ref=self.rec.at[slot],
            send_sem=self.send.at[h],
            recv_sem=self.recv.at[slot],
            device_id=to(q, t),
            device_id_type=MESH,
        )
        return same(p, s, q, t), lambda: pltpu.make_async_copy(self.pk.at[h], self.rec.at[slot], self.recv.at[slot]), far

    def wait(self, others):
        p, s, x, core, active, head = self.facts
        mine = jnp.logical_and(active, core == x).astype(jnp.int32)
        pl.semaphore_wait(pltpu.get_barrier_semaphore(), HEADS + others - mine)

    def start(self):
        p, s, x, core, active, head = self.facts

        def one(j, carry):
            here, near, far = self.copy(lax.rem(j + 3 * (s // 2) + 2 * p, HEADS))

            @pl.when(here)
            def _():
                near().start()

            @pl.when(jnp.logical_not(here))
            def _():
                far.start()

            return carry

        lax.fori_loop(0, HEADS, one, 0)

    def finish(self):
        active = self.facts[4]

        @pl.when(active)
        def _():
            def arrive(m, carry):
                pltpu.make_async_copy(self.rec.at[m], self.rec.at[m], self.recv.at[m]).wait()
                return carry

            lax.fori_loop(0, HOMES, arrive, 0)

        def sent(h, carry):
            here, near, far = self.copy(h)

            @pl.when(jnp.logical_not(here))
            def _():
                far.wait_send()

            return carry

        lax.fori_loop(0, HEADS, sent, 0)


FT = 512


def product(hi, lo, r_hi, r_lo, put):
    def one(i, carry):
        rows = pl.ds(pl.multiple_of(i * 2 * ROWS, 128), 2 * ROWS)
        h, l = hi[rows, :], lo[rows, :]
        put(i, dot_nn(h, r_hi[...]) + dot_nn(h, r_lo[...]) + dot_nn(l, r_hi[...]))
        return carry

    lax.fori_loop(0, 2, one, 0)


N_FF = 9
N_COLS = 5


def ff_kernel(rec, x_ref, g3, wo, wu, wd, gi1, gf1, gh1, sums, out3, drec, dy1_ref, S, C0, C1a, C1b, dap, lhs, lhs2, gi, gf, gh, gh_g, g_ref, out_ref, V, N1, U, GP, E, ACC, th, tl, r_hi, r_lo, cols_t, rows_t, c0, c1a, c1b, osem, dsend, drecv, *rsems):
    place = Place()
    sems = Sems(rsems)
    travel = ToHeads(dap, drec, dsend, drecv)
    travel.greet()
    place.greet(pltpu.get_barrier_semaphore(), False)

    def chunk(k, part=None):
        x_first = k % 2 == 0
        b1 = None if k < N_COLS else (c1a if x_first else c1b).at[(k - N_COLS) // 2]
        return Chunk(place, k, x_first, sems, c0.at[k], b1, part=part)

    for wide, flat in ((gi, gi1), (gf, gf1), (gh, gh1)):
        wide[...] = flat[...][None, :]
    g_ref[...] = g3[...].reshape(ROWS, D)
    rows_from_pairs(rec, V)
    na, rs_a = normed(V[...])
    V[...] = na
    put_split(lhs, na * gi[...])
    for j in range(3):
        cols = slice(256 * j, 256 * j + 256)
        N1[:, cols] = x_ref[:, cols] + halves_sum(dot_nn(lhs[...], wo[:, cols]))
    y1 = N1[...]
    out_ref[...] = y1
    ny, rs_y = normed(y1)
    N1[...] = ny
    put_split(lhs, ny * gf[...])

    def up(j, su):
        cols = pl.ds(pl.multiple_of(j * FT, FT), FT)
        z = halves_sum(dot_nn(lhs[...], wu[:, cols]))
        phi = 0.5 * (1.0 + lax.erf(z * math.sqrt(0.5)))
        u = z * phi
        U[:, cols] = u
        GP[:, cols] = phi + z * jnp.exp(-0.5 * z * z) * (1.0 / math.sqrt(2.0 * math.pi))
        return su + jnp.sum(u, -1, keepdims=True)

    zero = jnp.zeros((ROWS, 1), F32)
    mean = lax.fori_loop(0, FF // FT, up, zero) * (1.0 / FF)

    def spread(j, sv):
        cols = pl.ds(pl.multiple_of(j * FT, FT), FT)
        c = U[:, cols] - mean
        return sv + jnp.sum(c * c, -1, keepdims=True)

    rs_u = lax.rsqrt(lax.fori_loop(0, FF // FT, spread, zero) * (1.0 / FF) + LN_EPSILON)
    ACC[...] = jnp.zeros_like(ACC)

    def lower(j, carry):
        cols = pl.ds(pl.multiple_of(j * FT, FT), FT)
        n = (U[:, cols] - mean) * rs_u
        U[:, cols] = n
        put_split(lhs2, n * gh[:, cols])
        ACC[...] += halves_sum(dot_nn(lhs2[...], wd[cols, :]))
        return carry

    lax.fori_loop(0, FF // FT, lower, 0)
    out3[...] = (out_ref[...] + ACC[...]).reshape(ROWS, 1, D)

    travel.wait(3)
    r_hi[...], r_lo[...] = split(g_ref[...])

    def down(j, q):
        return chunk(N_COLS + q, lambda i, c: rows_t.at[j % 2, :, :, q])

    for j in range(5):
        if j < 4:
            cols = slice(D * j, D * j + D)
            put_turned(th, tl, U[:, cols] * gh[:, cols])
            if j >= 2:

                @pl.when(place.core != j % 2)
                def _(j=j):
                    for q in range(4):
                        down(j - 2, q).core(j // 2 - 1).wait_send()

            def put(i, v, j=j):
                rows_t[j % 2, pl.ds(2 * i, 2)] = v.reshape(2, 2, 4, PIECE, D)

            product(th, tl, r_hi, r_lo, put)

            @pl.when(place.core != j % 2)
            def _(j=j):
                for q in range(4):
                    down(j, q).core(j // 2).start()

        if j > 0:

            @pl.when(place.core == (j - 1) % 2)
            def _(j=j - 1):
                for q in range(4):
                    down(j, q).own_core(j // 2)

    for k in range(N_COLS, N_FF):
        chunk(k).one().start()

    put_split(lhs, g_ref[...])

    def back_down(j, sums):
        cols = pl.ds(pl.multiple_of(j * FT, FT), FT)
        e = halves_sum(dot_nt(lhs[...], wd[cols, :]))
        n = U[:, cols]
        gh_g[:, cols] = jnp.sum(e * n, 0, keepdims=True)
        f = e * gh[:, cols]
        E[:, cols] = f
        return sums[0] + jnp.sum(f, -1, keepdims=True), sums[1] + jnp.sum(f * n, -1, keepdims=True)

    sf, sfn = lax.fori_loop(0, FF // FT, back_down, (zero, zero))
    mf, mfn = sf * (1.0 / FF), sfn * (1.0 / FF)
    ACC[...] = jnp.zeros_like(ACC)

    def back_up(j, carry):
        cols = pl.ds(pl.multiple_of(j * FT, FT), FT)
        dz = (E[:, cols] - mf - U[:, cols] * mfn) * rs_u * GP[:, cols]
        E[:, cols] = dz
        put_split(lhs2, dz)
        ACC[...] += halves_sum(dot_nt(lhs2[...], wu[:, cols]))
        return carry

    lax.fori_loop(0, FF // FT, back_up, 0)
    e = ACC[...]
    ny = N1[...]
    S[2:3, :] = jnp.sum(e * ny, 0, keepdims=True)
    dy1 = g_ref[...] + norm_back(e * gf[...], ny, rs_y)
    dy1_ref[...] = dy1
    put_split(lhs, dy1)
    for j in range(3):
        cols = slice(256 * j, 256 * j + 256)
        ACC[:, cols] = halves_sum(dot_nt(lhs[...], wo[cols, :]))
    e = ACC[...]
    na = V[...]
    S[1:2, :] = jnp.sum(e * na, 0, keepdims=True)
    S[0:1, :] = jnp.zeros((1, D), F32)
    for j in range(4):
        S[3 + j : 4 + j, :] = gh_g[:, D * j : D * j + D]
    lane = lax.broadcasted_iota(jnp.int32, (1, 128), 1)
    S[7:8, :] = jnp.zeros((1, D), F32)
    S[7:8, 0:128] = sum(jnp.where(lane == i, sums[i : i + 1, :], 0.0) for i in range(PATTERNS))
    ACC[...] = norm_back(e * gi[...], na, rs_a)
    pairs_from_rows(ACC, dap)
    travel.start()

    def column(k):
        return chunk(k, lambda i, c: cols_t.at[k % 2, i, c])

    def out_copy(k):
        return pltpu.make_async_copy(c0.at[k], C0.at[k], osem.at[k])

    put_turned(th, tl, na * gi[...])
    r_hi[...], r_lo[...] = split(dy1)
    for k in range(N_COLS + 1):
        if k < N_COLS:
            if k >= 2:
                for i in range(2):
                    column(k - 2).core(i).wait_send()

            def put(i, v, k=k):
                cols_t[k % 2, i] = v.reshape(2, 4, 2, PIECE, D)

            product(th, tl, r_hi, r_lo, put)
            for i in range(2):
                column(k).core(i).start()
            if k == 0:
                put_turned(th, tl, ny * gf[...])
            if k + 1 < N_COLS:
                r_hi[...], r_lo[...] = split(E[:, D * k : D * k + D])
        if k > 0:
            for i in range(2):
                column(k - 1).own_core(i)
            out_copy(k - 1).start()

    def c1_copy(k):
        b1, out = (c1a, C1a) if k % 2 == 0 else (c1b, C1b)
        i = (k - N_COLS) // 2
        return pltpu.make_async_copy(b1.at[i], out.at[i], osem.at[k])

    for k in range(N_COLS, N_FF):
        chunk(k).arrived()
        c1_copy(k).start()
    travel.finish()
    for k in range(N_COLS - 2, N_COLS):
        for i in range(2):
            column(k).core(i).wait_send()
    for j in range(2, 4):

        @pl.when(place.core != j % 2)
        def _(j=j):
            for q in range(4):
                down(j, q).core(j // 2).wait_send()

    for k in range(N_COLS):
        out_copy(k).wait()
    for k in range(N_COLS, N_FF):
        chunk(k).one().wait_send()
        c1_copy(k).wait()


def feed_forward(rec, x, g, wo, wu, wd, gi, gf, gh, sums):
    act = jax.ShapeDtypeStruct((ROWS, D), F32)
    wide = pltpu.VMEM((ROWS, FF), F32)
    thin = pltpu.VMEM((ROWS, D), F32)
    return pl.pallas_call(
        ff_kernel,
        out_shape=[
            jax.ShapeDtypeStruct((ROWS, 1, D), F32),
            jax.ShapeDtypeStruct((HOMES, HALF, 128), F32),
            act,
            jax.ShapeDtypeStruct((8, D), F32),
            jax.ShapeDtypeStruct((N_COLS, 2, 4, 2, PIECE, D), F32),
            jax.ShapeDtypeStruct((2, 4, 2, PIECE, D), F32),
            jax.ShapeDtypeStruct((2, 2, 4, PIECE, D), F32),
        ],
        in_specs=[VM] * 10,
        out_specs=[VM, ANY, VM, VM, ANY, ANY, ANY],
        scratch_shapes=[
            pltpu.VMEM((HEADS, HALF, 128), F32),
            pltpu.VMEM((2 * ROWS, D), BF16),
            pltpu.VMEM((2 * ROWS, FT), BF16),
            pltpu.VMEM((1, D), F32),
            pltpu.VMEM((1, D), F32),
            pltpu.VMEM((1, FF), F32),
            pltpu.VMEM((1, FF), F32),
            thin,
            thin,
            thin,
            thin,
            wide,
            wide,
            wide,
            thin,
        ]
        + [
            pltpu.VMEM((D, ROWS), BF16),
            pltpu.VMEM((D, ROWS), BF16),
            pltpu.VMEM((ROWS, D), BF16),
            pltpu.VMEM((ROWS, D), BF16),
            pltpu.VMEM((2, 2, 2, 4, 2, PIECE, D), F32),
            pltpu.VMEM((2, 4, 2, 4, PIECE, D), F32),
            pltpu.VMEM((N_FF, 2, 4, 2, PIECE, D), F32),
            pltpu.VMEM((2, 4, 2, PIECE, D), F32),
            pltpu.VMEM((2, 2, 4, PIECE, D), F32),
            pltpu.SemaphoreType.DMA((N_FF,)),
            pltpu.SemaphoreType.DMA((HEADS,)),
            pltpu.SemaphoreType.DMA((HOMES,)),
        ]
        + Sems.scratch(N_FF),
        compiler_params=params(collective_id=4, has_side_effects=True),
    )(rec, x, g, wo, wu, wd, gi, gf, gh, sums)


def back_all_kernel(offs, drec, own, sib, ap, lse, C0, C1a, C1b, grec, wo_g, up_g, down_g, qst, kc, vc, kt, qc, dc, lt, k4, v4, kt4, q4, d4, lt4, k5, v5, kt5, q5, d5, lt5, dk, dv, dq, dk4, dv4, dk5, dv5, dq4, dq5, b1, b2, b3, b4, ds_out, came, lsem, send, recv, qsend, qrecv, fsend, frecv, c0, c1a, c1b, c2, zl, zr, csem, *rsems):
    place = Place()
    p, s, x, core, active, head = place_facts()
    b = core
    o2, o3, o4, o5 = offs[1], offs[2], offs[3], offs[4]
    kvf, qf, X, df = dk, dv.at[0:2], dv.at[2:4], dq
    dqp = qst

    barrier = pltpu.get_barrier_semaphore()
    expected = place.greet(barrier)

    def greet_heads(h, carry):
        q, t = head_device(h, x)

        @pl.when(jnp.logical_not(same(p, s, q, t)))
        def _():
            pl.semaphore_signal(barrier, inc=1, device_id=to(q, t), device_id_type=MESH)

        return carry

    lax.fori_loop(0, HEADS, greet_heads, 0)
    from_homes = HOMES - (core == x).astype(jnp.int32)
    pl.semaphore_wait(barrier, expected + active.astype(jnp.int32) * from_homes)

    def put(k, v):
        @pl.when(k == 0)
        def _():
            wo_g[...] = v

        @pl.when(jnp.logical_and(k > 0, k < 5))
        def _():
            up_g[:, pl.ds(pl.multiple_of((k - 1) * D, D), D)] = v

        @pl.when(k >= 5)
        def _():
            down_g[pl.ds(pl.multiple_of((k - 5) * PIECE, PIECE), PIECE), :] = v

    sems = Sems(rsems)

    def chunk(k):
        x_first = k % 2 == 0
        b0 = c0.at[k] if k < N_COLS else None
        b1 = (c1a if x_first else c1b).at[k // 2]
        return Chunk(
            place, k, x_first, sems, b0, b1, c2.at[k], zl.at[k], zr.at[k], put=lambda v: put(jnp.int32(k), v)
        )

    def load(k):
        if k < N_COLS:
            return pltpu.make_async_copy(C0.at[k], c0.at[k], csem.at[k])
        src, dst = (C1a, c1a) if k % 2 == 0 else (C1b, c1b)
        return pltpu.make_async_copy(src.at[(k - N_COLS) // 2], dst.at[k // 2], csem.at[k])

    PAIRS = ((5, 6), (7, 8), (0, 1), (2, 3), (4,))

    def reduction(*todo):
        for stage, pair in todo:
            for k in PAIRS[pair]:
                if stage == 1:
                    load(k).wait()
                    chunk(k).one().start()
                elif stage == 2 and k >= N_COLS:
                    load(k).wait()
                    chunk(k).two().start()
                else:
                    getattr(chunk(k), f"stage{stage}")()


    def local_copies(m):
        t = pl.multiple_of((m // 2) * ROWS, 64)
        c, d = 2 * b + lax.rem(m, 2), 2 * (1 - b) + lax.rem(m, 2)
        return [
            pltpu.make_async_copy(own.at[m, pl.ds(0, ROWS), :], kvf.at[c, pl.ds(t, ROWS), :], lsem.at[m, 0]),
            pltpu.make_async_copy(sib.at[m], kvf.at[d, pl.ds(t, ROWS), :], lsem.at[m, 1]),
            pltpu.make_async_copy(own.at[m, pl.ds(ROWS, HALF), :], qst.at[m], lsem.at[m, 2]),
        ]

    lse_copy = pltpu.make_async_copy(lse, X, lsem.at[HOMES, 0])

    @pl.when(active)
    def _():
        lse_copy.start()

        def start(m, carry):
            for c in local_copies(m):
                c.start()
            return carry

        lax.fori_loop(0, HOMES, start, 0)

    for pair in PAIRS:
        for k in pair:
            load(k).start()
    reduction((2, 0), (1, 2), (2, 1))

    @pl.when(active)
    def _():
        b1[...] = key_bias((2, 128), (4, 128), 4, 1, 2 * b, True)
        b2[...] = key_bias((1, 256), (2, 256), 4, 2, 2 * b, True)
        b3[...] = key_bias((1, 256), (1, 256), 1, 1, 0, True)
        e4 = class_facts4(o4, b)[1]
        b4[...] = key_bias((1, 256), (2, 256), 12, 6, 6 * e4, True)

        def wait(m, carry):
            for c in local_copies(m):
                c.wait()
            return carry

        lax.fori_loop(0, HOMES, wait, 0)
        lse_copy.wait()
        unpack_pairs(qst, 0, qf, 1.0 / math.sqrt(HD))

        def prepare(i, carry):
            c, t = i // 12, pl.multiple_of(lax.rem(i, 12) * 128, 128)
            k2, v2 = keys_and_values(kvf[c, pl.ds(t, 128), :])
            kc[c, pl.ds(t, 128), :] = k2.astype(BF16)
            vc[c, pl.ds(t, 128), :] = v2.astype(BF16)
            kt[c, :, pl.ds(t, 128)] = k2.T.astype(BF16)
            return carry

        lax.fori_loop(0, 48, prepare, 0)

        def prepare_q(i, carry):
            c, t = i // 12, pl.multiple_of(lax.rem(i, 12) * 128, 128)
            qc[c, pl.ds(t, 128), :] = query_quads(qf[c, pl.ds(t, 128), :])
            return carry

        lax.fori_loop(0, 24, prepare_q, 0)

    keys4, e4, (qc4, qv4) = class_facts4(o4, b)
    kc5, kv5 = lax.rem(o5, 4), o5 // 4
    qi4, qi5 = qc4 - 2 * b, lax.rem(kc5, 2)

    @pl.when(active)
    def _():
        for blk in range(4):
            r = slice(128 * blk, 128 * blk + 128)
            for e in range(2):
                c, v = keys4[e]
                k2, v2 = keys_and_values(kvf[c, pl.ds(v + 384 * blk, 128, stride=3), :])
                k4[e, r, :] = k2.astype(BF16)
                v4[e, r, :] = v2.astype(BF16)
                kt4[e, :, r] = k2.T.astype(BF16)
            q4[r, :] = query_quads(qf[qi4, pl.ds(qv4 + 384 * blk, 128, stride=3), :])
            rows = pl.ds(kv5 + 384 * blk, 128, stride=3)
            k2, v2 = keys_and_values(kvf[kc5, rows, :])
            k5[r, :] = k2.astype(BF16)
            v5[r, :] = v2.astype(BF16)
            kt5[:, r] = k2.T.astype(BF16)
            q5[r, :] = query_quads(qf[qi5, rows, :])
        dk[...] = jnp.zeros_like(dk)

    reduction((1, 3))

    @pl.when(active)
    def _():
        unpack_pairs(drec, 0, df, 1.0)

        def facts(m, carry):
            ci = lax.rem(m, 2)
            t = pl.multiple_of((m // 2) * ROWS, 32)
            prod = drec[m] * ap[m]
            low = lower_lanes(prod)
            d0 = jnp.sum(jnp.where(low, prod, 0.0), -1, keepdims=True)
            d1 = jnp.sum(jnp.where(low, 0.0, prod), -1, keepdims=True)
            for part, d in ((0, d0), (1, d1)):
                rows = pl.ds(t + HALF * part, HALF)
                l = X[ci, rows, :]
                X[ci, rows, :] = jnp.where(low, l, jnp.broadcast_to(d, l.shape))
            return carry

        lax.fori_loop(0, HOMES, facts, 0)

        def turned(v):
            w = v.T
            return jnp.concatenate([w[0:1, :], w[HD : HD + 1, :]], 0)

        def prepare_d(i, carry):
            c, t = i // 12, pl.multiple_of(lax.rem(i, 12) * 128, 128)
            rows = pl.ds(t, 128)
            dc[c, rows, :] = query_quads(df[c, rows, :])
            lt[i] = turned(X[c, rows, :])
            return carry

        lax.fori_loop(0, 24, prepare_d, 0)
        for blk in range(4):
            r = slice(128 * blk, 128 * blk + 128)
            rows = pl.ds(qv4 + 384 * blk, 128, stride=3)
            d4[r, :] = query_quads(df[qi4, rows, :])
            lt4[blk] = turned(X[qi4, rows, :])
            rows = pl.ds(kv5 + 384 * blk, 128, stride=3)
            d5[r, :] = query_quads(df[qi5, rows, :])
            lt5[blk] = turned(X[qi5, rows, :])
        dv[...] = jnp.zeros_like(dv)
        dq[...] = jnp.zeros_like(dq)

    def tile(k, v, kT, q, d, facts_pair, bias, classes):
        n = k.shape[0]
        each = n // classes
        edge = bias.shape[0] // classes
        s_ = dot_nt(doubled(k), q).reshape(classes, each, 256)
        last = s_[:, each - edge :] + bias[...].reshape(classes, edge, 256)
        s_ = last if each == edge else jnp.concatenate([s_[:, : each - edge], last], 1)
        s_ = s_.reshape(n, 256)
        l0, l1 = facts_pair
        row = jnp.concatenate([l0[0:1, :], l1[0:1, :]], 1)
        delta = jnp.concatenate([l0[1:2, :], l1[1:2, :]], 1)
        pr = jnp.exp(s_ - row)
        ds = pr * (dot_nt(doubled(v), d) - delta)
        hi, lo = split(pr)
        d2, q2_ = d[:, :128], q[:, :128]
        dv_new = dot_nn(jnp.concatenate([hi, lo], 1), jnp.concatenate([d2, d2], 0))
        hi, lo = split(ds)
        dk_new = dot_nn(jnp.concatenate([hi, lo], 1), jnp.concatenate([q2_, q2_], 0))
        dq_new = dot_nn(kT, hi) + dot_nn(kT, lo)
        return dk_new, dv_new, dq_new.T

    def kept(flag, v):
        return jnp.where(flag, v, 0.0)

    def tile2(base, qb):
        keys = 256 * (qb + 1)
        ks, qs = pl.ds(base, keys), pl.ds(base + 256 * qb, 256)
        blk = (base + 256 * qb) // 128
        a, c, e = tile(
            jnp.concatenate([kc[o2, ks, :], kc[o2 + 2, ks, :]], 0),
            jnp.concatenate([vc[o2, ks, :], vc[o2 + 2, ks, :]], 0),
            jnp.concatenate([kt[o2, :, ks], kt[o2 + 2, :, ks]], 1),
            qc[o2, qs, :],
            dc[o2, qs, :],
            (lt.at[12 * o2 + blk], lt.at[12 * o2 + blk + 1]),
            b2,
            2,
        )
        for par in range(2):
            f = o2 == par
            dk[par, ks, :] += kept(f, a[:keys])
            dk[par + 2, ks, :] += kept(f, a[keys:])
            dv[par, ks, :] += kept(f, c[:keys])
            dv[par + 2, ks, :] += kept(f, c[keys:])
            dq[par, qs, :] += kept(f, e)

    @pl.when(active)
    def _():
        for base, count in ((0, 4), (1024, 2)):
            for qb in range(count):
                tile2(base, qb)

    reduction((3, 0), (2, 2), (3, 1), (1, 4))

    def tile3(qb):
        ci = lax.rem(o3, 2)
        keys = 256 * (qb + 1)
        ks, qs = pl.ds(0, keys), pl.ds(256 * qb, 256)
        a, c, e = tile(
            kc[o3, ks, :],
            vc[o3, ks, :],
            kt[o3, :, ks],
            qc[ci, qs, :],
            dc[ci, qs, :],
            (lt.at[12 * ci + 2 * qb], lt.at[12 * ci + 2 * qb + 1]),
            b3,
            1,
        )
        for i in range(2):
            f = o3 == 2 * b + i
            dk[2 * b + i, ks, :] += kept(f, a)
            dv[2 * b + i, ks, :] += kept(f, c)
            dq[i, qs, :] += kept(f, e)

    def tiles45(qb):
        keys = 256 * (qb + 1)
        qs, ks = slice(256 * qb, 256 * qb + 256), slice(0, keys)
        a, c, e = tile(
            k4[:, ks, :].reshape(2 * keys, 128),
            v4[:, ks, :].reshape(2 * keys, 128),
            jnp.concatenate([kt4[0, :, ks], kt4[1, :, ks]], 1),
            q4[qs, :],
            d4[qs, :],
            (lt4.at[2 * qb], lt4.at[2 * qb + 1]),
            b4,
            2,
        )
        dk4[:, ks, :] += a.reshape(2, keys, 128)
        dv4[:, ks, :] += c.reshape(2, keys, 128)
        dq4[qs, :] = e
        a, c, e = tile(
            k5[ks, :], v5[ks, :], kt5[:, ks], q5[qs, :], d5[qs, :], (lt5.at[2 * qb], lt5.at[2 * qb + 1]), b3, 1
        )
        dk5[ks, :] += a
        dv5[ks, :] += c
        dq5[qs, :] = e

    @pl.when(active)
    def _():
        for qb in range(TOTAL // 256):
            tile3(qb)
        for ref in (dk4, dv4, dk5, dv5):
            ref[...] = jnp.zeros_like(ref)
        for qb in range(2):
            tiles45(qb)
        mine5 = kc5 // 2 == b
        for kind in range(12):
            c, rows = kind % 4, pl.ds(kind // 4, THIRD, stride=3)
            f0, f1, f5 = o4 == kind, o4 + 6 == kind, jnp.logical_and(o5 == kind, mine5)
            dk[c, rows, :] += kept(f0, dk4[0]) + kept(f1, dk4[1]) + kept(f5, dk5[...])
            dv[c, rows, :] += kept(f0, dv4[0]) + kept(f1, dv4[1]) + kept(f5, dv5[...])
        for ci in range(2):
            for v in range(3):
                rows = pl.ds(v, THIRD, stride=3)
                f4 = jnp.logical_and(qi4 == ci, qv4 == v)
                f5 = jnp.logical_and(jnp.logical_and(qi5 == ci, kv5 == v), mine5)
                dq[ci, rows, :] += kept(f4, dq4[...]) + kept(f5, dq5[...])

    reduction((4, 0), (4, 1), (2, 3), (3, 2))

    def segment(g):
        def at(t, n):
            return pl.ds(pl.multiple_of(512 * g + t, 128), n)

        for qb in range(4):
            keys = 128 * (qb + 1)
            ks, qs = at(0, keys), at(128 * qb, 128)
            a, c, e = tile(
                kc[:, ks, :].reshape(4 * keys, 128),
                vc[:, ks, :].reshape(4 * keys, 128),
                jnp.concatenate([kt[i, :, ks] for i in range(4)], 1),
                qc[:, qs, :].reshape(256, 256),
                dc[:, qs, :].reshape(256, 256),
                (lt.at[4 * g + qb], lt.at[12 + 4 * g + qb]),
                b1,
                4,
            )
            dk[:, ks, :] += a.reshape(4, keys, 128)
            dv[:, ks, :] += c.reshape(4, keys, 128)
            dq[:, qs, :] += e.reshape(2, 128, 128)

    def passed(m):
        return remote(ds_out.at[m], came.at[m], fsend.at[m], frecv.at[m], place.peer)

    def home_copies(m):
        q, t = home_device(core, m)
        kv = remote(came.at[m], grec.at[head, pl.ds(0, ROWS), :], send.at[m], recv.at[head], to(q, t))
        dq_ = remote(dqp.at[m], grec.at[head, pl.ds(ROWS, HALF), :], qsend.at[m], qrecv.at[head], to(q, t))
        return q, t, kv, dq_

    def rows_of(m):
        return pl.ds(pl.multiple_of((m // 2) * ROWS, 64), ROWS)

    def kv(c, m):
        k, v = dk[c, rows_of(m), :], dv[c, rows_of(m), :]
        return pick(k + swap(k), v + swap(v))

    def share(m, carry):
        ds_out[m] = kv(2 * (1 - b) + lax.rem(m, 2), m)
        passed(m).start()
        return carry

    def add(m, carry):
        q, t, far_kv, far_q = home_copies(m)
        ci = lax.rem(m, 2)
        v = dq[ci, rows_of(m), :]
        v = (v + swap(v)) * (1.0 / math.sqrt(HD))
        dqp[m] = pick(v[:HALF], v[HALF:])
        passed(m).wait_recv()
        came[m] += kv(2 * b + ci, m)

        @pl.when(same(p, s, q, t))
        def _():
            pltpu.make_async_copy(came.at[m], grec.at[head, pl.ds(0, ROWS), :], recv.at[head]).start()
            pltpu.make_async_copy(dqp.at[m], grec.at[head, pl.ds(ROWS, HALF), :], qrecv.at[head]).start()

        @pl.when(jnp.logical_not(same(p, s, q, t)))
        def _():
            far_kv.start()
            far_q.start()

        return carry

    def round_of(i, carry):
        g = jnp.where(i == 0, 0, 3 - i)

        @pl.when(active)
        def _():
            segment(g)
            lax.fori_loop(jnp.where(i == 0, 0, jnp.where(i == 1, 12, 4)), jnp.where(i == 0, 4, jnp.where(i == 1, 16, 12)), share, 0)

            @pl.when(i > 0)
            def _():
                lax.fori_loop(jnp.where(i == 1, 0, 12), jnp.where(i == 1, 4, 16), add, 0)

        @pl.when(i == 1)
        def _():
            reduction((5, 0), (5, 1), (2, 4), (3, 3), (4, 2))

        return carry

    lax.fori_loop(0, 3, round_of, 0)

    @pl.when(active)
    def _():
        lax.fori_loop(4, 12, add, 0)

    reduction((6, 0), (6, 1), (3, 4), (4, 3), (5, 2))
    reduction((4, 4), (5, 3), (6, 2))
    reduction((5, 4), (6, 3))
    reduction((6, 4))

    def from_head(h, carry):
        a = grec.at[h, pl.ds(0, ROWS), :]
        c = grec.at[h, pl.ds(ROWS, HALF), :]
        pltpu.make_async_copy(a, a, recv.at[h]).wait()
        pltpu.make_async_copy(c, c, qrecv.at[h]).wait()
        return carry

    lax.fori_loop(0, HEADS, from_head, 0)
    for k in range(N_FF):
        if k < N_COLS:
            chunk(k).one().wait_send()
        chunk(k).two().wait_send()
        chunk(k).line_sent()

    @pl.when(active)
    def _():
        def sent(m, carry):
            q, t, far_kv, far_q = home_copies(m)
            passed(m).wait_send()

            @pl.when(jnp.logical_not(same(p, s, q, t)))
            def _():
                far_kv.wait_send()
                far_q.wait_send()

            return carry

        lax.fori_loop(0, HOMES, sent, 0)


def backward_all(offs, drec, own, sib, ap, lse, C0, C1a, C1b, cid):
    dma = pltpu.SemaphoreType.DMA
    keys = pltpu.VMEM((4, TOTAL, 128), BF16)
    full = pltpu.VMEM((4, TOTAL, 128), F32)
    quad = pltpu.VMEM((2, TOTAL, 256), BF16)
    quad3 = pltpu.VMEM((THIRD, 256), BF16)
    pair3 = pltpu.VMEM((THIRD, 128), BF16)
    turned = pltpu.VMEM((128, THIRD), BF16)
    facts3 = pltpu.VMEM((4, 2, 128), F32)
    out3 = pltpu.VMEM((THIRD, 128), F32)
    packs = pltpu.VMEM((HOMES, ROWS, 128), F32)
    halves = pltpu.VMEM((HOMES, HALF, 128), F32)
    return pl.pallas_call(
        back_all_kernel,
        out_shape=[
            jax.ShapeDtypeStruct((HEADS, PACK, 128), F32),
            jax.ShapeDtypeStruct((PIECE, D), F32),
            jax.ShapeDtypeStruct((PIECE, FF), F32),
            jax.ShapeDtypeStruct((4 * PIECE, D), F32),
        ],
        in_specs=[SM, VM, ANY, ANY, VM, ANY, ANY, ANY, ANY],
        out_specs=[ANY, VM, VM, VM],
        scratch_shapes=[
            halves,
            keys,
            keys,
            pltpu.VMEM((4, 128, TOTAL), BF16),
            quad,
            quad,
            pltpu.VMEM((24, 2, 128), F32),
            pltpu.VMEM((2, THIRD, 128), BF16),
            pltpu.VMEM((2, THIRD, 128), BF16),
            pltpu.VMEM((2, 128, THIRD), BF16),
            quad3,
            quad3,
            facts3,
            pair3,
            pair3,
            turned,
            quad3,
            quad3,
            facts3,
            full,
            full,
            pltpu.VMEM((2, TOTAL, 128), F32),
            pltpu.VMEM((2, THIRD, 128), F32),
            pltpu.VMEM((2, THIRD, 128), F32),
            out3,
            out3,
            out3,
            out3,
            pltpu.VMEM((512, 256), F32),
            pltpu.VMEM((512, 256), F32),
            pltpu.VMEM((256, 256), F32),
            pltpu.VMEM((512, 256), F32),
            packs,
            packs,
            dma((HOMES + 1, 3)),
            dma((HOMES,)),
            dma((HEADS,)),
            dma((HOMES,)),
            dma((HEADS,)),
            dma((HOMES,)),
            dma((HOMES,)),
            pltpu.VMEM((N_COLS, 2, 4, 2, PIECE, D), F32),
            pltpu.VMEM((5, 4, 2, PIECE, D), F32),
            pltpu.VMEM((4, 2, 4, PIECE, D), F32),
            pltpu.VMEM((N_FF, 4, PIECE, D), F32),
            pltpu.VMEM((N_FF, 4, PIECE, D), F32),
            pltpu.VMEM((N_FF, 4, PIECE, D), F32),
            dma((N_FF,)),
        ]
        + Sems.scratch(N_FF),
        compiler_params=params(collective_id=cid, has_side_effects=True),
    )(offs, drec, own, sib, ap, lse, C0, C1a, C1b)


SEG1, SEG2, SEG3, SEG4, SEG5 = SEGMENTS
DILATION_ONE, DILATION_TWO, DILATION_THREE, DILATION_FOUR, DILATION_FIVE = DILATIONS
MASK_VALUE = -1e30
MATMUL_ACCURACY = lax.Precision.HIGHEST


def passed_along(value, axis, by):
    length = lax.axis_size(axis)
    return lax.ppermute(value, axis, [(i, (i + by) % length) for i in range(length)])


def run_is_live(distance, anchor_point, sequence_width, segment_length):
    return (anchor_point - (distance - 1) * sequence_width - 1) // segment_length == anchor_point // segment_length


def layer_norm(x, gain_vec):
    average = jnp.mean(x, -1, keepdims=True)
    centred = x - average
    variance = jnp.mean(centred * centred, -1, keepdims=True)
    return centred * lax.rsqrt(variance + LN_EPSILON) * gain_vec


def select_table(offsets_row, dilation_rate):
    return (jnp.arange(dilation_rate, dtype=jnp.int32)[:, None] == offsets_row[None, :]).astype(
        jnp.float32
    )


def spread_apart(x, select_option, dilation_rate):
    shaped = x.reshape(x.shape[0] // dilation_rate, dilation_rate, x.shape[1], x.shape[2])
    return jnp.einsum("trhd,rh->thd", shaped, select_option, precision=MATMUL_ACCURACY)


def spread_scalar_rows(x, select_option, dilation_rate):
    shaped = x.reshape(x.shape[0] // dilation_rate, dilation_rate, x.shape[1])
    return jnp.einsum("trh,rh->th", shaped, select_option, precision=MATMUL_ACCURACY)


def spread_rows(x, select_option):
    return jnp.einsum("thd,rh->trhd", x, select_option, precision=MATMUL_ACCURACY).reshape(
        -1, x.shape[1], x.shape[2]
    )


def spread_scalars(x, select_option):
    return jnp.einsum("th,rh->trh", x, select_option, precision=MATMUL_ACCURACY).reshape(
        -1, x.shape[1]
    )


def masked_score_matrix(sparse_queries, key_portion, query_position, key_position, segment_length):
    score_matrix = jnp.einsum(
        "ozt,bzt->zob", sparse_queries, key_portion, precision=MATMUL_ACCURACY
    ) * (1.0 / math.sqrt(key_portion.shape[-1]))
    q_cols = query_position.T[:, :, None]
    k_cols = key_position.T[:, None, :]
    permitted_mask = (k_cols <= q_cols) & (k_cols // segment_length == q_cols // segment_length)
    return (jnp.where(permitted_mask, score_matrix, MASK_VALUE), permitted_mask)


def prepare_pattern(
    query_sequence, key_sequence, value_sequence, offsets_row, dilation_rate, anchor_point
):
    select_option = select_table(offsets_row, dilation_rate)
    sparse_queries = spread_apart(query_sequence, select_option, dilation_rate)
    sparse_key_value = jnp.stack(
        (
            spread_apart(key_sequence, select_option, dilation_rate),
            spread_apart(value_sequence, select_option, dilation_rate),
        )
    )
    query_position = (
        anchor_point
        + jnp.arange(sparse_queries.shape[0], dtype=jnp.int32)[:, None] * dilation_rate
        + offsets_row[None, :]
    )
    return (select_option, sparse_queries, sparse_key_value, query_position)


def pattern_forward_pass(
    sparse_queries,
    sparse_key_value,
    query_position,
    reach,
    segment_length,
    anchor_point,
    sequence_width,
):
    masked_logits, permitted_mask = masked_score_matrix(
        sparse_queries, sparse_key_value[0], query_position, query_position, segment_length
    )
    row_max = jnp.max(masked_logits, -1)
    softmax_weights = jnp.where(permitted_mask, jnp.exp(masked_logits - row_max[..., None]), 0.0)
    state = (
        row_max,
        jnp.sum(softmax_weights, -1),
        jnp.einsum("tlj,jtb->tlb", softmax_weights, sparse_key_value[1], precision=MATMUL_ACCURACY),
    )

    def one_run(distance, carry):
        remote_key_value, state = carry
        remote_key_value = passed_along(remote_key_value, "seq", 1)
        key_position = query_position - distance * sequence_width

        def update(state_in):
            old_max, old_sum, old_acc = state_in
            masked_remote, permitted_remote = masked_score_matrix(
                sparse_queries, remote_key_value[0], query_position, key_position, segment_length
            )
            new_max = jnp.maximum(old_max, jnp.max(masked_remote, -1))
            weights_far = jnp.where(
                permitted_remote, jnp.exp(masked_remote - new_max[..., None]), 0.0
            )
            factor = jnp.exp(old_max - new_max)
            added = jnp.einsum(
                "tlj,jtb->tlb", weights_far, remote_key_value[1], precision=MATMUL_ACCURACY
            )
            return (
                new_max,
                old_sum * factor + jnp.sum(weights_far, -1),
                old_acc * factor[..., None] + added,
            )

        def unchanged(state_in):
            return state_in

        is_live = run_is_live(distance, anchor_point, sequence_width, segment_length)
        return remote_key_value, lax.cond(is_live, update, unchanged, state)

    state = lax.fori_loop(1, reach + 1, one_run, (sparse_key_value, state))[1]
    row_max, row_sum, accumulated = state
    mixture = jnp.transpose(accumulated / row_sum[..., None], (1, 0, 2))
    log_sum = (row_max + jnp.log(row_sum)).T
    return (mixture, log_sum)


def merge_patterns(forwards, prepared_inputs):
    full_lse = []
    full_mix = []
    for pattern_spec in range(len(forwards)):
        mixture, log_sum = forwards[pattern_spec]
        select_option = prepared_inputs[pattern_spec][0]
        covered = spread_scalars(jnp.ones_like(log_sum), select_option)
        full_lse.append(spread_scalars(log_sum, select_option) + (covered - 1.0) * 1e30)
        full_mix.append(spread_rows(mixture, select_option))
    stacked = jnp.stack(full_lse)
    row_max = jnp.max(stacked, 0)
    softmax_weights = jnp.exp(stacked - row_max)
    row_sum = jnp.sum(softmax_weights, 0)
    attended = full_mix[0] * softmax_weights[0][..., None]
    for pattern_spec in range(1, len(full_mix)):
        attended = attended + full_mix[pattern_spec] * softmax_weights[pattern_spec][..., None]
    return (attended / row_sum[..., None], row_max + jnp.log(row_sum))


def pattern_backward(
    select_option,
    dilation_rate,
    segment_length,
    anchor_point,
    sparse_queries,
    sparse_key_value,
    query_position,
    reach,
    sequence_gradient,
    row_difference,
    combined_logsumexp,
):
    sequence_width = sequence_gradient.shape[0]
    sparse_gradient = spread_apart(sequence_gradient, select_option, dilation_rate)
    sparse_output_grad = spread_scalar_rows(row_difference, select_option, dilation_rate).T
    sparse_logsumexp = spread_scalar_rows(combined_logsumexp, select_option, dilation_rate).T
    inverse_square_root = 1.0 / math.sqrt(sparse_queries.shape[-1])

    def portion_gradients(key_portion, value_portion, key_position):
        masked_logits, permitted_mask = masked_score_matrix(
            sparse_queries, key_portion, query_position, key_position, segment_length
        )
        softmax_weights = jnp.where(
            permitted_mask, jnp.exp(masked_logits - sparse_logsumexp[..., None]), 0.0
        )
        value_gradient = jnp.einsum(
            "tui,utx->itx", softmax_weights, sparse_gradient, precision=MATMUL_ACCURACY
        )
        pattern_gradient = jnp.einsum(
            "ozt,bzt->zob", sparse_gradient, value_portion, precision=MATMUL_ACCURACY
        )
        score_gradient = (
            softmax_weights
            * (pattern_gradient - sparse_output_grad[..., None])
            * inverse_square_root
        )
        query_gradient = jnp.einsum(
            "hqk,khd->qhd", score_gradient, key_portion, precision=MATMUL_ACCURACY
        )
        key_gradient = jnp.einsum(
            "tui,utx->itx", score_gradient, sparse_queries, precision=MATMUL_ACCURACY
        )
        return (query_gradient, jnp.stack((key_gradient, value_gradient)))

    query_gradient, key_value_gradient = portion_gradients(
        sparse_key_value[0], sparse_key_value[1], query_position
    )

    def one_run(distance, carry):
        remote_key_value, remote_gradient, query_sum = carry
        remote_key_value = passed_along(remote_key_value, "seq", 1)
        remote_gradient = passed_along(remote_gradient, "seq", 1)
        key_position = query_position - distance * sequence_width

        def far_grads():
            part_q, part_kv = portion_gradients(remote_key_value[0], remote_key_value[1], key_position)
            return query_sum + part_q, remote_gradient + part_kv

        def no_grads():
            return query_sum, remote_gradient

        is_live = run_is_live(distance, anchor_point, sequence_width, segment_length)
        query_sum, remote_gradient = lax.cond(is_live, far_grads, no_grads)
        return remote_key_value, remote_gradient, query_sum

    _, travelled, query_gradient = lax.fori_loop(
        1, reach + 1, one_run, (sparse_key_value, key_value_gradient, query_gradient)
    )
    return (query_gradient, passed_along(travelled, "seq", -reach))


def front_part(own_rows, w_qkv, gain_attn):
    return jnp.dot(layer_norm(own_rows, gain_attn), w_qkv, precision=MATMUL_ACCURACY)


def after_part(attn_rows, own_rows, w_out, w_up, w_down, gain_inner, gain_ffn, gain_hidden):
    residual = own_rows + jnp.dot(
        layer_norm(attn_rows, gain_inner), w_out, precision=MATMUL_ACCURACY
    )
    hidden = jax.nn.gelu(
        jnp.dot(layer_norm(residual, gain_ffn), w_up, precision=MATMUL_ACCURACY), approximate=False
    )
    return residual + jnp.dot(layer_norm(hidden, gain_hidden), w_down, precision=MATMUL_ACCURACY)


def shards(
    tokens,
    w_qkv,
    w_out,
    w_up,
    w_down,
    gain_attn,
    gain_inner,
    gain_ffn,
    gain_hidden,
    offsets,
    grad_out,
):
    w_qkv = w_qkv.astype(jnp.float32)
    w_out = w_out.astype(jnp.float32)
    w_up = w_up.astype(jnp.float32)
    w_down = w_down.astype(jnp.float32)
    groups = lax.axis_size("pat")
    local_rows = tokens.shape[0]
    sequence_width = local_rows * groups
    heads_here = HEADS // groups
    own_rows = tokens.reshape(local_rows, D)
    qkv_rows, front_back = jax.vjp(front_part, own_rows, w_qkv, gain_attn)
    gathered_qkv = lax.all_to_all(
        qkv_rows.reshape(local_rows, 1, 3, HEADS, HD),
        "pat",
        split_axis=3,
        concat_axis=1,
        tiled=True,
    )
    gathered_qkv = gathered_qkv.reshape(sequence_width, 3, heads_here, HD)
    head_offsets = lax.dynamic_slice_in_dim(
        offsets, lax.axis_index("pat") * heads_here, heads_here, 1
    )
    anchor_point = lax.axis_index("seq") * sequence_width
    dilation_rates = (DILATION_ONE, DILATION_TWO, DILATION_THREE, DILATION_FOUR, DILATION_FIVE)
    segment_lengths = (SEG1, SEG2, SEG3, SEG4, SEG5)
    reaches = [
        min((segment_lengths[pattern_spec] - 2) // sequence_width + 1, lax.axis_size("seq") - 1)
        for pattern_spec in range(PATTERNS)
    ]
    prepared_inputs = []
    for pattern_spec in range(PATTERNS):
        prepared_inputs.append(
            prepare_pattern(
                gathered_qkv[:, 0],
                gathered_qkv[:, 1],
                gathered_qkv[:, 2],
                head_offsets[pattern_spec],
                dilation_rates[pattern_spec],
                anchor_point,
            )
        )
    forwards = []
    for pattern_spec in range(PATTERNS):
        select_option, sparse_queries, sparse_key_value, query_position = prepared_inputs[
            pattern_spec
        ]
        forwards.append(
            pattern_forward_pass(
                sparse_queries,
                sparse_key_value,
                query_position,
                reaches[pattern_spec],
                segment_lengths[pattern_spec],
                anchor_point,
                sequence_width,
            )
        )
    lse_sums = jnp.stack([jnp.sum(entry[1]) for entry in forwards])
    totals = lax.psum(lse_sums, ("pat", "seq"))
    full_length = sequence_width * lax.axis_size("seq")
    counts = jnp.array(
        [
            float(full_length // dilation_rates[pattern_spec] * HEADS)
            for pattern_spec in range(PATTERNS)
        ],
        jnp.float32,
    )
    log_means = totals / counts
    attended, combined_logsumexp = merge_patterns(forwards, prepared_inputs)
    returned_rows = lax.all_to_all(
        attended.reshape(local_rows, groups, heads_here, HD),
        "pat",
        split_axis=1,
        concat_axis=2,
        tiled=True,
    )
    attn_rows = returned_rows.reshape(local_rows, D)
    result, after_back = jax.vjp(
        after_part, attn_rows, own_rows, w_out, w_up, w_down, gain_inner, gain_ffn, gain_hidden
    )
    g_attn, g_resid, g_out, g_up, g_down, g_inner, g_ffn, g_hidden = after_back(
        grad_out.reshape(local_rows, D)
    )
    sequence_gradient = lax.all_to_all(
        g_attn.reshape(local_rows, 1, HEADS, HD), "pat", split_axis=2, concat_axis=1, tiled=True
    )
    sequence_gradient = sequence_gradient.reshape(sequence_width, heads_here, HD)
    row_difference = jnp.sum(sequence_gradient * attended, -1)
    q_grads = []
    kv_grads = []
    for pattern_spec in range(PATTERNS):
        select_option, sparse_queries, sparse_key_value, query_position = prepared_inputs[
            pattern_spec
        ]
        part_q, part_kv = pattern_backward(
            select_option,
            dilation_rates[pattern_spec],
            segment_lengths[pattern_spec],
            anchor_point,
            sparse_queries,
            sparse_key_value,
            query_position,
            reaches[pattern_spec],
            sequence_gradient,
            row_difference,
            combined_logsumexp,
        )
        q_grads.append(part_q)
        kv_grads.append(part_kv)
    grad_total = jnp.zeros((sequence_width, 3, heads_here, HD), jnp.float32)
    for pattern_spec in range(PATTERNS):
        select_option = prepared_inputs[pattern_spec][0]
        grad_total = grad_total + jnp.stack(
            (
                spread_rows(q_grads[pattern_spec], select_option),
                spread_rows(kv_grads[pattern_spec][0], select_option),
                spread_rows(kv_grads[pattern_spec][1], select_option),
            ),
            1,
        )
    grad_back = lax.all_to_all(
        grad_total.reshape(local_rows, groups, 3, heads_here, HD),
        "pat",
        split_axis=1,
        concat_axis=3,
        tiled=True,
    )
    g_tokens, g_qkv, g_attn_gain = front_back(grad_back.reshape(local_rows, 3 * D))
    grad_tokens = (g_resid + g_tokens).reshape(local_rows, 1, D)
    summed = (
        lax.psum_scatter(g_qkv, ("pat", "seq"), scatter_dimension=0, tiled=True),
        lax.psum_scatter(g_out, ("pat", "seq"), scatter_dimension=0, tiled=True),
        lax.psum_scatter(g_up, ("pat", "seq"), scatter_dimension=0, tiled=True),
        lax.psum_scatter(g_down, ("pat", "seq"), scatter_dimension=0, tiled=True),
        lax.psum_scatter(g_attn_gain, ("pat", "seq"), scatter_dimension=0, tiled=True),
        lax.psum_scatter(g_inner, ("pat", "seq"), scatter_dimension=0, tiled=True),
        lax.psum_scatter(g_ffn, ("pat", "seq"), scatter_dimension=0, tiled=True),
        lax.psum_scatter(g_hidden, ("pat", "seq"), scatter_dimension=0, tiled=True),
    )
    return (
        result.reshape(local_rows, 1, D),
        grad_tokens,
        summed[0],
        summed[1],
        summed[2],
        summed[3],
        summed[4],
        summed[5],
        summed[6],
        summed[7],
        log_means,
    )


def fast_shards(tokens, w_qkv, w_out, w_up, w_down, gain_attn, gain_inner, gain_ffn, gain_hidden, offsets, grad_out):
    p, s = lax.axis_index("pat"), lax.axis_index("seq")
    active, head = head_here(p, s)
    mine = lax.dynamic_slice_in_dim(offsets, head, 1, 1)[:, 0]
    info = jnp.concatenate([jnp.stack([active.astype(jnp.int32), lax.rem(p, 2).astype(jnp.int32)]), mine])

    counts = [float(TOTAL * 4 // r * HEADS) for r in DILATIONS]
    pk, x = front(tokens, w_qkv, gain_attn)
    own, sib = to_heads(pk, True, 0)
    ap, lse, sums = attention_forward(info, own, sib)
    rec = to_homes(ap, 1)
    mixed, drec, dy1, S, C0, C1a, C1b = feed_forward(
        rec, x, grad_out, w_out, w_up, w_down, gain_inner, gain_ffn, gain_hidden, sums
    )
    grec, g_out, g_up, g_down = backward_all(mine, drec, own, sib, ap, lse, C0, C1a, C1b, 2)
    gx, g_qkv, *small = finish(grec, x, dy1, w_qkv, gain_attn, S, counts, 3)
    mixed, gx, g_qkv, g_out, g_up, g_down, *small = deliver(mixed, gx, g_qkv, g_out, g_up, g_down, *small)
    return (mixed, gx, g_qkv, g_out, g_up, g_down, *(v.reshape(-1) for v in small))


def fits(mesh):
    return mesh.shape["pat"] == 4 and mesh.shape["seq"] == RUNS


def solution(mesh):
    rows = P("seq", "pat", None)
    split_rows = P(("pat", "seq"), None)
    split_one = P(("pat", "seq"))
    planned = jax.shard_map(
        fast_shards,
        mesh=mesh,
        in_specs=(rows,) + (P(),) * 9 + (rows,),
        out_specs=(rows, rows) + (split_rows,) * 4 + (split_one,) * 4 + (P(),),
        check_vma=False,
    )
    general = jax.shard_map(
        shards,
        mesh=mesh,
        in_specs=(rows,) + (P(),) * 9 + (rows,),
        out_specs=(rows, rows) + (split_rows,) * 4 + (split_one,) * 4 + (P(),),
        check_vma=False,
    )

    def layer(tokens, *rest):
        if fits(mesh) and tokens.shape[0] == TOTAL:
            return planned(tokens, *rest)
        return general(tokens, *rest)

    return layer
```

```python
import functools
import math

import jax
import jax.numpy as jnp
from jax import lax
from jax.experimental import pallas as pl
from jax.experimental.pallas import tpu as pltpu
from jax.sharding import PartitionSpec as P

D = 768
HEADS = 12
HD = 64
FF = 3072
PATTERNS = 5
SEGMENTS = (2048, 4096, 8192, 16384, 32768)
DILATIONS = (1, 2, 4, 6, 12)
LN_EPSILON = 1e-05
NEG = -1e30
F32 = jnp.float32
BF16 = jnp.bfloat16
HIGHEST = lax.Precision.HIGHEST
VMEM_LIMIT = 60 * 1024 * 1024

ROWS = 192
HALF = ROWS // 2
RUNS = 8
TOTAL = ROWS * RUNS
PACK = ROWS + HALF
HOMES = 16
THIRD = TOTAL // 3
PIECE = 24
MESH = pl.DeviceIdType.MESH


def dot_nn(a, b):
    return lax.dot_general(a, b, (((1,), (0,)), ((), ())), preferred_element_type=F32)


def dot_nt(a, b):
    return lax.dot_general(a, b, (((1,), (1,)), ((), ())), preferred_element_type=F32)


def split(v):
    hi = v.astype(BF16)
    return hi, (v - hi.astype(F32)).astype(BF16)


def split32(v):
    hi = v.astype(BF16).astype(F32)
    return hi, v - hi


def lower_lanes(v):
    return lax.broadcasted_iota(jnp.int32, v.shape, v.ndim - 1) < HD


def swap(v):
    return pltpu.roll(v, HD, v.ndim - 1)


def pick(a, b):
    return jnp.where(lower_lanes(a), a, b)


def head_place(h):
    z = h // 3
    column = lax.rem(lax.rem(h, 3) + z + 1, 4)
    return column // 2, z * 2 + lax.rem(column, 2)


def head_here(p, s):
    z = s // 2
    column = (p // 2) * 2 + lax.rem(s, 2)
    k = lax.rem(column - z + 7, 4)
    return k < 3, z * 3 + jnp.minimum(k, 2)


def whole(*_):
    return pl.BlockSpec(memory_space=pltpu.VMEM)


VM = pl.BlockSpec(memory_space=pltpu.VMEM)
ANY = pl.BlockSpec(memory_space=pl.ANY)
SM = pl.BlockSpec(memory_space=pltpu.SMEM)


def params(**kw):
    return pltpu.CompilerParams(vmem_limit_bytes=VMEM_LIMIT, **kw)


def normed(v):
    centred = v - jnp.mean(v, -1, keepdims=True)
    rs = lax.rsqrt(jnp.mean(centred * centred, -1, keepdims=True) + LN_EPSILON)
    return centred * rs, rs


def put_split(ref, v):
    hi, lo = split(v)
    n = v.shape[0]
    ref[0:n, :] = hi
    ref[n : 2 * n, :] = lo


def front_kernel(x3, w_ref, gain_ref, pk_ref, x_ref, lhs):
    x = x3[...].reshape(ROWS, D)
    x_ref[...] = x
    n, _ = normed(x)
    put_split(lhs, n * gain_ref[...][None, :])
    for jj in range(3):
        parts = []
        for kind in range(3):
            c0 = kind * D + 256 * jj
            r = dot_nn(lhs[...], w_ref[:, c0 : c0 + 256])
            parts.append(r[:ROWS] + r[ROWS:])
        for half in range(2):
            q, k, v = (a[:, 128 * half : 128 * half + 128] for a in parts)
            h = 4 * jj + 2 * half
            pk_ref[h, 0:ROWS, :] = pick(k, swap(v))
            pk_ref[h + 1, 0:ROWS, :] = pick(swap(k), v)
            top, bottom = q[:HALF], q[HALF:]
            pk_ref[h, ROWS:PACK, :] = pick(top, swap(bottom))
            pk_ref[h + 1, ROWS:PACK, :] = pick(swap(top), bottom)


def front(x, w, gain):
    return pl.pallas_call(
        front_kernel,
        out_shape=[jax.ShapeDtypeStruct((HEADS, PACK, 128), F32)] + [jax.ShapeDtypeStruct((ROWS, D), F32)],
        in_specs=[VM] * 3,
        out_specs=[VM] * 2,
        scratch_shapes=[pltpu.VMEM((2 * ROWS, D), BF16)],
        compiler_params=params(),
    )(x, w, gain)


def place_facts():
    p, s = lax.axis_index("pat"), lax.axis_index("seq")
    x, core = p // 2, lax.rem(p, 2)
    active, head = head_here(p, s)
    return p, s, x, core, active, head


def home_device(core, m):
    return core * 2 + lax.rem(m, 2), m // 2


def head_device(h, b):
    hx, hs = head_place(h)
    return hx * 2 + b, hs


def same(p, s, q, t):
    return jnp.logical_and(p == q, s == t)


def to(p, s):
    return {"pat": p, "seq": s}


def scatter_kernel(forward, pk, own, *rest):
    if forward:
        sib, send, recv, fsend, frecv = rest
    else:
        send, recv = rest
    p, s, x, core, active, head = place_facts()
    slot = s * 2 + core
    barrier = pltpu.get_barrier_semaphore()

    @pl.when(active)
    def _():
        def greet(m, carry):
            q, t = home_device(core, m)

            @pl.when(jnp.logical_not(same(p, s, q, t)))
            def _():
                pl.semaphore_signal(barrier, inc=1, device_id=to(q, t), device_id_type=MESH)

            return carry

        lax.fori_loop(0, HOMES, greet, 0)
        if forward:
            pl.semaphore_signal(barrier, inc=1, device_id=to(x * 2 + 1 - core, s), device_id_type=MESH)

    mine = jnp.logical_and(active, core == x)
    waits = HEADS - mine.astype(jnp.int32)
    if forward:
        waits = waits + active.astype(jnp.int32)
    pl.semaphore_wait(barrier, waits)

    def copy(h):
        q, t = head_device(h, x)
        return q, t, pltpu.make_async_remote_copy(
            src_ref=pk.at[h],
            dst_ref=own.at[slot],
            send_sem=send.at[h],
            recv_sem=recv.at[slot],
            device_id=to(q, t),
            device_id_type=MESH,
        )

    def start(j, carry):
        h = lax.rem(j + 3 * (s // 2) + 2 * p, HEADS)
        q, t, remote = copy(h)

        @pl.when(same(p, s, q, t))
        def _():
            pltpu.make_async_copy(pk.at[h], own.at[slot], recv.at[slot]).start()

        @pl.when(jnp.logical_not(same(p, s, q, t)))
        def _():
            remote.start()

        return carry

    lax.fori_loop(0, HEADS, start, 0)

    def passed(m):
        return pltpu.make_async_remote_copy(
            src_ref=own.at[m, pl.ds(0, ROWS), :],
            dst_ref=sib.at[m],
            send_sem=fsend.at[m],
            recv_sem=frecv.at[m],
            device_id=to(x * 2 + 1 - core, s),
            device_id_type=MESH,
        )

    @pl.when(active)
    def _():
        def arrive(m, carry):
            pltpu.make_async_copy(own.at[m], own.at[m], recv.at[m]).wait()
            if forward:
                passed(m).start()
            return carry

        lax.fori_loop(0, HOMES, arrive, 0)
        if forward:

            def finish(m, carry):
                passed(m).wait()
                return carry

            lax.fori_loop(0, HOMES, finish, 0)

    def sent(h, carry):
        q, t, remote = copy(h)

        @pl.when(jnp.logical_not(same(p, s, q, t)))
        def _():
            remote.wait_send()

        return carry

    lax.fori_loop(0, HEADS, sent, 0)


def to_heads(packets, forward, cid):
    rows = packets.shape[1]
    shapes = [jax.ShapeDtypeStruct((HOMES, rows, 128), F32)]
    sems = [pltpu.SemaphoreType.DMA((HEADS,)), pltpu.SemaphoreType.DMA((HOMES,))]
    if forward:
        shapes.append(jax.ShapeDtypeStruct((HOMES, ROWS, 128), F32))
        sems += [pltpu.SemaphoreType.DMA((HOMES,)), pltpu.SemaphoreType.DMA((HOMES,))]
    return pl.pallas_call(
        functools.partial(scatter_kernel, forward),
        out_shape=shapes,
        in_specs=[ANY],
        out_specs=[ANY] * len(shapes),
        scratch_shapes=sems,
        compiler_params=params(collective_id=cid, has_side_effects=True),
    )(packets)


def home_barrier(p, s, x, core, active, barrier, also_sibling):
    def greet(h, carry):
        q, t = head_device(h, x)

        @pl.when(jnp.logical_not(same(p, s, q, t)))
        def _():
            pl.semaphore_signal(barrier, inc=1, device_id=to(q, t), device_id_type=MESH)

        return carry

    lax.fori_loop(0, HEADS, greet, 0)

    @pl.when(active)
    def _():
        if also_sibling:
            pl.semaphore_signal(barrier, inc=1, device_id=to(x * 2 + 1 - core, s), device_id_type=MESH)
        mine = (core == x).astype(jnp.int32)
        pl.semaphore_wait(barrier, HOMES - mine + (1 if also_sibling else 0))


def gather_kernel(pk, rec, send, recv):
    p, s, x, core, active, head = place_facts()
    barrier = pltpu.get_barrier_semaphore()
    home_barrier(p, s, x, core, active, barrier, False)

    def copy(m):
        q, t = home_device(core, m)
        return q, t, pltpu.make_async_remote_copy(
            src_ref=pk.at[m],
            dst_ref=rec.at[head],
            send_sem=send.at[m],
            recv_sem=recv.at[head],
            device_id=to(q, t),
            device_id_type=MESH,
        )

    @pl.when(active)
    def _():
        def start(j, carry):
            m = lax.rem(j + 2 * s + 1, HOMES)
            q, t, remote = copy(m)

            @pl.when(same(p, s, q, t))
            def _():
                pltpu.make_async_copy(pk.at[m], rec.at[head], recv.at[head]).start()

            @pl.when(jnp.logical_not(same(p, s, q, t)))
            def _():
                remote.start()

            return carry

        lax.fori_loop(0, HOMES, start, 0)

    def arrive(h, carry):
        pltpu.make_async_copy(rec.at[h], rec.at[h], recv.at[h]).wait()
        return carry

    lax.fori_loop(0, HEADS, arrive, 0)

    @pl.when(active)
    def _():
        def sent(m, carry):
            q, t, remote = copy(m)

            @pl.when(jnp.logical_not(same(p, s, q, t)))
            def _():
                remote.wait_send()

            return carry

        lax.fori_loop(0, HOMES, sent, 0)


def to_homes(packets, cid):
    rows = packets.shape[1]
    return pl.pallas_call(
        gather_kernel,
        out_shape=jax.ShapeDtypeStruct((HEADS, rows, 128), F32),
        in_specs=[ANY],
        out_specs=ANY,
        scratch_shapes=[pltpu.SemaphoreType.DMA((HOMES,)), pltpu.SemaphoreType.DMA((HEADS,))],
        compiler_params=params(collective_id=cid, has_side_effects=True),
    )(packets)


def tile_positions(rows, columns, row_classes, column_classes, t_step, class_step):
    r = lax.broadcasted_iota(jnp.int32, (rows, columns), 0)
    q = lax.broadcasted_iota(jnp.int32, (rows, columns), 1)
    rn, qn = rows // row_classes, columns // column_classes
    return (r % rn) * t_step + (r // rn) * class_step, (q % qn) * t_step + (q // qn) * class_step


def key_bias(q_shape, k_shape, t_step, class_step, shift, keys_first):
    nq, nk = q_shape[0] * q_shape[1], k_shape[0] * k_shape[1]
    if keys_first:
        kp, qp = tile_positions(nk, nq, k_shape[0], q_shape[0], t_step, class_step)
    else:
        qp, kp = tile_positions(nq, nk, q_shape[0], k_shape[0], t_step, class_step)
    return jnp.where(kp - qp <= shift, 0.0, NEG).astype(F32)


def unpack_keys(own, sib, b, kvf):
    def one(m, carry):
        c = 2 * b + lax.rem(m, 2)
        d = 2 * (1 - b) + lax.rem(m, 2)
        t = pl.multiple_of((m // 2) * ROWS, 64)
        kvf[c, pl.ds(t, ROWS), :] = own[m, 0:ROWS, :]
        kvf[d, pl.ds(t, ROWS), :] = sib[m]
        return carry

    lax.fori_loop(0, HOMES, one, 0)


def unpack_pairs(src, first, dst, scale):
    def one(m, carry):
        t = pl.multiple_of((m // 2) * ROWS, 32)
        v = src[m, first : first + HALF, :] * scale
        w = swap(v)
        dst[lax.rem(m, 2), pl.ds(t, HALF), :] = pick(v, w)
        dst[lax.rem(m, 2), pl.ds(t + HALF, HALF), :] = pick(w, v)
        return carry

    lax.fori_loop(0, HOMES, one, 0)


def keys_and_values(kv):
    hi, lo = split32(kv)
    k2 = pick(hi, swap(lo))
    v2 = pick(swap(hi), lo)
    return k2, v2


def doubled(v):
    return jnp.concatenate([v, v], 1)


def query_quads(qq):
    hi, lo = split32(qq)
    return jnp.concatenate([pick(hi, lo).astype(BF16), pick(lo, hi).astype(BF16)], 1)


def class_facts4(o4, b):
    keys = ((lax.rem(o4, 4), o4 // 4), (lax.rem(o4 + 6, 4), (o4 + 6) // 4))
    first = (keys[0][0] // 2) == b
    query = (jnp.where(first, keys[0][0], keys[1][0]), jnp.where(first, keys[0][1], keys[1][1]))
    return keys, jnp.where(first, 0, 1), query


def forward_kernel(info, own, sib, ap, lse, sums, kvf, kc, vc, qf, qc, k4, v4, q4, k5, v5, q5, acc, mx, R, b1, b2, b3, b4):
    active = info[0] == 1
    b = info[1]
    offs = [info[2 + i] for i in range(PATTERNS)]
    sums[...] = jnp.zeros_like(sums)

    @pl.when(active)
    def _():
        ones = jnp.ones((128, 128), BF16)
        unpack_keys(own, sib, b, kvf)
        unpack_pairs(own, ROWS, qf, 1.0 / math.sqrt(HD))

        def with_ones(v2):
            return jnp.concatenate([v2.astype(BF16), ones], 1)

        def prepare(i, carry):
            c, t = i // 12, pl.multiple_of(lax.rem(i, 12) * 128, 128)
            k2, v2 = keys_and_values(kvf[c, pl.ds(t, 128), :])
            kc[c, pl.ds(t, 128), :] = k2.astype(BF16)
            vc[c, pl.ds(t, 128), :] = with_ones(v2)
            return carry

        lax.fori_loop(0, 48, prepare, 0, unroll=2)

        def prepare_q(i, carry):
            c, t = i // 12, pl.multiple_of(lax.rem(i, 12) * 128, 128)
            qc[c, pl.ds(t, 128), :] = query_quads(qf[c, pl.ds(t, 128), :])
            return carry

        lax.fori_loop(0, 24, prepare_q, 0, unroll=2)

        keys4, e4, (qc4, qv4) = class_facts4(offs[3], b)
        kc5, kv5 = lax.rem(offs[4], 4), offs[4] // 4
        for blk in range(4):
            r = slice(128 * blk, 128 * blk + 128)
            for e in range(2):
                c, v = keys4[e]
                k2, v2 = keys_and_values(kvf[c, pl.ds(v + 384 * blk, 128, stride=3), :])
                k4[e, r, :] = k2.astype(BF16)
                v4[e, r, :] = with_ones(v2)
            q4[r, :] = query_quads(qf[qc4 - 2 * b, pl.ds(qv4 + 384 * blk, 128, stride=3), :])
            k2, v2 = keys_and_values(kvf[kc5, pl.ds(kv5 + 384 * blk, 128, stride=3), :])
            k5[r, :] = k2.astype(BF16)
            v5[r, :] = with_ones(v2)
            q5[r, :] = query_quads(qf[lax.rem(kc5, 2), pl.ds(kv5 + 384 * blk, 128, stride=3), :])

        b1[...] = key_bias((2, 128), (4, 128), 4, 1, 2 * b, False)
        b2[...] = key_bias((1, 256), (2, 256), 4, 2, 2 * b, False)
        b3[...] = key_bias((1, 512), (1, 512), 1, 1, 0, False)
        b4[...] = key_bias((1, 256), (2, 256), 12, 6, 6 * e4, False)

        def tile(start, q, k, v, bias, classes, first):
            n = q.shape[0]
            each = n // classes
            per = 1536 // classes if classes == 1 else 512
            s = dot_nt(q, doubled(k))
            wide = s.shape[1]
            own_rows = bias.shape[0] // classes
            s = s.reshape(classes, each, wide)
            edge = s[:, :own_rows] + bias[...].reshape(classes, own_rows, wide)
            s = edge if each == own_rows else jnp.concatenate([edge, s[:, own_rows:]], 1)
            s = s.reshape(n, wide)
            top = jnp.max(s, -1, keepdims=True)

            def where(c):
                return pl.ds(c * per + start, each)

            def load(ref):
                return jnp.concatenate([ref[where(c), :] for c in range(classes)], 0)

            def store(ref, value):
                for c in range(classes):
                    ref[where(c), :] = value[c * each : c * each + each]

            if first:
                m = jnp.broadcast_to(top, (n, 128))
            else:
                old = load(mx)
                m = jnp.maximum(old, top)
            p = jnp.exp(s - jnp.concatenate([m] * (wide // 128), 1))
            hi, lo = split(p)
            new = dot_nn(jnp.concatenate([hi, lo], 0), v)
            new = new[:n] + new[n:]
            if not first:
                new = load(acc) * doubled(jnp.exp(old - m)) + new
            store(acc, new)
            store(mx, m)

        def closed(pattern, rows):
            value, m = acc[rows, :], mx[rows, :]
            o, l = value[:, :128], value[:, 128:]
            sums[pattern : pattern + 1, :] += jnp.sum(m + jnp.log(l), 0, keepdims=True)
            lane = lax.broadcasted_iota(jnp.int32, m.shape, 1)
            return jnp.where(lane < HD, o + swap(o), jnp.where(lane < 96, l, m))

        def merge(pattern, ci, rows, of):
            r0, r1 = R[ci, rows, :], closed(pattern, of)
            m0 = jnp.broadcast_to(r0[:, 96:97], r0.shape)
            m1 = jnp.broadcast_to(r1[:, 96:97], r1.shape)
            m = jnp.maximum(m0, m1)
            both = r0 * jnp.exp(m0 - m) + r1 * jnp.exp(m1 - m)
            lane = lax.broadcasted_iota(jnp.int32, r0.shape, 1)
            R[ci, rows, :] = jnp.where(lane < 96, both, m)

        def q1(g, carry):
            base = 512 * g

            def at(t, n):
                return pl.ds(pl.multiple_of(base + t, 128), n)

            for kb in range(4):
                start = 128 * kb
                each = 512 - start
                ks = at(start, 128)
                tile(
                    start,
                    qc[:, at(start, each), :].reshape(2 * each, 256),
                    kc[:, ks, :].reshape(512, 128),
                    vc[:, ks, :].reshape(512, 256),
                    b1,
                    2,
                    kb == 0,
                )
            for c in range(2):
                for i in range(2):
                    R[c, at(256 * i, 256), :] = closed(0, pl.ds(512 * c + 256 * i, 256))
            return carry

        lax.fori_loop(0, 3, q1, 0)

        par = offs[1]
        for base, length in ((0, 1024), (1024, 512)):
            for start in range(0, length, 256):
                ks = slice(base + start, base + start + 256)
                tile(
                    start,
                    qc[par, base + start : base + length, :],
                    jnp.concatenate([kc[par, ks, :], kc[par + 2, ks, :]], 0),
                    jnp.concatenate([vc[par, ks, :], vc[par + 2, ks, :]], 0),
                    b2,
                    1,
                    start == 0,
                )

            def join2(i, carry, base=base):
                t = pl.multiple_of(i * 256, 256)
                merge(1, par, pl.ds(base + t, 256), pl.ds(t, 256))
                return carry

            lax.fori_loop(0, length // 256, join2, 0)

        o3 = offs[2]

        @pl.when(o3 // 2 == b)
        def _():
            ci = lax.rem(o3, 2)
            for start in range(0, TOTAL, 512):
                ks = slice(start, start + 512)
                tile(start, qc[ci, start:TOTAL, :], kc[o3, ks, :], vc[o3, ks, :], b3, 1, start == 0)

            def join3(i, carry):
                t = pl.multiple_of(i * 256, 256)
                merge(2, ci, pl.ds(t, 256), pl.ds(t, 256))
                return carry

            lax.fori_loop(0, TOTAL // 256, join3, 0)

        for start in range(0, THIRD, 256):
            ks = slice(start, start + 256)
            tile(
                start, q4[start:THIRD, :], k4[:, ks, :].reshape(512, 128), v4[:, ks, :].reshape(512, 256), b4, 1, start == 0
            )
        for i in range(2):
            merge(3, qc4 - 2 * b, pl.ds(qv4 + 768 * i, 256, stride=3), pl.ds(256 * i, 256))

        @pl.when(kc5 // 2 == b)
        def _():
            tile(0, q5[...], k5[...], v5[...], b3, 1, True)
            for i in range(2):
                merge(4, lax.rem(kc5, 2), pl.ds(kv5 + 768 * i, 256, stride=3), pl.ds(256 * i, 256))

        def finish(m, carry):
            ci = lax.rem(m, 2)
            rows = pl.ds(pl.multiple_of((m // 2) * ROWS, 64), ROWS)
            r = R[ci, rows, :]
            l = jnp.broadcast_to(r[:, HD : HD + 1], r.shape)
            out = r / l
            ap[m] = pick(out[:HALF], swap(out[HALF:]))
            lse[ci, rows, :] = jnp.broadcast_to(r[:, 96:97], r.shape) + jnp.log(l)
            return carry

        lax.fori_loop(0, HOMES, finish, 0, unroll=2)


def attention_forward(info, own, sib):
    state = pltpu.VMEM((2, TOTAL, 128), F32)
    return pl.pallas_call(
        forward_kernel,
        out_shape=[
            jax.ShapeDtypeStruct((HOMES, HALF, 128), F32),
            jax.ShapeDtypeStruct((2, TOTAL, 128), F32),
            jax.ShapeDtypeStruct((8, 128), F32),
        ],
        in_specs=[SM, VM, VM],
        out_specs=[VM, VM, VM],
        scratch_shapes=[
            pltpu.VMEM((4, TOTAL, 128), F32),
            pltpu.VMEM((4, TOTAL, 128), BF16),
            pltpu.VMEM((4, TOTAL, 256), BF16),
            state,
            pltpu.VMEM((2, TOTAL, 256), BF16),
            pltpu.VMEM((2, THIRD, 128), BF16),
            pltpu.VMEM((2, THIRD, 256), BF16),
            pltpu.VMEM((THIRD, 256), BF16),
            pltpu.VMEM((THIRD, 128), BF16),
            pltpu.VMEM((THIRD, 256), BF16),
            pltpu.VMEM((THIRD, 256), BF16),
            pltpu.VMEM((TOTAL, 256), F32),
            pltpu.VMEM((TOTAL, 128), F32),
            state,
            pltpu.VMEM((256, 512), F32),
            pltpu.VMEM((256, 512), F32),
            pltpu.VMEM((512, 512), F32),
            pltpu.VMEM((256, 512), F32),
        ],
        compiler_params=params(),
    )(info, own, sib)


class Place:
    def __init__(self):
        p, s = lax.axis_index("pat"), lax.axis_index("seq")
        self.p, self.s = p, s
        self.x, self.core, self.z, self.y = p // 2, lax.rem(p, 2), s // 2, lax.rem(s, 2)
        self.peer = to(self.x * 2 + 1 - self.core, s)
        self.xn = to((1 - self.x) * 2 + self.core, s)
        self.yn = to(p, self.z * 2 + 1 - self.y)
        self.left, self.right = to(p, s - 2), to(p, s + 2)

    def greet(self, barrier, line=True):
        for d in (self.peer, self.xn, self.yn):
            pl.semaphore_signal(barrier, inc=1, device_id=d, device_id_type=MESH)
        if not line:
            return 3

        @pl.when(self.z > 0)
        def _():
            pl.semaphore_signal(barrier, inc=1, device_id=self.left, device_id_type=MESH)

        @pl.when(self.z < 3)
        def _():
            pl.semaphore_signal(barrier, inc=1, device_id=self.right, device_id_type=MESH)

        return 3 + (self.z > 0).astype(jnp.int32) + (self.z < 3).astype(jnp.int32)


def remote(src, dst, a, b, d):
    return pltpu.make_async_remote_copy(
        src_ref=src, dst_ref=dst, send_sem=a, recv_sem=b, device_id=d, device_id_type=MESH
    )


def add_in(dst, src):
    lead = dst.shape[:-2]

    def one(i, carry):
        index = []
        for d in reversed(lead):
            index.insert(0, lax.rem(i, d))
            i = i // d
        dst[tuple(index)] += src[tuple(index)]
        return carry

    lax.fori_loop(0, math.prod(lead), one, 0)


class Sems:
    NAMES = ("sc", "rc", "s1", "r1", "s2", "r2", "sl", "rl", "sr", "rr")

    def __init__(self, refs):
        for name, ref in zip(self.NAMES, refs):
            setattr(self, name, ref)

    @staticmethod
    def scratch(n):
        dma = pltpu.SemaphoreType.DMA
        return [dma((n, 2)), dma((n, 2))] + [dma((n,)) for _ in range(8)]


class Chunk:
    def __init__(self, place, k, x_first, sems, b0=None, b1=None, b2=None, bl=None, br=None, part=None, put=None):
        self.at, self.k, self.x_first, self.sems = place, k, x_first, sems
        self.b0, self.b1, self.b2, self.bl, self.br = b0, b1, b2, bl, br
        self.part, self.put = part, put

    def core(self, i):
        k, m = self.k, self.sems
        return remote(self.part(i, 1 - self.at.core), self.b0.at[i], m.sc.at[k, i], m.rc.at[k, i], self.at.peer)

    def one(self):
        k, at, m = self.k, self.at, self.sems
        if self.x_first:
            return remote(self.b0.at[1 - at.x], self.b1, m.s1.at[k], m.r1.at[k], at.xn)
        return remote(self.b0.at[:, :, 1 - at.y], self.b1, m.s1.at[k], m.r1.at[k], at.yn)

    def two(self):
        k, at, m = self.k, self.at, self.sems
        if self.x_first:
            return remote(self.b1.at[:, 1 - at.y], self.b2, m.s2.at[k], m.r2.at[k], at.yn)
        return remote(self.b1.at[1 - at.x], self.b2, m.s2.at[k], m.r2.at[k], at.xn)

    def rightward(self, i):
        k, part, m = self.k, pl.ds(i + 1, 3 - i), self.sems
        src = self.b2 if i == 0 else self.bl
        return remote(src.at[part], self.bl.at[part], m.sr.at[k], m.rl.at[k], self.at.right)

    def leftward(self, i):
        k, part, m = self.k, pl.ds(0, i), self.sems
        src = self.b2 if i == 3 else self.br
        return remote(src.at[part], self.br.at[part], m.sl.at[k], m.rr.at[k], self.at.left)

    def own_core(self, i):
        self.core(i).wait_recv()
        add_in(self.b0.at[i], self.part(i, self.at.core))

    def stage1(self):
        for i in range(2):
            self.own_core(i)
        self.one().start()

    def arrived(self):
        self.one().wait_recv()
        add_in(self.b1, self.b0.at[self.at.x] if self.x_first else self.b0.at[:, :, self.at.y])

    def stage2(self):
        self.arrived()
        self.two().start()

    def stage3(self):
        self.two().wait_recv()
        add_in(self.b2, self.b1.at[:, self.at.y] if self.x_first else self.b1.at[self.at.x])

        @pl.when(self.at.z == 0)
        def _():
            self.rightward(0).start()

        @pl.when(self.at.z == 3)
        def _():
            self.leftward(3).start()

    def stage4(self):
        @pl.when(self.at.z == 1)
        def _():
            self.rightward(0).wait_recv()
            self.bl[2:4] += self.b2[2:4]
            self.rightward(1).start()

        @pl.when(self.at.z == 2)
        def _():
            self.leftward(3).wait_recv()
            self.br[0:2] += self.b2[0:2]
            self.leftward(2).start()

    def stage5(self):
        @pl.when(self.at.z == 2)
        def _():
            self.rightward(1).wait_recv()
            self.bl[3:4] += self.b2[3:4]
            self.rightward(2).start()

        @pl.when(self.at.z == 1)
        def _():
            self.leftward(2).wait_recv()
            self.br[0:1] += self.b2[0:1]
            self.leftward(1).start()

    def stage6(self):
        @pl.when(self.at.z == 3)
        def _():
            self.rightward(2).wait_recv()
            self.put(self.b2[3] + self.bl[3])

        @pl.when(self.at.z == 0)
        def _():
            self.leftward(1).wait_recv()
            self.put(self.b2[0] + self.br[0])

        @pl.when(self.at.z == 1)
        def _():
            self.put(self.b2[1] + self.bl[1] + self.br[1])

        @pl.when(self.at.z == 2)
        def _():
            self.put(self.b2[2] + self.bl[2] + self.br[2])

    def line_sent(self):
        for i in range(4):

            @pl.when(self.at.z == i)
            def _(i=i):
                if i < 3:
                    self.rightward(i).wait_send()
                if i > 0:
                    self.leftward(i).wait_send()


class Reducer:
    def __init__(self, place, n, part, scratch, put):
        self.place, self.n, self.part, self.put = place, n, part, put
        self.c0, self.c1a, self.c1b, self.c2, self.zl, self.zr = scratch[:6]
        self.sems = Sems(scratch[6:16])
        self.pairs = (n + 1) // 2

    @staticmethod
    def scratch(n, rows):
        bufs = [(n, 2, 4, 2), ((n + 1) // 2, 4, 2), (max(n // 2, 1), 2, 4), (n, 4), (n, 4), (n, 4)]
        return [pltpu.VMEM(b + (rows, D), F32) for b in bufs] + Sems.scratch(n)

    def chunk(self, k, parity):
        return Chunk(
            self.place,
            k,
            parity == 0,
            self.sems,
            self.c0.at[k],
            (self.c1b if parity else self.c1a).at[k // 2],
            self.c2.at[k],
            self.zl.at[k],
            self.zr.at[k],
            self.part(k),
            lambda v: self.put(k, v),
        )

    def send(self, first, after):
        def one(k, carry):
            for i in range(2):
                self.chunk(k, 0).core(i).start()
            return carry

        lax.fori_loop(first, after, one, 0)

    def one(self, stage, pair):
        for parity in range(2):
            k = 2 * pair + parity
            k = jnp.int32(k) if isinstance(k, int) else k

            @pl.when(jnp.logical_and(k >= 0, k < self.n))
            def _(k=k, parity=parity):
                getattr(self.chunk(k, parity), f"stage{stage}")()

    def early(self, pair):
        self.one(1, pair)

    def step(self, tau):
        self.one(1, tau)
        for stage in range(2, 7):
            self.one(stage, tau - stage)

    def finish(self):
        def one(k, carry):
            for parity in range(2):

                @pl.when(lax.rem(k, 2) == parity)
                def _(parity=parity):
                    c = self.chunk(k, parity)
                    for i in range(2):
                        c.core(i).wait_send()
                    c.one().wait_send()
                    c.two().wait_send()
                    c.line_sent()

            return carry

        lax.fori_loop(0, self.n, one, 0)


class SmallSum:
    def __init__(self, place, S, bufs, send, recv, put):
        self.at, self.S, self.send, self.recv, self.put = place, S, send, recv, put
        self.d0, self.d1, self.d2, self.dl, self.dr, self.t1, self.t2, self.t3, self.fl, self.fr = bufs

    @staticmethod
    def scratch():
        return [pltpu.VMEM((8, D), F32)] * 10 + [pltpu.SemaphoreType.DMA((5,)), pltpu.SemaphoreType.DMA((5,))]

    def hop(self, src, dst, i, d):
        return remote(src, dst, self.send.at[i], self.recv.at[i], d)

    def core(self):
        return self.hop(self.S, self.d0, 0, self.at.peer)

    def along_x(self):
        return self.hop(self.t1, self.d1, 1, self.at.xn)

    def along_y(self):
        return self.hop(self.t2, self.d2, 2, self.at.yn)

    def rightward(self, i):
        return self.hop(self.t3 if i == 0 else self.fl, self.dl, 3, self.at.right)

    def leftward(self, i):
        return self.hop(self.t3 if i == 3 else self.fr, self.dr, 4, self.at.left)

    def stage1(self):
        self.core().wait_recv()
        self.t1[...] = self.S[...] + self.d0[...]
        self.along_x().start()

    def stage2(self):
        self.along_x().wait_recv()
        self.t2[...] = self.t1[...] + self.d1[...]
        self.along_y().start()

    def stage3(self):
        self.along_y().wait_recv()
        self.t3[...] = self.t2[...] + self.d2[...]

        @pl.when(self.at.z == 0)
        def _():
            self.rightward(0).start()

        @pl.when(self.at.z == 3)
        def _():
            self.leftward(3).start()

    def from_left(self, i):
        self.rightward(i).wait_recv()
        self.fl[...] = self.dl[...] + self.t3[...]

    def from_right(self, i):
        self.leftward(i).wait_recv()
        self.fr[...] = self.dr[...] + self.t3[...]

    def stage4(self):
        @pl.when(self.at.z == 1)
        def _():
            self.from_left(0)
            self.rightward(1).start()

        @pl.when(self.at.z == 2)
        def _():
            self.from_right(3)
            self.leftward(2).start()

    def stage5(self):
        @pl.when(self.at.z == 2)
        def _():
            self.from_left(1)
            self.rightward(2).start()

        @pl.when(self.at.z == 1)
        def _():
            self.from_right(2)
            self.leftward(1).start()

    def stage6(self):
        @pl.when(self.at.z == 3)
        def _():
            self.from_left(2)
            self.put(self.fl[...])

        @pl.when(self.at.z == 0)
        def _():
            self.from_right(1)
            self.put(self.fr[...])

        @pl.when(jnp.logical_or(self.at.z == 1, self.at.z == 2))
        def _():
            self.put(self.fl[...] + self.dr[...])

    def finish(self):
        for c in (self.core(), self.along_x(), self.along_y()):
            c.wait_send()
        for i in range(4):

            @pl.when(self.at.z == i)
            def _(i=i):
                if i < 3:
                    self.rightward(i).wait_send()
                if i > 0:
                    self.leftward(i).wait_send()


def small_outputs(place, counts, outs, tot):
    ga, gi, gf, gh, means = outs

    def put(v):
        tot[...] = v
        d = place.p * RUNS + place.s
        for i, ref in enumerate((ga, gi, gf)):
            ref[...] = pltpu.roll(tot[i : i + 1, :], D - PIECE * d, 1)[:, :PIECE]
        row = tot[pl.ds(3 + d // 8, 1), :]
        gh[...] = pltpu.roll(row, D - 4 * PIECE * lax.rem(d, 8), 1)[:, : 4 * PIECE]
        lane = lax.broadcasted_iota(jnp.int32, (1, 128), 1)
        scale = jnp.full((1, 128), counts[0], F32)
        for i in range(1, PATTERNS):
            scale = jnp.where(lane == i, counts[i], scale)
        means[...] = (tot[7:8, :128] / scale)[:, :PATTERNS]

    return put


N_PIECES = 9
SUB = 8


def finish_kernel(counts, rec, x_ref, dy1_ref, w, ga1, S_in, gx, g_qkv, ga, gi, gf, gh, means, dqkv, lhs, th, tl, r_hi, r_lo, tiles, S, tot, gx2, *scratch):
    place = Place()
    barrier = pltpu.get_barrier_semaphore()
    expected = place.greet(barrier)
    for j in range(HEADS // 2):
        u, v = rec[2 * j, ROWS:PACK, :], rec[2 * j + 1, ROWS:PACK, :]
        cols = slice(128 * j, 128 * j + 128)
        dqkv[0:HALF, cols] = pick(u, swap(v))
        dqkv[HALF:ROWS, cols] = pick(swap(u), v)
        u, v = rec[2 * j, 0:ROWS, :], rec[2 * j + 1, 0:ROWS, :]
        dqkv[:, D + 128 * j : D + 128 * j + 128] = pick(u, swap(v))
        dqkv[:, 2 * D + 128 * j : 2 * D + 128 * j + 128] = pick(swap(u), v)
    gain = ga1[...][None, :]
    n, rs = normed(x_ref[...])
    put_turned(th, tl, n * gain)

    def part(k):
        rows = pl.ds(pl.multiple_of(lax.rem(k, 3) * SUB, SUB), SUB)
        return lambda i, c: tiles.at[k // 3, i, c, :, :, rows, :]

    def put(k, v):
        g_qkv[
            pl.ds(pl.multiple_of(lax.rem(k, 3) * SUB, SUB), SUB), pl.ds(pl.multiple_of((k // 3) * D, D), D)
        ] = v

    n_r = 16
    big = Reducer(place, N_PIECES, part, scratch[:n_r], put)
    rest = scratch[n_r:]
    small = SmallSum(
        place, S, rest[:10], rest[10], rest[11], small_outputs(place, counts, (ga, gi, gf, gh, means), tot)
    )

    def tile_of(j, carry):
        r_hi[...], r_lo[...] = split(dqkv[:, pl.ds(pl.multiple_of(D * j, D), D)])

        def one(i, inner):
            rows = pl.ds(pl.multiple_of(i * 2 * ROWS, 128), 2 * ROWS)
            h, l = th[rows, :], tl[rows, :]
            v = dot_nn(h, r_hi[...]) + dot_nn(h, r_lo[...]) + dot_nn(l, r_hi[...])
            tiles[j, i] = v.reshape(2, 4, 2, PIECE, D)
            return inner

        lax.fori_loop(0, 2, one, 0)

        @pl.when(j == 0)
        def _():
            pl.semaphore_wait(barrier, expected)

        big.send(3 * j, 3 * j + 3)

        @pl.when(j > 0)
        def _():
            big.early(j - 1)

        return carry

    lax.fori_loop(0, 3, tile_of, 0)
    gx2[...] = jnp.zeros_like(gx2)

    def back(j, carry):
        cols = pl.ds(pl.multiple_of(D * j, D), D)
        put_split(lhs, dqkv[:, cols])
        gx2[...] += halves_sum(dot_nt(lhs[...], w[:, cols]))
        return carry

    lax.fori_loop(0, 3, back, 0)
    e = gx2[...]
    S[...] = S_in[...]
    S[0:1, :] = jnp.sum(e * n, 0, keepdims=True)
    small.core().start()
    gx[...] = (dy1_ref[...] + norm_back(e * gain, n, rs)).reshape(ROWS, 1, D)
    small.stage1()

    def step(tau, carry):
        for stage in range(2, 7):

            @pl.when(tau == stage + 1)
            def _(stage=stage):
                getattr(small, f"stage{stage}")()

        big.step(tau)
        return carry

    lax.fori_loop(2, big.pairs + 6, step, 0)

    big.finish()
    small.finish()


def finish(rec, x, dy1, w, ga, S, counts, cid):
    return pl.pallas_call(
        functools.partial(finish_kernel, counts),
        out_shape=[jax.ShapeDtypeStruct((ROWS, 1, D), F32), jax.ShapeDtypeStruct((PIECE, 3 * D), F32)]
        + [jax.ShapeDtypeStruct((1, n), F32) for n in (PIECE, PIECE, PIECE, 4 * PIECE, PATTERNS)],
        in_specs=[VM] * 6,
        out_specs=[VM] * 7,
        scratch_shapes=[
            pltpu.VMEM((ROWS, 3 * D), F32),
            pltpu.VMEM((2 * ROWS, D), BF16),
            pltpu.VMEM((D, ROWS), BF16),
            pltpu.VMEM((D, ROWS), BF16),
            pltpu.VMEM((ROWS, D), BF16),
            pltpu.VMEM((ROWS, D), BF16),
            pltpu.VMEM((3, 2, 2, 4, 2, PIECE, D), F32),
            pltpu.VMEM((8, D), F32),
            pltpu.VMEM((8, D), F32),
            pltpu.VMEM((ROWS, D), F32),
        ]
        + Reducer.scratch(N_PIECES, SUB)
        + SmallSum.scratch(),
        compiler_params=params(collective_id=cid, has_side_effects=True),
    )(rec, x, dy1, w, ga, S)


def deliver_kernel(*refs):
    n = len(refs) // 2
    for src, dst in zip(refs[:n], refs[n:]):
        dst[...] = src[...]


def deliver(*arrays):
    return pl.pallas_call(
        deliver_kernel,
        out_shape=[jax.ShapeDtypeStruct(v.shape, v.dtype) for v in arrays],
        in_specs=[VM] * len(arrays),
        out_specs=[VM] * len(arrays),
        compiler_params=params(),
    )(*arrays)


def rows_from_pairs(rec, dst):
    for j in range(HEADS // 2):
        u, v = rec[2 * j], rec[2 * j + 1]
        cols = slice(128 * j, 128 * j + 128)
        dst[0:HALF, cols] = pick(u, swap(v))
        dst[HALF:ROWS, cols] = pick(swap(u), v)


def pairs_from_rows(src, dst):
    for j in range(HEADS // 2):
        top = src[0:HALF, 128 * j : 128 * j + 128]
        bottom = src[HALF:ROWS, 128 * j : 128 * j + 128]
        dst[2 * j] = pick(top, swap(bottom))
        dst[2 * j + 1] = pick(swap(top), bottom)


def halves_sum(r):
    return r[:ROWS] + r[ROWS:]


def norm_back(f, n, rs):
    return (f - jnp.mean(f, -1, keepdims=True) - n * jnp.mean(f * n, -1, keepdims=True)) * rs


def put_turned(hi_ref, lo_ref, v):
    for j in range(D // 128):
        t = v[:, 128 * j : 128 * j + 128].T
        hi, lo = split(t)
        hi_ref[128 * j : 128 * j + 128, :] = hi
        lo_ref[128 * j : 128 * j + 128, :] = lo


class ToHeads:
    def __init__(self, pk, rec, send, recv):
        self.pk, self.rec, self.send, self.recv = pk, rec, send, recv
        self.facts = place_facts()

    def greet(self):
        p, s, x, core, active, head = self.facts
        barrier = pltpu.get_barrier_semaphore()

        @pl.when(active)
        def _():
            def one(m, carry):
                q, t = home_device(core, m)

                @pl.when(jnp.logical_not(same(p, s, q, t)))
                def _():
                    pl.semaphore_signal(barrier, inc=1, device_id=to(q, t), device_id_type=MESH)

                return carry

            lax.fori_loop(0, HOMES, one, 0)

    def copy(self, h):
        p, s, x, core, active, head = self.facts
        slot = s * 2 + core
        q, t = head_device(h, x)
        far = pltpu.make_async_remote_copy(
            src_ref=self.pk.at[h],
            dst_ref=self.rec.at[slot],
            send_sem=self.send.at[h],
            recv_sem=self.recv.at[slot],
            device_id=to(q, t),
            device_id_type=MESH,
        )
        return same(p, s, q, t), lambda: pltpu.make_async_copy(self.pk.at[h], self.rec.at[slot], self.recv.at[slot]), far

    def wait(self, others):
        p, s, x, core, active, head = self.facts
        mine = jnp.logical_and(active, core == x).astype(jnp.int32)
        pl.semaphore_wait(pltpu.get_barrier_semaphore(), HEADS + others - mine)

    def start(self):
        p, s, x, core, active, head = self.facts

        def one(j, carry):
            here, near, far = self.copy(lax.rem(j + 3 * (s // 2) + 2 * p, HEADS))

            @pl.when(here)
            def _():
                near().start()

            @pl.when(jnp.logical_not(here))
            def _():
                far.start()

            return carry

        lax.fori_loop(0, HEADS, one, 0)

    def finish(self):
        active = self.facts[4]

        @pl.when(active)
        def _():
            def arrive(m, carry):
                pltpu.make_async_copy(self.rec.at[m], self.rec.at[m], self.recv.at[m]).wait()
                return carry

            lax.fori_loop(0, HOMES, arrive, 0)

        def sent(h, carry):
            here, near, far = self.copy(h)

            @pl.when(jnp.logical_not(here))
            def _():
                far.wait_send()

            return carry

        lax.fori_loop(0, HEADS, sent, 0)


FT = 512


def product(hi, lo, r_hi, r_lo, put):
    def one(i, carry):
        rows = pl.ds(pl.multiple_of(i * 2 * ROWS, 128), 2 * ROWS)
        h, l = hi[rows, :], lo[rows, :]
        put(i, dot_nn(h, r_hi[...]) + dot_nn(h, r_lo[...]) + dot_nn(l, r_hi[...]))
        return carry

    lax.fori_loop(0, 2, one, 0)


N_FF = 9
N_COLS = 5


def ff_kernel(rec, x_ref, g3, wo, wu, wd, gi1, gf1, gh1, sums, out3, drec, dy1_ref, S, C0, C1a, C1b, dap, lhs, lhs2, gi, gf, gh, gh_g, g_ref, out_ref, V, N1, U, GP, E, ACC, th, tl, r_hi, r_lo, cols_t, rows_t, c0, c1a, c1b, osem, dsend, drecv, *rsems):
    place = Place()
    sems = Sems(rsems)
    travel = ToHeads(dap, drec, dsend, drecv)
    travel.greet()
    place.greet(pltpu.get_barrier_semaphore(), False)

    def chunk(k, part=None):
        if not isinstance(k, int):
            return Chunk(place, k, True, sems, c0.at[k], part=part)
        x_first = k % 2 == 0
        b1 = None if k < N_COLS else (c1a if x_first else c1b).at[(k - N_COLS) // 2]
        return Chunk(place, k, x_first, sems, c0.at[k], b1, part=part)

    for wide, flat in ((gi, gi1), (gf, gf1), (gh, gh1)):
        wide[...] = flat[...][None, :]
    g_ref[...] = g3[...].reshape(ROWS, D)
    rows_from_pairs(rec, V)
    na, rs_a = normed(V[...])
    V[...] = na
    put_split(lhs, na * gi[...])

    def project(j, carry):
        cols = pl.ds(pl.multiple_of(256 * j, 256), 256)
        N1[:, cols] = x_ref[:, cols] + halves_sum(dot_nn(lhs[...], wo[:, cols]))
        return carry

    lax.fori_loop(0, 3, project, 0)
    y1 = N1[...]
    out_ref[...] = y1
    ny, rs_y = normed(y1)
    N1[...] = ny
    put_split(lhs, ny * gf[...])

    def up(j, su):
        cols = pl.ds(pl.multiple_of(j * FT, FT), FT)
        z = halves_sum(dot_nn(lhs[...], wu[:, cols]))
        phi = 0.5 * (1.0 + lax.erf(z * math.sqrt(0.5)))
        u = z * phi
        U[:, cols] = u
        GP[:, cols] = phi + z * jnp.exp(-0.5 * z * z) * (1.0 / math.sqrt(2.0 * math.pi))
        return su + jnp.sum(u, -1, keepdims=True)

    zero = jnp.zeros((ROWS, 1), F32)
    mean = lax.fori_loop(0, FF // FT, up, zero) * (1.0 / FF)

    def spread(j, sv):
        cols = pl.ds(pl.multiple_of(j * FT, FT), FT)
        c = U[:, cols] - mean
        return sv + jnp.sum(c * c, -1, keepdims=True)

    rs_u = lax.rsqrt(lax.fori_loop(0, FF // FT, spread, zero) * (1.0 / FF) + LN_EPSILON)
    ACC[...] = jnp.zeros_like(ACC)

    def lower(j, carry):
        cols = pl.ds(pl.multiple_of(j * FT, FT), FT)
        n = (U[:, cols] - mean) * rs_u
        U[:, cols] = n
        put_split(lhs2, n * gh[:, cols])
        ACC[...] += halves_sum(dot_nn(lhs2[...], wd[cols, :]))
        return carry

    lax.fori_loop(0, FF // FT, lower, 0)
    out3[...] = (out_ref[...] + ACC[...]).reshape(ROWS, 1, D)

    travel.wait(3)
    r_hi[...], r_lo[...] = split(g_ref[...])

    def down(j, q):
        return chunk(N_COLS + q, lambda i, c: rows_t.at[lax.rem(j, 2), :, :, q])

    def down_step(j, carry):
        @pl.when(j < 4)
        def _():
            cols = pl.ds(pl.multiple_of(D * j, D), D)
            put_turned(th, tl, U[:, cols] * gh[:, cols])
            sent = place.core != lax.rem(j, 2)

            @pl.when(jnp.logical_and(j >= 2, sent))
            def _():
                for q in range(4):
                    down(j - 2, q).core(j // 2 - 1).wait_send()

            def put(i, v):
                rows_t[lax.rem(j, 2), pl.ds(2 * i, 2)] = v.reshape(2, 2, 4, PIECE, D)

            product(th, tl, r_hi, r_lo, put)

            @pl.when(sent)
            def _():
                for q in range(4):
                    down(j, q).core(j // 2).start()

        @pl.when(jnp.logical_and(j > 0, place.core == lax.rem(j + 1, 2)))
        def _():
            for q in range(4):
                down(j - 1, q).own_core((j - 1) // 2)

        return carry

    lax.fori_loop(0, 5, down_step, 0)
    for k in range(N_COLS, N_FF):
        chunk(k).one().start()

    put_split(lhs, g_ref[...])

    def back_down(j, sums):
        cols = pl.ds(pl.multiple_of(j * FT, FT), FT)
        e = halves_sum(dot_nt(lhs[...], wd[cols, :]))
        n = U[:, cols]
        gh_g[:, cols] = jnp.sum(e * n, 0, keepdims=True)
        f = e * gh[:, cols]
        E[:, cols] = f
        return sums[0] + jnp.sum(f, -1, keepdims=True), sums[1] + jnp.sum(f * n, -1, keepdims=True)

    sf, sfn = lax.fori_loop(0, FF // FT, back_down, (zero, zero))
    mf, mfn = sf * (1.0 / FF), sfn * (1.0 / FF)
    ACC[...] = jnp.zeros_like(ACC)

    def back_up(j, carry):
        cols = pl.ds(pl.multiple_of(j * FT, FT), FT)
        dz = (E[:, cols] - mf - U[:, cols] * mfn) * rs_u * GP[:, cols]
        E[:, cols] = dz
        put_split(lhs2, dz)
        ACC[...] += halves_sum(dot_nt(lhs2[...], wu[:, cols]))
        return carry

    lax.fori_loop(0, FF // FT, back_up, 0)
    e = ACC[...]
    ny = N1[...]
    S[2:3, :] = jnp.sum(e * ny, 0, keepdims=True)
    dy1 = g_ref[...] + norm_back(e * gf[...], ny, rs_y)
    dy1_ref[...] = dy1
    put_split(lhs, dy1)

    def project_back(j, carry):
        cols = pl.ds(pl.multiple_of(256 * j, 256), 256)
        ACC[:, cols] = halves_sum(dot_nt(lhs[...], wo[cols, :]))
        return carry

    lax.fori_loop(0, 3, project_back, 0)
    e = ACC[...]
    na = V[...]
    S[1:2, :] = jnp.sum(e * na, 0, keepdims=True)
    S[0:1, :] = jnp.zeros((1, D), F32)
    for j in range(4):
        S[3 + j : 4 + j, :] = gh_g[:, D * j : D * j + D]
    lane = lax.broadcasted_iota(jnp.int32, (1, 128), 1)
    S[7:8, :] = jnp.zeros((1, D), F32)
    S[7:8, 0:128] = sum(jnp.where(lane == i, sums[i : i + 1, :], 0.0) for i in range(PATTERNS))
    ACC[...] = norm_back(e * gi[...], na, rs_a)
    pairs_from_rows(ACC, dap)
    travel.start()

    def column(k):
        return chunk(k, lambda i, c: cols_t.at[lax.rem(k, 2), i, c])

    def out_copy(k):
        return pltpu.make_async_copy(c0.at[k], C0.at[k], osem.at[k])

    put_turned(th, tl, na * gi[...])
    r_hi[...], r_lo[...] = split(dy1)

    def column_step(k, carry):
        @pl.when(k < N_COLS)
        def _():
            @pl.when(k >= 2)
            def _():
                for i in range(2):
                    column(k - 2).core(i).wait_send()

            @pl.when(k >= 1)
            def _():
                r_hi[...], r_lo[...] = split(E[:, pl.ds(pl.multiple_of(D * (k - 1), D), D)])

            def put(i, v):
                cols_t[lax.rem(k, 2), i] = v.reshape(2, 4, 2, PIECE, D)

            product(th, tl, r_hi, r_lo, put)
            for i in range(2):
                column(k).core(i).start()

            @pl.when(k == 0)
            def _():
                put_turned(th, tl, N1[...] * gf[...])

        @pl.when(k > 0)
        def _():
            for i in range(2):
                column(k - 1).own_core(i)
            out_copy(k - 1).start()

        return carry

    lax.fori_loop(0, N_COLS + 1, column_step, 0)

    def c1_copy(k):
        b1, out = (c1a, C1a) if k % 2 == 0 else (c1b, C1b)
        i = (k - N_COLS) // 2
        return pltpu.make_async_copy(b1.at[i], out.at[i], osem.at[k])

    for k in range(N_COLS, N_FF):
        chunk(k).arrived()
        c1_copy(k).start()
    travel.finish()
    for k in range(N_COLS - 2, N_COLS):
        for i in range(2):
            column(jnp.int32(k)).core(i).wait_send()
    for j in range(2, 4):

        @pl.when(place.core != j % 2)
        def _(j=j):
            for q in range(4):
                down(jnp.int32(j), q).core(j // 2).wait_send()

    for k in range(N_COLS):
        out_copy(k).wait()
    for k in range(N_COLS, N_FF):
        chunk(k).one().wait_send()
        c1_copy(k).wait()


def feed_forward(rec, x, g, wo, wu, wd, gi, gf, gh, sums):
    act = jax.ShapeDtypeStruct((ROWS, D), F32)
    wide = pltpu.VMEM((ROWS, FF), F32)
    thin = pltpu.VMEM((ROWS, D), F32)
    return pl.pallas_call(
        ff_kernel,
        out_shape=[
            jax.ShapeDtypeStruct((ROWS, 1, D), F32),
            jax.ShapeDtypeStruct((HOMES, HALF, 128), F32),
            act,
            jax.ShapeDtypeStruct((8, D), F32),
            jax.ShapeDtypeStruct((N_COLS, 2, 4, 2, PIECE, D), F32),
            jax.ShapeDtypeStruct((2, 4, 2, PIECE, D), F32),
            jax.ShapeDtypeStruct((2, 2, 4, PIECE, D), F32),
        ],
        in_specs=[VM] * 10,
        out_specs=[VM, ANY, VM, VM, ANY, ANY, ANY],
        scratch_shapes=[
            pltpu.VMEM((HEADS, HALF, 128), F32),
            pltpu.VMEM((2 * ROWS, D), BF16),
            pltpu.VMEM((2 * ROWS, FT), BF16),
            pltpu.VMEM((1, D), F32),
            pltpu.VMEM((1, D), F32),
            pltpu.VMEM((1, FF), F32),
            pltpu.VMEM((1, FF), F32),
            thin,
            thin,
            thin,
            thin,
            wide,
            wide,
            wide,
            thin,
        ]
        + [
            pltpu.VMEM((D, ROWS), BF16),
            pltpu.VMEM((D, ROWS), BF16),
            pltpu.VMEM((ROWS, D), BF16),
            pltpu.VMEM((ROWS, D), BF16),
            pltpu.VMEM((2, 2, 2, 4, 2, PIECE, D), F32),
            pltpu.VMEM((2, 4, 2, 4, PIECE, D), F32),
            pltpu.VMEM((N_FF, 2, 4, 2, PIECE, D), F32),
            pltpu.VMEM((2, 4, 2, PIECE, D), F32),
            pltpu.VMEM((2, 2, 4, PIECE, D), F32),
            pltpu.SemaphoreType.DMA((N_FF,)),
            pltpu.SemaphoreType.DMA((HEADS,)),
            pltpu.SemaphoreType.DMA((HOMES,)),
        ]
        + Sems.scratch(N_FF),
        compiler_params=params(collective_id=4, has_side_effects=True),
    )(rec, x, g, wo, wu, wd, gi, gf, gh, sums)


def back_all_kernel(offs, drec, own, sib, ap, lse, C0, C1a, C1b, grec, wo_g, up_g, down_g, qst, kc, vc, kt, qc, dc, lt, k4, v4, kt4, q4, d4, lt4, k5, v5, kt5, q5, d5, lt5, dk, dv, dq, dk4, dv4, dk5, dv5, dq4, dq5, b1, b2, b3, b4, dqt, ds_out, came, lsem, send, recv, qsend, qrecv, fsend, frecv, c0, c1a, c1b, c2, zl, zr, csem, *rsems):
    place = Place()
    p, s, x, core, active, head = place_facts()
    b = core
    o2, o3, o4, o5 = offs[1], offs[2], offs[3], offs[4]
    kvf, qf, X, df = dk, dv.at[0:2], dv.at[2:4], dq
    dqp = qst

    barrier = pltpu.get_barrier_semaphore()
    expected = place.greet(barrier)

    def greet_heads(h, carry):
        q, t = head_device(h, x)

        @pl.when(jnp.logical_not(same(p, s, q, t)))
        def _():
            pl.semaphore_signal(barrier, inc=1, device_id=to(q, t), device_id_type=MESH)

        return carry

    lax.fori_loop(0, HEADS, greet_heads, 0)
    from_homes = HOMES - (core == x).astype(jnp.int32)
    pl.semaphore_wait(barrier, expected + active.astype(jnp.int32) * from_homes)

    def put(k, v):
        @pl.when(k == 0)
        def _():
            wo_g[...] = v

        @pl.when(jnp.logical_and(k > 0, k < 5))
        def _():
            up_g[:, pl.ds(pl.multiple_of((k - 1) * D, D), D)] = v

        @pl.when(k >= 5)
        def _():
            down_g[pl.ds(pl.multiple_of((k - 5) * PIECE, PIECE), PIECE), :] = v

    sems = Sems(rsems)

    def chunk(k):
        x_first = k % 2 == 0
        b0 = c0.at[k] if k < N_COLS else None
        b1 = (c1a if x_first else c1b).at[k // 2]
        return Chunk(
            place, k, x_first, sems, b0, b1, c2.at[k], zl.at[k], zr.at[k], put=lambda v: put(jnp.int32(k), v)
        )

    def load(k):
        if k < N_COLS:
            return pltpu.make_async_copy(C0.at[k], c0.at[k], csem.at[k])
        src, dst = (C1a, c1a) if k % 2 == 0 else (C1b, c1b)
        return pltpu.make_async_copy(src.at[(k - N_COLS) // 2], dst.at[k // 2], csem.at[k])

    PAIRS = ((5, 6), (7, 8), (0, 1), (2, 3), (4,))

    def reduction(*todo):
        for stage, pair in todo:
            for k in PAIRS[pair]:
                if stage == 1:
                    load(k).wait()
                    chunk(k).one().start()
                elif stage == 2 and k >= N_COLS:
                    load(k).wait()
                    chunk(k).two().start()
                else:
                    getattr(chunk(k), f"stage{stage}")()


    def local_copies(m):
        t = pl.multiple_of((m // 2) * ROWS, 64)
        c, d = 2 * b + lax.rem(m, 2), 2 * (1 - b) + lax.rem(m, 2)
        return [
            pltpu.make_async_copy(own.at[m, pl.ds(0, ROWS), :], kvf.at[c, pl.ds(t, ROWS), :], lsem.at[m, 0]),
            pltpu.make_async_copy(sib.at[m], kvf.at[d, pl.ds(t, ROWS), :], lsem.at[m, 1]),
            pltpu.make_async_copy(own.at[m, pl.ds(ROWS, HALF), :], qst.at[m], lsem.at[m, 2]),
        ]

    lse_copy = pltpu.make_async_copy(lse, X, lsem.at[HOMES, 0])

    @pl.when(active)
    def _():
        lse_copy.start()

        def start(m, carry):
            for c in local_copies(m):
                c.start()
            return carry

        lax.fori_loop(0, HOMES, start, 0)

    for pair in PAIRS:
        for k in pair:
            load(k).start()
    reduction((2, 0), (1, 2), (2, 1))

    @pl.when(active)
    def _():
        b1[0] = key_bias((2, 128), (4, 128), 4, 1, 2 * b, True)
        b2[0] = key_bias((1, 256), (2, 256), 4, 2, 2 * b, True)
        b3[0] = key_bias((1, 256), (1, 256), 1, 1, 0, True)
        e4 = class_facts4(o4, b)[1]
        b4[0] = key_bias((1, 256), (2, 256), 12, 6, 6 * e4, True)
        for ref in (b1, b2, b3, b4):
            ref[1] = jnp.zeros(ref.shape[1:], F32)

        def wait(m, carry):
            for c in local_copies(m):
                c.wait()
            return carry

        lax.fori_loop(0, HOMES, wait, 0)
        lse_copy.wait()
        unpack_pairs(qst, 0, qf, 1.0 / math.sqrt(HD))

        def prepare(i, carry):
            c, t = i // 12, pl.multiple_of(lax.rem(i, 12) * 128, 128)
            k2, v2 = keys_and_values(kvf[c, pl.ds(t, 128), :])
            kc[c, pl.ds(t, 128), :] = k2.astype(BF16)
            vc[c, pl.ds(t, 128), :] = v2.astype(BF16)
            kt[c, :, pl.ds(t, 128)] = k2.T.astype(BF16)
            return carry

        lax.fori_loop(0, 48, prepare, 0)

        def prepare_q(i, carry):
            c, t = i // 12, pl.multiple_of(lax.rem(i, 12) * 128, 128)
            qc[c, pl.ds(t, 128), :] = query_quads(qf[c, pl.ds(t, 128), :])
            return carry

        lax.fori_loop(0, 24, prepare_q, 0)

    keys4, e4, (qc4, qv4) = class_facts4(o4, b)
    kc5, kv5 = lax.rem(o5, 4), o5 // 4
    qi4, qi5 = qc4 - 2 * b, lax.rem(kc5, 2)

    @pl.when(active)
    def _():
        for blk in range(4):
            r = slice(128 * blk, 128 * blk + 128)
            for e in range(2):
                c, v = keys4[e]
                k2, v2 = keys_and_values(kvf[c, pl.ds(v + 384 * blk, 128, stride=3), :])
                k4[e, r, :] = k2.astype(BF16)
                v4[e, r, :] = v2.astype(BF16)
                kt4[e, :, r] = k2.T.astype(BF16)
            q4[r, :] = query_quads(qf[qi4, pl.ds(qv4 + 384 * blk, 128, stride=3), :])
            rows = pl.ds(kv5 + 384 * blk, 128, stride=3)
            k2, v2 = keys_and_values(kvf[kc5, rows, :])
            k5[r, :] = k2.astype(BF16)
            v5[r, :] = v2.astype(BF16)
            kt5[:, r] = k2.T.astype(BF16)
            q5[r, :] = query_quads(qf[qi5, rows, :])
        dk[...] = jnp.zeros_like(dk)

    reduction((1, 3))

    @pl.when(active)
    def _():
        unpack_pairs(drec, 0, df, 1.0)

        def facts(m, carry):
            ci = lax.rem(m, 2)
            t = pl.multiple_of((m // 2) * ROWS, 32)
            prod = drec[m] * ap[m]
            low = lower_lanes(prod)
            d0 = jnp.sum(jnp.where(low, prod, 0.0), -1, keepdims=True)
            d1 = jnp.sum(jnp.where(low, 0.0, prod), -1, keepdims=True)
            for part, d in ((0, d0), (1, d1)):
                rows = pl.ds(t + HALF * part, HALF)
                l = X[ci, rows, :]
                X[ci, rows, :] = jnp.where(low, l, jnp.broadcast_to(d, l.shape))
            return carry

        lax.fori_loop(0, HOMES, facts, 0)

        def turned(v):
            w = v.T
            return jnp.concatenate([w[0:1, :], w[HD : HD + 1, :]], 0)

        def prepare_d(i, carry):
            c, t = i // 12, pl.multiple_of(lax.rem(i, 12) * 128, 128)
            rows = pl.ds(t, 128)
            dc[c, rows, :] = query_quads(df[c, rows, :])
            lt[i] = turned(X[c, rows, :])
            return carry

        lax.fori_loop(0, 24, prepare_d, 0)
        for blk in range(4):
            r = slice(128 * blk, 128 * blk + 128)
            rows = pl.ds(qv4 + 384 * blk, 128, stride=3)
            d4[r, :] = query_quads(df[qi4, rows, :])
            lt4[blk] = turned(X[qi4, rows, :])
            rows = pl.ds(kv5 + 384 * blk, 128, stride=3)
            d5[r, :] = query_quads(df[qi5, rows, :])
            lt5[blk] = turned(X[qi5, rows, :])
        dv[...] = jnp.zeros_like(dv)
        dq[...] = jnp.zeros_like(dq)

    def tile(k, v, kT, q, d, facts_pair, bias):
        s_ = dot_nt(doubled(k), q) + bias
        l0, l1 = facts_pair
        row = jnp.concatenate([l0[0:1, :], l1[0:1, :]], 1)
        delta = jnp.concatenate([l0[1:2, :], l1[1:2, :]], 1)
        pr = jnp.exp(s_ - row)
        ds = pr * (dot_nt(doubled(v), d) - delta)
        hi, lo = split(pr)
        d2, q2_ = d[:, :128], q[:, :128]
        dv_new = dot_nn(jnp.concatenate([hi, lo], 1), jnp.concatenate([d2, d2], 0))
        hi, lo = split(ds)
        dk_new = dot_nn(jnp.concatenate([hi, lo], 1), jnp.concatenate([q2_, q2_], 0))
        dqt[...] += dot_nn(doubled(kT), jnp.concatenate([hi, lo], 0))
        return dk_new, dv_new

    def kept(flag, v):
        return jnp.where(flag, v, 0.0)

    def at256(blk):
        return pl.ds(pl.multiple_of(256 * blk, 128), 256)

    def sweep(first, last, step, done):
        dqt[...] = jnp.zeros_like(dqt)

        def one(kb, carry):
            step(kb, jnp.where(kb == last, 0, 1))
            return carry

        lax.fori_loop(first, last + 1, one, 0)
        done(dqt[...].T)

    def q2(qb, carry):
        qs = at256(qb)

        def step(kb, which):
            ks = at256(kb)
            a, c = tile(
                jnp.concatenate([kc[o2, ks, :], kc[o2 + 2, ks, :]], 0),
                jnp.concatenate([vc[o2, ks, :], vc[o2 + 2, ks, :]], 0),
                jnp.concatenate([kt[o2, :, ks], kt[o2 + 2, :, ks]], 1),
                qc[o2, qs, :],
                dc[o2, qs, :],
                (lt.at[12 * o2 + 2 * qb], lt.at[12 * o2 + 2 * qb + 1]),
                b2[which],
            )
            for par in range(2):
                f = o2 == par
                dk[par, ks, :] += kept(f, a[:256])
                dk[par + 2, ks, :] += kept(f, a[256:])
                dv[par, ks, :] += kept(f, c[:256])
                dv[par + 2, ks, :] += kept(f, c[256:])

        def done(e):
            for par in range(2):
                dq[par, qs, :] += kept(o2 == par, e)

        sweep(jnp.where(qb >= 4, 4, 0), qb, step, done)
        return carry

    @pl.when(active)
    def _():
        lax.fori_loop(0, TOTAL // 256, q2, 0)

    reduction((3, 0), (2, 2), (3, 1), (1, 4))

    def q3(qb, carry):
        ci = lax.rem(o3, 2)
        qs = at256(qb)

        def step(kb, which):
            ks = at256(kb)
            a, c = tile(
                kc[o3, ks, :],
                vc[o3, ks, :],
                kt[o3, :, ks],
                qc[ci, qs, :],
                dc[ci, qs, :],
                (lt.at[12 * ci + 2 * qb], lt.at[12 * ci + 2 * qb + 1]),
                b3[which],
            )
            for i in range(2):
                f = o3 == 2 * b + i
                dk[2 * b + i, ks, :] += kept(f, a)
                dv[2 * b + i, ks, :] += kept(f, c)

        def done(e):
            for i in range(2):
                dq[i, qs, :] += kept(o3 == 2 * b + i, e)

        sweep(0, qb, step, done)
        return carry

    def q4_(qb, carry):
        qs = at256(qb)

        def step(kb, which):
            ks = at256(kb)
            a, c = tile(
                k4[:, ks, :].reshape(512, 128),
                v4[:, ks, :].reshape(512, 128),
                jnp.concatenate([kt4[0, :, ks], kt4[1, :, ks]], 1),
                q4[qs, :],
                d4[qs, :],
                (lt4.at[2 * qb], lt4.at[2 * qb + 1]),
                b4[which],
            )
            dk4[:, ks, :] += a.reshape(2, 256, 128)
            dv4[:, ks, :] += c.reshape(2, 256, 128)

        def done(e):
            dq4[qs, :] = e

        sweep(0, qb, step, done)
        return carry

    def q5_(qb, carry):
        qs = at256(qb)

        def step(kb, which):
            ks = at256(kb)
            a, c = tile(
                k5[ks, :], v5[ks, :], kt5[:, ks], q5[qs, :], d5[qs, :], (lt5.at[2 * qb], lt5.at[2 * qb + 1]), b3[which]
            )
            dk5[ks, :] += a
            dv5[ks, :] += c

        def done(e):
            dq5[qs, :] = e

        sweep(0, qb, step, done)
        return carry

    @pl.when(active)
    def _():
        lax.fori_loop(0, TOTAL // 256, q3, 0)
        for ref in (dk4, dv4, dk5, dv5):
            ref[...] = jnp.zeros_like(ref)
        lax.fori_loop(0, 2, q4_, 0)
        lax.fori_loop(0, 2, q5_, 0)
        mine5 = kc5 // 2 == b
        for kind in range(12):
            c, rows = kind % 4, pl.ds(kind // 4, THIRD, stride=3)
            f0, f1, f5 = o4 == kind, o4 + 6 == kind, jnp.logical_and(o5 == kind, mine5)
            dk[c, rows, :] += kept(f0, dk4[0]) + kept(f1, dk4[1]) + kept(f5, dk5[...])
            dv[c, rows, :] += kept(f0, dv4[0]) + kept(f1, dv4[1]) + kept(f5, dv5[...])
        for ci in range(2):
            for v in range(3):
                rows = pl.ds(v, THIRD, stride=3)
                f4 = jnp.logical_and(qi4 == ci, qv4 == v)
                f5 = jnp.logical_and(jnp.logical_and(qi5 == ci, kv5 == v), mine5)
                dq[ci, rows, :] += kept(f4, dq4[...]) + kept(f5, dq5[...])

    reduction((4, 0), (4, 1), (2, 3), (3, 2))

    def segment(g):
        def at(blk):
            return pl.ds(pl.multiple_of(512 * g + 128 * blk, 128), 128)

        def one(qb, carry):
            qs = at(qb)

            def step(kb, which):
                ks = at(kb)
                a, c = tile(
                    kc[:, ks, :].reshape(512, 128),
                    vc[:, ks, :].reshape(512, 128),
                    jnp.concatenate([kt[i, :, ks] for i in range(4)], 1),
                    qc[:, qs, :].reshape(256, 256),
                    dc[:, qs, :].reshape(256, 256),
                    (lt.at[4 * g + qb], lt.at[12 + 4 * g + qb]),
                    b1[which],
                )
                dk[:, ks, :] += a.reshape(4, 128, 128)
                dv[:, ks, :] += c.reshape(4, 128, 128)

            def done(e):
                dq[:, qs, :] += e.reshape(2, 128, 128)

            sweep(0, qb, step, done)
            return carry

        lax.fori_loop(0, 4, one, 0)

    def passed(m):
        return remote(ds_out.at[m], came.at[m], fsend.at[m], frecv.at[m], place.peer)

    def home_copies(m):
        q, t = home_device(core, m)
        kv = remote(came.at[m], grec.at[head, pl.ds(0, ROWS), :], send.at[m], recv.at[head], to(q, t))
        dq_ = remote(dqp.at[m], grec.at[head, pl.ds(ROWS, HALF), :], qsend.at[m], qrecv.at[head], to(q, t))
        return q, t, kv, dq_

    def rows_of(m):
        return pl.ds(pl.multiple_of((m // 2) * ROWS, 64), ROWS)

    def kv(c, m):
        k, v = dk[c, rows_of(m), :], dv[c, rows_of(m), :]
        return pick(k + swap(k), v + swap(v))

    def share(m, carry):
        ds_out[m] = kv(2 * (1 - b) + lax.rem(m, 2), m)
        passed(m).start()
        return carry

    def add(m, carry):
        q, t, far_kv, far_q = home_copies(m)
        ci = lax.rem(m, 2)
        v = dq[ci, rows_of(m), :]
        v = (v + swap(v)) * (1.0 / math.sqrt(HD))
        dqp[m] = pick(v[:HALF], v[HALF:])
        passed(m).wait_recv()
        came[m] += kv(2 * b + ci, m)

        @pl.when(same(p, s, q, t))
        def _():
            pltpu.make_async_copy(came.at[m], grec.at[head, pl.ds(0, ROWS), :], recv.at[head]).start()
            pltpu.make_async_copy(dqp.at[m], grec.at[head, pl.ds(ROWS, HALF), :], qrecv.at[head]).start()

        @pl.when(jnp.logical_not(same(p, s, q, t)))
        def _():
            far_kv.start()
            far_q.start()

        return carry

    def round_of(i, carry):
        g = jnp.where(i == 0, 0, 3 - i)

        @pl.when(active)
        def _():
            segment(g)
            lax.fori_loop(jnp.where(i == 0, 0, jnp.where(i == 1, 12, 4)), jnp.where(i == 0, 4, jnp.where(i == 1, 16, 12)), share, 0)

            @pl.when(i > 0)
            def _():
                lax.fori_loop(jnp.where(i == 1, 0, 12), jnp.where(i == 1, 4, 16), add, 0)

        @pl.when(i == 1)
        def _():
            reduction((5, 0), (5, 1), (2, 4), (3, 3), (4, 2))

        return carry

    lax.fori_loop(0, 3, round_of, 0)

    @pl.when(active)
    def _():
        lax.fori_loop(4, 12, add, 0)

    reduction((6, 0), (6, 1), (3, 4), (4, 3), (5, 2))
    reduction((4, 4), (5, 3), (6, 2))
    reduction((5, 4), (6, 3))
    reduction((6, 4))

    def from_head(h, carry):
        a = grec.at[h, pl.ds(0, ROWS), :]
        c = grec.at[h, pl.ds(ROWS, HALF), :]
        pltpu.make_async_copy(a, a, recv.at[h]).wait()
        pltpu.make_async_copy(c, c, qrecv.at[h]).wait()
        return carry

    lax.fori_loop(0, HEADS, from_head, 0)
    for k in range(N_FF):
        if k < N_COLS:
            chunk(k).one().wait_send()
        chunk(k).two().wait_send()
        chunk(k).line_sent()

    @pl.when(active)
    def _():
        def sent(m, carry):
            q, t, far_kv, far_q = home_copies(m)
            passed(m).wait_send()

            @pl.when(jnp.logical_not(same(p, s, q, t)))
            def _():
                far_kv.wait_send()
                far_q.wait_send()

            return carry

        lax.fori_loop(0, HOMES, sent, 0)


def backward_all(offs, drec, own, sib, ap, lse, C0, C1a, C1b, cid):
    dma = pltpu.SemaphoreType.DMA
    keys = pltpu.VMEM((4, TOTAL, 128), BF16)
    full = pltpu.VMEM((4, TOTAL, 128), F32)
    quad = pltpu.VMEM((2, TOTAL, 256), BF16)
    quad3 = pltpu.VMEM((THIRD, 256), BF16)
    pair3 = pltpu.VMEM((THIRD, 128), BF16)
    turned = pltpu.VMEM((128, THIRD), BF16)
    facts3 = pltpu.VMEM((4, 2, 128), F32)
    out3 = pltpu.VMEM((THIRD, 128), F32)
    packs = pltpu.VMEM((HOMES, ROWS, 128), F32)
    halves = pltpu.VMEM((HOMES, HALF, 128), F32)
    return pl.pallas_call(
        back_all_kernel,
        out_shape=[
            jax.ShapeDtypeStruct((HEADS, PACK, 128), F32),
            jax.ShapeDtypeStruct((PIECE, D), F32),
            jax.ShapeDtypeStruct((PIECE, FF), F32),
            jax.ShapeDtypeStruct((4 * PIECE, D), F32),
        ],
        in_specs=[SM, VM, ANY, ANY, VM, ANY, ANY, ANY, ANY],
        out_specs=[ANY, VM, VM, VM],
        scratch_shapes=[
            halves,
            keys,
            keys,
            pltpu.VMEM((4, 128, TOTAL), BF16),
            quad,
            quad,
            pltpu.VMEM((24, 2, 128), F32),
            pltpu.VMEM((2, THIRD, 128), BF16),
            pltpu.VMEM((2, THIRD, 128), BF16),
            pltpu.VMEM((2, 128, THIRD), BF16),
            quad3,
            quad3,
            facts3,
            pair3,
            pair3,
            turned,
            quad3,
            quad3,
            facts3,
            full,
            full,
            pltpu.VMEM((2, TOTAL, 128), F32),
            pltpu.VMEM((2, THIRD, 128), F32),
            pltpu.VMEM((2, THIRD, 128), F32),
            out3,
            out3,
            out3,
            out3,
            pltpu.VMEM((2, 512, 256), F32),
            pltpu.VMEM((2, 512, 256), F32),
            pltpu.VMEM((2, 256, 256), F32),
            pltpu.VMEM((2, 512, 256), F32),
            pltpu.VMEM((128, 256), F32),
            packs,
            packs,
            dma((HOMES + 1, 3)),
            dma((HOMES,)),
            dma((HEADS,)),
            dma((HOMES,)),
            dma((HEADS,)),
            dma((HOMES,)),
            dma((HOMES,)),
            pltpu.VMEM((N_COLS, 2, 4, 2, PIECE, D), F32),
            pltpu.VMEM((5, 4, 2, PIECE, D), F32),
            pltpu.VMEM((4, 2, 4, PIECE, D), F32),
            pltpu.VMEM((N_FF, 4, PIECE, D), F32),
            pltpu.VMEM((N_FF, 4, PIECE, D), F32),
            pltpu.VMEM((N_FF, 4, PIECE, D), F32),
            dma((N_FF,)),
        ]
        + Sems.scratch(N_FF),
        compiler_params=params(collective_id=cid, has_side_effects=True),
    )(offs, drec, own, sib, ap, lse, C0, C1a, C1b)


SEG1, SEG2, SEG3, SEG4, SEG5 = SEGMENTS
DILATION_ONE, DILATION_TWO, DILATION_THREE, DILATION_FOUR, DILATION_FIVE = DILATIONS
MASK_VALUE = -1e30
MATMUL_ACCURACY = lax.Precision.HIGHEST


def passed_along(value, axis, by):
    length = lax.axis_size(axis)
    return lax.ppermute(value, axis, [(i, (i + by) % length) for i in range(length)])


def run_is_live(distance, anchor_point, sequence_width, segment_length):
    return (anchor_point - (distance - 1) * sequence_width - 1) // segment_length == anchor_point // segment_length


def layer_norm(x, gain_vec):
    average = jnp.mean(x, -1, keepdims=True)
    centred = x - average
    variance = jnp.mean(centred * centred, -1, keepdims=True)
    return centred * lax.rsqrt(variance + LN_EPSILON) * gain_vec


def select_table(offsets_row, dilation_rate):
    return (jnp.arange(dilation_rate, dtype=jnp.int32)[:, None] == offsets_row[None, :]).astype(
        jnp.float32
    )


def spread_apart(x, select_option, dilation_rate):
    shaped = x.reshape(x.shape[0] // dilation_rate, dilation_rate, x.shape[1], x.shape[2])
    return jnp.einsum("trhd,rh->thd", shaped, select_option, precision=MATMUL_ACCURACY)


def spread_scalar_rows(x, select_option, dilation_rate):
    shaped = x.reshape(x.shape[0] // dilation_rate, dilation_rate, x.shape[1])
    return jnp.einsum("trh,rh->th", shaped, select_option, precision=MATMUL_ACCURACY)


def spread_rows(x, select_option):
    return jnp.einsum("thd,rh->trhd", x, select_option, precision=MATMUL_ACCURACY).reshape(
        -1, x.shape[1], x.shape[2]
    )


def spread_scalars(x, select_option):
    return jnp.einsum("th,rh->trh", x, select_option, precision=MATMUL_ACCURACY).reshape(
        -1, x.shape[1]
    )


def masked_score_matrix(sparse_queries, key_portion, query_position, key_position, segment_length):
    score_matrix = jnp.einsum(
        "ozt,bzt->zob", sparse_queries, key_portion, precision=MATMUL_ACCURACY
    ) * (1.0 / math.sqrt(key_portion.shape[-1]))
    q_cols = query_position.T[:, :, None]
    k_cols = key_position.T[:, None, :]
    permitted_mask = (k_cols <= q_cols) & (k_cols // segment_length == q_cols // segment_length)
    return (jnp.where(permitted_mask, score_matrix, MASK_VALUE), permitted_mask)


def prepare_pattern(
    query_sequence, key_sequence, value_sequence, offsets_row, dilation_rate, anchor_point
):
    select_option = select_table(offsets_row, dilation_rate)
    sparse_queries = spread_apart(query_sequence, select_option, dilation_rate)
    sparse_key_value = jnp.stack(
        (
            spread_apart(key_sequence, select_option, dilation_rate),
            spread_apart(value_sequence, select_option, dilation_rate),
        )
    )
    query_position = (
        anchor_point
        + jnp.arange(sparse_queries.shape[0], dtype=jnp.int32)[:, None] * dilation_rate
        + offsets_row[None, :]
    )
    return (select_option, sparse_queries, sparse_key_value, query_position)


def pattern_forward_pass(
    sparse_queries,
    sparse_key_value,
    query_position,
    reach,
    segment_length,
    anchor_point,
    sequence_width,
):
    masked_logits, permitted_mask = masked_score_matrix(
        sparse_queries, sparse_key_value[0], query_position, query_position, segment_length
    )
    row_max = jnp.max(masked_logits, -1)
    softmax_weights = jnp.where(permitted_mask, jnp.exp(masked_logits - row_max[..., None]), 0.0)
    state = (
        row_max,
        jnp.sum(softmax_weights, -1),
        jnp.einsum("tlj,jtb->tlb", softmax_weights, sparse_key_value[1], precision=MATMUL_ACCURACY),
    )

    def one_run(distance, carry):
        remote_key_value, state = carry
        remote_key_value = passed_along(remote_key_value, "seq", 1)
        key_position = query_position - distance * sequence_width

        def update(state_in):
            old_max, old_sum, old_acc = state_in
            masked_remote, permitted_remote = masked_score_matrix(
                sparse_queries, remote_key_value[0], query_position, key_position, segment_length
            )
            new_max = jnp.maximum(old_max, jnp.max(masked_remote, -1))
            weights_far = jnp.where(
                permitted_remote, jnp.exp(masked_remote - new_max[..., None]), 0.0
            )
            factor = jnp.exp(old_max - new_max)
            added = jnp.einsum(
                "tlj,jtb->tlb", weights_far, remote_key_value[1], precision=MATMUL_ACCURACY
            )
            return (
                new_max,
                old_sum * factor + jnp.sum(weights_far, -1),
                old_acc * factor[..., None] + added,
            )

        def unchanged(state_in):
            return state_in

        is_live = run_is_live(distance, anchor_point, sequence_width, segment_length)
        return remote_key_value, lax.cond(is_live, update, unchanged, state)

    state = lax.fori_loop(1, reach + 1, one_run, (sparse_key_value, state))[1]
    row_max, row_sum, accumulated = state
    mixture = jnp.transpose(accumulated / row_sum[..., None], (1, 0, 2))
    log_sum = (row_max + jnp.log(row_sum)).T
    return (mixture, log_sum)


def merge_patterns(forwards, prepared_inputs):
    full_lse = []
    full_mix = []
    for pattern_spec in range(len(forwards)):
        mixture, log_sum = forwards[pattern_spec]
        select_option = prepared_inputs[pattern_spec][0]
        covered = spread_scalars(jnp.ones_like(log_sum), select_option)
        full_lse.append(spread_scalars(log_sum, select_option) + (covered - 1.0) * 1e30)
        full_mix.append(spread_rows(mixture, select_option))
    stacked = jnp.stack(full_lse)
    row_max = jnp.max(stacked, 0)
    softmax_weights = jnp.exp(stacked - row_max)
    row_sum = jnp.sum(softmax_weights, 0)
    attended = full_mix[0] * softmax_weights[0][..., None]
    for pattern_spec in range(1, len(full_mix)):
        attended = attended + full_mix[pattern_spec] * softmax_weights[pattern_spec][..., None]
    return (attended / row_sum[..., None], row_max + jnp.log(row_sum))


def pattern_backward(
    select_option,
    dilation_rate,
    segment_length,
    anchor_point,
    sparse_queries,
    sparse_key_value,
    query_position,
    reach,
    sequence_gradient,
    row_difference,
    combined_logsumexp,
):
    sequence_width = sequence_gradient.shape[0]
    sparse_gradient = spread_apart(sequence_gradient, select_option, dilation_rate)
    sparse_output_grad = spread_scalar_rows(row_difference, select_option, dilation_rate).T
    sparse_logsumexp = spread_scalar_rows(combined_logsumexp, select_option, dilation_rate).T
    inverse_square_root = 1.0 / math.sqrt(sparse_queries.shape[-1])

    def portion_gradients(key_portion, value_portion, key_position):
        masked_logits, permitted_mask = masked_score_matrix(
            sparse_queries, key_portion, query_position, key_position, segment_length
        )
        softmax_weights = jnp.where(
            permitted_mask, jnp.exp(masked_logits - sparse_logsumexp[..., None]), 0.0
        )
        value_gradient = jnp.einsum(
            "tui,utx->itx", softmax_weights, sparse_gradient, precision=MATMUL_ACCURACY
        )
        pattern_gradient = jnp.einsum(
            "ozt,bzt->zob", sparse_gradient, value_portion, precision=MATMUL_ACCURACY
        )
        score_gradient = (
            softmax_weights
            * (pattern_gradient - sparse_output_grad[..., None])
            * inverse_square_root
        )
        query_gradient = jnp.einsum(
            "hqk,khd->qhd", score_gradient, key_portion, precision=MATMUL_ACCURACY
        )
        key_gradient = jnp.einsum(
            "tui,utx->itx", score_gradient, sparse_queries, precision=MATMUL_ACCURACY
        )
        return (query_gradient, jnp.stack((key_gradient, value_gradient)))

    query_gradient, key_value_gradient = portion_gradients(
        sparse_key_value[0], sparse_key_value[1], query_position
    )

    def one_run(distance, carry):
        remote_key_value, remote_gradient, query_sum = carry
        remote_key_value = passed_along(remote_key_value, "seq", 1)
        remote_gradient = passed_along(remote_gradient, "seq", 1)
        key_position = query_position - distance * sequence_width

        def far_grads():
            part_q, part_kv = portion_gradients(remote_key_value[0], remote_key_value[1], key_position)
            return query_sum + part_q, remote_gradient + part_kv

        def no_grads():
            return query_sum, remote_gradient

        is_live = run_is_live(distance, anchor_point, sequence_width, segment_length)
        query_sum, remote_gradient = lax.cond(is_live, far_grads, no_grads)
        return remote_key_value, remote_gradient, query_sum

    _, travelled, query_gradient = lax.fori_loop(
        1, reach + 1, one_run, (sparse_key_value, key_value_gradient, query_gradient)
    )
    return (query_gradient, passed_along(travelled, "seq", -reach))


def front_part(own_rows, w_qkv, gain_attn):
    return jnp.dot(layer_norm(own_rows, gain_attn), w_qkv, precision=MATMUL_ACCURACY)


def after_part(attn_rows, own_rows, w_out, w_up, w_down, gain_inner, gain_ffn, gain_hidden):
    residual = own_rows + jnp.dot(
        layer_norm(attn_rows, gain_inner), w_out, precision=MATMUL_ACCURACY
    )
    hidden = jax.nn.gelu(
        jnp.dot(layer_norm(residual, gain_ffn), w_up, precision=MATMUL_ACCURACY), approximate=False
    )
    return residual + jnp.dot(layer_norm(hidden, gain_hidden), w_down, precision=MATMUL_ACCURACY)


def shards(
    tokens,
    w_qkv,
    w_out,
    w_up,
    w_down,
    gain_attn,
    gain_inner,
    gain_ffn,
    gain_hidden,
    offsets,
    grad_out,
):
    w_qkv = w_qkv.astype(jnp.float32)
    w_out = w_out.astype(jnp.float32)
    w_up = w_up.astype(jnp.float32)
    w_down = w_down.astype(jnp.float32)
    groups = lax.axis_size("pat")
    local_rows = tokens.shape[0]
    sequence_width = local_rows * groups
    heads_here = HEADS // groups
    own_rows = tokens.reshape(local_rows, D)
    qkv_rows, front_back = jax.vjp(front_part, own_rows, w_qkv, gain_attn)
    gathered_qkv = lax.all_to_all(
        qkv_rows.reshape(local_rows, 1, 3, HEADS, HD),
        "pat",
        split_axis=3,
        concat_axis=1,
        tiled=True,
    )
    gathered_qkv = gathered_qkv.reshape(sequence_width, 3, heads_here, HD)
    head_offsets = lax.dynamic_slice_in_dim(
        offsets, lax.axis_index("pat") * heads_here, heads_here, 1
    )
    anchor_point = lax.axis_index("seq") * sequence_width
    dilation_rates = (DILATION_ONE, DILATION_TWO, DILATION_THREE, DILATION_FOUR, DILATION_FIVE)
    segment_lengths = (SEG1, SEG2, SEG3, SEG4, SEG5)
    reaches = [
        min((segment_lengths[pattern_spec] - 2) // sequence_width + 1, lax.axis_size("seq") - 1)
        for pattern_spec in range(PATTERNS)
    ]
    prepared_inputs = []
    for pattern_spec in range(PATTERNS):
        prepared_inputs.append(
            prepare_pattern(
                gathered_qkv[:, 0],
                gathered_qkv[:, 1],
                gathered_qkv[:, 2],
                head_offsets[pattern_spec],
                dilation_rates[pattern_spec],
                anchor_point,
            )
        )
    forwards = []
    for pattern_spec in range(PATTERNS):
        select_option, sparse_queries, sparse_key_value, query_position = prepared_inputs[
            pattern_spec
        ]
        forwards.append(
            pattern_forward_pass(
                sparse_queries,
                sparse_key_value,
                query_position,
                reaches[pattern_spec],
                segment_lengths[pattern_spec],
                anchor_point,
                sequence_width,
            )
        )
    lse_sums = jnp.stack([jnp.sum(entry[1]) for entry in forwards])
    totals = lax.psum(lse_sums, ("pat", "seq"))
    full_length = sequence_width * lax.axis_size("seq")
    counts = jnp.array(
        [
            float(full_length // dilation_rates[pattern_spec] * HEADS)
            for pattern_spec in range(PATTERNS)
        ],
        jnp.float32,
    )
    log_means = totals / counts
    attended, combined_logsumexp = merge_patterns(forwards, prepared_inputs)
    returned_rows = lax.all_to_all(
        attended.reshape(local_rows, groups, heads_here, HD),
        "pat",
        split_axis=1,
        concat_axis=2,
        tiled=True,
    )
    attn_rows = returned_rows.reshape(local_rows, D)
    result, after_back = jax.vjp(
        after_part, attn_rows, own_rows, w_out, w_up, w_down, gain_inner, gain_ffn, gain_hidden
    )
    g_attn, g_resid, g_out, g_up, g_down, g_inner, g_ffn, g_hidden = after_back(
        grad_out.reshape(local_rows, D)
    )
    sequence_gradient = lax.all_to_all(
        g_attn.reshape(local_rows, 1, HEADS, HD), "pat", split_axis=2, concat_axis=1, tiled=True
    )
    sequence_gradient = sequence_gradient.reshape(sequence_width, heads_here, HD)
    row_difference = jnp.sum(sequence_gradient * attended, -1)
    q_grads = []
    kv_grads = []
    for pattern_spec in range(PATTERNS):
        select_option, sparse_queries, sparse_key_value, query_position = prepared_inputs[
            pattern_spec
        ]
        part_q, part_kv = pattern_backward(
            select_option,
            dilation_rates[pattern_spec],
            segment_lengths[pattern_spec],
            anchor_point,
            sparse_queries,
            sparse_key_value,
            query_position,
            reaches[pattern_spec],
            sequence_gradient,
            row_difference,
            combined_logsumexp,
        )
        q_grads.append(part_q)
        kv_grads.append(part_kv)
    grad_total = jnp.zeros((sequence_width, 3, heads_here, HD), jnp.float32)
    for pattern_spec in range(PATTERNS):
        select_option = prepared_inputs[pattern_spec][0]
        grad_total = grad_total + jnp.stack(
            (
                spread_rows(q_grads[pattern_spec], select_option),
                spread_rows(kv_grads[pattern_spec][0], select_option),
                spread_rows(kv_grads[pattern_spec][1], select_option),
            ),
            1,
        )
    grad_back = lax.all_to_all(
        grad_total.reshape(local_rows, groups, 3, heads_here, HD),
        "pat",
        split_axis=1,
        concat_axis=3,
        tiled=True,
    )
    g_tokens, g_qkv, g_attn_gain = front_back(grad_back.reshape(local_rows, 3 * D))
    grad_tokens = (g_resid + g_tokens).reshape(local_rows, 1, D)
    summed = (
        lax.psum_scatter(g_qkv, ("pat", "seq"), scatter_dimension=0, tiled=True),
        lax.psum_scatter(g_out, ("pat", "seq"), scatter_dimension=0, tiled=True),
        lax.psum_scatter(g_up, ("pat", "seq"), scatter_dimension=0, tiled=True),
        lax.psum_scatter(g_down, ("pat", "seq"), scatter_dimension=0, tiled=True),
        lax.psum_scatter(g_attn_gain, ("pat", "seq"), scatter_dimension=0, tiled=True),
        lax.psum_scatter(g_inner, ("pat", "seq"), scatter_dimension=0, tiled=True),
        lax.psum_scatter(g_ffn, ("pat", "seq"), scatter_dimension=0, tiled=True),
        lax.psum_scatter(g_hidden, ("pat", "seq"), scatter_dimension=0, tiled=True),
    )
    return (
        result.reshape(local_rows, 1, D),
        grad_tokens,
        summed[0],
        summed[1],
        summed[2],
        summed[3],
        summed[4],
        summed[5],
        summed[6],
        summed[7],
        log_means,
    )


def fast_shards(tokens, w_qkv, w_out, w_up, w_down, gain_attn, gain_inner, gain_ffn, gain_hidden, offsets, grad_out):
    p, s = lax.axis_index("pat"), lax.axis_index("seq")
    active, head = head_here(p, s)
    mine = lax.dynamic_slice_in_dim(offsets, head, 1, 1)[:, 0]
    info = jnp.concatenate([jnp.stack([active.astype(jnp.int32), lax.rem(p, 2).astype(jnp.int32)]), mine])

    counts = [float(TOTAL * 4 // r * HEADS) for r in DILATIONS]
    pk, x = front(tokens, w_qkv, gain_attn)
    own, sib = to_heads(pk, True, 0)
    ap, lse, sums = attention_forward(info, own, sib)
    rec = to_homes(ap, 1)
    mixed, drec, dy1, S, C0, C1a, C1b = feed_forward(
        rec, x, grad_out, w_out, w_up, w_down, gain_inner, gain_ffn, gain_hidden, sums
    )
    grec, g_out, g_up, g_down = backward_all(mine, drec, own, sib, ap, lse, C0, C1a, C1b, 2)
    gx, g_qkv, *small = finish(grec, x, dy1, w_qkv, gain_attn, S, counts, 3)
    mixed, gx, g_qkv, g_out, g_up, g_down, *small = deliver(mixed, gx, g_qkv, g_out, g_up, g_down, *small)
    return (mixed, gx, g_qkv, g_out, g_up, g_down, *(v.reshape(-1) for v in small))


def fits(mesh):
    return mesh.shape["pat"] == 4 and mesh.shape["seq"] == RUNS


def solution(mesh):
    rows = P("seq", "pat", None)
    split_rows = P(("pat", "seq"), None)
    split_one = P(("pat", "seq"))
    planned = jax.shard_map(
        fast_shards,
        mesh=mesh,
        in_specs=(rows,) + (P(),) * 9 + (rows,),
        out_specs=(rows, rows) + (split_rows,) * 4 + (split_one,) * 4 + (P(),),
        check_vma=False,
    )
    general = jax.shard_map(
        shards,
        mesh=mesh,
        in_specs=(rows,) + (P(),) * 9 + (rows,),
        out_specs=(rows, rows) + (split_rows,) * 4 + (split_one,) * 4 + (P(),),
        check_vma=False,
    )

    def layer(tokens, *rest):
        if fits(mesh) and tokens.shape[0] == TOTAL:
            return planned(tokens, *rest)
        return general(tokens, *rest)

    return layer
```

```python
import functools
import math

import jax
import jax.numpy as jnp
from jax import lax
from jax.experimental import pallas as pl
from jax.experimental.pallas import tpu as pltpu
from jax.sharding import PartitionSpec as P

D = 768
HEADS = 12
HD = 64
FF = 3072
PATTERNS = 5
SEGMENTS = (2048, 4096, 8192, 16384, 32768)
DILATIONS = (1, 2, 4, 6, 12)
LN_EPSILON = 1e-05
NEG = -1e30
F32 = jnp.float32
BF16 = jnp.bfloat16
HIGHEST = lax.Precision.HIGHEST
VMEM_LIMIT = 60 * 1024 * 1024

ROWS = 192
HALF = ROWS // 2
RUNS = 8
TOTAL = ROWS * RUNS
PACK = ROWS + HALF
HOMES = 16
THIRD = TOTAL // 3
PIECE = 24
MESH = pl.DeviceIdType.MESH


def dot_nn(a, b):
    return lax.dot_general(a, b, (((1,), (0,)), ((), ())), preferred_element_type=F32)


def dot_nt(a, b):
    return lax.dot_general(a, b, (((1,), (1,)), ((), ())), preferred_element_type=F32)


def split(v):
    hi = v.astype(BF16)
    return hi, (v - hi.astype(F32)).astype(BF16)


def split32(v):
    hi = v.astype(BF16).astype(F32)
    return hi, v - hi


def lower_lanes(v):
    return lax.broadcasted_iota(jnp.int32, v.shape, v.ndim - 1) < HD


def swap(v):
    return pltpu.roll(v, HD, v.ndim - 1)


def pick(a, b):
    return jnp.where(lower_lanes(a), a, b)


def head_place(h):
    z = h // 3
    column = lax.rem(lax.rem(h, 3) + z + 1, 4)
    return column // 2, z * 2 + lax.rem(column, 2)


def head_here(p, s):
    z = s // 2
    column = (p // 2) * 2 + lax.rem(s, 2)
    k = lax.rem(column - z + 7, 4)
    return k < 3, z * 3 + jnp.minimum(k, 2)


def whole(*_):
    return pl.BlockSpec(memory_space=pltpu.VMEM)


VM = pl.BlockSpec(memory_space=pltpu.VMEM)
ANY = pl.BlockSpec(memory_space=pl.ANY)
SM = pl.BlockSpec(memory_space=pltpu.SMEM)


def params(**kw):
    return pltpu.CompilerParams(vmem_limit_bytes=VMEM_LIMIT, **kw)


def normed(v):
    centred = v - jnp.mean(v, -1, keepdims=True)
    rs = lax.rsqrt(jnp.mean(centred * centred, -1, keepdims=True) + LN_EPSILON)
    return centred * rs, rs


def put_split(ref, v):
    hi, lo = split(v)
    n = v.shape[0]
    ref[0:n, :] = hi
    ref[n : 2 * n, :] = lo


def front_kernel(x3, w_ref, gain_ref, pk_ref, x_ref, lhs):
    x = x3[...].reshape(ROWS, D)
    x_ref[...] = x
    n, _ = normed(x)
    put_split(lhs, n * gain_ref[...][None, :])
    for jj in range(3):
        parts = []
        for kind in range(3):
            c0 = kind * D + 256 * jj
            r = dot_nn(lhs[...], w_ref[:, c0 : c0 + 256])
            parts.append(r[:ROWS] + r[ROWS:])
        for half in range(2):
            q, k, v = (a[:, 128 * half : 128 * half + 128] for a in parts)
            h = 4 * jj + 2 * half
            pk_ref[h, 0:ROWS, :] = pick(k, swap(v))
            pk_ref[h + 1, 0:ROWS, :] = pick(swap(k), v)
            top, bottom = q[:HALF], q[HALF:]
            pk_ref[h, ROWS:PACK, :] = pick(top, swap(bottom))
            pk_ref[h + 1, ROWS:PACK, :] = pick(swap(top), bottom)


def front(x, w, gain):
    return pl.pallas_call(
        front_kernel,
        out_shape=[jax.ShapeDtypeStruct((HEADS, PACK, 128), F32)] + [jax.ShapeDtypeStruct((ROWS, D), F32)],
        in_specs=[VM] * 3,
        out_specs=[VM] * 2,
        scratch_shapes=[pltpu.VMEM((2 * ROWS, D), BF16)],
        compiler_params=params(),
    )(x, w, gain)


def place_facts():
    p, s = lax.axis_index("pat"), lax.axis_index("seq")
    x, core = p // 2, lax.rem(p, 2)
    active, head = head_here(p, s)
    return p, s, x, core, active, head


def home_device(core, m):
    return core * 2 + lax.rem(m, 2), m // 2


def head_device(h, b):
    hx, hs = head_place(h)
    return hx * 2 + b, hs


def same(p, s, q, t):
    return jnp.logical_and(p == q, s == t)


def to(p, s):
    return {"pat": p, "seq": s}


def scatter_kernel(forward, pk, own, *rest):
    if forward:
        sib, send, recv, fsend, frecv = rest
    else:
        send, recv = rest
    p, s, x, core, active, head = place_facts()
    slot = s * 2 + core
    barrier = pltpu.get_barrier_semaphore()

    @pl.when(active)
    def _():
        def greet(m, carry):
            q, t = home_device(core, m)

            @pl.when(jnp.logical_not(same(p, s, q, t)))
            def _():
                pl.semaphore_signal(barrier, inc=1, device_id=to(q, t), device_id_type=MESH)

            return carry

        lax.fori_loop(0, HOMES, greet, 0)
        if forward:
            pl.semaphore_signal(barrier, inc=1, device_id=to(x * 2 + 1 - core, s), device_id_type=MESH)

    mine = jnp.logical_and(active, core == x)
    waits = HEADS - mine.astype(jnp.int32)
    if forward:
        waits = waits + active.astype(jnp.int32)
    pl.semaphore_wait(barrier, waits)

    def copy(h):
        q, t = head_device(h, x)
        return q, t, pltpu.make_async_remote_copy(
            src_ref=pk.at[h],
            dst_ref=own.at[slot],
            send_sem=send.at[h],
            recv_sem=recv.at[slot],
            device_id=to(q, t),
            device_id_type=MESH,
        )

    def start(j, carry):
        h = lax.rem(j + 3 * (s // 2) + 2 * p, HEADS)
        q, t, remote = copy(h)

        @pl.when(same(p, s, q, t))
        def _():
            pltpu.make_async_copy(pk.at[h], own.at[slot], recv.at[slot]).start()

        @pl.when(jnp.logical_not(same(p, s, q, t)))
        def _():
            remote.start()

        return carry

    lax.fori_loop(0, HEADS, start, 0)

    def passed(m):
        return pltpu.make_async_remote_copy(
            src_ref=own.at[m, pl.ds(0, ROWS), :],
            dst_ref=sib.at[m],
            send_sem=fsend.at[m],
            recv_sem=frecv.at[m],
            device_id=to(x * 2 + 1 - core, s),
            device_id_type=MESH,
        )

    @pl.when(active)
    def _():
        def arrive(m, carry):
            pltpu.make_async_copy(own.at[m], own.at[m], recv.at[m]).wait()
            if forward:
                passed(m).start()
            return carry

        lax.fori_loop(0, HOMES, arrive, 0)
        if forward:

            def finish(m, carry):
                passed(m).wait()
                return carry

            lax.fori_loop(0, HOMES, finish, 0)

    def sent(h, carry):
        q, t, remote = copy(h)

        @pl.when(jnp.logical_not(same(p, s, q, t)))
        def _():
            remote.wait_send()

        return carry

    lax.fori_loop(0, HEADS, sent, 0)


def to_heads(packets, forward, cid):
    rows = packets.shape[1]
    shapes = [jax.ShapeDtypeStruct((HOMES, rows, 128), F32)]
    sems = [pltpu.SemaphoreType.DMA((HEADS,)), pltpu.SemaphoreType.DMA((HOMES,))]
    if forward:
        shapes.append(jax.ShapeDtypeStruct((HOMES, ROWS, 128), F32))
        sems += [pltpu.SemaphoreType.DMA((HOMES,)), pltpu.SemaphoreType.DMA((HOMES,))]
    return pl.pallas_call(
        functools.partial(scatter_kernel, forward),
        out_shape=shapes,
        in_specs=[ANY],
        out_specs=[ANY] * len(shapes),
        scratch_shapes=sems,
        compiler_params=params(collective_id=cid, has_side_effects=True),
    )(packets)


def home_barrier(p, s, x, core, active, barrier, also_sibling):
    def greet(h, carry):
        q, t = head_device(h, x)

        @pl.when(jnp.logical_not(same(p, s, q, t)))
        def _():
            pl.semaphore_signal(barrier, inc=1, device_id=to(q, t), device_id_type=MESH)

        return carry

    lax.fori_loop(0, HEADS, greet, 0)

    @pl.when(active)
    def _():
        if also_sibling:
            pl.semaphore_signal(barrier, inc=1, device_id=to(x * 2 + 1 - core, s), device_id_type=MESH)
        mine = (core == x).astype(jnp.int32)
        pl.semaphore_wait(barrier, HOMES - mine + (1 if also_sibling else 0))


def gather_kernel(pk, rec, send, recv):
    p, s, x, core, active, head = place_facts()
    barrier = pltpu.get_barrier_semaphore()
    home_barrier(p, s, x, core, active, barrier, False)

    def copy(m):
        q, t = home_device(core, m)
        return q, t, pltpu.make_async_remote_copy(
            src_ref=pk.at[m],
            dst_ref=rec.at[head],
            send_sem=send.at[m],
            recv_sem=recv.at[head],
            device_id=to(q, t),
            device_id_type=MESH,
        )

    @pl.when(active)
    def _():
        def start(j, carry):
            m = lax.rem(j + 2 * s + 1, HOMES)
            q, t, remote = copy(m)

            @pl.when(same(p, s, q, t))
            def _():
                pltpu.make_async_copy(pk.at[m], rec.at[head], recv.at[head]).start()

            @pl.when(jnp.logical_not(same(p, s, q, t)))
            def _():
                remote.start()

            return carry

        lax.fori_loop(0, HOMES, start, 0)

    def arrive(h, carry):
        pltpu.make_async_copy(rec.at[h], rec.at[h], recv.at[h]).wait()
        return carry

    lax.fori_loop(0, HEADS, arrive, 0)

    @pl.when(active)
    def _():
        def sent(m, carry):
            q, t, remote = copy(m)

            @pl.when(jnp.logical_not(same(p, s, q, t)))
            def _():
                remote.wait_send()

            return carry

        lax.fori_loop(0, HOMES, sent, 0)


def to_homes(packets, cid):
    rows = packets.shape[1]
    return pl.pallas_call(
        gather_kernel,
        out_shape=jax.ShapeDtypeStruct((HEADS, rows, 128), F32),
        in_specs=[ANY],
        out_specs=ANY,
        scratch_shapes=[pltpu.SemaphoreType.DMA((HOMES,)), pltpu.SemaphoreType.DMA((HEADS,))],
        compiler_params=params(collective_id=cid, has_side_effects=True),
    )(packets)


def tile_positions(rows, columns, row_classes, column_classes, t_step, class_step):
    r = lax.broadcasted_iota(jnp.int32, (rows, columns), 0)
    q = lax.broadcasted_iota(jnp.int32, (rows, columns), 1)
    rn, qn = rows // row_classes, columns // column_classes
    return (r % rn) * t_step + (r // rn) * class_step, (q % qn) * t_step + (q // qn) * class_step


def key_bias(q_shape, k_shape, t_step, class_step, shift, keys_first):
    nq, nk = q_shape[0] * q_shape[1], k_shape[0] * k_shape[1]
    if keys_first:
        kp, qp = tile_positions(nk, nq, k_shape[0], q_shape[0], t_step, class_step)
    else:
        qp, kp = tile_positions(nq, nk, q_shape[0], k_shape[0], t_step, class_step)
    return jnp.where(kp - qp <= shift, 0.0, NEG).astype(F32)


def unpack_keys(own, sib, b, kvf):
    def one(m, carry):
        c = 2 * b + lax.rem(m, 2)
        d = 2 * (1 - b) + lax.rem(m, 2)
        t = pl.multiple_of((m // 2) * ROWS, 64)
        kvf[c, pl.ds(t, ROWS), :] = own[m, 0:ROWS, :]
        kvf[d, pl.ds(t, ROWS), :] = sib[m]
        return carry

    lax.fori_loop(0, HOMES, one, 0)


def unpack_pairs(src, first, dst, scale):
    def one(m, carry):
        t = pl.multiple_of((m // 2) * ROWS, 32)
        v = src[m, first : first + HALF, :] * scale
        w = swap(v)
        dst[lax.rem(m, 2), pl.ds(t, HALF), :] = pick(v, w)
        dst[lax.rem(m, 2), pl.ds(t + HALF, HALF), :] = pick(w, v)
        return carry

    lax.fori_loop(0, HOMES, one, 0)


def keys_and_values(kv):
    hi, lo = split32(kv)
    k2 = pick(hi, swap(lo))
    v2 = pick(swap(hi), lo)
    return k2, v2


def doubled(v):
    return jnp.concatenate([v, v], 1)


def query_quads(qq):
    hi, lo = split32(qq)
    return jnp.concatenate([pick(hi, lo).astype(BF16), pick(lo, hi).astype(BF16)], 1)


def class_facts4(o4, b):
    keys = ((lax.rem(o4, 4), o4 // 4), (lax.rem(o4 + 6, 4), (o4 + 6) // 4))
    first = (keys[0][0] // 2) == b
    query = (jnp.where(first, keys[0][0], keys[1][0]), jnp.where(first, keys[0][1], keys[1][1]))
    return keys, jnp.where(first, 0, 1), query


def forward_kernel(info, own, sib, ap, lse, sums, kvf, kc, vc, qf, qc, k4, v4, q4, k5, v5, q5, acc, mx, R, b1, b2, b3, b4):
    active = info[0] == 1
    b = info[1]
    offs = [info[2 + i] for i in range(PATTERNS)]
    sums[...] = jnp.zeros_like(sums)

    @pl.when(active)
    def _():
        ones = jnp.ones((128, 128), BF16)
        unpack_keys(own, sib, b, kvf)
        unpack_pairs(own, ROWS, qf, 1.0 / math.sqrt(HD))

        def with_ones(v2):
            return jnp.concatenate([v2.astype(BF16), ones], 1)

        def prepare(i, carry):
            c, t = i // 12, pl.multiple_of(lax.rem(i, 12) * 128, 128)
            k2, v2 = keys_and_values(kvf[c, pl.ds(t, 128), :])
            kc[c, pl.ds(t, 128), :] = k2.astype(BF16)
            vc[c, pl.ds(t, 128), :] = with_ones(v2)
            return carry

        lax.fori_loop(0, 48, prepare, 0, unroll=2)

        def prepare_q(i, carry):
            c, t = i // 12, pl.multiple_of(lax.rem(i, 12) * 128, 128)
            qc[c, pl.ds(t, 128), :] = query_quads(qf[c, pl.ds(t, 128), :])
            return carry

        lax.fori_loop(0, 24, prepare_q, 0, unroll=2)

        keys4, e4, (qc4, qv4) = class_facts4(offs[3], b)
        kc5, kv5 = lax.rem(offs[4], 4), offs[4] // 4
        for blk in range(4):
            r = slice(128 * blk, 128 * blk + 128)
            for e in range(2):
                c, v = keys4[e]
                k2, v2 = keys_and_values(kvf[c, pl.ds(v + 384 * blk, 128, stride=3), :])
                k4[e, r, :] = k2.astype(BF16)
                v4[e, r, :] = with_ones(v2)
            q4[r, :] = query_quads(qf[qc4 - 2 * b, pl.ds(qv4 + 384 * blk, 128, stride=3), :])
            k2, v2 = keys_and_values(kvf[kc5, pl.ds(kv5 + 384 * blk, 128, stride=3), :])
            k5[r, :] = k2.astype(BF16)
            v5[r, :] = with_ones(v2)
            q5[r, :] = query_quads(qf[lax.rem(kc5, 2), pl.ds(kv5 + 384 * blk, 128, stride=3), :])

        b1[...] = key_bias((2, 128), (4, 128), 4, 1, 2 * b, False)
        b2[...] = key_bias((1, 256), (2, 256), 4, 2, 2 * b, False)
        b3[...] = key_bias((1, 512), (1, 512), 1, 1, 0, False)
        b4[...] = key_bias((1, 256), (2, 256), 12, 6, 6 * e4, False)

        def tile(start, q, k, v, bias, classes, first):
            n = q.shape[0]
            each = n // classes
            per = 1536 // classes if classes == 1 else 512
            s = dot_nt(q, doubled(k))
            wide = s.shape[1]
            own_rows = bias.shape[0] // classes
            s = s.reshape(classes, each, wide)
            edge = s[:, :own_rows] + bias[...].reshape(classes, own_rows, wide)
            s = edge if each == own_rows else jnp.concatenate([edge, s[:, own_rows:]], 1)
            s = s.reshape(n, wide)
            top = jnp.max(s, -1, keepdims=True)

            def where(c):
                return pl.ds(c * per + start, each)

            def load(ref):
                return jnp.concatenate([ref[where(c), :] for c in range(classes)], 0)

            def store(ref, value):
                for c in range(classes):
                    ref[where(c), :] = value[c * each : c * each + each]

            if first:
                m = jnp.broadcast_to(top, (n, 128))
            else:
                old = load(mx)
                m = jnp.maximum(old, top)
            p = jnp.exp(s - jnp.concatenate([m] * (wide // 128), 1))
            hi, lo = split(p)
            new = dot_nn(jnp.concatenate([hi, lo], 0), v)
            new = new[:n] + new[n:]
            if not first:
                new = load(acc) * doubled(jnp.exp(old - m)) + new
            store(acc, new)
            store(mx, m)

        def closed(pattern, rows):
            value, m = acc[rows, :], mx[rows, :]
            o, l = value[:, :128], value[:, 128:]
            sums[pattern : pattern + 1, :] += jnp.sum(m + jnp.log(l), 0, keepdims=True)
            lane = lax.broadcasted_iota(jnp.int32, m.shape, 1)
            return jnp.where(lane < HD, o + swap(o), jnp.where(lane < 96, l, m))

        def merge(pattern, ci, rows, of):
            r0, r1 = R[ci, rows, :], closed(pattern, of)
            m0 = jnp.broadcast_to(r0[:, 96:97], r0.shape)
            m1 = jnp.broadcast_to(r1[:, 96:97], r1.shape)
            m = jnp.maximum(m0, m1)
            both = r0 * jnp.exp(m0 - m) + r1 * jnp.exp(m1 - m)
            lane = lax.broadcasted_iota(jnp.int32, r0.shape, 1)
            R[ci, rows, :] = jnp.where(lane < 96, both, m)

        def q1(g, carry):
            base = 512 * g

            def at(t, n):
                return pl.ds(pl.multiple_of(base + t, 128), n)

            for kb in range(4):
                start = 128 * kb
                each = 512 - start
                ks = at(start, 128)
                tile(
                    start,
                    qc[:, at(start, each), :].reshape(2 * each, 256),
                    kc[:, ks, :].reshape(512, 128),
                    vc[:, ks, :].reshape(512, 256),
                    b1,
                    2,
                    kb == 0,
                )
            for c in range(2):
                for i in range(2):
                    R[c, at(256 * i, 256), :] = closed(0, pl.ds(512 * c + 256 * i, 256))
            return carry

        lax.fori_loop(0, 3, q1, 0)

        par = offs[1]
        for base, length in ((0, 1024), (1024, 512)):
            for start in range(0, length, 256):
                ks = slice(base + start, base + start + 256)
                tile(
                    start,
                    qc[par, base + start : base + length, :],
                    jnp.concatenate([kc[par, ks, :], kc[par + 2, ks, :]], 0),
                    jnp.concatenate([vc[par, ks, :], vc[par + 2, ks, :]], 0),
                    b2,
                    1,
                    start == 0,
                )

            def join2(i, carry, base=base):
                t = pl.multiple_of(i * 256, 256)
                merge(1, par, pl.ds(base + t, 256), pl.ds(t, 256))
                return carry

            lax.fori_loop(0, length // 256, join2, 0)

        o3 = offs[2]

        @pl.when(o3 // 2 == b)
        def _():
            ci = lax.rem(o3, 2)
            for start in range(0, TOTAL, 512):
                ks = slice(start, start + 512)
                tile(start, qc[ci, start:TOTAL, :], kc[o3, ks, :], vc[o3, ks, :], b3, 1, start == 0)

            def join3(i, carry):
                t = pl.multiple_of(i * 256, 256)
                merge(2, ci, pl.ds(t, 256), pl.ds(t, 256))
                return carry

            lax.fori_loop(0, TOTAL // 256, join3, 0)

        for start in range(0, THIRD, 256):
            ks = slice(start, start + 256)
            tile(
                start, q4[start:THIRD, :], k4[:, ks, :].reshape(512, 128), v4[:, ks, :].reshape(512, 256), b4, 1, start == 0
            )
        for i in range(2):
            merge(3, qc4 - 2 * b, pl.ds(qv4 + 768 * i, 256, stride=3), pl.ds(256 * i, 256))

        @pl.when(kc5 // 2 == b)
        def _():
            tile(0, q5[...], k5[...], v5[...], b3, 1, True)
            for i in range(2):
                merge(4, lax.rem(kc5, 2), pl.ds(kv5 + 768 * i, 256, stride=3), pl.ds(256 * i, 256))

        def finish(m, carry):
            ci = lax.rem(m, 2)
            rows = pl.ds(pl.multiple_of((m // 2) * ROWS, 64), ROWS)
            r = R[ci, rows, :]
            l = jnp.broadcast_to(r[:, HD : HD + 1], r.shape)
            out = r / l
            ap[m] = pick(out[:HALF], swap(out[HALF:]))
            lse[ci, rows, :] = jnp.broadcast_to(r[:, 96:97], r.shape) + jnp.log(l)
            return carry

        lax.fori_loop(0, HOMES, finish, 0, unroll=2)


def attention_forward(info, own, sib):
    state = pltpu.VMEM((2, TOTAL, 128), F32)
    return pl.pallas_call(
        forward_kernel,
        out_shape=[
            jax.ShapeDtypeStruct((HOMES, HALF, 128), F32),
            jax.ShapeDtypeStruct((2, TOTAL, 128), F32),
            jax.ShapeDtypeStruct((8, 128), F32),
        ],
        in_specs=[SM, VM, VM],
        out_specs=[VM, VM, VM],
        scratch_shapes=[
            pltpu.VMEM((4, TOTAL, 128), F32),
            pltpu.VMEM((4, TOTAL, 128), BF16),
            pltpu.VMEM((4, TOTAL, 256), BF16),
            state,
            pltpu.VMEM((2, TOTAL, 256), BF16),
            pltpu.VMEM((2, THIRD, 128), BF16),
            pltpu.VMEM((2, THIRD, 256), BF16),
            pltpu.VMEM((THIRD, 256), BF16),
            pltpu.VMEM((THIRD, 128), BF16),
            pltpu.VMEM((THIRD, 256), BF16),
            pltpu.VMEM((THIRD, 256), BF16),
            pltpu.VMEM((TOTAL, 256), F32),
            pltpu.VMEM((TOTAL, 128), F32),
            state,
            pltpu.VMEM((256, 512), F32),
            pltpu.VMEM((256, 512), F32),
            pltpu.VMEM((512, 512), F32),
            pltpu.VMEM((256, 512), F32),
        ],
        compiler_params=params(),
    )(info, own, sib)


class Place:
    def __init__(self):
        p, s = lax.axis_index("pat"), lax.axis_index("seq")
        self.p, self.s = p, s
        self.x, self.core, self.z, self.y = p // 2, lax.rem(p, 2), s // 2, lax.rem(s, 2)
        self.peer = to(self.x * 2 + 1 - self.core, s)
        self.xn = to((1 - self.x) * 2 + self.core, s)
        self.yn = to(p, self.z * 2 + 1 - self.y)
        self.left, self.right = to(p, s - 2), to(p, s + 2)

    def greet(self, barrier, line=True):
        for d in (self.peer, self.xn, self.yn):
            pl.semaphore_signal(barrier, inc=1, device_id=d, device_id_type=MESH)
        if not line:
            return 3

        @pl.when(self.z > 0)
        def _():
            pl.semaphore_signal(barrier, inc=1, device_id=self.left, device_id_type=MESH)

        @pl.when(self.z < 3)
        def _():
            pl.semaphore_signal(barrier, inc=1, device_id=self.right, device_id_type=MESH)

        return 3 + (self.z > 0).astype(jnp.int32) + (self.z < 3).astype(jnp.int32)


def remote(src, dst, a, b, d):
    return pltpu.make_async_remote_copy(
        src_ref=src, dst_ref=dst, send_sem=a, recv_sem=b, device_id=d, device_id_type=MESH
    )


def add_in(dst, src):
    lead = dst.shape[:-2]

    def one(i, carry):
        index = []
        for d in reversed(lead):
            index.insert(0, lax.rem(i, d))
            i = i // d
        dst[tuple(index)] += src[tuple(index)]
        return carry

    lax.fori_loop(0, math.prod(lead), one, 0)


class Sems:
    NAMES = ("sc", "rc", "s1", "r1", "s2", "r2", "sl", "rl", "sr", "rr")

    def __init__(self, refs):
        for name, ref in zip(self.NAMES, refs):
            setattr(self, name, ref)

    @staticmethod
    def scratch(n):
        dma = pltpu.SemaphoreType.DMA
        return [dma((n, 2)), dma((n, 2))] + [dma((n,)) for _ in range(8)]


class Chunk:
    def __init__(self, place, k, x_first, sems, b0=None, b1=None, b2=None, bl=None, br=None, part=None, put=None):
        self.at, self.k, self.x_first, self.sems = place, k, x_first, sems
        self.b0, self.b1, self.b2, self.bl, self.br = b0, b1, b2, bl, br
        self.part, self.put = part, put

    def core(self, i):
        k, m = self.k, self.sems
        return remote(self.part(i, 1 - self.at.core), self.b0.at[i], m.sc.at[k, i], m.rc.at[k, i], self.at.peer)

    def one(self):
        k, at, m = self.k, self.at, self.sems
        if self.x_first:
            return remote(self.b0.at[1 - at.x], self.b1, m.s1.at[k], m.r1.at[k], at.xn)
        return remote(self.b0.at[:, :, 1 - at.y], self.b1, m.s1.at[k], m.r1.at[k], at.yn)

    def two(self):
        k, at, m = self.k, self.at, self.sems
        if self.x_first:
            return remote(self.b1.at[:, 1 - at.y], self.b2, m.s2.at[k], m.r2.at[k], at.yn)
        return remote(self.b1.at[1 - at.x], self.b2, m.s2.at[k], m.r2.at[k], at.xn)

    def rightward(self, i):
        k, part, m = self.k, pl.ds(i + 1, 3 - i), self.sems
        src = self.b2 if i == 0 else self.bl
        return remote(src.at[part], self.bl.at[part], m.sr.at[k], m.rl.at[k], self.at.right)

    def leftward(self, i):
        k, part, m = self.k, pl.ds(0, i), self.sems
        src = self.b2 if i == 3 else self.br
        return remote(src.at[part], self.br.at[part], m.sl.at[k], m.rr.at[k], self.at.left)

    def own_core(self, i):
        self.core(i).wait_recv()
        add_in(self.b0.at[i], self.part(i, self.at.core))

    def stage1(self):
        for i in range(2):
            self.own_core(i)
        self.one().start()

    def arrived(self):
        self.one().wait_recv()
        add_in(self.b1, self.b0.at[self.at.x] if self.x_first else self.b0.at[:, :, self.at.y])

    def stage2(self):
        self.arrived()
        self.two().start()

    def stage3(self):
        self.two().wait_recv()
        add_in(self.b2, self.b1.at[:, self.at.y] if self.x_first else self.b1.at[self.at.x])

        @pl.when(self.at.z == 0)
        def _():
            self.rightward(0).start()

        @pl.when(self.at.z == 3)
        def _():
            self.leftward(3).start()

    def stage4(self):
        @pl.when(self.at.z == 1)
        def _():
            self.rightward(0).wait_recv()
            self.bl[2:4] += self.b2[2:4]
            self.rightward(1).start()

        @pl.when(self.at.z == 2)
        def _():
            self.leftward(3).wait_recv()
            self.br[0:2] += self.b2[0:2]
            self.leftward(2).start()

    def stage5(self):
        @pl.when(self.at.z == 2)
        def _():
            self.rightward(1).wait_recv()
            self.bl[3:4] += self.b2[3:4]
            self.rightward(2).start()

        @pl.when(self.at.z == 1)
        def _():
            self.leftward(2).wait_recv()
            self.br[0:1] += self.b2[0:1]
            self.leftward(1).start()

    def stage6(self):
        @pl.when(self.at.z == 3)
        def _():
            self.rightward(2).wait_recv()
            self.put(self.b2[3] + self.bl[3])

        @pl.when(self.at.z == 0)
        def _():
            self.leftward(1).wait_recv()
            self.put(self.b2[0] + self.br[0])

        @pl.when(self.at.z == 1)
        def _():
            self.put(self.b2[1] + self.bl[1] + self.br[1])

        @pl.when(self.at.z == 2)
        def _():
            self.put(self.b2[2] + self.bl[2] + self.br[2])

    def line_sent(self):
        for i in range(4):

            @pl.when(self.at.z == i)
            def _(i=i):
                if i < 3:
                    self.rightward(i).wait_send()
                if i > 0:
                    self.leftward(i).wait_send()


class Reducer:
    def __init__(self, place, n, part, scratch, put):
        self.place, self.n, self.part, self.put = place, n, part, put
        self.c0, self.c1a, self.c1b, self.c2, self.zl, self.zr = scratch[:6]
        self.sems = Sems(scratch[6:16])
        self.pairs = (n + 1) // 2

    @staticmethod
    def scratch(n, rows):
        bufs = [(n, 2, 4, 2), ((n + 1) // 2, 4, 2), (max(n // 2, 1), 2, 4), (n, 4), (n, 4), (n, 4)]
        return [pltpu.VMEM(b + (rows, D), F32) for b in bufs] + Sems.scratch(n)

    def chunk(self, k, parity):
        return Chunk(
            self.place,
            k,
            parity == 0,
            self.sems,
            self.c0.at[k],
            (self.c1b if parity else self.c1a).at[k // 2],
            self.c2.at[k],
            self.zl.at[k],
            self.zr.at[k],
            self.part(k),
            lambda v: self.put(k, v),
        )

    def send(self, first, after):
        def one(k, carry):
            for i in range(2):
                self.chunk(k, 0).core(i).start()
            return carry

        lax.fori_loop(first, after, one, 0)

    def one(self, stage, pair):
        for parity in range(2):
            k = 2 * pair + parity
            k = jnp.int32(k) if isinstance(k, int) else k

            @pl.when(jnp.logical_and(k >= 0, k < self.n))
            def _(k=k, parity=parity):
                getattr(self.chunk(k, parity), f"stage{stage}")()

    def early(self, pair):
        self.one(1, pair)

    def step(self, tau):
        self.one(1, tau)
        for stage in range(2, 7):
            self.one(stage, tau - stage)

    def finish(self):
        def one(k, carry):
            for parity in range(2):

                @pl.when(lax.rem(k, 2) == parity)
                def _(parity=parity):
                    c = self.chunk(k, parity)
                    for i in range(2):
                        c.core(i).wait_send()
                    c.one().wait_send()
                    c.two().wait_send()
                    c.line_sent()

            return carry

        lax.fori_loop(0, self.n, one, 0)


class SmallSum:
    def __init__(self, place, S, bufs, send, recv, put):
        self.at, self.S, self.send, self.recv, self.put = place, S, send, recv, put
        self.d0, self.d1, self.d2, self.dl, self.dr, self.t1, self.t2, self.t3, self.fl, self.fr = bufs

    @staticmethod
    def scratch():
        return [pltpu.VMEM((8, D), F32)] * 10 + [pltpu.SemaphoreType.DMA((5,)), pltpu.SemaphoreType.DMA((5,))]

    def hop(self, src, dst, i, d):
        return remote(src, dst, self.send.at[i], self.recv.at[i], d)

    def core(self):
        return self.hop(self.S, self.d0, 0, self.at.peer)

    def along_x(self):
        return self.hop(self.t1, self.d1, 1, self.at.xn)

    def along_y(self):
        return self.hop(self.t2, self.d2, 2, self.at.yn)

    def rightward(self, i):
        return self.hop(self.t3 if i == 0 else self.fl, self.dl, 3, self.at.right)

    def leftward(self, i):
        return self.hop(self.t3 if i == 3 else self.fr, self.dr, 4, self.at.left)

    def stage1(self):
        self.core().wait_recv()
        self.t1[...] = self.S[...] + self.d0[...]
        self.along_x().start()

    def stage2(self):
        self.along_x().wait_recv()
        self.t2[...] = self.t1[...] + self.d1[...]
        self.along_y().start()

    def stage3(self):
        self.along_y().wait_recv()
        self.t3[...] = self.t2[...] + self.d2[...]

        @pl.when(self.at.z == 0)
        def _():
            self.rightward(0).start()

        @pl.when(self.at.z == 3)
        def _():
            self.leftward(3).start()

    def from_left(self, i):
        self.rightward(i).wait_recv()
        self.fl[...] = self.dl[...] + self.t3[...]

    def from_right(self, i):
        self.leftward(i).wait_recv()
        self.fr[...] = self.dr[...] + self.t3[...]

    def stage4(self):
        @pl.when(self.at.z == 1)
        def _():
            self.from_left(0)
            self.rightward(1).start()

        @pl.when(self.at.z == 2)
        def _():
            self.from_right(3)
            self.leftward(2).start()

    def stage5(self):
        @pl.when(self.at.z == 2)
        def _():
            self.from_left(1)
            self.rightward(2).start()

        @pl.when(self.at.z == 1)
        def _():
            self.from_right(2)
            self.leftward(1).start()

    def stage6(self):
        @pl.when(self.at.z == 3)
        def _():
            self.from_left(2)
            self.put(self.fl[...])

        @pl.when(self.at.z == 0)
        def _():
            self.from_right(1)
            self.put(self.fr[...])

        @pl.when(jnp.logical_or(self.at.z == 1, self.at.z == 2))
        def _():
            self.put(self.fl[...] + self.dr[...])

    def finish(self):
        for c in (self.core(), self.along_x(), self.along_y()):
            c.wait_send()
        for i in range(4):

            @pl.when(self.at.z == i)
            def _(i=i):
                if i < 3:
                    self.rightward(i).wait_send()
                if i > 0:
                    self.leftward(i).wait_send()


def small_outputs(place, counts, outs, tot):
    ga, gi, gf, gh, means = outs

    def put(v):
        tot[...] = v
        d = place.p * RUNS + place.s
        for i, ref in enumerate((ga, gi, gf)):
            ref[...] = pltpu.roll(tot[i : i + 1, :], D - PIECE * d, 1)[:, :PIECE]
        row = tot[pl.ds(3 + d // 8, 1), :]
        gh[...] = pltpu.roll(row, D - 4 * PIECE * lax.rem(d, 8), 1)[:, : 4 * PIECE]
        lane = lax.broadcasted_iota(jnp.int32, (1, 128), 1)
        scale = jnp.full((1, 128), counts[0], F32)
        for i in range(1, PATTERNS):
            scale = jnp.where(lane == i, counts[i], scale)
        means[...] = (tot[7:8, :128] / scale)[:, :PATTERNS]

    return put


N_PIECES = 9
SUB = 8


def finish_kernel(counts, rec, x_ref, dy1_ref, w, ga1, S_in, gx, g_qkv, ga, gi, gf, gh, means, dqkv, lhs, th, tl, r_hi, r_lo, tiles, S, tot, gx2, *scratch):
    place = Place()
    barrier = pltpu.get_barrier_semaphore()
    expected = place.greet(barrier)
    for j in range(HEADS // 2):
        u, v = rec[2 * j, ROWS:PACK, :], rec[2 * j + 1, ROWS:PACK, :]
        cols = slice(128 * j, 128 * j + 128)
        dqkv[0:HALF, cols] = pick(u, swap(v))
        dqkv[HALF:ROWS, cols] = pick(swap(u), v)
        u, v = rec[2 * j, 0:ROWS, :], rec[2 * j + 1, 0:ROWS, :]
        dqkv[:, D + 128 * j : D + 128 * j + 128] = pick(u, swap(v))
        dqkv[:, 2 * D + 128 * j : 2 * D + 128 * j + 128] = pick(swap(u), v)
    gain = ga1[...][None, :]
    n, rs = normed(x_ref[...])
    put_turned(th, tl, n * gain)

    def part(k):
        rows = pl.ds(pl.multiple_of(lax.rem(k, 3) * SUB, SUB), SUB)
        return lambda i, c: tiles.at[k // 3, i, c, :, :, rows, :]

    def put(k, v):
        g_qkv[
            pl.ds(pl.multiple_of(lax.rem(k, 3) * SUB, SUB), SUB), pl.ds(pl.multiple_of((k // 3) * D, D), D)
        ] = v

    n_r = 16
    big = Reducer(place, N_PIECES, part, scratch[:n_r], put)
    rest = scratch[n_r:]
    small = SmallSum(
        place, S, rest[:10], rest[10], rest[11], small_outputs(place, counts, (ga, gi, gf, gh, means), tot)
    )

    def tile_of(j, carry):
        r_hi[...], r_lo[...] = split(dqkv[:, pl.ds(pl.multiple_of(D * j, D), D)])

        def one(i, inner):
            rows = pl.ds(pl.multiple_of(i * 2 * ROWS, 128), 2 * ROWS)
            h, l = th[rows, :], tl[rows, :]
            v = dot_nn(h, r_hi[...]) + dot_nn(h, r_lo[...]) + dot_nn(l, r_hi[...])
            tiles[j, i] = v.reshape(2, 4, 2, PIECE, D)
            return inner

        lax.fori_loop(0, 2, one, 0)

        @pl.when(j == 0)
        def _():
            pl.semaphore_wait(barrier, expected)

        big.send(3 * j, 3 * j + 3)

        @pl.when(j > 0)
        def _():
            big.early(j - 1)

        return carry

    lax.fori_loop(0, 3, tile_of, 0)
    gx2[...] = jnp.zeros_like(gx2)

    def back(j, carry):
        cols = pl.ds(pl.multiple_of(D * j, D), D)
        put_split(lhs, dqkv[:, cols])
        gx2[...] += halves_sum(dot_nt(lhs[...], w[:, cols]))
        return carry

    lax.fori_loop(0, 3, back, 0)
    e = gx2[...]
    S[...] = S_in[...]
    S[0:1, :] = jnp.sum(e * n, 0, keepdims=True)
    small.core().start()
    gx[...] = (dy1_ref[...] + norm_back(e * gain, n, rs)).reshape(ROWS, 1, D)
    small.stage1()

    def step(tau, carry):
        for stage in range(2, 7):

            @pl.when(tau == stage + 1)
            def _(stage=stage):
                getattr(small, f"stage{stage}")()

        big.step(tau)
        return carry

    lax.fori_loop(2, big.pairs + 6, step, 0)

    big.finish()
    small.finish()


def finish(rec, x, dy1, w, ga, S, counts, cid):
    return pl.pallas_call(
        functools.partial(finish_kernel, counts),
        out_shape=[jax.ShapeDtypeStruct((ROWS, 1, D), F32), jax.ShapeDtypeStruct((PIECE, 3 * D), F32)]
        + [jax.ShapeDtypeStruct((1, n), F32) for n in (PIECE, PIECE, PIECE, 4 * PIECE, PATTERNS)],
        in_specs=[VM] * 6,
        out_specs=[VM] * 7,
        scratch_shapes=[
            pltpu.VMEM((ROWS, 3 * D), F32),
            pltpu.VMEM((2 * ROWS, D), BF16),
            pltpu.VMEM((D, ROWS), BF16),
            pltpu.VMEM((D, ROWS), BF16),
            pltpu.VMEM((ROWS, D), BF16),
            pltpu.VMEM((ROWS, D), BF16),
            pltpu.VMEM((3, 2, 2, 4, 2, PIECE, D), F32),
            pltpu.VMEM((8, D), F32),
            pltpu.VMEM((8, D), F32),
            pltpu.VMEM((ROWS, D), F32),
        ]
        + Reducer.scratch(N_PIECES, SUB)
        + SmallSum.scratch(),
        compiler_params=params(collective_id=cid, has_side_effects=True),
    )(rec, x, dy1, w, ga, S)


def deliver_kernel(*refs):
    n = len(refs) // 2
    for src, dst in zip(refs[:n], refs[n:]):
        dst[...] = src[...]


def deliver(*arrays):
    return pl.pallas_call(
        deliver_kernel,
        out_shape=[jax.ShapeDtypeStruct(v.shape, v.dtype) for v in arrays],
        in_specs=[VM] * len(arrays),
        out_specs=[VM] * len(arrays),
        compiler_params=params(),
    )(*arrays)


def rows_from_pairs(rec, dst):
    for j in range(HEADS // 2):
        u, v = rec[2 * j], rec[2 * j + 1]
        cols = slice(128 * j, 128 * j + 128)
        dst[0:HALF, cols] = pick(u, swap(v))
        dst[HALF:ROWS, cols] = pick(swap(u), v)


def pairs_from_rows(src, dst):
    for j in range(HEADS // 2):
        top = src[0:HALF, 128 * j : 128 * j + 128]
        bottom = src[HALF:ROWS, 128 * j : 128 * j + 128]
        dst[2 * j] = pick(top, swap(bottom))
        dst[2 * j + 1] = pick(swap(top), bottom)


def halves_sum(r):
    return r[:ROWS] + r[ROWS:]


def norm_back(f, n, rs):
    return (f - jnp.mean(f, -1, keepdims=True) - n * jnp.mean(f * n, -1, keepdims=True)) * rs


def put_turned(hi_ref, lo_ref, v):
    for j in range(D // 128):
        t = v[:, 128 * j : 128 * j + 128].T
        hi, lo = split(t)
        hi_ref[128 * j : 128 * j + 128, :] = hi
        lo_ref[128 * j : 128 * j + 128, :] = lo


class ToHeads:
    def __init__(self, pk, rec, send, recv):
        self.pk, self.rec, self.send, self.recv = pk, rec, send, recv
        self.facts = place_facts()

    def greet(self):
        p, s, x, core, active, head = self.facts
        barrier = pltpu.get_barrier_semaphore()

        @pl.when(active)
        def _():
            def one(m, carry):
                q, t = home_device(core, m)

                @pl.when(jnp.logical_not(same(p, s, q, t)))
                def _():
                    pl.semaphore_signal(barrier, inc=1, device_id=to(q, t), device_id_type=MESH)

                return carry

            lax.fori_loop(0, HOMES, one, 0)

    def copy(self, h):
        p, s, x, core, active, head = self.facts
        slot = s * 2 + core
        q, t = head_device(h, x)
        far = pltpu.make_async_remote_copy(
            src_ref=self.pk.at[h],
            dst_ref=self.rec.at[slot],
            send_sem=self.send.at[h],
            recv_sem=self.recv.at[slot],
            device_id=to(q, t),
            device_id_type=MESH,
        )
        return same(p, s, q, t), lambda: pltpu.make_async_copy(self.pk.at[h], self.rec.at[slot], self.recv.at[slot]), far

    def wait(self, others):
        p, s, x, core, active, head = self.facts
        mine = jnp.logical_and(active, core == x).astype(jnp.int32)
        pl.semaphore_wait(pltpu.get_barrier_semaphore(), HEADS + others - mine)

    def start(self):
        p, s, x, core, active, head = self.facts

        def one(j, carry):
            here, near, far = self.copy(lax.rem(j + 3 * (s // 2) + 2 * p, HEADS))

            @pl.when(here)
            def _():
                near().start()

            @pl.when(jnp.logical_not(here))
            def _():
                far.start()

            return carry

        lax.fori_loop(0, HEADS, one, 0)

    def finish(self):
        active = self.facts[4]

        @pl.when(active)
        def _():
            def arrive(m, carry):
                pltpu.make_async_copy(self.rec.at[m], self.rec.at[m], self.recv.at[m]).wait()
                return carry

            lax.fori_loop(0, HOMES, arrive, 0)

        def sent(h, carry):
            here, near, far = self.copy(h)

            @pl.when(jnp.logical_not(here))
            def _():
                far.wait_send()

            return carry

        lax.fori_loop(0, HEADS, sent, 0)


FT = 1024


def product(hi, lo, r_hi, r_lo, put):
    def one(i, carry):
        rows = pl.ds(pl.multiple_of(i * 2 * ROWS, 128), 2 * ROWS)
        h, l = hi[rows, :], lo[rows, :]
        put(i, dot_nn(h, r_hi[...]) + dot_nn(h, r_lo[...]) + dot_nn(l, r_hi[...]))
        return carry

    lax.fori_loop(0, 2, one, 0)


N_FF = 9
N_COLS = 5


def ff_kernel(rec, x_ref, g3, wo, wu, wd, gi1, gf1, gh1, sums, out3, drec, dy1_ref, S, C0, C1a, C1b, dap, lhs, lhs2, gi, gf, gh, gh_g, g_ref, out_ref, V, N1, U, GP, E, ACC, th, tl, r_hi, r_lo, cols_t, rows_t, c0, c1a, c1b, osem, dsend, drecv, *rsems):
    place = Place()
    sems = Sems(rsems)
    travel = ToHeads(dap, drec, dsend, drecv)
    travel.greet()
    place.greet(pltpu.get_barrier_semaphore(), False)

    def chunk(k, part=None):
        if not isinstance(k, int):
            return Chunk(place, k, True, sems, c0.at[k], part=part)
        x_first = k % 2 == 0
        b1 = None if k < N_COLS else (c1a if x_first else c1b).at[(k - N_COLS) // 2]
        return Chunk(place, k, x_first, sems, c0.at[k], b1, part=part)

    for wide, flat in ((gi, gi1), (gf, gf1), (gh, gh1)):
        wide[...] = flat[...][None, :]
    g_ref[...] = g3[...].reshape(ROWS, D)
    rows_from_pairs(rec, V)
    na, rs_a = normed(V[...])
    V[...] = na
    put_split(lhs, na * gi[...])

    def project(j, carry):
        cols = pl.ds(pl.multiple_of(256 * j, 256), 256)
        N1[:, cols] = x_ref[:, cols] + halves_sum(dot_nn(lhs[...], wo[:, cols]))
        return carry

    lax.fori_loop(0, 3, project, 0)
    y1 = N1[...]
    out_ref[...] = y1
    ny, rs_y = normed(y1)
    N1[...] = ny
    put_split(lhs, ny * gf[...])

    def up(j, su):
        cols = pl.ds(pl.multiple_of(j * FT, FT), FT)
        z = halves_sum(dot_nn(lhs[...], wu[:, cols]))
        phi = 0.5 * (1.0 + lax.erf(z * math.sqrt(0.5)))
        u = z * phi
        U[:, cols] = u
        GP[:, cols] = phi + z * jnp.exp(-0.5 * z * z) * (1.0 / math.sqrt(2.0 * math.pi))
        return su + jnp.sum(u, -1, keepdims=True)

    zero = jnp.zeros((ROWS, 1), F32)
    mean = lax.fori_loop(0, FF // FT, up, zero) * (1.0 / FF)

    def spread(j, sv):
        cols = pl.ds(pl.multiple_of(j * FT, FT), FT)
        c = U[:, cols] - mean
        return sv + jnp.sum(c * c, -1, keepdims=True)

    rs_u = lax.rsqrt(lax.fori_loop(0, FF // FT, spread, zero) * (1.0 / FF) + LN_EPSILON)
    ACC[...] = jnp.zeros_like(ACC)

    def lower(j, carry):
        cols = pl.ds(pl.multiple_of(j * FT, FT), FT)
        n = (U[:, cols] - mean) * rs_u
        U[:, cols] = n
        put_split(lhs2, n * gh[:, cols])
        ACC[...] += halves_sum(dot_nn(lhs2[...], wd[cols, :]))
        return carry

    lax.fori_loop(0, FF // FT, lower, 0)
    out3[...] = (out_ref[...] + ACC[...]).reshape(ROWS, 1, D)

    travel.wait(3)
    r_hi[...], r_lo[...] = split(g_ref[...])

    def down(j, q):
        return chunk(N_COLS + q, lambda i, c: rows_t.at[lax.rem(j, 2), :, :, q])

    def down_step(j, carry):
        @pl.when(j < 4)
        def _():
            cols = pl.ds(pl.multiple_of(D * j, D), D)
            put_turned(th, tl, U[:, cols] * gh[:, cols])
            sent = place.core != lax.rem(j, 2)

            @pl.when(jnp.logical_and(j >= 2, sent))
            def _():
                for q in range(4):
                    down(j - 2, q).core(j // 2 - 1).wait_send()

            def put(i, v):
                rows_t[lax.rem(j, 2), pl.ds(2 * i, 2)] = v.reshape(2, 2, 4, PIECE, D)

            product(th, tl, r_hi, r_lo, put)

            @pl.when(sent)
            def _():
                for q in range(4):
                    down(j, q).core(j // 2).start()

        @pl.when(jnp.logical_and(j > 0, place.core == lax.rem(j + 1, 2)))
        def _():
            for q in range(4):
                down(j - 1, q).own_core((j - 1) // 2)

        return carry

    lax.fori_loop(0, 5, down_step, 0)
    for k in range(N_COLS, N_FF):
        chunk(k).one().start()

    put_split(lhs, g_ref[...])

    def back_down(j, sums):
        cols = pl.ds(pl.multiple_of(j * FT, FT), FT)
        e = halves_sum(dot_nt(lhs[...], wd[cols, :]))
        n = U[:, cols]
        gh_g[:, cols] = jnp.sum(e * n, 0, keepdims=True)
        f = e * gh[:, cols]
        E[:, cols] = f
        return sums[0] + jnp.sum(f, -1, keepdims=True), sums[1] + jnp.sum(f * n, -1, keepdims=True)

    sf, sfn = lax.fori_loop(0, FF // FT, back_down, (zero, zero))
    mf, mfn = sf * (1.0 / FF), sfn * (1.0 / FF)
    ACC[...] = jnp.zeros_like(ACC)

    def back_up(j, carry):
        cols = pl.ds(pl.multiple_of(j * FT, FT), FT)
        dz = (E[:, cols] - mf - U[:, cols] * mfn) * rs_u * GP[:, cols]
        E[:, cols] = dz
        put_split(lhs2, dz)
        ACC[...] += halves_sum(dot_nt(lhs2[...], wu[:, cols]))
        return carry

    lax.fori_loop(0, FF // FT, back_up, 0)
    e = ACC[...]
    ny = N1[...]
    S[2:3, :] = jnp.sum(e * ny, 0, keepdims=True)
    dy1 = g_ref[...] + norm_back(e * gf[...], ny, rs_y)
    dy1_ref[...] = dy1
    put_split(lhs, dy1)

    def project_back(j, carry):
        cols = pl.ds(pl.multiple_of(256 * j, 256), 256)
        ACC[:, cols] = halves_sum(dot_nt(lhs[...], wo[cols, :]))
        return carry

    lax.fori_loop(0, 3, project_back, 0)
    e = ACC[...]
    na = V[...]
    S[1:2, :] = jnp.sum(e * na, 0, keepdims=True)
    S[0:1, :] = jnp.zeros((1, D), F32)
    for j in range(4):
        S[3 + j : 4 + j, :] = gh_g[:, D * j : D * j + D]
    lane = lax.broadcasted_iota(jnp.int32, (1, 128), 1)
    S[7:8, :] = jnp.zeros((1, D), F32)
    S[7:8, 0:128] = sum(jnp.where(lane == i, sums[i : i + 1, :], 0.0) for i in range(PATTERNS))
    ACC[...] = norm_back(e * gi[...], na, rs_a)
    pairs_from_rows(ACC, dap)
    travel.start()

    def column(k):
        return chunk(k, lambda i, c: cols_t.at[lax.rem(k, 2), i, c])

    def out_copy(k):
        return pltpu.make_async_copy(c0.at[k], C0.at[k], osem.at[k])

    put_turned(th, tl, na * gi[...])
    r_hi[...], r_lo[...] = split(dy1)

    def column_step(k, carry):
        @pl.when(k < N_COLS)
        def _():
            @pl.when(k >= 2)
            def _():
                for i in range(2):
                    column(k - 2).core(i).wait_send()

            @pl.when(k >= 1)
            def _():
                r_hi[...], r_lo[...] = split(E[:, pl.ds(pl.multiple_of(D * (k - 1), D), D)])

            def put(i, v):
                cols_t[lax.rem(k, 2), i] = v.reshape(2, 4, 2, PIECE, D)

            product(th, tl, r_hi, r_lo, put)
            for i in range(2):
                column(k).core(i).start()

            @pl.when(k == 0)
            def _():
                put_turned(th, tl, N1[...] * gf[...])

        @pl.when(k > 0)
        def _():
            for i in range(2):
                column(k - 1).own_core(i)
            out_copy(k - 1).start()

        return carry

    lax.fori_loop(0, N_COLS + 1, column_step, 0)

    def c1_copy(k):
        b1, out = (c1a, C1a) if k % 2 == 0 else (c1b, C1b)
        i = (k - N_COLS) // 2
        return pltpu.make_async_copy(b1.at[i], out.at[i], osem.at[k])

    for k in range(N_COLS, N_FF):
        chunk(k).arrived()
        c1_copy(k).start()
    travel.finish()
    for k in range(N_COLS - 2, N_COLS):
        for i in range(2):
            column(jnp.int32(k)).core(i).wait_send()
    for j in range(2, 4):

        @pl.when(place.core != j % 2)
        def _(j=j):
            for q in range(4):
                down(jnp.int32(j), q).core(j // 2).wait_send()

    for k in range(N_COLS):
        out_copy(k).wait()
    for k in range(N_COLS, N_FF):
        chunk(k).one().wait_send()
        c1_copy(k).wait()


def feed_forward(rec, x, g, wo, wu, wd, gi, gf, gh, sums):
    act = jax.ShapeDtypeStruct((ROWS, D), F32)
    wide = pltpu.VMEM((ROWS, FF), F32)
    thin = pltpu.VMEM((ROWS, D), F32)
    return pl.pallas_call(
        ff_kernel,
        out_shape=[
            jax.ShapeDtypeStruct((ROWS, 1, D), F32),
            jax.ShapeDtypeStruct((HOMES, HALF, 128), F32),
            act,
            jax.ShapeDtypeStruct((8, D), F32),
            jax.ShapeDtypeStruct((N_COLS, 2, 4, 2, PIECE, D), F32),
            jax.ShapeDtypeStruct((2, 4, 2, PIECE, D), F32),
            jax.ShapeDtypeStruct((2, 2, 4, PIECE, D), F32),
        ],
        in_specs=[VM] * 10,
        out_specs=[VM, ANY, VM, VM, ANY, ANY, ANY],
        scratch_shapes=[
            pltpu.VMEM((HEADS, HALF, 128), F32),
            pltpu.VMEM((2 * ROWS, D), BF16),
            pltpu.VMEM((2 * ROWS, FT), BF16),
            pltpu.VMEM((1, D), F32),
            pltpu.VMEM((1, D), F32),
            pltpu.VMEM((1, FF), F32),
            pltpu.VMEM((1, FF), F32),
            thin,
            thin,
            thin,
            thin,
            wide,
            wide,
            wide,
            thin,
        ]
        + [
            pltpu.VMEM((D, ROWS), BF16),
            pltpu.VMEM((D, ROWS), BF16),
            pltpu.VMEM((ROWS, D), BF16),
            pltpu.VMEM((ROWS, D), BF16),
            pltpu.VMEM((2, 2, 2, 4, 2, PIECE, D), F32),
            pltpu.VMEM((2, 4, 2, 4, PIECE, D), F32),
            pltpu.VMEM((N_FF, 2, 4, 2, PIECE, D), F32),
            pltpu.VMEM((2, 4, 2, PIECE, D), F32),
            pltpu.VMEM((2, 2, 4, PIECE, D), F32),
            pltpu.SemaphoreType.DMA((N_FF,)),
            pltpu.SemaphoreType.DMA((HEADS,)),
            pltpu.SemaphoreType.DMA((HOMES,)),
        ]
        + Sems.scratch(N_FF),
        compiler_params=params(collective_id=4, has_side_effects=True),
    )(rec, x, g, wo, wu, wd, gi, gf, gh, sums)


def back_all_kernel(offs, drec, own, sib, ap, lse, C0, C1a, C1b, grec, wo_g, up_g, down_g, qst, kc, vc, kt, qc, dc, lt, k4, v4, kt4, q4, d4, lt4, k5, v5, kt5, q5, d5, lt5, dk, dv, dq, dk4, dv4, dk5, dv5, dq4, dq5, b1, b2, b3, b4, dqt, ds_out, came, lsem, send, recv, qsend, qrecv, fsend, frecv, c0, c1a, c1b, c2, zl, zr, csem, *rsems):
    place = Place()
    p, s, x, core, active, head = place_facts()
    b = core
    o2, o3, o4, o5 = offs[1], offs[2], offs[3], offs[4]
    kvf, qf, X, df = dk, dv.at[0:2], dv.at[2:4], dq
    dqp = qst

    barrier = pltpu.get_barrier_semaphore()
    expected = place.greet(barrier)

    def greet_heads(h, carry):
        q, t = head_device(h, x)

        @pl.when(jnp.logical_not(same(p, s, q, t)))
        def _():
            pl.semaphore_signal(barrier, inc=1, device_id=to(q, t), device_id_type=MESH)

        return carry

    lax.fori_loop(0, HEADS, greet_heads, 0)
    from_homes = HOMES - (core == x).astype(jnp.int32)
    pl.semaphore_wait(barrier, expected + active.astype(jnp.int32) * from_homes)

    def put(k, v):
        @pl.when(k == 0)
        def _():
            wo_g[...] = v

        @pl.when(jnp.logical_and(k > 0, k < 5))
        def _():
            up_g[:, pl.ds(pl.multiple_of((k - 1) * D, D), D)] = v

        @pl.when(k >= 5)
        def _():
            down_g[pl.ds(pl.multiple_of((k - 5) * PIECE, PIECE), PIECE), :] = v

    sems = Sems(rsems)

    def chunk(k):
        x_first = k % 2 == 0
        b0 = c0.at[k] if k < N_COLS else None
        b1 = (c1a if x_first else c1b).at[k // 2]
        return Chunk(
            place, k, x_first, sems, b0, b1, c2.at[k], zl.at[k], zr.at[k], put=lambda v: put(jnp.int32(k), v)
        )

    def load(k):
        if k < N_COLS:
            return pltpu.make_async_copy(C0.at[k], c0.at[k], csem.at[k])
        src, dst = (C1a, c1a) if k % 2 == 0 else (C1b, c1b)
        return pltpu.make_async_copy(src.at[(k - N_COLS) // 2], dst.at[k // 2], csem.at[k])

    PAIRS = ((5, 6), (7, 8), (0, 1), (2, 3), (4,))

    def reduction(*todo):
        for stage, pair in todo:
            for k in PAIRS[pair]:
                if stage == 1:
                    load(k).wait()
                    chunk(k).one().start()
                elif stage == 2 and k >= N_COLS:
                    load(k).wait()
                    chunk(k).two().start()
                else:
                    getattr(chunk(k), f"stage{stage}")()


    def local_copies(m):
        t = pl.multiple_of((m // 2) * ROWS, 64)
        c, d = 2 * b + lax.rem(m, 2), 2 * (1 - b) + lax.rem(m, 2)
        return [
            pltpu.make_async_copy(own.at[m, pl.ds(0, ROWS), :], kvf.at[c, pl.ds(t, ROWS), :], lsem.at[m, 0]),
            pltpu.make_async_copy(sib.at[m], kvf.at[d, pl.ds(t, ROWS), :], lsem.at[m, 1]),
            pltpu.make_async_copy(own.at[m, pl.ds(ROWS, HALF), :], qst.at[m], lsem.at[m, 2]),
        ]

    lse_copy = pltpu.make_async_copy(lse, X, lsem.at[HOMES, 0])

    @pl.when(active)
    def _():
        lse_copy.start()

        def start(m, carry):
            for c in local_copies(m):
                c.start()
            return carry

        lax.fori_loop(0, HOMES, start, 0)

    for pair in PAIRS:
        for k in pair:
            load(k).start()
    reduction((2, 0), (1, 2), (2, 1))

    @pl.when(active)
    def _():
        b1[...] = key_bias((2, 128), (4, 128), 4, 1, 2 * b, True)
        b2[...] = key_bias((1, 256), (2, 256), 4, 2, 2 * b, True)
        for i in range(2):
            b3[i] = key_bias((1, 256), (1, 512), 1, 1, 256 * i, True)
        b3[2] = jnp.zeros((512, 256), F32)
        e4 = class_facts4(o4, b)[1]
        b4[0] = key_bias((1, 256), (2, 256), 12, 6, 6 * e4, True)
        b4[1] = jnp.zeros((512, 256), F32)

        def wait(m, carry):
            for c in local_copies(m):
                c.wait()
            return carry

        lax.fori_loop(0, HOMES, wait, 0)
        lse_copy.wait()
        unpack_pairs(qst, 0, qf, 1.0 / math.sqrt(HD))

        def prepare(i, carry):
            c, t = i // 12, pl.multiple_of(lax.rem(i, 12) * 128, 128)
            k2, v2 = keys_and_values(kvf[c, pl.ds(t, 128), :])
            kc[c, pl.ds(t, 128), :] = k2.astype(BF16)
            vc[c, pl.ds(t, 128), :] = v2.astype(BF16)
            kt[c, :, pl.ds(t, 128)] = k2.T.astype(BF16)
            return carry

        lax.fori_loop(0, 48, prepare, 0)

        def prepare_q(i, carry):
            c, t = i // 12, pl.multiple_of(lax.rem(i, 12) * 128, 128)
            qc[c, pl.ds(t, 128), :] = query_quads(qf[c, pl.ds(t, 128), :])
            return carry

        lax.fori_loop(0, 24, prepare_q, 0)

    keys4, e4, (qc4, qv4) = class_facts4(o4, b)
    kc5, kv5 = lax.rem(o5, 4), o5 // 4
    qi4, qi5 = qc4 - 2 * b, lax.rem(kc5, 2)

    @pl.when(active)
    def _():
        for blk in range(4):
            r = slice(128 * blk, 128 * blk + 128)
            for e in range(2):
                c, v = keys4[e]
                k2, v2 = keys_and_values(kvf[c, pl.ds(v + 384 * blk, 128, stride=3), :])
                k4[e, r, :] = k2.astype(BF16)
                v4[e, r, :] = v2.astype(BF16)
                kt4[e, :, r] = k2.T.astype(BF16)
            q4[r, :] = query_quads(qf[qi4, pl.ds(qv4 + 384 * blk, 128, stride=3), :])
            rows = pl.ds(kv5 + 384 * blk, 128, stride=3)
            k2, v2 = keys_and_values(kvf[kc5, rows, :])
            k5[r, :] = k2.astype(BF16)
            v5[r, :] = v2.astype(BF16)
            kt5[:, r] = k2.T.astype(BF16)
            q5[r, :] = query_quads(qf[qi5, rows, :])
        dk[...] = jnp.zeros_like(dk)

    reduction((1, 3))

    @pl.when(active)
    def _():
        unpack_pairs(drec, 0, df, 1.0)

        def facts(m, carry):
            ci = lax.rem(m, 2)
            t = pl.multiple_of((m // 2) * ROWS, 32)
            prod = drec[m] * ap[m]
            low = lower_lanes(prod)
            d0 = jnp.sum(jnp.where(low, prod, 0.0), -1, keepdims=True)
            d1 = jnp.sum(jnp.where(low, 0.0, prod), -1, keepdims=True)
            for part, d in ((0, d0), (1, d1)):
                rows = pl.ds(t + HALF * part, HALF)
                l = X[ci, rows, :]
                X[ci, rows, :] = jnp.where(low, l, jnp.broadcast_to(d, l.shape))
            return carry

        lax.fori_loop(0, HOMES, facts, 0)

        def turned(v):
            w = v.T
            return jnp.concatenate([w[0:1, :], w[HD : HD + 1, :]], 0)

        def prepare_d(i, carry):
            c, t = i // 12, pl.multiple_of(lax.rem(i, 12) * 128, 128)
            rows = pl.ds(t, 128)
            dc[c, rows, :] = query_quads(df[c, rows, :])
            lt[i] = turned(X[c, rows, :])
            return carry

        lax.fori_loop(0, 24, prepare_d, 0)
        for blk in range(4):
            r = slice(128 * blk, 128 * blk + 128)
            rows = pl.ds(qv4 + 384 * blk, 128, stride=3)
            d4[r, :] = query_quads(df[qi4, rows, :])
            lt4[blk] = turned(X[qi4, rows, :])
            rows = pl.ds(kv5 + 384 * blk, 128, stride=3)
            d5[r, :] = query_quads(df[qi5, rows, :])
            lt5[blk] = turned(X[qi5, rows, :])
        dv[...] = jnp.zeros_like(dv)
        dq[...] = jnp.zeros_like(dq)

    def tile(k, v, kT, q, d, facts_pair, bias, classes=1):
        n = k.shape[0]
        each, edge = n // classes, bias.shape[0] // classes
        s_ = dot_nt(doubled(k), q)
        if each == edge:
            s_ = s_ + bias
        else:
            s_ = s_.reshape(classes, each, 256)
            last = s_[:, each - edge :] + bias.reshape(classes, edge, 256)
            s_ = jnp.concatenate([s_[:, : each - edge], last], 1).reshape(n, 256)
        l0, l1 = facts_pair
        row = jnp.concatenate([l0[0:1, :], l1[0:1, :]], 1)
        delta = jnp.concatenate([l0[1:2, :], l1[1:2, :]], 1)
        pr = jnp.exp(s_ - row)
        ds = pr * (dot_nt(doubled(v), d) - delta)
        hi, lo = split(pr)
        d2, q2_ = d[:, :128], q[:, :128]
        dv_new = dot_nn(jnp.concatenate([hi, lo], 1), jnp.concatenate([d2, d2], 0))
        hi, lo = split(ds)
        dk_new = dot_nn(jnp.concatenate([hi, lo], 1), jnp.concatenate([q2_, q2_], 0))
        dq_new = dot_nn(kT, hi) + dot_nn(kT, lo)
        return dk_new, dv_new, dq_new

    def kept(flag, v):
        return jnp.where(flag, v, 0.0)

    def at256(blk):
        return pl.ds(pl.multiple_of(256 * blk, 128), 256)

    def sweep(last, step, done):
        dqt[...] = jnp.zeros_like(dqt)

        def one(kb, carry):
            step(kb, kb == last)
            return carry

        lax.fori_loop(0, last + 1, one, 0)
        done(dqt[...].T)

    def tile2(base, qb):
        keys = 256 * (qb + 1)
        ks = pl.ds(pl.multiple_of(base, 1024), keys)
        qs = pl.ds(pl.multiple_of(base + 256 * qb, 256), 256)
        blk = (base + 256 * qb) // 128
        a, c, e = tile(
            jnp.concatenate([kc[o2, ks, :], kc[o2 + 2, ks, :]], 0),
            jnp.concatenate([vc[o2, ks, :], vc[o2 + 2, ks, :]], 0),
            jnp.concatenate([kt[o2, :, ks], kt[o2 + 2, :, ks]], 1),
            qc[o2, qs, :],
            dc[o2, qs, :],
            (lt.at[12 * o2 + blk], lt.at[12 * o2 + blk + 1]),
            b2[...],
            2,
        )
        e = e.T
        for par in range(2):
            f = o2 == par
            dk[par, ks, :] += kept(f, a[:keys])
            dk[par + 2, ks, :] += kept(f, a[keys:])
            dv[par, ks, :] += kept(f, c[:keys])
            dv[par + 2, ks, :] += kept(f, c[keys:])
            dq[par, qs, :] += kept(f, e)

    @pl.when(active)
    def _():
        def first_half(i, carry):
            for qb in range(2):
                tile2(1024 * i, qb)
            return carry

        lax.fori_loop(0, 2, first_half, 0)
        for qb in range(2, 4):
            tile2(0, qb)

    reduction((3, 0), (2, 2), (3, 1), (1, 4))

    def q3(qb, carry):
        ci = lax.rem(o3, 2)
        qs = at256(qb)

        def step(kb, own):
            ks = pl.ds(pl.multiple_of(512 * kb, 512), 512)
            a, c, e = tile(
                kc[o3, ks, :],
                vc[o3, ks, :],
                kt[o3, :, ks],
                qc[ci, qs, :],
                dc[ci, qs, :],
                (lt.at[12 * ci + 2 * qb], lt.at[12 * ci + 2 * qb + 1]),
                b3[jnp.where(own, lax.rem(qb, 2), 2)],
            )
            dqt[...] += e
            for i in range(2):
                f = o3 == 2 * b + i
                dk[2 * b + i, ks, :] += kept(f, a)
                dv[2 * b + i, ks, :] += kept(f, c)

        def done(e):
            for i in range(2):
                dq[i, qs, :] += kept(o3 == 2 * b + i, e)

        sweep(qb // 2, step, done)
        return carry

    def q4_(qb, carry):
        qs = at256(qb)

        def step(kb, own):
            ks = at256(kb)
            a, c, e = tile(
                k4[:, ks, :].reshape(512, 128),
                v4[:, ks, :].reshape(512, 128),
                jnp.concatenate([kt4[0, :, ks], kt4[1, :, ks]], 1),
                q4[qs, :],
                d4[qs, :],
                (lt4.at[2 * qb], lt4.at[2 * qb + 1]),
                b4[jnp.where(own, 0, 1)],
            )
            dqt[...] += e
            dk4[:, ks, :] += a.reshape(2, 256, 128)
            dv4[:, ks, :] += c.reshape(2, 256, 128)

        def done(e):
            dq4[qs, :] = e

        sweep(qb, step, done)
        return carry

    def q5_(qb, carry):
        qs = at256(qb)

        a, c, e = tile(
            k5[...], v5[...], kt5[...], q5[qs, :], d5[qs, :], (lt5.at[2 * qb], lt5.at[2 * qb + 1]), b3[qb]
        )
        dk5[...] += a
        dv5[...] += c
        dq5[qs, :] = e.T
        return carry

    @pl.when(active)
    def _():
        lax.fori_loop(0, TOTAL // 256, q3, 0)
        for ref in (dk4, dv4, dk5, dv5):
            ref[...] = jnp.zeros_like(ref)
        lax.fori_loop(0, 2, q4_, 0)
        lax.fori_loop(0, 2, q5_, 0)
        mine5 = kc5 // 2 == b
        for kind in range(12):
            c, rows = kind % 4, pl.ds(kind // 4, THIRD, stride=3)
            f0, f1, f5 = o4 == kind, o4 + 6 == kind, jnp.logical_and(o5 == kind, mine5)
            dk[c, rows, :] += kept(f0, dk4[0]) + kept(f1, dk4[1]) + kept(f5, dk5[...])
            dv[c, rows, :] += kept(f0, dv4[0]) + kept(f1, dv4[1]) + kept(f5, dv5[...])
        for ci in range(2):
            for v in range(3):
                rows = pl.ds(v, THIRD, stride=3)
                f4 = jnp.logical_and(qi4 == ci, qv4 == v)
                f5 = jnp.logical_and(jnp.logical_and(qi5 == ci, kv5 == v), mine5)
                dq[ci, rows, :] += kept(f4, dq4[...]) + kept(f5, dq5[...])

    reduction((4, 0), (4, 1), (2, 3), (3, 2))

    def segment(g):
        def at(t, n):
            return pl.ds(pl.multiple_of(512 * g + t, 128), n)

        for qb in range(4):
            keys = 128 * (qb + 1)
            ks, qs = at(0, keys), at(128 * qb, 128)
            a, c, e = tile(
                kc[:, ks, :].reshape(4 * keys, 128),
                vc[:, ks, :].reshape(4 * keys, 128),
                jnp.concatenate([kt[i, :, ks] for i in range(4)], 1),
                qc[:, qs, :].reshape(256, 256),
                dc[:, qs, :].reshape(256, 256),
                (lt.at[4 * g + qb], lt.at[12 + 4 * g + qb]),
                b1[...],
                4,
            )
            dk[:, ks, :] += a.reshape(4, keys, 128)
            dv[:, ks, :] += c.reshape(4, keys, 128)
            dq[:, qs, :] += e.T.reshape(2, 128, 128)

    def passed(m):
        return remote(ds_out.at[m], came.at[m], fsend.at[m], frecv.at[m], place.peer)

    def home_copies(m):
        q, t = home_device(core, m)
        kv = remote(came.at[m], grec.at[head, pl.ds(0, ROWS), :], send.at[m], recv.at[head], to(q, t))
        dq_ = remote(dqp.at[m], grec.at[head, pl.ds(ROWS, HALF), :], qsend.at[m], qrecv.at[head], to(q, t))
        return q, t, kv, dq_

    def rows_of(m):
        return pl.ds(pl.multiple_of((m // 2) * ROWS, 64), ROWS)

    def kv(c, m):
        k, v = dk[c, rows_of(m), :], dv[c, rows_of(m), :]
        return pick(k + swap(k), v + swap(v))

    def share(m, carry):
        ds_out[m] = kv(2 * (1 - b) + lax.rem(m, 2), m)
        passed(m).start()
        return carry

    def add(m, carry):
        q, t, far_kv, far_q = home_copies(m)
        ci = lax.rem(m, 2)
        v = dq[ci, rows_of(m), :]
        v = (v + swap(v)) * (1.0 / math.sqrt(HD))
        dqp[m] = pick(v[:HALF], v[HALF:])
        passed(m).wait_recv()
        came[m] += kv(2 * b + ci, m)

        @pl.when(same(p, s, q, t))
        def _():
            pltpu.make_async_copy(came.at[m], grec.at[head, pl.ds(0, ROWS), :], recv.at[head]).start()
            pltpu.make_async_copy(dqp.at[m], grec.at[head, pl.ds(ROWS, HALF), :], qrecv.at[head]).start()

        @pl.when(jnp.logical_not(same(p, s, q, t)))
        def _():
            far_kv.start()
            far_q.start()

        return carry

    def round_of(i, carry):
        g = jnp.where(i == 0, 0, 3 - i)

        @pl.when(active)
        def _():
            segment(g)
            lax.fori_loop(jnp.where(i == 0, 0, jnp.where(i == 1, 12, 4)), jnp.where(i == 0, 4, jnp.where(i == 1, 16, 12)), share, 0)

            @pl.when(i > 0)
            def _():
                lax.fori_loop(jnp.where(i == 1, 0, 12), jnp.where(i == 1, 4, 16), add, 0)

        @pl.when(i == 1)
        def _():
            reduction((5, 0), (5, 1), (2, 4), (3, 3), (4, 2))

        return carry

    lax.fori_loop(0, 3, round_of, 0)

    @pl.when(active)
    def _():
        lax.fori_loop(4, 12, add, 0)

    reduction((6, 0), (6, 1), (3, 4), (4, 3), (5, 2))
    reduction((4, 4), (5, 3), (6, 2))
    reduction((5, 4), (6, 3))
    reduction((6, 4))

    def from_head(h, carry):
        a = grec.at[h, pl.ds(0, ROWS), :]
        c = grec.at[h, pl.ds(ROWS, HALF), :]
        pltpu.make_async_copy(a, a, recv.at[h]).wait()
        pltpu.make_async_copy(c, c, qrecv.at[h]).wait()
        return carry

    lax.fori_loop(0, HEADS, from_head, 0)
    for k in range(N_FF):
        if k < N_COLS:
            chunk(k).one().wait_send()
        chunk(k).two().wait_send()
        chunk(k).line_sent()

    @pl.when(active)
    def _():
        def sent(m, carry):
            q, t, far_kv, far_q = home_copies(m)
            passed(m).wait_send()

            @pl.when(jnp.logical_not(same(p, s, q, t)))
            def _():
                far_kv.wait_send()
                far_q.wait_send()

            return carry

        lax.fori_loop(0, HOMES, sent, 0)


def backward_all(offs, drec, own, sib, ap, lse, C0, C1a, C1b, cid):
    dma = pltpu.SemaphoreType.DMA
    keys = pltpu.VMEM((4, TOTAL, 128), BF16)
    full = pltpu.VMEM((4, TOTAL, 128), F32)
    quad = pltpu.VMEM((2, TOTAL, 256), BF16)
    quad3 = pltpu.VMEM((THIRD, 256), BF16)
    pair3 = pltpu.VMEM((THIRD, 128), BF16)
    turned = pltpu.VMEM((128, THIRD), BF16)
    facts3 = pltpu.VMEM((4, 2, 128), F32)
    out3 = pltpu.VMEM((THIRD, 128), F32)
    packs = pltpu.VMEM((HOMES, ROWS, 128), F32)
    halves = pltpu.VMEM((HOMES, HALF, 128), F32)
    return pl.pallas_call(
        back_all_kernel,
        out_shape=[
            jax.ShapeDtypeStruct((HEADS, PACK, 128), F32),
            jax.ShapeDtypeStruct((PIECE, D), F32),
            jax.ShapeDtypeStruct((PIECE, FF), F32),
            jax.ShapeDtypeStruct((4 * PIECE, D), F32),
        ],
        in_specs=[SM, VM, ANY, ANY, VM, ANY, ANY, ANY, ANY],
        out_specs=[ANY, VM, VM, VM],
        scratch_shapes=[
            halves,
            keys,
            keys,
            pltpu.VMEM((4, 128, TOTAL), BF16),
            quad,
            quad,
            pltpu.VMEM((24, 2, 128), F32),
            pltpu.VMEM((2, THIRD, 128), BF16),
            pltpu.VMEM((2, THIRD, 128), BF16),
            pltpu.VMEM((2, 128, THIRD), BF16),
            quad3,
            quad3,
            facts3,
            pair3,
            pair3,
            turned,
            quad3,
            quad3,
            facts3,
            full,
            full,
            pltpu.VMEM((2, TOTAL, 128), F32),
            pltpu.VMEM((2, THIRD, 128), F32),
            pltpu.VMEM((2, THIRD, 128), F32),
            out3,
            out3,
            out3,
            out3,
            pltpu.VMEM((512, 256), F32),
            pltpu.VMEM((512, 256), F32),
            pltpu.VMEM((3, 512, 256), F32),
            pltpu.VMEM((2, 512, 256), F32),
            pltpu.VMEM((128, 256), F32),
            packs,
            packs,
            dma((HOMES + 1, 3)),
            dma((HOMES,)),
            dma((HEADS,)),
            dma((HOMES,)),
            dma((HEADS,)),
            dma((HOMES,)),
            dma((HOMES,)),
            pltpu.VMEM((N_COLS, 2, 4, 2, PIECE, D), F32),
            pltpu.VMEM((5, 4, 2, PIECE, D), F32),
            pltpu.VMEM((4, 2, 4, PIECE, D), F32),
            pltpu.VMEM((N_FF, 4, PIECE, D), F32),
            pltpu.VMEM((N_FF, 4, PIECE, D), F32),
            pltpu.VMEM((N_FF, 4, PIECE, D), F32),
            dma((N_FF,)),
        ]
        + Sems.scratch(N_FF),
        compiler_params=params(collective_id=cid, has_side_effects=True),
    )(offs, drec, own, sib, ap, lse, C0, C1a, C1b)


SEG1, SEG2, SEG3, SEG4, SEG5 = SEGMENTS
DILATION_ONE, DILATION_TWO, DILATION_THREE, DILATION_FOUR, DILATION_FIVE = DILATIONS
MASK_VALUE = -1e30
MATMUL_ACCURACY = lax.Precision.HIGHEST


def passed_along(value, axis, by):
    length = lax.axis_size(axis)
    return lax.ppermute(value, axis, [(i, (i + by) % length) for i in range(length)])


def run_is_live(distance, anchor_point, sequence_width, segment_length):
    return (anchor_point - (distance - 1) * sequence_width - 1) // segment_length == anchor_point // segment_length


def layer_norm(x, gain_vec):
    average = jnp.mean(x, -1, keepdims=True)
    centred = x - average
    variance = jnp.mean(centred * centred, -1, keepdims=True)
    return centred * lax.rsqrt(variance + LN_EPSILON) * gain_vec


def select_table(offsets_row, dilation_rate):
    return (jnp.arange(dilation_rate, dtype=jnp.int32)[:, None] == offsets_row[None, :]).astype(
        jnp.float32
    )


def spread_apart(x, select_option, dilation_rate):
    shaped = x.reshape(x.shape[0] // dilation_rate, dilation_rate, x.shape[1], x.shape[2])
    return jnp.einsum("trhd,rh->thd", shaped, select_option, precision=MATMUL_ACCURACY)


def spread_scalar_rows(x, select_option, dilation_rate):
    shaped = x.reshape(x.shape[0] // dilation_rate, dilation_rate, x.shape[1])
    return jnp.einsum("trh,rh->th", shaped, select_option, precision=MATMUL_ACCURACY)


def spread_rows(x, select_option):
    return jnp.einsum("thd,rh->trhd", x, select_option, precision=MATMUL_ACCURACY).reshape(
        -1, x.shape[1], x.shape[2]
    )


def spread_scalars(x, select_option):
    return jnp.einsum("th,rh->trh", x, select_option, precision=MATMUL_ACCURACY).reshape(
        -1, x.shape[1]
    )


def masked_score_matrix(sparse_queries, key_portion, query_position, key_position, segment_length):
    score_matrix = jnp.einsum(
        "ozt,bzt->zob", sparse_queries, key_portion, precision=MATMUL_ACCURACY
    ) * (1.0 / math.sqrt(key_portion.shape[-1]))
    q_cols = query_position.T[:, :, None]
    k_cols = key_position.T[:, None, :]
    permitted_mask = (k_cols <= q_cols) & (k_cols // segment_length == q_cols // segment_length)
    return (jnp.where(permitted_mask, score_matrix, MASK_VALUE), permitted_mask)


def prepare_pattern(
    query_sequence, key_sequence, value_sequence, offsets_row, dilation_rate, anchor_point
):
    select_option = select_table(offsets_row, dilation_rate)
    sparse_queries = spread_apart(query_sequence, select_option, dilation_rate)
    sparse_key_value = jnp.stack(
        (
            spread_apart(key_sequence, select_option, dilation_rate),
            spread_apart(value_sequence, select_option, dilation_rate),
        )
    )
    query_position = (
        anchor_point
        + jnp.arange(sparse_queries.shape[0], dtype=jnp.int32)[:, None] * dilation_rate
        + offsets_row[None, :]
    )
    return (select_option, sparse_queries, sparse_key_value, query_position)


def pattern_forward_pass(
    sparse_queries,
    sparse_key_value,
    query_position,
    reach,
    segment_length,
    anchor_point,
    sequence_width,
):
    masked_logits, permitted_mask = masked_score_matrix(
        sparse_queries, sparse_key_value[0], query_position, query_position, segment_length
    )
    row_max = jnp.max(masked_logits, -1)
    softmax_weights = jnp.where(permitted_mask, jnp.exp(masked_logits - row_max[..., None]), 0.0)
    state = (
        row_max,
        jnp.sum(softmax_weights, -1),
        jnp.einsum("tlj,jtb->tlb", softmax_weights, sparse_key_value[1], precision=MATMUL_ACCURACY),
    )

    def one_run(distance, carry):
        remote_key_value, state = carry
        remote_key_value = passed_along(remote_key_value, "seq", 1)
        key_position = query_position - distance * sequence_width

        def update(state_in):
            old_max, old_sum, old_acc = state_in
            masked_remote, permitted_remote = masked_score_matrix(
                sparse_queries, remote_key_value[0], query_position, key_position, segment_length
            )
            new_max = jnp.maximum(old_max, jnp.max(masked_remote, -1))
            weights_far = jnp.where(
                permitted_remote, jnp.exp(masked_remote - new_max[..., None]), 0.0
            )
            factor = jnp.exp(old_max - new_max)
            added = jnp.einsum(
                "tlj,jtb->tlb", weights_far, remote_key_value[1], precision=MATMUL_ACCURACY
            )
            return (
                new_max,
                old_sum * factor + jnp.sum(weights_far, -1),
                old_acc * factor[..., None] + added,
            )

        def unchanged(state_in):
            return state_in

        is_live = run_is_live(distance, anchor_point, sequence_width, segment_length)
        return remote_key_value, lax.cond(is_live, update, unchanged, state)

    state = lax.fori_loop(1, reach + 1, one_run, (sparse_key_value, state))[1]
    row_max, row_sum, accumulated = state
    mixture = jnp.transpose(accumulated / row_sum[..., None], (1, 0, 2))
    log_sum = (row_max + jnp.log(row_sum)).T
    return (mixture, log_sum)


def merge_patterns(forwards, prepared_inputs):
    full_lse = []
    full_mix = []
    for pattern_spec in range(len(forwards)):
        mixture, log_sum = forwards[pattern_spec]
        select_option = prepared_inputs[pattern_spec][0]
        covered = spread_scalars(jnp.ones_like(log_sum), select_option)
        full_lse.append(spread_scalars(log_sum, select_option) + (covered - 1.0) * 1e30)
        full_mix.append(spread_rows(mixture, select_option))
    stacked = jnp.stack(full_lse)
    row_max = jnp.max(stacked, 0)
    softmax_weights = jnp.exp(stacked - row_max)
    row_sum = jnp.sum(softmax_weights, 0)
    attended = full_mix[0] * softmax_weights[0][..., None]
    for pattern_spec in range(1, len(full_mix)):
        attended = attended + full_mix[pattern_spec] * softmax_weights[pattern_spec][..., None]
    return (attended / row_sum[..., None], row_max + jnp.log(row_sum))


def pattern_backward(
    select_option,
    dilation_rate,
    segment_length,
    anchor_point,
    sparse_queries,
    sparse_key_value,
    query_position,
    reach,
    sequence_gradient,
    row_difference,
    combined_logsumexp,
):
    sequence_width = sequence_gradient.shape[0]
    sparse_gradient = spread_apart(sequence_gradient, select_option, dilation_rate)
    sparse_output_grad = spread_scalar_rows(row_difference, select_option, dilation_rate).T
    sparse_logsumexp = spread_scalar_rows(combined_logsumexp, select_option, dilation_rate).T
    inverse_square_root = 1.0 / math.sqrt(sparse_queries.shape[-1])

    def portion_gradients(key_portion, value_portion, key_position):
        masked_logits, permitted_mask = masked_score_matrix(
            sparse_queries, key_portion, query_position, key_position, segment_length
        )
        softmax_weights = jnp.where(
            permitted_mask, jnp.exp(masked_logits - sparse_logsumexp[..., None]), 0.0
        )
        value_gradient = jnp.einsum(
            "tui,utx->itx", softmax_weights, sparse_gradient, precision=MATMUL_ACCURACY
        )
        pattern_gradient = jnp.einsum(
            "ozt,bzt->zob", sparse_gradient, value_portion, precision=MATMUL_ACCURACY
        )
        score_gradient = (
            softmax_weights
            * (pattern_gradient - sparse_output_grad[..., None])
            * inverse_square_root
        )
        query_gradient = jnp.einsum(
            "hqk,khd->qhd", score_gradient, key_portion, precision=MATMUL_ACCURACY
        )
        key_gradient = jnp.einsum(
            "tui,utx->itx", score_gradient, sparse_queries, precision=MATMUL_ACCURACY
        )
        return (query_gradient, jnp.stack((key_gradient, value_gradient)))

    query_gradient, key_value_gradient = portion_gradients(
        sparse_key_value[0], sparse_key_value[1], query_position
    )

    def one_run(distance, carry):
        remote_key_value, remote_gradient, query_sum = carry
        remote_key_value = passed_along(remote_key_value, "seq", 1)
        remote_gradient = passed_along(remote_gradient, "seq", 1)
        key_position = query_position - distance * sequence_width

        def far_grads():
            part_q, part_kv = portion_gradients(remote_key_value[0], remote_key_value[1], key_position)
            return query_sum + part_q, remote_gradient + part_kv

        def no_grads():
            return query_sum, remote_gradient

        is_live = run_is_live(distance, anchor_point, sequence_width, segment_length)
        query_sum, remote_gradient = lax.cond(is_live, far_grads, no_grads)
        return remote_key_value, remote_gradient, query_sum

    _, travelled, query_gradient = lax.fori_loop(
        1, reach + 1, one_run, (sparse_key_value, key_value_gradient, query_gradient)
    )
    return (query_gradient, passed_along(travelled, "seq", -reach))


def front_part(own_rows, w_qkv, gain_attn):
    return jnp.dot(layer_norm(own_rows, gain_attn), w_qkv, precision=MATMUL_ACCURACY)


def after_part(attn_rows, own_rows, w_out, w_up, w_down, gain_inner, gain_ffn, gain_hidden):
    residual = own_rows + jnp.dot(
        layer_norm(attn_rows, gain_inner), w_out, precision=MATMUL_ACCURACY
    )
    hidden = jax.nn.gelu(
        jnp.dot(layer_norm(residual, gain_ffn), w_up, precision=MATMUL_ACCURACY), approximate=False
    )
    return residual + jnp.dot(layer_norm(hidden, gain_hidden), w_down, precision=MATMUL_ACCURACY)


def shards(
    tokens,
    w_qkv,
    w_out,
    w_up,
    w_down,
    gain_attn,
    gain_inner,
    gain_ffn,
    gain_hidden,
    offsets,
    grad_out,
):
    w_qkv = w_qkv.astype(jnp.float32)
    w_out = w_out.astype(jnp.float32)
    w_up = w_up.astype(jnp.float32)
    w_down = w_down.astype(jnp.float32)
    groups = lax.axis_size("pat")
    local_rows = tokens.shape[0]
    sequence_width = local_rows * groups
    heads_here = HEADS // groups
    own_rows = tokens.reshape(local_rows, D)
    qkv_rows, front_back = jax.vjp(front_part, own_rows, w_qkv, gain_attn)
    gathered_qkv = lax.all_to_all(
        qkv_rows.reshape(local_rows, 1, 3, HEADS, HD),
        "pat",
        split_axis=3,
        concat_axis=1,
        tiled=True,
    )
    gathered_qkv = gathered_qkv.reshape(sequence_width, 3, heads_here, HD)
    head_offsets = lax.dynamic_slice_in_dim(
        offsets, lax.axis_index("pat") * heads_here, heads_here, 1
    )
    anchor_point = lax.axis_index("seq") * sequence_width
    dilation_rates = (DILATION_ONE, DILATION_TWO, DILATION_THREE, DILATION_FOUR, DILATION_FIVE)
    segment_lengths = (SEG1, SEG2, SEG3, SEG4, SEG5)
    reaches = [
        min((segment_lengths[pattern_spec] - 2) // sequence_width + 1, lax.axis_size("seq") - 1)
        for pattern_spec in range(PATTERNS)
    ]
    prepared_inputs = []
    for pattern_spec in range(PATTERNS):
        prepared_inputs.append(
            prepare_pattern(
                gathered_qkv[:, 0],
                gathered_qkv[:, 1],
                gathered_qkv[:, 2],
                head_offsets[pattern_spec],
                dilation_rates[pattern_spec],
                anchor_point,
            )
        )
    forwards = []
    for pattern_spec in range(PATTERNS):
        select_option, sparse_queries, sparse_key_value, query_position = prepared_inputs[
            pattern_spec
        ]
        forwards.append(
            pattern_forward_pass(
                sparse_queries,
                sparse_key_value,
                query_position,
                reaches[pattern_spec],
                segment_lengths[pattern_spec],
                anchor_point,
                sequence_width,
            )
        )
    lse_sums = jnp.stack([jnp.sum(entry[1]) for entry in forwards])
    totals = lax.psum(lse_sums, ("pat", "seq"))
    full_length = sequence_width * lax.axis_size("seq")
    counts = jnp.array(
        [
            float(full_length // dilation_rates[pattern_spec] * HEADS)
            for pattern_spec in range(PATTERNS)
        ],
        jnp.float32,
    )
    log_means = totals / counts
    attended, combined_logsumexp = merge_patterns(forwards, prepared_inputs)
    returned_rows = lax.all_to_all(
        attended.reshape(local_rows, groups, heads_here, HD),
        "pat",
        split_axis=1,
        concat_axis=2,
        tiled=True,
    )
    attn_rows = returned_rows.reshape(local_rows, D)
    result, after_back = jax.vjp(
        after_part, attn_rows, own_rows, w_out, w_up, w_down, gain_inner, gain_ffn, gain_hidden
    )
    g_attn, g_resid, g_out, g_up, g_down, g_inner, g_ffn, g_hidden = after_back(
        grad_out.reshape(local_rows, D)
    )
    sequence_gradient = lax.all_to_all(
        g_attn.reshape(local_rows, 1, HEADS, HD), "pat", split_axis=2, concat_axis=1, tiled=True
    )
    sequence_gradient = sequence_gradient.reshape(sequence_width, heads_here, HD)
    row_difference = jnp.sum(sequence_gradient * attended, -1)
    q_grads = []
    kv_grads = []
    for pattern_spec in range(PATTERNS):
        select_option, sparse_queries, sparse_key_value, query_position = prepared_inputs[
            pattern_spec
        ]
        part_q, part_kv = pattern_backward(
            select_option,
            dilation_rates[pattern_spec],
            segment_lengths[pattern_spec],
            anchor_point,
            sparse_queries,
            sparse_key_value,
            query_position,
            reaches[pattern_spec],
            sequence_gradient,
            row_difference,
            combined_logsumexp,
        )
        q_grads.append(part_q)
        kv_grads.append(part_kv)
    grad_total = jnp.zeros((sequence_width, 3, heads_here, HD), jnp.float32)
    for pattern_spec in range(PATTERNS):
        select_option = prepared_inputs[pattern_spec][0]
        grad_total = grad_total + jnp.stack(
            (
                spread_rows(q_grads[pattern_spec], select_option),
                spread_rows(kv_grads[pattern_spec][0], select_option),
                spread_rows(kv_grads[pattern_spec][1], select_option),
            ),
            1,
        )
    grad_back = lax.all_to_all(
        grad_total.reshape(local_rows, groups, 3, heads_here, HD),
        "pat",
        split_axis=1,
        concat_axis=3,
        tiled=True,
    )
    g_tokens, g_qkv, g_attn_gain = front_back(grad_back.reshape(local_rows, 3 * D))
    grad_tokens = (g_resid + g_tokens).reshape(local_rows, 1, D)
    summed = (
        lax.psum_scatter(g_qkv, ("pat", "seq"), scatter_dimension=0, tiled=True),
        lax.psum_scatter(g_out, ("pat", "seq"), scatter_dimension=0, tiled=True),
        lax.psum_scatter(g_up, ("pat", "seq"), scatter_dimension=0, tiled=True),
        lax.psum_scatter(g_down, ("pat", "seq"), scatter_dimension=0, tiled=True),
        lax.psum_scatter(g_attn_gain, ("pat", "seq"), scatter_dimension=0, tiled=True),
        lax.psum_scatter(g_inner, ("pat", "seq"), scatter_dimension=0, tiled=True),
        lax.psum_scatter(g_ffn, ("pat", "seq"), scatter_dimension=0, tiled=True),
        lax.psum_scatter(g_hidden, ("pat", "seq"), scatter_dimension=0, tiled=True),
    )
    return (
        result.reshape(local_rows, 1, D),
        grad_tokens,
        summed[0],
        summed[1],
        summed[2],
        summed[3],
        summed[4],
        summed[5],
        summed[6],
        summed[7],
        log_means,
    )


def fast_shards(tokens, w_qkv, w_out, w_up, w_down, gain_attn, gain_inner, gain_ffn, gain_hidden, offsets, grad_out):
    p, s = lax.axis_index("pat"), lax.axis_index("seq")
    active, head = head_here(p, s)
    mine = lax.dynamic_slice_in_dim(offsets, head, 1, 1)[:, 0]
    info = jnp.concatenate([jnp.stack([active.astype(jnp.int32), lax.rem(p, 2).astype(jnp.int32)]), mine])

    counts = [float(TOTAL * 4 // r * HEADS) for r in DILATIONS]
    pk, x = front(tokens, w_qkv, gain_attn)
    own, sib = to_heads(pk, True, 0)
    ap, lse, sums = attention_forward(info, own, sib)
    rec = to_homes(ap, 1)
    mixed, drec, dy1, S, C0, C1a, C1b = feed_forward(
        rec, x, grad_out, w_out, w_up, w_down, gain_inner, gain_ffn, gain_hidden, sums
    )
    grec, g_out, g_up, g_down = backward_all(mine, drec, own, sib, ap, lse, C0, C1a, C1b, 2)
    gx, g_qkv, *small = finish(grec, x, dy1, w_qkv, gain_attn, S, counts, 3)
    mixed, gx, g_qkv, g_out, g_up, g_down, *small = deliver(mixed, gx, g_qkv, g_out, g_up, g_down, *small)
    return (mixed, gx, g_qkv, g_out, g_up, g_down, *(v.reshape(-1) for v in small))


def fits(mesh):
    return mesh.shape["pat"] == 4 and mesh.shape["seq"] == RUNS


def solution(mesh):
    rows = P("seq", "pat", None)
    split_rows = P(("pat", "seq"), None)
    split_one = P(("pat", "seq"))
    planned = jax.shard_map(
        fast_shards,
        mesh=mesh,
        in_specs=(rows,) + (P(),) * 9 + (rows,),
        out_specs=(rows, rows) + (split_rows,) * 4 + (split_one,) * 4 + (P(),),
        check_vma=False,
    )
    general = jax.shard_map(
        shards,
        mesh=mesh,
        in_specs=(rows,) + (P(),) * 9 + (rows,),
        out_specs=(rows, rows) + (split_rows,) * 4 + (split_one,) * 4 + (P(),),
        check_vma=False,
    )

    def layer(tokens, *rest):
        if fits(mesh) and tokens.shape[0] == TOTAL:
            return planned(tokens, *rest)
        return general(tokens, *rest)

    return layer
```

```python
import functools
import math

import jax
import jax.numpy as jnp
from jax import lax
from jax.experimental import pallas as pl
from jax.experimental.pallas import tpu as pltpu
from jax.sharding import PartitionSpec as P

D = 768
HEADS = 12
HD = 64
FF = 3072
PATTERNS = 5
SEGMENTS = (2048, 4096, 8192, 16384, 32768)
DILATIONS = (1, 2, 4, 6, 12)
LN_EPSILON = 1e-05
NEG = -1e30
F32 = jnp.float32
BF16 = jnp.bfloat16
HIGHEST = lax.Precision.HIGHEST
VMEM_LIMIT = 60 * 1024 * 1024

ROWS = 192
HALF = ROWS // 2
RUNS = 8
TOTAL = ROWS * RUNS
PACK = ROWS + HALF
HOMES = 16
THIRD = TOTAL // 3
PIECE = 24
MESH = pl.DeviceIdType.MESH


def dot_nn(a, b):
    return lax.dot_general(a, b, (((1,), (0,)), ((), ())), preferred_element_type=F32)


def dot_nt(a, b):
    return lax.dot_general(a, b, (((1,), (1,)), ((), ())), preferred_element_type=F32)


def split(v):
    hi = v.astype(BF16)
    return hi, (v - hi.astype(F32)).astype(BF16)


def split32(v):
    hi = v.astype(BF16).astype(F32)
    return hi, v - hi


def lower_lanes(v):
    return lax.broadcasted_iota(jnp.int32, v.shape, v.ndim - 1) < HD


def swap(v):
    return pltpu.roll(v, HD, v.ndim - 1)


def pick(a, b):
    return jnp.where(lower_lanes(a), a, b)


def head_place(h):
    z = h // 3
    column = lax.rem(lax.rem(h, 3) + z + 1, 4)
    return column // 2, z * 2 + lax.rem(column, 2)


def head_here(p, s):
    z = s // 2
    column = (p // 2) * 2 + lax.rem(s, 2)
    k = lax.rem(column - z + 7, 4)
    return k < 3, z * 3 + jnp.minimum(k, 2)


def whole(*_):
    return pl.BlockSpec(memory_space=pltpu.VMEM)


VM = pl.BlockSpec(memory_space=pltpu.VMEM)
ANY = pl.BlockSpec(memory_space=pl.ANY)
SM = pl.BlockSpec(memory_space=pltpu.SMEM)


def params(**kw):
    return pltpu.CompilerParams(vmem_limit_bytes=VMEM_LIMIT, **kw)


def normed(v):
    centred = v - jnp.mean(v, -1, keepdims=True)
    rs = lax.rsqrt(jnp.mean(centred * centred, -1, keepdims=True) + LN_EPSILON)
    return centred * rs, rs


def put_split(ref, v):
    hi, lo = split(v)
    n = v.shape[0]
    ref[0:n, :] = hi
    ref[n : 2 * n, :] = lo


def front_kernel(x3, w_ref, gain_ref, pk_ref, x_ref, lhs):
    x = x3[...].reshape(ROWS, D)
    x_ref[...] = x
    n, _ = normed(x)
    put_split(lhs, n * gain_ref[...][None, :])
    for jj in range(3):
        parts = []
        for kind in range(3):
            c0 = kind * D + 256 * jj
            r = dot_nn(lhs[...], w_ref[:, c0 : c0 + 256])
            parts.append(r[:ROWS] + r[ROWS:])
        for half in range(2):
            q, k, v = (a[:, 128 * half : 128 * half + 128] for a in parts)
            h = 4 * jj + 2 * half
            pk_ref[h, 0:ROWS, :] = pick(k, swap(v))
            pk_ref[h + 1, 0:ROWS, :] = pick(swap(k), v)
            top, bottom = q[:HALF], q[HALF:]
            pk_ref[h, ROWS:PACK, :] = pick(top, swap(bottom))
            pk_ref[h + 1, ROWS:PACK, :] = pick(swap(top), bottom)


def front(x, w, gain):
    return pl.pallas_call(
        front_kernel,
        out_shape=[jax.ShapeDtypeStruct((HEADS, PACK, 128), F32)] + [jax.ShapeDtypeStruct((ROWS, D), F32)],
        in_specs=[VM] * 3,
        out_specs=[VM] * 2,
        scratch_shapes=[pltpu.VMEM((2 * ROWS, D), BF16)],
        compiler_params=params(),
    )(x, w, gain)


def place_facts():
    p, s = lax.axis_index("pat"), lax.axis_index("seq")
    x, core = p // 2, lax.rem(p, 2)
    active, head = head_here(p, s)
    return p, s, x, core, active, head


def home_device(core, m):
    return core * 2 + lax.rem(m, 2), m // 2


def head_device(h, b):
    hx, hs = head_place(h)
    return hx * 2 + b, hs


def same(p, s, q, t):
    return jnp.logical_and(p == q, s == t)


def to(p, s):
    return {"pat": p, "seq": s}


def scatter_kernel(forward, pk, own, *rest):
    if forward:
        sib, send, recv, fsend, frecv = rest
    else:
        send, recv = rest
    p, s, x, core, active, head = place_facts()
    slot = s * 2 + core
    barrier = pltpu.get_barrier_semaphore()

    @pl.when(active)
    def _():
        def greet(m, carry):
            q, t = home_device(core, m)

            @pl.when(jnp.logical_not(same(p, s, q, t)))
            def _():
                pl.semaphore_signal(barrier, inc=1, device_id=to(q, t), device_id_type=MESH)

            return carry

        lax.fori_loop(0, HOMES, greet, 0)
        if forward:
            pl.semaphore_signal(barrier, inc=1, device_id=to(x * 2 + 1 - core, s), device_id_type=MESH)

    mine = jnp.logical_and(active, core == x)
    waits = HEADS - mine.astype(jnp.int32)
    if forward:
        waits = waits + active.astype(jnp.int32)
    pl.semaphore_wait(barrier, waits)

    def copy(h):
        q, t = head_device(h, x)
        return q, t, pltpu.make_async_remote_copy(
            src_ref=pk.at[h],
            dst_ref=own.at[slot],
            send_sem=send.at[h],
            recv_sem=recv.at[slot],
            device_id=to(q, t),
            device_id_type=MESH,
        )

    def start(j, carry):
        h = lax.rem(j + 3 * (s // 2) + 2 * p, HEADS)
        q, t, remote = copy(h)

        @pl.when(same(p, s, q, t))
        def _():
            pltpu.make_async_copy(pk.at[h], own.at[slot], recv.at[slot]).start()

        @pl.when(jnp.logical_not(same(p, s, q, t)))
        def _():
            remote.start()

        return carry

    lax.fori_loop(0, HEADS, start, 0)

    def passed(m):
        return pltpu.make_async_remote_copy(
            src_ref=own.at[m, pl.ds(0, ROWS), :],
            dst_ref=sib.at[m],
            send_sem=fsend.at[m],
            recv_sem=frecv.at[m],
            device_id=to(x * 2 + 1 - core, s),
            device_id_type=MESH,
        )

    @pl.when(active)
    def _():
        def arrive(m, carry):
            pltpu.make_async_copy(own.at[m], own.at[m], recv.at[m]).wait()
            if forward:
                passed(m).start()
            return carry

        lax.fori_loop(0, HOMES, arrive, 0)
        if forward:

            def finish(m, carry):
                passed(m).wait()
                return carry

            lax.fori_loop(0, HOMES, finish, 0)

    def sent(h, carry):
        q, t, remote = copy(h)

        @pl.when(jnp.logical_not(same(p, s, q, t)))
        def _():
            remote.wait_send()

        return carry

    lax.fori_loop(0, HEADS, sent, 0)


def to_heads(packets, forward, cid):
    rows = packets.shape[1]
    shapes = [jax.ShapeDtypeStruct((HOMES, rows, 128), F32)]
    sems = [pltpu.SemaphoreType.DMA((HEADS,)), pltpu.SemaphoreType.DMA((HOMES,))]
    if forward:
        shapes.append(jax.ShapeDtypeStruct((HOMES, ROWS, 128), F32))
        sems += [pltpu.SemaphoreType.DMA((HOMES,)), pltpu.SemaphoreType.DMA((HOMES,))]
    return pl.pallas_call(
        functools.partial(scatter_kernel, forward),
        out_shape=shapes,
        in_specs=[ANY],
        out_specs=[ANY] * len(shapes),
        scratch_shapes=sems,
        compiler_params=params(collective_id=cid, has_side_effects=True),
    )(packets)


def home_barrier(p, s, x, core, active, barrier, also_sibling):
    def greet(h, carry):
        q, t = head_device(h, x)

        @pl.when(jnp.logical_not(same(p, s, q, t)))
        def _():
            pl.semaphore_signal(barrier, inc=1, device_id=to(q, t), device_id_type=MESH)

        return carry

    lax.fori_loop(0, HEADS, greet, 0)

    @pl.when(active)
    def _():
        if also_sibling:
            pl.semaphore_signal(barrier, inc=1, device_id=to(x * 2 + 1 - core, s), device_id_type=MESH)
        mine = (core == x).astype(jnp.int32)
        pl.semaphore_wait(barrier, HOMES - mine + (1 if also_sibling else 0))


def gather_kernel(pk, rec, send, recv):
    p, s, x, core, active, head = place_facts()
    barrier = pltpu.get_barrier_semaphore()
    home_barrier(p, s, x, core, active, barrier, False)

    def copy(m):
        q, t = home_device(core, m)
        return q, t, pltpu.make_async_remote_copy(
            src_ref=pk.at[m],
            dst_ref=rec.at[head],
            send_sem=send.at[m],
            recv_sem=recv.at[head],
            device_id=to(q, t),
            device_id_type=MESH,
        )

    @pl.when(active)
    def _():
        def start(j, carry):
            m = lax.rem(j + 2 * s + 1, HOMES)
            q, t, remote = copy(m)

            @pl.when(same(p, s, q, t))
            def _():
                pltpu.make_async_copy(pk.at[m], rec.at[head], recv.at[head]).start()

            @pl.when(jnp.logical_not(same(p, s, q, t)))
            def _():
                remote.start()

            return carry

        lax.fori_loop(0, HOMES, start, 0)

    def arrive(h, carry):
        pltpu.make_async_copy(rec.at[h], rec.at[h], recv.at[h]).wait()
        return carry

    lax.fori_loop(0, HEADS, arrive, 0)

    @pl.when(active)
    def _():
        def sent(m, carry):
            q, t, remote = copy(m)

            @pl.when(jnp.logical_not(same(p, s, q, t)))
            def _():
                remote.wait_send()

            return carry

        lax.fori_loop(0, HOMES, sent, 0)


def to_homes(packets, cid):
    rows = packets.shape[1]
    return pl.pallas_call(
        gather_kernel,
        out_shape=jax.ShapeDtypeStruct((HEADS, rows, 128), F32),
        in_specs=[ANY],
        out_specs=ANY,
        scratch_shapes=[pltpu.SemaphoreType.DMA((HOMES,)), pltpu.SemaphoreType.DMA((HEADS,))],
        compiler_params=params(collective_id=cid, has_side_effects=True),
    )(packets)


def tile_positions(rows, columns, row_classes, column_classes, t_step, class_step):
    r = lax.broadcasted_iota(jnp.int32, (rows, columns), 0)
    q = lax.broadcasted_iota(jnp.int32, (rows, columns), 1)
    rn, qn = rows // row_classes, columns // column_classes
    return (r % rn) * t_step + (r // rn) * class_step, (q % qn) * t_step + (q // qn) * class_step


def key_bias(q_shape, k_shape, t_step, class_step, shift, keys_first):
    nq, nk = q_shape[0] * q_shape[1], k_shape[0] * k_shape[1]
    if keys_first:
        kp, qp = tile_positions(nk, nq, k_shape[0], q_shape[0], t_step, class_step)
    else:
        qp, kp = tile_positions(nq, nk, q_shape[0], k_shape[0], t_step, class_step)
    return jnp.where(kp - qp <= shift, 0.0, NEG).astype(F32)


def unpack_keys(own, sib, b, kvf):
    def one(m, carry):
        c = 2 * b + lax.rem(m, 2)
        d = 2 * (1 - b) + lax.rem(m, 2)
        t = pl.multiple_of((m // 2) * ROWS, 64)
        kvf[c, pl.ds(t, ROWS), :] = own[m, 0:ROWS, :]
        kvf[d, pl.ds(t, ROWS), :] = sib[m]
        return carry

    lax.fori_loop(0, HOMES, one, 0)


def unpack_pairs(src, first, dst, scale):
    def one(m, carry):
        t = pl.multiple_of((m // 2) * ROWS, 32)
        v = src[m, first : first + HALF, :] * scale
        w = swap(v)
        dst[lax.rem(m, 2), pl.ds(t, HALF), :] = pick(v, w)
        dst[lax.rem(m, 2), pl.ds(t + HALF, HALF), :] = pick(w, v)
        return carry

    lax.fori_loop(0, HOMES, one, 0)


def keys_and_values(kv):
    hi, lo = split32(kv)
    k2 = pick(hi, swap(lo))
    v2 = pick(swap(hi), lo)
    return k2, v2


def doubled(v):
    return jnp.concatenate([v, v], 1)


def query_quads(qq):
    hi, lo = split32(qq)
    return jnp.concatenate([pick(hi, lo).astype(BF16), pick(lo, hi).astype(BF16)], 1)


def class_facts4(o4, b):
    keys = ((lax.rem(o4, 4), o4 // 4), (lax.rem(o4 + 6, 4), (o4 + 6) // 4))
    first = (keys[0][0] // 2) == b
    query = (jnp.where(first, keys[0][0], keys[1][0]), jnp.where(first, keys[0][1], keys[1][1]))
    return keys, jnp.where(first, 0, 1), query


def forward_kernel(offsets, own, sib, ap, lse, sums, kvf, kc, vc, qf, qc, k4, v4, q4, k5, v5, q5, acc, mx, R, b1, b2, b3, b4):
    p, s, x, b, active, head = place_facts()
    offs = [offsets[i, head] for i in range(PATTERNS)]
    sums[...] = jnp.zeros_like(sums)

    @pl.when(active)
    def _():
        ones = jnp.ones((128, 128), BF16)
        unpack_keys(own, sib, b, kvf)
        unpack_pairs(own, ROWS, qf, 1.0 / math.sqrt(HD))

        def with_ones(v2):
            return jnp.concatenate([v2.astype(BF16), ones], 1)

        def prepare(i, carry):
            c, t = i // 12, pl.multiple_of(lax.rem(i, 12) * 128, 128)
            k2, v2 = keys_and_values(kvf[c, pl.ds(t, 128), :])
            kc[c, pl.ds(t, 128), :] = k2.astype(BF16)
            vc[c, pl.ds(t, 128), :] = with_ones(v2)
            return carry

        lax.fori_loop(0, 48, prepare, 0, unroll=2)

        def prepare_q(i, carry):
            c, t = i // 12, pl.multiple_of(lax.rem(i, 12) * 128, 128)
            qc[c, pl.ds(t, 128), :] = query_quads(qf[c, pl.ds(t, 128), :])
            return carry

        lax.fori_loop(0, 24, prepare_q, 0, unroll=2)

        keys4, e4, (qc4, qv4) = class_facts4(offs[3], b)
        kc5, kv5 = lax.rem(offs[4], 4), offs[4] // 4
        for blk in range(4):
            r = slice(128 * blk, 128 * blk + 128)
            for e in range(2):
                c, v = keys4[e]
                k2, v2 = keys_and_values(kvf[c, pl.ds(v + 384 * blk, 128, stride=3), :])
                k4[e, r, :] = k2.astype(BF16)
                v4[e, r, :] = with_ones(v2)
            q4[r, :] = query_quads(qf[qc4 - 2 * b, pl.ds(qv4 + 384 * blk, 128, stride=3), :])
            k2, v2 = keys_and_values(kvf[kc5, pl.ds(kv5 + 384 * blk, 128, stride=3), :])
            k5[r, :] = k2.astype(BF16)
            v5[r, :] = with_ones(v2)
            q5[r, :] = query_quads(qf[lax.rem(kc5, 2), pl.ds(kv5 + 384 * blk, 128, stride=3), :])

        b1[...] = key_bias((2, 128), (4, 128), 4, 1, 2 * b, False)
        b2[...] = key_bias((1, 256), (2, 256), 4, 2, 2 * b, False)
        b3[...] = key_bias((1, 512), (1, 512), 1, 1, 0, False)
        b4[...] = key_bias((1, 256), (2, 256), 12, 6, 6 * e4, False)

        def tile(start, q, k, v, bias, classes, first):
            n = q.shape[0]
            each = n // classes
            per = 1536 // classes if classes == 1 else 512
            s = dot_nt(q, doubled(k))
            wide = s.shape[1]
            own_rows = bias.shape[0] // classes
            s = s.reshape(classes, each, wide)
            edge = s[:, :own_rows] + bias[...].reshape(classes, own_rows, wide)
            s = edge if each == own_rows else jnp.concatenate([edge, s[:, own_rows:]], 1)
            s = s.reshape(n, wide)
            top = jnp.max(s, -1, keepdims=True)

            def where(c):
                return pl.ds(c * per + start, each)

            def load(ref):
                return jnp.concatenate([ref[where(c), :] for c in range(classes)], 0)

            def store(ref, value):
                for c in range(classes):
                    ref[where(c), :] = value[c * each : c * each + each]

            if first:
                m = jnp.broadcast_to(top, (n, 128))
            else:
                old = load(mx)
                m = jnp.maximum(old, top)
            hi, lo = split(jnp.exp(s - jnp.concatenate([m] * (wide // 128), 1)))
            new = dot_nn(jnp.concatenate([hi, lo], 0), v)
            new = new[:n] + new[n:]
            if not first:
                new = load(acc) * doubled(jnp.exp(old - m)) + new
            store(acc, new)
            store(mx, m)

        def closed(pattern, rows):
            value, m = acc[rows, :], mx[rows, :]
            o, l = value[:, :128], value[:, 128:]
            sums[pattern : pattern + 1, :] += jnp.sum(m + jnp.log(l), 0, keepdims=True)
            lane = lax.broadcasted_iota(jnp.int32, m.shape, 1)
            return jnp.where(lane < HD, o + swap(o), jnp.where(lane < 96, l, m))

        def merge(pattern, ci, rows, of):
            r0, r1 = R[ci, rows, :], closed(pattern, of)
            m0 = jnp.broadcast_to(r0[:, 96:97], r0.shape)
            m1 = jnp.broadcast_to(r1[:, 96:97], r1.shape)
            m = jnp.maximum(m0, m1)
            both = r0 * jnp.exp(m0 - m) + r1 * jnp.exp(m1 - m)
            lane = lax.broadcasted_iota(jnp.int32, r0.shape, 1)
            R[ci, rows, :] = jnp.where(lane < 96, both, m)

        def q1(g, carry):
            base = 512 * g

            def at(t, n):
                return pl.ds(pl.multiple_of(base + t, 128), n)

            for kb in range(4):
                start = 128 * kb
                each = 512 - start
                ks = at(start, 128)
                tile(
                    start,
                    qc[:, at(start, each), :].reshape(2 * each, 256),
                    kc[:, ks, :].reshape(512, 128),
                    vc[:, ks, :].reshape(512, 256),
                    b1,
                    2,
                    kb == 0,
                )
            for c in range(2):
                for i in range(2):
                    R[c, at(256 * i, 256), :] = closed(0, pl.ds(512 * c + 256 * i, 256))
            return carry

        lax.fori_loop(0, 3, q1, 0)

        par = offs[1]
        for base, length in ((0, 1024), (1024, 512)):
            for start in range(0, length, 256):
                ks = slice(base + start, base + start + 256)
                tile(
                    start,
                    qc[par, base + start : base + length, :],
                    jnp.concatenate([kc[par, ks, :], kc[par + 2, ks, :]], 0),
                    jnp.concatenate([vc[par, ks, :], vc[par + 2, ks, :]], 0),
                    b2,
                    1,
                    start == 0,
                )

            def join2(i, carry, base=base):
                t = pl.multiple_of(i * 256, 256)
                merge(1, par, pl.ds(base + t, 256), pl.ds(t, 256))
                return carry

            lax.fori_loop(0, length // 256, join2, 0)

        o3 = offs[2]

        @pl.when(o3 // 2 == b)
        def _():
            ci = lax.rem(o3, 2)
            for start in range(0, TOTAL, 512):
                ks = slice(start, start + 512)
                tile(start, qc[ci, start:TOTAL, :], kc[o3, ks, :], vc[o3, ks, :], b3, 1, start == 0)

            def join3(i, carry):
                t = pl.multiple_of(i * 256, 256)
                merge(2, ci, pl.ds(t, 256), pl.ds(t, 256))
                return carry

            lax.fori_loop(0, TOTAL // 256, join3, 0)

        for start in range(0, THIRD, 256):
            ks = slice(start, start + 256)
            tile(
                start, q4[start:THIRD, :], k4[:, ks, :].reshape(512, 128), v4[:, ks, :].reshape(512, 256), b4, 1, start == 0
            )
        for i in range(2):
            merge(3, qc4 - 2 * b, pl.ds(qv4 + 768 * i, 256, stride=3), pl.ds(256 * i, 256))

        @pl.when(kc5 // 2 == b)
        def _():
            tile(0, q5[...], k5[...], v5[...], b3, 1, True)
            for i in range(2):
                merge(4, lax.rem(kc5, 2), pl.ds(kv5 + 768 * i, 256, stride=3), pl.ds(256 * i, 256))

        def finish(m, carry):
            ci = lax.rem(m, 2)
            rows = pl.ds(pl.multiple_of((m // 2) * ROWS, 64), ROWS)
            r = R[ci, rows, :]
            l = jnp.broadcast_to(r[:, HD : HD + 1], r.shape)
            out = r / l
            ap[m] = pick(out[:HALF], swap(out[HALF:]))
            lse[ci, rows, :] = jnp.broadcast_to(r[:, 96:97], r.shape) + jnp.log(l)
            return carry

        lax.fori_loop(0, HOMES, finish, 0, unroll=2)


def attention_forward(offsets, own, sib):
    state = pltpu.VMEM((2, TOTAL, 128), F32)
    return pl.pallas_call(
        forward_kernel,
        out_shape=[
            jax.ShapeDtypeStruct((HOMES, HALF, 128), F32),
            jax.ShapeDtypeStruct((2, TOTAL, 128), F32),
            jax.ShapeDtypeStruct((8, 128), F32),
        ],
        in_specs=[SM, VM, VM],
        out_specs=[VM, VM, VM],
        scratch_shapes=[
            pltpu.VMEM((4, TOTAL, 128), F32),
            pltpu.VMEM((4, TOTAL, 128), BF16),
            pltpu.VMEM((4, TOTAL, 256), BF16),
            state,
            pltpu.VMEM((2, TOTAL, 256), BF16),
            pltpu.VMEM((2, THIRD, 128), BF16),
            pltpu.VMEM((2, THIRD, 256), BF16),
            pltpu.VMEM((THIRD, 256), BF16),
            pltpu.VMEM((THIRD, 128), BF16),
            pltpu.VMEM((THIRD, 256), BF16),
            pltpu.VMEM((THIRD, 256), BF16),
            pltpu.VMEM((TOTAL, 256), F32),
            pltpu.VMEM((TOTAL, 128), F32),
            state,
            pltpu.VMEM((256, 512), F32),
            pltpu.VMEM((256, 512), F32),
            pltpu.VMEM((512, 512), F32),
            pltpu.VMEM((256, 512), F32),
        ],
        compiler_params=params(),
    )(offsets, own, sib)


class Place:
    def __init__(self):
        p, s = lax.axis_index("pat"), lax.axis_index("seq")
        self.p, self.s = p, s
        self.x, self.core, self.z, self.y = p // 2, lax.rem(p, 2), s // 2, lax.rem(s, 2)
        self.peer = to(self.x * 2 + 1 - self.core, s)
        self.xn = to((1 - self.x) * 2 + self.core, s)
        self.yn = to(p, self.z * 2 + 1 - self.y)
        self.left, self.right = to(p, s - 2), to(p, s + 2)

    def greet(self, barrier, line=True):
        for d in (self.peer, self.xn, self.yn):
            pl.semaphore_signal(barrier, inc=1, device_id=d, device_id_type=MESH)
        if not line:
            return 3

        @pl.when(self.z > 0)
        def _():
            pl.semaphore_signal(barrier, inc=1, device_id=self.left, device_id_type=MESH)

        @pl.when(self.z < 3)
        def _():
            pl.semaphore_signal(barrier, inc=1, device_id=self.right, device_id_type=MESH)

        return 3 + (self.z > 0).astype(jnp.int32) + (self.z < 3).astype(jnp.int32)


def remote(src, dst, a, b, d):
    return pltpu.make_async_remote_copy(
        src_ref=src, dst_ref=dst, send_sem=a, recv_sem=b, device_id=d, device_id_type=MESH
    )


def add_in(dst, src):
    lead = dst.shape[:-2]

    def one(i, carry):
        index = []
        for d in reversed(lead):
            index.insert(0, lax.rem(i, d))
            i = i // d
        dst[tuple(index)] += src[tuple(index)]
        return carry

    lax.fori_loop(0, math.prod(lead), one, 0)


class Sems:
    NAMES = ("sc", "rc", "s1", "r1", "s2", "r2", "sl", "rl", "sr", "rr")

    def __init__(self, refs):
        for name, ref in zip(self.NAMES, refs):
            setattr(self, name, ref)

    @staticmethod
    def scratch(n):
        dma = pltpu.SemaphoreType.DMA
        return [dma((n, 2)), dma((n, 2))] + [dma((n,)) for _ in range(8)]


class Chunk:
    def __init__(self, place, k, x_first, sems, b0=None, b1=None, b2=None, bl=None, br=None, part=None, put=None):
        self.at, self.k, self.x_first, self.sems = place, k, x_first, sems
        self.b0, self.b1, self.b2, self.bl, self.br = b0, b1, b2, bl, br
        self.part, self.put = part, put

    def core(self, i):
        k, m = self.k, self.sems
        return remote(self.part(i, 1 - self.at.core), self.b0.at[i], m.sc.at[k, i], m.rc.at[k, i], self.at.peer)

    def one(self):
        k, at, m = self.k, self.at, self.sems
        if self.x_first:
            return remote(self.b0.at[1 - at.x], self.b1, m.s1.at[k], m.r1.at[k], at.xn)
        return remote(self.b0.at[:, :, 1 - at.y], self.b1, m.s1.at[k], m.r1.at[k], at.yn)

    def two(self):
        k, at, m = self.k, self.at, self.sems
        if self.x_first:
            return remote(self.b1.at[:, 1 - at.y], self.b2, m.s2.at[k], m.r2.at[k], at.yn)
        return remote(self.b1.at[1 - at.x], self.b2, m.s2.at[k], m.r2.at[k], at.xn)

    def rightward(self, i):
        k, part, m = self.k, pl.ds(i + 1, 3 - i), self.sems
        src = self.b2 if i == 0 else self.bl
        return remote(src.at[part], self.bl.at[part], m.sr.at[k], m.rl.at[k], self.at.right)

    def leftward(self, i):
        k, part, m = self.k, pl.ds(0, i), self.sems
        src = self.b2 if i == 3 else self.br
        return remote(src.at[part], self.br.at[part], m.sl.at[k], m.rr.at[k], self.at.left)

    def own_core(self, i):
        self.core(i).wait_recv()
        add_in(self.b0.at[i], self.part(i, self.at.core))

    def stage1(self):
        for i in range(2):
            self.own_core(i)
        self.one().start()

    def arrived(self):
        self.one().wait_recv()
        add_in(self.b1, self.b0.at[self.at.x] if self.x_first else self.b0.at[:, :, self.at.y])

    def stage2(self):
        self.arrived()
        self.two().start()

    def stage3(self):
        self.two().wait_recv()
        add_in(self.b2, self.b1.at[:, self.at.y] if self.x_first else self.b1.at[self.at.x])

        @pl.when(self.at.z == 0)
        def _():
            self.rightward(0).start()

        @pl.when(self.at.z == 3)
        def _():
            self.leftward(3).start()

    def stage4(self):
        @pl.when(self.at.z == 1)
        def _():
            self.rightward(0).wait_recv()
            self.bl[2:4] += self.b2[2:4]
            self.rightward(1).start()

        @pl.when(self.at.z == 2)
        def _():
            self.leftward(3).wait_recv()
            self.br[0:2] += self.b2[0:2]
            self.leftward(2).start()

    def stage5(self):
        @pl.when(self.at.z == 2)
        def _():
            self.rightward(1).wait_recv()
            self.bl[3:4] += self.b2[3:4]
            self.rightward(2).start()

        @pl.when(self.at.z == 1)
        def _():
            self.leftward(2).wait_recv()
            self.br[0:1] += self.b2[0:1]
            self.leftward(1).start()

    def stage6(self):
        @pl.when(self.at.z == 3)
        def _():
            self.rightward(2).wait_recv()
            self.put(self.b2[3] + self.bl[3])

        @pl.when(self.at.z == 0)
        def _():
            self.leftward(1).wait_recv()
            self.put(self.b2[0] + self.br[0])

        @pl.when(self.at.z == 1)
        def _():
            self.put(self.b2[1] + self.bl[1] + self.br[1])

        @pl.when(self.at.z == 2)
        def _():
            self.put(self.b2[2] + self.bl[2] + self.br[2])

    def line_sent(self):
        for i in range(4):

            @pl.when(self.at.z == i)
            def _(i=i):
                if i < 3:
                    self.rightward(i).wait_send()
                if i > 0:
                    self.leftward(i).wait_send()


class Reducer:
    def __init__(self, place, n, part, scratch, put):
        self.place, self.n, self.part, self.put = place, n, part, put
        self.c0, self.c1a, self.c1b, self.c2, self.zl, self.zr = scratch[:6]
        self.sems = Sems(scratch[6:16])
        self.pairs = (n + 1) // 2

    @staticmethod
    def scratch(n, rows):
        bufs = [(n, 2, 4, 2), ((n + 1) // 2, 4, 2), (max(n // 2, 1), 2, 4), (n, 4), (n, 4), (n, 4)]
        return [pltpu.VMEM(b + (rows, D), F32) for b in bufs] + Sems.scratch(n)

    def chunk(self, k, parity):
        return Chunk(
            self.place,
            k,
            parity == 0,
            self.sems,
            self.c0.at[k],
            (self.c1b if parity else self.c1a).at[k // 2],
            self.c2.at[k],
            self.zl.at[k],
            self.zr.at[k],
            self.part(k),
            lambda v: self.put(k, v),
        )

    def send(self, first, after):
        def one(k, carry):
            for i in range(2):
                self.chunk(k, 0).core(i).start()
            return carry

        lax.fori_loop(first, after, one, 0)

    def one(self, stage, pair):
        for parity in range(2):
            k = 2 * pair + parity
            k = jnp.int32(k) if isinstance(k, int) else k

            @pl.when(jnp.logical_and(k >= 0, k < self.n))
            def _(k=k, parity=parity):
                getattr(self.chunk(k, parity), f"stage{stage}")()

    def early(self, pair):
        self.one(1, pair)

    def step(self, tau):
        self.one(1, tau)
        for stage in range(2, 7):
            self.one(stage, tau - stage)

    def finish(self):
        def one(k, carry):
            for parity in range(2):

                @pl.when(lax.rem(k, 2) == parity)
                def _(parity=parity):
                    c = self.chunk(k, parity)
                    for i in range(2):
                        c.core(i).wait_send()
                    c.one().wait_send()
                    c.two().wait_send()
                    c.line_sent()

            return carry

        lax.fori_loop(0, self.n, one, 0)


class SmallSum:
    def __init__(self, place, S, bufs, send, recv, put):
        self.at, self.S, self.send, self.recv, self.put = place, S, send, recv, put
        self.d0, self.d1, self.d2, self.dl, self.dr, self.t1, self.t2, self.t3, self.fl, self.fr = bufs

    @staticmethod
    def scratch():
        return [pltpu.VMEM((8, D), F32)] * 10 + [pltpu.SemaphoreType.DMA((5,)), pltpu.SemaphoreType.DMA((5,))]

    def hop(self, src, dst, i, d):
        return remote(src, dst, self.send.at[i], self.recv.at[i], d)

    def core(self):
        return self.hop(self.S, self.d0, 0, self.at.peer)

    def along_x(self):
        return self.hop(self.t1, self.d1, 1, self.at.xn)

    def along_y(self):
        return self.hop(self.t2, self.d2, 2, self.at.yn)

    def rightward(self, i):
        return self.hop(self.t3 if i == 0 else self.fl, self.dl, 3, self.at.right)

    def leftward(self, i):
        return self.hop(self.t3 if i == 3 else self.fr, self.dr, 4, self.at.left)

    def stage1(self):
        self.core().wait_recv()
        self.t1[...] = self.S[...] + self.d0[...]
        self.along_x().start()

    def stage2(self):
        self.along_x().wait_recv()
        self.t2[...] = self.t1[...] + self.d1[...]
        self.along_y().start()

    def stage3(self):
        self.along_y().wait_recv()
        self.t3[...] = self.t2[...] + self.d2[...]

        @pl.when(self.at.z == 0)
        def _():
            self.rightward(0).start()

        @pl.when(self.at.z == 3)
        def _():
            self.leftward(3).start()

    def from_left(self, i):
        self.rightward(i).wait_recv()
        self.fl[...] = self.dl[...] + self.t3[...]

    def from_right(self, i):
        self.leftward(i).wait_recv()
        self.fr[...] = self.dr[...] + self.t3[...]

    def stage4(self):
        @pl.when(self.at.z == 1)
        def _():
            self.from_left(0)
            self.rightward(1).start()

        @pl.when(self.at.z == 2)
        def _():
            self.from_right(3)
            self.leftward(2).start()

    def stage5(self):
        @pl.when(self.at.z == 2)
        def _():
            self.from_left(1)
            self.rightward(2).start()

        @pl.when(self.at.z == 1)
        def _():
            self.from_right(2)
            self.leftward(1).start()

    def stage6(self):
        @pl.when(self.at.z == 3)
        def _():
            self.from_left(2)
            self.put(self.fl[...])

        @pl.when(self.at.z == 0)
        def _():
            self.from_right(1)
            self.put(self.fr[...])

        @pl.when(jnp.logical_or(self.at.z == 1, self.at.z == 2))
        def _():
            self.put(self.fl[...] + self.dr[...])

    def finish(self):
        for c in (self.core(), self.along_x(), self.along_y()):
            c.wait_send()
        for i in range(4):

            @pl.when(self.at.z == i)
            def _(i=i):
                if i < 3:
                    self.rightward(i).wait_send()
                if i > 0:
                    self.leftward(i).wait_send()


def small_outputs(place, counts, outs, tot):
    ga, gi, gf, gh, means = outs

    def put(v):
        tot[...] = v
        d = place.p * RUNS + place.s
        for i, ref in enumerate((ga, gi, gf)):
            ref[...] = pltpu.roll(tot[i : i + 1, :], D - PIECE * d, 1)[:, :PIECE]
        row = tot[pl.ds(3 + d // 8, 1), :]
        gh[...] = pltpu.roll(row, D - 4 * PIECE * lax.rem(d, 8), 1)[:, : 4 * PIECE]
        lane = lax.broadcasted_iota(jnp.int32, (1, 128), 1)
        scale = jnp.full((1, 128), counts[0], F32)
        for i in range(1, PATTERNS):
            scale = jnp.where(lane == i, counts[i], scale)
        means[...] = (tot[7:8, :128] / scale)[:, :PATTERNS]

    return put


N_PIECES = 9
SUB = 8


def finish_kernel(counts, rec, x_ref, dy1_ref, w_hbm, ga1, S_in, gx, g_qkv, ga, gi, gf, gh, means, dqkv, lhs, th, tl, r_hi, r_lo, tiles, S, tot, gx2, w, wsem, *scratch):
    fetch = pltpu.make_async_copy(w_hbm, w, wsem)
    fetch.start()
    place = Place()
    barrier = pltpu.get_barrier_semaphore()
    expected = place.greet(barrier)
    for j in range(HEADS // 2):
        u, v = rec[2 * j, ROWS:PACK, :], rec[2 * j + 1, ROWS:PACK, :]
        cols = slice(128 * j, 128 * j + 128)
        dqkv[0:HALF, cols] = pick(u, swap(v))
        dqkv[HALF:ROWS, cols] = pick(swap(u), v)
        u, v = rec[2 * j, 0:ROWS, :], rec[2 * j + 1, 0:ROWS, :]
        dqkv[:, D + 128 * j : D + 128 * j + 128] = pick(u, swap(v))
        dqkv[:, 2 * D + 128 * j : 2 * D + 128 * j + 128] = pick(swap(u), v)
    gain = ga1[...][None, :]
    n, rs = normed(x_ref[...])
    put_turned(th, tl, n * gain)

    def part(k):
        rows = pl.ds(pl.multiple_of(lax.rem(k, 3) * SUB, SUB), SUB)
        return lambda i, c: tiles.at[k // 3, i, c, :, :, rows, :]

    def put(k, v):
        g_qkv[
            pl.ds(pl.multiple_of(lax.rem(k, 3) * SUB, SUB), SUB), pl.ds(pl.multiple_of((k // 3) * D, D), D)
        ] = v

    n_r = 16
    big = Reducer(place, N_PIECES, part, scratch[:n_r], put)
    rest = scratch[n_r:]
    small = SmallSum(
        place, S, rest[:10], rest[10], rest[11], small_outputs(place, counts, (ga, gi, gf, gh, means), tot)
    )

    def tile_of(j, carry):
        r_hi[...], r_lo[...] = split(dqkv[:, pl.ds(pl.multiple_of(D * j, D), D)])

        def one(i, inner):
            rows = pl.ds(pl.multiple_of(i * 2 * ROWS, 128), 2 * ROWS)
            h, l = th[rows, :], tl[rows, :]
            v = dot_nn(h, r_hi[...]) + dot_nn(h, r_lo[...]) + dot_nn(l, r_hi[...])
            tiles[j, i] = v.reshape(2, 4, 2, PIECE, D)
            return inner

        lax.fori_loop(0, 2, one, 0)

        @pl.when(j == 0)
        def _():
            pl.semaphore_wait(barrier, expected)

        big.send(3 * j, 3 * j + 3)

        @pl.when(j > 0)
        def _():
            big.early(j - 1)

        return carry

    lax.fori_loop(0, 3, tile_of, 0)
    gx2[...] = jnp.zeros_like(gx2)
    fetch.wait()

    def back(j, carry):
        cols = pl.ds(pl.multiple_of(D * j, D), D)
        put_split(lhs, dqkv[:, cols])
        gx2[...] += halves_sum(dot_nt(lhs[...], w[:, cols]))
        return carry

    lax.fori_loop(0, 3, back, 0)
    e = gx2[...]
    S[...] = S_in[...]
    S[0:1, :] = jnp.sum(e * n, 0, keepdims=True)
    small.core().start()
    gx[...] = (dy1_ref[...] + norm_back(e * gain, n, rs)).reshape(ROWS, 1, D)
    small.stage1()

    def step(tau, carry):
        for stage in range(2, 7):

            @pl.when(tau == stage + 1)
            def _(stage=stage):
                getattr(small, f"stage{stage}")()

        big.step(tau)
        return carry

    lax.fori_loop(2, big.pairs + 6, step, 0)

    big.finish()
    small.finish()


def finish(rec, x, dy1, w, ga, S, counts, cid):
    return pl.pallas_call(
        functools.partial(finish_kernel, counts),
        out_shape=[jax.ShapeDtypeStruct((ROWS, 1, D), F32), jax.ShapeDtypeStruct((PIECE, 3 * D), F32)]
        + [jax.ShapeDtypeStruct((1, n), F32) for n in (PIECE, PIECE, PIECE, 4 * PIECE, PATTERNS)],
        in_specs=[VM, VM, VM, ANY, VM, VM],
        out_specs=[VM] * 7,
        scratch_shapes=[
            pltpu.VMEM((ROWS, 3 * D), F32),
            pltpu.VMEM((2 * ROWS, D), BF16),
            pltpu.VMEM((D, ROWS), BF16),
            pltpu.VMEM((D, ROWS), BF16),
            pltpu.VMEM((ROWS, D), BF16),
            pltpu.VMEM((ROWS, D), BF16),
            pltpu.VMEM((3, 2, 2, 4, 2, PIECE, D), F32),
            pltpu.VMEM((8, D), F32),
            pltpu.VMEM((8, D), F32),
            pltpu.VMEM((ROWS, D), F32),
            pltpu.VMEM((D, 3 * D), BF16),
            pltpu.SemaphoreType.DMA,
        ]
        + Reducer.scratch(N_PIECES, SUB)
        + SmallSum.scratch(),
        compiler_params=params(collective_id=cid, has_side_effects=True),
    )(rec, x, dy1, w, ga, S)


def deliver_kernel(*refs):
    n = len(refs) // 2
    for src, dst in zip(refs[:n], refs[n:]):
        dst[...] = src[...]


def deliver(*arrays):
    return pl.pallas_call(
        deliver_kernel,
        out_shape=[jax.ShapeDtypeStruct(v.shape, v.dtype) for v in arrays],
        in_specs=[VM] * len(arrays),
        out_specs=[VM] * len(arrays),
        compiler_params=params(),
    )(*arrays)


def rows_from_pairs(rec, dst):
    for j in range(HEADS // 2):
        u, v = rec[2 * j], rec[2 * j + 1]
        cols = slice(128 * j, 128 * j + 128)
        dst[0:HALF, cols] = pick(u, swap(v))
        dst[HALF:ROWS, cols] = pick(swap(u), v)


def pairs_from_rows(src, dst):
    for j in range(HEADS // 2):
        top = src[0:HALF, 128 * j : 128 * j + 128]
        bottom = src[HALF:ROWS, 128 * j : 128 * j + 128]
        dst[2 * j] = pick(top, swap(bottom))
        dst[2 * j + 1] = pick(swap(top), bottom)


def halves_sum(r):
    return r[:ROWS] + r[ROWS:]


def norm_back(f, n, rs):
    return (f - jnp.mean(f, -1, keepdims=True) - n * jnp.mean(f * n, -1, keepdims=True)) * rs


def put_turned(hi_ref, lo_ref, v):
    for j in range(D // 128):
        t = v[:, 128 * j : 128 * j + 128].T
        hi, lo = split(t)
        hi_ref[128 * j : 128 * j + 128, :] = hi
        lo_ref[128 * j : 128 * j + 128, :] = lo


class ToHeads:
    def __init__(self, pk, rec, send, recv):
        self.pk, self.rec, self.send, self.recv = pk, rec, send, recv
        self.facts = place_facts()

    def greet(self):
        p, s, x, core, active, head = self.facts
        barrier = pltpu.get_barrier_semaphore()

        @pl.when(active)
        def _():
            def one(m, carry):
                q, t = home_device(core, m)

                @pl.when(jnp.logical_not(same(p, s, q, t)))
                def _():
                    pl.semaphore_signal(barrier, inc=1, device_id=to(q, t), device_id_type=MESH)

                return carry

            lax.fori_loop(0, HOMES, one, 0)

    def copy(self, h):
        p, s, x, core, active, head = self.facts
        slot = s * 2 + core
        q, t = head_device(h, x)
        far = pltpu.make_async_remote_copy(
            src_ref=self.pk.at[h],
            dst_ref=self.rec.at[slot],
            send_sem=self.send.at[h],
            recv_sem=self.recv.at[slot],
            device_id=to(q, t),
            device_id_type=MESH,
        )
        return same(p, s, q, t), lambda: pltpu.make_async_copy(self.pk.at[h], self.rec.at[slot], self.recv.at[slot]), far

    def wait(self, others):
        p, s, x, core, active, head = self.facts
        mine = jnp.logical_and(active, core == x).astype(jnp.int32)
        pl.semaphore_wait(pltpu.get_barrier_semaphore(), HEADS + others - mine)

    def start(self):
        p, s, x, core, active, head = self.facts

        def one(j, carry):
            here, near, far = self.copy(lax.rem(j + 3 * (s // 2) + 2 * p, HEADS))

            @pl.when(here)
            def _():
                near().start()

            @pl.when(jnp.logical_not(here))
            def _():
                far.start()

            return carry

        lax.fori_loop(0, HEADS, one, 0)

    def finish(self):
        active = self.facts[4]

        @pl.when(active)
        def _():
            def arrive(m, carry):
                pltpu.make_async_copy(self.rec.at[m], self.rec.at[m], self.recv.at[m]).wait()
                return carry

            lax.fori_loop(0, HOMES, arrive, 0)

        def sent(h, carry):
            here, near, far = self.copy(h)

            @pl.when(jnp.logical_not(here))
            def _():
                far.wait_send()

            return carry

        lax.fori_loop(0, HEADS, sent, 0)


FT = 1024


def product(hi, lo, r_hi, r_lo, put):
    def one(i, carry):
        rows = pl.ds(pl.multiple_of(i * 2 * ROWS, 128), 2 * ROWS)
        h, l = hi[rows, :], lo[rows, :]
        put(i, dot_nn(h, r_hi[...]) + dot_nn(h, r_lo[...]) + dot_nn(l, r_hi[...]))
        return carry

    lax.fori_loop(0, 2, one, 0)


N_FF = 9
N_COLS = 5


def ff_kernel(rec, x_ref, g3, wo_hbm, wu_hbm, wd_hbm, gi1, gf1, gh1, sums, out3, drec, dy1_ref, S, C0, C1a, C1b, dap, lhs, lhs2, gi, gf, gh, gh_g, g_ref, out_ref, V, N1, U, GP, E, ACC, th, tl, r_hi, r_lo, cols_t, rows_t, c0, c1a, c1b, osem, wo, wu, wd, wsem, dsend, drecv, *rsems):
    place = Place()
    sems = Sems(rsems)
    fetch = [
        pltpu.make_async_copy(src, dst, wsem.at[i])
        for i, (src, dst) in enumerate(((wo_hbm, wo), (wu_hbm, wu), (wd_hbm, wd)))
    ]
    for c in fetch:
        c.start()
    travel = ToHeads(dap, drec, dsend, drecv)
    travel.greet()
    place.greet(pltpu.get_barrier_semaphore(), False)

    def chunk(k, part=None):
        if not isinstance(k, int):
            return Chunk(place, k, True, sems, c0.at[k], part=part)
        x_first = k % 2 == 0
        b1 = None if k < N_COLS else (c1a if x_first else c1b).at[(k - N_COLS) // 2]
        return Chunk(place, k, x_first, sems, c0.at[k], b1, part=part)

    for wide, flat in ((gi, gi1), (gf, gf1), (gh, gh1)):
        wide[...] = flat[...][None, :]
    g_ref[...] = g3[...].reshape(ROWS, D)
    rows_from_pairs(rec, V)
    na, rs_a = normed(V[...])
    V[...] = na
    put_split(lhs, na * gi[...])
    fetch[0].wait()

    def project(j, carry):
        cols = pl.ds(pl.multiple_of(256 * j, 256), 256)
        N1[:, cols] = x_ref[:, cols] + halves_sum(dot_nn(lhs[...], wo[:, cols]))
        return carry

    lax.fori_loop(0, 3, project, 0)
    y1 = N1[...]
    out_ref[...] = y1
    ny, rs_y = normed(y1)
    N1[...] = ny
    put_split(lhs, ny * gf[...])
    fetch[1].wait()

    def up(j, su):
        cols = pl.ds(pl.multiple_of(j * FT, FT), FT)
        z = halves_sum(dot_nn(lhs[...], wu[:, cols]))
        phi = 0.5 * (1.0 + lax.erf(z * math.sqrt(0.5)))
        u = z * phi
        U[:, cols] = u
        GP[:, cols] = phi + z * jnp.exp(-0.5 * z * z) * (1.0 / math.sqrt(2.0 * math.pi))
        return su + jnp.sum(u, -1, keepdims=True)

    zero = jnp.zeros((ROWS, 1), F32)
    mean = lax.fori_loop(0, FF // FT, up, zero) * (1.0 / FF)

    def spread(j, sv):
        cols = pl.ds(pl.multiple_of(j * FT, FT), FT)
        c = U[:, cols] - mean
        return sv + jnp.sum(c * c, -1, keepdims=True)

    rs_u = lax.rsqrt(lax.fori_loop(0, FF // FT, spread, zero) * (1.0 / FF) + LN_EPSILON)
    ACC[...] = jnp.zeros_like(ACC)
    fetch[2].wait()

    def lower(j, carry):
        cols = pl.ds(pl.multiple_of(j * FT, FT), FT)
        n = (U[:, cols] - mean) * rs_u
        U[:, cols] = n
        put_split(lhs2, n * gh[:, cols])
        ACC[...] += halves_sum(dot_nn(lhs2[...], wd[cols, :]))
        return carry

    lax.fori_loop(0, FF // FT, lower, 0)
    out3[...] = (out_ref[...] + ACC[...]).reshape(ROWS, 1, D)

    travel.wait(3)
    r_hi[...], r_lo[...] = split(g_ref[...])

    def down(j, q):
        return chunk(N_COLS + q, lambda i, c: rows_t.at[lax.rem(j, 2), :, :, q])

    def down_step(j, carry):
        @pl.when(j < 4)
        def _():
            cols = pl.ds(pl.multiple_of(D * j, D), D)
            put_turned(th, tl, U[:, cols] * gh[:, cols])
            sent = place.core != lax.rem(j, 2)

            @pl.when(jnp.logical_and(j >= 2, sent))
            def _():
                for q in range(4):
                    down(j - 2, q).core(j // 2 - 1).wait_send()

            def put(i, v):
                rows_t[lax.rem(j, 2), pl.ds(2 * i, 2)] = v.reshape(2, 2, 4, PIECE, D)

            product(th, tl, r_hi, r_lo, put)

            @pl.when(sent)
            def _():
                for q in range(4):
                    down(j, q).core(j // 2).start()

        @pl.when(jnp.logical_and(j > 0, place.core == lax.rem(j + 1, 2)))
        def _():
            for q in range(4):
                down(j - 1, q).own_core((j - 1) // 2)

        return carry

    lax.fori_loop(0, 5, down_step, 0)
    for k in range(N_COLS, N_FF):
        chunk(k).one().start()

    put_split(lhs, g_ref[...])

    def back_down(j, sums):
        cols = pl.ds(pl.multiple_of(j * FT, FT), FT)
        e = halves_sum(dot_nt(lhs[...], wd[cols, :]))
        n = U[:, cols]
        gh_g[:, cols] = jnp.sum(e * n, 0, keepdims=True)
        f = e * gh[:, cols]
        E[:, cols] = f
        return sums[0] + jnp.sum(f, -1, keepdims=True), sums[1] + jnp.sum(f * n, -1, keepdims=True)

    sf, sfn = lax.fori_loop(0, FF // FT, back_down, (zero, zero))
    mf, mfn = sf * (1.0 / FF), sfn * (1.0 / FF)
    ACC[...] = jnp.zeros_like(ACC)

    def back_up(j, carry):
        cols = pl.ds(pl.multiple_of(j * FT, FT), FT)
        dz = (E[:, cols] - mf - U[:, cols] * mfn) * rs_u * GP[:, cols]
        E[:, cols] = dz
        put_split(lhs2, dz)
        ACC[...] += halves_sum(dot_nt(lhs2[...], wu[:, cols]))
        return carry

    lax.fori_loop(0, FF // FT, back_up, 0)
    e = ACC[...]
    ny = N1[...]
    S[2:3, :] = jnp.sum(e * ny, 0, keepdims=True)
    dy1 = g_ref[...] + norm_back(e * gf[...], ny, rs_y)
    dy1_ref[...] = dy1
    put_split(lhs, dy1)

    def project_back(j, carry):
        cols = pl.ds(pl.multiple_of(256 * j, 256), 256)
        ACC[:, cols] = halves_sum(dot_nt(lhs[...], wo[cols, :]))
        return carry

    lax.fori_loop(0, 3, project_back, 0)
    e = ACC[...]
    na = V[...]
    S[1:2, :] = jnp.sum(e * na, 0, keepdims=True)
    S[0:1, :] = jnp.zeros((1, D), F32)
    for j in range(4):
        S[3 + j : 4 + j, :] = gh_g[:, D * j : D * j + D]
    lane = lax.broadcasted_iota(jnp.int32, (1, 128), 1)
    S[7:8, :] = jnp.zeros((1, D), F32)
    S[7:8, 0:128] = sum(jnp.where(lane == i, sums[i : i + 1, :], 0.0) for i in range(PATTERNS))
    ACC[...] = norm_back(e * gi[...], na, rs_a)
    pairs_from_rows(ACC, dap)
    travel.start()

    def column(k):
        return chunk(k, lambda i, c: cols_t.at[lax.rem(k, 2), i, c])

    def out_copy(k):
        return pltpu.make_async_copy(c0.at[k], C0.at[k], osem.at[k])

    put_turned(th, tl, na * gi[...])
    r_hi[...], r_lo[...] = split(dy1)

    def column_step(k, carry):
        @pl.when(k < N_COLS)
        def _():
            @pl.when(k >= 2)
            def _():
                for i in range(2):
                    column(k - 2).core(i).wait_send()

            @pl.when(k >= 1)
            def _():
                r_hi[...], r_lo[...] = split(E[:, pl.ds(pl.multiple_of(D * (k - 1), D), D)])

            def put(i, v):
                cols_t[lax.rem(k, 2), i] = v.reshape(2, 4, 2, PIECE, D)

            product(th, tl, r_hi, r_lo, put)
            for i in range(2):
                column(k).core(i).start()

            @pl.when(k == 0)
            def _():
                put_turned(th, tl, N1[...] * gf[...])

        @pl.when(k > 0)
        def _():
            for i in range(2):
                column(k - 1).own_core(i)
            out_copy(k - 1).start()

        return carry

    lax.fori_loop(0, N_COLS + 1, column_step, 0)

    def c1_copy(k):
        b1, out = (c1a, C1a) if k % 2 == 0 else (c1b, C1b)
        i = (k - N_COLS) // 2
        return pltpu.make_async_copy(b1.at[i], out.at[i], osem.at[k])

    for k in range(N_COLS, N_FF):
        chunk(k).arrived()
        c1_copy(k).start()
    travel.finish()
    for k in range(N_COLS - 2, N_COLS):
        for i in range(2):
            column(jnp.int32(k)).core(i).wait_send()
    for j in range(2, 4):

        @pl.when(place.core != j % 2)
        def _(j=j):
            for q in range(4):
                down(jnp.int32(j), q).core(j // 2).wait_send()

    for k in range(N_COLS):
        out_copy(k).wait()
    for k in range(N_COLS, N_FF):
        chunk(k).one().wait_send()
        c1_copy(k).wait()


def feed_forward(rec, x, g, wo, wu, wd, gi, gf, gh, sums):
    act = jax.ShapeDtypeStruct((ROWS, D), F32)
    wide = pltpu.VMEM((ROWS, FF), F32)
    thin = pltpu.VMEM((ROWS, D), F32)
    return pl.pallas_call(
        ff_kernel,
        out_shape=[
            jax.ShapeDtypeStruct((ROWS, 1, D), F32),
            jax.ShapeDtypeStruct((HOMES, HALF, 128), F32),
            act,
            jax.ShapeDtypeStruct((8, D), F32),
            jax.ShapeDtypeStruct((N_COLS, 2, 4, 2, PIECE, D), F32),
            jax.ShapeDtypeStruct((2, 4, 2, PIECE, D), F32),
            jax.ShapeDtypeStruct((2, 2, 4, PIECE, D), F32),
        ],
        in_specs=[VM, VM, VM, ANY, ANY, ANY] + [VM] * 4,
        out_specs=[VM, ANY, VM, VM, ANY, ANY, ANY],
        scratch_shapes=[
            pltpu.VMEM((HEADS, HALF, 128), F32),
            pltpu.VMEM((2 * ROWS, D), BF16),
            pltpu.VMEM((2 * ROWS, FT), BF16),
            pltpu.VMEM((1, D), F32),
            pltpu.VMEM((1, D), F32),
            pltpu.VMEM((1, FF), F32),
            pltpu.VMEM((1, FF), F32),
            thin,
            thin,
            thin,
            thin,
            wide,
            wide,
            wide,
            thin,
        ]
        + [
            pltpu.VMEM((D, ROWS), BF16),
            pltpu.VMEM((D, ROWS), BF16),
            pltpu.VMEM((ROWS, D), BF16),
            pltpu.VMEM((ROWS, D), BF16),
            pltpu.VMEM((2, 2, 2, 4, 2, PIECE, D), F32),
            pltpu.VMEM((2, 4, 2, 4, PIECE, D), F32),
            pltpu.VMEM((N_FF, 2, 4, 2, PIECE, D), F32),
            pltpu.VMEM((2, 4, 2, PIECE, D), F32),
            pltpu.VMEM((2, 2, 4, PIECE, D), F32),
            pltpu.SemaphoreType.DMA((N_FF,)),
            pltpu.VMEM((D, D), BF16),
            pltpu.VMEM((D, FF), BF16),
            pltpu.VMEM((FF, D), BF16),
            pltpu.SemaphoreType.DMA((3,)),
            pltpu.SemaphoreType.DMA((HEADS,)),
            pltpu.SemaphoreType.DMA((HOMES,)),
        ]
        + Sems.scratch(N_FF),
        compiler_params=params(collective_id=4, has_side_effects=True),
    )(rec, x, g, wo, wu, wd, gi, gf, gh, sums)


def back_all_kernel(offs, drec, own, sib, ap, lse, C0, C1a, C1b, grec, wo_g, up_g, down_g, qst, kc, vc, kt, qc, dc, lt, k4, v4, kt4, q4, d4, lt4, k5, v5, kt5, q5, d5, lt5, dk, dv, dq, dk4, dv4, dk5, dv5, dq4, dq5, b1, b2, b3, b4, dqt, ds_out, came, lsem, send, recv, qsend, qrecv, fsend, frecv, c0, c1a, c1b, c2, zl, zr, csem, *rsems):
    place = Place()
    p, s, x, core, active, head = place_facts()
    b = core
    o2, o3, o4, o5 = (offs[i, head] for i in range(1, PATTERNS))
    kvf, qf, X, df = dk, dv.at[0:2], dv.at[2:4], dq
    dqp = qst

    barrier = pltpu.get_barrier_semaphore()
    expected = place.greet(barrier)

    def greet_heads(h, carry):
        q, t = head_device(h, x)

        @pl.when(jnp.logical_not(same(p, s, q, t)))
        def _():
            pl.semaphore_signal(barrier, inc=1, device_id=to(q, t), device_id_type=MESH)

        return carry

    lax.fori_loop(0, HEADS, greet_heads, 0)
    from_homes = HOMES - (core == x).astype(jnp.int32)
    pl.semaphore_wait(barrier, expected + active.astype(jnp.int32) * from_homes)

    def put(k, v):
        @pl.when(k == 0)
        def _():
            wo_g[...] = v

        @pl.when(jnp.logical_and(k > 0, k < 5))
        def _():
            up_g[:, pl.ds(pl.multiple_of((k - 1) * D, D), D)] = v

        @pl.when(k >= 5)
        def _():
            down_g[pl.ds(pl.multiple_of((k - 5) * PIECE, PIECE), PIECE), :] = v

    sems = Sems(rsems)

    def chunk(k):
        x_first = k % 2 == 0
        b0 = c0.at[k] if k < N_COLS else None
        b1 = (c1a if x_first else c1b).at[k // 2]
        return Chunk(
            place, k, x_first, sems, b0, b1, c2.at[k], zl.at[k], zr.at[k], put=lambda v: put(jnp.int32(k), v)
        )

    def load(k):
        if k < N_COLS:
            return pltpu.make_async_copy(C0.at[k], c0.at[k], csem.at[k])
        src, dst = (C1a, c1a) if k % 2 == 0 else (C1b, c1b)
        return pltpu.make_async_copy(src.at[(k - N_COLS) // 2], dst.at[k // 2], csem.at[k])

    PAIRS = ((5, 6), (7, 8), (0, 1), (2, 3), (4,))

    def reduction(*todo):
        for stage, pair in todo:
            for k in PAIRS[pair]:
                if stage == 1:
                    load(k).wait()
                    chunk(k).one().start()
                elif stage == 2 and k >= N_COLS:
                    load(k).wait()
                    chunk(k).two().start()
                else:
                    getattr(chunk(k), f"stage{stage}")()


    def local_copies(m):
        t = pl.multiple_of((m // 2) * ROWS, 64)
        c, d = 2 * b + lax.rem(m, 2), 2 * (1 - b) + lax.rem(m, 2)
        return [
            pltpu.make_async_copy(own.at[m, pl.ds(0, ROWS), :], kvf.at[c, pl.ds(t, ROWS), :], lsem.at[m, 0]),
            pltpu.make_async_copy(sib.at[m], kvf.at[d, pl.ds(t, ROWS), :], lsem.at[m, 1]),
            pltpu.make_async_copy(own.at[m, pl.ds(ROWS, HALF), :], qst.at[m], lsem.at[m, 2]),
        ]

    lse_copy = pltpu.make_async_copy(lse, X, lsem.at[HOMES, 0])

    @pl.when(active)
    def _():
        lse_copy.start()

        def start(m, carry):
            for c in local_copies(m):
                c.start()
            return carry

        lax.fori_loop(0, HOMES, start, 0)

    for pair in PAIRS:
        for k in pair:
            load(k).start()
    reduction((2, 0), (1, 2), (2, 1))

    @pl.when(active)
    def _():
        b1[0] = key_bias((2, 128), (4, 128), 4, 1, 2 * b, True)
        b2[0] = key_bias((1, 256), (2, 256), 4, 2, 2 * b, True)
        b3[0] = key_bias((1, 256), (1, 256), 1, 1, 0, True)
        e4 = class_facts4(o4, b)[1]
        b4[0] = key_bias((1, 256), (2, 256), 12, 6, 6 * e4, True)
        for ref in (b1, b2, b3, b4):
            ref[1] = jnp.zeros(ref.shape[1:], F32)

        def wait(m, carry):
            for c in local_copies(m):
                c.wait()
            return carry

        lax.fori_loop(0, HOMES, wait, 0)
        lse_copy.wait()
        unpack_pairs(qst, 0, qf, 1.0 / math.sqrt(HD))

        def prepare(i, carry):
            c, t = i // 12, pl.multiple_of(lax.rem(i, 12) * 128, 128)
            k2, v2 = keys_and_values(kvf[c, pl.ds(t, 128), :])
            kc[c, pl.ds(t, 128), :] = k2.astype(BF16)
            vc[c, pl.ds(t, 128), :] = v2.astype(BF16)
            kt[c, :, pl.ds(t, 128)] = k2.T.astype(BF16)
            return carry

        lax.fori_loop(0, 48, prepare, 0)

        def prepare_q(i, carry):
            c, t = i // 12, pl.multiple_of(lax.rem(i, 12) * 128, 128)
            qc[c, pl.ds(t, 128), :] = query_quads(qf[c, pl.ds(t, 128), :])
            return carry

        lax.fori_loop(0, 24, prepare_q, 0)

    keys4, e4, (qc4, qv4) = class_facts4(o4, b)
    kc5, kv5 = lax.rem(o5, 4), o5 // 4
    qi4, qi5 = qc4 - 2 * b, lax.rem(kc5, 2)

    @pl.when(active)
    def _():
        for blk in range(4):
            r = slice(128 * blk, 128 * blk + 128)
            for e in range(2):
                c, v = keys4[e]
                k2, v2 = keys_and_values(kvf[c, pl.ds(v + 384 * blk, 128, stride=3), :])
                k4[e, r, :] = k2.astype(BF16)
                v4[e, r, :] = v2.astype(BF16)
                kt4[e, :, r] = k2.T.astype(BF16)
            q4[r, :] = query_quads(qf[qi4, pl.ds(qv4 + 384 * blk, 128, stride=3), :])
            rows = pl.ds(kv5 + 384 * blk, 128, stride=3)
            k2, v2 = keys_and_values(kvf[kc5, rows, :])
            k5[r, :] = k2.astype(BF16)
            v5[r, :] = v2.astype(BF16)
            kt5[:, r] = k2.T.astype(BF16)
            q5[r, :] = query_quads(qf[qi5, rows, :])
        dk[...] = jnp.zeros_like(dk)

    reduction((1, 3))

    @pl.when(active)
    def _():
        unpack_pairs(drec, 0, df, 1.0)

        def facts(m, carry):
            ci = lax.rem(m, 2)
            t = pl.multiple_of((m // 2) * ROWS, 32)
            prod = drec[m] * ap[m]
            low = lower_lanes(prod)
            d0 = jnp.sum(jnp.where(low, prod, 0.0), -1, keepdims=True)
            d1 = jnp.sum(jnp.where(low, 0.0, prod), -1, keepdims=True)
            for part, d in ((0, d0), (1, d1)):
                rows = pl.ds(t + HALF * part, HALF)
                l = X[ci, rows, :]
                X[ci, rows, :] = jnp.where(low, l, jnp.broadcast_to(d, l.shape))
            return carry

        lax.fori_loop(0, HOMES, facts, 0)

        def turned(v):
            w = v.T
            return jnp.concatenate([w[0:1, :], w[HD : HD + 1, :]], 0)

        def prepare_d(i, carry):
            c, t = i // 12, pl.multiple_of(lax.rem(i, 12) * 128, 128)
            rows = pl.ds(t, 128)
            dc[c, rows, :] = query_quads(df[c, rows, :])
            lt[i] = turned(X[c, rows, :])
            return carry

        lax.fori_loop(0, 24, prepare_d, 0)
        for blk in range(4):
            r = slice(128 * blk, 128 * blk + 128)
            rows = pl.ds(qv4 + 384 * blk, 128, stride=3)
            d4[r, :] = query_quads(df[qi4, rows, :])
            lt4[blk] = turned(X[qi4, rows, :])
            rows = pl.ds(kv5 + 384 * blk, 128, stride=3)
            d5[r, :] = query_quads(df[qi5, rows, :])
            lt5[blk] = turned(X[qi5, rows, :])
        dv[...] = jnp.zeros_like(dv)
        dq[...] = jnp.zeros_like(dq)

    def tile(k, v, kT, q, d, facts_pair, bias):
        s_ = dot_nt(doubled(k), q) + bias
        l0, l1 = facts_pair
        row = jnp.concatenate([l0[0:1, :], l1[0:1, :]], 1)
        delta = jnp.concatenate([l0[1:2, :], l1[1:2, :]], 1)
        pr = jnp.exp(s_ - row)
        ds = pr * (dot_nt(doubled(v), d) - delta)
        hi, lo = split(pr)
        d2, q2_ = d[:, :128], q[:, :128]
        dv_new = dot_nn(jnp.concatenate([hi, lo], 1), jnp.concatenate([d2, d2], 0))
        hi, lo = split(ds)
        dk_new = dot_nn(jnp.concatenate([hi, lo], 1), jnp.concatenate([q2_, q2_], 0))
        dqt[...] += dot_nn(doubled(kT), jnp.concatenate([hi, lo], 0))
        return dk_new, dv_new

    def kept(flag, v):
        return jnp.where(flag, v, 0.0)

    def at256(blk):
        return pl.ds(pl.multiple_of(256 * blk, 128), 256)

    def sweep(first, last, step, done):
        dqt[...] = jnp.zeros_like(dqt)

        def one(kb, carry):
            step(kb, jnp.where(kb == last, 0, 1))
            return carry

        lax.fori_loop(first, last + 1, one, 0)
        done(dqt[...].T)

    def q2(qb, carry):
        qs = at256(qb)

        def step(kb, which):
            ks = at256(kb)
            a, c = tile(
                jnp.concatenate([kc[o2, ks, :], kc[o2 + 2, ks, :]], 0),
                jnp.concatenate([vc[o2, ks, :], vc[o2 + 2, ks, :]], 0),
                jnp.concatenate([kt[o2, :, ks], kt[o2 + 2, :, ks]], 1),
                qc[o2, qs, :],
                dc[o2, qs, :],
                (lt.at[12 * o2 + 2 * qb], lt.at[12 * o2 + 2 * qb + 1]),
                b2[which],
            )
            for par in range(2):
                f = o2 == par
                dk[par, ks, :] += kept(f, a[:256])
                dk[par + 2, ks, :] += kept(f, a[256:])
                dv[par, ks, :] += kept(f, c[:256])
                dv[par + 2, ks, :] += kept(f, c[256:])

        def done(e):
            for par in range(2):
                dq[par, qs, :] += kept(o2 == par, e)

        sweep(jnp.where(qb >= 4, 4, 0), qb, step, done)
        return carry

    @pl.when(active)
    def _():
        lax.fori_loop(0, TOTAL // 256, q2, 0)

    reduction((3, 0), (3, 1), (2, 2), (1, 4))

    def q3(qb, carry):
        ci = lax.rem(o3, 2)
        qs = at256(qb)

        def step(kb, which):
            ks = at256(kb)
            a, c = tile(
                kc[o3, ks, :],
                vc[o3, ks, :],
                kt[o3, :, ks],
                qc[ci, qs, :],
                dc[ci, qs, :],
                (lt.at[12 * ci + 2 * qb], lt.at[12 * ci + 2 * qb + 1]),
                b3[which],
            )
            for i in range(2):
                f = o3 == 2 * b + i
                dk[2 * b + i, ks, :] += kept(f, a)
                dv[2 * b + i, ks, :] += kept(f, c)

        def done(e):
            for i in range(2):
                dq[i, qs, :] += kept(o3 == 2 * b + i, e)

        sweep(0, qb, step, done)
        return carry

    def q4_(qb, carry):
        qs = at256(qb)

        def step(kb, which):
            ks = at256(kb)
            a, c = tile(
                k4[:, ks, :].reshape(512, 128),
                v4[:, ks, :].reshape(512, 128),
                jnp.concatenate([kt4[0, :, ks], kt4[1, :, ks]], 1),
                q4[qs, :],
                d4[qs, :],
                (lt4.at[2 * qb], lt4.at[2 * qb + 1]),
                b4[which],
            )
            dk4[:, ks, :] += a.reshape(2, 256, 128)
            dv4[:, ks, :] += c.reshape(2, 256, 128)

        def done(e):
            dq4[qs, :] = e

        sweep(0, qb, step, done)
        return carry

    def q5_(qb, carry):
        qs = at256(qb)

        def step(kb, which):
            ks = at256(kb)
            a, c = tile(
                k5[ks, :], v5[ks, :], kt5[:, ks], q5[qs, :], d5[qs, :], (lt5.at[2 * qb], lt5.at[2 * qb + 1]), b3[which]
            )
            dk5[ks, :] += a
            dv5[ks, :] += c

        def done(e):
            dq5[qs, :] = e

        sweep(0, qb, step, done)
        return carry

    @pl.when(active)
    def _():
        lax.fori_loop(0, TOTAL // 256, q3, 0)

    reduction((4, 0), (4, 1), (2, 3))

    @pl.when(active)
    def _():
        for ref in (dk4, dv4, dk5, dv5):
            ref[...] = jnp.zeros_like(ref)
        lax.fori_loop(0, 2, q4_, 0)
        lax.fori_loop(0, 2, q5_, 0)
        mine5 = kc5 // 2 == b
        for kind in range(12):
            c, rows = kind % 4, pl.ds(kind // 4, THIRD, stride=3)
            f0, f1, f5 = o4 == kind, o4 + 6 == kind, jnp.logical_and(o5 == kind, mine5)
            dk[c, rows, :] += kept(f0, dk4[0]) + kept(f1, dk4[1]) + kept(f5, dk5[...])
            dv[c, rows, :] += kept(f0, dv4[0]) + kept(f1, dv4[1]) + kept(f5, dv5[...])
        for ci in range(2):
            for v in range(3):
                rows = pl.ds(v, THIRD, stride=3)
                f4 = jnp.logical_and(qi4 == ci, qv4 == v)
                f5 = jnp.logical_and(jnp.logical_and(qi5 == ci, kv5 == v), mine5)
                dq[ci, rows, :] += kept(f4, dq4[...]) + kept(f5, dq5[...])

    reduction((5, 0), (5, 1), (3, 2))

    def segment(g):
        def at(blk):
            return pl.ds(pl.multiple_of(512 * g + 128 * blk, 128), 128)

        def one(qb, carry):
            qs = at(qb)

            def step(kb, which):
                ks = at(kb)
                a, c = tile(
                    kc[:, ks, :].reshape(512, 128),
                    vc[:, ks, :].reshape(512, 128),
                    jnp.concatenate([kt[i, :, ks] for i in range(4)], 1),
                    qc[:, qs, :].reshape(256, 256),
                    dc[:, qs, :].reshape(256, 256),
                    (lt.at[4 * g + qb], lt.at[12 + 4 * g + qb]),
                    b1[which],
                )
                dk[:, ks, :] += a.reshape(4, 128, 128)
                dv[:, ks, :] += c.reshape(4, 128, 128)

            def done(e):
                dq[:, qs, :] += e.reshape(2, 128, 128)

            sweep(0, qb, step, done)
            return carry

        lax.fori_loop(0, 4, one, 0)

    def passed(m):
        return remote(ds_out.at[m], came.at[m], fsend.at[m], frecv.at[m], place.peer)

    def home_copies(m):
        q, t = home_device(core, m)
        kv = remote(came.at[m], grec.at[head, pl.ds(0, ROWS), :], send.at[m], recv.at[head], to(q, t))
        dq_ = remote(dqp.at[m], grec.at[head, pl.ds(ROWS, HALF), :], qsend.at[m], qrecv.at[head], to(q, t))
        return q, t, kv, dq_

    def rows_of(m):
        return pl.ds(pl.multiple_of((m // 2) * ROWS, 64), ROWS)

    def kv(c, m):
        k, v = dk[c, rows_of(m), :], dv[c, rows_of(m), :]
        return pick(k + swap(k), v + swap(v))

    def share(m, carry):
        ds_out[m] = kv(2 * (1 - b) + lax.rem(m, 2), m)
        passed(m).start()
        return carry

    def add(m, carry):
        q, t, far_kv, far_q = home_copies(m)
        ci = lax.rem(m, 2)
        v = dq[ci, rows_of(m), :]
        v = (v + swap(v)) * (1.0 / math.sqrt(HD))
        dqp[m] = pick(v[:HALF], v[HALF:])
        passed(m).wait_recv()
        came[m] += kv(2 * b + ci, m)

        @pl.when(same(p, s, q, t))
        def _():
            pltpu.make_async_copy(came.at[m], grec.at[head, pl.ds(0, ROWS), :], recv.at[head]).start()
            pltpu.make_async_copy(dqp.at[m], grec.at[head, pl.ds(ROWS, HALF), :], qrecv.at[head]).start()

        @pl.when(jnp.logical_not(same(p, s, q, t)))
        def _():
            far_kv.start()
            far_q.start()

        return carry

    def round_of(i, carry):
        g = jnp.where(i == 0, 0, 3 - i)

        @pl.when(active)
        def _():
            segment(g)
            lax.fori_loop(jnp.where(i == 0, 0, jnp.where(i == 1, 12, 4)), jnp.where(i == 0, 4, jnp.where(i == 1, 16, 12)), share, 0)

            @pl.when(i > 0)
            def _():
                lax.fori_loop(jnp.where(i == 1, 0, 12), jnp.where(i == 1, 4, 16), add, 0)

        @pl.when(i == 0)
        def _():
            reduction((6, 0), (6, 1), (4, 2), (2, 4))

        @pl.when(i == 1)
        def _():
            reduction((3, 3), (3, 4), (5, 2))

        return carry

    lax.fori_loop(0, 3, round_of, 0)

    @pl.when(active)
    def _():
        lax.fori_loop(4, 12, add, 0)

    reduction((4, 3), (4, 4), (6, 2))
    reduction((5, 3), (5, 4))
    reduction((6, 3), (6, 4))

    def from_head(h, carry):
        a = grec.at[h, pl.ds(0, ROWS), :]
        c = grec.at[h, pl.ds(ROWS, HALF), :]
        pltpu.make_async_copy(a, a, recv.at[h]).wait()
        pltpu.make_async_copy(c, c, qrecv.at[h]).wait()
        return carry

    lax.fori_loop(0, HEADS, from_head, 0)
    for k in range(N_FF):
        if k < N_COLS:
            chunk(k).one().wait_send()
        chunk(k).two().wait_send()
        chunk(k).line_sent()

    @pl.when(active)
    def _():
        def sent(m, carry):
            q, t, far_kv, far_q = home_copies(m)
            passed(m).wait_send()

            @pl.when(jnp.logical_not(same(p, s, q, t)))
            def _():
                far_kv.wait_send()
                far_q.wait_send()

            return carry

        lax.fori_loop(0, HOMES, sent, 0)


def backward_all(offs, drec, own, sib, ap, lse, C0, C1a, C1b, cid):
    dma = pltpu.SemaphoreType.DMA
    keys = pltpu.VMEM((4, TOTAL, 128), BF16)
    full = pltpu.VMEM((4, TOTAL, 128), F32)
    quad = pltpu.VMEM((2, TOTAL, 256), BF16)
    quad3 = pltpu.VMEM((THIRD, 256), BF16)
    pair3 = pltpu.VMEM((THIRD, 128), BF16)
    turned = pltpu.VMEM((128, THIRD), BF16)
    facts3 = pltpu.VMEM((4, 2, 128), F32)
    out3 = pltpu.VMEM((THIRD, 128), F32)
    packs = pltpu.VMEM((HOMES, ROWS, 128), F32)
    halves = pltpu.VMEM((HOMES, HALF, 128), F32)
    return pl.pallas_call(
        back_all_kernel,
        out_shape=[
            jax.ShapeDtypeStruct((HEADS, PACK, 128), F32),
            jax.ShapeDtypeStruct((PIECE, D), F32),
            jax.ShapeDtypeStruct((PIECE, FF), F32),
            jax.ShapeDtypeStruct((4 * PIECE, D), F32),
        ],
        in_specs=[SM, VM, ANY, ANY, VM, ANY, ANY, ANY, ANY],
        out_specs=[ANY, VM, VM, VM],
        scratch_shapes=[
            halves,
            keys,
            keys,
            pltpu.VMEM((4, 128, TOTAL), BF16),
            quad,
            quad,
            pltpu.VMEM((24, 2, 128), F32),
            pltpu.VMEM((2, THIRD, 128), BF16),
            pltpu.VMEM((2, THIRD, 128), BF16),
            pltpu.VMEM((2, 128, THIRD), BF16),
            quad3,
            quad3,
            facts3,
            pair3,
            pair3,
            turned,
            quad3,
            quad3,
            facts3,
            full,
            full,
            pltpu.VMEM((2, TOTAL, 128), F32),
            pltpu.VMEM((2, THIRD, 128), F32),
            pltpu.VMEM((2, THIRD, 128), F32),
            out3,
            out3,
            out3,
            out3,
            pltpu.VMEM((2, 512, 256), F32),
            pltpu.VMEM((2, 512, 256), F32),
            pltpu.VMEM((2, 256, 256), F32),
            pltpu.VMEM((2, 512, 256), F32),
            pltpu.VMEM((128, 256), F32),
            packs,
            packs,
            dma((HOMES + 1, 3)),
            dma((HOMES,)),
            dma((HEADS,)),
            dma((HOMES,)),
            dma((HEADS,)),
            dma((HOMES,)),
            dma((HOMES,)),
            pltpu.VMEM((N_COLS, 2, 4, 2, PIECE, D), F32),
            pltpu.VMEM((5, 4, 2, PIECE, D), F32),
            pltpu.VMEM((4, 2, 4, PIECE, D), F32),
            pltpu.VMEM((N_FF, 4, PIECE, D), F32),
            pltpu.VMEM((N_FF, 4, PIECE, D), F32),
            pltpu.VMEM((N_FF, 4, PIECE, D), F32),
            dma((N_FF,)),
        ]
        + Sems.scratch(N_FF),
        compiler_params=params(collective_id=cid, has_side_effects=True),
    )(offs, drec, own, sib, ap, lse, C0, C1a, C1b)


SEG1, SEG2, SEG3, SEG4, SEG5 = SEGMENTS
DILATION_ONE, DILATION_TWO, DILATION_THREE, DILATION_FOUR, DILATION_FIVE = DILATIONS
MASK_VALUE = -1e30
MATMUL_ACCURACY = lax.Precision.HIGHEST


def passed_along(value, axis, by):
    length = lax.axis_size(axis)
    return lax.ppermute(value, axis, [(i, (i + by) % length) for i in range(length)])


def run_is_live(distance, anchor_point, sequence_width, segment_length):
    return (anchor_point - (distance - 1) * sequence_width - 1) // segment_length == anchor_point // segment_length


def layer_norm(x, gain_vec):
    average = jnp.mean(x, -1, keepdims=True)
    centred = x - average
    variance = jnp.mean(centred * centred, -1, keepdims=True)
    return centred * lax.rsqrt(variance + LN_EPSILON) * gain_vec


def select_table(offsets_row, dilation_rate):
    return (jnp.arange(dilation_rate, dtype=jnp.int32)[:, None] == offsets_row[None, :]).astype(
        jnp.float32
    )


def spread_apart(x, select_option, dilation_rate):
    shaped = x.reshape(x.shape[0] // dilation_rate, dilation_rate, x.shape[1], x.shape[2])
    return jnp.einsum("trhd,rh->thd", shaped, select_option, precision=MATMUL_ACCURACY)


def spread_scalar_rows(x, select_option, dilation_rate):
    shaped = x.reshape(x.shape[0] // dilation_rate, dilation_rate, x.shape[1])
    return jnp.einsum("trh,rh->th", shaped, select_option, precision=MATMUL_ACCURACY)


def spread_rows(x, select_option):
    return jnp.einsum("thd,rh->trhd", x, select_option, precision=MATMUL_ACCURACY).reshape(
        -1, x.shape[1], x.shape[2]
    )


def spread_scalars(x, select_option):
    return jnp.einsum("th,rh->trh", x, select_option, precision=MATMUL_ACCURACY).reshape(
        -1, x.shape[1]
    )


def masked_score_matrix(sparse_queries, key_portion, query_position, key_position, segment_length):
    score_matrix = jnp.einsum(
        "ozt,bzt->zob", sparse_queries, key_portion, precision=MATMUL_ACCURACY
    ) * (1.0 / math.sqrt(key_portion.shape[-1]))
    q_cols = query_position.T[:, :, None]
    k_cols = key_position.T[:, None, :]
    permitted_mask = (k_cols <= q_cols) & (k_cols // segment_length == q_cols // segment_length)
    return (jnp.where(permitted_mask, score_matrix, MASK_VALUE), permitted_mask)


def prepare_pattern(
    query_sequence, key_sequence, value_sequence, offsets_row, dilation_rate, anchor_point
):
    select_option = select_table(offsets_row, dilation_rate)
    sparse_queries = spread_apart(query_sequence, select_option, dilation_rate)
    sparse_key_value = jnp.stack(
        (
            spread_apart(key_sequence, select_option, dilation_rate),
            spread_apart(value_sequence, select_option, dilation_rate),
        )
    )
    query_position = (
        anchor_point
        + jnp.arange(sparse_queries.shape[0], dtype=jnp.int32)[:, None] * dilation_rate
        + offsets_row[None, :]
    )
    return (select_option, sparse_queries, sparse_key_value, query_position)


def pattern_forward_pass(
    sparse_queries,
    sparse_key_value,
    query_position,
    reach,
    segment_length,
    anchor_point,
    sequence_width,
):
    masked_logits, permitted_mask = masked_score_matrix(
        sparse_queries, sparse_key_value[0], query_position, query_position, segment_length
    )
    row_max = jnp.max(masked_logits, -1)
    softmax_weights = jnp.where(permitted_mask, jnp.exp(masked_logits - row_max[..., None]), 0.0)
    state = (
        row_max,
        jnp.sum(softmax_weights, -1),
        jnp.einsum("tlj,jtb->tlb", softmax_weights, sparse_key_value[1], precision=MATMUL_ACCURACY),
    )

    def one_run(distance, carry):
        remote_key_value, state = carry
        remote_key_value = passed_along(remote_key_value, "seq", 1)
        key_position = query_position - distance * sequence_width

        def update(state_in):
            old_max, old_sum, old_acc = state_in
            masked_remote, permitted_remote = masked_score_matrix(
                sparse_queries, remote_key_value[0], query_position, key_position, segment_length
            )
            new_max = jnp.maximum(old_max, jnp.max(masked_remote, -1))
            weights_far = jnp.where(
                permitted_remote, jnp.exp(masked_remote - new_max[..., None]), 0.0
            )
            factor = jnp.exp(old_max - new_max)
            added = jnp.einsum(
                "tlj,jtb->tlb", weights_far, remote_key_value[1], precision=MATMUL_ACCURACY
            )
            return (
                new_max,
                old_sum * factor + jnp.sum(weights_far, -1),
                old_acc * factor[..., None] + added,
            )

        def unchanged(state_in):
            return state_in

        is_live = run_is_live(distance, anchor_point, sequence_width, segment_length)
        return remote_key_value, lax.cond(is_live, update, unchanged, state)

    state = lax.fori_loop(1, reach + 1, one_run, (sparse_key_value, state))[1]
    row_max, row_sum, accumulated = state
    mixture = jnp.transpose(accumulated / row_sum[..., None], (1, 0, 2))
    log_sum = (row_max + jnp.log(row_sum)).T
    return (mixture, log_sum)


def merge_patterns(forwards, prepared_inputs):
    full_lse = []
    full_mix = []
    for pattern_spec in range(len(forwards)):
        mixture, log_sum = forwards[pattern_spec]
        select_option = prepared_inputs[pattern_spec][0]
        covered = spread_scalars(jnp.ones_like(log_sum), select_option)
        full_lse.append(spread_scalars(log_sum, select_option) + (covered - 1.0) * 1e30)
        full_mix.append(spread_rows(mixture, select_option))
    stacked = jnp.stack(full_lse)
    row_max = jnp.max(stacked, 0)
    softmax_weights = jnp.exp(stacked - row_max)
    row_sum = jnp.sum(softmax_weights, 0)
    attended = full_mix[0] * softmax_weights[0][..., None]
    for pattern_spec in range(1, len(full_mix)):
        attended = attended + full_mix[pattern_spec] * softmax_weights[pattern_spec][..., None]
    return (attended / row_sum[..., None], row_max + jnp.log(row_sum))


def pattern_backward(
    select_option,
    dilation_rate,
    segment_length,
    anchor_point,
    sparse_queries,
    sparse_key_value,
    query_position,
    reach,
    sequence_gradient,
    row_difference,
    combined_logsumexp,
):
    sequence_width = sequence_gradient.shape[0]
    sparse_gradient = spread_apart(sequence_gradient, select_option, dilation_rate)
    sparse_output_grad = spread_scalar_rows(row_difference, select_option, dilation_rate).T
    sparse_logsumexp = spread_scalar_rows(combined_logsumexp, select_option, dilation_rate).T
    inverse_square_root = 1.0 / math.sqrt(sparse_queries.shape[-1])

    def portion_gradients(key_portion, value_portion, key_position):
        masked_logits, permitted_mask = masked_score_matrix(
            sparse_queries, key_portion, query_position, key_position, segment_length
        )
        softmax_weights = jnp.where(
            permitted_mask, jnp.exp(masked_logits - sparse_logsumexp[..., None]), 0.0
        )
        value_gradient = jnp.einsum(
            "tui,utx->itx", softmax_weights, sparse_gradient, precision=MATMUL_ACCURACY
        )
        pattern_gradient = jnp.einsum(
            "ozt,bzt->zob", sparse_gradient, value_portion, precision=MATMUL_ACCURACY
        )
        score_gradient = (
            softmax_weights
            * (pattern_gradient - sparse_output_grad[..., None])
            * inverse_square_root
        )
        query_gradient = jnp.einsum(
            "hqk,khd->qhd", score_gradient, key_portion, precision=MATMUL_ACCURACY
        )
        key_gradient = jnp.einsum(
            "tui,utx->itx", score_gradient, sparse_queries, precision=MATMUL_ACCURACY
        )
        return (query_gradient, jnp.stack((key_gradient, value_gradient)))

    query_gradient, key_value_gradient = portion_gradients(
        sparse_key_value[0], sparse_key_value[1], query_position
    )

    def one_run(distance, carry):
        remote_key_value, remote_gradient, query_sum = carry
        remote_key_value = passed_along(remote_key_value, "seq", 1)
        remote_gradient = passed_along(remote_gradient, "seq", 1)
        key_position = query_position - distance * sequence_width

        def far_grads():
            part_q, part_kv = portion_gradients(remote_key_value[0], remote_key_value[1], key_position)
            return query_sum + part_q, remote_gradient + part_kv

        def no_grads():
            return query_sum, remote_gradient

        is_live = run_is_live(distance, anchor_point, sequence_width, segment_length)
        query_sum, remote_gradient = lax.cond(is_live, far_grads, no_grads)
        return remote_key_value, remote_gradient, query_sum

    _, travelled, query_gradient = lax.fori_loop(
        1, reach + 1, one_run, (sparse_key_value, key_value_gradient, query_gradient)
    )
    return (query_gradient, passed_along(travelled, "seq", -reach))


def front_part(own_rows, w_qkv, gain_attn):
    return jnp.dot(layer_norm(own_rows, gain_attn), w_qkv, precision=MATMUL_ACCURACY)


def after_part(attn_rows, own_rows, w_out, w_up, w_down, gain_inner, gain_ffn, gain_hidden):
    residual = own_rows + jnp.dot(
        layer_norm(attn_rows, gain_inner), w_out, precision=MATMUL_ACCURACY
    )
    hidden = jax.nn.gelu(
        jnp.dot(layer_norm(residual, gain_ffn), w_up, precision=MATMUL_ACCURACY), approximate=False
    )
    return residual + jnp.dot(layer_norm(hidden, gain_hidden), w_down, precision=MATMUL_ACCURACY)


def shards(
    tokens,
    w_qkv,
    w_out,
    w_up,
    w_down,
    gain_attn,
    gain_inner,
    gain_ffn,
    gain_hidden,
    offsets,
    grad_out,
):
    w_qkv = w_qkv.astype(jnp.float32)
    w_out = w_out.astype(jnp.float32)
    w_up = w_up.astype(jnp.float32)
    w_down = w_down.astype(jnp.float32)
    groups = lax.axis_size("pat")
    local_rows = tokens.shape[0]
    sequence_width = local_rows * groups
    heads_here = HEADS // groups
    own_rows = tokens.reshape(local_rows, D)
    qkv_rows, front_back = jax.vjp(front_part, own_rows, w_qkv, gain_attn)
    gathered_qkv = lax.all_to_all(
        qkv_rows.reshape(local_rows, 1, 3, HEADS, HD),
        "pat",
        split_axis=3,
        concat_axis=1,
        tiled=True,
    )
    gathered_qkv = gathered_qkv.reshape(sequence_width, 3, heads_here, HD)
    head_offsets = lax.dynamic_slice_in_dim(
        offsets, lax.axis_index("pat") * heads_here, heads_here, 1
    )
    anchor_point = lax.axis_index("seq") * sequence_width
    dilation_rates = (DILATION_ONE, DILATION_TWO, DILATION_THREE, DILATION_FOUR, DILATION_FIVE)
    segment_lengths = (SEG1, SEG2, SEG3, SEG4, SEG5)
    reaches = [
        min((segment_lengths[pattern_spec] - 2) // sequence_width + 1, lax.axis_size("seq") - 1)
        for pattern_spec in range(PATTERNS)
    ]
    prepared_inputs = []
    for pattern_spec in range(PATTERNS):
        prepared_inputs.append(
            prepare_pattern(
                gathered_qkv[:, 0],
                gathered_qkv[:, 1],
                gathered_qkv[:, 2],
                head_offsets[pattern_spec],
                dilation_rates[pattern_spec],
                anchor_point,
            )
        )
    forwards = []
    for pattern_spec in range(PATTERNS):
        select_option, sparse_queries, sparse_key_value, query_position = prepared_inputs[
            pattern_spec
        ]
        forwards.append(
            pattern_forward_pass(
                sparse_queries,
                sparse_key_value,
                query_position,
                reaches[pattern_spec],
                segment_lengths[pattern_spec],
                anchor_point,
                sequence_width,
            )
        )
    lse_sums = jnp.stack([jnp.sum(entry[1]) for entry in forwards])
    totals = lax.psum(lse_sums, ("pat", "seq"))
    full_length = sequence_width * lax.axis_size("seq")
    counts = jnp.array(
        [
            float(full_length // dilation_rates[pattern_spec] * HEADS)
            for pattern_spec in range(PATTERNS)
        ],
        jnp.float32,
    )
    log_means = totals / counts
    attended, combined_logsumexp = merge_patterns(forwards, prepared_inputs)
    returned_rows = lax.all_to_all(
        attended.reshape(local_rows, groups, heads_here, HD),
        "pat",
        split_axis=1,
        concat_axis=2,
        tiled=True,
    )
    attn_rows = returned_rows.reshape(local_rows, D)
    result, after_back = jax.vjp(
        after_part, attn_rows, own_rows, w_out, w_up, w_down, gain_inner, gain_ffn, gain_hidden
    )
    g_attn, g_resid, g_out, g_up, g_down, g_inner, g_ffn, g_hidden = after_back(
        grad_out.reshape(local_rows, D)
    )
    sequence_gradient = lax.all_to_all(
        g_attn.reshape(local_rows, 1, HEADS, HD), "pat", split_axis=2, concat_axis=1, tiled=True
    )
    sequence_gradient = sequence_gradient.reshape(sequence_width, heads_here, HD)
    row_difference = jnp.sum(sequence_gradient * attended, -1)
    q_grads = []
    kv_grads = []
    for pattern_spec in range(PATTERNS):
        select_option, sparse_queries, sparse_key_value, query_position = prepared_inputs[
            pattern_spec
        ]
        part_q, part_kv = pattern_backward(
            select_option,
            dilation_rates[pattern_spec],
            segment_lengths[pattern_spec],
            anchor_point,
            sparse_queries,
            sparse_key_value,
            query_position,
            reaches[pattern_spec],
            sequence_gradient,
            row_difference,
            combined_logsumexp,
        )
        q_grads.append(part_q)
        kv_grads.append(part_kv)
    grad_total = jnp.zeros((sequence_width, 3, heads_here, HD), jnp.float32)
    for pattern_spec in range(PATTERNS):
        select_option = prepared_inputs[pattern_spec][0]
        grad_total = grad_total + jnp.stack(
            (
                spread_rows(q_grads[pattern_spec], select_option),
                spread_rows(kv_grads[pattern_spec][0], select_option),
                spread_rows(kv_grads[pattern_spec][1], select_option),
            ),
            1,
        )
    grad_back = lax.all_to_all(
        grad_total.reshape(local_rows, groups, 3, heads_here, HD),
        "pat",
        split_axis=1,
        concat_axis=3,
        tiled=True,
    )
    g_tokens, g_qkv, g_attn_gain = front_back(grad_back.reshape(local_rows, 3 * D))
    grad_tokens = (g_resid + g_tokens).reshape(local_rows, 1, D)
    summed = (
        lax.psum_scatter(g_qkv, ("pat", "seq"), scatter_dimension=0, tiled=True),
        lax.psum_scatter(g_out, ("pat", "seq"), scatter_dimension=0, tiled=True),
        lax.psum_scatter(g_up, ("pat", "seq"), scatter_dimension=0, tiled=True),
        lax.psum_scatter(g_down, ("pat", "seq"), scatter_dimension=0, tiled=True),
        lax.psum_scatter(g_attn_gain, ("pat", "seq"), scatter_dimension=0, tiled=True),
        lax.psum_scatter(g_inner, ("pat", "seq"), scatter_dimension=0, tiled=True),
        lax.psum_scatter(g_ffn, ("pat", "seq"), scatter_dimension=0, tiled=True),
        lax.psum_scatter(g_hidden, ("pat", "seq"), scatter_dimension=0, tiled=True),
    )
    return (
        result.reshape(local_rows, 1, D),
        grad_tokens,
        summed[0],
        summed[1],
        summed[2],
        summed[3],
        summed[4],
        summed[5],
        summed[6],
        summed[7],
        log_means,
    )


def fast_shards(tokens, w_qkv, w_out, w_up, w_down, gain_attn, gain_inner, gain_ffn, gain_hidden, offsets, grad_out):
    counts = [float(TOTAL * 4 // r * HEADS) for r in DILATIONS]
    pk, x = front(tokens, w_qkv, gain_attn)
    own, sib = to_heads(pk, True, 0)
    ap, lse, sums = attention_forward(offsets, own, sib)
    rec = to_homes(ap, 1)
    mixed, drec, dy1, S, C0, C1a, C1b = feed_forward(
        rec, x, grad_out, w_out, w_up, w_down, gain_inner, gain_ffn, gain_hidden, sums
    )
    grec, g_out, g_up, g_down = backward_all(offsets, drec, own, sib, ap, lse, C0, C1a, C1b, 2)
    gx, g_qkv, *small = finish(grec, x, dy1, w_qkv, gain_attn, S, counts, 3)
    mixed, gx, g_qkv, g_out, g_up, g_down, *small = deliver(mixed, gx, g_qkv, g_out, g_up, g_down, *small)
    return (mixed, gx, g_qkv, g_out, g_up, g_down, *(v.reshape(-1) for v in small))


def fits(mesh):
    return mesh.shape["pat"] == 4 and mesh.shape["seq"] == RUNS


def solution(mesh):
    rows = P("seq", "pat", None)
    split_rows = P(("pat", "seq"), None)
    split_one = P(("pat", "seq"))
    planned = jax.shard_map(
        fast_shards,
        mesh=mesh,
        in_specs=(rows,) + (P(),) * 9 + (rows,),
        out_specs=(rows, rows) + (split_rows,) * 4 + (split_one,) * 4 + (P(),),
        check_vma=False,
    )
    general = jax.shard_map(
        shards,
        mesh=mesh,
        in_specs=(rows,) + (P(),) * 9 + (rows,),
        out_specs=(rows, rows) + (split_rows,) * 4 + (split_one,) * 4 + (P(),),
        check_vma=False,
    )

    def layer(tokens, *rest):
        if fits(mesh) and tokens.shape[0] == TOTAL:
            return planned(tokens, *rest)
        return general(tokens, *rest)

    return layer
```

```python
import functools
import math

import jax
import jax.numpy as jnp
from jax import lax
from jax.experimental import pallas as pl
from jax.experimental.pallas import tpu as pltpu
from jax.sharding import PartitionSpec as P

D = 768
HEADS = 12
HD = 64
FF = 3072
PATTERNS = 5
SEGMENTS = (2048, 4096, 8192, 16384, 32768)
DILATIONS = (1, 2, 4, 6, 12)
LN_EPSILON = 1e-05
NEG = -1e30
F32 = jnp.float32
BF16 = jnp.bfloat16
HIGHEST = lax.Precision.HIGHEST
VMEM_LIMIT = 60 * 1024 * 1024

ROWS = 192
HALF = ROWS // 2
RUNS = 8
TOTAL = ROWS * RUNS
PACK = ROWS + HALF
HOMES = 16
THIRD = TOTAL // 3
PIECE = 24
MESH = pl.DeviceIdType.MESH


def dot_nn(a, b):
    return lax.dot_general(a, b, (((1,), (0,)), ((), ())), preferred_element_type=F32)


def dot_nt(a, b):
    return lax.dot_general(a, b, (((1,), (1,)), ((), ())), preferred_element_type=F32)


def split(v):
    hi = v.astype(BF16)
    return hi, (v - hi.astype(F32)).astype(BF16)


def split32(v):
    hi = v.astype(BF16).astype(F32)
    return hi, v - hi


def lower_lanes(v):
    return lax.broadcasted_iota(jnp.int32, v.shape, v.ndim - 1) < HD


def swap(v):
    return pltpu.roll(v, HD, v.ndim - 1)


def pick(a, b):
    return jnp.where(lower_lanes(a), a, b)


def head_place(h):
    z = h // 3
    column = lax.rem(lax.rem(h, 3) + z + 1, 4)
    return column // 2, z * 2 + lax.rem(column, 2)


def head_here(p, s):
    z = s // 2
    column = (p // 2) * 2 + lax.rem(s, 2)
    k = lax.rem(column - z + 7, 4)
    return k < 3, z * 3 + jnp.minimum(k, 2)


def whole(*_):
    return pl.BlockSpec(memory_space=pltpu.VMEM)


VM = pl.BlockSpec(memory_space=pltpu.VMEM)
ANY = pl.BlockSpec(memory_space=pl.ANY)
SM = pl.BlockSpec(memory_space=pltpu.SMEM)


def params(**kw):
    return pltpu.CompilerParams(vmem_limit_bytes=VMEM_LIMIT, **kw)


def normed(v):
    centred = v - jnp.mean(v, -1, keepdims=True)
    rs = lax.rsqrt(jnp.mean(centred * centred, -1, keepdims=True) + LN_EPSILON)
    return centred * rs, rs


def put_split(ref, v):
    hi, lo = split(v)
    n = v.shape[0]
    ref[0:n, :] = hi
    ref[n : 2 * n, :] = lo


def front_kernel(x3, w_ref, gain_ref, pk_ref, x_ref, lhs):
    x = x3[...].reshape(ROWS, D)
    x_ref[...] = x
    n, _ = normed(x)
    put_split(lhs, n * gain_ref[...][None, :])
    for jj in range(3):
        parts = []
        for kind in range(3):
            c0 = kind * D + 256 * jj
            r = dot_nn(lhs[...], w_ref[:, c0 : c0 + 256])
            parts.append(r[:ROWS] + r[ROWS:])
        for half in range(2):
            q, k, v = (a[:, 128 * half : 128 * half + 128] for a in parts)
            h = 4 * jj + 2 * half
            pk_ref[h, 0:ROWS, :] = pick(k, swap(v))
            pk_ref[h + 1, 0:ROWS, :] = pick(swap(k), v)
            top, bottom = q[:HALF], q[HALF:]
            pk_ref[h, ROWS:PACK, :] = pick(top, swap(bottom))
            pk_ref[h + 1, ROWS:PACK, :] = pick(swap(top), bottom)


def front(x, w, gain):
    return pl.pallas_call(
        front_kernel,
        out_shape=[jax.ShapeDtypeStruct((HEADS, PACK, 128), F32)] + [jax.ShapeDtypeStruct((ROWS, D), F32)],
        in_specs=[VM] * 3,
        out_specs=[VM] * 2,
        scratch_shapes=[pltpu.VMEM((2 * ROWS, D), BF16)],
        compiler_params=params(),
    )(x, w, gain)


def place_facts():
    p, s = lax.axis_index("pat"), lax.axis_index("seq")
    x, core = p // 2, lax.rem(p, 2)
    active, head = head_here(p, s)
    return p, s, x, core, active, head


def home_device(core, m):
    return core * 2 + lax.rem(m, 2), m // 2


def head_device(h, b):
    hx, hs = head_place(h)
    return hx * 2 + b, hs


def same(p, s, q, t):
    return jnp.logical_and(p == q, s == t)


def to(p, s):
    return {"pat": p, "seq": s}


def scatter_kernel(forward, pk, own, *rest):
    if forward:
        sib, send, recv, fsend, frecv = rest
    else:
        send, recv = rest
    p, s, x, core, active, head = place_facts()
    slot = s * 2 + core
    barrier = pltpu.get_barrier_semaphore()

    @pl.when(active)
    def _():
        def greet(m, carry):
            q, t = home_device(core, m)

            @pl.when(jnp.logical_not(same(p, s, q, t)))
            def _():
                pl.semaphore_signal(barrier, inc=1, device_id=to(q, t), device_id_type=MESH)

            return carry

        lax.fori_loop(0, HOMES, greet, 0)
        if forward:
            pl.semaphore_signal(barrier, inc=1, device_id=to(x * 2 + 1 - core, s), device_id_type=MESH)

    mine = jnp.logical_and(active, core == x)
    waits = HEADS - mine.astype(jnp.int32)
    if forward:
        waits = waits + active.astype(jnp.int32)
    pl.semaphore_wait(barrier, waits)

    def copy(h):
        q, t = head_device(h, x)
        return q, t, pltpu.make_async_remote_copy(
            src_ref=pk.at[h],
            dst_ref=own.at[slot],
            send_sem=send.at[h],
            recv_sem=recv.at[slot],
            device_id=to(q, t),
            device_id_type=MESH,
        )

    def start(j, carry):
        h = lax.rem(j + 3 * (s // 2) + 2 * p, HEADS)
        q, t, remote = copy(h)

        @pl.when(same(p, s, q, t))
        def _():
            pltpu.make_async_copy(pk.at[h], own.at[slot], recv.at[slot]).start()

        @pl.when(jnp.logical_not(same(p, s, q, t)))
        def _():
            remote.start()

        return carry

    lax.fori_loop(0, HEADS, start, 0)

    def passed(m):
        return pltpu.make_async_remote_copy(
            src_ref=own.at[m, pl.ds(0, ROWS), :],
            dst_ref=sib.at[m],
            send_sem=fsend.at[m],
            recv_sem=frecv.at[m],
            device_id=to(x * 2 + 1 - core, s),
            device_id_type=MESH,
        )

    @pl.when(active)
    def _():
        def arrive(m, carry):
            pltpu.make_async_copy(own.at[m], own.at[m], recv.at[m]).wait()
            if forward:
                passed(m).start()
            return carry

        lax.fori_loop(0, HOMES, arrive, 0)
        if forward:

            def finish(m, carry):
                passed(m).wait()
                return carry

            lax.fori_loop(0, HOMES, finish, 0)

    def sent(h, carry):
        q, t, remote = copy(h)

        @pl.when(jnp.logical_not(same(p, s, q, t)))
        def _():
            remote.wait_send()

        return carry

    lax.fori_loop(0, HEADS, sent, 0)


def to_heads(packets, forward, cid):
    rows = packets.shape[1]
    shapes = [jax.ShapeDtypeStruct((HOMES, rows, 128), F32)]
    sems = [pltpu.SemaphoreType.DMA((HEADS,)), pltpu.SemaphoreType.DMA((HOMES,))]
    if forward:
        shapes.append(jax.ShapeDtypeStruct((HOMES, ROWS, 128), F32))
        sems += [pltpu.SemaphoreType.DMA((HOMES,)), pltpu.SemaphoreType.DMA((HOMES,))]
    return pl.pallas_call(
        functools.partial(scatter_kernel, forward),
        out_shape=shapes,
        in_specs=[ANY],
        out_specs=[ANY] * len(shapes),
        scratch_shapes=sems,
        compiler_params=params(collective_id=cid, has_side_effects=True),
    )(packets)


def home_barrier(p, s, x, core, active, barrier, also_sibling):
    def greet(h, carry):
        q, t = head_device(h, x)

        @pl.when(jnp.logical_not(same(p, s, q, t)))
        def _():
            pl.semaphore_signal(barrier, inc=1, device_id=to(q, t), device_id_type=MESH)

        return carry

    lax.fori_loop(0, HEADS, greet, 0)

    @pl.when(active)
    def _():
        if also_sibling:
            pl.semaphore_signal(barrier, inc=1, device_id=to(x * 2 + 1 - core, s), device_id_type=MESH)
        mine = (core == x).astype(jnp.int32)
        pl.semaphore_wait(barrier, HOMES - mine + (1 if also_sibling else 0))


def gather_kernel(pk, rec, send, recv):
    p, s, x, core, active, head = place_facts()
    barrier = pltpu.get_barrier_semaphore()
    home_barrier(p, s, x, core, active, barrier, False)

    def copy(m):
        q, t = home_device(core, m)
        return q, t, pltpu.make_async_remote_copy(
            src_ref=pk.at[m],
            dst_ref=rec.at[head],
            send_sem=send.at[m],
            recv_sem=recv.at[head],
            device_id=to(q, t),
            device_id_type=MESH,
        )

    @pl.when(active)
    def _():
        def start(j, carry):
            m = lax.rem(j + 2 * s + 1, HOMES)
            q, t, remote = copy(m)

            @pl.when(same(p, s, q, t))
            def _():
                pltpu.make_async_copy(pk.at[m], rec.at[head], recv.at[head]).start()

            @pl.when(jnp.logical_not(same(p, s, q, t)))
            def _():
                remote.start()

            return carry

        lax.fori_loop(0, HOMES, start, 0)

    def arrive(h, carry):
        pltpu.make_async_copy(rec.at[h], rec.at[h], recv.at[h]).wait()
        return carry

    lax.fori_loop(0, HEADS, arrive, 0)

    @pl.when(active)
    def _():
        def sent(m, carry):
            q, t, remote = copy(m)

            @pl.when(jnp.logical_not(same(p, s, q, t)))
            def _():
                remote.wait_send()

            return carry

        lax.fori_loop(0, HOMES, sent, 0)


def to_homes(packets, cid):
    rows = packets.shape[1]
    return pl.pallas_call(
        gather_kernel,
        out_shape=jax.ShapeDtypeStruct((HEADS, rows, 128), F32),
        in_specs=[ANY],
        out_specs=ANY,
        scratch_shapes=[pltpu.SemaphoreType.DMA((HOMES,)), pltpu.SemaphoreType.DMA((HEADS,))],
        compiler_params=params(collective_id=cid, has_side_effects=True),
    )(packets)


def tile_positions(rows, columns, row_classes, column_classes, t_step, class_step):
    r = lax.broadcasted_iota(jnp.int32, (rows, columns), 0)
    q = lax.broadcasted_iota(jnp.int32, (rows, columns), 1)
    rn, qn = rows // row_classes, columns // column_classes
    return (r % rn) * t_step + (r // rn) * class_step, (q % qn) * t_step + (q // qn) * class_step


def key_bias(q_shape, k_shape, t_step, class_step, shift, keys_first):
    nq, nk = q_shape[0] * q_shape[1], k_shape[0] * k_shape[1]
    if keys_first:
        kp, qp = tile_positions(nk, nq, k_shape[0], q_shape[0], t_step, class_step)
    else:
        qp, kp = tile_positions(nq, nk, q_shape[0], k_shape[0], t_step, class_step)
    return jnp.where(kp - qp <= shift, 0.0, NEG).astype(F32)


def unpack_keys(own, sib, b, kvf):
    def one(m, carry):
        c = 2 * b + lax.rem(m, 2)
        d = 2 * (1 - b) + lax.rem(m, 2)
        t = pl.multiple_of((m // 2) * ROWS, 64)
        kvf[c, pl.ds(t, ROWS), :] = own[m, 0:ROWS, :]
        kvf[d, pl.ds(t, ROWS), :] = sib[m]
        return carry

    lax.fori_loop(0, HOMES, one, 0)


def unpack_pairs(src, first, dst, scale):
    def one(m, carry):
        t = pl.multiple_of((m // 2) * ROWS, 32)
        v = src[m, first : first + HALF, :] * scale
        w = swap(v)
        dst[lax.rem(m, 2), pl.ds(t, HALF), :] = pick(v, w)
        dst[lax.rem(m, 2), pl.ds(t + HALF, HALF), :] = pick(w, v)
        return carry

    lax.fori_loop(0, HOMES, one, 0)


def keys_and_values(kv):
    hi, lo = split32(kv)
    k2 = pick(hi, swap(lo))
    v2 = pick(swap(hi), lo)
    return k2, v2


def doubled(v):
    return jnp.concatenate([v, v], 1)


def query_quads(qq):
    hi, lo = split32(qq)
    return jnp.concatenate([pick(hi, lo).astype(BF16), pick(lo, hi).astype(BF16)], 1)


def class_facts4(o4, b):
    keys = ((lax.rem(o4, 4), o4 // 4), (lax.rem(o4 + 6, 4), (o4 + 6) // 4))
    first = (keys[0][0] // 2) == b
    query = (jnp.where(first, keys[0][0], keys[1][0]), jnp.where(first, keys[0][1], keys[1][1]))
    return keys, jnp.where(first, 0, 1), query


def forward_kernel(offsets, own, sib, ap, lse, sums, kvf, kc, vc, qf, qc, k4, v4, q4, k5, v5, q5, acc, mx, R, b1, b2, b3, b4):
    p, s, x, b, active, head = place_facts()
    offs = [offsets[i, head] for i in range(PATTERNS)]
    sums[...] = jnp.zeros_like(sums)

    @pl.when(active)
    def _():
        ones = jnp.ones((128, 128), BF16)
        unpack_keys(own, sib, b, kvf)
        unpack_pairs(own, ROWS, qf, 1.0 / math.sqrt(HD))

        def with_ones(v2):
            return jnp.concatenate([v2.astype(BF16), ones], 1)

        def prepare(i, carry):
            c, t = i // 12, pl.multiple_of(lax.rem(i, 12) * 128, 128)
            k2, v2 = keys_and_values(kvf[c, pl.ds(t, 128), :])
            kc[c, pl.ds(t, 128), :] = k2.astype(BF16)
            vc[c, pl.ds(t, 128), :] = with_ones(v2)
            return carry

        lax.fori_loop(0, 48, prepare, 0, unroll=2)

        def prepare_q(i, carry):
            c, t = i // 12, pl.multiple_of(lax.rem(i, 12) * 128, 128)
            qc[c, pl.ds(t, 128), :] = query_quads(qf[c, pl.ds(t, 128), :])
            return carry

        lax.fori_loop(0, 24, prepare_q, 0, unroll=2)

        keys4, e4, (qc4, qv4) = class_facts4(offs[3], b)
        kc5, kv5 = lax.rem(offs[4], 4), offs[4] // 4
        for blk in range(4):
            r = slice(128 * blk, 128 * blk + 128)
            for e in range(2):
                c, v = keys4[e]
                k2, v2 = keys_and_values(kvf[c, pl.ds(v + 384 * blk, 128, stride=3), :])
                k4[e, r, :] = k2.astype(BF16)
                v4[e, r, :] = with_ones(v2)
            q4[r, :] = query_quads(qf[qc4 - 2 * b, pl.ds(qv4 + 384 * blk, 128, stride=3), :])
            k2, v2 = keys_and_values(kvf[kc5, pl.ds(kv5 + 384 * blk, 128, stride=3), :])
            k5[r, :] = k2.astype(BF16)
            v5[r, :] = with_ones(v2)
            q5[r, :] = query_quads(qf[lax.rem(kc5, 2), pl.ds(kv5 + 384 * blk, 128, stride=3), :])

        b1[...] = key_bias((2, 128), (4, 128), 4, 1, 2 * b, False)
        for i in range(2):
            b2[i] = key_bias((1, 512), (2, 256), 4, 2, 2 * b - 1024 * i, False)
            b4[i] = key_bias((1, 512), (2, 256), 12, 6, 6 * e4 - 3072 * i, False)
        b2[2] = jnp.zeros((512, 512), F32)
        b3[0] = key_bias((1, 512), (1, 512), 1, 1, 0, False)
        b3[1] = jnp.zeros((512, 512), F32)

        def tile(start, q, k, v, bias, classes, first):
            n = q.shape[0]
            each = n // classes
            per = 1536 // classes if classes == 1 else 512
            s = dot_nt(q, doubled(k))
            wide = s.shape[1]
            own_rows = bias.shape[0] // classes
            s = s.reshape(classes, each, wide)
            edge = s[:, :own_rows] + bias[...].reshape(classes, own_rows, wide)
            s = edge if each == own_rows else jnp.concatenate([edge, s[:, own_rows:]], 1)
            s = s.reshape(n, wide)
            top = jnp.max(s, -1, keepdims=True)

            def where(c):
                return pl.ds(c * per + start, each)

            def load(ref):
                return jnp.concatenate([ref[where(c), :] for c in range(classes)], 0)

            def store(ref, value):
                for c in range(classes):
                    ref[where(c), :] = value[c * each : c * each + each]

            if first:
                m = jnp.broadcast_to(top, (n, 128))
            else:
                old = load(mx)
                m = jnp.maximum(old, top)
            hi, lo = split(jnp.exp(s - jnp.concatenate([m] * (wide // 128), 1)))
            new = dot_nn(jnp.concatenate([hi, lo], 0), v)
            new = new[:n] + new[n:]
            if not first:
                new = load(acc) * doubled(jnp.exp(old - m)) + new
            store(acc, new)
            store(mx, m)

        def block(q, k, v, bias):
            s = dot_nt(q, doubled(k)) + bias
            old = mx[0:512, :]
            m = jnp.maximum(old, jnp.max(s, -1, keepdims=True))
            hi, lo = split(jnp.exp(s - jnp.concatenate([m] * 4, 1)))
            new = dot_nn(jnp.concatenate([hi, lo], 0), v)
            acc[0:512, :] = acc[0:512, :] * doubled(jnp.exp(old - m)) + new[:512] + new[512:]
            mx[0:512, :] = m

        def fresh():
            acc[0:512, :] = jnp.zeros((512, 256), F32)
            mx[0:512, :] = jnp.full((512, 128), NEG, F32)

        def closed(pattern, rows):
            value, m = acc[rows, :], mx[rows, :]
            o, l = value[:, :128], value[:, 128:]
            sums[pattern : pattern + 1, :] += jnp.sum(m + jnp.log(l), 0, keepdims=True)
            lane = lax.broadcasted_iota(jnp.int32, m.shape, 1)
            return jnp.where(lane < HD, o + swap(o), jnp.where(lane < 96, l, m))

        def merge(pattern, ci, rows, of):
            r0, r1 = R[ci, rows, :], closed(pattern, of)
            m0 = jnp.broadcast_to(r0[:, 96:97], r0.shape)
            m1 = jnp.broadcast_to(r1[:, 96:97], r1.shape)
            m = jnp.maximum(m0, m1)
            both = r0 * jnp.exp(m0 - m) + r1 * jnp.exp(m1 - m)
            lane = lax.broadcasted_iota(jnp.int32, r0.shape, 1)
            R[ci, rows, :] = jnp.where(lane < 96, both, m)

        def q1(g, carry):
            base = 512 * g

            def at(t, n):
                return pl.ds(pl.multiple_of(base + t, 128), n)

            for kb in range(4):
                start = 128 * kb
                each = 512 - start
                ks = at(start, 128)
                tile(
                    start,
                    qc[:, at(start, each), :].reshape(2 * each, 256),
                    kc[:, ks, :].reshape(512, 128),
                    vc[:, ks, :].reshape(512, 256),
                    b1,
                    2,
                    kb == 0,
                )
            for c in range(2):
                for i in range(2):
                    R[c, at(256 * i, 256), :] = closed(0, pl.ds(512 * c + 256 * i, 256))
            return carry

        lax.fori_loop(0, 3, q1, 0)

        par = offs[1]

        def q2(i, carry):
            rows = pl.ds(pl.multiple_of(512 * i, 512), 512)
            first = jnp.where(i == 2, 4, 0)
            fresh()

            def one(kb, inner):
                ks = pl.ds(pl.multiple_of(256 * kb, 256), 256)
                block(
                    qc[par, rows, :],
                    jnp.concatenate([kc[par, ks, :], kc[par + 2, ks, :]], 0),
                    jnp.concatenate([vc[par, ks, :], vc[par + 2, ks, :]], 0),
                    b2[jnp.where(kb >= 2 * i, kb - 2 * i, 2)],
                )
                return inner

            lax.fori_loop(first, 2 * i + 2, one, 0)
            merge(1, par, rows, pl.ds(0, 512))
            return carry

        lax.fori_loop(0, TOTAL // 512, q2, 0)

        o3 = offs[2]

        @pl.when(o3 // 2 == b)
        def _():
            ci = lax.rem(o3, 2)

            def q3(i, carry):
                rows = pl.ds(pl.multiple_of(512 * i, 512), 512)
                fresh()

                def one(kb, inner):
                    ks = pl.ds(pl.multiple_of(512 * kb, 512), 512)
                    block(qc[ci, rows, :], kc[o3, ks, :], vc[o3, ks, :], b3[jnp.where(kb == i, 0, 1)])
                    return inner

                lax.fori_loop(0, i + 1, one, 0)
                merge(2, ci, rows, pl.ds(0, 512))
                return carry

            lax.fori_loop(0, TOTAL // 512, q3, 0)

        fresh()

        def one4(kb, carry):
            ks = pl.ds(pl.multiple_of(256 * kb, 256), 256)
            block(q4[...], k4[:, ks, :].reshape(512, 128), v4[:, ks, :].reshape(512, 256), b4[kb])
            return carry

        lax.fori_loop(0, 2, one4, 0)
        merge(3, qc4 - 2 * b, pl.ds(qv4, THIRD, stride=3), pl.ds(0, 512))

        @pl.when(kc5 // 2 == b)
        def _():
            fresh()
            block(q5[...], k5[...], v5[...], b3[0])
            merge(4, lax.rem(kc5, 2), pl.ds(kv5, THIRD, stride=3), pl.ds(0, 512))

        def finish(m, carry):
            ci = lax.rem(m, 2)
            rows = pl.ds(pl.multiple_of((m // 2) * ROWS, 64), ROWS)
            r = R[ci, rows, :]
            l = jnp.broadcast_to(r[:, HD : HD + 1], r.shape)
            out = r / l
            ap[m] = pick(out[:HALF], swap(out[HALF:]))
            lse[ci, rows, :] = jnp.broadcast_to(r[:, 96:97], r.shape) + jnp.log(l)
            return carry

        lax.fori_loop(0, HOMES, finish, 0, unroll=2)


def attention_forward(offsets, own, sib):
    state = pltpu.VMEM((2, TOTAL, 128), F32)
    return pl.pallas_call(
        forward_kernel,
        out_shape=[
            jax.ShapeDtypeStruct((HOMES, HALF, 128), F32),
            jax.ShapeDtypeStruct((2, TOTAL, 128), F32),
            jax.ShapeDtypeStruct((8, 128), F32),
        ],
        in_specs=[SM, VM, VM],
        out_specs=[VM, VM, VM],
        scratch_shapes=[
            pltpu.VMEM((4, TOTAL, 128), F32),
            pltpu.VMEM((4, TOTAL, 128), BF16),
            pltpu.VMEM((4, TOTAL, 256), BF16),
            state,
            pltpu.VMEM((2, TOTAL, 256), BF16),
            pltpu.VMEM((2, THIRD, 128), BF16),
            pltpu.VMEM((2, THIRD, 256), BF16),
            pltpu.VMEM((THIRD, 256), BF16),
            pltpu.VMEM((THIRD, 128), BF16),
            pltpu.VMEM((THIRD, 256), BF16),
            pltpu.VMEM((THIRD, 256), BF16),
            pltpu.VMEM((TOTAL, 256), F32),
            pltpu.VMEM((TOTAL, 128), F32),
            state,
            pltpu.VMEM((256, 512), F32),
            pltpu.VMEM((3, 512, 512), F32),
            pltpu.VMEM((2, 512, 512), F32),
            pltpu.VMEM((2, 512, 512), F32),
        ],
        compiler_params=params(),
    )(offsets, own, sib)


class Place:
    def __init__(self):
        p, s = lax.axis_index("pat"), lax.axis_index("seq")
        self.p, self.s = p, s
        self.x, self.core, self.z, self.y = p // 2, lax.rem(p, 2), s // 2, lax.rem(s, 2)
        self.peer = to(self.x * 2 + 1 - self.core, s)
        self.xn = to((1 - self.x) * 2 + self.core, s)
        self.yn = to(p, self.z * 2 + 1 - self.y)
        self.left, self.right = to(p, s - 2), to(p, s + 2)

    def greet(self, barrier, line=True):
        for d in (self.peer, self.xn, self.yn):
            pl.semaphore_signal(barrier, inc=1, device_id=d, device_id_type=MESH)
        if not line:
            return 3

        @pl.when(self.z > 0)
        def _():
            pl.semaphore_signal(barrier, inc=1, device_id=self.left, device_id_type=MESH)

        @pl.when(self.z < 3)
        def _():
            pl.semaphore_signal(barrier, inc=1, device_id=self.right, device_id_type=MESH)

        return 3 + (self.z > 0).astype(jnp.int32) + (self.z < 3).astype(jnp.int32)


def remote(src, dst, a, b, d):
    return pltpu.make_async_remote_copy(
        src_ref=src, dst_ref=dst, send_sem=a, recv_sem=b, device_id=d, device_id_type=MESH
    )


def add_in(dst, src):
    lead = dst.shape[:-2]

    def one(i, carry):
        index = []
        for d in reversed(lead):
            index.insert(0, lax.rem(i, d))
            i = i // d
        dst[tuple(index)] += src[tuple(index)]
        return carry

    lax.fori_loop(0, math.prod(lead), one, 0)


class Sems:
    NAMES = ("sc", "rc", "s1", "r1", "s2", "r2", "sl", "rl", "sr", "rr")

    def __init__(self, refs):
        for name, ref in zip(self.NAMES, refs):
            setattr(self, name, ref)

    @staticmethod
    def scratch(n):
        dma = pltpu.SemaphoreType.DMA
        return [dma((n, 2)), dma((n, 2))] + [dma((n,)) for _ in range(8)]


class Chunk:
    def __init__(self, place, k, x_first, sems, b0=None, b1=None, b2=None, bl=None, br=None, part=None, put=None):
        self.at, self.k, self.x_first, self.sems = place, k, x_first, sems
        self.b0, self.b1, self.b2, self.bl, self.br = b0, b1, b2, bl, br
        self.part, self.put = part, put

    def core(self, i):
        k, m = self.k, self.sems
        return remote(self.part(i, 1 - self.at.core), self.b0.at[i], m.sc.at[k, i], m.rc.at[k, i], self.at.peer)

    def one(self):
        k, at, m = self.k, self.at, self.sems
        if self.x_first:
            return remote(self.b0.at[1 - at.x], self.b1, m.s1.at[k], m.r1.at[k], at.xn)
        return remote(self.b0.at[:, :, 1 - at.y], self.b1, m.s1.at[k], m.r1.at[k], at.yn)

    def two(self):
        k, at, m = self.k, self.at, self.sems
        if self.x_first:
            return remote(self.b1.at[:, 1 - at.y], self.b2, m.s2.at[k], m.r2.at[k], at.yn)
        return remote(self.b1.at[1 - at.x], self.b2, m.s2.at[k], m.r2.at[k], at.xn)

    def rightward(self, i):
        k, part, m = self.k, pl.ds(i + 1, 3 - i), self.sems
        src = self.b2 if i == 0 else self.bl
        return remote(src.at[part], self.bl.at[part], m.sr.at[k], m.rl.at[k], self.at.right)

    def leftward(self, i):
        k, part, m = self.k, pl.ds(0, i), self.sems
        src = self.b2 if i == 3 else self.br
        return remote(src.at[part], self.br.at[part], m.sl.at[k], m.rr.at[k], self.at.left)

    def own_core(self, i):
        self.core(i).wait_recv()
        add_in(self.b0.at[i], self.part(i, self.at.core))

    def stage1(self):
        for i in range(2):
            self.own_core(i)
        self.one().start()

    def arrived(self):
        self.one().wait_recv()
        add_in(self.b1, self.b0.at[self.at.x] if self.x_first else self.b0.at[:, :, self.at.y])

    def stage2(self):
        self.arrived()
        self.two().start()

    def stage3(self):
        self.two().wait_recv()
        add_in(self.b2, self.b1.at[:, self.at.y] if self.x_first else self.b1.at[self.at.x])

        @pl.when(self.at.z == 0)
        def _():
            self.rightward(0).start()

        @pl.when(self.at.z == 3)
        def _():
            self.leftward(3).start()

    def stage4(self):
        @pl.when(self.at.z == 1)
        def _():
            self.rightward(0).wait_recv()
            self.bl[2:4] += self.b2[2:4]
            self.rightward(1).start()

        @pl.when(self.at.z == 2)
        def _():
            self.leftward(3).wait_recv()
            self.br[0:2] += self.b2[0:2]
            self.leftward(2).start()

    def stage5(self):
        @pl.when(self.at.z == 2)
        def _():
            self.rightward(1).wait_recv()
            self.bl[3:4] += self.b2[3:4]
            self.rightward(2).start()

        @pl.when(self.at.z == 1)
        def _():
            self.leftward(2).wait_recv()
            self.br[0:1] += self.b2[0:1]
            self.leftward(1).start()

    def stage6(self):
        @pl.when(self.at.z == 3)
        def _():
            self.rightward(2).wait_recv()
            self.put(self.b2[3] + self.bl[3])

        @pl.when(self.at.z == 0)
        def _():
            self.leftward(1).wait_recv()
            self.put(self.b2[0] + self.br[0])

        @pl.when(self.at.z == 1)
        def _():
            self.put(self.b2[1] + self.bl[1] + self.br[1])

        @pl.when(self.at.z == 2)
        def _():
            self.put(self.b2[2] + self.bl[2] + self.br[2])

    def line_sent(self):
        for i in range(4):

            @pl.when(self.at.z == i)
            def _(i=i):
                if i < 3:
                    self.rightward(i).wait_send()
                if i > 0:
                    self.leftward(i).wait_send()


class Reducer:
    def __init__(self, place, n, part, scratch, put):
        self.place, self.n, self.part, self.put = place, n, part, put
        self.c0, self.c1a, self.c1b, self.c2, self.zl, self.zr = scratch[:6]
        self.sems = Sems(scratch[6:16])
        self.pairs = (n + 1) // 2

    @staticmethod
    def scratch(n, rows):
        bufs = [(n, 2, 4, 2), ((n + 1) // 2, 4, 2), (max(n // 2, 1), 2, 4), (n, 4), (n, 4), (n, 4)]
        return [pltpu.VMEM(b + (rows, D), F32) for b in bufs] + Sems.scratch(n)

    def chunk(self, k, parity):
        return Chunk(
            self.place,
            k,
            parity == 0,
            self.sems,
            self.c0.at[k],
            (self.c1b if parity else self.c1a).at[k // 2],
            self.c2.at[k],
            self.zl.at[k],
            self.zr.at[k],
            self.part(k),
            lambda v: self.put(k, v),
        )

    def send(self, first, after):
        def one(k, carry):
            for i in range(2):
                self.chunk(k, 0).core(i).start()
            return carry

        lax.fori_loop(first, after, one, 0)

    def one(self, stage, pair):
        for parity in range(2):
            k = 2 * pair + parity
            k = jnp.int32(k) if isinstance(k, int) else k

            @pl.when(jnp.logical_and(k >= 0, k < self.n))
            def _(k=k, parity=parity):
                getattr(self.chunk(k, parity), f"stage{stage}")()

    def early(self, pair):
        self.one(1, pair)

    def step(self, tau):
        self.one(1, tau)
        for stage in range(2, 7):
            self.one(stage, tau - stage)

    def finish(self):
        def one(k, carry):
            for parity in range(2):

                @pl.when(lax.rem(k, 2) == parity)
                def _(parity=parity):
                    c = self.chunk(k, parity)
                    for i in range(2):
                        c.core(i).wait_send()
                    c.one().wait_send()
                    c.two().wait_send()
                    c.line_sent()

            return carry

        lax.fori_loop(0, self.n, one, 0)


class SmallSum:
    def __init__(self, place, S, bufs, send, recv, put):
        self.at, self.S, self.send, self.recv, self.put = place, S, send, recv, put
        self.d0, self.d1, self.d2, self.dl, self.dr, self.t1, self.t2, self.t3, self.fl, self.fr = bufs

    @staticmethod
    def scratch():
        return [pltpu.VMEM((8, D), F32)] * 10 + [pltpu.SemaphoreType.DMA((5,)), pltpu.SemaphoreType.DMA((5,))]

    def hop(self, src, dst, i, d):
        return remote(src, dst, self.send.at[i], self.recv.at[i], d)

    def core(self):
        return self.hop(self.S, self.d0, 0, self.at.peer)

    def along_x(self):
        return self.hop(self.t1, self.d1, 1, self.at.xn)

    def along_y(self):
        return self.hop(self.t2, self.d2, 2, self.at.yn)

    def rightward(self, i):
        return self.hop(self.t3 if i == 0 else self.fl, self.dl, 3, self.at.right)

    def leftward(self, i):
        return self.hop(self.t3 if i == 3 else self.fr, self.dr, 4, self.at.left)

    def stage1(self):
        self.core().wait_recv()
        self.t1[...] = self.S[...] + self.d0[...]
        self.along_x().start()

    def stage2(self):
        self.along_x().wait_recv()
        self.t2[...] = self.t1[...] + self.d1[...]
        self.along_y().start()

    def stage3(self):
        self.along_y().wait_recv()
        self.t3[...] = self.t2[...] + self.d2[...]

        @pl.when(self.at.z == 0)
        def _():
            self.rightward(0).start()

        @pl.when(self.at.z == 3)
        def _():
            self.leftward(3).start()

    def from_left(self, i):
        self.rightward(i).wait_recv()
        self.fl[...] = self.dl[...] + self.t3[...]

    def from_right(self, i):
        self.leftward(i).wait_recv()
        self.fr[...] = self.dr[...] + self.t3[...]

    def stage4(self):
        @pl.when(self.at.z == 1)
        def _():
            self.from_left(0)
            self.rightward(1).start()

        @pl.when(self.at.z == 2)
        def _():
            self.from_right(3)
            self.leftward(2).start()

    def stage5(self):
        @pl.when(self.at.z == 2)
        def _():
            self.from_left(1)
            self.rightward(2).start()

        @pl.when(self.at.z == 1)
        def _():
            self.from_right(2)
            self.leftward(1).start()

    def stage6(self):
        @pl.when(self.at.z == 3)
        def _():
            self.from_left(2)
            self.put(self.fl[...])

        @pl.when(self.at.z == 0)
        def _():
            self.from_right(1)
            self.put(self.fr[...])

        @pl.when(jnp.logical_or(self.at.z == 1, self.at.z == 2))
        def _():
            self.put(self.fl[...] + self.dr[...])

    def finish(self):
        for c in (self.core(), self.along_x(), self.along_y()):
            c.wait_send()
        for i in range(4):

            @pl.when(self.at.z == i)
            def _(i=i):
                if i < 3:
                    self.rightward(i).wait_send()
                if i > 0:
                    self.leftward(i).wait_send()


def small_outputs(place, counts, outs, tot):
    ga, gi, gf, gh, means = outs

    def put(v):
        tot[...] = v
        d = place.p * RUNS + place.s
        for i, ref in enumerate((ga, gi, gf)):
            ref[...] = pltpu.roll(tot[i : i + 1, :], D - PIECE * d, 1)[:, :PIECE]
        row = tot[pl.ds(3 + d // 8, 1), :]
        gh[...] = pltpu.roll(row, D - 4 * PIECE * lax.rem(d, 8), 1)[:, : 4 * PIECE]
        lane = lax.broadcasted_iota(jnp.int32, (1, 128), 1)
        scale = jnp.full((1, 128), counts[0], F32)
        for i in range(1, PATTERNS):
            scale = jnp.where(lane == i, counts[i], scale)
        means[...] = (tot[7:8, :128] / scale)[:, :PATTERNS]

    return put


N_PIECES = 9
SUB = 8


def finish_kernel(counts, rec, x_ref, dy1_ref, w_hbm, ga1, S_in, gx, g_qkv, ga, gi, gf, gh, means, dqkv, lhs, th, tl, r_hi, r_lo, tiles, S, tot, gx2, w, wsem, *scratch):
    fetch = pltpu.make_async_copy(w_hbm, w, wsem)
    fetch.start()
    place = Place()
    barrier = pltpu.get_barrier_semaphore()
    expected = place.greet(barrier)
    for j in range(HEADS // 2):
        u, v = rec[2 * j, ROWS:PACK, :], rec[2 * j + 1, ROWS:PACK, :]
        cols = slice(128 * j, 128 * j + 128)
        dqkv[0:HALF, cols] = pick(u, swap(v))
        dqkv[HALF:ROWS, cols] = pick(swap(u), v)
        u, v = rec[2 * j, 0:ROWS, :], rec[2 * j + 1, 0:ROWS, :]
        dqkv[:, D + 128 * j : D + 128 * j + 128] = pick(u, swap(v))
        dqkv[:, 2 * D + 128 * j : 2 * D + 128 * j + 128] = pick(swap(u), v)
    gain = ga1[...][None, :]
    n, rs = normed(x_ref[...])
    put_turned(th, tl, n * gain)

    def part(k):
        rows = pl.ds(pl.multiple_of(lax.rem(k, 3) * SUB, SUB), SUB)
        return lambda i, c: tiles.at[k // 3, i, c, :, :, rows, :]

    def put(k, v):
        g_qkv[
            pl.ds(pl.multiple_of(lax.rem(k, 3) * SUB, SUB), SUB), pl.ds(pl.multiple_of((k // 3) * D, D), D)
        ] = v

    n_r = 16
    big = Reducer(place, N_PIECES, part, scratch[:n_r], put)
    rest = scratch[n_r:]
    small = SmallSum(
        place, S, rest[:10], rest[10], rest[11], small_outputs(place, counts, (ga, gi, gf, gh, means), tot)
    )

    def tile_of(j, carry):
        r_hi[...], r_lo[...] = split(dqkv[:, pl.ds(pl.multiple_of(D * j, D), D)])

        def one(i, inner):
            rows = pl.ds(pl.multiple_of(i * 2 * ROWS, 128), 2 * ROWS)
            h, l = th[rows, :], tl[rows, :]
            v = dot_nn(h, r_hi[...]) + dot_nn(h, r_lo[...]) + dot_nn(l, r_hi[...])
            tiles[j, i] = v.reshape(2, 4, 2, PIECE, D)
            return inner

        lax.fori_loop(0, 2, one, 0)

        @pl.when(j == 0)
        def _():
            pl.semaphore_wait(barrier, expected)

        big.send(3 * j, 3 * j + 3)

        @pl.when(j > 0)
        def _():
            big.early(j - 1)

        return carry

    lax.fori_loop(0, 3, tile_of, 0)
    gx2[...] = jnp.zeros_like(gx2)
    fetch.wait()

    def back(j, carry):
        cols = pl.ds(pl.multiple_of(D * j, D), D)
        put_split(lhs, dqkv[:, cols])
        gx2[...] += halves_sum(dot_nt(lhs[...], w[:, cols]))
        return carry

    lax.fori_loop(0, 3, back, 0)
    e = gx2[...]
    S[...] = S_in[...]
    S[0:1, :] = jnp.sum(e * n, 0, keepdims=True)
    small.core().start()
    gx[...] = (dy1_ref[...] + norm_back(e * gain, n, rs)).reshape(ROWS, 1, D)
    small.stage1()

    def step(tau, carry):
        for stage in range(2, 7):

            @pl.when(tau == stage + 1)
            def _(stage=stage):
                getattr(small, f"stage{stage}")()

        big.step(tau)
        return carry

    lax.fori_loop(2, big.pairs + 6, step, 0)

    big.finish()
    small.finish()


def finish(rec, x, dy1, w, ga, S, counts, cid):
    return pl.pallas_call(
        functools.partial(finish_kernel, counts),
        out_shape=[jax.ShapeDtypeStruct((ROWS, 1, D), F32), jax.ShapeDtypeStruct((PIECE, 3 * D), F32)]
        + [jax.ShapeDtypeStruct((1, n), F32) for n in (PIECE, PIECE, PIECE, 4 * PIECE, PATTERNS)],
        in_specs=[VM, VM, VM, ANY, VM, VM],
        out_specs=[VM] * 7,
        scratch_shapes=[
            pltpu.VMEM((ROWS, 3 * D), F32),
            pltpu.VMEM((2 * ROWS, D), BF16),
            pltpu.VMEM((D, ROWS), BF16),
            pltpu.VMEM((D, ROWS), BF16),
            pltpu.VMEM((ROWS, D), BF16),
            pltpu.VMEM((ROWS, D), BF16),
            pltpu.VMEM((3, 2, 2, 4, 2, PIECE, D), F32),
            pltpu.VMEM((8, D), F32),
            pltpu.VMEM((8, D), F32),
            pltpu.VMEM((ROWS, D), F32),
            pltpu.VMEM((D, 3 * D), BF16),
            pltpu.SemaphoreType.DMA,
        ]
        + Reducer.scratch(N_PIECES, SUB)
        + SmallSum.scratch(),
        compiler_params=params(collective_id=cid, has_side_effects=True),
    )(rec, x, dy1, w, ga, S)


def deliver_kernel(*refs):
    n = len(refs) // 2
    for src, dst in zip(refs[:n], refs[n:]):
        dst[...] = src[...]


def deliver(*arrays):
    return pl.pallas_call(
        deliver_kernel,
        out_shape=[jax.ShapeDtypeStruct(v.shape, v.dtype) for v in arrays],
        in_specs=[VM] * len(arrays),
        out_specs=[VM] * len(arrays),
        compiler_params=params(),
    )(*arrays)


def rows_from_pairs(rec, dst):
    for j in range(HEADS // 2):
        u, v = rec[2 * j], rec[2 * j + 1]
        cols = slice(128 * j, 128 * j + 128)
        dst[0:HALF, cols] = pick(u, swap(v))
        dst[HALF:ROWS, cols] = pick(swap(u), v)


def pairs_from_rows(src, dst):
    for j in range(HEADS // 2):
        top = src[0:HALF, 128 * j : 128 * j + 128]
        bottom = src[HALF:ROWS, 128 * j : 128 * j + 128]
        dst[2 * j] = pick(top, swap(bottom))
        dst[2 * j + 1] = pick(swap(top), bottom)


def halves_sum(r):
    return r[:ROWS] + r[ROWS:]


def norm_back(f, n, rs):
    return (f - jnp.mean(f, -1, keepdims=True) - n * jnp.mean(f * n, -1, keepdims=True)) * rs


def put_turned(hi_ref, lo_ref, v):
    for j in range(D // 128):
        t = v[:, 128 * j : 128 * j + 128].T
        hi, lo = split(t)
        hi_ref[128 * j : 128 * j + 128, :] = hi
        lo_ref[128 * j : 128 * j + 128, :] = lo


class ToHeads:
    def __init__(self, pk, rec, send, recv):
        self.pk, self.rec, self.send, self.recv = pk, rec, send, recv
        self.facts = place_facts()

    def greet(self):
        p, s, x, core, active, head = self.facts
        barrier = pltpu.get_barrier_semaphore()

        @pl.when(active)
        def _():
            def one(m, carry):
                q, t = home_device(core, m)

                @pl.when(jnp.logical_not(same(p, s, q, t)))
                def _():
                    pl.semaphore_signal(barrier, inc=1, device_id=to(q, t), device_id_type=MESH)

                return carry

            lax.fori_loop(0, HOMES, one, 0)

    def copy(self, h):
        p, s, x, core, active, head = self.facts
        slot = s * 2 + core
        q, t = head_device(h, x)
        far = pltpu.make_async_remote_copy(
            src_ref=self.pk.at[h],
            dst_ref=self.rec.at[slot],
            send_sem=self.send.at[h],
            recv_sem=self.recv.at[slot],
            device_id=to(q, t),
            device_id_type=MESH,
        )
        return same(p, s, q, t), lambda: pltpu.make_async_copy(self.pk.at[h], self.rec.at[slot], self.recv.at[slot]), far

    def wait(self, others):
        p, s, x, core, active, head = self.facts
        mine = jnp.logical_and(active, core == x).astype(jnp.int32)
        pl.semaphore_wait(pltpu.get_barrier_semaphore(), HEADS + others - mine)

    def start(self):
        p, s, x, core, active, head = self.facts

        def one(j, carry):
            here, near, far = self.copy(lax.rem(j + 3 * (s // 2) + 2 * p, HEADS))

            @pl.when(here)
            def _():
                near().start()

            @pl.when(jnp.logical_not(here))
            def _():
                far.start()

            return carry

        lax.fori_loop(0, HEADS, one, 0)

    def finish(self):
        active = self.facts[4]

        @pl.when(active)
        def _():
            def arrive(m, carry):
                pltpu.make_async_copy(self.rec.at[m], self.rec.at[m], self.recv.at[m]).wait()
                return carry

            lax.fori_loop(0, HOMES, arrive, 0)

        def sent(h, carry):
            here, near, far = self.copy(h)

            @pl.when(jnp.logical_not(here))
            def _():
                far.wait_send()

            return carry

        lax.fori_loop(0, HEADS, sent, 0)


FT = 1024


def product(hi, lo, r_hi, r_lo, put):
    def one(i, carry):
        rows = pl.ds(pl.multiple_of(i * 2 * ROWS, 128), 2 * ROWS)
        h, l = hi[rows, :], lo[rows, :]
        put(i, dot_nn(h, r_hi[...]) + dot_nn(h, r_lo[...]) + dot_nn(l, r_hi[...]))
        return carry

    lax.fori_loop(0, 2, one, 0)


N_FF = 9
N_COLS = 5


def ff_kernel(rec, x_ref, g3, wo_hbm, wu_hbm, wd_hbm, gi1, gf1, gh1, sums, out3, drec, dy1_ref, S, C0, C1a, C1b, dap, lhs, lhs2, gi, gf, gh, gh_g, g_ref, out_ref, V, N1, U, GP, E, ACC, th, tl, r_hi, r_lo, cols_t, rows_t, c0, c1a, c1b, osem, wo, wu, wd, wsem, dsend, drecv, *rsems):
    place = Place()
    sems = Sems(rsems)
    fetch = [
        pltpu.make_async_copy(src, dst, wsem.at[i])
        for i, (src, dst) in enumerate(((wo_hbm, wo), (wu_hbm, wu), (wd_hbm, wd)))
    ]
    for c in fetch:
        c.start()
    travel = ToHeads(dap, drec, dsend, drecv)
    travel.greet()
    place.greet(pltpu.get_barrier_semaphore(), False)

    def chunk(k, part=None):
        if not isinstance(k, int):
            return Chunk(place, k, True, sems, c0.at[k], part=part)
        x_first = k % 2 == 0
        b1 = None if k < N_COLS else (c1a if x_first else c1b).at[(k - N_COLS) // 2]
        return Chunk(place, k, x_first, sems, c0.at[k], b1, part=part)

    for wide, flat in ((gi, gi1), (gf, gf1), (gh, gh1)):
        wide[...] = flat[...][None, :]
    g_ref[...] = g3[...].reshape(ROWS, D)
    rows_from_pairs(rec, V)
    na, rs_a = normed(V[...])
    V[...] = na
    put_split(lhs, na * gi[...])
    fetch[0].wait()

    def project(j, carry):
        cols = pl.ds(pl.multiple_of(256 * j, 256), 256)
        N1[:, cols] = x_ref[:, cols] + halves_sum(dot_nn(lhs[...], wo[:, cols]))
        return carry

    lax.fori_loop(0, 3, project, 0)
    y1 = N1[...]
    out_ref[...] = y1
    ny, rs_y = normed(y1)
    N1[...] = ny
    put_split(lhs, ny * gf[...])
    fetch[1].wait()

    def up(j, su):
        cols = pl.ds(pl.multiple_of(j * FT, FT), FT)
        z = halves_sum(dot_nn(lhs[...], wu[:, cols]))
        phi = 0.5 * (1.0 + lax.erf(z * math.sqrt(0.5)))
        u = z * phi
        U[:, cols] = u
        GP[:, cols] = phi + z * jnp.exp(-0.5 * z * z) * (1.0 / math.sqrt(2.0 * math.pi))
        return su + jnp.sum(u, -1, keepdims=True)

    zero = jnp.zeros((ROWS, 1), F32)
    mean = lax.fori_loop(0, FF // FT, up, zero) * (1.0 / FF)

    def spread(j, sv):
        cols = pl.ds(pl.multiple_of(j * FT, FT), FT)
        c = U[:, cols] - mean
        return sv + jnp.sum(c * c, -1, keepdims=True)

    rs_u = lax.rsqrt(lax.fori_loop(0, FF // FT, spread, zero) * (1.0 / FF) + LN_EPSILON)
    ACC[...] = jnp.zeros_like(ACC)
    fetch[2].wait()

    def lower(j, carry):
        cols = pl.ds(pl.multiple_of(j * FT, FT), FT)
        n = (U[:, cols] - mean) * rs_u
        U[:, cols] = n
        put_split(lhs2, n * gh[:, cols])
        ACC[...] += halves_sum(dot_nn(lhs2[...], wd[cols, :]))
        return carry

    lax.fori_loop(0, FF // FT, lower, 0)
    out3[...] = (out_ref[...] + ACC[...]).reshape(ROWS, 1, D)

    travel.wait(3)
    r_hi[...], r_lo[...] = split(g_ref[...])

    def down(j, q):
        return chunk(N_COLS + q, lambda i, c: rows_t.at[lax.rem(j, 2), :, :, q])

    def down_step(j, carry):
        @pl.when(j < 4)
        def _():
            cols = pl.ds(pl.multiple_of(D * j, D), D)
            put_turned(th, tl, U[:, cols] * gh[:, cols])
            sent = place.core != lax.rem(j, 2)

            @pl.when(jnp.logical_and(j >= 2, sent))
            def _():
                for q in range(4):
                    down(j - 2, q).core(j // 2 - 1).wait_send()

            def put(i, v):
                rows_t[lax.rem(j, 2), pl.ds(2 * i, 2)] = v.reshape(2, 2, 4, PIECE, D)

            product(th, tl, r_hi, r_lo, put)

            @pl.when(sent)
            def _():
                for q in range(4):
                    down(j, q).core(j // 2).start()

        @pl.when(jnp.logical_and(j > 0, place.core == lax.rem(j + 1, 2)))
        def _():
            for q in range(4):
                down(j - 1, q).own_core((j - 1) // 2)

        return carry

    lax.fori_loop(0, 5, down_step, 0)
    for k in range(N_COLS, N_FF):
        chunk(k).one().start()

    put_split(lhs, g_ref[...])

    def back_down(j, sums):
        cols = pl.ds(pl.multiple_of(j * FT, FT), FT)
        e = halves_sum(dot_nt(lhs[...], wd[cols, :]))
        n = U[:, cols]
        gh_g[:, cols] = jnp.sum(e * n, 0, keepdims=True)
        f = e * gh[:, cols]
        E[:, cols] = f
        return sums[0] + jnp.sum(f, -1, keepdims=True), sums[1] + jnp.sum(f * n, -1, keepdims=True)

    sf, sfn = lax.fori_loop(0, FF // FT, back_down, (zero, zero))
    mf, mfn = sf * (1.0 / FF), sfn * (1.0 / FF)
    ACC[...] = jnp.zeros_like(ACC)

    def back_up(j, carry):
        cols = pl.ds(pl.multiple_of(j * FT, FT), FT)
        dz = (E[:, cols] - mf - U[:, cols] * mfn) * rs_u * GP[:, cols]
        E[:, cols] = dz
        put_split(lhs2, dz)
        ACC[...] += halves_sum(dot_nt(lhs2[...], wu[:, cols]))
        return carry

    lax.fori_loop(0, FF // FT, back_up, 0)
    e = ACC[...]
    ny = N1[...]
    S[2:3, :] = jnp.sum(e * ny, 0, keepdims=True)
    dy1 = g_ref[...] + norm_back(e * gf[...], ny, rs_y)
    dy1_ref[...] = dy1
    put_split(lhs, dy1)

    def project_back(j, carry):
        cols = pl.ds(pl.multiple_of(256 * j, 256), 256)
        ACC[:, cols] = halves_sum(dot_nt(lhs[...], wo[cols, :]))
        return carry

    lax.fori_loop(0, 3, project_back, 0)
    e = ACC[...]
    na = V[...]
    S[1:2, :] = jnp.sum(e * na, 0, keepdims=True)
    S[0:1, :] = jnp.zeros((1, D), F32)
    for j in range(4):
        S[3 + j : 4 + j, :] = gh_g[:, D * j : D * j + D]
    lane = lax.broadcasted_iota(jnp.int32, (1, 128), 1)
    S[7:8, :] = jnp.zeros((1, D), F32)
    S[7:8, 0:128] = sum(jnp.where(lane == i, sums[i : i + 1, :], 0.0) for i in range(PATTERNS))
    ACC[...] = norm_back(e * gi[...], na, rs_a)
    pairs_from_rows(ACC, dap)
    travel.start()

    def column(k):
        return chunk(k, lambda i, c: cols_t.at[lax.rem(k, 2), i, c])

    def out_copy(k):
        return pltpu.make_async_copy(c0.at[k], C0.at[k], osem.at[k])

    put_turned(th, tl, na * gi[...])
    r_hi[...], r_lo[...] = split(dy1)

    def column_step(k, carry):
        @pl.when(k < N_COLS)
        def _():
            @pl.when(k >= 2)
            def _():
                for i in range(2):
                    column(k - 2).core(i).wait_send()

            @pl.when(k >= 1)
            def _():
                r_hi[...], r_lo[...] = split(E[:, pl.ds(pl.multiple_of(D * (k - 1), D), D)])

            def put(i, v):
                cols_t[lax.rem(k, 2), i] = v.reshape(2, 4, 2, PIECE, D)

            product(th, tl, r_hi, r_lo, put)
            for i in range(2):
                column(k).core(i).start()

            @pl.when(k == 0)
            def _():
                put_turned(th, tl, N1[...] * gf[...])

        @pl.when(k > 0)
        def _():
            for i in range(2):
                column(k - 1).own_core(i)
            out_copy(k - 1).start()

        return carry

    lax.fori_loop(0, N_COLS + 1, column_step, 0)

    def c1_copy(k):
        b1, out = (c1a, C1a) if k % 2 == 0 else (c1b, C1b)
        i = (k - N_COLS) // 2
        return pltpu.make_async_copy(b1.at[i], out.at[i], osem.at[k])

    for k in range(N_COLS, N_FF):
        chunk(k).arrived()
        c1_copy(k).start()
    travel.finish()
    for k in range(N_COLS - 2, N_COLS):
        for i in range(2):
            column(jnp.int32(k)).core(i).wait_send()
    for j in range(2, 4):

        @pl.when(place.core != j % 2)
        def _(j=j):
            for q in range(4):
                down(jnp.int32(j), q).core(j // 2).wait_send()

    for k in range(N_COLS):
        out_copy(k).wait()
    for k in range(N_COLS, N_FF):
        chunk(k).one().wait_send()
        c1_copy(k).wait()


def feed_forward(rec, x, g, wo, wu, wd, gi, gf, gh, sums):
    act = jax.ShapeDtypeStruct((ROWS, D), F32)
    wide = pltpu.VMEM((ROWS, FF), F32)
    thin = pltpu.VMEM((ROWS, D), F32)
    return pl.pallas_call(
        ff_kernel,
        out_shape=[
            jax.ShapeDtypeStruct((ROWS, 1, D), F32),
            jax.ShapeDtypeStruct((HOMES, HALF, 128), F32),
            act,
            jax.ShapeDtypeStruct((8, D), F32),
            jax.ShapeDtypeStruct((N_COLS, 2, 4, 2, PIECE, D), F32),
            jax.ShapeDtypeStruct((2, 4, 2, PIECE, D), F32),
            jax.ShapeDtypeStruct((2, 2, 4, PIECE, D), F32),
        ],
        in_specs=[VM, VM, VM, ANY, ANY, ANY] + [VM] * 4,
        out_specs=[VM, ANY, VM, VM, ANY, ANY, ANY],
        scratch_shapes=[
            pltpu.VMEM((HEADS, HALF, 128), F32),
            pltpu.VMEM((2 * ROWS, D), BF16),
            pltpu.VMEM((2 * ROWS, FT), BF16),
            pltpu.VMEM((1, D), F32),
            pltpu.VMEM((1, D), F32),
            pltpu.VMEM((1, FF), F32),
            pltpu.VMEM((1, FF), F32),
            thin,
            thin,
            thin,
            thin,
            wide,
            wide,
            wide,
            thin,
        ]
        + [
            pltpu.VMEM((D, ROWS), BF16),
            pltpu.VMEM((D, ROWS), BF16),
            pltpu.VMEM((ROWS, D), BF16),
            pltpu.VMEM((ROWS, D), BF16),
            pltpu.VMEM((2, 2, 2, 4, 2, PIECE, D), F32),
            pltpu.VMEM((2, 4, 2, 4, PIECE, D), F32),
            pltpu.VMEM((N_FF, 2, 4, 2, PIECE, D), F32),
            pltpu.VMEM((2, 4, 2, PIECE, D), F32),
            pltpu.VMEM((2, 2, 4, PIECE, D), F32),
            pltpu.SemaphoreType.DMA((N_FF,)),
            pltpu.VMEM((D, D), BF16),
            pltpu.VMEM((D, FF), BF16),
            pltpu.VMEM((FF, D), BF16),
            pltpu.SemaphoreType.DMA((3,)),
            pltpu.SemaphoreType.DMA((HEADS,)),
            pltpu.SemaphoreType.DMA((HOMES,)),
        ]
        + Sems.scratch(N_FF),
        compiler_params=params(collective_id=4, has_side_effects=True),
    )(rec, x, g, wo, wu, wd, gi, gf, gh, sums)


def back_all_kernel(offs, drec, own, sib, ap, lse, C0, C1a, C1b, grec, wo_g, up_g, down_g, qst, kc, vc, kt, qc, dc, lt, k4, v4, kt4, q4, d4, lt4, k5, v5, kt5, q5, d5, lt5, dk, dv, dq, dk4, dv4, dk5, dv5, dq4, dq5, b1, b2, b3, b4, dqt, ds_out, came, lsem, send, recv, qsend, qrecv, fsend, frecv, c0, c1a, c1b, c2, zl, zr, csem, *rsems):
    place = Place()
    p, s, x, core, active, head = place_facts()
    b = core
    o2, o3, o4, o5 = (offs[i, head] for i in range(1, PATTERNS))
    kvf, qf, X, df = dk, dv.at[0:2], dv.at[2:4], dq
    dqp = qst

    barrier = pltpu.get_barrier_semaphore()
    expected = place.greet(barrier)

    def greet_heads(h, carry):
        q, t = head_device(h, x)

        @pl.when(jnp.logical_not(same(p, s, q, t)))
        def _():
            pl.semaphore_signal(barrier, inc=1, device_id=to(q, t), device_id_type=MESH)

        return carry

    lax.fori_loop(0, HEADS, greet_heads, 0)
    from_homes = HOMES - (core == x).astype(jnp.int32)
    pl.semaphore_wait(barrier, expected + active.astype(jnp.int32) * from_homes)

    def put(k, v):
        @pl.when(k == 0)
        def _():
            wo_g[...] = v

        @pl.when(jnp.logical_and(k > 0, k < 5))
        def _():
            up_g[:, pl.ds(pl.multiple_of((k - 1) * D, D), D)] = v

        @pl.when(k >= 5)
        def _():
            down_g[pl.ds(pl.multiple_of((k - 5) * PIECE, PIECE), PIECE), :] = v

    sems = Sems(rsems)

    def chunk(k):
        x_first = k % 2 == 0
        b0 = c0.at[k] if k < N_COLS else None
        b1 = (c1a if x_first else c1b).at[k // 2]
        return Chunk(
            place, k, x_first, sems, b0, b1, c2.at[k], zl.at[k], zr.at[k], put=lambda v: put(jnp.int32(k), v)
        )

    def load(k):
        if k < N_COLS:
            return pltpu.make_async_copy(C0.at[k], c0.at[k], csem.at[k])
        src, dst = (C1a, c1a) if k % 2 == 0 else (C1b, c1b)
        return pltpu.make_async_copy(src.at[(k - N_COLS) // 2], dst.at[k // 2], csem.at[k])

    PAIRS = ((5, 6), (7, 8), (0, 1), (2, 3), (4,))

    def reduction(*todo):
        for stage, pair in todo:
            for k in PAIRS[pair]:
                if stage == 1:
                    load(k).wait()
                    chunk(k).one().start()
                elif stage == 2 and k >= N_COLS:
                    load(k).wait()
                    chunk(k).two().start()
                else:
                    getattr(chunk(k), f"stage{stage}")()


    def local_copies(m):
        t = pl.multiple_of((m // 2) * ROWS, 64)
        c, d = 2 * b + lax.rem(m, 2), 2 * (1 - b) + lax.rem(m, 2)
        return [
            pltpu.make_async_copy(own.at[m, pl.ds(0, ROWS), :], kvf.at[c, pl.ds(t, ROWS), :], lsem.at[m, 0]),
            pltpu.make_async_copy(sib.at[m], kvf.at[d, pl.ds(t, ROWS), :], lsem.at[m, 1]),
            pltpu.make_async_copy(own.at[m, pl.ds(ROWS, HALF), :], qst.at[m], lsem.at[m, 2]),
        ]

    lse_copy = pltpu.make_async_copy(lse, X, lsem.at[HOMES, 0])

    @pl.when(active)
    def _():
        lse_copy.start()

        def start(m, carry):
            for c in local_copies(m):
                c.start()
            return carry

        lax.fori_loop(0, HOMES, start, 0)

    for pair in PAIRS:
        for k in pair:
            load(k).start()
    reduction((2, 0), (1, 2), (2, 1))

    @pl.when(active)
    def _():
        b1[...] = key_bias((2, 128), (4, 128), 4, 1, 2 * b, True)
        b2[...] = key_bias((1, 256), (2, 256), 4, 2, 2 * b, True)
        for i in range(2):
            b3[i] = key_bias((1, 256), (1, 512), 1, 1, 256 * i, True)
        b3[2] = jnp.zeros((512, 256), F32)
        e4 = class_facts4(o4, b)[1]
        b4[0] = key_bias((1, 256), (2, 256), 12, 6, 6 * e4, True)
        b4[1] = jnp.zeros((512, 256), F32)

        def wait(m, carry):
            for c in local_copies(m):
                c.wait()
            return carry

        lax.fori_loop(0, HOMES, wait, 0)
        lse_copy.wait()
        unpack_pairs(qst, 0, qf, 1.0 / math.sqrt(HD))

        def prepare(i, carry):
            c, t = i // 12, pl.multiple_of(lax.rem(i, 12) * 128, 128)
            k2, v2 = keys_and_values(kvf[c, pl.ds(t, 128), :])
            kc[c, pl.ds(t, 128), :] = k2.astype(BF16)
            vc[c, pl.ds(t, 128), :] = v2.astype(BF16)
            kt[c, :, pl.ds(t, 128)] = k2.T.astype(BF16)
            return carry

        lax.fori_loop(0, 48, prepare, 0)

        def prepare_q(i, carry):
            c, t = i // 12, pl.multiple_of(lax.rem(i, 12) * 128, 128)
            qc[c, pl.ds(t, 128), :] = query_quads(qf[c, pl.ds(t, 128), :])
            return carry

        lax.fori_loop(0, 24, prepare_q, 0)

    keys4, e4, (qc4, qv4) = class_facts4(o4, b)
    kc5, kv5 = lax.rem(o5, 4), o5 // 4
    qi4, qi5 = qc4 - 2 * b, lax.rem(kc5, 2)

    @pl.when(active)
    def _():
        for blk in range(4):
            r = slice(128 * blk, 128 * blk + 128)
            for e in range(2):
                c, v = keys4[e]
                k2, v2 = keys_and_values(kvf[c, pl.ds(v + 384 * blk, 128, stride=3), :])
                k4[e, r, :] = k2.astype(BF16)
                v4[e, r, :] = v2.astype(BF16)
                kt4[e, :, r] = k2.T.astype(BF16)
            q4[r, :] = query_quads(qf[qi4, pl.ds(qv4 + 384 * blk, 128, stride=3), :])
            rows = pl.ds(kv5 + 384 * blk, 128, stride=3)
            k2, v2 = keys_and_values(kvf[kc5, rows, :])
            k5[r, :] = k2.astype(BF16)
            v5[r, :] = v2.astype(BF16)
            kt5[:, r] = k2.T.astype(BF16)
            q5[r, :] = query_quads(qf[qi5, rows, :])
        dk[...] = jnp.zeros_like(dk)

    reduction((1, 3))

    @pl.when(active)
    def _():
        unpack_pairs(drec, 0, df, 1.0)

        def facts(m, carry):
            ci = lax.rem(m, 2)
            t = pl.multiple_of((m // 2) * ROWS, 32)
            prod = drec[m] * ap[m]
            low = lower_lanes(prod)
            d0 = jnp.sum(jnp.where(low, prod, 0.0), -1, keepdims=True)
            d1 = jnp.sum(jnp.where(low, 0.0, prod), -1, keepdims=True)
            for part, d in ((0, d0), (1, d1)):
                rows = pl.ds(t + HALF * part, HALF)
                l = X[ci, rows, :]
                X[ci, rows, :] = jnp.where(low, l, jnp.broadcast_to(d, l.shape))
            return carry

        lax.fori_loop(0, HOMES, facts, 0)

        def turned(v):
            w = v.T
            return jnp.concatenate([w[0:1, :], w[HD : HD + 1, :]], 0)

        def prepare_d(i, carry):
            c, t = i // 12, pl.multiple_of(lax.rem(i, 12) * 128, 128)
            rows = pl.ds(t, 128)
            dc[c, rows, :] = query_quads(df[c, rows, :])
            lt[i] = turned(X[c, rows, :])
            return carry

        lax.fori_loop(0, 24, prepare_d, 0)
        for blk in range(4):
            r = slice(128 * blk, 128 * blk + 128)
            rows = pl.ds(qv4 + 384 * blk, 128, stride=3)
            d4[r, :] = query_quads(df[qi4, rows, :])
            lt4[blk] = turned(X[qi4, rows, :])
            rows = pl.ds(kv5 + 384 * blk, 128, stride=3)
            d5[r, :] = query_quads(df[qi5, rows, :])
            lt5[blk] = turned(X[qi5, rows, :])
        dv[...] = jnp.zeros_like(dv)
        dq[...] = jnp.zeros_like(dq)

    def tile(k, v, kT, q, d, facts_pair, bias, classes=1):
        n = k.shape[0]
        each, edge = n // classes, bias.shape[0] // classes
        s_ = dot_nt(doubled(k), q)
        if each == edge:
            s_ = s_ + bias
        else:
            s_ = s_.reshape(classes, each, 256)
            last = s_[:, each - edge :] + bias.reshape(classes, edge, 256)
            s_ = jnp.concatenate([s_[:, : each - edge], last], 1).reshape(n, 256)
        l0, l1 = facts_pair
        row = jnp.concatenate([l0[0:1, :], l1[0:1, :]], 1)
        delta = jnp.concatenate([l0[1:2, :], l1[1:2, :]], 1)
        pr = jnp.exp(s_ - row)
        ds = pr * (dot_nt(doubled(v), d) - delta)
        hi, lo = split(pr)
        d2, q2_ = d[:, :128], q[:, :128]
        dv_new = dot_nn(jnp.concatenate([hi, lo], 1), jnp.concatenate([d2, d2], 0))
        hi, lo = split(ds)
        dk_new = dot_nn(jnp.concatenate([hi, lo], 1), jnp.concatenate([q2_, q2_], 0))
        dq_new = dot_nn(kT, hi) + dot_nn(kT, lo)
        return dk_new, dv_new, dq_new

    def kept(flag, v):
        return jnp.where(flag, v, 0.0)

    def at256(blk):
        return pl.ds(pl.multiple_of(256 * blk, 128), 256)

    def sweep(last, step, done):
        dqt[...] = jnp.zeros_like(dqt)

        def one(kb, carry):
            step(kb, kb == last)
            return carry

        lax.fori_loop(0, last + 1, one, 0)
        done(dqt[...].T)

    def tile2(base, qb):
        keys = 256 * (qb + 1)
        ks = pl.ds(pl.multiple_of(base, 1024), keys)
        qs = pl.ds(pl.multiple_of(base + 256 * qb, 256), 256)
        blk = (base + 256 * qb) // 128
        a, c, e = tile(
            jnp.concatenate([kc[o2, ks, :], kc[o2 + 2, ks, :]], 0),
            jnp.concatenate([vc[o2, ks, :], vc[o2 + 2, ks, :]], 0),
            jnp.concatenate([kt[o2, :, ks], kt[o2 + 2, :, ks]], 1),
            qc[o2, qs, :],
            dc[o2, qs, :],
            (lt.at[12 * o2 + blk], lt.at[12 * o2 + blk + 1]),
            b2[...],
            2,
        )
        e = e.T
        for par in range(2):
            f = o2 == par
            dk[par, ks, :] += kept(f, a[:keys])
            dk[par + 2, ks, :] += kept(f, a[keys:])
            dv[par, ks, :] += kept(f, c[:keys])
            dv[par + 2, ks, :] += kept(f, c[keys:])
            dq[par, qs, :] += kept(f, e)

    @pl.when(active)
    def _():
        def first_half(i, carry):
            for qb in range(2):
                tile2(1024 * i, qb)
            return carry

        lax.fori_loop(0, 2, first_half, 0)
        for qb in range(2, 4):
            tile2(0, qb)

    reduction((3, 0), (2, 2), (3, 1), (1, 4))

    def q3(qb, carry):
        ci = lax.rem(o3, 2)
        qs = at256(qb)

        def step(kb, own):
            ks = pl.ds(pl.multiple_of(512 * kb, 512), 512)
            a, c, e = tile(
                kc[o3, ks, :],
                vc[o3, ks, :],
                kt[o3, :, ks],
                qc[ci, qs, :],
                dc[ci, qs, :],
                (lt.at[12 * ci + 2 * qb], lt.at[12 * ci + 2 * qb + 1]),
                b3[jnp.where(own, lax.rem(qb, 2), 2)],
            )
            dqt[...] += e
            for i in range(2):
                f = o3 == 2 * b + i
                dk[2 * b + i, ks, :] += kept(f, a)
                dv[2 * b + i, ks, :] += kept(f, c)

        def done(e):
            for i in range(2):
                dq[i, qs, :] += kept(o3 == 2 * b + i, e)

        sweep(qb // 2, step, done)
        return carry

    def q4_(qb, carry):
        qs = at256(qb)

        def step(kb, own):
            ks = at256(kb)
            a, c, e = tile(
                k4[:, ks, :].reshape(512, 128),
                v4[:, ks, :].reshape(512, 128),
                jnp.concatenate([kt4[0, :, ks], kt4[1, :, ks]], 1),
                q4[qs, :],
                d4[qs, :],
                (lt4.at[2 * qb], lt4.at[2 * qb + 1]),
                b4[jnp.where(own, 0, 1)],
            )
            dqt[...] += e
            dk4[:, ks, :] += a.reshape(2, 256, 128)
            dv4[:, ks, :] += c.reshape(2, 256, 128)

        def done(e):
            dq4[qs, :] = e

        sweep(qb, step, done)
        return carry

    def q5_(qb, carry):
        qs = at256(qb)

        a, c, e = tile(
            k5[...], v5[...], kt5[...], q5[qs, :], d5[qs, :], (lt5.at[2 * qb], lt5.at[2 * qb + 1]), b3[qb]
        )
        dk5[...] += a
        dv5[...] += c
        dq5[qs, :] = e.T
        return carry

    @pl.when(active)
    def _():
        lax.fori_loop(0, TOTAL // 256, q3, 0)
        for ref in (dk4, dv4, dk5, dv5):
            ref[...] = jnp.zeros_like(ref)
        lax.fori_loop(0, 2, q4_, 0)
        lax.fori_loop(0, 2, q5_, 0)
        mine5 = kc5 // 2 == b
        for kind in range(12):
            c, rows = kind % 4, pl.ds(kind // 4, THIRD, stride=3)
            f0, f1, f5 = o4 == kind, o4 + 6 == kind, jnp.logical_and(o5 == kind, mine5)
            dk[c, rows, :] += kept(f0, dk4[0]) + kept(f1, dk4[1]) + kept(f5, dk5[...])
            dv[c, rows, :] += kept(f0, dv4[0]) + kept(f1, dv4[1]) + kept(f5, dv5[...])
        for ci in range(2):
            for v in range(3):
                rows = pl.ds(v, THIRD, stride=3)
                f4 = jnp.logical_and(qi4 == ci, qv4 == v)
                f5 = jnp.logical_and(jnp.logical_and(qi5 == ci, kv5 == v), mine5)
                dq[ci, rows, :] += kept(f4, dq4[...]) + kept(f5, dq5[...])

    reduction((4, 0), (4, 1), (2, 3), (3, 2))

    def segment(g):
        def at(t, n):
            return pl.ds(pl.multiple_of(512 * g + t, 128), n)

        for qb in range(4):
            keys = 128 * (qb + 1)
            ks, qs = at(0, keys), at(128 * qb, 128)
            a, c, e = tile(
                kc[:, ks, :].reshape(4 * keys, 128),
                vc[:, ks, :].reshape(4 * keys, 128),
                jnp.concatenate([kt[i, :, ks] for i in range(4)], 1),
                qc[:, qs, :].reshape(256, 256),
                dc[:, qs, :].reshape(256, 256),
                (lt.at[4 * g + qb], lt.at[12 + 4 * g + qb]),
                b1[...],
                4,
            )
            dk[:, ks, :] += a.reshape(4, keys, 128)
            dv[:, ks, :] += c.reshape(4, keys, 128)
            dq[:, qs, :] += e.T.reshape(2, 128, 128)

    def passed(m):
        return remote(ds_out.at[m], came.at[m], fsend.at[m], frecv.at[m], place.peer)

    def home_copies(m):
        q, t = home_device(core, m)
        kv = remote(came.at[m], grec.at[head, pl.ds(0, ROWS), :], send.at[m], recv.at[head], to(q, t))
        dq_ = remote(dqp.at[m], grec.at[head, pl.ds(ROWS, HALF), :], qsend.at[m], qrecv.at[head], to(q, t))
        return q, t, kv, dq_

    def rows_of(m):
        return pl.ds(pl.multiple_of((m // 2) * ROWS, 64), ROWS)

    def kv(c, m):
        k, v = dk[c, rows_of(m), :], dv[c, rows_of(m), :]
        return pick(k + swap(k), v + swap(v))

    def share(m, carry):
        ds_out[m] = kv(2 * (1 - b) + lax.rem(m, 2), m)
        passed(m).start()
        return carry

    def add(m, carry):
        q, t, far_kv, far_q = home_copies(m)
        ci = lax.rem(m, 2)
        v = dq[ci, rows_of(m), :]
        v = (v + swap(v)) * (1.0 / math.sqrt(HD))
        dqp[m] = pick(v[:HALF], v[HALF:])
        passed(m).wait_recv()
        came[m] += kv(2 * b + ci, m)

        @pl.when(same(p, s, q, t))
        def _():
            pltpu.make_async_copy(came.at[m], grec.at[head, pl.ds(0, ROWS), :], recv.at[head]).start()
            pltpu.make_async_copy(dqp.at[m], grec.at[head, pl.ds(ROWS, HALF), :], qrecv.at[head]).start()

        @pl.when(jnp.logical_not(same(p, s, q, t)))
        def _():
            far_kv.start()
            far_q.start()

        return carry

    def round_of(i, carry):
        g = jnp.where(i == 0, 0, 3 - i)

        @pl.when(active)
        def _():
            segment(g)
            lax.fori_loop(jnp.where(i == 0, 0, jnp.where(i == 1, 12, 4)), jnp.where(i == 0, 4, jnp.where(i == 1, 16, 12)), share, 0)

            @pl.when(i > 0)
            def _():
                lax.fori_loop(jnp.where(i == 1, 0, 12), jnp.where(i == 1, 4, 16), add, 0)

        @pl.when(i == 1)
        def _():
            reduction((5, 0), (5, 1), (2, 4), (3, 3), (4, 2))

        return carry

    lax.fori_loop(0, 3, round_of, 0)

    @pl.when(active)
    def _():
        lax.fori_loop(4, 12, add, 0)

    reduction((6, 0), (6, 1), (3, 4), (4, 3), (5, 2))
    reduction((4, 4), (5, 3), (6, 2))
    reduction((5, 4), (6, 3))
    reduction((6, 4))

    def from_head(h, carry):
        a = grec.at[h, pl.ds(0, ROWS), :]
        c = grec.at[h, pl.ds(ROWS, HALF), :]
        pltpu.make_async_copy(a, a, recv.at[h]).wait()
        pltpu.make_async_copy(c, c, qrecv.at[h]).wait()
        return carry

    lax.fori_loop(0, HEADS, from_head, 0)
    for k in range(N_FF):
        if k < N_COLS:
            chunk(k).one().wait_send()
        chunk(k).two().wait_send()
        chunk(k).line_sent()

    @pl.when(active)
    def _():
        def sent(m, carry):
            q, t, far_kv, far_q = home_copies(m)
            passed(m).wait_send()

            @pl.when(jnp.logical_not(same(p, s, q, t)))
            def _():
                far_kv.wait_send()
                far_q.wait_send()

            return carry

        lax.fori_loop(0, HOMES, sent, 0)


def backward_all(offs, drec, own, sib, ap, lse, C0, C1a, C1b, cid):
    dma = pltpu.SemaphoreType.DMA
    keys = pltpu.VMEM((4, TOTAL, 128), BF16)
    full = pltpu.VMEM((4, TOTAL, 128), F32)
    quad = pltpu.VMEM((2, TOTAL, 256), BF16)
    quad3 = pltpu.VMEM((THIRD, 256), BF16)
    pair3 = pltpu.VMEM((THIRD, 128), BF16)
    turned = pltpu.VMEM((128, THIRD), BF16)
    facts3 = pltpu.VMEM((4, 2, 128), F32)
    out3 = pltpu.VMEM((THIRD, 128), F32)
    packs = pltpu.VMEM((HOMES, ROWS, 128), F32)
    halves = pltpu.VMEM((HOMES, HALF, 128), F32)
    return pl.pallas_call(
        back_all_kernel,
        out_shape=[
            jax.ShapeDtypeStruct((HEADS, PACK, 128), F32),
            jax.ShapeDtypeStruct((PIECE, D), F32),
            jax.ShapeDtypeStruct((PIECE, FF), F32),
            jax.ShapeDtypeStruct((4 * PIECE, D), F32),
        ],
        in_specs=[SM, VM, ANY, ANY, VM, ANY, ANY, ANY, ANY],
        out_specs=[ANY, VM, VM, VM],
        scratch_shapes=[
            halves,
            keys,
            keys,
            pltpu.VMEM((4, 128, TOTAL), BF16),
            quad,
            quad,
            pltpu.VMEM((24, 2, 128), F32),
            pltpu.VMEM((2, THIRD, 128), BF16),
            pltpu.VMEM((2, THIRD, 128), BF16),
            pltpu.VMEM((2, 128, THIRD), BF16),
            quad3,
            quad3,
            facts3,
            pair3,
            pair3,
            turned,
            quad3,
            quad3,
            facts3,
            full,
            full,
            pltpu.VMEM((2, TOTAL, 128), F32),
            pltpu.VMEM((2, THIRD, 128), F32),
            pltpu.VMEM((2, THIRD, 128), F32),
            out3,
            out3,
            out3,
            out3,
            pltpu.VMEM((512, 256), F32),
            pltpu.VMEM((512, 256), F32),
            pltpu.VMEM((3, 512, 256), F32),
            pltpu.VMEM((2, 512, 256), F32),
            pltpu.VMEM((128, 256), F32),
            packs,
            packs,
            dma((HOMES + 1, 3)),
            dma((HOMES,)),
            dma((HEADS,)),
            dma((HOMES,)),
            dma((HEADS,)),
            dma((HOMES,)),
            dma((HOMES,)),
            pltpu.VMEM((N_COLS, 2, 4, 2, PIECE, D), F32),
            pltpu.VMEM((5, 4, 2, PIECE, D), F32),
            pltpu.VMEM((4, 2, 4, PIECE, D), F32),
            pltpu.VMEM((N_FF, 4, PIECE, D), F32),
            pltpu.VMEM((N_FF, 4, PIECE, D), F32),
            pltpu.VMEM((N_FF, 4, PIECE, D), F32),
            dma((N_FF,)),
        ]
        + Sems.scratch(N_FF),
        compiler_params=params(collective_id=cid, has_side_effects=True),
    )(offs, drec, own, sib, ap, lse, C0, C1a, C1b)


SEG1, SEG2, SEG3, SEG4, SEG5 = SEGMENTS
DILATION_ONE, DILATION_TWO, DILATION_THREE, DILATION_FOUR, DILATION_FIVE = DILATIONS
MASK_VALUE = -1e30
MATMUL_ACCURACY = lax.Precision.HIGHEST


def passed_along(value, axis, by):
    length = lax.axis_size(axis)
    return lax.ppermute(value, axis, [(i, (i + by) % length) for i in range(length)])


def run_is_live(distance, anchor_point, sequence_width, segment_length):
    return (anchor_point - (distance - 1) * sequence_width - 1) // segment_length == anchor_point // segment_length


def layer_norm(x, gain_vec):
    average = jnp.mean(x, -1, keepdims=True)
    centred = x - average
    variance = jnp.mean(centred * centred, -1, keepdims=True)
    return centred * lax.rsqrt(variance + LN_EPSILON) * gain_vec


def select_table(offsets_row, dilation_rate):
    return (jnp.arange(dilation_rate, dtype=jnp.int32)[:, None] == offsets_row[None, :]).astype(
        jnp.float32
    )


def spread_apart(x, select_option, dilation_rate):
    shaped = x.reshape(x.shape[0] // dilation_rate, dilation_rate, x.shape[1], x.shape[2])
    return jnp.einsum("trhd,rh->thd", shaped, select_option, precision=MATMUL_ACCURACY)


def spread_scalar_rows(x, select_option, dilation_rate):
    shaped = x.reshape(x.shape[0] // dilation_rate, dilation_rate, x.shape[1])
    return jnp.einsum("trh,rh->th", shaped, select_option, precision=MATMUL_ACCURACY)


def spread_rows(x, select_option):
    return jnp.einsum("thd,rh->trhd", x, select_option, precision=MATMUL_ACCURACY).reshape(
        -1, x.shape[1], x.shape[2]
    )


def spread_scalars(x, select_option):
    return jnp.einsum("th,rh->trh", x, select_option, precision=MATMUL_ACCURACY).reshape(
        -1, x.shape[1]
    )


def masked_score_matrix(sparse_queries, key_portion, query_position, key_position, segment_length):
    score_matrix = jnp.einsum(
        "ozt,bzt->zob", sparse_queries, key_portion, precision=MATMUL_ACCURACY
    ) * (1.0 / math.sqrt(key_portion.shape[-1]))
    q_cols = query_position.T[:, :, None]
    k_cols = key_position.T[:, None, :]
    permitted_mask = (k_cols <= q_cols) & (k_cols // segment_length == q_cols // segment_length)
    return (jnp.where(permitted_mask, score_matrix, MASK_VALUE), permitted_mask)


def prepare_pattern(
    query_sequence, key_sequence, value_sequence, offsets_row, dilation_rate, anchor_point
):
    select_option = select_table(offsets_row, dilation_rate)
    sparse_queries = spread_apart(query_sequence, select_option, dilation_rate)
    sparse_key_value = jnp.stack(
        (
            spread_apart(key_sequence, select_option, dilation_rate),
            spread_apart(value_sequence, select_option, dilation_rate),
        )
    )
    query_position = (
        anchor_point
        + jnp.arange(sparse_queries.shape[0], dtype=jnp.int32)[:, None] * dilation_rate
        + offsets_row[None, :]
    )
    return (select_option, sparse_queries, sparse_key_value, query_position)


def pattern_forward_pass(
    sparse_queries,
    sparse_key_value,
    query_position,
    reach,
    segment_length,
    anchor_point,
    sequence_width,
):
    masked_logits, permitted_mask = masked_score_matrix(
        sparse_queries, sparse_key_value[0], query_position, query_position, segment_length
    )
    row_max = jnp.max(masked_logits, -1)
    softmax_weights = jnp.where(permitted_mask, jnp.exp(masked_logits - row_max[..., None]), 0.0)
    state = (
        row_max,
        jnp.sum(softmax_weights, -1),
        jnp.einsum("tlj,jtb->tlb", softmax_weights, sparse_key_value[1], precision=MATMUL_ACCURACY),
    )

    def one_run(distance, carry):
        remote_key_value, state = carry
        remote_key_value = passed_along(remote_key_value, "seq", 1)
        key_position = query_position - distance * sequence_width

        def update(state_in):
            old_max, old_sum, old_acc = state_in
            masked_remote, permitted_remote = masked_score_matrix(
                sparse_queries, remote_key_value[0], query_position, key_position, segment_length
            )
            new_max = jnp.maximum(old_max, jnp.max(masked_remote, -1))
            weights_far = jnp.where(
                permitted_remote, jnp.exp(masked_remote - new_max[..., None]), 0.0
            )
            factor = jnp.exp(old_max - new_max)
            added = jnp.einsum(
                "tlj,jtb->tlb", weights_far, remote_key_value[1], precision=MATMUL_ACCURACY
            )
            return (
                new_max,
                old_sum * factor + jnp.sum(weights_far, -1),
                old_acc * factor[..., None] + added,
            )

        def unchanged(state_in):
            return state_in

        is_live = run_is_live(distance, anchor_point, sequence_width, segment_length)
        return remote_key_value, lax.cond(is_live, update, unchanged, state)

    state = lax.fori_loop(1, reach + 1, one_run, (sparse_key_value, state))[1]
    row_max, row_sum, accumulated = state
    mixture = jnp.transpose(accumulated / row_sum[..., None], (1, 0, 2))
    log_sum = (row_max + jnp.log(row_sum)).T
    return (mixture, log_sum)


def merge_patterns(forwards, prepared_inputs):
    full_lse = []
    full_mix = []
    for pattern_spec in range(len(forwards)):
        mixture, log_sum = forwards[pattern_spec]
        select_option = prepared_inputs[pattern_spec][0]
        covered = spread_scalars(jnp.ones_like(log_sum), select_option)
        full_lse.append(spread_scalars(log_sum, select_option) + (covered - 1.0) * 1e30)
        full_mix.append(spread_rows(mixture, select_option))
    stacked = jnp.stack(full_lse)
    row_max = jnp.max(stacked, 0)
    softmax_weights = jnp.exp(stacked - row_max)
    row_sum = jnp.sum(softmax_weights, 0)
    attended = full_mix[0] * softmax_weights[0][..., None]
    for pattern_spec in range(1, len(full_mix)):
        attended = attended + full_mix[pattern_spec] * softmax_weights[pattern_spec][..., None]
    return (attended / row_sum[..., None], row_max + jnp.log(row_sum))


def pattern_backward(
    select_option,
    dilation_rate,
    segment_length,
    anchor_point,
    sparse_queries,
    sparse_key_value,
    query_position,
    reach,
    sequence_gradient,
    row_difference,
    combined_logsumexp,
):
    sequence_width = sequence_gradient.shape[0]
    sparse_gradient = spread_apart(sequence_gradient, select_option, dilation_rate)
    sparse_output_grad = spread_scalar_rows(row_difference, select_option, dilation_rate).T
    sparse_logsumexp = spread_scalar_rows(combined_logsumexp, select_option, dilation_rate).T
    inverse_square_root = 1.0 / math.sqrt(sparse_queries.shape[-1])

    def portion_gradients(key_portion, value_portion, key_position):
        masked_logits, permitted_mask = masked_score_matrix(
            sparse_queries, key_portion, query_position, key_position, segment_length
        )
        softmax_weights = jnp.where(
            permitted_mask, jnp.exp(masked_logits - sparse_logsumexp[..., None]), 0.0
        )
        value_gradient = jnp.einsum(
            "tui,utx->itx", softmax_weights, sparse_gradient, precision=MATMUL_ACCURACY
        )
        pattern_gradient = jnp.einsum(
            "ozt,bzt->zob", sparse_gradient, value_portion, precision=MATMUL_ACCURACY
        )
        score_gradient = (
            softmax_weights
            * (pattern_gradient - sparse_output_grad[..., None])
            * inverse_square_root
        )
        query_gradient = jnp.einsum(
            "hqk,khd->qhd", score_gradient, key_portion, precision=MATMUL_ACCURACY
        )
        key_gradient = jnp.einsum(
            "tui,utx->itx", score_gradient, sparse_queries, precision=MATMUL_ACCURACY
        )
        return (query_gradient, jnp.stack((key_gradient, value_gradient)))

    query_gradient, key_value_gradient = portion_gradients(
        sparse_key_value[0], sparse_key_value[1], query_position
    )

    def one_run(distance, carry):
        remote_key_value, remote_gradient, query_sum = carry
        remote_key_value = passed_along(remote_key_value, "seq", 1)
        remote_gradient = passed_along(remote_gradient, "seq", 1)
        key_position = query_position - distance * sequence_width

        def far_grads():
            part_q, part_kv = portion_gradients(remote_key_value[0], remote_key_value[1], key_position)
            return query_sum + part_q, remote_gradient + part_kv

        def no_grads():
            return query_sum, remote_gradient

        is_live = run_is_live(distance, anchor_point, sequence_width, segment_length)
        query_sum, remote_gradient = lax.cond(is_live, far_grads, no_grads)
        return remote_key_value, remote_gradient, query_sum

    _, travelled, query_gradient = lax.fori_loop(
        1, reach + 1, one_run, (sparse_key_value, key_value_gradient, query_gradient)
    )
    return (query_gradient, passed_along(travelled, "seq", -reach))


def front_part(own_rows, w_qkv, gain_attn):
    return jnp.dot(layer_norm(own_rows, gain_attn), w_qkv, precision=MATMUL_ACCURACY)


def after_part(attn_rows, own_rows, w_out, w_up, w_down, gain_inner, gain_ffn, gain_hidden):
    residual = own_rows + jnp.dot(
        layer_norm(attn_rows, gain_inner), w_out, precision=MATMUL_ACCURACY
    )
    hidden = jax.nn.gelu(
        jnp.dot(layer_norm(residual, gain_ffn), w_up, precision=MATMUL_ACCURACY), approximate=False
    )
    return residual + jnp.dot(layer_norm(hidden, gain_hidden), w_down, precision=MATMUL_ACCURACY)


def shards(
    tokens,
    w_qkv,
    w_out,
    w_up,
    w_down,
    gain_attn,
    gain_inner,
    gain_ffn,
    gain_hidden,
    offsets,
    grad_out,
):
    w_qkv = w_qkv.astype(jnp.float32)
    w_out = w_out.astype(jnp.float32)
    w_up = w_up.astype(jnp.float32)
    w_down = w_down.astype(jnp.float32)
    groups = lax.axis_size("pat")
    local_rows = tokens.shape[0]
    sequence_width = local_rows * groups
    heads_here = HEADS // groups
    own_rows = tokens.reshape(local_rows, D)
    qkv_rows, front_back = jax.vjp(front_part, own_rows, w_qkv, gain_attn)
    gathered_qkv = lax.all_to_all(
        qkv_rows.reshape(local_rows, 1, 3, HEADS, HD),
        "pat",
        split_axis=3,
        concat_axis=1,
        tiled=True,
    )
    gathered_qkv = gathered_qkv.reshape(sequence_width, 3, heads_here, HD)
    head_offsets = lax.dynamic_slice_in_dim(
        offsets, lax.axis_index("pat") * heads_here, heads_here, 1
    )
    anchor_point = lax.axis_index("seq") * sequence_width
    dilation_rates = (DILATION_ONE, DILATION_TWO, DILATION_THREE, DILATION_FOUR, DILATION_FIVE)
    segment_lengths = (SEG1, SEG2, SEG3, SEG4, SEG5)
    reaches = [
        min((segment_lengths[pattern_spec] - 2) // sequence_width + 1, lax.axis_size("seq") - 1)
        for pattern_spec in range(PATTERNS)
    ]
    prepared_inputs = []
    for pattern_spec in range(PATTERNS):
        prepared_inputs.append(
            prepare_pattern(
                gathered_qkv[:, 0],
                gathered_qkv[:, 1],
                gathered_qkv[:, 2],
                head_offsets[pattern_spec],
                dilation_rates[pattern_spec],
                anchor_point,
            )
        )
    forwards = []
    for pattern_spec in range(PATTERNS):
        select_option, sparse_queries, sparse_key_value, query_position = prepared_inputs[
            pattern_spec
        ]
        forwards.append(
            pattern_forward_pass(
                sparse_queries,
                sparse_key_value,
                query_position,
                reaches[pattern_spec],
                segment_lengths[pattern_spec],
                anchor_point,
                sequence_width,
            )
        )
    lse_sums = jnp.stack([jnp.sum(entry[1]) for entry in forwards])
    totals = lax.psum(lse_sums, ("pat", "seq"))
    full_length = sequence_width * lax.axis_size("seq")
    counts = jnp.array(
        [
            float(full_length // dilation_rates[pattern_spec] * HEADS)
            for pattern_spec in range(PATTERNS)
        ],
        jnp.float32,
    )
    log_means = totals / counts
    attended, combined_logsumexp = merge_patterns(forwards, prepared_inputs)
    returned_rows = lax.all_to_all(
        attended.reshape(local_rows, groups, heads_here, HD),
        "pat",
        split_axis=1,
        concat_axis=2,
        tiled=True,
    )
    attn_rows = returned_rows.reshape(local_rows, D)
    result, after_back = jax.vjp(
        after_part, attn_rows, own_rows, w_out, w_up, w_down, gain_inner, gain_ffn, gain_hidden
    )
    g_attn, g_resid, g_out, g_up, g_down, g_inner, g_ffn, g_hidden = after_back(
        grad_out.reshape(local_rows, D)
    )
    sequence_gradient = lax.all_to_all(
        g_attn.reshape(local_rows, 1, HEADS, HD), "pat", split_axis=2, concat_axis=1, tiled=True
    )
    sequence_gradient = sequence_gradient.reshape(sequence_width, heads_here, HD)
    row_difference = jnp.sum(sequence_gradient * attended, -1)
    q_grads = []
    kv_grads = []
    for pattern_spec in range(PATTERNS):
        select_option, sparse_queries, sparse_key_value, query_position = prepared_inputs[
            pattern_spec
        ]
        part_q, part_kv = pattern_backward(
            select_option,
            dilation_rates[pattern_spec],
            segment_lengths[pattern_spec],
            anchor_point,
            sparse_queries,
            sparse_key_value,
            query_position,
            reaches[pattern_spec],
            sequence_gradient,
            row_difference,
            combined_logsumexp,
        )
        q_grads.append(part_q)
        kv_grads.append(part_kv)
    grad_total = jnp.zeros((sequence_width, 3, heads_here, HD), jnp.float32)
    for pattern_spec in range(PATTERNS):
        select_option = prepared_inputs[pattern_spec][0]
        grad_total = grad_total + jnp.stack(
            (
                spread_rows(q_grads[pattern_spec], select_option),
                spread_rows(kv_grads[pattern_spec][0], select_option),
                spread_rows(kv_grads[pattern_spec][1], select_option),
            ),
            1,
        )
    grad_back = lax.all_to_all(
        grad_total.reshape(local_rows, groups, 3, heads_here, HD),
        "pat",
        split_axis=1,
        concat_axis=3,
        tiled=True,
    )
    g_tokens, g_qkv, g_attn_gain = front_back(grad_back.reshape(local_rows, 3 * D))
    grad_tokens = (g_resid + g_tokens).reshape(local_rows, 1, D)
    summed = (
        lax.psum_scatter(g_qkv, ("pat", "seq"), scatter_dimension=0, tiled=True),
        lax.psum_scatter(g_out, ("pat", "seq"), scatter_dimension=0, tiled=True),
        lax.psum_scatter(g_up, ("pat", "seq"), scatter_dimension=0, tiled=True),
        lax.psum_scatter(g_down, ("pat", "seq"), scatter_dimension=0, tiled=True),
        lax.psum_scatter(g_attn_gain, ("pat", "seq"), scatter_dimension=0, tiled=True),
        lax.psum_scatter(g_inner, ("pat", "seq"), scatter_dimension=0, tiled=True),
        lax.psum_scatter(g_ffn, ("pat", "seq"), scatter_dimension=0, tiled=True),
        lax.psum_scatter(g_hidden, ("pat", "seq"), scatter_dimension=0, tiled=True),
    )
    return (
        result.reshape(local_rows, 1, D),
        grad_tokens,
        summed[0],
        summed[1],
        summed[2],
        summed[3],
        summed[4],
        summed[5],
        summed[6],
        summed[7],
        log_means,
    )


def fast_shards(tokens, w_qkv, w_out, w_up, w_down, gain_attn, gain_inner, gain_ffn, gain_hidden, offsets, grad_out):
    counts = [float(TOTAL * 4 // r * HEADS) for r in DILATIONS]
    pk, x = front(tokens, w_qkv, gain_attn)
    own, sib = to_heads(pk, True, 0)
    ap, lse, sums = attention_forward(offsets, own, sib)
    rec = to_homes(ap, 1)
    mixed, drec, dy1, S, C0, C1a, C1b = feed_forward(
        rec, x, grad_out, w_out, w_up, w_down, gain_inner, gain_ffn, gain_hidden, sums
    )
    grec, g_out, g_up, g_down = backward_all(offsets, drec, own, sib, ap, lse, C0, C1a, C1b, 2)
    gx, g_qkv, *small = finish(grec, x, dy1, w_qkv, gain_attn, S, counts, 3)
    mixed, gx, g_qkv, g_out, g_up, g_down, *small = deliver(mixed, gx, g_qkv, g_out, g_up, g_down, *small)
    return (mixed, gx, g_qkv, g_out, g_up, g_down, *(v.reshape(-1) for v in small))


def fits(mesh):
    return mesh.shape["pat"] == 4 and mesh.shape["seq"] == RUNS


def solution(mesh):
    rows = P("seq", "pat", None)
    split_rows = P(("pat", "seq"), None)
    split_one = P(("pat", "seq"))
    planned = jax.shard_map(
        fast_shards,
        mesh=mesh,
        in_specs=(rows,) + (P(),) * 9 + (rows,),
        out_specs=(rows, rows) + (split_rows,) * 4 + (split_one,) * 4 + (P(),),
        check_vma=False,
    )
    general = jax.shard_map(
        shards,
        mesh=mesh,
        in_specs=(rows,) + (P(),) * 9 + (rows,),
        out_specs=(rows, rows) + (split_rows,) * 4 + (split_one,) * 4 + (P(),),
        check_vma=False,
    )

    def layer(tokens, *rest):
        if fits(mesh) and tokens.shape[0] == TOTAL:
            return planned(tokens, *rest)
        return general(tokens, *rest)

    return layer
```

```python
import functools
import math

import jax
import jax.numpy as jnp
from jax import lax
from jax.experimental import pallas as pl
from jax.experimental.pallas import tpu as pltpu
from jax.sharding import PartitionSpec as P

D = 768
HEADS = 12
HD = 64
FF = 3072
PATTERNS = 5
SEGMENTS = (2048, 4096, 8192, 16384, 32768)
DILATIONS = (1, 2, 4, 6, 12)
LN_EPSILON = 1e-05
NEG = -1e30
F32 = jnp.float32
BF16 = jnp.bfloat16
HIGHEST = lax.Precision.HIGHEST
VMEM_LIMIT = 60 * 1024 * 1024

ROWS = 192
HALF = ROWS // 2
RUNS = 8
TOTAL = ROWS * RUNS
PACK = ROWS + HALF
HOMES = 16
THIRD = TOTAL // 3
PIECE = 24
MESH = pl.DeviceIdType.MESH


def dot_nn(a, b):
    return lax.dot_general(a, b, (((1,), (0,)), ((), ())), preferred_element_type=F32)


def dot_nt(a, b):
    return lax.dot_general(a, b, (((1,), (1,)), ((), ())), preferred_element_type=F32)


def split(v):
    hi = v.astype(BF16)
    return hi, (v - hi.astype(F32)).astype(BF16)


def split32(v):
    hi = v.astype(BF16).astype(F32)
    return hi, v - hi


def lower_lanes(v):
    return lax.broadcasted_iota(jnp.int32, v.shape, v.ndim - 1) < HD


def swap(v):
    return pltpu.roll(v, HD, v.ndim - 1)


def pick(a, b):
    return jnp.where(lower_lanes(a), a, b)


def head_place(h):
    z = h // 3
    column = lax.rem(lax.rem(h, 3) + z + 1, 4)
    return column // 2, z * 2 + lax.rem(column, 2)


def head_here(p, s):
    z = s // 2
    column = (p // 2) * 2 + lax.rem(s, 2)
    k = lax.rem(column - z + 7, 4)
    return k < 3, z * 3 + jnp.minimum(k, 2)


def whole(*_):
    return pl.BlockSpec(memory_space=pltpu.VMEM)


VM = pl.BlockSpec(memory_space=pltpu.VMEM)
ANY = pl.BlockSpec(memory_space=pl.ANY)
SM = pl.BlockSpec(memory_space=pltpu.SMEM)


def params(**kw):
    return pltpu.CompilerParams(vmem_limit_bytes=VMEM_LIMIT, **kw)


def normed(v):
    centred = v - jnp.mean(v, -1, keepdims=True)
    rs = lax.rsqrt(jnp.mean(centred * centred, -1, keepdims=True) + LN_EPSILON)
    return centred * rs, rs


def put_split(ref, v):
    hi, lo = split(v)
    n = v.shape[0]
    ref[0:n, :] = hi
    ref[n : 2 * n, :] = lo


def front_kernel(x3, w_ref, gain_ref, pk_ref, x_ref, lhs):
    x = x3[...].reshape(ROWS, D)
    x_ref[...] = x
    n, _ = normed(x)
    put_split(lhs, n * gain_ref[...][None, :])
    for jj in range(3):
        parts = []
        for kind in range(3):
            c0 = kind * D + 256 * jj
            r = dot_nn(lhs[...], w_ref[:, c0 : c0 + 256])
            parts.append(r[:ROWS] + r[ROWS:])
        for half in range(2):
            q, k, v = (a[:, 128 * half : 128 * half + 128] for a in parts)
            h = 4 * jj + 2 * half
            pk_ref[h, 0:ROWS, :] = pick(k, swap(v))
            pk_ref[h + 1, 0:ROWS, :] = pick(swap(k), v)
            top, bottom = q[:HALF], q[HALF:]
            pk_ref[h, ROWS:PACK, :] = pick(top, swap(bottom))
            pk_ref[h + 1, ROWS:PACK, :] = pick(swap(top), bottom)


def front(x, w, gain):
    return pl.pallas_call(
        front_kernel,
        out_shape=[jax.ShapeDtypeStruct((HEADS, PACK, 128), F32)] + [jax.ShapeDtypeStruct((ROWS, D), F32)],
        in_specs=[VM] * 3,
        out_specs=[VM] * 2,
        scratch_shapes=[pltpu.VMEM((2 * ROWS, D), BF16)],
        compiler_params=params(),
    )(x, w, gain)


def place_facts():
    p, s = lax.axis_index("pat"), lax.axis_index("seq")
    x, core = p // 2, lax.rem(p, 2)
    active, head = head_here(p, s)
    return p, s, x, core, active, head


def home_device(core, m):
    return core * 2 + lax.rem(m, 2), m // 2


def head_device(h, b):
    hx, hs = head_place(h)
    return hx * 2 + b, hs


def same(p, s, q, t):
    return jnp.logical_and(p == q, s == t)


def to(p, s):
    return {"pat": p, "seq": s}


def scatter_kernel(forward, pk, own, *rest):
    if forward:
        sib, send, recv, fsend, frecv = rest
    else:
        send, recv = rest
    p, s, x, core, active, head = place_facts()
    slot = s * 2 + core
    barrier = pltpu.get_barrier_semaphore()

    @pl.when(active)
    def _():
        def greet(m, carry):
            q, t = home_device(core, m)

            @pl.when(jnp.logical_not(same(p, s, q, t)))
            def _():
                pl.semaphore_signal(barrier, inc=1, device_id=to(q, t), device_id_type=MESH)

            return carry

        lax.fori_loop(0, HOMES, greet, 0)
        if forward:
            pl.semaphore_signal(barrier, inc=1, device_id=to(x * 2 + 1 - core, s), device_id_type=MESH)

    mine = jnp.logical_and(active, core == x)
    waits = HEADS - mine.astype(jnp.int32)
    if forward:
        waits = waits + active.astype(jnp.int32)
    pl.semaphore_wait(barrier, waits)

    def copy(h):
        q, t = head_device(h, x)
        return q, t, pltpu.make_async_remote_copy(
            src_ref=pk.at[h],
            dst_ref=own.at[slot],
            send_sem=send.at[h],
            recv_sem=recv.at[slot],
            device_id=to(q, t),
            device_id_type=MESH,
        )

    def start(j, carry):
        h = lax.rem(j + 3 * (s // 2) + 2 * p, HEADS)
        q, t, remote = copy(h)

        @pl.when(same(p, s, q, t))
        def _():
            pltpu.make_async_copy(pk.at[h], own.at[slot], recv.at[slot]).start()

        @pl.when(jnp.logical_not(same(p, s, q, t)))
        def _():
            remote.start()

        return carry

    lax.fori_loop(0, HEADS, start, 0)

    def passed(m):
        return pltpu.make_async_remote_copy(
            src_ref=own.at[m, pl.ds(0, ROWS), :],
            dst_ref=sib.at[m],
            send_sem=fsend.at[m],
            recv_sem=frecv.at[m],
            device_id=to(x * 2 + 1 - core, s),
            device_id_type=MESH,
        )

    @pl.when(active)
    def _():
        def arrive(m, carry):
            pltpu.make_async_copy(own.at[m], own.at[m], recv.at[m]).wait()
            if forward:
                passed(m).start()
            return carry

        lax.fori_loop(0, HOMES, arrive, 0)
        if forward:

            def finish(m, carry):
                passed(m).wait()
                return carry

            lax.fori_loop(0, HOMES, finish, 0)

    def sent(h, carry):
        q, t, remote = copy(h)

        @pl.when(jnp.logical_not(same(p, s, q, t)))
        def _():
            remote.wait_send()

        return carry

    lax.fori_loop(0, HEADS, sent, 0)


def to_heads(packets, forward, cid):
    rows = packets.shape[1]
    shapes = [jax.ShapeDtypeStruct((HOMES, rows, 128), F32)]
    sems = [pltpu.SemaphoreType.DMA((HEADS,)), pltpu.SemaphoreType.DMA((HOMES,))]
    if forward:
        shapes.append(jax.ShapeDtypeStruct((HOMES, ROWS, 128), F32))
        sems += [pltpu.SemaphoreType.DMA((HOMES,)), pltpu.SemaphoreType.DMA((HOMES,))]
    return pl.pallas_call(
        functools.partial(scatter_kernel, forward),
        out_shape=shapes,
        in_specs=[ANY],
        out_specs=[ANY] * len(shapes),
        scratch_shapes=sems,
        compiler_params=params(collective_id=cid, has_side_effects=True),
    )(packets)


def home_barrier(p, s, x, core, active, barrier, also_sibling):
    def greet(h, carry):
        q, t = head_device(h, x)

        @pl.when(jnp.logical_not(same(p, s, q, t)))
        def _():
            pl.semaphore_signal(barrier, inc=1, device_id=to(q, t), device_id_type=MESH)

        return carry

    lax.fori_loop(0, HEADS, greet, 0)

    @pl.when(active)
    def _():
        if also_sibling:
            pl.semaphore_signal(barrier, inc=1, device_id=to(x * 2 + 1 - core, s), device_id_type=MESH)
        mine = (core == x).astype(jnp.int32)
        pl.semaphore_wait(barrier, HOMES - mine + (1 if also_sibling else 0))


def gather_kernel(pk, rec, send, recv):
    p, s, x, core, active, head = place_facts()
    barrier = pltpu.get_barrier_semaphore()
    home_barrier(p, s, x, core, active, barrier, False)

    def copy(m):
        q, t = home_device(core, m)
        return q, t, pltpu.make_async_remote_copy(
            src_ref=pk.at[m],
            dst_ref=rec.at[head],
            send_sem=send.at[m],
            recv_sem=recv.at[head],
            device_id=to(q, t),
            device_id_type=MESH,
        )

    @pl.when(active)
    def _():
        def start(j, carry):
            m = lax.rem(j + 2 * s + 1, HOMES)
            q, t, remote = copy(m)

            @pl.when(same(p, s, q, t))
            def _():
                pltpu.make_async_copy(pk.at[m], rec.at[head], recv.at[head]).start()

            @pl.when(jnp.logical_not(same(p, s, q, t)))
            def _():
                remote.start()

            return carry

        lax.fori_loop(0, HOMES, start, 0)

    def arrive(h, carry):
        pltpu.make_async_copy(rec.at[h], rec.at[h], recv.at[h]).wait()
        return carry

    lax.fori_loop(0, HEADS, arrive, 0)

    @pl.when(active)
    def _():
        def sent(m, carry):
            q, t, remote = copy(m)

            @pl.when(jnp.logical_not(same(p, s, q, t)))
            def _():
                remote.wait_send()

            return carry

        lax.fori_loop(0, HOMES, sent, 0)


def to_homes(packets, cid):
    rows = packets.shape[1]
    return pl.pallas_call(
        gather_kernel,
        out_shape=jax.ShapeDtypeStruct((HEADS, rows, 128), F32),
        in_specs=[ANY],
        out_specs=ANY,
        scratch_shapes=[pltpu.SemaphoreType.DMA((HOMES,)), pltpu.SemaphoreType.DMA((HEADS,))],
        compiler_params=params(collective_id=cid, has_side_effects=True),
    )(packets)


def tile_positions(rows, columns, row_classes, column_classes, t_step, class_step):
    r = lax.broadcasted_iota(jnp.int32, (rows, columns), 0)
    q = lax.broadcasted_iota(jnp.int32, (rows, columns), 1)
    rn, qn = rows // row_classes, columns // column_classes
    return (r % rn) * t_step + (r // rn) * class_step, (q % qn) * t_step + (q // qn) * class_step


def key_bias(q_shape, k_shape, t_step, class_step, shift, keys_first):
    nq, nk = q_shape[0] * q_shape[1], k_shape[0] * k_shape[1]
    if keys_first:
        kp, qp = tile_positions(nk, nq, k_shape[0], q_shape[0], t_step, class_step)
    else:
        qp, kp = tile_positions(nq, nk, q_shape[0], k_shape[0], t_step, class_step)
    return jnp.where(kp - qp <= shift, 0.0, NEG).astype(F32)


def unpack_keys(own, sib, b, kvf):
    def one(m, carry):
        c = 2 * b + lax.rem(m, 2)
        d = 2 * (1 - b) + lax.rem(m, 2)
        t = pl.multiple_of((m // 2) * ROWS, 64)
        kvf[c, pl.ds(t, ROWS), :] = own[m, 0:ROWS, :]
        kvf[d, pl.ds(t, ROWS), :] = sib[m]
        return carry

    lax.fori_loop(0, HOMES, one, 0)


def unpack_pairs(src, first, dst, scale):
    def one(m, carry):
        t = pl.multiple_of((m // 2) * ROWS, 32)
        v = src[m, first : first + HALF, :] * scale
        w = swap(v)
        dst[lax.rem(m, 2), pl.ds(t, HALF), :] = pick(v, w)
        dst[lax.rem(m, 2), pl.ds(t + HALF, HALF), :] = pick(w, v)
        return carry

    lax.fori_loop(0, HOMES, one, 0)


def keys_and_values(kv):
    hi, lo = split32(kv)
    k2 = pick(hi, swap(lo))
    v2 = pick(swap(hi), lo)
    return k2, v2


def doubled(v):
    return jnp.concatenate([v, v], 1)


def query_quads(qq):
    hi, lo = split32(qq)
    return jnp.concatenate([pick(hi, lo).astype(BF16), pick(lo, hi).astype(BF16)], 1)


def class_facts4(o4, b):
    keys = ((lax.rem(o4, 4), o4 // 4), (lax.rem(o4 + 6, 4), (o4 + 6) // 4))
    first = (keys[0][0] // 2) == b
    query = (jnp.where(first, keys[0][0], keys[1][0]), jnp.where(first, keys[0][1], keys[1][1]))
    return keys, jnp.where(first, 0, 1), query


def forward_kernel(offsets, own, sib, ap, lse, sums, kvf, kc, vc, qf, qc, k4, v4, q4, k5, v5, q5, acc, mx, R, b1, b2, b3, b4):
    p, s, x, b, active, head = place_facts()
    offs = [offsets[i, head] for i in range(PATTERNS)]
    sums[...] = jnp.zeros_like(sums)

    @pl.when(active)
    def _():
        ones = jnp.ones((128, 128), BF16)
        unpack_keys(own, sib, b, kvf)
        unpack_pairs(own, ROWS, qf, 1.0 / math.sqrt(HD))

        def with_ones(v2):
            return jnp.concatenate([v2.astype(BF16), ones], 1)

        def prepare(i, carry):
            c, t = i // 12, pl.multiple_of(lax.rem(i, 12) * 128, 128)
            k2, v2 = keys_and_values(kvf[c, pl.ds(t, 128), :])
            kc[c, pl.ds(t, 128), :] = k2.astype(BF16)
            vc[c, pl.ds(t, 128), :] = with_ones(v2)
            return carry

        lax.fori_loop(0, 48, prepare, 0, unroll=2)

        def prepare_q(i, carry):
            c, t = i // 12, pl.multiple_of(lax.rem(i, 12) * 128, 128)
            qc[c, pl.ds(t, 128), :] = query_quads(qf[c, pl.ds(t, 128), :])
            return carry

        lax.fori_loop(0, 24, prepare_q, 0, unroll=2)

        keys4, e4, (qc4, qv4) = class_facts4(offs[3], b)
        kc5, kv5 = lax.rem(offs[4], 4), offs[4] // 4
        for blk in range(4):
            r = slice(128 * blk, 128 * blk + 128)
            for e in range(2):
                c, v = keys4[e]
                k2, v2 = keys_and_values(kvf[c, pl.ds(v + 384 * blk, 128, stride=3), :])
                k4[e, r, :] = k2.astype(BF16)
                v4[e, r, :] = with_ones(v2)
            q4[r, :] = query_quads(qf[qc4 - 2 * b, pl.ds(qv4 + 384 * blk, 128, stride=3), :])
            k2, v2 = keys_and_values(kvf[kc5, pl.ds(kv5 + 384 * blk, 128, stride=3), :])
            k5[r, :] = k2.astype(BF16)
            v5[r, :] = with_ones(v2)
            q5[r, :] = query_quads(qf[lax.rem(kc5, 2), pl.ds(kv5 + 384 * blk, 128, stride=3), :])

        b1[...] = key_bias((2, 128), (4, 128), 4, 1, 2 * b, False)
        b2[...] = key_bias((1, 256), (2, 256), 4, 2, 2 * b, False)
        b3[...] = key_bias((1, 512), (1, 512), 1, 1, 0, False)
        b4[...] = key_bias((1, 256), (2, 256), 12, 6, 6 * e4, False)

        def tile(start, q, k, v, bias, classes, first):
            n = q.shape[0]
            each = n // classes
            per = 1536 // classes if classes == 1 else 512
            s = dot_nt(q, doubled(k))
            wide = s.shape[1]
            own_rows = bias.shape[0] // classes
            s = s.reshape(classes, each, wide)
            edge = s[:, :own_rows] + bias[...].reshape(classes, own_rows, wide)
            s = edge if each == own_rows else jnp.concatenate([edge, s[:, own_rows:]], 1)
            s = s.reshape(n, wide)
            top = jnp.max(s, -1, keepdims=True)

            def where(c):
                return pl.ds(c * per + start, each)

            def load(ref):
                return jnp.concatenate([ref[where(c), :] for c in range(classes)], 0)

            def store(ref, value):
                for c in range(classes):
                    ref[where(c), :] = value[c * each : c * each + each]

            if first:
                m = jnp.broadcast_to(top, (n, 128))
            else:
                old = load(mx)
                m = jnp.maximum(old, top)
            hi, lo = split(jnp.exp(s - jnp.concatenate([m] * (wide // 128), 1)))
            new = dot_nn(jnp.concatenate([hi, lo], 0), v)
            new = new[:n] + new[n:]
            if not first:
                new = load(acc) * doubled(jnp.exp(old - m)) + new
            store(acc, new)
            store(mx, m)

        def closed(pattern, rows):
            value, m = acc[rows, :], mx[rows, :]
            o, l = value[:, :128], value[:, 128:]
            sums[pattern : pattern + 1, :] += jnp.sum(m + jnp.log(l), 0, keepdims=True)
            lane = lax.broadcasted_iota(jnp.int32, m.shape, 1)
            return jnp.where(lane < HD, o + swap(o), jnp.where(lane < 96, l, m))

        def merge(pattern, ci, rows, of):
            r0, r1 = R[ci, rows, :], closed(pattern, of)
            m0 = jnp.broadcast_to(r0[:, 96:97], r0.shape)
            m1 = jnp.broadcast_to(r1[:, 96:97], r1.shape)
            m = jnp.maximum(m0, m1)
            both = r0 * jnp.exp(m0 - m) + r1 * jnp.exp(m1 - m)
            lane = lax.broadcasted_iota(jnp.int32, r0.shape, 1)
            R[ci, rows, :] = jnp.where(lane < 96, both, m)

        def q1(g, carry):
            base = 512 * g

            def at(t, n):
                return pl.ds(pl.multiple_of(base + t, 128), n)

            for kb in range(4):
                start = 128 * kb
                each = 512 - start
                ks = at(start, 128)
                tile(
                    start,
                    qc[:, at(start, each), :].reshape(2 * each, 256),
                    kc[:, ks, :].reshape(512, 128),
                    vc[:, ks, :].reshape(512, 256),
                    b1,
                    2,
                    kb == 0,
                )
            for c in range(2):
                for i in range(2):
                    R[c, at(256 * i, 256), :] = closed(0, pl.ds(512 * c + 256 * i, 256))
            return carry

        lax.fori_loop(0, 3, q1, 0)

        par = offs[1]
        for base, length in ((0, 1024), (1024, 512)):
            for start in range(0, length, 256):
                ks = slice(base + start, base + start + 256)
                tile(
                    start,
                    qc[par, base + start : base + length, :],
                    jnp.concatenate([kc[par, ks, :], kc[par + 2, ks, :]], 0),
                    jnp.concatenate([vc[par, ks, :], vc[par + 2, ks, :]], 0),
                    b2,
                    1,
                    start == 0,
                )

            def join2(i, carry, base=base):
                t = pl.multiple_of(i * 256, 256)
                merge(1, par, pl.ds(base + t, 256), pl.ds(t, 256))
                return carry

            lax.fori_loop(0, length // 256, join2, 0)

        o3 = offs[2]

        @pl.when(o3 // 2 == b)
        def _():
            ci = lax.rem(o3, 2)
            for start in range(0, TOTAL, 512):
                ks = slice(start, start + 512)
                tile(start, qc[ci, start:TOTAL, :], kc[o3, ks, :], vc[o3, ks, :], b3, 1, start == 0)

            def join3(i, carry):
                t = pl.multiple_of(i * 256, 256)
                merge(2, ci, pl.ds(t, 256), pl.ds(t, 256))
                return carry

            lax.fori_loop(0, TOTAL // 256, join3, 0)

        for start in range(0, THIRD, 256):
            ks = slice(start, start + 256)
            tile(
                start, q4[start:THIRD, :], k4[:, ks, :].reshape(512, 128), v4[:, ks, :].reshape(512, 256), b4, 1, start == 0
            )
        for i in range(2):
            merge(3, qc4 - 2 * b, pl.ds(qv4 + 768 * i, 256, stride=3), pl.ds(256 * i, 256))

        @pl.when(kc5 // 2 == b)
        def _():
            tile(0, q5[...], k5[...], v5[...], b3, 1, True)
            for i in range(2):
                merge(4, lax.rem(kc5, 2), pl.ds(kv5 + 768 * i, 256, stride=3), pl.ds(256 * i, 256))

        def finish(m, carry):
            ci = lax.rem(m, 2)
            rows = pl.ds(pl.multiple_of((m // 2) * ROWS, 64), ROWS)
            r = R[ci, rows, :]
            l = jnp.broadcast_to(r[:, HD : HD + 1], r.shape)
            out = r / l
            ap[m] = pick(out[:HALF], swap(out[HALF:]))
            lse[ci, rows, :] = jnp.broadcast_to(r[:, 96:97], r.shape) + jnp.log(l)
            return carry

        lax.fori_loop(0, HOMES, finish, 0, unroll=2)


def attention_forward(offsets, own, sib):
    state = pltpu.VMEM((2, TOTAL, 128), F32)
    return pl.pallas_call(
        forward_kernel,
        out_shape=[
            jax.ShapeDtypeStruct((HOMES, HALF, 128), F32),
            jax.ShapeDtypeStruct((2, TOTAL, 128), F32),
            jax.ShapeDtypeStruct((8, 128), F32),
        ],
        in_specs=[SM, VM, VM],
        out_specs=[VM, VM, VM],
        scratch_shapes=[
            pltpu.VMEM((4, TOTAL, 128), F32),
            pltpu.VMEM((4, TOTAL, 128), BF16),
            pltpu.VMEM((4, TOTAL, 256), BF16),
            state,
            pltpu.VMEM((2, TOTAL, 256), BF16),
            pltpu.VMEM((2, THIRD, 128), BF16),
            pltpu.VMEM((2, THIRD, 256), BF16),
            pltpu.VMEM((THIRD, 256), BF16),
            pltpu.VMEM((THIRD, 128), BF16),
            pltpu.VMEM((THIRD, 256), BF16),
            pltpu.VMEM((THIRD, 256), BF16),
            pltpu.VMEM((TOTAL, 256), F32),
            pltpu.VMEM((TOTAL, 128), F32),
            state,
            pltpu.VMEM((256, 512), F32),
            pltpu.VMEM((256, 512), F32),
            pltpu.VMEM((512, 512), F32),
            pltpu.VMEM((256, 512), F32),
        ],
        compiler_params=params(),
    )(offsets, own, sib)


class Place:
    def __init__(self):
        p, s = lax.axis_index("pat"), lax.axis_index("seq")
        self.p, self.s = p, s
        self.x, self.core, self.z, self.y = p // 2, lax.rem(p, 2), s // 2, lax.rem(s, 2)
        self.peer = to(self.x * 2 + 1 - self.core, s)
        self.xn = to((1 - self.x) * 2 + self.core, s)
        self.yn = to(p, self.z * 2 + 1 - self.y)
        self.left, self.right = to(p, s - 2), to(p, s + 2)

    def greet(self, barrier, line=True):
        for d in (self.peer, self.xn, self.yn):
            pl.semaphore_signal(barrier, inc=1, device_id=d, device_id_type=MESH)
        if not line:
            return 3

        @pl.when(self.z > 0)
        def _():
            pl.semaphore_signal(barrier, inc=1, device_id=self.left, device_id_type=MESH)

        @pl.when(self.z < 3)
        def _():
            pl.semaphore_signal(barrier, inc=1, device_id=self.right, device_id_type=MESH)

        return 3 + (self.z > 0).astype(jnp.int32) + (self.z < 3).astype(jnp.int32)


def remote(src, dst, a, b, d):
    return pltpu.make_async_remote_copy(
        src_ref=src, dst_ref=dst, send_sem=a, recv_sem=b, device_id=d, device_id_type=MESH
    )


def add_in(dst, src):
    lead = dst.shape[:-2]

    def one(i, carry):
        index = []
        for d in reversed(lead):
            index.insert(0, lax.rem(i, d))
            i = i // d
        dst[tuple(index)] += src[tuple(index)]
        return carry

    lax.fori_loop(0, math.prod(lead), one, 0)


class Sems:
    NAMES = ("sc", "rc", "s1", "r1", "s2", "r2", "sl", "rl", "sr", "rr")

    def __init__(self, refs):
        for name, ref in zip(self.NAMES, refs):
            setattr(self, name, ref)

    @staticmethod
    def scratch(n):
        dma = pltpu.SemaphoreType.DMA
        return [dma((n, 2)), dma((n, 2))] + [dma((n,)) for _ in range(8)]


class Chunk:
    def __init__(self, place, k, x_first, sems, b0=None, b1=None, b2=None, bl=None, br=None, part=None, put=None):
        self.at, self.k, self.x_first, self.sems = place, k, x_first, sems
        self.b0, self.b1, self.b2, self.bl, self.br = b0, b1, b2, bl, br
        self.part, self.put = part, put

    def core(self, i):
        k, m = self.k, self.sems
        return remote(self.part(i, 1 - self.at.core), self.b0.at[i], m.sc.at[k, i], m.rc.at[k, i], self.at.peer)

    def one(self):
        k, at, m = self.k, self.at, self.sems
        if self.x_first:
            return remote(self.b0.at[1 - at.x], self.b1, m.s1.at[k], m.r1.at[k], at.xn)
        return remote(self.b0.at[:, :, 1 - at.y], self.b1, m.s1.at[k], m.r1.at[k], at.yn)

    def two(self):
        k, at, m = self.k, self.at, self.sems
        if self.x_first:
            return remote(self.b1.at[:, 1 - at.y], self.b2, m.s2.at[k], m.r2.at[k], at.yn)
        return remote(self.b1.at[1 - at.x], self.b2, m.s2.at[k], m.r2.at[k], at.xn)

    def rightward(self, i):
        k, part, m = self.k, pl.ds(i + 1, 3 - i), self.sems
        src = self.b2 if i == 0 else self.bl
        return remote(src.at[part], self.bl.at[part], m.sr.at[k], m.rl.at[k], self.at.right)

    def leftward(self, i):
        k, part, m = self.k, pl.ds(0, i), self.sems
        src = self.b2 if i == 3 else self.br
        return remote(src.at[part], self.br.at[part], m.sl.at[k], m.rr.at[k], self.at.left)

    def own_core(self, i):
        self.core(i).wait_recv()
        add_in(self.b0.at[i], self.part(i, self.at.core))

    def stage1(self):
        for i in range(2):
            self.own_core(i)
        self.one().start()

    def arrived(self):
        self.one().wait_recv()
        add_in(self.b1, self.b0.at[self.at.x] if self.x_first else self.b0.at[:, :, self.at.y])

    def stage2(self):
        self.arrived()
        self.two().start()

    def stage3(self):
        self.two().wait_recv()
        add_in(self.b2, self.b1.at[:, self.at.y] if self.x_first else self.b1.at[self.at.x])

        @pl.when(self.at.z == 0)
        def _():
            self.rightward(0).start()

        @pl.when(self.at.z == 3)
        def _():
            self.leftward(3).start()

    def stage4(self):
        @pl.when(self.at.z == 1)
        def _():
            self.rightward(0).wait_recv()
            self.bl[2:4] += self.b2[2:4]
            self.rightward(1).start()

        @pl.when(self.at.z == 2)
        def _():
            self.leftward(3).wait_recv()
            self.br[0:2] += self.b2[0:2]
            self.leftward(2).start()

    def stage5(self):
        @pl.when(self.at.z == 2)
        def _():
            self.rightward(1).wait_recv()
            self.bl[3:4] += self.b2[3:4]
            self.rightward(2).start()

        @pl.when(self.at.z == 1)
        def _():
            self.leftward(2).wait_recv()
            self.br[0:1] += self.b2[0:1]
            self.leftward(1).start()

    def stage6(self):
        @pl.when(self.at.z == 3)
        def _():
            self.rightward(2).wait_recv()
            self.put(self.b2[3] + self.bl[3])

        @pl.when(self.at.z == 0)
        def _():
            self.leftward(1).wait_recv()
            self.put(self.b2[0] + self.br[0])

        @pl.when(self.at.z == 1)
        def _():
            self.put(self.b2[1] + self.bl[1] + self.br[1])

        @pl.when(self.at.z == 2)
        def _():
            self.put(self.b2[2] + self.bl[2] + self.br[2])

    def line_sent(self):
        for i in range(4):

            @pl.when(self.at.z == i)
            def _(i=i):
                if i < 3:
                    self.rightward(i).wait_send()
                if i > 0:
                    self.leftward(i).wait_send()


class Reducer:
    def __init__(self, place, n, part, scratch, put):
        self.place, self.n, self.part, self.put = place, n, part, put
        self.c0, self.c1a, self.c1b, self.c2, self.zl, self.zr = scratch[:6]
        self.sems = Sems(scratch[6:16])
        self.pairs = (n + 1) // 2

    @staticmethod
    def scratch(n, rows):
        bufs = [(n, 2, 4, 2), ((n + 1) // 2, 4, 2), (max(n // 2, 1), 2, 4), (n, 4), (n, 4), (n, 4)]
        return [pltpu.VMEM(b + (rows, D), F32) for b in bufs] + Sems.scratch(n)

    def chunk(self, k, parity):
        return Chunk(
            self.place,
            k,
            parity == 0,
            self.sems,
            self.c0.at[k],
            (self.c1b if parity else self.c1a).at[k // 2],
            self.c2.at[k],
            self.zl.at[k],
            self.zr.at[k],
            self.part(k),
            lambda v: self.put(k, v),
        )

    def send(self, first, after):
        def one(k, carry):
            for i in range(2):
                self.chunk(k, 0).core(i).start()
            return carry

        lax.fori_loop(first, after, one, 0)

    def one(self, stage, pair):
        for parity in range(2):
            k = 2 * pair + parity
            k = jnp.int32(k) if isinstance(k, int) else k

            @pl.when(jnp.logical_and(k >= 0, k < self.n))
            def _(k=k, parity=parity):
                getattr(self.chunk(k, parity), f"stage{stage}")()

    def early(self, pair):
        self.one(1, pair)

    def step(self, tau):
        self.one(1, tau)
        for stage in range(2, 7):
            self.one(stage, tau - stage)

    def finish(self):
        def one(k, carry):
            for parity in range(2):

                @pl.when(lax.rem(k, 2) == parity)
                def _(parity=parity):
                    c = self.chunk(k, parity)
                    for i in range(2):
                        c.core(i).wait_send()
                    c.one().wait_send()
                    c.two().wait_send()
                    c.line_sent()

            return carry

        lax.fori_loop(0, self.n, one, 0)


class SmallSum:
    def __init__(self, place, S, bufs, send, recv, put):
        self.at, self.S, self.send, self.recv, self.put = place, S, send, recv, put
        self.d0, self.d1, self.d2, self.dl, self.dr, self.t1, self.t2, self.t3, self.fl, self.fr = bufs

    @staticmethod
    def scratch():
        return [pltpu.VMEM((8, D), F32)] * 10 + [pltpu.SemaphoreType.DMA((5,)), pltpu.SemaphoreType.DMA((5,))]

    def hop(self, src, dst, i, d):
        return remote(src, dst, self.send.at[i], self.recv.at[i], d)

    def core(self):
        return self.hop(self.S, self.d0, 0, self.at.peer)

    def along_x(self):
        return self.hop(self.t1, self.d1, 1, self.at.xn)

    def along_y(self):
        return self.hop(self.t2, self.d2, 2, self.at.yn)

    def rightward(self, i):
        return self.hop(self.t3 if i == 0 else self.fl, self.dl, 3, self.at.right)

    def leftward(self, i):
        return self.hop(self.t3 if i == 3 else self.fr, self.dr, 4, self.at.left)

    def stage1(self):
        self.core().wait_recv()
        self.t1[...] = self.S[...] + self.d0[...]
        self.along_x().start()

    def stage2(self):
        self.along_x().wait_recv()
        self.t2[...] = self.t1[...] + self.d1[...]
        self.along_y().start()

    def stage3(self):
        self.along_y().wait_recv()
        self.t3[...] = self.t2[...] + self.d2[...]

        @pl.when(self.at.z == 0)
        def _():
            self.rightward(0).start()

        @pl.when(self.at.z == 3)
        def _():
            self.leftward(3).start()

    def from_left(self, i):
        self.rightward(i).wait_recv()
        self.fl[...] = self.dl[...] + self.t3[...]

    def from_right(self, i):
        self.leftward(i).wait_recv()
        self.fr[...] = self.dr[...] + self.t3[...]

    def stage4(self):
        @pl.when(self.at.z == 1)
        def _():
            self.from_left(0)
            self.rightward(1).start()

        @pl.when(self.at.z == 2)
        def _():
            self.from_right(3)
            self.leftward(2).start()

    def stage5(self):
        @pl.when(self.at.z == 2)
        def _():
            self.from_left(1)
            self.rightward(2).start()

        @pl.when(self.at.z == 1)
        def _():
            self.from_right(2)
            self.leftward(1).start()

    def stage6(self):
        @pl.when(self.at.z == 3)
        def _():
            self.from_left(2)
            self.put(self.fl[...])

        @pl.when(self.at.z == 0)
        def _():
            self.from_right(1)
            self.put(self.fr[...])

        @pl.when(jnp.logical_or(self.at.z == 1, self.at.z == 2))
        def _():
            self.put(self.fl[...] + self.dr[...])

    def finish(self):
        for c in (self.core(), self.along_x(), self.along_y()):
            c.wait_send()
        for i in range(4):

            @pl.when(self.at.z == i)
            def _(i=i):
                if i < 3:
                    self.rightward(i).wait_send()
                if i > 0:
                    self.leftward(i).wait_send()


def small_outputs(place, counts, outs, tot):
    ga, gi, gf, gh, means = outs

    def put(v):
        tot[...] = v
        d = place.p * RUNS + place.s
        for i, ref in enumerate((ga, gi, gf)):
            ref[...] = pltpu.roll(tot[i : i + 1, :], D - PIECE * d, 1)[:, :PIECE]
        row = tot[pl.ds(3 + d // 8, 1), :]
        gh[...] = pltpu.roll(row, D - 4 * PIECE * lax.rem(d, 8), 1)[:, : 4 * PIECE]
        lane = lax.broadcasted_iota(jnp.int32, (1, 128), 1)
        scale = jnp.full((1, 128), counts[0], F32)
        for i in range(1, PATTERNS):
            scale = jnp.where(lane == i, counts[i], scale)
        means[...] = (tot[7:8, :128] / scale)[:, :PATTERNS]

    return put


N_PIECES = 9
SUB = 8


def finish_kernel(counts, rec, x_ref, dy1_ref, w_hbm, ga1, S_in, gx, g_qkv, ga, gi, gf, gh, means, dqkv, lhs, th, tl, r_hi, r_lo, tiles, S, tot, gx2, w, wsem, *scratch):
    fetch = pltpu.make_async_copy(w_hbm, w, wsem)
    fetch.start()
    place = Place()
    barrier = pltpu.get_barrier_semaphore()
    expected = place.greet(barrier)
    for j in range(HEADS // 2):
        u, v = rec[2 * j, ROWS:PACK, :], rec[2 * j + 1, ROWS:PACK, :]
        cols = slice(128 * j, 128 * j + 128)
        dqkv[0:HALF, cols] = pick(u, swap(v))
        dqkv[HALF:ROWS, cols] = pick(swap(u), v)
        u, v = rec[2 * j, 0:ROWS, :], rec[2 * j + 1, 0:ROWS, :]
        dqkv[:, D + 128 * j : D + 128 * j + 128] = pick(u, swap(v))
        dqkv[:, 2 * D + 128 * j : 2 * D + 128 * j + 128] = pick(swap(u), v)
    gain = ga1[...][None, :]
    n, rs = normed(x_ref[...])
    put_turned(th, tl, n * gain)

    def part(k):
        rows = pl.ds(pl.multiple_of(lax.rem(k, 3) * SUB, SUB), SUB)
        return lambda i, c: tiles.at[k // 3, i, c, :, :, rows, :]

    def put(k, v):
        g_qkv[
            pl.ds(pl.multiple_of(lax.rem(k, 3) * SUB, SUB), SUB), pl.ds(pl.multiple_of((k // 3) * D, D), D)
        ] = v

    n_r = 16
    big = Reducer(place, N_PIECES, part, scratch[:n_r], put)
    rest = scratch[n_r:]
    small = SmallSum(
        place, S, rest[:10], rest[10], rest[11], small_outputs(place, counts, (ga, gi, gf, gh, means), tot)
    )

    def tile_of(j, carry):
        r_hi[...], r_lo[...] = split(dqkv[:, pl.ds(pl.multiple_of(D * j, D), D)])

        def one(i, inner):
            rows = pl.ds(pl.multiple_of(i * 2 * ROWS, 128), 2 * ROWS)
            h, l = th[rows, :], tl[rows, :]
            v = dot_nn(h, r_hi[...]) + dot_nn(h, r_lo[...]) + dot_nn(l, r_hi[...])
            tiles[j, i] = v.reshape(2, 4, 2, PIECE, D)
            return inner

        lax.fori_loop(0, 2, one, 0)

        @pl.when(j == 0)
        def _():
            pl.semaphore_wait(barrier, expected)

        big.send(3 * j, 3 * j + 3)

        @pl.when(j > 0)
        def _():
            big.early(j - 1)

        return carry

    lax.fori_loop(0, 3, tile_of, 0)
    gx2[...] = jnp.zeros_like(gx2)
    fetch.wait()

    def back(j, carry):
        cols = pl.ds(pl.multiple_of(D * j, D), D)
        put_split(lhs, dqkv[:, cols])
        gx2[...] += halves_sum(dot_nt(lhs[...], w[:, cols]))
        return carry

    lax.fori_loop(0, 3, back, 0)
    e = gx2[...]
    S[...] = S_in[...]
    S[0:1, :] = jnp.sum(e * n, 0, keepdims=True)
    small.core().start()
    gx[...] = (dy1_ref[...] + norm_back(e * gain, n, rs)).reshape(ROWS, 1, D)
    small.stage1()

    def step(tau, carry):
        for stage in range(2, 7):

            @pl.when(tau == stage + 1)
            def _(stage=stage):
                getattr(small, f"stage{stage}")()

        big.step(tau)
        return carry

    lax.fori_loop(2, big.pairs + 6, step, 0)

    big.finish()
    small.finish()


def finish(rec, x, dy1, w, ga, S, counts, cid):
    return pl.pallas_call(
        functools.partial(finish_kernel, counts),
        out_shape=[jax.ShapeDtypeStruct((ROWS, 1, D), F32), jax.ShapeDtypeStruct((PIECE, 3 * D), F32)]
        + [jax.ShapeDtypeStruct((1, n), F32) for n in (PIECE, PIECE, PIECE, 4 * PIECE, PATTERNS)],
        in_specs=[VM, VM, VM, ANY, VM, VM],
        out_specs=[VM] * 7,
        scratch_shapes=[
            pltpu.VMEM((ROWS, 3 * D), F32),
            pltpu.VMEM((2 * ROWS, D), BF16),
            pltpu.VMEM((D, ROWS), BF16),
            pltpu.VMEM((D, ROWS), BF16),
            pltpu.VMEM((ROWS, D), BF16),
            pltpu.VMEM((ROWS, D), BF16),
            pltpu.VMEM((3, 2, 2, 4, 2, PIECE, D), F32),
            pltpu.VMEM((8, D), F32),
            pltpu.VMEM((8, D), F32),
            pltpu.VMEM((ROWS, D), F32),
            pltpu.VMEM((D, 3 * D), BF16),
            pltpu.SemaphoreType.DMA,
        ]
        + Reducer.scratch(N_PIECES, SUB)
        + SmallSum.scratch(),
        compiler_params=params(collective_id=cid, has_side_effects=True),
    )(rec, x, dy1, w, ga, S)


def deliver_kernel(*refs):
    n = len(refs) // 2
    for src, dst in zip(refs[:n], refs[n:]):
        dst[...] = src[...]


def deliver(*arrays):
    return pl.pallas_call(
        deliver_kernel,
        out_shape=[jax.ShapeDtypeStruct(v.shape, v.dtype) for v in arrays],
        in_specs=[VM] * len(arrays),
        out_specs=[VM] * len(arrays),
        compiler_params=params(),
    )(*arrays)


def rows_from_pairs(rec, dst):
    for j in range(HEADS // 2):
        u, v = rec[2 * j], rec[2 * j + 1]
        cols = slice(128 * j, 128 * j + 128)
        dst[0:HALF, cols] = pick(u, swap(v))
        dst[HALF:ROWS, cols] = pick(swap(u), v)


def pairs_from_rows(src, dst):
    for j in range(HEADS // 2):
        top = src[0:HALF, 128 * j : 128 * j + 128]
        bottom = src[HALF:ROWS, 128 * j : 128 * j + 128]
        dst[2 * j] = pick(top, swap(bottom))
        dst[2 * j + 1] = pick(swap(top), bottom)


def halves_sum(r):
    return r[:ROWS] + r[ROWS:]


def norm_back(f, n, rs):
    return (f - jnp.mean(f, -1, keepdims=True) - n * jnp.mean(f * n, -1, keepdims=True)) * rs


def put_turned(hi_ref, lo_ref, v):
    for j in range(D // 128):
        t = v[:, 128 * j : 128 * j + 128].T
        hi, lo = split(t)
        hi_ref[128 * j : 128 * j + 128, :] = hi
        lo_ref[128 * j : 128 * j + 128, :] = lo


class ToHeads:
    def __init__(self, pk, rec, send, recv):
        self.pk, self.rec, self.send, self.recv = pk, rec, send, recv
        self.facts = place_facts()

    def greet(self):
        p, s, x, core, active, head = self.facts
        barrier = pltpu.get_barrier_semaphore()

        @pl.when(active)
        def _():
            def one(m, carry):
                q, t = home_device(core, m)

                @pl.when(jnp.logical_not(same(p, s, q, t)))
                def _():
                    pl.semaphore_signal(barrier, inc=1, device_id=to(q, t), device_id_type=MESH)

                return carry

            lax.fori_loop(0, HOMES, one, 0)

    def copy(self, h):
        p, s, x, core, active, head = self.facts
        slot = s * 2 + core
        q, t = head_device(h, x)
        far = pltpu.make_async_remote_copy(
            src_ref=self.pk.at[h],
            dst_ref=self.rec.at[slot],
            send_sem=self.send.at[h],
            recv_sem=self.recv.at[slot],
            device_id=to(q, t),
            device_id_type=MESH,
        )
        return same(p, s, q, t), lambda: pltpu.make_async_copy(self.pk.at[h], self.rec.at[slot], self.recv.at[slot]), far

    def wait(self, others):
        p, s, x, core, active, head = self.facts
        mine = jnp.logical_and(active, core == x).astype(jnp.int32)
        pl.semaphore_wait(pltpu.get_barrier_semaphore(), HEADS + others - mine)

    def start(self):
        p, s, x, core, active, head = self.facts

        def one(j, carry):
            here, near, far = self.copy(lax.rem(j + 3 * (s // 2) + 2 * p, HEADS))

            @pl.when(here)
            def _():
                near().start()

            @pl.when(jnp.logical_not(here))
            def _():
                far.start()

            return carry

        lax.fori_loop(0, HEADS, one, 0)

    def finish(self):
        active = self.facts[4]

        @pl.when(active)
        def _():
            def arrive(m, carry):
                pltpu.make_async_copy(self.rec.at[m], self.rec.at[m], self.recv.at[m]).wait()
                return carry

            lax.fori_loop(0, HOMES, arrive, 0)

        def sent(h, carry):
            here, near, far = self.copy(h)

            @pl.when(jnp.logical_not(here))
            def _():
                far.wait_send()

            return carry

        lax.fori_loop(0, HEADS, sent, 0)


FT = 1024


def product(hi, lo, r_hi, r_lo, put):
    def one(i, carry):
        rows = pl.ds(pl.multiple_of(i * 2 * ROWS, 128), 2 * ROWS)
        h, l = hi[rows, :], lo[rows, :]
        put(i, dot_nn(h, r_hi[...]) + dot_nn(h, r_lo[...]) + dot_nn(l, r_hi[...]))
        return carry

    lax.fori_loop(0, 2, one, 0)


N_FF = 9
N_COLS = 5


def ff_kernel(rec, x_ref, g3, wo_hbm, wu_hbm, wd_hbm, gi1, gf1, gh1, sums, out3, drec, dy1_ref, S, C0, C1a, C1b, dap, lhs, lhs2, gi, gf, gh, gh_g, g_ref, out_ref, V, N1, U, GP, E, ACC, th, tl, r_hi, r_lo, cols_t, rows_t, c0, c1a, c1b, osem, wo, wu, wd, wsem, dsend, drecv, *rsems):
    place = Place()
    sems = Sems(rsems)
    fetch = [
        pltpu.make_async_copy(src, dst, wsem.at[i])
        for i, (src, dst) in enumerate(((wo_hbm, wo), (wu_hbm, wu), (wd_hbm, wd)))
    ]
    for c in fetch:
        c.start()
    travel = ToHeads(dap, drec, dsend, drecv)
    travel.greet()
    place.greet(pltpu.get_barrier_semaphore(), False)

    def chunk(k, part=None):
        if not isinstance(k, int):
            return Chunk(place, k, True, sems, c0.at[k], part=part)
        x_first = k % 2 == 0
        b1 = None if k < N_COLS else (c1a if x_first else c1b).at[(k - N_COLS) // 2]
        return Chunk(place, k, x_first, sems, c0.at[k], b1, part=part)

    for wide, flat in ((gi, gi1), (gf, gf1), (gh, gh1)):
        wide[...] = flat[...][None, :]
    g_ref[...] = g3[...].reshape(ROWS, D)
    rows_from_pairs(rec, V)
    na, rs_a = normed(V[...])
    V[...] = na
    put_split(lhs, na * gi[...])
    fetch[0].wait()

    def project(j, carry):
        cols = pl.ds(pl.multiple_of(256 * j, 256), 256)
        N1[:, cols] = x_ref[:, cols] + halves_sum(dot_nn(lhs[...], wo[:, cols]))
        return carry

    lax.fori_loop(0, 3, project, 0)
    y1 = N1[...]
    out_ref[...] = y1
    ny, rs_y = normed(y1)
    N1[...] = ny
    put_split(lhs, ny * gf[...])
    fetch[1].wait()

    def up(j, su):
        cols = pl.ds(pl.multiple_of(j * FT, FT), FT)
        z = halves_sum(dot_nn(lhs[...], wu[:, cols]))
        phi = 0.5 * (1.0 + lax.erf(z * math.sqrt(0.5)))
        u = z * phi
        U[:, cols] = u
        GP[:, cols] = phi + z * jnp.exp(-0.5 * z * z) * (1.0 / math.sqrt(2.0 * math.pi))
        return su + jnp.sum(u, -1, keepdims=True)

    zero = jnp.zeros((ROWS, 1), F32)
    mean = lax.fori_loop(0, FF // FT, up, zero) * (1.0 / FF)

    def spread(j, sv):
        cols = pl.ds(pl.multiple_of(j * FT, FT), FT)
        c = U[:, cols] - mean
        return sv + jnp.sum(c * c, -1, keepdims=True)

    rs_u = lax.rsqrt(lax.fori_loop(0, FF // FT, spread, zero) * (1.0 / FF) + LN_EPSILON)
    ACC[...] = jnp.zeros_like(ACC)
    fetch[2].wait()

    def lower(j, carry):
        cols = pl.ds(pl.multiple_of(j * FT, FT), FT)
        n = (U[:, cols] - mean) * rs_u
        U[:, cols] = n
        put_split(lhs2, n * gh[:, cols])
        ACC[...] += halves_sum(dot_nn(lhs2[...], wd[cols, :]))
        return carry

    lax.fori_loop(0, FF // FT, lower, 0)
    out3[...] = (out_ref[...] + ACC[...]).reshape(ROWS, 1, D)

    travel.wait(3)
    r_hi[...], r_lo[...] = split(g_ref[...])

    def down(j, q):
        return chunk(N_COLS + q, lambda i, c: rows_t.at[lax.rem(j, 2), :, :, q])

    def down_step(j, carry):
        @pl.when(j < 4)
        def _():
            cols = pl.ds(pl.multiple_of(D * j, D), D)
            put_turned(th, tl, U[:, cols] * gh[:, cols])
            sent = place.core != lax.rem(j, 2)

            @pl.when(jnp.logical_and(j >= 2, sent))
            def _():
                for q in range(4):
                    down(j - 2, q).core(j // 2 - 1).wait_send()

            def put(i, v):
                rows_t[lax.rem(j, 2), pl.ds(2 * i, 2)] = v.reshape(2, 2, 4, PIECE, D)

            product(th, tl, r_hi, r_lo, put)

            @pl.when(sent)
            def _():
                for q in range(4):
                    down(j, q).core(j // 2).start()

        @pl.when(jnp.logical_and(j > 0, place.core == lax.rem(j + 1, 2)))
        def _():
            for q in range(4):
                down(j - 1, q).own_core((j - 1) // 2)

        return carry

    lax.fori_loop(0, 5, down_step, 0)
    for k in range(N_COLS, N_FF):
        chunk(k).one().start()

    put_split(lhs, g_ref[...])

    def back_down(j, sums):
        cols = pl.ds(pl.multiple_of(j * FT, FT), FT)
        e = halves_sum(dot_nt(lhs[...], wd[cols, :]))
        n = U[:, cols]
        gh_g[:, cols] = jnp.sum(e * n, 0, keepdims=True)
        f = e * gh[:, cols]
        E[:, cols] = f
        return sums[0] + jnp.sum(f, -1, keepdims=True), sums[1] + jnp.sum(f * n, -1, keepdims=True)

    sf, sfn = lax.fori_loop(0, FF // FT, back_down, (zero, zero))
    mf, mfn = sf * (1.0 / FF), sfn * (1.0 / FF)
    ACC[...] = jnp.zeros_like(ACC)

    def back_up(j, carry):
        cols = pl.ds(pl.multiple_of(j * FT, FT), FT)
        dz = (E[:, cols] - mf - U[:, cols] * mfn) * rs_u * GP[:, cols]
        E[:, cols] = dz
        put_split(lhs2, dz)
        ACC[...] += halves_sum(dot_nt(lhs2[...], wu[:, cols]))
        return carry

    lax.fori_loop(0, FF // FT, back_up, 0)
    e = ACC[...]
    ny = N1[...]
    S[2:3, :] = jnp.sum(e * ny, 0, keepdims=True)
    dy1 = g_ref[...] + norm_back(e * gf[...], ny, rs_y)
    dy1_ref[...] = dy1
    put_split(lhs, dy1)

    def project_back(j, carry):
        cols = pl.ds(pl.multiple_of(256 * j, 256), 256)
        ACC[:, cols] = halves_sum(dot_nt(lhs[...], wo[cols, :]))
        return carry

    lax.fori_loop(0, 3, project_back, 0)
    e = ACC[...]
    na = V[...]
    S[1:2, :] = jnp.sum(e * na, 0, keepdims=True)
    S[0:1, :] = jnp.zeros((1, D), F32)
    for j in range(4):
        S[3 + j : 4 + j, :] = gh_g[:, D * j : D * j + D]
    lane = lax.broadcasted_iota(jnp.int32, (1, 128), 1)
    S[7:8, :] = jnp.zeros((1, D), F32)
    S[7:8, 0:128] = sum(jnp.where(lane == i, sums[i : i + 1, :], 0.0) for i in range(PATTERNS))
    ACC[...] = norm_back(e * gi[...], na, rs_a)
    pairs_from_rows(ACC, dap)
    travel.start()

    def column(k):
        return chunk(k, lambda i, c: cols_t.at[lax.rem(k, 2), i, c])

    def out_copy(k):
        return pltpu.make_async_copy(c0.at[k], C0.at[k], osem.at[k])

    put_turned(th, tl, na * gi[...])
    r_hi[...], r_lo[...] = split(dy1)

    def column_step(k, carry):
        @pl.when(k < N_COLS)
        def _():
            @pl.when(k >= 2)
            def _():
                for i in range(2):
                    column(k - 2).core(i).wait_send()

            @pl.when(k >= 1)
            def _():
                r_hi[...], r_lo[...] = split(E[:, pl.ds(pl.multiple_of(D * (k - 1), D), D)])

            def put(i, v):
                cols_t[lax.rem(k, 2), i] = v.reshape(2, 4, 2, PIECE, D)

            product(th, tl, r_hi, r_lo, put)
            for i in range(2):
                column(k).core(i).start()

            @pl.when(k == 0)
            def _():
                put_turned(th, tl, N1[...] * gf[...])

        @pl.when(k > 0)
        def _():
            for i in range(2):
                column(k - 1).own_core(i)
            out_copy(k - 1).start()

        return carry

    lax.fori_loop(0, N_COLS + 1, column_step, 0)

    def c1_copy(k):
        b1, out = (c1a, C1a) if k % 2 == 0 else (c1b, C1b)
        i = (k - N_COLS) // 2
        return pltpu.make_async_copy(b1.at[i], out.at[i], osem.at[k])

    for k in range(N_COLS, N_FF):
        chunk(k).arrived()
        c1_copy(k).start()
    travel.finish()
    for k in range(N_COLS - 2, N_COLS):
        for i in range(2):
            column(jnp.int32(k)).core(i).wait_send()
    for j in range(2, 4):

        @pl.when(place.core != j % 2)
        def _(j=j):
            for q in range(4):
                down(jnp.int32(j), q).core(j // 2).wait_send()

    for k in range(N_COLS):
        out_copy(k).wait()
    for k in range(N_COLS, N_FF):
        chunk(k).one().wait_send()
        c1_copy(k).wait()


def feed_forward(rec, x, g, wo, wu, wd, gi, gf, gh, sums):
    act = jax.ShapeDtypeStruct((ROWS, D), F32)
    wide = pltpu.VMEM((ROWS, FF), F32)
    thin = pltpu.VMEM((ROWS, D), F32)
    return pl.pallas_call(
        ff_kernel,
        out_shape=[
            jax.ShapeDtypeStruct((ROWS, 1, D), F32),
            jax.ShapeDtypeStruct((HOMES, HALF, 128), F32),
            act,
            jax.ShapeDtypeStruct((8, D), F32),
            jax.ShapeDtypeStruct((N_COLS, 2, 4, 2, PIECE, D), F32),
            jax.ShapeDtypeStruct((2, 4, 2, PIECE, D), F32),
            jax.ShapeDtypeStruct((2, 2, 4, PIECE, D), F32),
        ],
        in_specs=[VM, VM, VM, ANY, ANY, ANY] + [VM] * 4,
        out_specs=[VM, ANY, VM, VM, ANY, ANY, ANY],
        scratch_shapes=[
            pltpu.VMEM((HEADS, HALF, 128), F32),
            pltpu.VMEM((2 * ROWS, D), BF16),
            pltpu.VMEM((2 * ROWS, FT), BF16),
            pltpu.VMEM((1, D), F32),
            pltpu.VMEM((1, D), F32),
            pltpu.VMEM((1, FF), F32),
            pltpu.VMEM((1, FF), F32),
            thin,
            thin,
            thin,
            thin,
            wide,
            wide,
            wide,
            thin,
        ]
        + [
            pltpu.VMEM((D, ROWS), BF16),
            pltpu.VMEM((D, ROWS), BF16),
            pltpu.VMEM((ROWS, D), BF16),
            pltpu.VMEM((ROWS, D), BF16),
            pltpu.VMEM((2, 2, 2, 4, 2, PIECE, D), F32),
            pltpu.VMEM((2, 4, 2, 4, PIECE, D), F32),
            pltpu.VMEM((N_FF, 2, 4, 2, PIECE, D), F32),
            pltpu.VMEM((2, 4, 2, PIECE, D), F32),
            pltpu.VMEM((2, 2, 4, PIECE, D), F32),
            pltpu.SemaphoreType.DMA((N_FF,)),
            pltpu.VMEM((D, D), BF16),
            pltpu.VMEM((D, FF), BF16),
            pltpu.VMEM((FF, D), BF16),
            pltpu.SemaphoreType.DMA((3,)),
            pltpu.SemaphoreType.DMA((HEADS,)),
            pltpu.SemaphoreType.DMA((HOMES,)),
        ]
        + Sems.scratch(N_FF),
        compiler_params=params(collective_id=4, has_side_effects=True),
    )(rec, x, g, wo, wu, wd, gi, gf, gh, sums)


def back_all_kernel(offs, drec, own, sib, ap, lse, C0, C1a, C1b, grec, wo_g, up_g, down_g, qst, kc, vc, kt, qc, dc, lt, k4, v4, kt4, q4, d4, lt4, k5, v5, kt5, q5, d5, lt5, dk, dv, dq, dk4, dv4, dk5, dv5, dq4, dq5, b1, b2, b3, b4, dqt, ds_out, came, lsem, send, recv, qsend, qrecv, fsend, frecv, c0, c1a, c1b, c2, zl, zr, csem, *rsems):
    place = Place()
    p, s, x, core, active, head = place_facts()
    b = core
    o2, o3, o4, o5 = (offs[i, head] for i in range(1, PATTERNS))
    kvf, qf, X, df = dk, dv.at[0:2], dv.at[2:4], dq
    dqp = qst

    barrier = pltpu.get_barrier_semaphore()
    expected = place.greet(barrier)

    def greet_heads(h, carry):
        q, t = head_device(h, x)

        @pl.when(jnp.logical_not(same(p, s, q, t)))
        def _():
            pl.semaphore_signal(barrier, inc=1, device_id=to(q, t), device_id_type=MESH)

        return carry

    lax.fori_loop(0, HEADS, greet_heads, 0)
    from_homes = HOMES - (core == x).astype(jnp.int32)
    pl.semaphore_wait(barrier, expected + active.astype(jnp.int32) * from_homes)

    def put(k, v):
        @pl.when(k == 0)
        def _():
            wo_g[...] = v

        @pl.when(jnp.logical_and(k > 0, k < 5))
        def _():
            up_g[:, pl.ds(pl.multiple_of((k - 1) * D, D), D)] = v

        @pl.when(k >= 5)
        def _():
            down_g[pl.ds(pl.multiple_of((k - 5) * PIECE, PIECE), PIECE), :] = v

    sems = Sems(rsems)

    def chunk(k):
        x_first = k % 2 == 0
        b0 = c0.at[k] if k < N_COLS else None
        b1 = (c1a if x_first else c1b).at[k // 2]
        return Chunk(
            place, k, x_first, sems, b0, b1, c2.at[k], zl.at[k], zr.at[k], put=lambda v: put(jnp.int32(k), v)
        )

    def load(k):
        if k < N_COLS:
            return pltpu.make_async_copy(C0.at[k], c0.at[k], csem.at[k])
        src, dst = (C1a, c1a) if k % 2 == 0 else (C1b, c1b)
        return pltpu.make_async_copy(src.at[(k - N_COLS) // 2], dst.at[k // 2], csem.at[k])

    PAIRS = ((5, 6), (7, 8), (0, 1), (2, 3), (4,))

    def reduction(*todo):
        for stage, pair in todo:
            for k in PAIRS[pair]:
                if stage == 1:
                    load(k).wait()
                    chunk(k).one().start()
                elif stage == 2 and k >= N_COLS:
                    load(k).wait()
                    chunk(k).two().start()
                else:
                    getattr(chunk(k), f"stage{stage}")()


    def local_copies(m):
        t = pl.multiple_of((m // 2) * ROWS, 64)
        c, d = 2 * b + lax.rem(m, 2), 2 * (1 - b) + lax.rem(m, 2)
        return [
            pltpu.make_async_copy(own.at[m, pl.ds(0, ROWS), :], kvf.at[c, pl.ds(t, ROWS), :], lsem.at[m, 0]),
            pltpu.make_async_copy(sib.at[m], kvf.at[d, pl.ds(t, ROWS), :], lsem.at[m, 1]),
            pltpu.make_async_copy(own.at[m, pl.ds(ROWS, HALF), :], qst.at[m], lsem.at[m, 2]),
        ]

    lse_copy = pltpu.make_async_copy(lse, X, lsem.at[HOMES, 0])

    @pl.when(active)
    def _():
        lse_copy.start()

        def start(m, carry):
            for c in local_copies(m):
                c.start()
            return carry

        lax.fori_loop(0, HOMES, start, 0)

    for pair in PAIRS:
        for k in pair:
            load(k).start()
    reduction((2, 0), (1, 2), (2, 1))

    @pl.when(active)
    def _():
        b1[0] = key_bias((2, 128), (4, 128), 4, 1, 2 * b, True)
        b2[0] = key_bias((1, 256), (2, 256), 4, 2, 2 * b, True)
        b3[0] = key_bias((1, 256), (1, 256), 1, 1, 0, True)
        e4 = class_facts4(o4, b)[1]
        b4[0] = key_bias((1, 256), (2, 256), 12, 6, 6 * e4, True)
        for ref in (b1, b2, b3, b4):
            ref[1] = jnp.zeros(ref.shape[1:], F32)

        def wait(m, carry):
            for c in local_copies(m):
                c.wait()
            return carry

        lax.fori_loop(0, HOMES, wait, 0)
        lse_copy.wait()
        unpack_pairs(qst, 0, qf, 1.0 / math.sqrt(HD))

        def prepare(i, carry):
            c, t = i // 12, pl.multiple_of(lax.rem(i, 12) * 128, 128)
            k2, v2 = keys_and_values(kvf[c, pl.ds(t, 128), :])
            kc[c, pl.ds(t, 128), :] = k2.astype(BF16)
            vc[c, pl.ds(t, 128), :] = v2.astype(BF16)
            kt[c, :, pl.ds(t, 128)] = k2.T.astype(BF16)
            return carry

        lax.fori_loop(0, 48, prepare, 0)

        def prepare_q(i, carry):
            c, t = i // 12, pl.multiple_of(lax.rem(i, 12) * 128, 128)
            qc[c, pl.ds(t, 128), :] = query_quads(qf[c, pl.ds(t, 128), :])
            return carry

        lax.fori_loop(0, 24, prepare_q, 0)

    keys4, e4, (qc4, qv4) = class_facts4(o4, b)
    kc5, kv5 = lax.rem(o5, 4), o5 // 4
    qi4, qi5 = qc4 - 2 * b, lax.rem(kc5, 2)

    @pl.when(active)
    def _():
        for blk in range(4):
            r = slice(128 * blk, 128 * blk + 128)
            for e in range(2):
                c, v = keys4[e]
                k2, v2 = keys_and_values(kvf[c, pl.ds(v + 384 * blk, 128, stride=3), :])
                k4[e, r, :] = k2.astype(BF16)
                v4[e, r, :] = v2.astype(BF16)
                kt4[e, :, r] = k2.T.astype(BF16)
            q4[r, :] = query_quads(qf[qi4, pl.ds(qv4 + 384 * blk, 128, stride=3), :])
            rows = pl.ds(kv5 + 384 * blk, 128, stride=3)
            k2, v2 = keys_and_values(kvf[kc5, rows, :])
            k5[r, :] = k2.astype(BF16)
            v5[r, :] = v2.astype(BF16)
            kt5[:, r] = k2.T.astype(BF16)
            q5[r, :] = query_quads(qf[qi5, rows, :])
        dk[...] = jnp.zeros_like(dk)

    reduction((1, 3))

    @pl.when(active)
    def _():
        unpack_pairs(drec, 0, df, 1.0)

        def facts(m, carry):
            ci = lax.rem(m, 2)
            t = pl.multiple_of((m // 2) * ROWS, 32)
            prod = drec[m] * ap[m]
            low = lower_lanes(prod)
            d0 = jnp.sum(jnp.where(low, prod, 0.0), -1, keepdims=True)
            d1 = jnp.sum(jnp.where(low, 0.0, prod), -1, keepdims=True)
            for part, d in ((0, d0), (1, d1)):
                rows = pl.ds(t + HALF * part, HALF)
                l = X[ci, rows, :]
                X[ci, rows, :] = jnp.where(low, l, jnp.broadcast_to(d, l.shape))
            return carry

        lax.fori_loop(0, HOMES, facts, 0)

        def turned(v):
            w = v.T
            return jnp.concatenate([w[0:1, :], w[HD : HD + 1, :]], 0)

        def prepare_d(i, carry):
            c, t = i // 12, pl.multiple_of(lax.rem(i, 12) * 128, 128)
            rows = pl.ds(t, 128)
            dc[c, rows, :] = query_quads(df[c, rows, :])
            lt[i] = turned(X[c, rows, :])
            return carry

        lax.fori_loop(0, 24, prepare_d, 0)
        for blk in range(4):
            r = slice(128 * blk, 128 * blk + 128)
            rows = pl.ds(qv4 + 384 * blk, 128, stride=3)
            d4[r, :] = query_quads(df[qi4, rows, :])
            lt4[blk] = turned(X[qi4, rows, :])
            rows = pl.ds(kv5 + 384 * blk, 128, stride=3)
            d5[r, :] = query_quads(df[qi5, rows, :])
            lt5[blk] = turned(X[qi5, rows, :])
        dv[...] = jnp.zeros_like(dv)
        dq[...] = jnp.zeros_like(dq)

    def tile(k, v, kT, q, d, facts_pair, bias):
        s_ = dot_nt(doubled(k), q) + bias
        l0, l1 = facts_pair
        row = jnp.concatenate([l0[0:1, :], l1[0:1, :]], 1)
        delta = jnp.concatenate([l0[1:2, :], l1[1:2, :]], 1)
        pr = jnp.exp(s_ - row)
        ds = pr * (dot_nt(doubled(v), d) - delta)
        hi, lo = split(pr)
        d2, q2_ = d[:, :128], q[:, :128]
        dv_new = dot_nn(jnp.concatenate([hi, lo], 1), jnp.concatenate([d2, d2], 0))
        hi, lo = split(ds)
        dk_new = dot_nn(jnp.concatenate([hi, lo], 1), jnp.concatenate([q2_, q2_], 0))
        dqt[...] += dot_nn(doubled(kT), jnp.concatenate([hi, lo], 0))
        return dk_new, dv_new

    def kept(flag, v):
        return jnp.where(flag, v, 0.0)

    def at256(blk):
        return pl.ds(pl.multiple_of(256 * blk, 128), 256)

    def sweep(first, last, step, done):
        dqt[...] = jnp.zeros_like(dqt)

        def one(kb, carry):
            step(kb, jnp.where(kb == last, 0, 1))
            return carry

        lax.fori_loop(first, last + 1, one, 0)
        done(dqt[...].T)

    def q2(qb, carry):
        qs = at256(qb)

        def step(kb, which):
            ks = at256(kb)
            a, c = tile(
                jnp.concatenate([kc[o2, ks, :], kc[o2 + 2, ks, :]], 0),
                jnp.concatenate([vc[o2, ks, :], vc[o2 + 2, ks, :]], 0),
                jnp.concatenate([kt[o2, :, ks], kt[o2 + 2, :, ks]], 1),
                qc[o2, qs, :],
                dc[o2, qs, :],
                (lt.at[12 * o2 + 2 * qb], lt.at[12 * o2 + 2 * qb + 1]),
                b2[which],
            )
            for par in range(2):
                f = o2 == par
                dk[par, ks, :] += kept(f, a[:256])
                dk[par + 2, ks, :] += kept(f, a[256:])
                dv[par, ks, :] += kept(f, c[:256])
                dv[par + 2, ks, :] += kept(f, c[256:])

        def done(e):
            for par in range(2):
                dq[par, qs, :] += kept(o2 == par, e)

        sweep(jnp.where(qb >= 4, 4, 0), qb, step, done)
        return carry

    @pl.when(active)
    def _():
        lax.fori_loop(0, TOTAL // 256, q2, 0)

    reduction((3, 0), (2, 2), (3, 1), (1, 4))

    def q3(qb, carry):
        ci = lax.rem(o3, 2)
        qs = at256(qb)

        def step(kb, which):
            ks = at256(kb)
            a, c = tile(
                kc[o3, ks, :],
                vc[o3, ks, :],
                kt[o3, :, ks],
                qc[ci, qs, :],
                dc[ci, qs, :],
                (lt.at[12 * ci + 2 * qb], lt.at[12 * ci + 2 * qb + 1]),
                b3[which],
            )
            for i in range(2):
                f = o3 == 2 * b + i
                dk[2 * b + i, ks, :] += kept(f, a)
                dv[2 * b + i, ks, :] += kept(f, c)

        def done(e):
            for i in range(2):
                dq[i, qs, :] += kept(o3 == 2 * b + i, e)

        sweep(0, qb, step, done)
        return carry

    def q4_(qb, carry):
        qs = at256(qb)

        def step(kb, which):
            ks = at256(kb)
            a, c = tile(
                k4[:, ks, :].reshape(512, 128),
                v4[:, ks, :].reshape(512, 128),
                jnp.concatenate([kt4[0, :, ks], kt4[1, :, ks]], 1),
                q4[qs, :],
                d4[qs, :],
                (lt4.at[2 * qb], lt4.at[2 * qb + 1]),
                b4[which],
            )
            dk4[:, ks, :] += a.reshape(2, 256, 128)
            dv4[:, ks, :] += c.reshape(2, 256, 128)

        def done(e):
            dq4[qs, :] = e

        sweep(0, qb, step, done)
        return carry

    def q5_(qb, carry):
        qs = at256(qb)

        def step(kb, which):
            ks = at256(kb)
            a, c = tile(
                k5[ks, :], v5[ks, :], kt5[:, ks], q5[qs, :], d5[qs, :], (lt5.at[2 * qb], lt5.at[2 * qb + 1]), b3[which]
            )
            dk5[ks, :] += a
            dv5[ks, :] += c

        def done(e):
            dq5[qs, :] = e

        sweep(0, qb, step, done)
        return carry

    @pl.when(active)
    def _():
        lax.fori_loop(0, TOTAL // 256, q3, 0)
        for ref in (dk4, dv4, dk5, dv5):
            ref[...] = jnp.zeros_like(ref)
        lax.fori_loop(0, 2, q4_, 0)
        lax.fori_loop(0, 2, q5_, 0)
        mine5 = kc5 // 2 == b
        for kind in range(12):
            c, rows = kind % 4, pl.ds(kind // 4, THIRD, stride=3)
            f0, f1, f5 = o4 == kind, o4 + 6 == kind, jnp.logical_and(o5 == kind, mine5)
            dk[c, rows, :] += kept(f0, dk4[0]) + kept(f1, dk4[1]) + kept(f5, dk5[...])
            dv[c, rows, :] += kept(f0, dv4[0]) + kept(f1, dv4[1]) + kept(f5, dv5[...])
        for ci in range(2):
            for v in range(3):
                rows = pl.ds(v, THIRD, stride=3)
                f4 = jnp.logical_and(qi4 == ci, qv4 == v)
                f5 = jnp.logical_and(jnp.logical_and(qi5 == ci, kv5 == v), mine5)
                dq[ci, rows, :] += kept(f4, dq4[...]) + kept(f5, dq5[...])

    reduction((4, 0), (4, 1), (2, 3), (3, 2))

    def segment(g):
        def at(blk):
            return pl.ds(pl.multiple_of(512 * g + 128 * blk, 128), 128)

        def one(qb, carry):
            qs = at(qb)

            def step(kb, which):
                ks = at(kb)
                a, c = tile(
                    kc[:, ks, :].reshape(512, 128),
                    vc[:, ks, :].reshape(512, 128),
                    jnp.concatenate([kt[i, :, ks] for i in range(4)], 1),
                    qc[:, qs, :].reshape(256, 256),
                    dc[:, qs, :].reshape(256, 256),
                    (lt.at[4 * g + qb], lt.at[12 + 4 * g + qb]),
                    b1[which],
                )
                dk[:, ks, :] += a.reshape(4, 128, 128)
                dv[:, ks, :] += c.reshape(4, 128, 128)

            def done(e):
                dq[:, qs, :] += e.reshape(2, 128, 128)

            sweep(0, qb, step, done)
            return carry

        lax.fori_loop(0, 4, one, 0)

    def passed(m):
        return remote(ds_out.at[m], came.at[m], fsend.at[m], frecv.at[m], place.peer)

    def home_copies(m):
        q, t = home_device(core, m)
        kv = remote(came.at[m], grec.at[head, pl.ds(0, ROWS), :], send.at[m], recv.at[head], to(q, t))
        dq_ = remote(dqp.at[m], grec.at[head, pl.ds(ROWS, HALF), :], qsend.at[m], qrecv.at[head], to(q, t))
        return q, t, kv, dq_

    def rows_of(m):
        return pl.ds(pl.multiple_of((m // 2) * ROWS, 64), ROWS)

    def kv(c, m):
        k, v = dk[c, rows_of(m), :], dv[c, rows_of(m), :]
        return pick(k + swap(k), v + swap(v))

    def share(m, carry):
        ds_out[m] = kv(2 * (1 - b) + lax.rem(m, 2), m)
        passed(m).start()
        return carry

    def add(m, carry):
        q, t, far_kv, far_q = home_copies(m)
        ci = lax.rem(m, 2)
        v = dq[ci, rows_of(m), :]
        v = (v + swap(v)) * (1.0 / math.sqrt(HD))
        dqp[m] = pick(v[:HALF], v[HALF:])
        passed(m).wait_recv()
        came[m] += kv(2 * b + ci, m)

        @pl.when(same(p, s, q, t))
        def _():
            pltpu.make_async_copy(came.at[m], grec.at[head, pl.ds(0, ROWS), :], recv.at[head]).start()
            pltpu.make_async_copy(dqp.at[m], grec.at[head, pl.ds(ROWS, HALF), :], qrecv.at[head]).start()

        @pl.when(jnp.logical_not(same(p, s, q, t)))
        def _():
            far_kv.start()
            far_q.start()

        return carry

    def round_of(i, carry):
        g = jnp.where(i == 0, 0, 3 - i)

        @pl.when(active)
        def _():
            segment(g)
            lax.fori_loop(jnp.where(i == 0, 0, jnp.where(i == 1, 12, 4)), jnp.where(i == 0, 4, jnp.where(i == 1, 16, 12)), share, 0)

            @pl.when(i > 0)
            def _():
                lax.fori_loop(jnp.where(i == 1, 0, 12), jnp.where(i == 1, 4, 16), add, 0)

        @pl.when(i == 1)
        def _():
            reduction((5, 0), (5, 1), (2, 4), (3, 3), (4, 2))

        return carry

    lax.fori_loop(0, 3, round_of, 0)

    @pl.when(active)
    def _():
        lax.fori_loop(4, 12, add, 0)

    reduction((6, 0), (6, 1), (3, 4), (4, 3), (5, 2))
    reduction((4, 4), (5, 3), (6, 2))
    reduction((5, 4), (6, 3))
    reduction((6, 4))

    def from_head(h, carry):
        a = grec.at[h, pl.ds(0, ROWS), :]
        c = grec.at[h, pl.ds(ROWS, HALF), :]
        pltpu.make_async_copy(a, a, recv.at[h]).wait()
        pltpu.make_async_copy(c, c, qrecv.at[h]).wait()
        return carry

    lax.fori_loop(0, HEADS, from_head, 0)
    for k in range(N_FF):
        if k < N_COLS:
            chunk(k).one().wait_send()
        chunk(k).two().wait_send()
        chunk(k).line_sent()

    @pl.when(active)
    def _():
        def sent(m, carry):
            q, t, far_kv, far_q = home_copies(m)
            passed(m).wait_send()

            @pl.when(jnp.logical_not(same(p, s, q, t)))
            def _():
                far_kv.wait_send()
                far_q.wait_send()

            return carry

        lax.fori_loop(0, HOMES, sent, 0)


def backward_all(offs, drec, own, sib, ap, lse, C0, C1a, C1b, cid):
    dma = pltpu.SemaphoreType.DMA
    keys = pltpu.VMEM((4, TOTAL, 128), BF16)
    full = pltpu.VMEM((4, TOTAL, 128), F32)
    quad = pltpu.VMEM((2, TOTAL, 256), BF16)
    quad3 = pltpu.VMEM((THIRD, 256), BF16)
    pair3 = pltpu.VMEM((THIRD, 128), BF16)
    turned = pltpu.VMEM((128, THIRD), BF16)
    facts3 = pltpu.VMEM((4, 2, 128), F32)
    out3 = pltpu.VMEM((THIRD, 128), F32)
    packs = pltpu.VMEM((HOMES, ROWS, 128), F32)
    halves = pltpu.VMEM((HOMES, HALF, 128), F32)
    return pl.pallas_call(
        back_all_kernel,
        out_shape=[
            jax.ShapeDtypeStruct((HEADS, PACK, 128), F32),
            jax.ShapeDtypeStruct((PIECE, D), F32),
            jax.ShapeDtypeStruct((PIECE, FF), F32),
            jax.ShapeDtypeStruct((4 * PIECE, D), F32),
        ],
        in_specs=[SM, VM, ANY, ANY, VM, ANY, ANY, ANY, ANY],
        out_specs=[ANY, VM, VM, VM],
        scratch_shapes=[
            halves,
            keys,
            keys,
            pltpu.VMEM((4, 128, TOTAL), BF16),
            quad,
            quad,
            pltpu.VMEM((24, 2, 128), F32),
            pltpu.VMEM((2, THIRD, 128), BF16),
            pltpu.VMEM((2, THIRD, 128), BF16),
            pltpu.VMEM((2, 128, THIRD), BF16),
            quad3,
            quad3,
            facts3,
            pair3,
            pair3,
            turned,
            quad3,
            quad3,
            facts3,
            full,
            full,
            pltpu.VMEM((2, TOTAL, 128), F32),
            pltpu.VMEM((2, THIRD, 128), F32),
            pltpu.VMEM((2, THIRD, 128), F32),
            out3,
            out3,
            out3,
            out3,
            pltpu.VMEM((2, 512, 256), F32),
            pltpu.VMEM((2, 512, 256), F32),
            pltpu.VMEM((2, 256, 256), F32),
            pltpu.VMEM((2, 512, 256), F32),
            pltpu.VMEM((128, 256), F32),
            packs,
            packs,
            dma((HOMES + 1, 3)),
            dma((HOMES,)),
            dma((HEADS,)),
            dma((HOMES,)),
            dma((HEADS,)),
            dma((HOMES,)),
            dma((HOMES,)),
            pltpu.VMEM((N_COLS, 2, 4, 2, PIECE, D), F32),
            pltpu.VMEM((5, 4, 2, PIECE, D), F32),
            pltpu.VMEM((4, 2, 4, PIECE, D), F32),
            pltpu.VMEM((N_FF, 4, PIECE, D), F32),
            pltpu.VMEM((N_FF, 4, PIECE, D), F32),
            pltpu.VMEM((N_FF, 4, PIECE, D), F32),
            dma((N_FF,)),
        ]
        + Sems.scratch(N_FF),
        compiler_params=params(collective_id=cid, has_side_effects=True),
    )(offs, drec, own, sib, ap, lse, C0, C1a, C1b)


SEG1, SEG2, SEG3, SEG4, SEG5 = SEGMENTS
DILATION_ONE, DILATION_TWO, DILATION_THREE, DILATION_FOUR, DILATION_FIVE = DILATIONS
MASK_VALUE = -1e30
MATMUL_ACCURACY = lax.Precision.HIGHEST


def passed_along(value, axis, by):
    length = lax.axis_size(axis)
    return lax.ppermute(value, axis, [(i, (i + by) % length) for i in range(length)])


def run_is_live(distance, anchor_point, sequence_width, segment_length):
    return (anchor_point - (distance - 1) * sequence_width - 1) // segment_length == anchor_point // segment_length


def layer_norm(x, gain_vec):
    average = jnp.mean(x, -1, keepdims=True)
    centred = x - average
    variance = jnp.mean(centred * centred, -1, keepdims=True)
    return centred * lax.rsqrt(variance + LN_EPSILON) * gain_vec


def select_table(offsets_row, dilation_rate):
    return (jnp.arange(dilation_rate, dtype=jnp.int32)[:, None] == offsets_row[None, :]).astype(
        jnp.float32
    )


def spread_apart(x, select_option, dilation_rate):
    shaped = x.reshape(x.shape[0] // dilation_rate, dilation_rate, x.shape[1], x.shape[2])
    return jnp.einsum("trhd,rh->thd", shaped, select_option, precision=MATMUL_ACCURACY)


def spread_scalar_rows(x, select_option, dilation_rate):
    shaped = x.reshape(x.shape[0] // dilation_rate, dilation_rate, x.shape[1])
    return jnp.einsum("trh,rh->th", shaped, select_option, precision=MATMUL_ACCURACY)


def spread_rows(x, select_option):
    return jnp.einsum("thd,rh->trhd", x, select_option, precision=MATMUL_ACCURACY).reshape(
        -1, x.shape[1], x.shape[2]
    )


def spread_scalars(x, select_option):
    return jnp.einsum("th,rh->trh", x, select_option, precision=MATMUL_ACCURACY).reshape(
        -1, x.shape[1]
    )


def masked_score_matrix(sparse_queries, key_portion, query_position, key_position, segment_length):
    score_matrix = jnp.einsum(
        "ozt,bzt->zob", sparse_queries, key_portion, precision=MATMUL_ACCURACY
    ) * (1.0 / math.sqrt(key_portion.shape[-1]))
    q_cols = query_position.T[:, :, None]
    k_cols = key_position.T[:, None, :]
    permitted_mask = (k_cols <= q_cols) & (k_cols // segment_length == q_cols // segment_length)
    return (jnp.where(permitted_mask, score_matrix, MASK_VALUE), permitted_mask)


def prepare_pattern(
    query_sequence, key_sequence, value_sequence, offsets_row, dilation_rate, anchor_point
):
    select_option = select_table(offsets_row, dilation_rate)
    sparse_queries = spread_apart(query_sequence, select_option, dilation_rate)
    sparse_key_value = jnp.stack(
        (
            spread_apart(key_sequence, select_option, dilation_rate),
            spread_apart(value_sequence, select_option, dilation_rate),
        )
    )
    query_position = (
        anchor_point
        + jnp.arange(sparse_queries.shape[0], dtype=jnp.int32)[:, None] * dilation_rate
        + offsets_row[None, :]
    )
    return (select_option, sparse_queries, sparse_key_value, query_position)


def pattern_forward_pass(
    sparse_queries,
    sparse_key_value,
    query_position,
    reach,
    segment_length,
    anchor_point,
    sequence_width,
):
    masked_logits, permitted_mask = masked_score_matrix(
        sparse_queries, sparse_key_value[0], query_position, query_position, segment_length
    )
    row_max = jnp.max(masked_logits, -1)
    softmax_weights = jnp.where(permitted_mask, jnp.exp(masked_logits - row_max[..., None]), 0.0)
    state = (
        row_max,
        jnp.sum(softmax_weights, -1),
        jnp.einsum("tlj,jtb->tlb", softmax_weights, sparse_key_value[1], precision=MATMUL_ACCURACY),
    )

    def one_run(distance, carry):
        remote_key_value, state = carry
        remote_key_value = passed_along(remote_key_value, "seq", 1)
        key_position = query_position - distance * sequence_width

        def update(state_in):
            old_max, old_sum, old_acc = state_in
            masked_remote, permitted_remote = masked_score_matrix(
                sparse_queries, remote_key_value[0], query_position, key_position, segment_length
            )
            new_max = jnp.maximum(old_max, jnp.max(masked_remote, -1))
            weights_far = jnp.where(
                permitted_remote, jnp.exp(masked_remote - new_max[..., None]), 0.0
            )
            factor = jnp.exp(old_max - new_max)
            added = jnp.einsum(
                "tlj,jtb->tlb", weights_far, remote_key_value[1], precision=MATMUL_ACCURACY
            )
            return (
                new_max,
                old_sum * factor + jnp.sum(weights_far, -1),
                old_acc * factor[..., None] + added,
            )

        def unchanged(state_in):
            return state_in

        is_live = run_is_live(distance, anchor_point, sequence_width, segment_length)
        return remote_key_value, lax.cond(is_live, update, unchanged, state)

    state = lax.fori_loop(1, reach + 1, one_run, (sparse_key_value, state))[1]
    row_max, row_sum, accumulated = state
    mixture = jnp.transpose(accumulated / row_sum[..., None], (1, 0, 2))
    log_sum = (row_max + jnp.log(row_sum)).T
    return (mixture, log_sum)


def merge_patterns(forwards, prepared_inputs):
    full_lse = []
    full_mix = []
    for pattern_spec in range(len(forwards)):
        mixture, log_sum = forwards[pattern_spec]
        select_option = prepared_inputs[pattern_spec][0]
        covered = spread_scalars(jnp.ones_like(log_sum), select_option)
        full_lse.append(spread_scalars(log_sum, select_option) + (covered - 1.0) * 1e30)
        full_mix.append(spread_rows(mixture, select_option))
    stacked = jnp.stack(full_lse)
    row_max = jnp.max(stacked, 0)
    softmax_weights = jnp.exp(stacked - row_max)
    row_sum = jnp.sum(softmax_weights, 0)
    attended = full_mix[0] * softmax_weights[0][..., None]
    for pattern_spec in range(1, len(full_mix)):
        attended = attended + full_mix[pattern_spec] * softmax_weights[pattern_spec][..., None]
    return (attended / row_sum[..., None], row_max + jnp.log(row_sum))


def pattern_backward(
    select_option,
    dilation_rate,
    segment_length,
    anchor_point,
    sparse_queries,
    sparse_key_value,
    query_position,
    reach,
    sequence_gradient,
    row_difference,
    combined_logsumexp,
):
    sequence_width = sequence_gradient.shape[0]
    sparse_gradient = spread_apart(sequence_gradient, select_option, dilation_rate)
    sparse_output_grad = spread_scalar_rows(row_difference, select_option, dilation_rate).T
    sparse_logsumexp = spread_scalar_rows(combined_logsumexp, select_option, dilation_rate).T
    inverse_square_root = 1.0 / math.sqrt(sparse_queries.shape[-1])

    def portion_gradients(key_portion, value_portion, key_position):
        masked_logits, permitted_mask = masked_score_matrix(
            sparse_queries, key_portion, query_position, key_position, segment_length
        )
        softmax_weights = jnp.where(
            permitted_mask, jnp.exp(masked_logits - sparse_logsumexp[..., None]), 0.0
        )
        value_gradient = jnp.einsum(
            "tui,utx->itx", softmax_weights, sparse_gradient, precision=MATMUL_ACCURACY
        )
        pattern_gradient = jnp.einsum(
            "ozt,bzt->zob", sparse_gradient, value_portion, precision=MATMUL_ACCURACY
        )
        score_gradient = (
            softmax_weights
            * (pattern_gradient - sparse_output_grad[..., None])
            * inverse_square_root
        )
        query_gradient = jnp.einsum(
            "hqk,khd->qhd", score_gradient, key_portion, precision=MATMUL_ACCURACY
        )
        key_gradient = jnp.einsum(
            "tui,utx->itx", score_gradient, sparse_queries, precision=MATMUL_ACCURACY
        )
        return (query_gradient, jnp.stack((key_gradient, value_gradient)))

    query_gradient, key_value_gradient = portion_gradients(
        sparse_key_value[0], sparse_key_value[1], query_position
    )

    def one_run(distance, carry):
        remote_key_value, remote_gradient, query_sum = carry
        remote_key_value = passed_along(remote_key_value, "seq", 1)
        remote_gradient = passed_along(remote_gradient, "seq", 1)
        key_position = query_position - distance * sequence_width

        def far_grads():
            part_q, part_kv = portion_gradients(remote_key_value[0], remote_key_value[1], key_position)
            return query_sum + part_q, remote_gradient + part_kv

        def no_grads():
            return query_sum, remote_gradient

        is_live = run_is_live(distance, anchor_point, sequence_width, segment_length)
        query_sum, remote_gradient = lax.cond(is_live, far_grads, no_grads)
        return remote_key_value, remote_gradient, query_sum

    _, travelled, query_gradient = lax.fori_loop(
        1, reach + 1, one_run, (sparse_key_value, key_value_gradient, query_gradient)
    )
    return (query_gradient, passed_along(travelled, "seq", -reach))


def front_part(own_rows, w_qkv, gain_attn):
    return jnp.dot(layer_norm(own_rows, gain_attn), w_qkv, precision=MATMUL_ACCURACY)


def after_part(attn_rows, own_rows, w_out, w_up, w_down, gain_inner, gain_ffn, gain_hidden):
    residual = own_rows + jnp.dot(
        layer_norm(attn_rows, gain_inner), w_out, precision=MATMUL_ACCURACY
    )
    hidden = jax.nn.gelu(
        jnp.dot(layer_norm(residual, gain_ffn), w_up, precision=MATMUL_ACCURACY), approximate=False
    )
    return residual + jnp.dot(layer_norm(hidden, gain_hidden), w_down, precision=MATMUL_ACCURACY)


def shards(
    tokens,
    w_qkv,
    w_out,
    w_up,
    w_down,
    gain_attn,
    gain_inner,
    gain_ffn,
    gain_hidden,
    offsets,
    grad_out,
):
    w_qkv = w_qkv.astype(jnp.float32)
    w_out = w_out.astype(jnp.float32)
    w_up = w_up.astype(jnp.float32)
    w_down = w_down.astype(jnp.float32)
    groups = lax.axis_size("pat")
    local_rows = tokens.shape[0]
    sequence_width = local_rows * groups
    heads_here = HEADS // groups
    own_rows = tokens.reshape(local_rows, D)
    qkv_rows, front_back = jax.vjp(front_part, own_rows, w_qkv, gain_attn)
    gathered_qkv = lax.all_to_all(
        qkv_rows.reshape(local_rows, 1, 3, HEADS, HD),
        "pat",
        split_axis=3,
        concat_axis=1,
        tiled=True,
    )
    gathered_qkv = gathered_qkv.reshape(sequence_width, 3, heads_here, HD)
    head_offsets = lax.dynamic_slice_in_dim(
        offsets, lax.axis_index("pat") * heads_here, heads_here, 1
    )
    anchor_point = lax.axis_index("seq") * sequence_width
    dilation_rates = (DILATION_ONE, DILATION_TWO, DILATION_THREE, DILATION_FOUR, DILATION_FIVE)
    segment_lengths = (SEG1, SEG2, SEG3, SEG4, SEG5)
    reaches = [
        min((segment_lengths[pattern_spec] - 2) // sequence_width + 1, lax.axis_size("seq") - 1)
        for pattern_spec in range(PATTERNS)
    ]
    prepared_inputs = []
    for pattern_spec in range(PATTERNS):
        prepared_inputs.append(
            prepare_pattern(
                gathered_qkv[:, 0],
                gathered_qkv[:, 1],
                gathered_qkv[:, 2],
                head_offsets[pattern_spec],
                dilation_rates[pattern_spec],
                anchor_point,
            )
        )
    forwards = []
    for pattern_spec in range(PATTERNS):
        select_option, sparse_queries, sparse_key_value, query_position = prepared_inputs[
            pattern_spec
        ]
        forwards.append(
            pattern_forward_pass(
                sparse_queries,
                sparse_key_value,
                query_position,
                reaches[pattern_spec],
                segment_lengths[pattern_spec],
                anchor_point,
                sequence_width,
            )
        )
    lse_sums = jnp.stack([jnp.sum(entry[1]) for entry in forwards])
    totals = lax.psum(lse_sums, ("pat", "seq"))
    full_length = sequence_width * lax.axis_size("seq")
    counts = jnp.array(
        [
            float(full_length // dilation_rates[pattern_spec] * HEADS)
            for pattern_spec in range(PATTERNS)
        ],
        jnp.float32,
    )
    log_means = totals / counts
    attended, combined_logsumexp = merge_patterns(forwards, prepared_inputs)
    returned_rows = lax.all_to_all(
        attended.reshape(local_rows, groups, heads_here, HD),
        "pat",
        split_axis=1,
        concat_axis=2,
        tiled=True,
    )
    attn_rows = returned_rows.reshape(local_rows, D)
    result, after_back = jax.vjp(
        after_part, attn_rows, own_rows, w_out, w_up, w_down, gain_inner, gain_ffn, gain_hidden
    )
    g_attn, g_resid, g_out, g_up, g_down, g_inner, g_ffn, g_hidden = after_back(
        grad_out.reshape(local_rows, D)
    )
    sequence_gradient = lax.all_to_all(
        g_attn.reshape(local_rows, 1, HEADS, HD), "pat", split_axis=2, concat_axis=1, tiled=True
    )
    sequence_gradient = sequence_gradient.reshape(sequence_width, heads_here, HD)
    row_difference = jnp.sum(sequence_gradient * attended, -1)
    q_grads = []
    kv_grads = []
    for pattern_spec in range(PATTERNS):
        select_option, sparse_queries, sparse_key_value, query_position = prepared_inputs[
            pattern_spec
        ]
        part_q, part_kv = pattern_backward(
            select_option,
            dilation_rates[pattern_spec],
            segment_lengths[pattern_spec],
            anchor_point,
            sparse_queries,
            sparse_key_value,
            query_position,
            reaches[pattern_spec],
            sequence_gradient,
            row_difference,
            combined_logsumexp,
        )
        q_grads.append(part_q)
        kv_grads.append(part_kv)
    grad_total = jnp.zeros((sequence_width, 3, heads_here, HD), jnp.float32)
    for pattern_spec in range(PATTERNS):
        select_option = prepared_inputs[pattern_spec][0]
        grad_total = grad_total + jnp.stack(
            (
                spread_rows(q_grads[pattern_spec], select_option),
                spread_rows(kv_grads[pattern_spec][0], select_option),
                spread_rows(kv_grads[pattern_spec][1], select_option),
            ),
            1,
        )
    grad_back = lax.all_to_all(
        grad_total.reshape(local_rows, groups, 3, heads_here, HD),
        "pat",
        split_axis=1,
        concat_axis=3,
        tiled=True,
    )
    g_tokens, g_qkv, g_attn_gain = front_back(grad_back.reshape(local_rows, 3 * D))
    grad_tokens = (g_resid + g_tokens).reshape(local_rows, 1, D)
    summed = (
        lax.psum_scatter(g_qkv, ("pat", "seq"), scatter_dimension=0, tiled=True),
        lax.psum_scatter(g_out, ("pat", "seq"), scatter_dimension=0, tiled=True),
        lax.psum_scatter(g_up, ("pat", "seq"), scatter_dimension=0, tiled=True),
        lax.psum_scatter(g_down, ("pat", "seq"), scatter_dimension=0, tiled=True),
        lax.psum_scatter(g_attn_gain, ("pat", "seq"), scatter_dimension=0, tiled=True),
        lax.psum_scatter(g_inner, ("pat", "seq"), scatter_dimension=0, tiled=True),
        lax.psum_scatter(g_ffn, ("pat", "seq"), scatter_dimension=0, tiled=True),
        lax.psum_scatter(g_hidden, ("pat", "seq"), scatter_dimension=0, tiled=True),
    )
    return (
        result.reshape(local_rows, 1, D),
        grad_tokens,
        summed[0],
        summed[1],
        summed[2],
        summed[3],
        summed[4],
        summed[5],
        summed[6],
        summed[7],
        log_means,
    )


def fast_shards(tokens, w_qkv, w_out, w_up, w_down, gain_attn, gain_inner, gain_ffn, gain_hidden, offsets, grad_out):
    counts = [float(TOTAL * 4 // r * HEADS) for r in DILATIONS]
    pk, x = front(tokens, w_qkv, gain_attn)
    own, sib = to_heads(pk, True, 0)
    ap, lse, sums = attention_forward(offsets, own, sib)
    rec = to_homes(ap, 1)
    mixed, drec, dy1, S, C0, C1a, C1b = feed_forward(
        rec, x, grad_out, w_out, w_up, w_down, gain_inner, gain_ffn, gain_hidden, sums
    )
    grec, g_out, g_up, g_down = backward_all(offsets, drec, own, sib, ap, lse, C0, C1a, C1b, 2)
    gx, g_qkv, *small = finish(grec, x, dy1, w_qkv, gain_attn, S, counts, 3)
    mixed, gx, g_qkv, g_out, g_up, g_down, *small = deliver(mixed, gx, g_qkv, g_out, g_up, g_down, *small)
    return (mixed, gx, g_qkv, g_out, g_up, g_down, *(v.reshape(-1) for v in small))


def fits(mesh):
    return mesh.shape["pat"] == 4 and mesh.shape["seq"] == RUNS


def solution(mesh):
    rows = P("seq", "pat", None)
    split_rows = P(("pat", "seq"), None)
    split_one = P(("pat", "seq"))
    planned = jax.shard_map(
        fast_shards,
        mesh=mesh,
        in_specs=(rows,) + (P(),) * 9 + (rows,),
        out_specs=(rows, rows) + (split_rows,) * 4 + (split_one,) * 4 + (P(),),
        check_vma=False,
    )
    general = jax.shard_map(
        shards,
        mesh=mesh,
        in_specs=(rows,) + (P(),) * 9 + (rows,),
        out_specs=(rows, rows) + (split_rows,) * 4 + (split_one,) * 4 + (P(),),
        check_vma=False,
    )

    def layer(tokens, *rest):
        if fits(mesh) and tokens.shape[0] == TOTAL:
            return planned(tokens, *rest)
        return general(tokens, *rest)

    return layer
```
